32 devices in a mesh: dp: 4 (over y, core), fsdp: 8 (over z, x).
Axes of the slice: x: 2, y: 2, z: 4, core: 2. Of those that a mesh axis runs over, the one named last changes fastest.
Arguments:
- tokens: bfloat16 [65536, 512], P(('dp', 'fsdp')), may hold values from -6 to 6
- grad_out: bfloat16 [65536, 512], P(('dp', 'fsdp')), may hold values from -6 to 6
- routes: int32 [65536, 8], P(('dp', 'fsdp')), may hold values from 0 to 23, all different within a row
- segments: int32 [64, 1024], P(('dp', 'fsdp')), may hold values from 0 to 3, never falling along the last dimension, each value on 1 to 512 neighbouring positions
- params: float32 [3748864], P(('dp', 'fsdp'))
- first_moment: float32 [3748864], P(('dp', 'fsdp'))
- second_moment: float32 [3748864], P(('dp', 'fsdp'))
- ema_weights: float32 [3748864], P(('dp', 'fsdp'))
Outputs:
- output: bfloat16 [65536, 512], P(('dp', 'fsdp'))
- input_grad: float32 [65536, 512], P(('dp', 'fsdp'))
- expert_load: float32 [24], replicated
- grad_norm: float32 [1], replicated
- new_params: float32 [3748864], P(('dp', 'fsdp'))
- new_first: float32 [3748864], P(('dp', 'fsdp'))
- new_second: float32 [3748864], P(('dp', 'fsdp'))
- new_ema: float32 [3748864], P(('dp', 'fsdp'))
- gain_grads: float32 [2, 512], replicated
The draws below stay inside these ranges and needn't reach their ends.
Inputs may be any that keep to these rules, and one draw needn't show every extreme that they name: `routes`: each token names 8 different head experts. `segments`: document numbers never fall along a packed row.
All inputs are finite; a program needn't handle non-finite values.
Results may differ from the reference program's by a relative error of at most 0.012.
The reference program's roundings to bfloat16 on the way count: a program that leaves them out, or rounds other values in their place, can miss the bound.
Values may be sent and summed in bfloat16 or wider, within the bound.
A program may use at most 320 MiB of HBM per device.

```python
import math
import jax
import jax.numpy as jnp
import numpy as np
from jax import lax

D = 512
E = 24
TOPK = 8
H = 64
FF = 2048
LEN = 1024
STEP = 10
SEQUENCES = 64
TOKENS = 65536
P_SIZE = 3748864


def entry_layout():
    amounts = [D, D, D * E, D * H, D * H, D * E * H, E * H * D, D * FF, FF * D]
    spreads = [0.1, 0.1, 0.5 / D ** 0.5, D ** (-0.5), 20.0 * D ** (-0.5), D ** (-0.5), 0.25 * (TOPK / H) ** 0.5, D ** (-0.5), 1.5 / FF ** 0.5]
    centers = [1.0, 1.0, 0.0, 0.0, 0.0, 0.0, 0.0, 0.0, 0.0]
    spread_all = jnp.concatenate([jnp.full((amount,), spread, jnp.float32) for amount, spread in zip(amounts, spreads)])
    center_all = jnp.concatenate([jnp.full((amount,), center, jnp.float32) for amount, center in zip(amounts, centers)])
    return (spread_all, center_all)


def draw_params(key, part):
    key = jax.random.fold_in(key, 11)
    spread_all, center_all = entry_layout()
    noise = jax.random.truncated_normal(key, -3.0, 3.0, (P_SIZE,), jnp.float32)
    return center_all + spread_all * noise


def draw_ema_weights(key, part):
    key = jax.random.fold_in(key, 12)
    spread_all, center_all = entry_layout()
    noise = jax.random.truncated_normal(key, -3.0, 3.0, (P_SIZE,), jnp.float32)
    return center_all + spread_all * noise


def draw_first_moment(key, part):
    key = jax.random.fold_in(key, 13)
    typical = 1.0 / P_SIZE ** 0.5
    noise = jax.random.truncated_normal(key, -4.0, 4.0, (P_SIZE,), jnp.float32)
    return 0.11 * typical * noise


def draw_second_moment(key, part):
    key = jax.random.fold_in(key, 14)
    typical = 1.0 / P_SIZE ** 0.5
    factor = jnp.exp(jax.random.uniform(key, (P_SIZE,), jnp.float32, jnp.log(0.5), jnp.log(4.0)))
    return 0.0526 * typical * typical * factor


def level_of(rng, dims, split, smallest, largest):
    factor_of = 1.0
    for dim, shards_of in split:
        heights = jax.random.uniform(jax.random.fold_in(jax.random.fold_in(rng, 6), dim), (shards_of,), jnp.float32, smallest / len(split), largest / len(split))
        factor_of = factor_of * jnp.repeat(jnp.exp(heights), dims[dim] // shards_of).reshape((-1,) + (1,) * (len(dims) - 1 - dim))
    return factor_of


def different_ones(stream_key, rows, count, top, lift):
    order = jax.random.permutation(jax.random.fold_in(stream_key, 1), count)
    favour = order
    for power in range(3):
        favour = favour * favour // count
    favour = favour * lift // count
    lots = jax.random.randint(jax.random.fold_in(stream_key, 2), (rows, count), 0, 4096) + favour
    fixed_rows = jax.random.permutation(jax.random.fold_in(stream_key, 3), rows)[jnp.arange(count) % rows]
    lots = jnp.where(jnp.arange(rows)[:, None] == fixed_rows[None, :], 1 << 14, lots)
    score = lots * count + jnp.arange(count)
    return lax.top_k(score.astype(jnp.int32), top)[1].astype(jnp.int32)


def length_profile(count, total, bound, skew):
    portions = [(1 << 20) // math.isqrt(grade ** skew) + 1 for grade in range(2, count + 1)]
    rest, holding = total - bound - (count - 1), [1] * (count - 1)
    while rest > 0:
        movable = [i for i in range(count - 1) if holding[i] < bound]
        whole, left = sum([portions[i] for i in movable]), rest
        for i in movable:
            extra = min(bound - holding[i], max(1, left * portions[i] // whole), rest)
            holding[i] = holding[i] + extra
            rest = rest - extra
    return np.array([bound] + holding)


def uneven(key, count, total, limit, lean):
    if count == 2:
        one = jax.random.randint(key, (), max(1, total - limit), min(limit, total - 1) + 1)
        return jnp.stack([one, total - one])
    sizes = jnp.asarray(length_profile(count, total, limit, lean), jnp.int32)
    pairs = (count - 1) // 2
    giver, sink = sizes[1:1 + 2 * pairs:2], sizes[2:2 + 2 * pairs:2]
    room = jnp.minimum(giver - 1, limit - sink)
    moved = jax.random.randint(jax.random.fold_in(key, 1), (pairs,), 0, 1 << 20) % (room + 1)
    sizes = sizes.at[1:1 + 2 * pairs:2].set(giver - moved).at[2:2 + 2 * pairs:2].set(sink + moved)
    return sizes[jax.random.permutation(jax.random.fold_in(key, 2), count)]


def bell_draw(own_key, dims, scale, most, cuts=(), kind=jnp.bfloat16):
    gain = level_of(own_key, dims, cuts, -0.22, 0.18) if cuts else 1.0
    array = jax.random.normal(own_key, dims, jnp.float32) * scale * gain
    return jnp.minimum(jnp.maximum(array, -most), most).astype(kind)


def setup_inputs(seed: int = 0) -> dict:
    key_list = jax.random.split(jax.random.key(seed), 9)
    return {
        "tokens": bell_draw(key_list[0], (TOKENS, D), 1.0, 6.0, ((0, 32),)),
        "grad_out": bell_draw(key_list[1], (TOKENS, D), 1.0, 6.0, ((0, 32),)),
        "routes": different_ones(key_list[2], TOKENS, E, TOPK, 2730),
        "segments": jax.vmap(lambda own: jnp.searchsorted(jnp.cumsum(uneven(own, 4, LEN, LEN // 2, 1)), jnp.arange(LEN), side="right"))(jax.random.split(key_list[3], SEQUENCES)).reshape((SEQUENCES, LEN)).astype(jnp.int32),
        "params": draw_params(jax.random.fold_in(key_list[8], 71), 0),
        "first_moment": draw_first_moment(jax.random.fold_in(key_list[8], 71), 0),
        "second_moment": draw_second_moment(jax.random.fold_in(key_list[8], 71), 0),
        "ema_weights": draw_ema_weights(jax.random.fold_in(key_list[8], 71), 0),
    }


@jax.custom_vjp
def low(v):
    return lax.optimization_barrier(v.astype(jnp.bfloat16)).astype(jnp.float32)

@jax.custom_vjp
def low_back(v):
    return v

def low_keep(v):
    return (low(v), None)

def low_pass(kept, grad):
    return (grad,)

def back_keep(v):
    return (v, None)

def back_low(kept, grad):
    return (low(grad),)
low.defvjp(low_keep, low_pass)
low_back.defvjp(back_keep, back_low)
top_precision = lax.Precision.HIGHEST
NORM_EPS = 1e-06
CLIP_LIMIT = 1.0
BETA_FIRST = 0.9
BETA_SECOND = 0.95
LEARN_RATE = 0.1
DECAY_RATE = 0.1
ADAM_EPS = 1e-08
EMA_KEEP = 0.9
NEG_LARGE = -1e+30

def matmul(operand_a, operand_b):
    return jnp.dot(operand_a, operand_b, precision=top_precision, preferred_element_type=jnp.float32)

def piece_shapes():
    return ((D,), (D,), (D, E), (D, H), (D, H), (D, E * H), (E * H, D), (D, FF), (FF, D))

def split_flat(flat_values):
    pieces = []
    offset = 0
    for dimensions in piece_shapes():
        amount = 1
        for extent in dimensions:
            amount = amount * extent
        pieces.append(flat_values[offset:offset + amount].reshape(dimensions))
        offset = offset + amount
    return pieces

def rms_scale(values):
    return lax.rsqrt(lax.optimization_barrier(jnp.mean(values * values, axis=-1, keepdims=True)) + NORM_EPS)

def sequence_forward(flat_params, inputs, route_row, segment_row):
    gain_one, gain_two, router, key_map, value_map, query_map, out_map, up_map, down_map = split_flat(low(flat_params))
    length = inputs.shape[0]
    block_rows = min(512, length)
    blocks = length // block_rows
    normed = low(inputs * rms_scale(inputs) * gain_one)
    logits = low_back(matmul(normed, router))
    onehot = (route_row[:, :, None] == jnp.arange(E, dtype=jnp.int32)[None, None, :]).astype(jnp.float32)
    chosen = jnp.einsum('lke,le->lk', onehot, logits, precision=top_precision)
    gate_values = jax.nn.softmax(chosen, axis=-1)
    queries_all = low_back(low(matmul(normed, query_map))).reshape(length, E, H)
    queries = jnp.einsum('lke,leh->lkh', onehot, queries_all, precision=top_precision)
    key_rows = low_back(low(matmul(normed, key_map)))
    values = low_back(low(matmul(normed, value_map)))
    positions = jnp.arange(length, dtype=jnp.int32)

    def attend(block_items):
        query_block, place_block, segment_block = block_items
        raw_scores = low_back(jnp.einsum('bkh,uh->bku', query_block, key_rows, precision=top_precision))
        allowed = (positions[None, :] <= place_block[:, None]) & (segment_row[None, :] == segment_block[:, None])
        scores = jnp.where(allowed[:, None, :], raw_scores * H ** (-0.5), NEG_LARGE)
        soft_weights = low(jax.nn.softmax(scores, axis=-1))
        return low_back(jnp.einsum('bku,uh->bkh', soft_weights, values, precision=top_precision))
    attended = lax.map(jax.checkpoint(attend), (queries.reshape(blocks, block_rows, TOPK, H), positions.reshape(blocks, block_rows), segment_row.reshape(blocks, block_rows)))
    attended = attended.reshape(length, TOPK, H)
    mixed = jnp.einsum('lke,lkh->leh', onehot, gate_values[:, :, None] * attended, precision=top_precision)
    mixed = low_back(low(mixed.reshape(length, E * H)))
    residual = inputs + low_back(matmul(mixed, out_map))
    second = low(residual * rms_scale(residual) * gain_two)
    hidden_pre = low_back(matmul(second, up_map))
    hidden = low(jax.nn.gelu(hidden_pre, approximate=False))
    return residual + matmul(hidden, down_map)

def reference(tokens, grad_out, routes, segments, params, first_moment, second_moment, ema_weights):
    sequences = segments.shape[0]
    length = segments.shape[1]
    inputs_all = tokens.astype(jnp.float32).reshape(sequences, length, D)
    cotangent_all = grad_out.astype(jnp.float32).reshape(sequences, length, D)
    routes_all = routes.reshape(sequences, length, TOPK)

    def per_sequence(grad_sum, seq_items):
        inputs, cotangent, route_row, segment_row = seq_items
        outputs, pullback = jax.vjp(lambda flat_params, values: sequence_forward(flat_params, values, route_row, segment_row), params, inputs)
        grad_flat, grad_inputs = pullback(cotangent)
        return (grad_sum + grad_flat, (outputs, grad_inputs))
    grad_total, (outputs, grad_inputs) = lax.scan(per_sequence, jnp.zeros_like(params), (inputs_all, cotangent_all, routes_all, segments))
    gain_grads = grad_total[:2 * D].reshape(2, D)
    onehot_all = (routes[:, :, None] == jnp.arange(E, dtype=jnp.int32)[None, None, :]).astype(jnp.float32)
    expert_load = lax.optimization_barrier(jnp.sum(onehot_all, axis=(0, 1))) * (E / (TOKENS * TOPK))
    grad_norm = jnp.sqrt(jnp.sum(grad_total * grad_total))
    clipped = grad_total * (CLIP_LIMIT / jnp.maximum(grad_norm, CLIP_LIMIT))
    new_first = BETA_FIRST * first_moment + (1.0 - BETA_FIRST) * clipped
    new_second = BETA_SECOND * second_moment + (1.0 - BETA_SECOND) * clipped * clipped
    first_hat = new_first / (1.0 - BETA_FIRST ** STEP)
    second_hat = new_second / (1.0 - BETA_SECOND ** STEP)
    new_params = params * (1.0 - LEARN_RATE * DECAY_RATE) - LEARN_RATE * first_hat / (jnp.sqrt(second_hat) + ADAM_EPS)
    new_ema = EMA_KEEP * ema_weights + (1.0 - EMA_KEEP) * new_params
    return (outputs.reshape(TOKENS, D).astype(jnp.bfloat16), grad_inputs.reshape(TOKENS, D), expert_load, grad_norm.reshape(1), new_params, new_first, new_second, new_ema, gain_grads)
```

```python
import functools

import jax
import jax.numpy as jnp
from jax import lax
from jax.experimental import pallas as pl
from jax.experimental.pallas import tpu as pltpu
from jax.sharding import PartitionSpec as P

D = 512
E = 24
TOPK = 8
H = 64
FF = 2048
STEP = 10

NORM_EPS = 1e-06
CLIP_LIMIT = 1.0
BETA_FIRST = 0.9
BETA_SECOND = 0.95
LEARN_RATE = 0.1
DECAY_RATE = 0.1
ADAM_EPS = 1e-08
EMA_KEEP = 0.9
NEG_LARGE = -1e30

QW = E * H
KROW = QW
VROW = QW + H
RROW = QW + 2 * H
ALLW = 1696
LEN = 1024
TB = 256
NB = LEN // TB
FC = 512
MIB = 1 << 20

F32 = jnp.float32
BF16 = jnp.bfloat16


def piece_shapes():
    return ((D,), (D,), (D, E), (D, H), (D, H), (D, E * H), (E * H, D), (D, FF), (FF, D))


def split_flat(flat_values):
    pieces = []
    offset = 0
    for dimensions in piece_shapes():
        amount = 1
        for extent in dimensions:
            amount = amount * extent
        pieces.append(flat_values[offset : offset + amount].reshape(dimensions))
        offset = offset + amount
    return pieces


def nn(a, b):
    return lax.dot_general(a, b, (((1,), (0,)), ((), ())), preferred_element_type=F32)


def nt(a, b):
    return lax.dot_general(a, b, (((1,), (1,)), ((), ())), preferred_element_type=F32)


def tn(a, b):
    return lax.dot_general(a, b, (((0,), (0,)), ((), ())), preferred_element_type=F32)


def rms_scale(values):
    return lax.rsqrt(jnp.mean(values * values, axis=-1, keepdims=True) + NORM_EPS)


def slot_of(routes, k, rows):
    return jnp.broadcast_to(routes[k : k + 1, :], (rows, routes.shape[1]))


def pick_heads(route_ref, source_ref, k):
    route = jnp.broadcast_to(route_ref[k : k + 1, :], (H, route_ref.shape[1]))
    taken = source_ref[0:H, :]
    for e in range(1, E):
        taken = jnp.where(route == e, source_ref[e * H : (e + 1) * H, :], taken)
    return taken


def place_heads(route_ref, source_ref, e):
    total = jnp.zeros((H, route_ref.shape[1]), F32)
    for k in range(TOPK):
        route = jnp.broadcast_to(route_ref[k : k + 1, :], (H, route_ref.shape[1]))
        total = jnp.where(route == e, source_ref[k * H : (k + 1) * H, :], total)
    return total


def key_mask(first_key, first_query, rows, start_row):
    keys = lax.broadcasted_iota(jnp.int32, (rows, TB), 0) + first_key
    queries = lax.broadcasted_iota(jnp.int32, (rows, TB), 1) + first_query
    return (keys <= queries) & (keys >= start_row)


def head_forward_kernel(
    spans, x_ref, gain_ref, wall_ref, route_ref, start_ref,
    q_ref, att_ref, gate_ref, lse_ref, kv_ref, kvt_ref,
    all_scr, k_scr, vt_scr,
):
    step = pl.program_id(0)
    place = lax.rem(step, NB)
    here = pl.multiple_of(place * TB, TB)
    x = x_ref[...].astype(F32)
    normed = (x * rms_scale(x) * gain_ref[...]).astype(BF16)
    all_scr[...] = nt(wall_ref[...], normed)
    kt = all_scr[KROW : KROW + H, :]
    vt = all_scr[VROW : VROW + H, :]
    logits = all_scr[RROW : RROW + E, :]
    kvt = jnp.concatenate([kt, vt], axis=0)
    kv = kvt.T.astype(BF16)
    kv_ref[...] = kv
    kvt_ref[...] = kvt.astype(BF16)
    k_scr[pl.ds(here, TB), :] = kv[:, :H]
    vt_scr[:, pl.ds(here, TB)] = vt.astype(BF16)
    routes = route_ref[...]
    experts = lax.broadcasted_iota(jnp.int32, (E, TB), 0)
    chosen = jnp.concatenate(
        [
            jnp.sum(jnp.where(slot_of(routes, k, E) == experts, logits, 0.0), axis=0, keepdims=True)
            for k in range(TOPK)
        ],
        axis=0,
    )
    raised = jnp.exp(chosen - jnp.max(chosen, axis=0, keepdims=True))
    gate_ref[...] = raised / jnp.sum(raised, axis=0, keepdims=True)
    for k in range(TOPK):
        query = pick_heads(route_ref, all_scr, k).astype(BF16)
        q_ref[k * H : (k + 1) * H, :] = query * jnp.asarray(H ** (-0.5), BF16)

    def attend(blocks):
        rows = blocks * TB
        first_key = pl.multiple_of((place - (blocks - 1)) * TB, TB)
        mask = key_mask(first_key, here, rows, start_ref[...])
        keys = k_scr[pl.ds(first_key, rows), :]
        values = vt_scr[:, pl.ds(first_key, rows)]
        for k in range(TOPK):
            scores = jnp.where(mask, nn(keys, q_ref[k * H : (k + 1) * H, :]), NEG_LARGE)
            top = jnp.max(scores, axis=0, keepdims=True)
            raised = jnp.exp(scores - top)
            total = jnp.sum(raised, axis=0, keepdims=True)
            probs = (raised * (1.0 / total)).astype(BF16)
            att_ref[k * H : (k + 1) * H, :] = nn(values, probs)
            lse_ref[k : k + 1, :] = top + jnp.log(total)

    for blocks in range(1, min(3, NB) + 1):

        @pl.when(spans[step] == blocks)
        def _():
            attend(blocks)


def gelu_parts(v):
    size = jnp.abs(v) * 0.7071067811865476
    bell = jnp.exp(-(size * size))
    t = 1.0 / (1.0 + 0.3275911 * size)
    series = t * (
        0.254829592
        + t * (-0.284496736 + t * (1.421413741 + t * (-1.453152027 + t * 1.061405429)))
    )
    tail = 0.5 * series * bell
    cdf = jnp.where(v < 0.0, tail, 1.0 - tail)
    return cdf, bell * 0.3989422804014327


def middle_kernel(
    x_ref, dy_ref, gain_ref, wo_ref, w1_ref, w2_ref, route_ref, gate_ref, att_ref,
    out_ref, dres_ref, datt_ref, delta_ref, dlogit_ref, dwo_ref, dw1_ref, dw2t_ref, dgain_ref,
    slot_scr, head_scr, mix_scr,
):
    step = pl.program_id(0)

    @pl.when(step == 0)
    def _():
        dwo_ref[...] = jnp.zeros_like(dwo_ref)
        dw1_ref[...] = jnp.zeros_like(dw1_ref)
        dw2t_ref[...] = jnp.zeros_like(dw2t_ref)
        dgain_ref[...] = jnp.zeros_like(dgain_ref)

    routes = route_ref[...]
    tokens = routes.shape[1]
    gates = gate_ref[...]
    for k in range(TOPK):
        slot_scr[k * H : (k + 1) * H, :] = gates[k : k + 1, :] * att_ref[k * H : (k + 1) * H, :]
    for e in range(E):
        mix_scr[e * H : (e + 1) * H, :] = place_heads(route_ref, slot_scr, e).astype(BF16)
    x = x_ref[...].astype(F32)
    dy = dy_ref[...]
    mixed = mix_scr[...]
    residual = x + tn(mixed, wo_ref[...])
    scale = rms_scale(residual)
    gain = gain_ref[...]
    second = (residual * scale * gain).astype(BF16)
    second_t = second.T
    dy_t = dy.T
    out = residual
    dsecond = jnp.zeros((tokens, D), F32)
    for c in range(0, FF, FC):
        up = w1_ref[:, c : c + FC]
        down = w2_ref[c : c + FC, :]
        pre = nn(second, up)
        cdf, density = gelu_parts(pre)
        hidden = (pre * cdf).astype(BF16)
        dpre = (nt(dy, down) * (cdf + pre * density)).astype(BF16)
        out = out + nn(hidden, down)
        dsecond = dsecond + nt(dpre, up)
        dw2t_ref[:, c : c + FC] += nn(dy_t, hidden)
        dw1_ref[:, c : c + FC] += nn(second_t, dpre)
    out_ref[...] = out.astype(BF16)
    dgain_ref[...] += jnp.sum(dsecond * residual * scale, axis=0, keepdims=True)
    weighted = gain * dsecond
    dres = (
        dy.astype(F32)
        + scale * weighted
        - residual * (scale * scale * scale) * jnp.mean(weighted * residual, axis=-1, keepdims=True)
    )
    dres_ref[...] = dres
    branch = dres.astype(BF16)
    dwo_ref[...] += nn(mixed, branch)
    head_scr[...] = nt(wo_ref[...], branch).astype(BF16).astype(F32)
    dgates = []
    for k in range(TOPK):
        rows = slice(k * H, (k + 1) * H)
        dslot = pick_heads(route_ref, head_scr, k)
        attended = att_ref[rows, :]
        dgates.append(jnp.sum(dslot * attended, axis=0, keepdims=True))
        datt = (gates[k : k + 1, :] * dslot).astype(BF16)
        datt_ref[rows, :] = datt
        delta_ref[k : k + 1, :] = jnp.sum(datt.astype(F32) * attended, axis=0, keepdims=True)
    dgate = jnp.concatenate(dgates, axis=0)
    dchosen = gates * (dgate - jnp.sum(gates * dgate, axis=0, keepdims=True))
    experts = lax.broadcasted_iota(jnp.int32, (E, tokens), 0)
    dlogits = jnp.zeros((E, tokens), F32)
    for k in range(TOPK):
        dlogits = jnp.where(
            slot_of(routes, k, E) == experts,
            jnp.broadcast_to(dchosen[k : k + 1, :], (E, tokens)),
            dlogits,
        )
    dlogit_ref[...] = dlogits


def head_backward_kernel(
    spans, x_ref, gain_ref, wall_ref, route_ref, start_ref, q_ref, datt_ref, lse_ref, delta_ref,
    kv_ref, kvt_ref, dlogit_ref, dres_ref,
    dx_ref, dwall_ref, dgain_ref,
    dk_scr, dv_scr, dq_scr, dall_scr,
):
    step = pl.program_id(0)
    place = NB - 1 - lax.rem(step, NB)
    here = pl.multiple_of(place * TB, TB)

    @pl.when(step == 0)
    def _():
        dwall_ref[...] = jnp.zeros_like(dwall_ref)
        dgain_ref[...] = jnp.zeros_like(dgain_ref)

    @pl.when(lax.rem(step, NB) == 0)
    def _():
        dk_scr[...] = jnp.zeros_like(dk_scr)
        dv_scr[...] = jnp.zeros_like(dv_scr)

    def attend(blocks):
        rows = blocks * TB
        first_key = pl.multiple_of((place - (blocks - 1)) * TB, TB)
        mask = key_mask(first_key, here, rows, start_ref[...])
        keys = kv_ref[pl.ds(first_key, rows), :H]
        values = kv_ref[pl.ds(first_key, rows), H:]
        keys_t = kvt_ref[:H, pl.ds(first_key, rows)]
        dk = jnp.zeros((rows, H), F32)
        dv = jnp.zeros((rows, H), F32)
        for k in range(TOPK):
            part = slice(k * H, (k + 1) * H)
            query = q_ref[part, :]
            datt = datt_ref[part, :]
            scores = jnp.where(mask, nn(keys, query), NEG_LARGE)
            probs = jnp.exp(scores - lse_ref[k : k + 1, :])
            dscore = (probs * (nn(values, datt) - delta_ref[k : k + 1, :])).astype(BF16)
            dv = dv + nt(probs.astype(BF16), datt)
            dk = dk + nt(dscore, query)
            dq_scr[part, :] = nn(keys_t, dscore) * (H ** (-0.5))
        dk_scr[pl.ds(first_key, rows), :] += dk
        dv_scr[pl.ds(first_key, rows), :] += dv

    for blocks in range(1, min(3, NB) + 1):

        @pl.when(spans[(step // NB) * NB + place] == blocks)
        def _():
            attend(blocks)

    for e in range(E):
        dall_scr[e * H : (e + 1) * H, :] = place_heads(route_ref, dq_scr, e).astype(BF16)
    dkv = jnp.concatenate([dk_scr[pl.ds(here, TB), :], dv_scr[pl.ds(here, TB), :]], axis=1)
    dall_scr[KROW : KROW + 2 * H, :] = dkv.T.astype(BF16)
    dall_scr[RROW : RROW + 32, :] = jnp.concatenate(
        [dlogit_ref[...], jnp.zeros((32 - E, TB), F32)], axis=0
    ).astype(BF16)
    x = x_ref[...].astype(F32)
    scale = rms_scale(x)
    gain = gain_ref[...]
    normed = (x * scale * gain).astype(BF16)
    dall = dall_scr[...]
    dwall_ref[...] += nn(dall, normed)
    dnormed = tn(dall, wall_ref[...])
    dgain_ref[...] += jnp.sum(dnormed * x * scale, axis=0, keepdims=True)
    weighted = gain * dnormed
    dx_ref[...] = (
        dres_ref[...]
        + scale * weighted
        - x * (scale * scale * scale) * jnp.mean(weighted * x, axis=-1, keepdims=True)
    )


def whole(shape):
    return pl.BlockSpec(shape, lambda *_: (0,) * len(shape), pipeline_mode=pl.Buffered(1))


def kept(shape):
    return pl.BlockSpec(shape, lambda *_: (0,) * len(shape))


def struct(shape, kind=F32):
    return jax.ShapeDtypeStruct(shape, kind)


def params_for(mib):
    return pltpu.CompilerParams(vmem_limit_bytes=mib * MIB)


def head_forward(tokens, gain, wall, routes_t, start, spans):
    count = tokens.shape[0]
    steps = count // TB
    across = lambda rows: pl.BlockSpec((rows, TB), lambda b, *_: (0, b))
    down = lambda columns: pl.BlockSpec((TB, columns), lambda b, *_: (b, 0))
    return pl.pallas_call(
        head_forward_kernel,
        grid_spec=pltpu.PrefetchScalarGridSpec(
            num_scalar_prefetch=1,
            grid=(steps,),
            in_specs=[down(D), whole((1, D)), whole((ALLW, D)), across(TOPK), across(1)],
            out_specs=[across(TOPK * H), across(TOPK * H), across(TOPK), across(TOPK), down(2 * H), across(2 * H)],
            scratch_shapes=[
                pltpu.VMEM((ALLW, TB), F32),
                pltpu.VMEM((LEN, H), BF16),
                pltpu.VMEM((H, LEN), BF16),
            ],
        ),
        out_shape=[
            struct((TOPK * H, count), BF16),
            struct((TOPK * H, count)),
            struct((TOPK, count)),
            struct((TOPK, count)),
            struct((count, 2 * H), BF16),
            struct((2 * H, count), BF16),
        ],
        compiler_params=params_for(56),
        name="head_forward",
    )(spans, tokens, gain, wall, routes_t, start)


def middle(tokens, grad_out, gain, wo, w1, w2, routes_t, gates, attended):
    count = tokens.shape[0]
    steps = count // TB
    across = lambda rows: pl.BlockSpec((rows, TB), lambda b: (0, b))
    down = lambda columns: pl.BlockSpec((TB, columns), lambda b: (b, 0))
    return pl.pallas_call(
        middle_kernel,
        grid=(steps,),
        in_specs=[
            down(D), down(D), whole((1, D)), whole((QW, D)), whole((D, FF)), whole((FF, D)),
            across(TOPK), across(TOPK), across(TOPK * H),
        ],
        out_specs=[
            down(D), down(D), across(TOPK * H), across(TOPK), across(E),
            kept((QW, D)), kept((D, FF)), kept((D, FF)), kept((1, D)),
        ],
        out_shape=[
            struct((count, D), BF16),
            struct((count, D)),
            struct((TOPK * H, count), BF16),
            struct((TOPK, count)),
            struct((E, count)),
            struct((QW, D)),
            struct((D, FF)),
            struct((D, FF)),
            struct((1, D)),
        ],
        scratch_shapes=[
            pltpu.VMEM((TOPK * H, TB), F32),
            pltpu.VMEM((QW, TB), F32),
            pltpu.VMEM((QW, TB), BF16),
        ],
        compiler_params=params_for(56),
        name="middle",
    )(tokens, grad_out, gain, wo, w1, w2, routes_t, gates, attended)


def head_backward(tokens, gain, wall, routes_t, start, spans, queries, datt, lse, delta, kv, kvt, dlogits, dres):
    count = tokens.shape[0]
    steps = count // TB

    def place(b):
        return (b // NB) * NB + NB - 1 - b % NB

    across = lambda rows: pl.BlockSpec((rows, TB), lambda b, *_: (0, place(b)))
    down = lambda columns: pl.BlockSpec((TB, columns), lambda b, *_: (place(b), 0))
    return pl.pallas_call(
        head_backward_kernel,
        grid_spec=pltpu.PrefetchScalarGridSpec(
            num_scalar_prefetch=1,
            grid=(steps,),
            in_specs=[
                down(D), whole((1, D)), whole((ALLW, D)), across(TOPK), across(1),
                across(TOPK * H), across(TOPK * H), across(TOPK), across(TOPK),
                pl.BlockSpec((LEN, 2 * H), lambda b, *_: (b // NB, 0)),
                pl.BlockSpec((2 * H, LEN), lambda b, *_: (0, b // NB)),
                across(E), down(D),
            ],
            out_specs=[down(D), kept((ALLW, D)), kept((1, D))],
            scratch_shapes=[
                pltpu.VMEM((LEN, H), F32),
                pltpu.VMEM((LEN, H), F32),
                pltpu.VMEM((TOPK * H, TB), F32),
                pltpu.VMEM((ALLW, TB), BF16),
            ],
        ),
        out_shape=[struct((count, D)), struct((ALLW, D)), struct((1, D))],
        compiler_params=params_for(56),
        name="head_backward",
    )(spans, tokens, gain, wall, routes_t, start, queries, datt, lse, delta, kv, kvt, dlogits, dres)


def document_starts(segments):
    positions = jnp.zeros(segments.shape, jnp.int32)
    for number in range(1, 4):
        below = jnp.sum((segments < number).astype(jnp.int32), axis=1, keepdims=True)
        positions = jnp.where(segments == number, below, positions)
    blocks = jnp.arange(segments.shape[1] // TB, dtype=jnp.int32)[None, :]
    spans = blocks - positions[:, ::TB] // TB + 1
    return positions.reshape(1, -1), spans.reshape(-1)


def block_step(weights, tokens, grad_out, routes, segments):
    gain_one, gain_two, router, key_map, value_map, query_map, out_map, up_map, down_map = weights
    wall = jnp.concatenate(
        [query_map.T, key_map.T, value_map.T, router.T, jnp.zeros((ALLW - RROW - E, D), BF16)], axis=0
    )
    gain_one = gain_one.astype(F32).reshape(1, D)
    gain_two = gain_two.astype(F32).reshape(1, D)
    routes_t = routes.T
    start, spans = document_starts(segments)
    queries, attended, gates, lse, kv, kvt = head_forward(tokens, gain_one, wall, routes_t, start, spans)
    out, dres, datt, delta, dlogits, dwo, dw1, dw2t, dgain_two = middle(
        tokens, grad_out, gain_two, out_map, up_map, down_map, routes_t, gates, attended
    )
    dx, dwall, dgain_one = head_backward(
        tokens, gain_one, wall, routes_t, start, spans, queries, datt, lse, delta, kv, kvt, dlogits, dres
    )
    grads = (
        dgain_one.reshape(-1),
        dgain_two.reshape(-1),
        dwall[RROW : RROW + E].T,
        dwall[KROW : KROW + H].T,
        dwall[VROW : VROW + H].T,
        dwall[:QW].T,
        dwo,
        dw1,
        dw2t.T,
    )
    return out, dx, grads


def per_device(
    tokens, grad_out, routes, segments, params, first_moment, second_moment, ema_weights
):
    devices_all = lax.axis_size(("dp", "fsdp"))
    params_low = params.astype(jnp.bfloat16)
    weights = split_flat(lax.all_gather(params_low, ("dp", "fsdp"), axis=0, tiled=True))
    local_counts = jnp.sum(
        (routes[:, :, None] == jnp.arange(E, dtype=jnp.int32)).astype(F32), axis=(0, 1)
    )
    count_sum = lax.psum(local_counts, ("dp", "fsdp"))
    output, input_grad, grad_sums = block_step(weights, tokens, grad_out, routes, segments)
    gain_partial = jnp.stack([grad_sums[0], grad_sums[1]], axis=0)
    grad_flat = jnp.concatenate([grad_piece.reshape(-1) for grad_piece in grad_sums])
    grad_shard = lax.psum_scatter(grad_flat, ("dp", "fsdp"), scatter_dimension=0, tiled=True)
    partial_square = jnp.sum(grad_shard * grad_shard)
    square_sum, gain_grads = lax.psum((partial_square, gain_partial), ("dp", "fsdp"))
    total_tokens = tokens.shape[0] * devices_all
    expert_load = count_sum * (E / (total_tokens * TOPK))
    grad_norm = jnp.sqrt(square_sum)
    clipped = grad_shard * (CLIP_LIMIT / jnp.maximum(grad_norm, CLIP_LIMIT))
    new_first = BETA_FIRST * first_moment + (1.0 - BETA_FIRST) * clipped
    new_second = BETA_SECOND * second_moment + (1.0 - BETA_SECOND) * clipped * clipped
    first_hat = new_first / (1.0 - BETA_FIRST**STEP)
    second_hat = new_second / (1.0 - BETA_SECOND**STEP)
    new_params = params * (1.0 - LEARN_RATE * DECAY_RATE) - LEARN_RATE * first_hat / (
        jnp.sqrt(second_hat) + ADAM_EPS
    )
    new_ema = EMA_KEEP * ema_weights + (1.0 - EMA_KEEP) * new_params
    return (
        output,
        input_grad,
        expert_load,
        grad_norm.reshape(1),
        new_params,
        new_first,
        new_second,
        new_ema,
        gain_grads,
    )


def solution(mesh):
    row = P(("dp", "fsdp"), None)
    flat = P(("dp", "fsdp"))
    return jax.shard_map(
        per_device,
        mesh=mesh,
        in_specs=(row, row, row, row, flat, flat, flat, flat),
        out_specs=(row, row, P(), P(), flat, flat, flat, flat, P()),
        check_vma=False,
    )
```

```python
import functools

import jax
import jax.numpy as jnp
from jax import lax
from jax.experimental import pallas as pl
from jax.experimental.pallas import tpu as pltpu
from jax.sharding import PartitionSpec as P

D = 512
E = 24
TOPK = 8
H = 64
FF = 2048
STEP = 10

NORM_EPS = 1e-06
CLIP_LIMIT = 1.0
BETA_FIRST = 0.9
BETA_SECOND = 0.95
LEARN_RATE = 0.1
DECAY_RATE = 0.1
ADAM_EPS = 1e-08
EMA_KEEP = 0.9
NEG_LARGE = -1e30

QW = E * H
KROW = QW
VROW = QW + H
RROW = QW + 2 * H
ALLW = 1696
LEN = 1024
TB = 256
NB = LEN // TB
FC = 512
MIB = 1 << 20

WR_ROW = 8
WK_ROW = 104
WV_ROW = 360
WQ_ROW = 616
WO_ROW = 6760
W1_ROW = 12904
W2_ROW = 21096
ALL_ROWS = 29288
UNIT = 16 * 128
MESH = pl.DeviceIdType.MESH

F32 = jnp.float32
BF16 = jnp.bfloat16


def nn(a, b):
    return lax.dot_general(a, b, (((1,), (0,)), ((), ())), preferred_element_type=F32)


def nt(a, b):
    return lax.dot_general(a, b, (((1,), (1,)), ((), ())), preferred_element_type=F32)


def tn(a, b):
    return lax.dot_general(a, b, (((0,), (0,)), ((), ())), preferred_element_type=F32)


def rms_scale(values):
    return lax.rsqrt(jnp.mean(values * values, axis=-1, keepdims=True) + NORM_EPS)


def slot_of(routes, k, rows):
    return jnp.broadcast_to(routes[k : k + 1, :], (rows, routes.shape[1]))


def pick_heads(route_ref, source_ref, k):
    route = jnp.broadcast_to(route_ref[k : k + 1, :], (H, route_ref.shape[1]))
    taken = source_ref[0:H, :]
    for e in range(1, E):
        taken = jnp.where(route == e, source_ref[e * H : (e + 1) * H, :], taken)
    return taken


def place_heads(route_ref, source_ref, e):
    total = jnp.zeros((H, route_ref.shape[1]), F32)
    for k in range(TOPK):
        route = jnp.broadcast_to(route_ref[k : k + 1, :], (H, route_ref.shape[1]))
        total = jnp.where(route == e, source_ref[k * H : (k + 1) * H, :], total)
    return total


def key_mask(first_key, first_query, rows, start_row):
    keys = lax.broadcasted_iota(jnp.int32, (rows, TB), 0) + first_key
    queries = lax.broadcasted_iota(jnp.int32, (rows, TB), 1) + first_query
    return (keys <= queries) & (keys >= start_row)


def head_forward_kernel(
    spans, x_ref, gain_ref, wall_ref, route_ref, start_ref,
    q_ref, att_ref, gate_ref, lse_ref, kv_ref, kvt_ref,
    all_scr, k_scr, vt_scr,
):
    step = pl.program_id(0)
    place = lax.rem(step, NB)
    here = pl.multiple_of(place * TB, TB)
    x = x_ref[...].astype(F32)
    normed = (x * rms_scale(x) * gain_ref[...]).astype(BF16)
    all_scr[...] = nt(wall_ref[...], normed)
    kt = all_scr[KROW : KROW + H, :]
    vt = all_scr[VROW : VROW + H, :]
    logits = all_scr[RROW : RROW + E, :]
    kvt = jnp.concatenate([kt, vt], axis=0)
    kv = kvt.T.astype(BF16)
    kv_ref[...] = kv
    kvt_ref[...] = kvt.astype(BF16)
    k_scr[pl.ds(here, TB), :] = kv[:, :H]
    vt_scr[:, pl.ds(here, TB)] = vt.astype(BF16)
    routes = route_ref[...]
    experts = lax.broadcasted_iota(jnp.int32, (E, TB), 0)
    chosen = jnp.concatenate(
        [
            jnp.sum(jnp.where(slot_of(routes, k, E) == experts, logits, 0.0), axis=0, keepdims=True)
            for k in range(TOPK)
        ],
        axis=0,
    )
    raised = jnp.exp(chosen - jnp.max(chosen, axis=0, keepdims=True))
    gate_ref[...] = raised / jnp.sum(raised, axis=0, keepdims=True)
    for k in range(TOPK):
        query = pick_heads(route_ref, all_scr, k).astype(BF16)
        q_ref[k * H : (k + 1) * H, :] = query * jnp.asarray(H ** (-0.5), BF16)

    def attend(blocks):
        rows = blocks * TB
        first_key = pl.multiple_of((place - (blocks - 1)) * TB, TB)
        mask = key_mask(first_key, here, rows, start_ref[...])
        keys = k_scr[pl.ds(first_key, rows), :]
        values = vt_scr[:, pl.ds(first_key, rows)]
        for k in range(TOPK):
            scores = jnp.where(mask, nn(keys, q_ref[k * H : (k + 1) * H, :]), NEG_LARGE)
            top = jnp.max(scores, axis=0, keepdims=True)
            raised = jnp.exp(scores - top)
            total = jnp.sum(raised, axis=0, keepdims=True)
            probs = (raised * (1.0 / total)).astype(BF16)
            att_ref[k * H : (k + 1) * H, :] = nn(values, probs)
            lse_ref[k : k + 1, :] = top + jnp.log(total)

    for blocks in range(1, min(3, NB) + 1):

        @pl.when(spans[step] == blocks)
        def _():
            attend(blocks)


def picks(rows, stride, first):
    at = lax.broadcasted_iota(jnp.int32, (rows, D), 1)
    row = lax.broadcasted_iota(jnp.int32, (rows, D), 0)
    return (at == row * stride + first).astype(F32)


def exact(product, a, b):
    return lax.dot_general(
        a, b, (product, ((), ())), precision=lax.Precision.HIGHEST, preferred_element_type=F32
    )


def gelu_parts(v):
    size = jnp.abs(v) * 0.7071067811865476
    bell = jnp.exp(-(size * size))
    t = 1.0 / (1.0 + 0.3275911 * size)
    series = t * (
        0.254829592
        + t * (-0.284496736 + t * (1.421413741 + t * (-1.453152027 + t * 1.061405429)))
    )
    tail = 0.5 * series * bell
    cdf = jnp.where(v < 0.0, tail, 1.0 - tail)
    return cdf, bell * 0.3989422804014327


def middle_kernel(
    x_ref, dy_ref, gain_ref, wo_ref, w1_ref, w2_ref, route_ref, gate_ref, att_ref,
    out_ref, dres_ref, datt_ref, delta_ref, dlogit_ref, flat_ref, dgain_ref,
    slot_scr, head_scr, mix_scr, dwo_ref, dw1_ref, dw2t_ref, rows_scr, row_sem,
):
    step = pl.program_id(0)

    @pl.when(step == 0)
    def _():
        dwo_ref[...] = jnp.zeros_like(dwo_ref)
        dw1_ref[...] = jnp.zeros_like(dw1_ref)
        dw2t_ref[...] = jnp.zeros_like(dw2t_ref)
        dgain_ref[...] = jnp.zeros_like(dgain_ref)

    routes = route_ref[...]
    tokens = routes.shape[1]
    gates = gate_ref[...]
    for k in range(TOPK):
        slot_scr[k * H : (k + 1) * H, :] = gates[k : k + 1, :] * att_ref[k * H : (k + 1) * H, :]
    for e in range(E):
        mix_scr[e * H : (e + 1) * H, :] = place_heads(route_ref, slot_scr, e).astype(BF16)
    x = x_ref[...].astype(F32)
    dy = dy_ref[...]
    mixed = mix_scr[...]
    residual = x + tn(mixed, wo_ref[...])
    scale = rms_scale(residual)
    gain = gain_ref[...]
    second = (residual * scale * gain).astype(BF16)
    second_t = second.T
    dy_t = dy.T
    out = residual
    dsecond = jnp.zeros((tokens, D), F32)
    for c in range(0, FF, FC):
        up = w1_ref[:, c : c + FC]
        down = w2_ref[c : c + FC, :]
        pre = nn(second, up)
        cdf, density = gelu_parts(pre)
        hidden = (pre * cdf).astype(BF16)
        dpre = (nt(dy, down) * (cdf + pre * density)).astype(BF16)
        out = out + nn(hidden, down)
        dsecond = dsecond + nt(dpre, up)
        dw2t_ref[:, c : c + FC] += nn(dy_t, hidden)
        dw1_ref[:, c : c + FC] += nn(second_t, dpre)
    out_ref[...] = out.astype(BF16)
    dgain_ref[...] += jnp.sum(dsecond * residual * scale, axis=0, keepdims=True)
    weighted = gain * dsecond
    dres = (
        dy.astype(F32)
        + scale * weighted
        - residual * (scale * scale * scale) * jnp.mean(weighted * residual, axis=-1, keepdims=True)
    )
    dres_ref[...] = dres
    branch = dres.astype(BF16)
    dwo_ref[...] += nn(mixed, branch)
    head_scr[...] = nt(wo_ref[...], branch).astype(BF16).astype(F32)
    dgates = []
    for k in range(TOPK):
        rows = slice(k * H, (k + 1) * H)
        dslot = pick_heads(route_ref, head_scr, k)
        attended = att_ref[rows, :]
        dgates.append(jnp.sum(dslot * attended, axis=0, keepdims=True))
        datt = (gates[k : k + 1, :] * dslot).astype(BF16)
        datt_ref[rows, :] = datt
        delta_ref[k : k + 1, :] = jnp.sum(datt.astype(F32) * attended, axis=0, keepdims=True)
    dgate = jnp.concatenate(dgates, axis=0)
    dchosen = gates * (dgate - jnp.sum(gates * dgate, axis=0, keepdims=True))
    experts = lax.broadcasted_iota(jnp.int32, (E, tokens), 0)
    dlogits = jnp.zeros((E, tokens), F32)
    for k in range(TOPK):
        dlogits = jnp.where(
            slot_of(routes, k, E) == experts,
            jnp.broadcast_to(dchosen[k : k + 1, :], (E, tokens)),
            dlogits,
        )
    dlogit_ref[...] = dlogits

    @pl.when(step == pl.num_programs(0) - 1)
    def _():
        pieces = []
        for c in range(D // 128):
            lanes = slice(c * 128, (c + 1) * 128)
            rows_scr[pl.ds(c, QW, stride=4), :] = dwo_ref[:, lanes]
        pieces.append((0, QW * 4))
        first = QW * 4
        for c in range(FF // 128):
            rows_scr[pl.ds(first + c, D, stride=16), :] = dw1_ref[:, c * 128 : (c + 1) * 128]
        pieces.append((first, D * 16))
        first = first + D * 16
        for c in range(D // 128):
            rows_scr[pl.ds(first + c, FF, stride=4), :] = dw2t_ref[c * 128 : (c + 1) * 128, :].T
        pieces.append((first, FF * 4))
        copies = []
        for number, (begin, count) in enumerate(pieces):
            copy = pltpu.make_async_copy(
                rows_scr.at[pl.ds(begin, count), :],
                flat_ref.at[pl.ds(WO_ROW + begin, count), :],
                row_sem.at[number],
            )
            copy.start()
            copies.append(copy)
        for copy in copies:
            copy.wait()


def head_backward_kernel(
    spans, x_ref, gain_ref, wall_ref, route_ref, start_ref, q_ref, datt_ref, lse_ref, delta_ref,
    kv_ref, kvt_ref, dlogit_ref, dres_ref, dgain_two_ref, flat_in,
    dx_ref, flat_ref,
    dk_scr, dv_scr, dq_scr, dall_scr, dwall_ref, dgain_ref, rows_scr, row_sem,
):
    step = pl.program_id(0)
    place = NB - 1 - lax.rem(step, NB)
    here = pl.multiple_of(place * TB, TB)

    @pl.when(step == 0)
    def _():
        dwall_ref[...] = jnp.zeros_like(dwall_ref)
        dgain_ref[...] = jnp.zeros_like(dgain_ref)

    @pl.when(lax.rem(step, NB) == 0)
    def _():
        dk_scr[...] = jnp.zeros_like(dk_scr)
        dv_scr[...] = jnp.zeros_like(dv_scr)

    def attend(blocks):
        rows = blocks * TB
        first_key = pl.multiple_of((place - (blocks - 1)) * TB, TB)
        mask = key_mask(first_key, here, rows, start_ref[...])
        keys = kv_ref[pl.ds(first_key, rows), :H]
        values = kv_ref[pl.ds(first_key, rows), H:]
        keys_t = kvt_ref[:H, pl.ds(first_key, rows)]
        dk = jnp.zeros((rows, H), F32)
        dv = jnp.zeros((rows, H), F32)
        for k in range(TOPK):
            part = slice(k * H, (k + 1) * H)
            query = q_ref[part, :]
            datt = datt_ref[part, :]
            scores = jnp.where(mask, nn(keys, query), NEG_LARGE)
            probs = jnp.exp(scores - lse_ref[k : k + 1, :])
            dscore = (probs * (nn(values, datt) - delta_ref[k : k + 1, :])).astype(BF16)
            dv = dv + nt(probs.astype(BF16), datt)
            dk = dk + nt(dscore, query)
            dq_scr[part, :] = nn(keys_t, dscore) * (H ** (-0.5))
        dk_scr[pl.ds(first_key, rows), :] += dk
        dv_scr[pl.ds(first_key, rows), :] += dv

    for blocks in range(1, min(3, NB) + 1):

        @pl.when(spans[(step // NB) * NB + place] == blocks)
        def _():
            attend(blocks)

    for e in range(E):
        dall_scr[e * H : (e + 1) * H, :] = place_heads(route_ref, dq_scr, e).astype(BF16)
    dkv = jnp.concatenate([dk_scr[pl.ds(here, TB), :], dv_scr[pl.ds(here, TB), :]], axis=1)
    dall_scr[KROW : KROW + 2 * H, :] = dkv.T.astype(BF16)
    dall_scr[RROW : RROW + 32, :] = jnp.concatenate(
        [dlogit_ref[...], jnp.zeros((32 - E, TB), F32)], axis=0
    ).astype(BF16)
    x = x_ref[...].astype(F32)
    scale = rms_scale(x)
    gain = gain_ref[...]
    normed = (x * scale * gain).astype(BF16)
    dall = dall_scr[...]
    dwall_ref[...] += nn(dall, normed)
    dnormed = tn(dall, wall_ref[...])
    dgain_ref[...] += jnp.sum(dnormed * x * scale, axis=0, keepdims=True)
    weighted = gain * dnormed
    dx_ref[...] = (
        dres_ref[...]
        + scale * weighted
        - x * (scale * scale * scale) * jnp.mean(weighted * x, axis=-1, keepdims=True)
    )

    @pl.when(step == pl.num_programs(0) - 1)
    def _():
        for c in range(D // 128):
            lanes = slice(c * 128, (c + 1) * 128)
            rows_scr[c : c + 1, :] = dgain_ref[:, lanes]
            rows_scr[4 + c : 5 + c, :] = dgain_two_ref[:, lanes]
        router_t = dwall_ref[RROW : RROW + E, :]
        across = jnp.concatenate(
            [exact(((1,), (1,)), router_t, picks(32, 16, b)) for b in range(16)], axis=0
        ).T
        for j in range(3):
            rows_scr[pl.ds(WR_ROW + j, 32, stride=3), :] = across[:, j * 128 : (j + 1) * 128]
        for first, row in ((KROW, WK_ROW), (VROW, WV_ROW)):
            part = dwall_ref[first : first + H, :]
            rows_scr[row : row + 256, :] = jnp.concatenate(
                [exact(((1,), (1,)), picks(256, 2, b), part) for b in range(2)], axis=1
            )
        for c in range(QW // 128):
            rows_scr[pl.ds(WQ_ROW + c, D, stride=12), :] = dwall_ref[c * 128 : (c + 1) * 128, :].T
        copy = pltpu.make_async_copy(
            rows_scr, flat_ref.at[pl.ds(0, WO_ROW), :], row_sem.at[0]
        )
        copy.start()
        copy.wait()


def whole(shape):
    return pl.BlockSpec(shape, lambda *_: (0,) * len(shape), pipeline_mode=pl.Buffered(1))


def kept(shape):
    return pl.BlockSpec(shape, lambda *_: (0,) * len(shape))


def struct(shape, kind=F32):
    return jax.ShapeDtypeStruct(shape, kind)


def params_for(mib):
    return pltpu.CompilerParams(vmem_limit_bytes=mib * MIB)


def head_forward(tokens, gain, wall, routes_t, start, spans):
    count = tokens.shape[0]
    steps = count // TB
    across = lambda rows: pl.BlockSpec((rows, TB), lambda b, *_: (0, b))
    down = lambda columns: pl.BlockSpec((TB, columns), lambda b, *_: (b, 0))
    return pl.pallas_call(
        head_forward_kernel,
        grid_spec=pltpu.PrefetchScalarGridSpec(
            num_scalar_prefetch=1,
            grid=(steps,),
            in_specs=[down(D), whole((1, D)), whole((ALLW, D)), across(TOPK), across(1)],
            out_specs=[across(TOPK * H), across(TOPK * H), across(TOPK), across(TOPK), down(2 * H), across(2 * H)],
            scratch_shapes=[
                pltpu.VMEM((ALLW, TB), F32),
                pltpu.VMEM((LEN, H), BF16),
                pltpu.VMEM((H, LEN), BF16),
            ],
        ),
        out_shape=[
            struct((TOPK * H, count), BF16),
            struct((TOPK * H, count)),
            struct((TOPK, count)),
            struct((TOPK, count)),
            struct((count, 2 * H), BF16),
            struct((2 * H, count), BF16),
        ],
        compiler_params=params_for(56),
        name="head_forward",
    )(spans, tokens, gain, wall, routes_t, start)


def middle(flat_rows, tokens, grad_out, gain, wo, w1, w2, routes_t, gates, attended):
    count = tokens.shape[0]
    steps = count // TB
    across = lambda rows: pl.BlockSpec((rows, TB), lambda b: (0, b))
    down = lambda columns: pl.BlockSpec((TB, columns), lambda b: (b, 0))
    return pl.pallas_call(
        middle_kernel,
        grid=(steps,),
        in_specs=[
            down(D), down(D), whole((1, D)), whole((QW, D)), whole((D, FF)), whole((FF, D)),
            across(TOPK), across(TOPK), across(TOPK * H),
        ],
        out_specs=[
            down(D), down(D), across(TOPK * H), across(TOPK), across(E),
            pl.BlockSpec(memory_space=pl.ANY), kept((1, D)),
        ],
        out_shape=[
            struct((count, D), BF16),
            struct((count, D)),
            struct((TOPK * H, count), BF16),
            struct((TOPK, count)),
            struct((E, count)),
            struct((flat_rows, 128)),
            struct((1, D)),
        ],
        scratch_shapes=[
            pltpu.VMEM((TOPK * H, TB), F32),
            pltpu.VMEM((QW, TB), F32),
            pltpu.VMEM((QW, TB), BF16),
            pltpu.VMEM((QW, D), F32),
            pltpu.VMEM((D, FF), F32),
            pltpu.VMEM((D, FF), F32),
            pltpu.VMEM((ALL_ROWS - WO_ROW, 128), F32),
            pltpu.SemaphoreType.DMA((3,)),
        ],
        compiler_params=params_for(56),
        name="middle",
    )(tokens, grad_out, gain, wo, w1, w2, routes_t, gates, attended)


def head_backward(
    tokens, gain, wall, routes_t, start, spans, queries, datt, lse, delta, kv, kvt, dlogits, dres,
    dgain_two, flat,
):
    count = tokens.shape[0]
    steps = count // TB

    def place(b):
        return (b // NB) * NB + NB - 1 - b % NB

    across = lambda rows: pl.BlockSpec((rows, TB), lambda b, *_: (0, place(b)))
    down = lambda columns: pl.BlockSpec((TB, columns), lambda b, *_: (place(b), 0))
    return pl.pallas_call(
        head_backward_kernel,
        grid_spec=pltpu.PrefetchScalarGridSpec(
            num_scalar_prefetch=1,
            grid=(steps,),
            in_specs=[
                down(D), whole((1, D)), whole((ALLW, D)), across(TOPK), across(1),
                across(TOPK * H), across(TOPK * H), across(TOPK), across(TOPK),
                pl.BlockSpec((LEN, 2 * H), lambda b, *_: (b // NB, 0)),
                pl.BlockSpec((2 * H, LEN), lambda b, *_: (0, b // NB)),
                across(E), down(D), whole((1, D)), pl.BlockSpec(memory_space=pl.ANY),
            ],
            out_specs=[down(D), pl.BlockSpec(memory_space=pl.ANY)],
            scratch_shapes=[
                pltpu.VMEM((LEN, H), F32),
                pltpu.VMEM((LEN, H), F32),
                pltpu.VMEM((TOPK * H, TB), F32),
                pltpu.VMEM((ALLW, TB), BF16),
                pltpu.VMEM((ALLW, D), F32),
                pltpu.VMEM((1, D), F32),
                pltpu.VMEM((WO_ROW, 128), F32),
                pltpu.SemaphoreType.DMA((1,)),
            ],
        ),
        out_shape=[struct((count, D)), struct(flat.shape)],
        input_output_aliases={15: 1},
        compiler_params=params_for(56),
        name="head_backward",
    )(
        spans, tokens, gain, wall, routes_t, start, queries, datt, lse, delta, kv, kvt, dlogits, dres,
        dgain_two, flat,
    )


def document_starts(segments):
    positions = jnp.zeros(segments.shape, jnp.int32)
    for number in range(1, 4):
        below = jnp.sum((segments < number).astype(jnp.int32), axis=1, keepdims=True)
        positions = jnp.where(segments == number, below, positions)
    blocks = jnp.arange(segments.shape[1] // TB, dtype=jnp.int32)[None, :]
    spans = blocks - positions[:, ::TB] // TB + 1
    return positions.reshape(1, -1), spans.reshape(-1)


class Places:
    def __init__(self, shards, over):
        self.shards = shards
        self.over = over
        self.many = shards * over
        self.z_size = over // 2
        self.x_size = 2
        self.y_size = shards // 2
        self.swaps = self.x_size == self.y_size
        self.a_size, self.b_size = self.x_size, self.y_size

    def mine(self):
        shard = lax.axis_index("dp")
        other = lax.axis_index("fsdp")
        return lax.rem(shard, 2), lax.div(other, 2), lax.rem(other, 2), lax.div(shard, 2)

    def ab(self, core, x, y):
        if not self.swaps:
            return x, y
        return jnp.where(core == 0, x, y), jnp.where(core == 0, y, x)

    def device(self, core, a, b, z):
        x, y = self.ab(core, a, b)
        return (y * 2 + core, z * 2 + x)

    def number(self, core, a, b, z):
        shard, other = self.device(core, a, b, z)
        return shard * self.over + other

    def a_at(self, a, step):
        return lax.rem(a + step, self.a_size)

    def b_at(self, b, step):
        return lax.rem(b + step, self.b_size)

    def z_at(self, z, step):
        return lax.rem(z + step, self.z_size)


def window_rows(shard_size, many):
    units = [(shard_size * d) // UNIT for d in range(many + 1)]
    return 16 * (max(b - a for a, b in zip(units, units[1:])) + 1)


def first_row(shard_size, number):
    return pl.multiple_of(lax.div(number * shard_size, UNIT) * 16, 16)


def greet(devices):
    barrier = pltpu.get_barrier_semaphore()
    for device in devices:
        pl.semaphore_signal(barrier, inc=1, device_id=device, device_id_type=MESH)
    pl.semaphore_wait(barrier, len(devices))


def gather_kernel(
    places, shard_size, own_ref,
    wall_ref, gain_one_ref, gain_two_ref, wo_ref, w1_ref, w2_ref,
    land, flat, send_sem, recv_sem,
):
    core, z, x, y = places.mine()
    a, b = places.ab(core, x, y)
    other = (y * 2 + 1 - core, z * 2 + x)
    z_steps = range(1, places.z_size)
    a_steps = range(1, places.a_size)
    b_steps = range(1, places.b_size)
    near_a = [places.device(core, places.a_at(a, s), b, z) for s in a_steps]
    near_b = [places.device(core, a, places.b_at(b, s), z) for s in b_steps]
    near_z = [places.device(core, a, b, places.z_at(z, s)) for s in z_steps]
    me = places.number(core, a, b, z)
    land[me] = own_ref[...]
    greet(near_z + near_a + near_b + [other])
    sent = []

    def moved(owner, device, slot):
        return pltpu.make_async_remote_copy(
            src_ref=land.at[owner],
            dst_ref=land.at[owner],
            send_sem=send_sem.at[slot],
            recv_sem=recv_sem.at[owner],
            device_id=device,
            device_id_type=MESH,
        )

    def send(owner, devices):
        for device in devices:
            copy = moved(owner, device, len(sent))
            copy.start()
            sent.append(copy)

    def arrived(owner):
        moved(owner, other, 0).wait_recv()

    send(me, near_z + near_a + near_b + [other])
    for s in z_steps:
        owner = places.number(core, a, b, places.z_at(z, s))
        arrived(owner)
        send(owner, near_a + near_b + [other])
    for t in a_steps:
        for s in range(places.z_size):
            owner = places.number(core, places.a_at(a, t), b, places.z_at(z, s))
            arrived(owner)
            send(owner, near_b + [other])
    for u in b_steps:
        for t in range(places.a_size):
            for s in range(places.z_size):
                owner = places.number(core, places.a_at(a, t), places.b_at(b, u), places.z_at(z, s))
                arrived(owner)
                send(owner, [other])
    there_a, there_b = places.ab(1 - core, x, y)
    for u in range(places.b_size):
        for t in range(places.a_size):
            for s in range(places.z_size):
                arrived(
                    places.number(
                        1 - core, places.a_at(there_a, t), places.b_at(there_b, u), places.z_at(z, s)
                    )
                )
    for copy in sent:
        copy.wait_send()

    window = own_ref.shape[0]
    flat[0:16, :] = jnp.zeros((16, 128), F32)

    def lay(number, carry):
        row = first_row(shard_size, number)
        flat[pl.ds(row, 16), :] += land[number, 0:16, :].astype(F32)
        flat[pl.ds(row + 16, window - 16), :] = land[number, 16:window, :].astype(F32)
        return carry

    lax.fori_loop(0, places.many, lay, 0)
    for c in range(D // 128):
        lanes = slice(c * 128, (c + 1) * 128)
        gain_one_ref[:, lanes] = flat[c : c + 1, :]
        gain_two_ref[:, lanes] = flat[4 + c : 5 + c, :]
        wo_ref[:, lanes] = flat[pl.ds(WO_ROW + c, QW, stride=4), :].astype(BF16)
        w2_ref[:, lanes] = flat[pl.ds(W2_ROW + c, FF, stride=4), :].astype(BF16)
    for c in range(FF // 128):
        w1_ref[:, c * 128 : (c + 1) * 128] = flat[pl.ds(W1_ROW + c, D, stride=16), :].astype(BF16)
    for c in range(QW // 128):
        wall_ref[c * 128 : (c + 1) * 128, :] = flat[pl.ds(WQ_ROW + c, D, stride=12), :].T.astype(BF16)
    for first, row in ((KROW, WK_ROW), (VROW, WV_ROW)):
        pair = flat[row : row + 256, :].T.astype(BF16)
        wall_ref[first : first + H, :] = (
            nn(pair[:H], picks(256, 2, 0).astype(BF16)) + nn(pair[H:], picks(256, 2, 1).astype(BF16))
        ).astype(BF16)
    across = jnp.concatenate(
        [flat[pl.ds(WR_ROW + j, 32, stride=3), :] for j in range(3)], axis=1
    ).T.astype(BF16)
    router_t = jnp.zeros((E, D), F32)
    for part in range(16):
        router_t = router_t + nn(across[part * E : (part + 1) * E, :], picks(32, 16, part).astype(BF16))
    wall_ref[RROW:ALLW, :] = jnp.concatenate(
        [router_t, jnp.zeros((ALLW - RROW - E, D), F32)], axis=0
    ).astype(BF16)


def gather_weights(places, shard_size, own):
    window = own.shape[0]
    rows = (shard_size * (places.many - 1)) // UNIT * 16 + window
    vmem = pl.BlockSpec(memory_space=pltpu.VMEM)
    return pl.pallas_call(
        functools.partial(gather_kernel, places, shard_size),
        in_specs=[vmem],
        out_specs=[vmem] * 6,
        out_shape=[
            struct((ALLW, D), BF16),
            struct((1, D)),
            struct((1, D)),
            struct((QW, D), BF16),
            struct((D, FF), BF16),
            struct((FF, D), BF16),
        ],
        scratch_shapes=[
            pltpu.VMEM((places.many, window, 128), BF16),
            pltpu.VMEM((rows, 128), F32),
            pltpu.SemaphoreType.DMA((places.many,)),
            pltpu.SemaphoreType.DMA((places.many,)),
        ],
        compiler_params=pltpu.CompilerParams(
            collective_id=0, has_side_effects=True, vmem_limit_bytes=56 * MIB
        ),
        name="gather_weights",
    )(own)


STAT = 24


def reduce_kernel(
    places, shard_size, flat_ref, count_ref,
    out_ref, total_ref, gain_ref, load_ref,
    part, outgo, income, stats, part_sem, send_sem, recv_sem, stat_send, stat_recv,
):
    core, z, x, y = places.mine()
    a, b = places.ab(core, x, y)
    there_a, there_b = places.ab(1 - core, x, y)
    other = (y * 2 + 1 - core, z * 2 + x)
    me = places.number(core, a, b, z)
    window = out_ref.shape[0]
    order = [
        (u, t, s)
        for u in reversed(range(places.b_size))
        for t in reversed(range(places.a_size))
        for s in reversed(range(places.z_size))
    ]

    def owner_at(kind, from_a, from_b, u, t, s):
        return places.number(kind, places.a_at(from_a, t), places.b_at(from_b, u), places.z_at(z, s))

    def fetch(owner):
        return pltpu.make_async_copy(
            flat_ref.at[pl.ds(first_row(shard_size, owner), window), :],
            part.at[owner],
            part_sem.at[owner],
        )

    theirs = [owner_at(1 - core, there_a, there_b, *where) for where in order]
    ours = [owner_at(core, a, b, *where) for where in order]
    for owner in theirs + ours:
        fetch(owner).start()

    barrier = pltpu.get_barrier_semaphore()

    def hello(j, carry):
        number = lax.rem(me + j, places.many)
        pl.semaphore_signal(
            barrier,
            inc=1,
            device_id=(lax.div(number, places.over), lax.rem(number, places.over)),
            device_id_type=MESH,
        )
        return carry

    lax.fori_loop(1, places.many, hello, 0)
    pl.semaphore_wait(barrier, places.many - 1)
    slots = {}
    sent = []

    def moved(key, device):
        slot = slots.setdefault(key, len(slots))
        return pltpu.make_async_remote_copy(
            src_ref=outgo.at[slot],
            dst_ref=income.at[slot],
            send_sem=send_sem.at[slot],
            recv_sem=recv_sem.at[slot],
            device_id=device,
            device_id_type=MESH,
        )

    def send(key, device, values):
        copy = moved(key, device)
        outgo[slots[key]] = values.astype(BF16)
        copy.start()
        sent.append(copy)

    def taken(key):
        moved(key, other).wait_recv()
        return income[slots[key]].astype(F32)

    for where, owner in zip(order, theirs):
        fetch(owner).wait()
        send(("core",) + where, other, part[owner])
    for (u, t, s), owner in zip(order, ours):
        fetch(owner).wait()
        total = part[owner] + taken(("core", u, t, s))
        if u > 0:
            send(("b", u, t, s), places.device(core, a, places.b_at(b, u), z), total)
            continue
        for step in range(1, places.b_size):
            total = total + taken(("b", step, t, s))
        if t > 0:
            send(("a", t, s), places.device(core, places.a_at(a, t), b, z), total)
            continue
        for step in range(1, places.a_size):
            total = total + taken(("a", step, s))
        if s > 0:
            send(("z", s), places.device(core, a, b, places.z_at(z, s)), total)
            continue
        for step in range(1, places.z_size):
            total = total + taken(("z", step))
        out_ref[...] = total
        begin = me * shard_size - lax.div(me * shard_size, UNIT) * UNIT
        at = (
            lax.broadcasted_iota(jnp.int32, (window, 128), 0) * 128
            + lax.broadcasted_iota(jnp.int32, (window, 128), 1)
        )
        inside = jnp.where((at >= begin) & (at < begin + shard_size), total, 0.0)
        stats[0, 0:8, :] = jnp.broadcast_to(jnp.sum(inside * inside, axis=0, keepdims=True), (8, 128))
        stats[0, 8:16, :] = total[0:8, :]
        stats[0, 16:24, :] = jnp.broadcast_to(count_ref[...], (8, 128))

    def told(j):
        number = lax.rem(me + j, places.many)
        return pltpu.make_async_remote_copy(
            src_ref=stats.at[0],
            dst_ref=stats.at[j],
            send_sem=stat_send.at[j],
            recv_sem=stat_recv.at[j],
            device_id=(lax.div(number, places.over), lax.rem(number, places.over)),
            device_id_type=MESH,
        )

    def tell(j, carry):
        told(j).start()
        return carry

    def hear(j, carry):
        told(j).wait()
        return carry

    lax.fori_loop(1, places.many, tell, 0)
    for copy in sent:
        copy.wait_send()
    lax.fori_loop(1, places.many, hear, 0)
    total_ref[...] = jnp.broadcast_to(
        jnp.sum(jnp.sum(stats[:, 0:8, :], axis=0), axis=1, keepdims=True), (8, 128)
    )
    load_ref[...] = jnp.sum(stats[:, 16:24, :], axis=0)
    gain_ref[...] = stats[me, 8:16, :]


def reduce_grads(places, shard_size, window, flat, counts):
    vmem = pl.BlockSpec(memory_space=pltpu.VMEM)
    many = places.many
    return pl.pallas_call(
        functools.partial(reduce_kernel, places, shard_size),
        in_specs=[pl.BlockSpec(memory_space=pl.ANY), vmem],
        out_specs=[vmem] * 4,
        out_shape=[struct((window, 128)), struct((8, 128)), struct((8, 128)), struct((8, 128))],
        scratch_shapes=[
            pltpu.VMEM((many, window, 128), F32),
            pltpu.VMEM((many, window, 128), BF16),
            pltpu.VMEM((many, window, 128), BF16),
            pltpu.VMEM((many, STAT, 128), F32),
            pltpu.SemaphoreType.DMA((many,)),
            pltpu.SemaphoreType.DMA((many,)),
            pltpu.SemaphoreType.DMA((many,)),
            pltpu.SemaphoreType.DMA((many,)),
            pltpu.SemaphoreType.DMA((many,)),
        ],
        compiler_params=pltpu.CompilerParams(
            collective_id=1, has_side_effects=True, vmem_limit_bytes=56 * MIB
        ),
        name="reduce_grads",
    )(flat, counts)


def block_step(flat_rows, weights, tokens, grad_out, routes, segments):
    wall, gain_one, gain_two, out_map, up_map, down_map = weights
    routes_t = routes.T
    start, spans = document_starts(segments)
    queries, attended, gates, lse, kv, kvt = head_forward(tokens, gain_one, wall, routes_t, start, spans)
    out, dres, datt, delta, dlogits, flat, dgain_two = middle(
        flat_rows, tokens, grad_out, gain_two, out_map, up_map, down_map, routes_t, gates, attended
    )
    dx, flat = head_backward(
        tokens, gain_one, wall, routes_t, start, spans, queries, datt, lse, delta, kv, kvt, dlogits, dres,
        dgain_two, flat,
    )
    return out, dx, flat


def per_device(
    shards, over, tokens, grad_out, routes, segments, params, first_moment, second_moment, ema_weights
):
    places = Places(shards, over)
    shard_size = params.shape[0]
    window = window_rows(shard_size, places.many)
    flat_rows = (shard_size * (places.many - 1)) // UNIT * 16 + window
    me = lax.axis_index("dp") * over + lax.axis_index("fsdp")
    begin = lax.rem(me * shard_size, UNIT)
    own = lax.dynamic_update_slice(
        jnp.zeros((window * 128,), BF16), params.astype(BF16), (begin,)
    ).reshape(window, 128)
    weights = gather_weights(places, shard_size, own)
    counts = jnp.sum(
        (routes[:, :, None] == jnp.arange(128, dtype=jnp.int32)).astype(F32), axis=(0, 1)
    ).reshape(1, 128)
    output, input_grad, flat = block_step(flat_rows, weights, tokens, grad_out, routes, segments)
    reduced, square_sum, gain_grads, loads = reduce_grads(places, shard_size, window, flat, counts)
    grad_shard = lax.dynamic_slice(reduced.reshape(-1), (begin,), (shard_size,))
    total_tokens = tokens.shape[0] * places.many
    expert_load = loads[0, :E] * (E / (total_tokens * TOPK))
    grad_norm = jnp.sqrt(square_sum[0, 0])
    clipped = grad_shard * (CLIP_LIMIT / jnp.maximum(grad_norm, CLIP_LIMIT))
    new_first = BETA_FIRST * first_moment + (1.0 - BETA_FIRST) * clipped
    new_second = BETA_SECOND * second_moment + (1.0 - BETA_SECOND) * clipped * clipped
    first_hat = new_first / (1.0 - BETA_FIRST**STEP)
    second_hat = new_second / (1.0 - BETA_SECOND**STEP)
    new_params = params * (1.0 - LEARN_RATE * DECAY_RATE) - LEARN_RATE * first_hat / (
        jnp.sqrt(second_hat) + ADAM_EPS
    )
    new_ema = EMA_KEEP * ema_weights + (1.0 - EMA_KEEP) * new_params
    return (
        output,
        input_grad,
        expert_load,
        grad_norm.reshape(1),
        new_params,
        new_first,
        new_second,
        new_ema,
        gain_grads.reshape(2, D),
    )


def solution(mesh):
    row = P(("dp", "fsdp"), None)
    flat = P(("dp", "fsdp"))
    return jax.shard_map(
        functools.partial(per_device, mesh.shape["dp"], mesh.shape["fsdp"]),
        mesh=mesh,
        in_specs=(row, row, row, row, flat, flat, flat, flat),
        out_specs=(row, row, P(), P(), flat, flat, flat, flat, P()),
        check_vma=False,
    )
```

```python
import functools
import itertools

import jax
import jax.numpy as jnp
from jax import lax
from jax.experimental import pallas as pl
from jax.experimental.pallas import tpu as pltpu
from jax.sharding import PartitionSpec as P

D = 512
E = 24
TOPK = 8
H = 64
FF = 2048
STEP = 10

NORM_EPS = 1e-06
CLIP_LIMIT = 1.0
BETA_FIRST = 0.9
BETA_SECOND = 0.95
LEARN_RATE = 0.1
DECAY_RATE = 0.1
ADAM_EPS = 1e-08
EMA_KEEP = 0.9
NEG_LARGE = -1e30

QW = E * H
KROW = QW
VROW = QW + H
RROW = QW + 2 * H
ALLW = 1696
LEN = 1024
TB = 256
NB = LEN // TB
FC = 512
MIB = 1 << 20

WR_ROW = 8
WK_ROW = 104
WV_ROW = 360
WQ_ROW = 616
WO_ROW = 6760
W1_ROW = 12904
W2_ROW = 21096
ALL_ROWS = 29288
UNIT = 16 * 128
MESH = pl.DeviceIdType.MESH

F32 = jnp.float32
BF16 = jnp.bfloat16


def nn(a, b):
    return lax.dot_general(a, b, (((1,), (0,)), ((), ())), preferred_element_type=F32)


def nt(a, b):
    return lax.dot_general(a, b, (((1,), (1,)), ((), ())), preferred_element_type=F32)


def tn(a, b):
    return lax.dot_general(a, b, (((0,), (0,)), ((), ())), preferred_element_type=F32)


def rms_scale(values):
    return lax.rsqrt(jnp.mean(values * values, axis=-1, keepdims=True) + NORM_EPS)


def slot_of(routes, k, rows):
    return jnp.broadcast_to(routes[k : k + 1, :], (rows, routes.shape[1]))


def pick_heads(route_ref, source_ref, k):
    route = jnp.broadcast_to(route_ref[k : k + 1, :], (H, route_ref.shape[1]))
    taken = source_ref[0:H, :]
    for e in range(1, E):
        taken = jnp.where(route == e, source_ref[e * H : (e + 1) * H, :], taken)
    return taken


def place_heads(route_ref, source_ref, e):
    total = jnp.zeros((H, route_ref.shape[1]), F32)
    for k in range(TOPK):
        route = jnp.broadcast_to(route_ref[k : k + 1, :], (H, route_ref.shape[1]))
        total = jnp.where(route == e, source_ref[k * H : (k + 1) * H, :], total)
    return total


def key_mask(first_key, first_query, rows, start_row):
    keys = lax.broadcasted_iota(jnp.int32, (rows, TB), 0) + first_key
    queries = lax.broadcasted_iota(jnp.int32, (rows, TB), 1) + first_query
    return (keys <= queries) & (keys >= start_row)


def head_forward_kernel(
    order, shard_size, early, steps, x_ref, gain_ref, wall_ref, route_ref, start_ref, own_ref, tail_ref,
    q_ref, att_ref, gate_ref, lse_ref, kv_ref, kvt_ref, wo_ref, w1_ref, w2_ref,
    all_scr, k_scr, vt_scr, land, flat, send_sem, recv_sem,
):
    step = pl.program_id(0)
    place = lax.rem(step, NB)
    order = order()
    turns = in_steps(
        gather_turns(order, lambda owner: owner >= early, own_ref, land, send_sem, recv_sem), steps
    )
    for number, turn in enumerate(turns):

        @pl.when(step == number)
        def _(number=number, turn=turn):
            if number == 0:
                greet(order)
            for act in turn:
                act()

    here = pl.multiple_of(place * TB, TB)
    x = x_ref[...].astype(F32)
    normed = (x * rms_scale(x) * gain_ref[...]).astype(BF16)
    all_scr[...] = nt(wall_ref[...], normed)
    kt = all_scr[KROW : KROW + H, :]
    vt = all_scr[VROW : VROW + H, :]
    logits = all_scr[RROW : RROW + E, :]
    kvt = jnp.concatenate([kt, vt], axis=0)
    kv = kvt.T.astype(BF16)
    kv_ref[...] = kv
    kvt_ref[...] = kvt.astype(BF16)
    k_scr[pl.ds(here, TB), :] = kv[:, :H]
    vt_scr[:, pl.ds(here, TB)] = vt.astype(BF16)
    routes = route_ref[...]
    experts = lax.broadcasted_iota(jnp.int32, (E, TB), 0)
    chosen = jnp.concatenate(
        [
            jnp.sum(jnp.where(slot_of(routes, k, E) == experts, logits, 0.0), axis=0, keepdims=True)
            for k in range(TOPK)
        ],
        axis=0,
    )
    raised = jnp.exp(chosen - jnp.max(chosen, axis=0, keepdims=True))
    gate_ref[...] = raised / jnp.sum(raised, axis=0, keepdims=True)
    for k in range(TOPK):
        query = pick_heads(route_ref, all_scr, k).astype(BF16)
        q_ref[k * H : (k + 1) * H, :] = query * jnp.asarray(H ** (-0.5), BF16)

    def attend(blocks):
        rows = blocks * TB
        first_key = pl.multiple_of((place - (blocks - 1)) * TB, TB)
        mask = key_mask(first_key, here, rows, start_ref[...])
        keys = k_scr[pl.ds(first_key, rows), :]
        values = vt_scr[:, pl.ds(first_key, rows)]
        for k in range(TOPK):
            scores = jnp.where(mask, nn(keys, q_ref[k * H : (k + 1) * H, :]), NEG_LARGE)
            top = jnp.max(scores, axis=0, keepdims=True)
            raised = jnp.exp(scores - top)
            total = jnp.sum(raised, axis=0, keepdims=True)
            probs = (raised * (1.0 / total)).astype(BF16)
            att_ref[k * H : (k + 1) * H, :] = nn(values, probs)
            lse_ref[k : k + 1, :] = top + jnp.log(total)

    most = min(3, NB)
    for blocks in range(1, most + 1):

        @pl.when(place == blocks - 1 if blocks < most else place >= blocks - 1)
        def _():
            attend(blocks)

    @pl.when(step == steps - 1)
    def _():
        flat[0 : tail_ref.shape[0], :] = tail_ref[...]
        lay_blocks(shard_size, land, flat, early, order.many, WO_ROW)
        for c in range(D // 128):
            lanes = slice(c * 128, (c + 1) * 128)
            wo_ref[:, lanes] = flat[pl.ds(c, QW, stride=4), :].astype(BF16)
            w2_ref[:, lanes] = flat[pl.ds(W2_ROW - WO_ROW + c, FF, stride=4), :].astype(BF16)
        for c in range(FF // 128):
            w1_ref[:, c * 128 : (c + 1) * 128] = flat[
                pl.ds(W1_ROW - WO_ROW + c, D, stride=16), :
            ].astype(BF16)


def picks(rows, stride, first):
    at = lax.broadcasted_iota(jnp.int32, (rows, D), 1)
    row = lax.broadcasted_iota(jnp.int32, (rows, D), 0)
    return (at == row * stride + first).astype(F32)


def exact(product, a, b):
    return lax.dot_general(
        a, b, (product, ((), ())), precision=lax.Precision.HIGHEST, preferred_element_type=F32
    )


def gelu_parts(v):
    size = jnp.abs(v) * 0.7071067811865476
    bell = jnp.exp(-(size * size))
    t = 1.0 / (1.0 + 0.3275911 * size)
    series = t * (
        0.254829592
        + t * (-0.284496736 + t * (1.421413741 + t * (-1.453152027 + t * 1.061405429)))
    )
    tail = 0.5 * series * bell
    cdf = jnp.where(v < 0.0, tail, 1.0 - tail)
    return cdf, bell * 0.3989422804014327


def middle_kernel(
    x_ref, dy_ref, gain_ref, wo_ref, w1_ref, w2_ref, route_ref, gate_ref, att_ref,
    out_ref, dres_ref, datt_ref, delta_ref, dlogit_ref, flat_ref, dgain_ref,
    slot_scr, head_scr, mix_scr, dwo_ref, dw1_ref, dw2t_ref, rows_scr, row_sem,
):
    step = pl.program_id(0)

    @pl.when(step == 0)
    def _():
        dwo_ref[...] = jnp.zeros_like(dwo_ref)
        dw1_ref[...] = jnp.zeros_like(dw1_ref)
        dw2t_ref[...] = jnp.zeros_like(dw2t_ref)
        dgain_ref[...] = jnp.zeros_like(dgain_ref)

    routes = route_ref[...]
    tokens = routes.shape[1]
    gates = gate_ref[...]
    for k in range(TOPK):
        slot_scr[k * H : (k + 1) * H, :] = gates[k : k + 1, :] * att_ref[k * H : (k + 1) * H, :]
    for e in range(E):
        mix_scr[e * H : (e + 1) * H, :] = place_heads(route_ref, slot_scr, e).astype(BF16)
    x = x_ref[...].astype(F32)
    dy = dy_ref[...]
    mixed = mix_scr[...]
    residual = x + tn(mixed, wo_ref[...])
    scale = rms_scale(residual)
    gain = gain_ref[...]
    second = (residual * scale * gain).astype(BF16)
    second_t = second.T
    dy_t = dy.T
    out = residual
    dsecond = jnp.zeros((tokens, D), F32)
    for c in range(0, FF, FC):
        up = w1_ref[:, c : c + FC]
        down = w2_ref[c : c + FC, :]
        pre = nn(second, up)
        cdf, density = gelu_parts(pre)
        hidden = (pre * cdf).astype(BF16)
        dpre = (nt(dy, down) * (cdf + pre * density)).astype(BF16)
        out = out + nn(hidden, down)
        dsecond = dsecond + nt(dpre, up)
        dw2t_ref[:, c : c + FC] += nn(dy_t, hidden)
        dw1_ref[:, c : c + FC] += nn(second_t, dpre)
    out_ref[...] = out.astype(BF16)
    dgain_ref[...] += jnp.sum(dsecond * residual * scale, axis=0, keepdims=True)
    weighted = gain * dsecond
    dres = (
        dy.astype(F32)
        + scale * weighted
        - residual * (scale * scale * scale) * jnp.mean(weighted * residual, axis=-1, keepdims=True)
    )
    dres_ref[...] = dres
    branch = dres.astype(BF16)
    dwo_ref[...] += nn(mixed, branch)
    head_scr[...] = nt(wo_ref[...], branch).astype(BF16).astype(F32)
    dgates = []
    for k in range(TOPK):
        rows = slice(k * H, (k + 1) * H)
        dslot = pick_heads(route_ref, head_scr, k)
        attended = att_ref[rows, :]
        dgates.append(jnp.sum(dslot * attended, axis=0, keepdims=True))
        datt = (gates[k : k + 1, :] * dslot).astype(BF16)
        datt_ref[rows, :] = datt
        delta_ref[k : k + 1, :] = jnp.sum(datt.astype(F32) * attended, axis=0, keepdims=True)
    dgate = jnp.concatenate(dgates, axis=0)
    dchosen = gates * (dgate - jnp.sum(gates * dgate, axis=0, keepdims=True))
    experts = lax.broadcasted_iota(jnp.int32, (E, tokens), 0)
    dlogits = jnp.zeros((E, tokens), F32)
    for k in range(TOPK):
        dlogits = jnp.where(
            slot_of(routes, k, E) == experts,
            jnp.broadcast_to(dchosen[k : k + 1, :], (E, tokens)),
            dlogits,
        )
    dlogit_ref[...] = dlogits

    @pl.when(step == pl.num_programs(0) - 1)
    def _():
        pieces = []
        for c in range(D // 128):
            lanes = slice(c * 128, (c + 1) * 128)
            rows_scr[pl.ds(c, QW, stride=4), :] = dwo_ref[:, lanes]
        pieces.append((0, QW * 4))
        first = QW * 4
        for c in range(FF // 128):
            rows_scr[pl.ds(first + c, D, stride=16), :] = dw1_ref[:, c * 128 : (c + 1) * 128]
        pieces.append((first, D * 16))
        first = first + D * 16
        for c in range(D // 128):
            rows_scr[pl.ds(first + c, FF, stride=4), :] = dw2t_ref[c * 128 : (c + 1) * 128, :].T
        pieces.append((first, FF * 4))
        copies = []
        for number, (begin, count) in enumerate(pieces):
            copy = pltpu.make_async_copy(
                rows_scr.at[pl.ds(begin, count), :],
                flat_ref.at[pl.ds(begin, count), :],
                row_sem.at[number],
            )
            copy.start()
            copies.append(copy)
        for copy in copies:
            copy.wait()


def head_backward_kernel(
    order, shard_size, early, steps, x_ref, gain_ref, wall_ref, route_ref, start_ref, q_ref, datt_ref, lse_ref, delta_ref,
    kv_ref, kvt_ref, dlogit_ref, dres_ref, dgain_two_ref, late_ref,
    dx_ref, flat_ref, sum_ref,
    dk_scr, dv_scr, dq_scr, dall_scr, dwall_ref, dgain_ref, rows_scr, row_sem,
    part, outgo, income, part_sem, send_sem, recv_sem,
):
    step = pl.program_id(0)
    place = NB - 1 - lax.rem(step, NB)
    order = order()
    window = sum_ref.shape[0]

    def fetch(owner):
        row = pl.multiple_of(first_row(shard_size, owner) - WO_ROW, 8)
        return pltpu.make_async_copy(
            late_ref.at[pl.ds(row, window), :], part.at[owner - early], part_sem.at[owner - early]
        )

    def finish(total):
        sum_ref[...] = total

    turns = in_steps(
        reduce_turns(
            order, lambda owner: owner >= early, fetch, Shifted(part, early), outgo, income,
            send_sem, recv_sem, finish,
        ),
        steps,
    )
    for number, turn in enumerate(turns):

        @pl.when(step == number)
        def _(number=number, turn=turn):
            if number == 0:
                greet(order)
                sum_ref[...] = jnp.zeros_like(sum_ref)
            for act in turn:
                act()

    here = pl.multiple_of(place * TB, TB)

    @pl.when(step == 0)
    def _():
        dwall_ref[...] = jnp.zeros_like(dwall_ref)
        dgain_ref[...] = jnp.zeros_like(dgain_ref)

    @pl.when(lax.rem(step, NB) == 0)
    def _():
        dk_scr[...] = jnp.zeros_like(dk_scr)
        dv_scr[...] = jnp.zeros_like(dv_scr)

    def attend(blocks):
        rows = blocks * TB
        first_key = pl.multiple_of((place - (blocks - 1)) * TB, TB)
        mask = key_mask(first_key, here, rows, start_ref[...])
        keys = kv_ref[pl.ds(first_key, rows), :H]
        values = kv_ref[pl.ds(first_key, rows), H:]
        keys_t = kvt_ref[:H, pl.ds(first_key, rows)]
        dk = jnp.zeros((rows, H), F32)
        dv = jnp.zeros((rows, H), F32)
        for k in range(TOPK):
            part = slice(k * H, (k + 1) * H)
            query = q_ref[part, :]
            datt = datt_ref[part, :]
            scores = jnp.where(mask, nn(keys, query), NEG_LARGE)
            probs = jnp.exp(scores - lse_ref[k : k + 1, :])
            dscore = (probs * (nn(values, datt) - delta_ref[k : k + 1, :])).astype(BF16)
            dv = dv + nt(probs.astype(BF16), datt)
            dk = dk + nt(dscore, query)
            dq_scr[part, :] = nn(keys_t, dscore) * (H ** (-0.5))
        dk_scr[pl.ds(first_key, rows), :] += dk
        dv_scr[pl.ds(first_key, rows), :] += dv

    most = min(3, NB)
    for blocks in range(1, most + 1):

        @pl.when(place == blocks - 1 if blocks < most else place >= blocks - 1)
        def _():
            attend(blocks)

    for e in range(E):
        dall_scr[e * H : (e + 1) * H, :] = place_heads(route_ref, dq_scr, e).astype(BF16)
    dkv = jnp.concatenate([dk_scr[pl.ds(here, TB), :], dv_scr[pl.ds(here, TB), :]], axis=1)
    dall_scr[KROW : KROW + 2 * H, :] = dkv.T.astype(BF16)
    dall_scr[RROW : RROW + 32, :] = jnp.concatenate(
        [dlogit_ref[...], jnp.zeros((32 - E, TB), F32)], axis=0
    ).astype(BF16)
    x = x_ref[...].astype(F32)
    scale = rms_scale(x)
    gain = gain_ref[...]
    normed = (x * scale * gain).astype(BF16)
    dall = dall_scr[...]
    dwall_ref[...] += nn(dall, normed)
    dnormed = tn(dall, wall_ref[...])
    dgain_ref[...] += jnp.sum(dnormed * x * scale, axis=0, keepdims=True)
    weighted = gain * dnormed
    dx_ref[...] = (
        dres_ref[...]
        + scale * weighted
        - x * (scale * scale * scale) * jnp.mean(weighted * x, axis=-1, keepdims=True)
    )

    @pl.when(step == pl.num_programs(0) - 1)
    def _():
        for c in range(D // 128):
            lanes = slice(c * 128, (c + 1) * 128)
            rows_scr[c : c + 1, :] = dgain_ref[:, lanes]
            rows_scr[4 + c : 5 + c, :] = dgain_two_ref[:, lanes]
        router_t = dwall_ref[RROW : RROW + E, :]
        across = jnp.concatenate(
            [exact(((1,), (1,)), router_t, picks(32, 16, b)) for b in range(16)], axis=0
        ).T
        for j in range(3):
            rows_scr[pl.ds(WR_ROW + j, 32, stride=3), :] = across[:, j * 128 : (j + 1) * 128]
        for first, row in ((KROW, WK_ROW), (VROW, WV_ROW)):
            part = dwall_ref[first : first + H, :]
            rows_scr[row : row + 256, :] = jnp.concatenate(
                [exact(((1,), (1,)), picks(256, 2, b), part) for b in range(2)], axis=1
            )
        for c in range(QW // 128):
            rows_scr[pl.ds(WQ_ROW + c, D, stride=12), :] = dwall_ref[c * 128 : (c + 1) * 128, :].T
        extra = flat_ref.shape[0] - WO_ROW
        copies = [
            pltpu.make_async_copy(rows_scr, flat_ref.at[pl.ds(0, WO_ROW), :], row_sem.at[0]),
            pltpu.make_async_copy(
                late_ref.at[pl.ds(0, extra), :], flat_ref.at[pl.ds(WO_ROW, extra), :], row_sem.at[1]
            ),
        ]
        for copy in copies:
            copy.start()
        for copy in copies:
            copy.wait()


def whole(shape):
    return pl.BlockSpec(shape, lambda *_: (0,) * len(shape), pipeline_mode=pl.Buffered(1))


def kept(shape):
    return pl.BlockSpec(shape, lambda *_: (0,) * len(shape))


def struct(shape, kind=F32):
    return jax.ShapeDtypeStruct(shape, kind)


def params_for(mib):
    return pltpu.CompilerParams(vmem_limit_bytes=mib * MIB)


def head_forward(shards, over, shard_size, tokens, gain, wall, routes_t, start, own, tail):
    count = tokens.shape[0]
    steps = count // TB
    many = shards * over
    window = own.shape[0]
    early = early_owners(shard_size, over)
    rows = (shard_size * (many - 1)) // UNIT * 16 + window - WO_ROW
    order = functools.partial(Order, shards, over, "zxy", "zyx")
    across = lambda rows: pl.BlockSpec((rows, TB), lambda b: (0, b))
    down = lambda columns: pl.BlockSpec((TB, columns), lambda b: (b, 0))
    return pl.pallas_call(
        functools.partial(head_forward_kernel, order, shard_size, early, steps),
        grid=(steps,),
        in_specs=[
            down(D), whole((1, D)), whole((ALLW, D)), across(TOPK), across(1),
            whole(own.shape), whole(tail.shape),
        ],
        out_specs=[
            across(TOPK * H), across(TOPK * H), across(TOPK), across(TOPK), down(2 * H), across(2 * H),
            whole((QW, D)), whole((D, FF)), whole((FF, D)),
        ],
        scratch_shapes=[
            pltpu.VMEM((ALLW, TB), F32),
            pltpu.VMEM((LEN, H), BF16),
            pltpu.VMEM((H, LEN), BF16),
            pltpu.VMEM((many, window, 128), BF16),
            pltpu.VMEM((rows, 128), F32),
            pltpu.SemaphoreType.DMA((many,)),
            pltpu.SemaphoreType.DMA((many,)),
        ],
        out_shape=[
            struct((TOPK * H, count), BF16),
            struct((TOPK * H, count)),
            struct((TOPK, count)),
            struct((TOPK, count)),
            struct((count, 2 * H), BF16),
            struct((2 * H, count), BF16),
            struct((QW, D), BF16),
            struct((D, FF), BF16),
            struct((FF, D), BF16),
        ],
        compiler_params=pltpu.CompilerParams(
            collective_id=2, has_side_effects=True, vmem_limit_bytes=56 * MIB
        ),
        name="head_forward",
    )(tokens, gain, wall, routes_t, start, own, tail)


def middle(flat_rows, tokens, grad_out, gain, wo, w1, w2, routes_t, gates, attended):
    count = tokens.shape[0]
    steps = count // TB
    across = lambda rows: pl.BlockSpec((rows, TB), lambda b: (0, b))
    down = lambda columns: pl.BlockSpec((TB, columns), lambda b: (b, 0))
    return pl.pallas_call(
        middle_kernel,
        grid=(steps,),
        in_specs=[
            down(D), down(D), whole((1, D)), whole((QW, D)), whole((D, FF)), whole((FF, D)),
            across(TOPK), across(TOPK), across(TOPK * H),
        ],
        out_specs=[
            down(D), down(D), across(TOPK * H), across(TOPK), across(E),
            pl.BlockSpec(memory_space=pl.ANY), kept((1, D)),
        ],
        out_shape=[
            struct((count, D), BF16),
            struct((count, D)),
            struct((TOPK * H, count), BF16),
            struct((TOPK, count)),
            struct((E, count)),
            struct((flat_rows, 128)),
            struct((1, D)),
        ],
        scratch_shapes=[
            pltpu.VMEM((TOPK * H, TB), F32),
            pltpu.VMEM((QW, TB), F32),
            pltpu.VMEM((QW, TB), BF16),
            pltpu.VMEM((QW, D), F32),
            pltpu.VMEM((D, FF), F32),
            pltpu.VMEM((D, FF), F32),
            pltpu.VMEM((ALL_ROWS - WO_ROW, 128), F32),
            pltpu.SemaphoreType.DMA((3,)),
        ],
        compiler_params=params_for(56),
        name="middle",
    )(tokens, grad_out, gain, wo, w1, w2, routes_t, gates, attended)


class Shifted:
    def __init__(self, ref, by):
        self.ref = ref
        self.by = by

    def __getitem__(self, number):
        return self.ref[number - self.by]


def head_backward(
    shards, over, shard_size, window,
    tokens, gain, wall, routes_t, start, queries, datt, lse, delta, kv, kvt, dlogits, dres, dgain_two, late,
):
    count = tokens.shape[0]
    steps = count // TB
    many = shards * over
    early = early_owners(shard_size, over)
    early_rows = (shard_size * (early - 1)) // UNIT * 16 + window
    order = functools.partial(Order, shards, over, "zxy", "zyx")

    def place(b):
        return (b // NB) * NB + NB - 1 - b % NB

    across = lambda rows: pl.BlockSpec((rows, TB), lambda b: (0, place(b)))
    down = lambda columns: pl.BlockSpec((TB, columns), lambda b: (place(b), 0))
    return pl.pallas_call(
        functools.partial(head_backward_kernel, order, shard_size, early, steps),
        grid=(steps,),
        in_specs=[
            down(D), whole((1, D)), whole((ALLW, D)), across(TOPK), across(1),
            across(TOPK * H), across(TOPK * H), across(TOPK), across(TOPK),
            pl.BlockSpec((LEN, 2 * H), lambda b: (b // NB, 0)),
            pl.BlockSpec((2 * H, LEN), lambda b: (0, b // NB)),
            across(E), down(D), whole((1, D)), pl.BlockSpec(memory_space=pl.ANY),
        ],
        out_specs=[down(D), pl.BlockSpec(memory_space=pl.ANY), whole((window, 128))],
        scratch_shapes=[
            pltpu.VMEM((LEN, H), F32),
            pltpu.VMEM((LEN, H), F32),
            pltpu.VMEM((TOPK * H, TB), F32),
            pltpu.VMEM((ALLW, TB), BF16),
            pltpu.VMEM((ALLW, D), F32),
            pltpu.VMEM((1, D), F32),
            pltpu.VMEM((WO_ROW, 128), F32),
            pltpu.SemaphoreType.DMA((2,)),
            pltpu.VMEM((many - early, window, 128), F32),
            pltpu.VMEM((many, window, 128), BF16),
            pltpu.VMEM((many, window, 128), BF16),
            pltpu.SemaphoreType.DMA((many - early,)),
            pltpu.SemaphoreType.DMA((many,)),
            pltpu.SemaphoreType.DMA((many,)),
        ],
        out_shape=[struct((count, D)), struct((early_rows, 128)), struct((window, 128))],
        compiler_params=pltpu.CompilerParams(
            collective_id=3, has_side_effects=True, vmem_limit_bytes=60 * MIB
        ),
        name="head_backward",
    )(
        tokens, gain, wall, routes_t, start, queries, datt, lse, delta, kv, kvt, dlogits, dres,
        dgain_two, late,
    )


def document_starts(segments):
    positions = jnp.zeros(segments.shape, jnp.int32)
    for number in range(1, 4):
        below = jnp.sum((segments < number).astype(jnp.int32), axis=1, keepdims=True)
        positions = jnp.where(segments == number, below, positions)
    return positions.reshape(1, -1)


class Order:
    def __init__(self, shards, over, first, second):
        size = {"x": 2, "y": shards // 2, "z": over // 2}
        if [size[axis] for axis in first] != [size[axis] for axis in second]:
            second = first
        self.over = over
        self.many = shards * over
        self.orders = (first, second)
        self.sizes = [size[axis] for axis in first]
        self.z_at = [axis == "z" for axis in first]
        shard = lax.axis_index("dp")
        other = lax.axis_index("fsdp")
        self.here = {"x": lax.rem(other, 2), "y": lax.div(shard, 2), "z": lax.div(other, 2)}
        self.core = lax.rem(shard, 2)
        self.me = shard * over + other
        self.partner = (shard + 1 - 2 * self.core, other)

    def place(self, core):
        return [
            jnp.where(core == 0, self.here[one], self.here[two]) for one, two in zip(*self.orders)
        ]

    def device(self, core, place):
        at = {
            axis: jnp.where(core == 0, place[self.orders[0].index(axis)], place[self.orders[1].index(axis)])
            for axis in "xyz"
        }
        return (at["y"] * 2 + core, at["z"] * 2 + at["x"])

    def number(self, core, place):
        shard, other = self.device(core, place)
        return shard * self.over + other

    def moved(self, place, offsets):
        return [lax.rem(p + step, size) for p, step, size in zip(place, offsets, self.sizes)]

    def owner(self, core, offsets):
        return self.number(core, self.moved(self.place(core), offsets))

    def offsets(self):
        return list(itertools.product(*[range(size) for size in self.sizes]))

    def rank(self, offsets):
        return sum(step if z else int(step > 0) for step, z in zip(offsets, self.z_at))

    def along(self, axis):
        for step in range(1, self.sizes[axis]):
            yield [step if i == axis else 0 for i in range(3)]


def greet(order):
    devices = [order.device(order.core, order.moved(order.place(order.core), one)) for i in range(3) for one in order.along(i)]
    devices.append(order.partner)
    barrier = pltpu.get_barrier_semaphore()
    for device in devices:
        pl.semaphore_signal(barrier, inc=1, device_id=device, device_id_type=MESH)
    pl.semaphore_wait(barrier, len(devices))


def window_rows(shard_size, many):
    units = [(shard_size * d) // UNIT for d in range(many + 1)]
    return 16 * (max(b - a for a, b in zip(units, units[1:])) + 1)


def first_row(shard_size, number):
    return pl.multiple_of(lax.div(number * shard_size, UNIT) * 16, 16)


def early_owners(shard_size, over):
    group = shard_size * over
    return -(-(WO_ROW * 128) // group) * over


def gather_turns(order, wanted, own_ref, land, send_sem, recv_sem):
    core = order.core
    place = order.place(core)
    slots = {}

    def copy(owner, device, key):
        return pltpu.make_async_remote_copy(
            src_ref=land.at[owner],
            dst_ref=land.at[owner],
            send_sem=send_sem.at[slots.setdefault(key, len(slots))],
            recv_sem=recv_sem.at[owner],
            device_id=device,
            device_id_type=MESH,
        )

    def targets(offsets):
        used = [i for i in range(3) if offsets[i]]
        after = max(used) + 1 if used else 0
        found = [
            order.device(core, order.moved(place, step))
            for axis in range(after, 3)
            for step in order.along(axis)
        ]
        return found + [order.partner]

    def when_wanted(owner, act):
        pl.when(wanted(owner))(act)

    turns = {}

    def pass_on(offsets):
        owner = order.owner(core, offsets)

        def act():
            if any(offsets):
                copy(owner, order.partner, (offsets, 0)).wait_recv()
            else:
                land[owner] = own_ref[...]
            for number, device in enumerate(targets(offsets)):
                copy(owner, device, (offsets, number)).start()

        when_wanted(owner, act)

    def close(offsets):
        owner = order.owner(core, offsets)

        def act():
            for number, device in enumerate(targets(offsets)):
                copy(owner, device, (offsets, number)).wait_send()

        when_wanted(owner, act)

    def from_partner(offsets):
        owner = order.owner(1 - core, offsets)

        def act():
            copy(owner, order.partner, (offsets, 0)).wait_recv()

        when_wanted(owner, act)

    ordered = sorted(order.offsets(), key=lambda one: (order.rank(one), sum(1 for v in one if v)))
    for offsets in ordered:
        turns.setdefault(order.rank(offsets), []).append(functools.partial(pass_on, offsets))
    last = max(turns) + 1
    turns[last] = [functools.partial(from_partner, one) for one in ordered]
    turns[last] += [functools.partial(close, one) for one in ordered]
    return [turns[i] for i in sorted(turns)]


def lay_blocks(shard_size, land, flat, first, last, origin):
    window = land.shape[1]

    def lay(number, carry):
        row = pl.multiple_of(first_row(shard_size, number) - origin, 8)
        flat[pl.ds(row, 16), :] += land[number, 0:16, :].astype(F32)
        flat[pl.ds(row + 16, window - 16), :] = land[number, 16:window, :].astype(F32)
        return carry

    lax.fori_loop(first, last, lay, 0)


def gather_kernel(
    order, shard_size, early, own_ref,
    wall_ref, gain_one_ref, gain_two_ref, tail_ref,
    land, flat, send_sem, recv_sem,
):
    order = order()
    greet(order)
    for turn in gather_turns(order, lambda owner: owner < early, own_ref, land, send_sem, recv_sem):
        for act in turn:
            act()
    flat[0:16, :] = jnp.zeros((16, 128), F32)
    lay_blocks(shard_size, land, flat, 0, early, 0)
    tail_ref[...] = flat[WO_ROW : WO_ROW + tail_ref.shape[0], :]
    for c in range(D // 128):
        lanes = slice(c * 128, (c + 1) * 128)
        gain_one_ref[:, lanes] = flat[c : c + 1, :]
        gain_two_ref[:, lanes] = flat[4 + c : 5 + c, :]
    for c in range(QW // 128):
        wall_ref[c * 128 : (c + 1) * 128, :] = flat[pl.ds(WQ_ROW + c, D, stride=12), :].T.astype(BF16)
    for first, row in ((KROW, WK_ROW), (VROW, WV_ROW)):
        pair = flat[row : row + 256, :].T.astype(BF16)
        wall_ref[first : first + H, :] = (
            nn(pair[:H], picks(256, 2, 0).astype(BF16)) + nn(pair[H:], picks(256, 2, 1).astype(BF16))
        ).astype(BF16)
    across = jnp.concatenate(
        [flat[pl.ds(WR_ROW + j, 32, stride=3), :] for j in range(3)], axis=1
    ).T.astype(BF16)
    router_t = jnp.zeros((E, D), F32)
    for part in range(16):
        router_t = router_t + nn(across[part * E : (part + 1) * E, :], picks(32, 16, part).astype(BF16))
    wall_ref[RROW:ALLW, :] = jnp.concatenate(
        [router_t, jnp.zeros((ALLW - RROW - E, D), F32)], axis=0
    ).astype(BF16)


def gather_early(shards, over, shard_size, own):
    window = own.shape[0]
    early = early_owners(shard_size, over)
    rows = (shard_size * (early - 1)) // UNIT * 16 + window
    vmem = pl.BlockSpec(memory_space=pltpu.VMEM)
    order = functools.partial(Order, shards, over, "yzx", "yzx")
    return pl.pallas_call(
        functools.partial(gather_kernel, order, shard_size, early),
        in_specs=[vmem],
        out_specs=[vmem] * 4,
        out_shape=[
            struct((ALLW, D), BF16),
            struct((1, D)),
            struct((1, D)),
            struct((rows - WO_ROW, 128)),
        ],
        scratch_shapes=[
            pltpu.VMEM((early, window, 128), BF16),
            pltpu.VMEM((rows, 128), F32),
            pltpu.SemaphoreType.DMA((shards * over,)),
            pltpu.SemaphoreType.DMA((early,)),
        ],
        compiler_params=pltpu.CompilerParams(
            collective_id=0, has_side_effects=True, vmem_limit_bytes=56 * MIB
        ),
        name="gather_early",
    )(own)


def reduce_turns(order, wanted, fetch, part, outgo, income, send_sem, recv_sem, finish):
    core = order.core
    place = order.place(core)
    slots = {}

    def copy(key, device):
        slot = slots.setdefault(key, len(slots))
        return pltpu.make_async_remote_copy(
            src_ref=outgo.at[slot],
            dst_ref=income.at[slot],
            send_sem=send_sem.at[slot],
            recv_sem=recv_sem.at[slot],
            device_id=device,
            device_id_type=MESH,
        )

    def last_axis(offsets):
        return max([i for i in range(3) if offsets[i]], default=-1)

    def sends(key, device, values):
        one = copy(key, device)
        outgo[slots[key]] = values.astype(BF16)
        one.start()

    def taken(key):
        copy(key, order.partner).wait_recv()
        return income[slots[key]].astype(F32)

    def begin(offsets):
        for kind in (1 - core, core):
            owner = order.owner(kind, offsets)
            pl.when(wanted(owner))(lambda owner=owner: fetch(owner).start())

    def to_partner(offsets):
        owner = order.owner(1 - core, offsets)

        def act():
            fetch(owner).wait()
            sends(("core", offsets), order.partner, part[owner])

        pl.when(wanted(owner))(act)

    def onward(offsets):
        owner = order.owner(core, offsets)
        axis = last_axis(offsets)

        def act():
            fetch(owner).wait()
            total = part[owner] + taken(("core", offsets))
            for later in range(2, axis, -1):
                for step in order.along(later):
                    total = total + taken((later, tuple(o + s for o, s in zip(offsets, step))))
            if axis < 0:
                finish(total)
            else:
                step = [offsets[i] if i == axis else 0 for i in range(3)]
                sends((axis, offsets), order.device(core, order.moved(place, step)), total)

        pl.when(wanted(owner))(act)

    def close(offsets):
        def act():
            copy(("core", offsets), order.partner).wait_send()

        pl.when(wanted(order.owner(1 - core, offsets)))(act)
        axis = last_axis(offsets)
        if axis >= 0:
            def act_on():
                copy((axis, offsets), order.partner).wait_send()

            pl.when(wanted(order.owner(core, offsets)))(act_on)

    z = order.z_at.index(True)
    turns = {0: []}
    backward = sorted(order.offsets(), key=lambda one: (-one[z], [-v for v in one[::-1]]))
    for offsets in backward:
        turns[0].append(functools.partial(begin, offsets))
    for offsets in backward:
        late = order.sizes[z] - 1 - offsets[z]
        turns.setdefault(late, []).append(functools.partial(to_partner, offsets))
    for offsets in backward:
        late = order.sizes[z] - 1 - offsets[z]
        axis = last_axis(offsets)
        turns.setdefault(late + 3 - max(axis, 0), []).append(functools.partial(onward, offsets))
    turns[max(turns) + 1] = [functools.partial(close, one) for one in backward]
    return [turns[i] for i in sorted(turns)]


def in_steps(turns, steps):
    spread = [[] for _ in range(steps)]
    for number, turn in enumerate(turns):
        spread[number * steps // len(turns) if len(turns) > steps else number] += turn
    return spread


STAT = 24


def reduce_kernel(
    order, shard_size, early, flat_ref, late_ref, count_ref,
    out_ref, total_ref, gain_ref, load_ref,
    part, outgo, income, stats, part_sem, send_sem, recv_sem, stat_send, stat_recv,
):
    order = order()
    me = order.me
    many = order.many
    window = out_ref.shape[0]

    def fetch(owner):
        return pltpu.make_async_copy(
            flat_ref.at[pl.ds(first_row(shard_size, owner), window), :],
            part.at[owner],
            part_sem.at[owner],
        )

    barrier = pltpu.get_barrier_semaphore()

    def hello(j, carry):
        number = lax.rem(me + j, many)
        pl.semaphore_signal(
            barrier,
            inc=1,
            device_id=(lax.div(number, order.over), lax.rem(number, order.over)),
            device_id_type=MESH,
        )
        return carry

    lax.fori_loop(1, many, hello, 0)
    pl.semaphore_wait(barrier, many - 1)

    @pl.when(me >= early)
    def _():
        out_ref[...] = late_ref[...]

    def finish(total):
        out_ref[...] = total

    turns = reduce_turns(
        order, lambda owner: owner < early, fetch, part, outgo, income, send_sem, recv_sem, finish
    )
    for turn in turns:
        for act in turn:
            act()
    total = out_ref[...]
    begin = me * shard_size - lax.div(me * shard_size, UNIT) * UNIT
    at = (
        lax.broadcasted_iota(jnp.int32, (window, 128), 0) * 128
        + lax.broadcasted_iota(jnp.int32, (window, 128), 1)
    )
    inside = jnp.where((at >= begin) & (at < begin + shard_size), total, 0.0)
    stats[0, 0:8, :] = jnp.broadcast_to(jnp.sum(inside * inside, axis=0, keepdims=True), (8, 128))
    stats[0, 8:16, :] = total[0:8, :]
    stats[0, 16:24, :] = jnp.broadcast_to(count_ref[...], (8, 128))

    def told(j):
        number = lax.rem(me + j, many)
        return pltpu.make_async_remote_copy(
            src_ref=stats.at[0],
            dst_ref=stats.at[j],
            send_sem=stat_send.at[j],
            recv_sem=stat_recv.at[j],
            device_id=(lax.div(number, order.over), lax.rem(number, order.over)),
            device_id_type=MESH,
        )

    def tell(j, carry):
        told(j).start()
        return carry

    def hear(j, carry):
        told(j).wait()
        return carry

    lax.fori_loop(1, many, tell, 0)
    lax.fori_loop(1, many, hear, 0)
    total_ref[...] = jnp.broadcast_to(
        jnp.sum(jnp.sum(stats[:, 0:8, :], axis=0), axis=1, keepdims=True), (8, 128)
    )
    load_ref[...] = jnp.sum(stats[:, 16:24, :], axis=0)
    gain_ref[...] = stats[me, 8:16, :]


def reduce_early(shards, over, shard_size, window, flat, late, counts):
    vmem = pl.BlockSpec(memory_space=pltpu.VMEM)
    many = shards * over
    early = early_owners(shard_size, over)
    order = functools.partial(Order, shards, over, "yzx", "yzx")
    return pl.pallas_call(
        functools.partial(reduce_kernel, order, shard_size, early),
        in_specs=[pl.BlockSpec(memory_space=pl.ANY), vmem, vmem],
        out_specs=[vmem] * 4,
        out_shape=[struct((window, 128)), struct((8, 128)), struct((8, 128)), struct((8, 128))],
        scratch_shapes=[
            pltpu.VMEM((early, window, 128), F32),
            pltpu.VMEM((many, window, 128), BF16),
            pltpu.VMEM((many, window, 128), BF16),
            pltpu.VMEM((many, STAT, 128), F32),
            pltpu.SemaphoreType.DMA((early,)),
            pltpu.SemaphoreType.DMA((many,)),
            pltpu.SemaphoreType.DMA((many,)),
            pltpu.SemaphoreType.DMA((many,)),
            pltpu.SemaphoreType.DMA((many,)),
        ],
        compiler_params=pltpu.CompilerParams(
            collective_id=1, has_side_effects=True, vmem_limit_bytes=56 * MIB
        ),
        name="reduce_early",
    )(flat, late, counts)


def per_device(
    shards, over, tokens, grad_out, routes, segments, params, first_moment, second_moment, ema_weights
):
    shard_size = params.shape[0]
    window = window_rows(shard_size, shards * over)
    late_rows = (shard_size * (shards * over - 1)) // UNIT * 16 + window - WO_ROW
    me = lax.axis_index("dp") * over + lax.axis_index("fsdp")
    begin = lax.rem(me * shard_size, UNIT)
    own = lax.dynamic_update_slice(
        jnp.zeros((window * 128,), BF16), params.astype(BF16), (begin,)
    ).reshape(window, 128)
    wall, gain_one, gain_two, tail = gather_early(shards, over, shard_size, own)
    routes_t = routes.T
    start = document_starts(segments)
    queries, attended, gates, lse, kv, kvt, wo, w1, w2 = head_forward(
        shards, over, shard_size, tokens, gain_one, wall, routes_t, start, own, tail
    )
    output, dres, datt, delta, dlogits, late, dgain_two = middle(
        late_rows, tokens, grad_out, gain_two, wo, w1, w2, routes_t, gates, attended
    )
    input_grad, flat, late_sum = head_backward(
        shards, over, shard_size, window, tokens, gain_one, wall, routes_t, start, queries, datt, lse,
        delta, kv, kvt, dlogits, dres, dgain_two, late,
    )
    counts = jnp.sum(
        (routes[:, :, None] == jnp.arange(128, dtype=jnp.int32)).astype(F32), axis=(0, 1)
    ).reshape(1, 128)
    reduced, square_sum, gain_grads, loads = reduce_early(
        shards, over, shard_size, window, flat, late_sum, counts
    )
    grad_shard = lax.dynamic_slice(reduced.reshape(-1), (begin,), (shard_size,))
    total_tokens = tokens.shape[0] * shards * over
    expert_load = loads[0, :E] * (E / (total_tokens * TOPK))
    grad_norm = jnp.sqrt(square_sum[0, 0])
    clipped = grad_shard * (CLIP_LIMIT / jnp.maximum(grad_norm, CLIP_LIMIT))
    new_first = BETA_FIRST * first_moment + (1.0 - BETA_FIRST) * clipped
    new_second = BETA_SECOND * second_moment + (1.0 - BETA_SECOND) * clipped * clipped
    first_hat = new_first / (1.0 - BETA_FIRST**STEP)
    second_hat = new_second / (1.0 - BETA_SECOND**STEP)
    new_params = params * (1.0 - LEARN_RATE * DECAY_RATE) - LEARN_RATE * first_hat / (
        jnp.sqrt(second_hat) + ADAM_EPS
    )
    new_ema = EMA_KEEP * ema_weights + (1.0 - EMA_KEEP) * new_params
    return (
        output,
        input_grad,
        expert_load,
        grad_norm.reshape(1),
        new_params,
        new_first,
        new_second,
        new_ema,
        gain_grads.reshape(2, D),
    )


def solution(mesh):
    row = P(("dp", "fsdp"), None)
    flat = P(("dp", "fsdp"))
    return jax.shard_map(
        functools.partial(per_device, mesh.shape["dp"], mesh.shape["fsdp"]),
        mesh=mesh,
        in_specs=(row, row, row, row, flat, flat, flat, flat),
        out_specs=(row, row, P(), P(), flat, flat, flat, flat, P()),
        check_vma=False,
    )
```

```python
import functools
import itertools

import jax
import jax.numpy as jnp
from jax import lax
from jax.experimental import pallas as pl
from jax.experimental.pallas import tpu as pltpu
from jax.sharding import PartitionSpec as P

D = 512
E = 24
TOPK = 8
H = 64
FF = 2048
STEP = 10

NORM_EPS = 1e-06
CLIP_LIMIT = 1.0
BETA_FIRST = 0.9
BETA_SECOND = 0.95
LEARN_RATE = 0.1
DECAY_RATE = 0.1
ADAM_EPS = 1e-08
EMA_KEEP = 0.9
NEG_LARGE = -1e30

QW = E * H
KROW = QW
VROW = QW + H
RROW = QW + 2 * H
ALLW = 1696
LEN = 1024
TB = 256
NB = LEN // TB
FC = 512
MIB = 1 << 20

WR_ROW = 8
WK_ROW = 104
WV_ROW = 360
WQ_ROW = 616
WO_ROW = 6760
W1_ROW = 12904
W2_ROW = 21096
ALL_ROWS = 29288
UNIT = 16 * 128
MESH = pl.DeviceIdType.MESH

F32 = jnp.float32
BF16 = jnp.bfloat16


def nn(a, b):
    return lax.dot_general(a, b, (((1,), (0,)), ((), ())), preferred_element_type=F32)


def nt(a, b):
    return lax.dot_general(a, b, (((1,), (1,)), ((), ())), preferred_element_type=F32)


def tn(a, b):
    return lax.dot_general(a, b, (((0,), (0,)), ((), ())), preferred_element_type=F32)


def rms_scale(values):
    return lax.rsqrt(jnp.mean(values * values, axis=-1, keepdims=True) + NORM_EPS)


def slot_of(routes, k, rows):
    return jnp.broadcast_to(routes[k : k + 1, :], (rows, routes.shape[1]))


def pick_heads(route_ref, source_ref, k):
    route = jnp.broadcast_to(route_ref[k : k + 1, :], (H, route_ref.shape[1]))
    taken = source_ref[0:H, :]
    for e in range(1, E):
        taken = jnp.where(route == e, source_ref[e * H : (e + 1) * H, :], taken)
    return taken


def place_heads(route_ref, source_ref, e):
    total = jnp.zeros((H, route_ref.shape[1]), F32)
    for k in range(TOPK):
        route = jnp.broadcast_to(route_ref[k : k + 1, :], (H, route_ref.shape[1]))
        total = jnp.where(route == e, source_ref[k * H : (k + 1) * H, :], total)
    return total


def key_mask(first_key, first_query, rows, start_row):
    keys = lax.broadcasted_iota(jnp.int32, (rows, TB), 0) + first_key
    queries = lax.broadcasted_iota(jnp.int32, (rows, TB), 1) + first_query
    return (keys <= queries) & (keys >= start_row)


def head_forward_kernel(
    mesh, shard_size, early, steps, x_ref, route_ref, segment_ref, own_ref,
    q_ref, att_ref, gate_ref, lse_ref, kv_ref, kvt_ref, start_ref,
    wall_ref, gain_ref, gain_two_ref, wo_ref, w1_ref, w2_ref, count_ref,
    all_scr, k_scr, vt_scr, count_scr, land, flat, send_sem, recv_sem,
):
    step = pl.program_id(0)
    place = lax.rem(step, NB)
    here = pl.multiple_of(place * TB, TB)
    mesh = mesh()

    @pl.when(step == 0)
    def _():
        mesh.greet_near()
        for _, action in gather_events(
            mesh, lambda owner: owner < early, own_ref, land, send_sem, recv_sem
        ):
            action()
        flat[0:16, :] = jnp.zeros((16, 128), F32)
        lay_blocks(shard_size, land, flat, 0, early)
        early_matrices(flat, wall_ref, gain_ref, gain_two_ref)
        count_scr[...] = jnp.zeros_like(count_scr)

    spread = at_polls(
        gather_events(mesh, lambda owner: owner >= early, own_ref, land, send_sem, recv_sem), 2 * steps
    )
    poll(step, 0, spread)
    row = segment_ref[pl.ds(lax.div(step, NB), 1), :]
    segments = segment_ref[pl.ds(lax.div(step, NB), 1), pl.ds(here, TB)]
    start = jnp.zeros((1, TB), jnp.int32)
    for number in range(1, 4):
        below = jnp.sum((row < number).astype(jnp.int32), axis=1, keepdims=True)
        start = jnp.where(segments == number, below, start)
    start_ref[...] = start
    x = x_ref[...].astype(F32)
    normed = (x * rms_scale(x) * gain_ref[...]).astype(BF16)
    all_scr[...] = nt(wall_ref[...], normed)
    kt = all_scr[KROW : KROW + H, :]
    vt = all_scr[VROW : VROW + H, :]
    logits = all_scr[RROW : RROW + E, :]
    kvt = jnp.concatenate([kt, vt], axis=0)
    kv = kvt.T.astype(BF16)
    kv_ref[...] = kv
    kvt_ref[...] = kvt.astype(BF16)
    k_scr[pl.ds(here, TB), :] = kv[:, :H]
    vt_scr[:, pl.ds(here, TB)] = vt.astype(BF16)
    routes = route_ref[...]
    experts = lax.broadcasted_iota(jnp.int32, (E, TB), 0)
    chosen = []
    counts = count_scr[...]
    for k in range(TOPK):
        named = slot_of(routes, k, E) == experts
        chosen.append(jnp.sum(jnp.where(named, logits, 0.0), axis=0, keepdims=True))
        counts = counts + named.astype(F32)
    count_scr[...] = counts
    chosen = jnp.concatenate(chosen, axis=0)
    raised = jnp.exp(chosen - jnp.max(chosen, axis=0, keepdims=True))
    gate_ref[...] = raised / jnp.sum(raised, axis=0, keepdims=True)
    for k in range(TOPK):
        query = pick_heads(route_ref, all_scr, k).astype(BF16)
        q_ref[k * H : (k + 1) * H, :] = query * jnp.asarray(H ** (-0.5), BF16)
    poll(step, 1, spread)

    def attend(blocks):
        rows = blocks * TB
        first_key = pl.multiple_of((place - (blocks - 1)) * TB, TB)
        mask = key_mask(first_key, here, rows, start)
        keys = k_scr[pl.ds(first_key, rows), :]
        values = vt_scr[:, pl.ds(first_key, rows)]
        for k in range(TOPK):
            scores = jnp.where(mask, nn(keys, q_ref[k * H : (k + 1) * H, :]), NEG_LARGE)
            top = jnp.max(scores, axis=0, keepdims=True)
            raised = jnp.exp(scores - top)
            total = jnp.sum(raised, axis=0, keepdims=True)
            probs = (raised * (1.0 / total)).astype(BF16)
            att_ref[k * H : (k + 1) * H, :] = nn(values, probs)
            lse_ref[k : k + 1, :] = top + jnp.log(total)

    most = min(3, NB)
    for blocks in range(1, most + 1):

        @pl.when(place == blocks - 1 if blocks < most else place >= blocks - 1)
        def _(blocks=blocks):
            attend(blocks)

    @pl.when(step == steps - 1)
    def _():
        lay_blocks(shard_size, land, flat, early, mesh.many)
        late_matrices(flat, wo_ref, w1_ref, w2_ref)
        held = jnp.sum(count_scr[...], axis=1, keepdims=True)
        count_ref[...] = jnp.broadcast_to(held, (E, 128))


def picks(rows, stride, first):
    at = lax.broadcasted_iota(jnp.int32, (rows, D), 1)
    row = lax.broadcasted_iota(jnp.int32, (rows, D), 0)
    return (at == row * stride + first).astype(F32)


def exact(product, a, b):
    return lax.dot_general(
        a, b, (product, ((), ())), precision=lax.Precision.HIGHEST, preferred_element_type=F32
    )


def gelu_parts(v):
    size = jnp.abs(v) * 0.7071067811865476
    bell = jnp.exp(-(size * size))
    t = 1.0 / (1.0 + 0.3275911 * size)
    series = t * (
        0.254829592
        + t * (-0.284496736 + t * (1.421413741 + t * (-1.453152027 + t * 1.061405429)))
    )
    tail = 0.5 * series * bell
    cdf = jnp.where(v < 0.0, tail, 1.0 - tail)
    return cdf, bell * 0.3989422804014327


def middle_kernel(
    x_ref, dy_ref, gain_ref, wo_ref, w1_ref, w2_ref, route_ref, gate_ref, att_ref,
    out_ref, dres_ref, datt_ref, delta_ref, dlogit_ref, flat_ref, dgain_ref,
    slot_scr, head_scr, mix_scr, dwo_ref, dw1_ref, dw2t_ref, rows_scr, row_sem,
):
    step = pl.program_id(0)

    @pl.when(step == 0)
    def _():
        dwo_ref[...] = jnp.zeros_like(dwo_ref)
        dw1_ref[...] = jnp.zeros_like(dw1_ref)
        dw2t_ref[...] = jnp.zeros_like(dw2t_ref)
        dgain_ref[...] = jnp.zeros_like(dgain_ref)

    routes = route_ref[...]
    tokens = routes.shape[1]
    gates = gate_ref[...]
    for k in range(TOPK):
        slot_scr[k * H : (k + 1) * H, :] = gates[k : k + 1, :] * att_ref[k * H : (k + 1) * H, :]
    for e in range(E):
        mix_scr[e * H : (e + 1) * H, :] = place_heads(route_ref, slot_scr, e).astype(BF16)
    x = x_ref[...].astype(F32)
    dy = dy_ref[...]
    mixed = mix_scr[...]
    residual = x + tn(mixed, wo_ref[...])
    scale = rms_scale(residual)
    gain = gain_ref[...]
    second = (residual * scale * gain).astype(BF16)
    second_t = second.T
    dy_t = dy.T
    out = residual
    dsecond = jnp.zeros((tokens, D), F32)
    for c in range(0, FF, FC):
        up = w1_ref[:, c : c + FC]
        down = w2_ref[c : c + FC, :]
        pre = nn(second, up)
        cdf, density = gelu_parts(pre)
        hidden = (pre * cdf).astype(BF16)
        dpre = (nt(dy, down) * (cdf + pre * density)).astype(BF16)
        out = out + nn(hidden, down)
        dsecond = dsecond + nt(dpre, up)
        dw2t_ref[:, c : c + FC] += nn(dy_t, hidden)
        dw1_ref[:, c : c + FC] += nn(second_t, dpre)
    out_ref[...] = out.astype(BF16)
    dgain_ref[...] += jnp.sum(dsecond * residual * scale, axis=0, keepdims=True)
    weighted = gain * dsecond
    dres = (
        dy.astype(F32)
        + scale * weighted
        - residual * (scale * scale * scale) * jnp.mean(weighted * residual, axis=-1, keepdims=True)
    )
    dres_ref[...] = dres
    branch = dres.astype(BF16)
    dwo_ref[...] += nn(mixed, branch)
    head_scr[...] = nt(wo_ref[...], branch).astype(BF16).astype(F32)
    dgates = []
    for k in range(TOPK):
        rows = slice(k * H, (k + 1) * H)
        dslot = pick_heads(route_ref, head_scr, k)
        attended = att_ref[rows, :]
        dgates.append(jnp.sum(dslot * attended, axis=0, keepdims=True))
        datt = (gates[k : k + 1, :] * dslot).astype(BF16)
        datt_ref[rows, :] = datt
        delta_ref[k : k + 1, :] = jnp.sum(datt.astype(F32) * attended, axis=0, keepdims=True)
    dgate = jnp.concatenate(dgates, axis=0)
    dchosen = gates * (dgate - jnp.sum(gates * dgate, axis=0, keepdims=True))
    experts = lax.broadcasted_iota(jnp.int32, (E, tokens), 0)
    dlogits = jnp.zeros((E, tokens), F32)
    for k in range(TOPK):
        dlogits = jnp.where(
            slot_of(routes, k, E) == experts,
            jnp.broadcast_to(dchosen[k : k + 1, :], (E, tokens)),
            dlogits,
        )
    dlogit_ref[...] = dlogits

    @pl.when(step == pl.num_programs(0) - 1)
    def _():
        pieces = []
        for c in range(D // 128):
            lanes = slice(c * 128, (c + 1) * 128)
            rows_scr[pl.ds(c, QW, stride=4), :] = dwo_ref[:, lanes]
        pieces.append((0, QW * 4))
        first = QW * 4
        for c in range(FF // 128):
            rows_scr[pl.ds(first + c, D, stride=16), :] = dw1_ref[:, c * 128 : (c + 1) * 128]
        pieces.append((first, D * 16))
        first = first + D * 16
        for c in range(D // 128):
            rows_scr[pl.ds(first + c, FF, stride=4), :] = dw2t_ref[c * 128 : (c + 1) * 128, :].T
        pieces.append((first, FF * 4))
        copies = []
        for number, (begin, count) in enumerate(pieces):
            copy = pltpu.make_async_copy(
                rows_scr.at[pl.ds(begin, count), :],
                flat_ref.at[pl.ds(begin, count), :],
                row_sem.at[number],
            )
            copy.start()
            copies.append(copy)
        for copy in copies:
            copy.wait()


def head_backward_kernel(
    mesh, shard_size, early, steps, x_ref, gain_ref, wall_ref, route_ref, start_ref, q_ref, datt_ref,
    lse_ref, delta_ref, kv_ref, kvt_ref, dlogit_ref, dres_ref, dgain_two_ref, count_ref, late_ref,
    dx_ref, out_ref, total_ref, sum_ref,
    dk_scr, dv_scr, dq_scr, dall_scr, dwall_ref, dgain_ref, rows_scr,
    part, outgo, income, stats, part_sem, send_sem, recv_sem, stat_send, stat_recv,
):
    step = pl.program_id(0)
    place = NB - 1 - lax.rem(step, NB)
    mesh = mesh()
    many = mesh.many
    window = out_ref.shape[0]
    extra = rows_scr.shape[0] - WO_ROW

    def fetch(number):
        row = pl.multiple_of(first_row(shard_size, number + early) - WO_ROW, 8)
        return pltpu.make_async_copy(
            late_ref.at[pl.ds(row, window), :], part.at[number], part_sem.at[number]
        )

    rest = pltpu.make_async_copy(
        late_ref.at[pl.ds(0, extra), :], rows_scr.at[pl.ds(WO_ROW, extra), :], part_sem.at[many - early]
    )

    @pl.when(step == 0)
    def _():
        rest.start()

        def begin(number, carry):
            fetch(number).start()
            return carry

        lax.fori_loop(0, many - early, begin, 0)
        mesh.greet_all()

    def late_block(owner):
        fetch(owner - early).wait()
        return part[owner - early]

    def finish(total):
        out_ref[...] = total

    spread = at_polls(
        reduce_events(
            mesh, lambda owner: owner >= early, late_block, outgo, income, send_sem, recv_sem, finish
        ),
        2 * steps,
    )
    poll(step, 0, spread)
    here = pl.multiple_of(place * TB, TB)

    @pl.when(step == 0)
    def _():
        dwall_ref[...] = jnp.zeros_like(dwall_ref)
        dgain_ref[...] = jnp.zeros_like(dgain_ref)

    @pl.when(lax.rem(step, NB) == 0)
    def _():
        dk_scr[...] = jnp.zeros_like(dk_scr)
        dv_scr[...] = jnp.zeros_like(dv_scr)

    def attend(blocks):
        rows = blocks * TB
        first_key = pl.multiple_of((place - (blocks - 1)) * TB, TB)
        mask = key_mask(first_key, here, rows, start_ref[...])
        keys = kv_ref[pl.ds(first_key, rows), :H]
        values = kv_ref[pl.ds(first_key, rows), H:]
        keys_t = kvt_ref[:H, pl.ds(first_key, rows)]
        dk = jnp.zeros((rows, H), F32)
        dv = jnp.zeros((rows, H), F32)
        for k in range(TOPK):
            part = slice(k * H, (k + 1) * H)
            query = q_ref[part, :]
            datt = datt_ref[part, :]
            scores = jnp.where(mask, nn(keys, query), NEG_LARGE)
            probs = jnp.exp(scores - lse_ref[k : k + 1, :])
            dscore = (probs * (nn(values, datt) - delta_ref[k : k + 1, :])).astype(BF16)
            dv = dv + nt(probs.astype(BF16), datt)
            dk = dk + nt(dscore, query)
            dq_scr[part, :] = nn(keys_t, dscore) * (H ** (-0.5))
        dk_scr[pl.ds(first_key, rows), :] += dk
        dv_scr[pl.ds(first_key, rows), :] += dv

    most = min(3, NB)
    for blocks in range(1, most + 1):

        @pl.when(place == blocks - 1 if blocks < most else place >= blocks - 1)
        def _():
            attend(blocks)

    poll(step, 1, spread)
    for e in range(E):
        dall_scr[e * H : (e + 1) * H, :] = place_heads(route_ref, dq_scr, e).astype(BF16)
    dkv = jnp.concatenate([dk_scr[pl.ds(here, TB), :], dv_scr[pl.ds(here, TB), :]], axis=1)
    dall_scr[KROW : KROW + 2 * H, :] = dkv.T.astype(BF16)
    dall_scr[RROW : RROW + 32, :] = jnp.concatenate(
        [dlogit_ref[...], jnp.zeros((32 - E, TB), F32)], axis=0
    ).astype(BF16)
    x = x_ref[...].astype(F32)
    scale = rms_scale(x)
    gain = gain_ref[...]
    normed = (x * scale * gain).astype(BF16)
    dall = dall_scr[...]
    dwall_ref[...] += nn(dall, normed)
    dnormed = tn(dall, wall_ref[...])
    dgain_ref[...] += jnp.sum(dnormed * x * scale, axis=0, keepdims=True)
    weighted = gain * dnormed
    dx_ref[...] = (
        dres_ref[...]
        + scale * weighted
        - x * (scale * scale * scale) * jnp.mean(weighted * x, axis=-1, keepdims=True)
    )

    @pl.when(step == pl.num_programs(0) - 1)
    def _():
        for c in range(D // 128):
            lanes = slice(c * 128, (c + 1) * 128)
            rows_scr[c : c + 1, :] = dgain_ref[:, lanes]
            rows_scr[4 + c : 5 + c, :] = dgain_two_ref[:, lanes]
        router_t = dwall_ref[RROW : RROW + E, :]
        across = jnp.concatenate(
            [exact(((1,), (1,)), router_t, picks(32, 16, b)) for b in range(16)], axis=0
        ).T
        for j in range(3):
            rows_scr[pl.ds(WR_ROW + j, 32, stride=3), :] = across[:, j * 128 : (j + 1) * 128]
        for first, row in ((KROW, WK_ROW), (VROW, WV_ROW)):
            part = dwall_ref[first : first + H, :]
            rows_scr[row : row + 256, :] = jnp.concatenate(
                [exact(((1,), (1,)), picks(256, 2, b), part) for b in range(2)], axis=1
            )
        for c in range(QW // 128):
            rows_scr[pl.ds(WQ_ROW + c, D, stride=12), :] = dwall_ref[c * 128 : (c + 1) * 128, :].T
        rest.wait()
        for _, action in reduce_events(
            mesh, lambda owner: owner < early,
            lambda owner: rows_scr[pl.ds(first_row(shard_size, owner), window), :],
            outgo, income, send_sem, recv_sem, finish,
        ):
            action()
        total = out_ref[...]
        begin = mesh.me * shard_size - lax.div(mesh.me * shard_size, UNIT) * UNIT
        at = (
            lax.broadcasted_iota(jnp.int32, (window, 128), 0) * 128
            + lax.broadcasted_iota(jnp.int32, (window, 128), 1)
        )
        inside = jnp.where((at >= begin) & (at < begin + shard_size), total, 0.0)
        stats[0, 0:8, :] = jnp.broadcast_to(jnp.sum(inside * inside, axis=0, keepdims=True), (8, 128))
        stats[0, 8:16, :] = total[0:8, :]
        stats[0, 16 : 16 + E, :] = count_ref[...]

        def told(j):
            return pltpu.make_async_remote_copy(
                src_ref=stats.at[0],
                dst_ref=stats.at[j],
                send_sem=stat_send.at[j],
                recv_sem=stat_recv.at[j],
                device_id=mesh.nth(lax.rem(mesh.me + j, many)),
                device_id_type=MESH,
            )

        def tell(j, carry):
            told(j).start()
            return carry

        def hear(j, carry):
            told(j).wait()
            return carry

        lax.fori_loop(1, many, tell, 0)
        lax.fori_loop(1, many, hear, 0)
        total_ref[...] = jnp.broadcast_to(
            jnp.sum(jnp.sum(stats[:, 0:8, :], axis=0), axis=1, keepdims=True), (8, 128)
        )
        sum_ref[0:8, :] = stats[mesh.me, 8:16, :]
        sum_ref[8 : 8 + E, :] = jnp.sum(stats[:, 16 : 16 + E, :], axis=0)


def whole(shape):
    return pl.BlockSpec(shape, lambda *_: (0,) * len(shape), pipeline_mode=pl.Buffered(1))


def kept(shape):
    return pl.BlockSpec(shape, lambda *_: (0,) * len(shape))


def struct(shape, kind=F32):
    return jax.ShapeDtypeStruct(shape, kind)


def params_for(mib):
    return pltpu.CompilerParams(vmem_limit_bytes=mib * MIB)


def head_forward(shards, over, shard_size, tokens, routes_t, segments, own):
    count = tokens.shape[0]
    steps = count // TB
    many = shards * over
    window = own.shape[0]
    early = early_owners(shard_size, over)
    rows = (shard_size * (many - 1)) // UNIT * 16 + window
    mesh = functools.partial(Mesh3, shards, over)
    across = lambda rows: pl.BlockSpec((rows, TB), lambda b: (0, b))
    down = lambda columns: pl.BlockSpec((TB, columns), lambda b: (b, 0))
    return pl.pallas_call(
        functools.partial(head_forward_kernel, mesh, shard_size, early, steps),
        grid=(steps,),
        in_specs=[down(D), across(TOPK), whole(segments.shape), whole(own.shape)],
        out_specs=[
            across(TOPK * H), across(TOPK * H), across(TOPK), across(TOPK), down(2 * H), across(2 * H),
            across(1), whole((ALLW, D)), whole((1, D)), whole((1, D)),
            whole((QW, D)), whole((D, FF)), whole((FF, D)), whole((E, 128)),
        ],
        scratch_shapes=[
            pltpu.VMEM((ALLW, TB), F32),
            pltpu.VMEM((LEN, H), BF16),
            pltpu.VMEM((H, LEN), BF16),
            pltpu.VMEM((E, TB), F32),
            pltpu.VMEM((many, window, 128), BF16),
            pltpu.VMEM((rows, 128), F32),
            pltpu.SemaphoreType.DMA((many,)),
            pltpu.SemaphoreType.DMA((many,)),
        ],
        out_shape=[
            struct((TOPK * H, count), BF16),
            struct((TOPK * H, count)),
            struct((TOPK, count)),
            struct((TOPK, count)),
            struct((count, 2 * H), BF16),
            struct((2 * H, count), BF16),
            struct((1, count), jnp.int32),
            struct((ALLW, D), BF16),
            struct((1, D)),
            struct((1, D)),
            struct((QW, D), BF16),
            struct((D, FF), BF16),
            struct((FF, D), BF16),
            struct((E, 128)),
        ],
        compiler_params=pltpu.CompilerParams(
            collective_id=0, has_side_effects=True, vmem_limit_bytes=60 * MIB
        ),
        name="head_forward",
    )(tokens, routes_t, segments, own)


def middle(flat_rows, tokens, grad_out, gain, wo, w1, w2, routes_t, gates, attended):
    count = tokens.shape[0]
    steps = count // TB
    across = lambda rows: pl.BlockSpec((rows, TB), lambda b: (0, b))
    down = lambda columns: pl.BlockSpec((TB, columns), lambda b: (b, 0))
    return pl.pallas_call(
        middle_kernel,
        grid=(steps,),
        in_specs=[
            down(D), down(D), whole((1, D)), whole((QW, D)), whole((D, FF)), whole((FF, D)),
            across(TOPK), across(TOPK), across(TOPK * H),
        ],
        out_specs=[
            down(D), down(D), across(TOPK * H), across(TOPK), across(E),
            pl.BlockSpec(memory_space=pl.ANY), kept((1, D)),
        ],
        out_shape=[
            struct((count, D), BF16),
            struct((count, D)),
            struct((TOPK * H, count), BF16),
            struct((TOPK, count)),
            struct((E, count)),
            struct((flat_rows, 128)),
            struct((1, D)),
        ],
        scratch_shapes=[
            pltpu.VMEM((TOPK * H, TB), F32),
            pltpu.VMEM((QW, TB), F32),
            pltpu.VMEM((QW, TB), BF16),
            pltpu.VMEM((QW, D), F32),
            pltpu.VMEM((D, FF), F32),
            pltpu.VMEM((D, FF), F32),
            pltpu.VMEM((ALL_ROWS - WO_ROW, 128), F32),
            pltpu.SemaphoreType.DMA((3,)),
        ],
        compiler_params=params_for(56),
        name="middle",
    )(tokens, grad_out, gain, wo, w1, w2, routes_t, gates, attended)


def head_backward(
    shards, over, shard_size, window, tokens, gain, wall, routes_t, start, queries, datt, lse, delta,
    kv, kvt, dlogits, dres, dgain_two, counts, late,
):
    count = tokens.shape[0]
    steps = count // TB
    many = shards * over
    early = early_owners(shard_size, over)
    early_rows = (shard_size * (early - 1)) // UNIT * 16 + window
    mesh = functools.partial(Mesh3, shards, over)

    def place(b):
        return (b // NB) * NB + NB - 1 - b % NB

    across = lambda rows: pl.BlockSpec((rows, TB), lambda b: (0, place(b)))
    down = lambda columns: pl.BlockSpec((TB, columns), lambda b: (place(b), 0))
    return pl.pallas_call(
        functools.partial(head_backward_kernel, mesh, shard_size, early, steps),
        grid=(steps,),
        in_specs=[
            down(D), whole((1, D)), whole((ALLW, D)), across(TOPK), across(1),
            across(TOPK * H), across(TOPK * H), across(TOPK), across(TOPK),
            pl.BlockSpec((LEN, 2 * H), lambda b: (b // NB, 0)),
            pl.BlockSpec((2 * H, LEN), lambda b: (0, b // NB)),
            across(E), down(D), whole((1, D)), whole((E, 128)), pl.BlockSpec(memory_space=pl.ANY),
        ],
        out_specs=[down(D), whole((window, 128)), whole((8, 128)), whole((8 + E, 128))],
        scratch_shapes=[
            pltpu.VMEM((LEN, H), F32),
            pltpu.VMEM((LEN, H), F32),
            pltpu.VMEM((TOPK * H, TB), F32),
            pltpu.VMEM((ALLW, TB), BF16),
            pltpu.VMEM((ALLW, D), F32),
            pltpu.VMEM((1, D), F32),
            pltpu.VMEM((early_rows, 128), F32),
            pltpu.VMEM((many - early, window, 128), F32),
            pltpu.VMEM((many, window, 128), BF16),
            pltpu.VMEM((many, window, 128), BF16),
            pltpu.VMEM((many, 16 + E, 128), F32),
            pltpu.SemaphoreType.DMA((many - early + 1,)),
            pltpu.SemaphoreType.DMA((many,)),
            pltpu.SemaphoreType.DMA((many,)),
            pltpu.SemaphoreType.DMA((many,)),
            pltpu.SemaphoreType.DMA((many,)),
        ],
        out_shape=[
            struct((count, D)), struct((window, 128)), struct((8, 128)), struct((8 + E, 128))
        ],
        compiler_params=pltpu.CompilerParams(
            collective_id=1, has_side_effects=True, vmem_limit_bytes=60 * MIB
        ),
        name="head_backward",
    )(
        tokens, gain, wall, routes_t, start, queries, datt, lse, delta, kv, kvt, dlogits, dres,
        dgain_two, counts, late,
    )


class Mesh3:
    def __init__(self, shards, over):
        shard = lax.axis_index("dp")
        other = lax.axis_index("fsdp")
        self.over = over
        self.many = shards * over
        self.sizes = {"x": 2, "y": shards // 2, "z": over // 2}
        self.here = {"x": lax.rem(other, 2), "y": lax.div(shard, 2), "z": lax.div(other, 2)}
        self.core = lax.rem(shard, 2)
        self.me = shard * over + other
        self.partner = (shard + 1 - 2 * self.core, other)

    def moved(self, steps):
        return {
            axis: lax.rem(self.here[axis] + steps.get(axis, 0), self.sizes[axis]) for axis in "xyz"
        }

    def device(self, core, steps):
        at = self.moved(steps)
        return (at["y"] * 2 + core, at["z"] * 2 + at["x"])

    def number(self, core, steps):
        shard, other = self.device(core, steps)
        return shard * self.over + other

    def nth(self, number):
        return (lax.div(number, self.over), lax.rem(number, self.over))

    def greet_near(self):
        devices = [
            self.device(self.core, {axis: step})
            for axis in "xyz"
            for step in range(1, self.sizes[axis])
        ] + [self.partner]
        barrier = pltpu.get_barrier_semaphore()
        for device in devices:
            pl.semaphore_signal(barrier, inc=1, device_id=device, device_id_type=MESH)
        pl.semaphore_wait(barrier, len(devices))

    def greet_all(self):
        barrier = pltpu.get_barrier_semaphore()

        def hello(j, carry):
            device = self.nth(lax.rem(self.me + j, self.many))
            pl.semaphore_signal(barrier, inc=1, device_id=device, device_id_type=MESH)
            return carry

        lax.fori_loop(1, self.many, hello, 0)
        pl.semaphore_wait(barrier, self.many - 1)


def along_z(step):
    return {1: (0, 3), 2: (1, 5), 3: (3, 8)}.get(step, (step, 2 * step + 2))


class Kind:
    def __init__(self, mesh, core, axes):
        self.mesh = mesh
        self.core = core
        self.axes = axes
        ranges = [range(mesh.sizes[axis]) for axis in axes]
        self.offsets = list(itertools.product(*ranges))
        self.index = {one: number for number, one in enumerate(self.offsets)}

    def owner(self, offsets):
        return self.mesh.number(self.core, dict(zip(self.axes, offsets)))

    def last(self, offsets):
        return max([i for i in range(3) if offsets[i]], default=-1)

    def turn(self, offsets):
        total = 0
        for axis, step in zip(self.axes, offsets):
            if step:
                total += along_z(step)[1] if axis == "z" else 2
        return total

    def hops(self, offsets):
        for i in range(self.last(offsets) + 1, 3):
            for step in range(1, self.mesh.sizes[self.axes[i]]):
                delay = along_z(step)[0] if self.axes[i] == "z" else 0
                yield i, step, self.turn(offsets) + delay

    def ahead(self, i, step):
        return self.mesh.device(self.core, {self.axes[i]: step})


AXES = ("yzx", "zxy")


def gather_events(mesh, wanted, own_ref, land, send_sem, recv_sem):
    events = []
    many = mesh.many
    kinds = [Kind(mesh, core, AXES[core]) for core in range(2)]
    end = max(kind.turn(one) for kind in kinds for one in kind.offsets) + 2

    def copy(owner, device, slot):
        return pltpu.make_async_remote_copy(
            src_ref=land.at[owner],
            dst_ref=land.at[owner],
            send_sem=send_sem.at[slot],
            recv_sem=recv_sem.at[owner],
            device_id=device,
            device_id_type=MESH,
        )

    def event(turn, condition, action):
        events.append((turn, lambda: pl.when(condition)(action)))

    for kind in kinds:
        slots = itertools.count()
        for offsets in kind.offsets:
            owner = kind.owner(offsets)
            ours = (mesh.core == kind.core) & wanted(owner)
            theirs = (mesh.core != kind.core) & wanted(owner)
            slot = next(slots)

            def come(owner=owner, offsets=offsets, slot=slot):
                if any(offsets):
                    copy(owner, mesh.partner, slot).wait_recv()
                else:
                    land[owner] = own_ref[...]
                copy(owner, mesh.partner, slot).start()

            def across(owner=owner, slot=slot):
                copy(owner, mesh.partner, slot).wait_recv()

            def done(owner=owner, slot=slot):
                copy(owner, mesh.partner, slot).wait_send()

            event(kind.turn(offsets), ours, come)
            event(end, theirs, across)
            event(end, ours, done)
            for i, step, turn in kind.hops(offsets):
                slot = next(slots)
                device = kind.ahead(i, step)

                def send(owner=owner, device=device, slot=slot):
                    copy(owner, device, slot).start()

                def sent(owner=owner, device=device, slot=slot):
                    copy(owner, device, slot).wait_send()

                event(turn, ours, send)
                event(end, ours, sent)
    return sorted(events, key=lambda one: one[0])


def reduce_events(mesh, wanted, load, outgo, income, send_sem, recv_sem, finish):
    events = []
    half = mesh.many // 2
    kinds = [Kind(mesh, core, AXES[core]) for core in range(2)]
    end = max(kind.turn(one) for kind in kinds for one in kind.offsets) + 2

    def copy(slot, device):
        return pltpu.make_async_remote_copy(
            src_ref=outgo.at[slot],
            dst_ref=income.at[slot],
            send_sem=send_sem.at[slot],
            recv_sem=recv_sem.at[slot],
            device_id=device,
            device_id_type=MESH,
        )

    def event(turn, condition, action):
        events.append((turn, lambda: pl.when(condition)(action)))

    def sends(slot, device, values):
        outgo[slot] = values.astype(BF16)
        copy(slot, device).start()

    def taken(slot):
        copy(slot, mesh.partner).wait_recv()
        return income[slot].astype(F32)

    for kind in kinds:
        slots = {}
        for offsets in kind.offsets:
            if any(offsets):
                slots[offsets] = half + len(slots)
        for offsets in kind.offsets:
            owner = kind.owner(offsets)
            ours = (mesh.core == kind.core) & wanted(owner)
            theirs = (mesh.core != kind.core) & wanted(owner)
            number = kind.index[offsets]
            axis = kind.last(offsets)
            turn = end - kind.turn(offsets)

            def hand(owner=owner, number=number):
                sends(number, mesh.partner, load(owner))

            def handed(number=number):
                copy(number, mesh.partner).wait_send()

            def onward(owner=owner, offsets=offsets, number=number, axis=axis, kind=kind, slots=slots):
                total = load(owner) + taken(number)
                for i, step, _ in kind.hops(offsets):
                    longer = tuple(step if j == i else o for j, o in enumerate(offsets))
                    total = total + taken(slots[longer])
                if axis < 0:
                    finish(total)
                else:
                    sends(slots[offsets], kind.ahead(axis, offsets[axis]), total)

            event(turn - 2, theirs, hand)
            event(end + 1, theirs, handed)
            event(turn, ours, onward)
            if axis >= 0:

                def passed(slot=slots[offsets]):
                    copy(slot, mesh.partner).wait_send()

                event(end + 1, ours, passed)
    return sorted(events, key=lambda one: one[0])


def at_polls(events, polls):
    last = events[-1][0]
    spread = [[] for _ in range(polls)]
    for turn, action in events:
        spread[turn if last < polls else turn * (polls - 1) // last].append(action)
    return spread


def poll(step, half, spread):
    for number in range(len(spread) // 2):
        actions = spread[2 * number + half]
        if actions:

            @pl.when(step == number)
            def _(actions=actions):
                for action in actions:
                    action()


def window_rows(shard_size, many):
    units = [(shard_size * d) // UNIT for d in range(many + 1)]
    return 16 * (max(b - a for a, b in zip(units, units[1:])) + 1)


def first_row(shard_size, number):
    return pl.multiple_of(lax.div(number * shard_size, UNIT) * 16, 16)


def early_owners(shard_size, over):
    group = shard_size * over
    return -(-(WO_ROW * 128) // group) * over


def lay_blocks(shard_size, land, flat, first, last):
    window = land.shape[1]

    def lay(number, carry):
        row = first_row(shard_size, number)
        flat[pl.ds(row, 16), :] += land[number, 0:16, :].astype(F32)
        flat[pl.ds(row + 16, window - 16), :] = land[number, 16:window, :].astype(F32)
        return carry

    lax.fori_loop(first, last, lay, 0)


def early_matrices(flat, wall_ref, gain_one_ref, gain_two_ref):
    for c in range(D // 128):
        lanes = slice(c * 128, (c + 1) * 128)
        gain_one_ref[:, lanes] = flat[c : c + 1, :]
        gain_two_ref[:, lanes] = flat[4 + c : 5 + c, :]
    for c in range(QW // 128):
        wall_ref[c * 128 : (c + 1) * 128, :] = flat[pl.ds(WQ_ROW + c, D, stride=12), :].T.astype(BF16)
    for first, row in ((KROW, WK_ROW), (VROW, WV_ROW)):
        pair = flat[row : row + 256, :].T.astype(BF16)
        wall_ref[first : first + H, :] = (
            nn(pair[:H], picks(256, 2, 0).astype(BF16)) + nn(pair[H:], picks(256, 2, 1).astype(BF16))
        ).astype(BF16)
    across = jnp.concatenate(
        [flat[pl.ds(WR_ROW + j, 32, stride=3), :] for j in range(3)], axis=1
    ).T.astype(BF16)
    router_t = jnp.zeros((E, D), F32)
    for part in range(16):
        router_t = router_t + nn(across[part * E : (part + 1) * E, :], picks(32, 16, part).astype(BF16))
    wall_ref[RROW:ALLW, :] = jnp.concatenate(
        [router_t, jnp.zeros((ALLW - RROW - E, D), F32)], axis=0
    ).astype(BF16)


def late_matrices(flat, wo_ref, w1_ref, w2_ref):
    for c in range(D // 128):
        lanes = slice(c * 128, (c + 1) * 128)
        wo_ref[:, lanes] = flat[pl.ds(WO_ROW + c, QW, stride=4), :].astype(BF16)
        w2_ref[:, lanes] = flat[pl.ds(W2_ROW + c, FF, stride=4), :].astype(BF16)
    for c in range(FF // 128):
        w1_ref[:, c * 128 : (c + 1) * 128] = flat[pl.ds(W1_ROW + c, D, stride=16), :].astype(BF16)


def per_device(
    shards, over, tokens, grad_out, routes, segments, params, first_moment, second_moment, ema_weights
):
    shard_size = params.shape[0]
    window = window_rows(shard_size, shards * over)
    late_rows = (shard_size * (shards * over - 1)) // UNIT * 16 + window - WO_ROW
    me = lax.axis_index("dp") * over + lax.axis_index("fsdp")
    begin = lax.rem(me * shard_size, UNIT)
    own = lax.dynamic_slice(
        jnp.pad(params.astype(BF16), (UNIT, window * 128 - shard_size)), (UNIT - begin,), (window * 128,)
    ).reshape(window, 128)
    routes_t = routes.T
    (
        queries, attended, gates, lse, kv, kvt, start, wall, gain_one, gain_two, wo, w1, w2, counts
    ) = head_forward(shards, over, shard_size, tokens, routes_t, segments, own)
    output, dres, datt, delta, dlogits, late, dgain_two = middle(
        late_rows, tokens, grad_out, gain_two, wo, w1, w2, routes_t, gates, attended
    )
    input_grad, reduced, square_sum, sums = head_backward(
        shards, over, shard_size, window, tokens, gain_one, wall, routes_t, start, queries, datt, lse,
        delta, kv, kvt, dlogits, dres, dgain_two, counts, late,
    )
    grad_shard = lax.dynamic_slice(reduced.reshape(-1), (begin,), (shard_size,))
    total_tokens = tokens.shape[0] * shards * over
    expert_load = sums[8:, 0] * (E / (total_tokens * TOPK))
    grad_norm = jnp.sqrt(square_sum[0, 0])
    clipped = grad_shard * (CLIP_LIMIT / jnp.maximum(grad_norm, CLIP_LIMIT))
    new_first = BETA_FIRST * first_moment + (1.0 - BETA_FIRST) * clipped
    new_second = BETA_SECOND * second_moment + (1.0 - BETA_SECOND) * clipped * clipped
    first_hat = new_first / (1.0 - BETA_FIRST**STEP)
    second_hat = new_second / (1.0 - BETA_SECOND**STEP)
    new_params = params * (1.0 - LEARN_RATE * DECAY_RATE) - LEARN_RATE * first_hat / (
        jnp.sqrt(second_hat) + ADAM_EPS
    )
    new_ema = EMA_KEEP * ema_weights + (1.0 - EMA_KEEP) * new_params
    return (
        output,
        input_grad,
        expert_load,
        grad_norm.reshape(1),
        new_params,
        new_first,
        new_second,
        new_ema,
        sums[:8].reshape(2, D),
    )


def solution(mesh):
    row = P(("dp", "fsdp"), None)
    flat = P(("dp", "fsdp"))
    return jax.shard_map(
        functools.partial(per_device, mesh.shape["dp"], mesh.shape["fsdp"]),
        mesh=mesh,
        in_specs=(row, row, row, row, flat, flat, flat, flat),
        out_specs=(row, row, P(), P(), flat, flat, flat, flat, P()),
        check_vma=False,
    )
```

```python
import functools
import itertools

import jax
import jax.numpy as jnp
from jax import lax
from jax.experimental import pallas as pl
from jax.experimental.pallas import tpu as pltpu
from jax.sharding import PartitionSpec as P

D = 512
E = 24
TOPK = 8
H = 64
FF = 2048
STEP = 10

NORM_EPS = 1e-06
CLIP_LIMIT = 1.0
BETA_FIRST = 0.9
BETA_SECOND = 0.95
LEARN_RATE = 0.1
DECAY_RATE = 0.1
ADAM_EPS = 1e-08
EMA_KEEP = 0.9
NEG_LARGE = -1e30

QW = E * H
KROW = QW
VROW = QW + H
RROW = QW + 2 * H
ALLW = 1696
LEN = 1024
TB = 256
NB = LEN // TB
FC = 512
MIB = 1 << 20

WR_ROW = 8
WK_ROW = 104
WV_ROW = 360
WQ_ROW = 616
WO_ROW = 6760
W1_ROW = 12904
W2_ROW = 21096
ALL_ROWS = 29288
UNIT = 16 * 128
MESH = pl.DeviceIdType.MESH

F32 = jnp.float32
BF16 = jnp.bfloat16


def nn(a, b):
    return lax.dot_general(a, b, (((1,), (0,)), ((), ())), preferred_element_type=F32)


def nt(a, b):
    return lax.dot_general(a, b, (((1,), (1,)), ((), ())), preferred_element_type=F32)


def tn(a, b):
    return lax.dot_general(a, b, (((0,), (0,)), ((), ())), preferred_element_type=F32)


def rms_scale(values):
    return lax.rsqrt(jnp.mean(values * values, axis=-1, keepdims=True) + NORM_EPS)


def slot_of(routes, k, rows):
    return jnp.broadcast_to(routes[k : k + 1, :], (rows, routes.shape[1]))


def pick_heads(route_ref, source_ref, k):
    route = jnp.broadcast_to(route_ref[k : k + 1, :], (H, route_ref.shape[1]))
    taken = source_ref[0:H, :]
    for e in range(1, E):
        taken = jnp.where(route == e, source_ref[e * H : (e + 1) * H, :], taken)
    return taken


def place_heads(route_ref, source_ref, e):
    total = jnp.zeros((H, route_ref.shape[1]), F32)
    for k in range(TOPK):
        route = jnp.broadcast_to(route_ref[k : k + 1, :], (H, route_ref.shape[1]))
        total = jnp.where(route == e, source_ref[k * H : (k + 1) * H, :], total)
    return total


def key_mask(first_key, first_query, rows, start_row):
    keys = lax.broadcasted_iota(jnp.int32, (rows, TB), 0) + first_key
    queries = lax.broadcasted_iota(jnp.int32, (rows, TB), 1) + first_query
    return (keys <= queries) & (keys >= start_row)


def head_forward_kernel(
    steps, x_ref, route_ref, segment_ref, wall_ref, gain_ref,
    q_ref, att_ref, gate_ref, lse_ref, kv_ref, kvt_ref, start_ref, count_ref,
    all_scr, k_scr, vt_scr, count_scr,
):
    step = pl.program_id(0)
    place = lax.rem(step, NB)
    here = pl.multiple_of(place * TB, TB)

    @pl.when(step == 0)
    def _():
        count_scr[...] = jnp.zeros_like(count_scr)

    row = segment_ref[pl.ds(lax.div(step, NB), 1), :]
    segments = segment_ref[pl.ds(lax.div(step, NB), 1), pl.ds(here, TB)]
    start = jnp.zeros((1, TB), jnp.int32)
    for number in range(1, 4):
        below = jnp.sum((row < number).astype(jnp.int32), axis=1, keepdims=True)
        start = jnp.where(segments == number, below, start)
    start_ref[...] = start
    x = x_ref[...].astype(F32)
    normed = (x * rms_scale(x) * gain_ref[...]).astype(BF16)
    all_scr[...] = nt(wall_ref[...], normed)
    kt = all_scr[KROW : KROW + H, :]
    vt = all_scr[VROW : VROW + H, :]
    logits = all_scr[RROW : RROW + E, :]
    kvt = jnp.concatenate([kt, vt], axis=0)
    kv = kvt.T.astype(BF16)
    kv_ref[...] = kv
    kvt_ref[...] = kvt.astype(BF16)
    k_scr[pl.ds(here, TB), :] = kv[:, :H]
    vt_scr[:, pl.ds(here, TB)] = vt.astype(BF16)
    routes = route_ref[...]
    experts = lax.broadcasted_iota(jnp.int32, (E, TB), 0)
    chosen = []
    counts = count_scr[...]
    for k in range(TOPK):
        named = slot_of(routes, k, E) == experts
        chosen.append(jnp.sum(jnp.where(named, logits, 0.0), axis=0, keepdims=True))
        counts = counts + named.astype(F32)
    count_scr[...] = counts
    chosen = jnp.concatenate(chosen, axis=0)
    raised = jnp.exp(chosen - jnp.max(chosen, axis=0, keepdims=True))
    gate_ref[...] = raised / jnp.sum(raised, axis=0, keepdims=True)
    for k in range(TOPK):
        query = pick_heads(route_ref, all_scr, k).astype(BF16)
        q_ref[k * H : (k + 1) * H, :] = query * jnp.asarray(H ** (-0.5), BF16)

    def attend(blocks):
        rows = blocks * TB
        first_key = pl.multiple_of((place - (blocks - 1)) * TB, TB)
        mask = key_mask(first_key, here, rows, start)
        keys = k_scr[pl.ds(first_key, rows), :]
        values = vt_scr[:, pl.ds(first_key, rows)]
        for k in range(TOPK):
            scores = jnp.where(mask, nn(keys, q_ref[k * H : (k + 1) * H, :]), NEG_LARGE)
            top = jnp.max(scores, axis=0, keepdims=True)
            raised = jnp.exp(scores - top)
            total = jnp.sum(raised, axis=0, keepdims=True)
            probs = (raised * (1.0 / total)).astype(BF16)
            att_ref[k * H : (k + 1) * H, :] = nn(values, probs)
            lse_ref[k : k + 1, :] = top + jnp.log(total)

    span = place - lax.div(jnp.min(start), TB) + 1
    for blocks in range(1, min(3, NB) + 1):

        @pl.when(span == blocks)
        def _(blocks=blocks):
            attend(blocks)

    @pl.when(step == steps - 1)
    def _():
        held = jnp.sum(count_scr[...], axis=1, keepdims=True)
        count_ref[...] = jnp.broadcast_to(held, (E, 128))


def picks(rows, stride, first):
    at = lax.broadcasted_iota(jnp.int32, (rows, D), 1)
    row = lax.broadcasted_iota(jnp.int32, (rows, D), 0)
    return (at == row * stride + first).astype(F32)


def exact(product, a, b):
    return lax.dot_general(
        a, b, (product, ((), ())), precision=lax.Precision.HIGHEST, preferred_element_type=F32
    )


def gelu_parts(v):
    size = jnp.abs(v) * 0.7071067811865476
    bell = jnp.exp(-(size * size))
    t = 1.0 / (1.0 + 0.3275911 * size)
    series = t * (
        0.254829592
        + t * (-0.284496736 + t * (1.421413741 + t * (-1.453152027 + t * 1.061405429)))
    )
    tail = 0.5 * series * bell
    cdf = jnp.where(v < 0.0, tail, 1.0 - tail)
    return cdf, bell * 0.3989422804014327


def middle_kernel(
    shard_size, early, many, x_ref, dy_ref, gain_ref, tail_ref, land_ref, route_ref, gate_ref, att_ref,
    out_ref, dres_ref, datt_ref, delta_ref, dlogit_ref, window_ref, extra_ref, dgain_ref,
    slot_scr, head_scr, mix_scr, dwo_ref, dw1_ref, dw2t_ref, wo_ref, w1_ref, w2_ref, rows_scr,
    stage, stage_sem,
):
    step = pl.program_id(0)

    @pl.when(step == 0)
    def _():
        rows_scr[0 : tail_ref.shape[0], :] = tail_ref[...]
        lay_blocks(shard_size, land_ref, rows_scr, early, many, WO_ROW)
        late_matrices(rows_scr, wo_ref, w1_ref, w2_ref)
        dwo_ref[...] = jnp.zeros_like(dwo_ref)
        dw1_ref[...] = jnp.zeros_like(dw1_ref)
        dw2t_ref[...] = jnp.zeros_like(dw2t_ref)
        dgain_ref[...] = jnp.zeros_like(dgain_ref)

    routes = route_ref[...]
    tokens = routes.shape[1]
    gates = gate_ref[...]
    for k in range(TOPK):
        slot_scr[k * H : (k + 1) * H, :] = gates[k : k + 1, :] * att_ref[k * H : (k + 1) * H, :]
    for e in range(E):
        mix_scr[e * H : (e + 1) * H, :] = place_heads(route_ref, slot_scr, e).astype(BF16)
    x = x_ref[...].astype(F32)
    dy = dy_ref[...]
    mixed = mix_scr[...]
    residual = x + tn(mixed, wo_ref[...])
    scale = rms_scale(residual)
    gain = gain_ref[...]
    second = (residual * scale * gain).astype(BF16)
    second_t = second.T
    dy_t = dy.T
    out = residual
    dsecond = jnp.zeros((tokens, D), F32)
    for c in range(0, FF, FC):
        up = w1_ref[:, c : c + FC]
        down = w2_ref[c : c + FC, :]
        pre = nn(second, up)
        cdf, density = gelu_parts(pre)
        hidden = (pre * cdf).astype(BF16)
        dpre = (nt(dy, down) * (cdf + pre * density)).astype(BF16)
        out = out + nn(hidden, down)
        dsecond = dsecond + nt(dpre, up)
        dw2t_ref[:, c : c + FC] += nn(dy_t, hidden)
        dw1_ref[:, c : c + FC] += nn(second_t, dpre)
    out_ref[...] = out.astype(BF16)
    dgain_ref[...] += jnp.sum(dsecond * residual * scale, axis=0, keepdims=True)
    weighted = gain * dsecond
    dres = (
        dy.astype(F32)
        + scale * weighted
        - residual * (scale * scale * scale) * jnp.mean(weighted * residual, axis=-1, keepdims=True)
    )
    dres_ref[...] = dres
    branch = dres.astype(BF16)
    dwo_ref[...] += nn(mixed, branch)
    head_scr[...] = nt(wo_ref[...], branch).astype(BF16).astype(F32)
    dgates = []
    for k in range(TOPK):
        rows = slice(k * H, (k + 1) * H)
        dslot = pick_heads(route_ref, head_scr, k)
        attended = att_ref[rows, :]
        dgates.append(jnp.sum(dslot * attended, axis=0, keepdims=True))
        datt = (gates[k : k + 1, :] * dslot).astype(BF16)
        datt_ref[rows, :] = datt
        delta_ref[k : k + 1, :] = jnp.sum(datt.astype(F32) * attended, axis=0, keepdims=True)
    dgate = jnp.concatenate(dgates, axis=0)
    dchosen = gates * (dgate - jnp.sum(gates * dgate, axis=0, keepdims=True))
    experts = lax.broadcasted_iota(jnp.int32, (E, tokens), 0)
    dlogits = jnp.zeros((E, tokens), F32)
    for k in range(TOPK):
        dlogits = jnp.where(
            slot_of(routes, k, E) == experts,
            jnp.broadcast_to(dchosen[k : k + 1, :], (E, tokens)),
            dlogits,
        )
    dlogit_ref[...] = dlogits

    @pl.when(step == pl.num_programs(0) - 1)
    def _():
        for c in range(D // 128):
            lanes = slice(c * 128, (c + 1) * 128)
            rows_scr[pl.ds(c, QW, stride=4), :] = dwo_ref[:, lanes]
            rows_scr[pl.ds(W2_ROW - WO_ROW + c, FF, stride=4), :] = dw2t_ref[lanes, :].T
        for c in range(FF // 128):
            rows_scr[pl.ds(W1_ROW - WO_ROW + c, D, stride=16), :] = dw1_ref[:, c * 128 : (c + 1) * 128]
        extra_ref[...] = rows_scr[0 : extra_ref.shape[0], :]
        window = stage.shape[1]

        def put(number):
            return pltpu.make_async_copy(
                stage.at[number],
                window_ref.at[pl.ds(pl.multiple_of((number + early) * window, 16), window), :],
                stage_sem.at[number],
            )

        def cut(number, carry):
            row = pl.multiple_of(first_row(shard_size, number + early) - WO_ROW, 8)
            stage[number] = rows_scr[pl.ds(row, window), :].astype(BF16)
            put(number).start()
            return carry

        def leave(number, carry):
            put(number).wait()
            return carry

        lax.fori_loop(0, many - early, cut, 0)
        lax.fori_loop(0, many - early, leave, 0)


def head_backward_kernel(
    x_ref, gain_ref, wall_ref, route_ref, start_ref, q_ref, datt_ref,
    lse_ref, delta_ref, kv_ref, kvt_ref, dlogit_ref, dres_ref, dgain_two_ref, extra_ref,
    dx_ref, flat_ref,
    dk_scr, dv_scr, dq_scr, dall_scr, dwall_ref, dgain_ref, rows_scr, row_sem,
):
    step = pl.program_id(0)
    place = NB - 1 - lax.rem(step, NB)
    here = pl.multiple_of(place * TB, TB)

    @pl.when(step == 0)
    def _():
        dwall_ref[...] = jnp.zeros_like(dwall_ref)
        dgain_ref[...] = jnp.zeros_like(dgain_ref)

    @pl.when(lax.rem(step, NB) == 0)
    def _():
        dk_scr[...] = jnp.zeros_like(dk_scr)
        dv_scr[...] = jnp.zeros_like(dv_scr)

    def attend(blocks):
        rows = blocks * TB
        first_key = pl.multiple_of((place - (blocks - 1)) * TB, TB)
        mask = key_mask(first_key, here, rows, start_ref[...])
        keys = kv_ref[pl.ds(first_key, rows), :H]
        values = kv_ref[pl.ds(first_key, rows), H:]
        keys_t = kvt_ref[:H, pl.ds(first_key, rows)]
        dk = jnp.zeros((rows, H), F32)
        dv = jnp.zeros((rows, H), F32)
        for k in range(TOPK):
            part = slice(k * H, (k + 1) * H)
            query = q_ref[part, :]
            datt = datt_ref[part, :]
            scores = jnp.where(mask, nn(keys, query), NEG_LARGE)
            probs = jnp.exp(scores - lse_ref[k : k + 1, :])
            dscore = (probs * (nn(values, datt) - delta_ref[k : k + 1, :])).astype(BF16)
            dv = dv + nt(probs.astype(BF16), datt)
            dk = dk + nt(dscore, query)
            dq_scr[part, :] = nn(keys_t, dscore) * (H ** (-0.5))
        dk_scr[pl.ds(first_key, rows), :] += dk
        dv_scr[pl.ds(first_key, rows), :] += dv

    span = place - lax.div(jnp.min(start_ref[...]), TB) + 1
    for blocks in range(1, min(3, NB) + 1):

        @pl.when(span == blocks)
        def _(blocks=blocks):
            attend(blocks)

    for e in range(E):
        dall_scr[e * H : (e + 1) * H, :] = place_heads(route_ref, dq_scr, e).astype(BF16)
    dkv = jnp.concatenate([dk_scr[pl.ds(here, TB), :], dv_scr[pl.ds(here, TB), :]], axis=1)
    dall_scr[KROW : KROW + 2 * H, :] = dkv.T.astype(BF16)
    dall_scr[RROW : RROW + 32, :] = jnp.concatenate(
        [dlogit_ref[...], jnp.zeros((32 - E, TB), F32)], axis=0
    ).astype(BF16)
    x = x_ref[...].astype(F32)
    scale = rms_scale(x)
    gain = gain_ref[...]
    normed = (x * scale * gain).astype(BF16)
    dall = dall_scr[...]
    dwall_ref[...] += nn(dall, normed)
    dnormed = tn(dall, wall_ref[...])
    dgain_ref[...] += jnp.sum(dnormed * x * scale, axis=0, keepdims=True)
    weighted = gain * dnormed
    dx_ref[...] = (
        dres_ref[...]
        + scale * weighted
        - x * (scale * scale * scale) * jnp.mean(weighted * x, axis=-1, keepdims=True)
    )

    @pl.when(step == pl.num_programs(0) - 1)
    def _():
        for c in range(D // 128):
            lanes = slice(c * 128, (c + 1) * 128)
            rows_scr[c : c + 1, :] = dgain_ref[:, lanes]
            rows_scr[4 + c : 5 + c, :] = dgain_two_ref[:, lanes]
        router_t = dwall_ref[RROW : RROW + E, :]
        across = jnp.concatenate(
            [exact(((1,), (1,)), router_t, picks(32, 16, b)) for b in range(16)], axis=0
        ).T
        for j in range(3):
            rows_scr[pl.ds(WR_ROW + j, 32, stride=3), :] = across[:, j * 128 : (j + 1) * 128]
        for first, row in ((KROW, WK_ROW), (VROW, WV_ROW)):
            part = dwall_ref[first : first + H, :]
            rows_scr[row : row + 256, :] = jnp.concatenate(
                [exact(((1,), (1,)), picks(256, 2, b), part) for b in range(2)], axis=1
            )
        for c in range(QW // 128):
            rows_scr[pl.ds(WQ_ROW + c, D, stride=12), :] = dwall_ref[c * 128 : (c + 1) * 128, :].T
        extra = extra_ref.shape[0]
        rows_scr[WO_ROW : WO_ROW + extra, :] = extra_ref[...]
        copy = pltpu.make_async_copy(rows_scr, flat_ref, row_sem.at[0])
        copy.start()
        copy.wait()


def whole(shape):
    return pl.BlockSpec(shape, lambda *_: (0,) * len(shape), pipeline_mode=pl.Buffered(1))


def kept(shape):
    return pl.BlockSpec(shape, lambda *_: (0,) * len(shape))


def struct(shape, kind=F32):
    return jax.ShapeDtypeStruct(shape, kind)


def params_for(mib):
    return pltpu.CompilerParams(vmem_limit_bytes=mib * MIB)


def head_forward(tokens, routes_t, segments, wall, gain):
    count = tokens.shape[0]
    steps = count // TB
    across = lambda rows: pl.BlockSpec((rows, TB), lambda b: (0, b))
    down = lambda columns: pl.BlockSpec((TB, columns), lambda b: (b, 0))
    return pl.pallas_call(
        functools.partial(head_forward_kernel, steps),
        grid=(steps,),
        in_specs=[down(D), across(TOPK), whole(segments.shape), whole((ALLW, D)), whole((1, D))],
        out_specs=[
            across(TOPK * H), across(TOPK * H), across(TOPK), across(TOPK), down(2 * H), across(2 * H),
            across(1), whole((E, 128)),
        ],
        scratch_shapes=[
            pltpu.VMEM((ALLW, TB), F32),
            pltpu.VMEM((LEN, H), BF16),
            pltpu.VMEM((H, LEN), BF16),
            pltpu.VMEM((E, TB), F32),
        ],
        out_shape=[
            struct((TOPK * H, count), BF16),
            struct((TOPK * H, count)),
            struct((TOPK, count)),
            struct((TOPK, count)),
            struct((count, 2 * H), BF16),
            struct((2 * H, count), BF16),
            struct((1, count), jnp.int32),
            struct((E, 128)),
        ],
        compiler_params=params_for(56),
        name="head_forward",
        cost_estimate=pl.CostEstimate(flops=10_000_000_000, bytes_accessed=16_000_000, transcendentals=0),
    )(tokens, routes_t, segments, wall, gain)


def middle(shard_size, early, many, tokens, grad_out, gain, tail, land, routes_t, gates, attended):
    count = tokens.shape[0]
    steps = count // TB
    window = land.shape[1]
    rows = (shard_size * (many - 1)) // UNIT * 16 + window - WO_ROW
    across = lambda rows: pl.BlockSpec((rows, TB), lambda b: (0, b))
    down = lambda columns: pl.BlockSpec((TB, columns), lambda b: (b, 0))
    return pl.pallas_call(
        functools.partial(middle_kernel, shard_size, early, many),
        grid=(steps,),
        in_specs=[
            down(D), down(D), whole((1, D)), whole(tail.shape), whole(land.shape),
            across(TOPK), across(TOPK), across(TOPK * H),
        ],
        out_specs=[
            down(D), down(D), across(TOPK * H), across(TOPK), across(E),
            pl.BlockSpec(memory_space=pl.ANY), whole(tail.shape), whole((1, D)),
        ],
        out_shape=[
            struct((count, D), BF16),
            struct((count, D)),
            struct((TOPK * H, count), BF16),
            struct((TOPK, count)),
            struct((E, count)),
            struct((many * window, 128), BF16),
            struct(tail.shape),
            struct((1, D)),
        ],
        scratch_shapes=[
            pltpu.VMEM((TOPK * H, TB), F32),
            pltpu.VMEM((QW, TB), F32),
            pltpu.VMEM((QW, TB), BF16),
            pltpu.VMEM((QW, D), F32),
            pltpu.VMEM((D, FF), F32),
            pltpu.VMEM((D, FF), F32),
            pltpu.VMEM((QW, D), BF16),
            pltpu.VMEM((D, FF), BF16),
            pltpu.VMEM((FF, D), BF16),
            pltpu.VMEM((rows, 128), F32),
            pltpu.VMEM((many - early, window, 128), BF16),
            pltpu.SemaphoreType.DMA((many - early,)),
        ],
        compiler_params=params_for(60),
        name="middle",
        cost_estimate=pl.CostEstimate(flops=40_000_000_000, bytes_accessed=32_000_000, transcendentals=0),
    )(tokens, grad_out, gain, tail, land, routes_t, gates, attended)


def head_backward(
    tokens, gain, wall, routes_t, start, queries, datt, lse, delta, kv, kvt, dlogits, dres, dgain_two, extra
):
    count = tokens.shape[0]
    steps = count // TB
    early_rows = WO_ROW + extra.shape[0]

    def place(b):
        return (b // NB) * NB + NB - 1 - b % NB

    across = lambda rows: pl.BlockSpec((rows, TB), lambda b: (0, place(b)))
    down = lambda columns: pl.BlockSpec((TB, columns), lambda b: (place(b), 0))
    return pl.pallas_call(
        head_backward_kernel,
        grid=(steps,),
        in_specs=[
            down(D), whole((1, D)), whole((ALLW, D)), across(TOPK), across(1),
            across(TOPK * H), across(TOPK * H), across(TOPK), across(TOPK),
            pl.BlockSpec((LEN, 2 * H), lambda b: (b // NB, 0)),
            pl.BlockSpec((2 * H, LEN), lambda b: (0, b // NB)),
            across(E), down(D), whole((1, D)), whole(extra.shape),
        ],
        out_specs=[down(D), pl.BlockSpec(memory_space=pl.ANY)],
        scratch_shapes=[
            pltpu.VMEM((LEN, H), F32),
            pltpu.VMEM((LEN, H), F32),
            pltpu.VMEM((TOPK * H, TB), F32),
            pltpu.VMEM((ALLW, TB), BF16),
            pltpu.VMEM((ALLW, D), F32),
            pltpu.VMEM((1, D), F32),
            pltpu.VMEM((early_rows, 128), F32),
            pltpu.SemaphoreType.DMA((1,)),
        ],
        out_shape=[struct((count, D)), struct((early_rows, 128))],
        compiler_params=params_for(56),
        name="head_backward",
        cost_estimate=pl.CostEstimate(flops=30_000_000_000, bytes_accessed=24_000_000, transcendentals=0),
    )(
        tokens, gain, wall, routes_t, start, queries, datt, lse, delta, kv, kvt, dlogits, dres,
        dgain_two, extra,
    )


class Mesh3:
    def __init__(self, shards, over):
        shard = lax.axis_index("dp")
        other = lax.axis_index("fsdp")
        self.over = over
        self.many = shards * over
        self.sizes = {"x": 2, "y": shards // 2, "z": over // 2}
        self.here = {"x": lax.rem(other, 2), "y": lax.div(shard, 2), "z": lax.div(other, 2)}
        self.core = lax.rem(shard, 2)
        self.me = shard * over + other
        self.partner = (shard + 1 - 2 * self.core, other)

    def moved(self, steps):
        return {
            axis: lax.rem(self.here[axis] + steps.get(axis, 0), self.sizes[axis]) for axis in "xyz"
        }

    def device(self, core, steps):
        at = self.moved(steps)
        return (at["y"] * 2 + core, at["z"] * 2 + at["x"])

    def number(self, core, steps):
        shard, other = self.device(core, steps)
        return shard * self.over + other

    def nth(self, number):
        return (lax.div(number, self.over), lax.rem(number, self.over))

    def greet_near(self):
        devices = [
            self.device(self.core, {axis: step})
            for axis in "xyz"
            for step in range(1, self.sizes[axis])
        ] + [self.partner]
        barrier = pltpu.get_barrier_semaphore()
        for device in devices:
            pl.semaphore_signal(barrier, inc=1, device_id=device, device_id_type=MESH)
        pl.semaphore_wait(barrier, len(devices))

    def greet_all(self):
        barrier = pltpu.get_barrier_semaphore()

        def hello(j, carry):
            device = self.nth(lax.rem(self.me + j, self.many))
            pl.semaphore_signal(barrier, inc=1, device_id=device, device_id_type=MESH)
            return carry

        lax.fori_loop(1, self.many, hello, 0)
        pl.semaphore_wait(barrier, self.many - 1)


def along_z(step):
    return {1: (0, 3), 2: (1, 5), 3: (3, 8)}.get(step, (step, 2 * step + 2))


class Kind:
    def __init__(self, mesh, core, axes):
        self.mesh = mesh
        self.core = core
        self.axes = axes
        ranges = [range(mesh.sizes[axis]) for axis in axes]
        self.offsets = list(itertools.product(*ranges))
        self.index = {one: number for number, one in enumerate(self.offsets)}

    def owner(self, offsets):
        return self.mesh.number(self.core, dict(zip(self.axes, offsets)))

    def last(self, offsets):
        return max([i for i in range(3) if offsets[i]], default=-1)

    def turn(self, offsets):
        total = 0
        for axis, step in zip(self.axes, offsets):
            if step:
                total += along_z(step)[1] if axis == "z" else 2
        return total

    def hops(self, offsets):
        for i in range(self.last(offsets) + 1, 3):
            for step in range(1, self.mesh.sizes[self.axes[i]]):
                delay = along_z(step)[0] if self.axes[i] == "z" else 0
                yield i, step, self.turn(offsets) + delay

    def ahead(self, i, step):
        return self.mesh.device(self.core, {self.axes[i]: step})


AXES = ("yzx", "zxy")


def gather_events(mesh, wanted, own_ref, land, send_sem, recv_sem):
    events = []
    many = mesh.many
    kinds = [Kind(mesh, core, AXES[core]) for core in range(2)]
    end = max(kind.turn(one) for kind in kinds for one in kind.offsets) + 2

    def copy(owner, device, slot):
        return pltpu.make_async_remote_copy(
            src_ref=land.at[owner],
            dst_ref=land.at[owner],
            send_sem=send_sem.at[slot],
            recv_sem=recv_sem.at[owner],
            device_id=device,
            device_id_type=MESH,
        )

    def event(turn, condition, action):
        events.append((turn, lambda: pl.when(condition)(action)))

    for kind in kinds:
        slots = itertools.count()
        for offsets in kind.offsets:
            owner = kind.owner(offsets)
            ours = (mesh.core == kind.core) & wanted(owner)
            theirs = (mesh.core != kind.core) & wanted(owner)
            slot = next(slots)

            def come(owner=owner, offsets=offsets, slot=slot):
                if any(offsets):
                    copy(owner, mesh.partner, slot).wait_recv()
                else:
                    land[owner] = own_ref[...]
                copy(owner, mesh.partner, slot).start()

            def across(owner=owner, slot=slot):
                copy(owner, mesh.partner, slot).wait_recv()

            def done(owner=owner, slot=slot):
                copy(owner, mesh.partner, slot).wait_send()

            event(kind.turn(offsets), ours, come)
            event(end, theirs, across)
            event(end, ours, done)
            for i, step, turn in kind.hops(offsets):
                slot = next(slots)
                device = kind.ahead(i, step)

                def send(owner=owner, device=device, slot=slot):
                    copy(owner, device, slot).start()

                def sent(owner=owner, device=device, slot=slot):
                    copy(owner, device, slot).wait_send()

                event(turn, ours, send)
                event(end, ours, sent)
    return sorted(events, key=lambda one: one[0])


def reduce_events(mesh, wanted, load, outgo, income, send_sem, recv_sem, finish):
    events = []
    half = mesh.many // 2
    kinds = [Kind(mesh, core, AXES[core]) for core in range(2)]
    end = max(kind.turn(one) for kind in kinds for one in kind.offsets) + 2

    def copy(slot, device):
        return pltpu.make_async_remote_copy(
            src_ref=outgo.at[slot],
            dst_ref=income.at[slot],
            send_sem=send_sem.at[slot],
            recv_sem=recv_sem.at[slot],
            device_id=device,
            device_id_type=MESH,
        )

    def event(turn, condition, action):
        events.append((turn, lambda: pl.when(condition)(action)))

    def sends(slot, device, values):
        outgo[slot] = values.astype(BF16)
        copy(slot, device).start()

    def taken(slot):
        copy(slot, mesh.partner).wait_recv()
        return income[slot].astype(F32)

    for kind in kinds:
        slots = {}
        for offsets in kind.offsets:
            if any(offsets):
                slots[offsets] = half + len(slots)
        for offsets in kind.offsets:
            owner = kind.owner(offsets)
            ours = (mesh.core == kind.core) & wanted(owner)
            theirs = (mesh.core != kind.core) & wanted(owner)
            number = kind.index[offsets]
            axis = kind.last(offsets)
            turn = end - kind.turn(offsets)

            def hand(owner=owner, number=number):
                sends(number, mesh.partner, load(owner))

            def handed(number=number):
                copy(number, mesh.partner).wait_send()

            def onward(owner=owner, offsets=offsets, number=number, axis=axis, kind=kind, slots=slots):
                total = load(owner) + taken(number)
                for i, step, _ in kind.hops(offsets):
                    longer = tuple(step if j == i else o for j, o in enumerate(offsets))
                    total = total + taken(slots[longer])
                if axis < 0:
                    finish(total)
                else:
                    sends(slots[offsets], kind.ahead(axis, offsets[axis]), total)

            event(turn - 2, theirs, hand)
            event(end + 1, theirs, handed)
            event(turn, ours, onward)
            if axis >= 0:

                def passed(slot=slots[offsets]):
                    copy(slot, mesh.partner).wait_send()

                event(end + 1, ours, passed)
    return sorted(events, key=lambda one: one[0])


def at_polls(events, polls):
    last = events[-1][0]
    spread = [[] for _ in range(polls)]
    for turn, action in events:
        spread[turn if last < polls else turn * (polls - 1) // last].append(action)
    return spread


def poll(step, half, spread):
    for number in range(len(spread) // 2):
        actions = spread[2 * number + half]
        if actions:

            @pl.when(step == number)
            def _(actions=actions):
                for action in actions:
                    action()


def window_rows(shard_size, many):
    units = [(shard_size * d) // UNIT for d in range(many + 1)]
    return 16 * (max(b - a for a, b in zip(units, units[1:])) + 1)


def first_row(shard_size, number):
    return pl.multiple_of(lax.div(number * shard_size, UNIT) * 16, 16)


def early_owners(shard_size, over):
    group = shard_size * over
    return -(-(WO_ROW * 128) // group) * over


def lay_blocks(shard_size, land, flat, first, last, origin):
    window = land.shape[1]

    def lay(number, carry):
        row = pl.multiple_of(first_row(shard_size, number) - origin, 8)
        flat[pl.ds(row, 16), :] += land[number, 0:16, :].astype(F32)
        flat[pl.ds(row + 16, window - 16), :] = land[number, 16:window, :].astype(F32)
        return carry

    lax.fori_loop(first, last, lay, 0)


def early_matrices(flat, wall_ref, gain_one_ref, gain_two_ref):
    for c in range(D // 128):
        lanes = slice(c * 128, (c + 1) * 128)
        gain_one_ref[:, lanes] = flat[c : c + 1, :]
        gain_two_ref[:, lanes] = flat[4 + c : 5 + c, :]
    for c in range(QW // 128):
        wall_ref[c * 128 : (c + 1) * 128, :] = flat[pl.ds(WQ_ROW + c, D, stride=12), :].T.astype(BF16)
    for first, row in ((KROW, WK_ROW), (VROW, WV_ROW)):
        pair = flat[row : row + 256, :].T.astype(BF16)
        wall_ref[first : first + H, :] = (
            nn(pair[:H], picks(256, 2, 0).astype(BF16)) + nn(pair[H:], picks(256, 2, 1).astype(BF16))
        ).astype(BF16)
    across = jnp.concatenate(
        [flat[pl.ds(WR_ROW + j, 32, stride=3), :] for j in range(3)], axis=1
    ).T.astype(BF16)
    router_t = jnp.zeros((E, D), F32)
    for part in range(16):
        router_t = router_t + nn(across[part * E : (part + 1) * E, :], picks(32, 16, part).astype(BF16))
    wall_ref[RROW:ALLW, :] = jnp.concatenate(
        [router_t, jnp.zeros((ALLW - RROW - E, D), F32)], axis=0
    ).astype(BF16)


def late_matrices(flat, wo_ref, w1_ref, w2_ref):
    for c in range(D // 128):
        lanes = slice(c * 128, (c + 1) * 128)
        wo_ref[:, lanes] = flat[pl.ds(c, QW, stride=4), :].astype(BF16)
        w2_ref[:, lanes] = flat[pl.ds(W2_ROW - WO_ROW + c, FF, stride=4), :].astype(BF16)
    for c in range(FF // 128):
        w1_ref[:, c * 128 : (c + 1) * 128] = flat[
            pl.ds(W1_ROW - WO_ROW + c, D, stride=16), :
        ].astype(BF16)


def gather_kernel(
    mesh, shard_size, early, own_ref,
    wall_ref, gain_one_ref, gain_two_ref, tail_ref,
    land, flat, send_sem, recv_sem,
):
    mesh = mesh()
    mesh.greet_near()
    for _, action in gather_events(mesh, lambda owner: owner < early, own_ref, land, send_sem, recv_sem):
        action()
    flat[0:16, :] = jnp.zeros((16, 128), F32)
    lay_blocks(shard_size, land, flat, 0, early, 0)
    early_matrices(flat, wall_ref, gain_one_ref, gain_two_ref)
    tail_ref[...] = flat[WO_ROW : WO_ROW + tail_ref.shape[0], :]


def gather_early(shards, over, shard_size, own):
    window = own.shape[0]
    early = early_owners(shard_size, over)
    rows = (shard_size * (early - 1)) // UNIT * 16 + window
    vmem = pl.BlockSpec(memory_space=pltpu.VMEM)
    mesh = functools.partial(Mesh3, shards, over)
    return pl.pallas_call(
        functools.partial(gather_kernel, mesh, shard_size, early),
        in_specs=[vmem],
        out_specs=[vmem] * 4,
        out_shape=[
            struct((ALLW, D), BF16),
            struct((1, D)),
            struct((1, D)),
            struct((rows - WO_ROW, 128)),
        ],
        scratch_shapes=[
            pltpu.VMEM((early, window, 128), BF16),
            pltpu.VMEM((rows, 128), F32),
            pltpu.SemaphoreType.DMA((shards * over,)),
            pltpu.SemaphoreType.DMA((early,)),
        ],
        compiler_params=pltpu.CompilerParams(
            collective_id=0, has_side_effects=True, vmem_limit_bytes=56 * MIB
        ),
        name="gather_early",
        cost_estimate=pl.CostEstimate(flops=0, bytes_accessed=60_000_000, transcendentals=0),
    )(own)


def reduce_kernel(
    mesh, shard_size, early, flat_ref, late_ref, count_ref,
    out_ref, total_ref, sum_ref,
    part, outgo, income, stats, part_sem, send_sem, recv_sem, stat_send, stat_recv,
):
    mesh = mesh()
    many = mesh.many
    window = out_ref.shape[0]

    def fetch(owner):
        return pltpu.make_async_copy(
            flat_ref.at[pl.ds(first_row(shard_size, owner), window), :],
            part.at[owner],
            part_sem.at[owner],
        )

    for owner in range(early):
        fetch(owner).start()
    mesh.greet_all()
    @pl.when(mesh.me >= early)
    def _():
        out_ref[...] = late_ref[...].astype(F32)

    def finish(total):
        out_ref[...] = total

    def block(owner):
        fetch(owner).wait()
        return part[owner]

    for _, action in reduce_events(
        mesh, lambda owner: owner < early, block, outgo, income, send_sem, recv_sem, finish
    ):
        action()
    total = out_ref[...]
    begin = mesh.me * shard_size - lax.div(mesh.me * shard_size, UNIT) * UNIT
    at = (
        lax.broadcasted_iota(jnp.int32, (window, 128), 0) * 128
        + lax.broadcasted_iota(jnp.int32, (window, 128), 1)
    )
    inside = jnp.where((at >= begin) & (at < begin + shard_size), total, 0.0)
    stats[0, 0:8, :] = jnp.broadcast_to(jnp.sum(inside * inside, axis=0, keepdims=True), (8, 128))
    stats[0, 8:16, :] = total[0:8, :]
    stats[0, 16 : 16 + E, :] = count_ref[...]

    def told(j):
        return pltpu.make_async_remote_copy(
            src_ref=stats.at[0],
            dst_ref=stats.at[j],
            send_sem=stat_send.at[j],
            recv_sem=stat_recv.at[j],
            device_id=mesh.nth(lax.rem(mesh.me + j, many)),
            device_id_type=MESH,
        )

    def tell(j, carry):
        told(j).start()
        return carry

    def hear(j, carry):
        told(j).wait()
        return carry

    lax.fori_loop(1, many, tell, 0)
    lax.fori_loop(1, many, hear, 0)
    total_ref[...] = jnp.broadcast_to(
        jnp.sum(jnp.sum(stats[:, 0:8, :], axis=0), axis=1, keepdims=True), (8, 128)
    )
    sum_ref[0:8, :] = stats[mesh.me, 8:16, :]
    sum_ref[8 : 8 + E, :] = jnp.sum(stats[:, 16 : 16 + E, :], axis=0)


def reduce_early(shards, over, shard_size, window, flat, late, counts):
    vmem = pl.BlockSpec(memory_space=pltpu.VMEM)
    many = shards * over
    early = early_owners(shard_size, over)
    mesh = functools.partial(Mesh3, shards, over)
    return pl.pallas_call(
        functools.partial(reduce_kernel, mesh, shard_size, early),
        in_specs=[pl.BlockSpec(memory_space=pl.ANY), vmem, vmem],
        out_specs=[vmem] * 3,
        out_shape=[struct((window, 128)), struct((8, 128)), struct((8 + E, 128))],
        scratch_shapes=[
            pltpu.VMEM((early, window, 128), F32),
            pltpu.VMEM((many, window, 128), BF16),
            pltpu.VMEM((many, window, 128), BF16),
            pltpu.VMEM((many, 16 + E, 128), F32),
            pltpu.SemaphoreType.DMA((early,)),
            pltpu.SemaphoreType.DMA((many,)),
            pltpu.SemaphoreType.DMA((many,)),
            pltpu.SemaphoreType.DMA((many,)),
            pltpu.SemaphoreType.DMA((many,)),
        ],
        compiler_params=pltpu.CompilerParams(
            collective_id=1, has_side_effects=True, vmem_limit_bytes=56 * MIB
        ),
        name="reduce_early",
        cost_estimate=pl.CostEstimate(flops=0, bytes_accessed=60_000_000, transcendentals=0),
    )(flat, late, counts)


def per_device(
    shards, over, tokens, grad_out, routes, segments, params, first_moment, second_moment, ema_weights
):
    shard_size = params.shape[0]
    window = window_rows(shard_size, shards * over)
    early = early_owners(shard_size, over)
    me = lax.axis_index("dp") * over + lax.axis_index("fsdp")
    begin = lax.rem(me * shard_size, UNIT)
    own = lax.dynamic_slice(
        jnp.pad(params.astype(BF16), (UNIT, window * 128 - shard_size)), (UNIT - begin,), (window * 128,)
    ).reshape(window, 128)
    routes_t = routes.T
    wall, gain_one, gain_two, tail = gather_early(shards, over, shard_size, own)
    land = lax.all_gather(own, ("dp", "fsdp"), axis=0, tiled=True).reshape(-1, window, 128)
    queries, attended, gates, lse, kv, kvt, start, counts = head_forward(
        tokens, routes_t, segments, wall, gain_one
    )
    output, dres, datt, delta, dlogits, windows, extra, dgain_two = middle(
        shard_size, early, shards * over, tokens, grad_out, gain_two, tail, land, routes_t, gates, attended
    )
    late_sum = lax.psum_scatter(windows, ("dp", "fsdp"), scatter_dimension=0, tiled=True)
    input_grad, flat = head_backward(
        tokens, gain_one, wall, routes_t, start, queries, datt, lse, delta, kv, kvt, dlogits, dres,
        dgain_two, extra,
    )
    reduced, square_sum, sums = reduce_early(shards, over, shard_size, window, flat, late_sum, counts)
    grad_shard = lax.dynamic_slice(reduced.reshape(-1), (begin,), (shard_size,))
    total_tokens = tokens.shape[0] * shards * over
    expert_load = sums[8:, 0] * (E / (total_tokens * TOPK))
    grad_norm = jnp.sqrt(square_sum[0, 0])
    clipped = grad_shard * (CLIP_LIMIT / jnp.maximum(grad_norm, CLIP_LIMIT))
    new_first = BETA_FIRST * first_moment + (1.0 - BETA_FIRST) * clipped
    new_second = BETA_SECOND * second_moment + (1.0 - BETA_SECOND) * clipped * clipped
    first_hat = new_first / (1.0 - BETA_FIRST**STEP)
    second_hat = new_second / (1.0 - BETA_SECOND**STEP)
    new_params = params * (1.0 - LEARN_RATE * DECAY_RATE) - LEARN_RATE * first_hat / (
        jnp.sqrt(second_hat) + ADAM_EPS
    )
    new_ema = EMA_KEEP * ema_weights + (1.0 - EMA_KEEP) * new_params
    return (
        output,
        input_grad,
        expert_load,
        grad_norm.reshape(1),
        new_params,
        new_first,
        new_second,
        new_ema,
        sums[:8].reshape(2, D),
    )


def solution(mesh):
    row = P(("dp", "fsdp"), None)
    flat = P(("dp", "fsdp"))
    return jax.shard_map(
        functools.partial(per_device, mesh.shape["dp"], mesh.shape["fsdp"]),
        mesh=mesh,
        in_specs=(row, row, row, row, flat, flat, flat, flat),
        out_specs=(row, row, P(), P(), flat, flat, flat, flat, P()),
        check_vma=False,
    )
```

```python
import functools
import itertools

import jax
import jax.numpy as jnp
from jax import lax
from jax.experimental import pallas as pl
from jax.experimental.pallas import tpu as pltpu
from jax.sharding import PartitionSpec as P

D = 512
E = 24
TOPK = 8
H = 64
FF = 2048
STEP = 10

NORM_EPS = 1e-06
CLIP_LIMIT = 1.0
BETA_FIRST = 0.9
BETA_SECOND = 0.95
LEARN_RATE = 0.1
DECAY_RATE = 0.1
ADAM_EPS = 1e-08
EMA_KEEP = 0.9
NEG_LARGE = -1e30

QW = E * H
KROW = QW
VROW = QW + H
RROW = QW + 2 * H
ALLW = 1696
LEN = 1024
TB = 256
NB = LEN // TB
FC = 512
MIB = 1 << 20

WR_ROW = 8
WK_ROW = 104
WV_ROW = 360
WQ_ROW = 616
WO_ROW = 6760
W1_ROW = 12904
W2_ROW = 21096
ALL_ROWS = 29288
UNIT = 16 * 128
MESH = pl.DeviceIdType.MESH

F32 = jnp.float32
BF16 = jnp.bfloat16


def nn(a, b):
    return lax.dot_general(a, b, (((1,), (0,)), ((), ())), preferred_element_type=F32)


def nt(a, b):
    return lax.dot_general(a, b, (((1,), (1,)), ((), ())), preferred_element_type=F32)


def tn(a, b):
    return lax.dot_general(a, b, (((0,), (0,)), ((), ())), preferred_element_type=F32)


def rms_scale(values):
    return lax.rsqrt(jnp.mean(values * values, axis=-1, keepdims=True) + NORM_EPS)


def slot_of(routes, k, rows):
    return jnp.broadcast_to(routes[k : k + 1, :], (rows, routes.shape[1]))


def pick_heads(route_ref, source_ref, k):
    route = jnp.broadcast_to(route_ref[k : k + 1, :], (H, route_ref.shape[1]))
    taken = source_ref[0:H, :]
    for e in range(1, E):
        taken = jnp.where(route == e, source_ref[e * H : (e + 1) * H, :], taken)
    return taken


def place_heads(route_ref, source_ref, e):
    total = jnp.zeros((H, route_ref.shape[1]), F32)
    for k in range(TOPK):
        route = jnp.broadcast_to(route_ref[k : k + 1, :], (H, route_ref.shape[1]))
        total = jnp.where(route == e, source_ref[k * H : (k + 1) * H, :], total)
    return total


def key_mask(first_key, first_query, rows, start_row):
    keys = lax.broadcasted_iota(jnp.int32, (rows, TB), 0) + first_key
    queries = lax.broadcasted_iota(jnp.int32, (rows, TB), 1) + first_query
    return (keys <= queries) & (keys >= start_row)


def head_forward_kernel(
    steps, x_ref, route_ref, segment_ref, wall_ref, gain_ref,
    q_ref, att_ref, gate_ref, lse_ref, kv_ref, kvt_ref, start_ref, count_ref,
    all_scr, k_scr, vt_scr, count_scr,
):
    step = pl.program_id(0)
    place = lax.rem(step, NB)
    here = pl.multiple_of(place * TB, TB)

    @pl.when(step == 0)
    def _():
        count_scr[...] = jnp.zeros_like(count_scr)

    row = segment_ref[pl.ds(lax.div(step, NB), 1), :]
    segments = segment_ref[pl.ds(lax.div(step, NB), 1), pl.ds(here, TB)]
    start = jnp.zeros((1, TB), jnp.int32)
    for number in range(1, 4):
        below = jnp.sum((row < number).astype(jnp.int32), axis=1, keepdims=True)
        start = jnp.where(segments == number, below, start)
    start_ref[...] = start
    x = x_ref[...].astype(F32)
    normed = (x * rms_scale(x) * gain_ref[...]).astype(BF16)
    all_scr[...] = nt(wall_ref[...], normed)
    kt = all_scr[KROW : KROW + H, :]
    vt = all_scr[VROW : VROW + H, :]
    logits = all_scr[RROW : RROW + E, :]
    kvt = jnp.concatenate([kt, vt], axis=0)
    kv = kvt.T.astype(BF16)
    kv_ref[...] = kv
    kvt_ref[...] = kvt.astype(BF16)
    k_scr[pl.ds(here, TB), :] = kv[:, :H]
    vt_scr[:, pl.ds(here, TB)] = vt.astype(BF16)
    routes = route_ref[...]
    experts = lax.broadcasted_iota(jnp.int32, (E, TB), 0)
    chosen = []
    counts = count_scr[...]
    for k in range(TOPK):
        named = slot_of(routes, k, E) == experts
        chosen.append(jnp.sum(jnp.where(named, logits, 0.0), axis=0, keepdims=True))
        counts = counts + named.astype(F32)
    count_scr[...] = counts
    chosen = jnp.concatenate(chosen, axis=0)
    raised = jnp.exp(chosen - jnp.max(chosen, axis=0, keepdims=True))
    gate_ref[...] = raised / jnp.sum(raised, axis=0, keepdims=True)
    for k in range(TOPK):
        query = pick_heads(route_ref, all_scr, k).astype(BF16)
        q_ref[k * H : (k + 1) * H, :] = query * jnp.asarray(H ** (-0.5), BF16)

    def attend(blocks):
        rows = blocks * TB
        first_key = pl.multiple_of((place - (blocks - 1)) * TB, TB)
        mask = key_mask(first_key, here, rows, start)
        keys = k_scr[pl.ds(first_key, rows), :]
        values = vt_scr[:, pl.ds(first_key, rows)]
        for k in range(TOPK):
            scores = jnp.where(mask, nn(keys, q_ref[k * H : (k + 1) * H, :]), NEG_LARGE)
            top = jnp.max(scores, axis=0, keepdims=True)
            raised = jnp.exp(scores - top)
            total = jnp.sum(raised, axis=0, keepdims=True)
            probs = (raised * (1.0 / total)).astype(BF16)
            att_ref[k * H : (k + 1) * H, :] = nn(values, probs)
            lse_ref[k : k + 1, :] = top + jnp.log(total)

    span = place - lax.div(jnp.min(start), TB) + 1
    for blocks in range(1, min(3, NB) + 1):

        @pl.when(span == blocks)
        def _(blocks=blocks):
            attend(blocks)

    @pl.when(step == steps - 1)
    def _():
        held = jnp.sum(count_scr[...], axis=1, keepdims=True)
        lane = lax.broadcasted_iota(jnp.int32, (E, 128), 1)
        row = lax.broadcasted_iota(jnp.int32, (E, 128), 0)
        count_ref[...] = jnp.sum(jnp.where(lane == row, held, 0.0), axis=0, keepdims=True)


def picks(rows, stride, first):
    at = lax.broadcasted_iota(jnp.int32, (rows, D), 1)
    row = lax.broadcasted_iota(jnp.int32, (rows, D), 0)
    return (at == row * stride + first).astype(F32)


def exact(product, a, b):
    return lax.dot_general(
        a, b, (product, ((), ())), precision=lax.Precision.HIGHEST, preferred_element_type=F32
    )


def gelu_parts(v):
    size = jnp.abs(v) * 0.7071067811865476
    bell = jnp.exp(-(size * size))
    t = 1.0 / (1.0 + 0.3275911 * size)
    series = t * (
        0.254829592
        + t * (-0.284496736 + t * (1.421413741 + t * (-1.453152027 + t * 1.061405429)))
    )
    tail = 0.5 * series * bell
    cdf = jnp.where(v < 0.0, tail, 1.0 - tail)
    return cdf, bell * 0.3989422804014327


def middle_kernel(
    shard_size, early, many, x_ref, dy_ref, gain_ref, tail_ref, land_ref, route_ref, gate_ref, att_ref,
    out_ref, dres_ref, datt_ref, delta_ref, dlogit_ref, flat_ref, extra_ref, dgain_ref,
    slot_scr, head_scr, mix_scr, dwo_ref, dw1_ref, dw2t_ref, wo_ref, w1_ref, w2_ref, rows_scr,
    row_sem,
):
    step = pl.program_id(0)

    @pl.when(step == 0)
    def _():
        rows_scr[0 : tail_ref.shape[0], :] = tail_ref[...]
        lay_blocks(shard_size, land_ref, rows_scr, early, many, WO_ROW)
        late_matrices(rows_scr, wo_ref, w1_ref, w2_ref)
        dwo_ref[...] = jnp.zeros_like(dwo_ref)
        dw1_ref[...] = jnp.zeros_like(dw1_ref)
        dw2t_ref[...] = jnp.zeros_like(dw2t_ref)
        dgain_ref[...] = jnp.zeros_like(dgain_ref)

    routes = route_ref[...]
    tokens = routes.shape[1]
    gates = gate_ref[...]
    for k in range(TOPK):
        slot_scr[k * H : (k + 1) * H, :] = gates[k : k + 1, :] * att_ref[k * H : (k + 1) * H, :]
    for e in range(E):
        mix_scr[e * H : (e + 1) * H, :] = place_heads(route_ref, slot_scr, e).astype(BF16)
    x = x_ref[...].astype(F32)
    dy = dy_ref[...]
    mixed = mix_scr[...]
    residual = x + tn(mixed, wo_ref[...])
    scale = rms_scale(residual)
    gain = gain_ref[...]
    second = (residual * scale * gain).astype(BF16)
    second_t = second.T
    dy_t = dy.T
    out = residual
    dsecond = jnp.zeros((tokens, D), F32)
    for c in range(0, FF, FC):
        up = w1_ref[:, c : c + FC]
        down = w2_ref[c : c + FC, :]
        pre = nn(second, up)
        cdf, density = gelu_parts(pre)
        hidden = (pre * cdf).astype(BF16)
        dpre = (nt(dy, down) * (cdf + pre * density)).astype(BF16)
        out = out + nn(hidden, down)
        dsecond = dsecond + nt(dpre, up)
        dw2t_ref[:, c : c + FC] += nn(dy_t, hidden)
        dw1_ref[:, c : c + FC] += nn(second_t, dpre)
    out_ref[...] = out.astype(BF16)
    dgain_ref[...] += jnp.sum(dsecond * residual * scale, axis=0, keepdims=True)
    weighted = gain * dsecond
    dres = (
        dy.astype(F32)
        + scale * weighted
        - residual * (scale * scale * scale) * jnp.mean(weighted * residual, axis=-1, keepdims=True)
    )
    dres_ref[...] = dres
    branch = dres.astype(BF16)
    dwo_ref[...] += nn(mixed, branch)
    head_scr[...] = nt(wo_ref[...], branch).astype(BF16).astype(F32)
    dgates = []
    for k in range(TOPK):
        rows = slice(k * H, (k + 1) * H)
        dslot = pick_heads(route_ref, head_scr, k)
        attended = att_ref[rows, :]
        dgates.append(jnp.sum(dslot * attended, axis=0, keepdims=True))
        datt = (gates[k : k + 1, :] * dslot).astype(BF16)
        datt_ref[rows, :] = datt
        delta_ref[k : k + 1, :] = jnp.sum(datt.astype(F32) * attended, axis=0, keepdims=True)
    dgate = jnp.concatenate(dgates, axis=0)
    dchosen = gates * (dgate - jnp.sum(gates * dgate, axis=0, keepdims=True))
    experts = lax.broadcasted_iota(jnp.int32, (E, tokens), 0)
    dlogits = jnp.zeros((E, tokens), F32)
    for k in range(TOPK):
        dlogits = jnp.where(
            slot_of(routes, k, E) == experts,
            jnp.broadcast_to(dchosen[k : k + 1, :], (E, tokens)),
            dlogits,
        )
    dlogit_ref[...] = dlogits

    @pl.when(step == pl.num_programs(0) - 1)
    def _():
        for c in range(D // 128):
            lanes = slice(c * 128, (c + 1) * 128)
            rows_scr[pl.ds(c, QW, stride=4), :] = dwo_ref[:, lanes]
            rows_scr[pl.ds(W2_ROW - WO_ROW + c, FF, stride=4), :] = dw2t_ref[lanes, :].T
        for c in range(FF // 128):
            rows_scr[pl.ds(W1_ROW - WO_ROW + c, D, stride=16), :] = dw1_ref[:, c * 128 : (c + 1) * 128]
        extra_ref[...] = rows_scr[0 : extra_ref.shape[0], :]
        copy = pltpu.make_async_copy(rows_scr, flat_ref, row_sem.at[0])
        copy.start()
        copy.wait()


def head_backward_kernel(
    x_ref, gain_ref, wall_ref, route_ref, start_ref, q_ref, datt_ref,
    lse_ref, delta_ref, kv_ref, kvt_ref, dlogit_ref, dres_ref, dgain_two_ref, extra_ref,
    dx_ref, flat_ref,
    dk_scr, dv_scr, dq_scr, dall_scr, dwall_ref, dgain_ref, rows_scr, row_sem,
):
    step = pl.program_id(0)
    place = NB - 1 - lax.rem(step, NB)
    here = pl.multiple_of(place * TB, TB)

    @pl.when(step == 0)
    def _():
        dwall_ref[...] = jnp.zeros_like(dwall_ref)
        dgain_ref[...] = jnp.zeros_like(dgain_ref)

    @pl.when(lax.rem(step, NB) == 0)
    def _():
        dk_scr[...] = jnp.zeros_like(dk_scr)
        dv_scr[...] = jnp.zeros_like(dv_scr)

    def attend(blocks):
        rows = blocks * TB
        first_key = pl.multiple_of((place - (blocks - 1)) * TB, TB)
        mask = key_mask(first_key, here, rows, start_ref[...])
        keys = kv_ref[pl.ds(first_key, rows), :H]
        values = kv_ref[pl.ds(first_key, rows), H:]
        keys_t = kvt_ref[:H, pl.ds(first_key, rows)]
        dk = jnp.zeros((rows, H), F32)
        dv = jnp.zeros((rows, H), F32)
        for k in range(TOPK):
            part = slice(k * H, (k + 1) * H)
            query = q_ref[part, :]
            datt = datt_ref[part, :]
            scores = jnp.where(mask, nn(keys, query), NEG_LARGE)
            probs = jnp.exp(scores - lse_ref[k : k + 1, :])
            dscore = (probs * (nn(values, datt) - delta_ref[k : k + 1, :])).astype(BF16)
            dv = dv + nt(probs.astype(BF16), datt)
            dk = dk + nt(dscore, query)
            dq_scr[part, :] = nn(keys_t, dscore) * (H ** (-0.5))
        dk_scr[pl.ds(first_key, rows), :] += dk
        dv_scr[pl.ds(first_key, rows), :] += dv

    span = place - lax.div(jnp.min(start_ref[...]), TB) + 1
    for blocks in range(1, min(3, NB) + 1):

        @pl.when(span == blocks)
        def _(blocks=blocks):
            attend(blocks)

    for e in range(E):
        dall_scr[e * H : (e + 1) * H, :] = place_heads(route_ref, dq_scr, e).astype(BF16)
    dkv = jnp.concatenate([dk_scr[pl.ds(here, TB), :], dv_scr[pl.ds(here, TB), :]], axis=1)
    dall_scr[KROW : KROW + 2 * H, :] = dkv.T.astype(BF16)
    dall_scr[RROW : RROW + 32, :] = jnp.concatenate(
        [dlogit_ref[...], jnp.zeros((32 - E, TB), F32)], axis=0
    ).astype(BF16)
    x = x_ref[...].astype(F32)
    scale = rms_scale(x)
    gain = gain_ref[...]
    normed = (x * scale * gain).astype(BF16)
    dall = dall_scr[...]
    dwall_ref[...] += nn(dall, normed)
    dnormed = tn(dall, wall_ref[...])
    dgain_ref[...] += jnp.sum(dnormed * x * scale, axis=0, keepdims=True)
    weighted = gain * dnormed
    dx_ref[...] = (
        dres_ref[...]
        + scale * weighted
        - x * (scale * scale * scale) * jnp.mean(weighted * x, axis=-1, keepdims=True)
    )

    @pl.when(step == pl.num_programs(0) - 1)
    def _():
        for c in range(D // 128):
            lanes = slice(c * 128, (c + 1) * 128)
            rows_scr[c : c + 1, :] = dgain_ref[:, lanes]
            rows_scr[4 + c : 5 + c, :] = dgain_two_ref[:, lanes]
        router_t = dwall_ref[RROW : RROW + E, :]
        across = jnp.concatenate(
            [exact(((1,), (1,)), router_t, picks(32, 16, b)) for b in range(16)], axis=0
        ).T
        for j in range(3):
            rows_scr[pl.ds(WR_ROW + j, 32, stride=3), :] = across[:, j * 128 : (j + 1) * 128]
        for first, row in ((KROW, WK_ROW), (VROW, WV_ROW)):
            part = dwall_ref[first : first + H, :]
            rows_scr[row : row + 256, :] = jnp.concatenate(
                [exact(((1,), (1,)), picks(256, 2, b), part) for b in range(2)], axis=1
            )
        for c in range(QW // 128):
            rows_scr[pl.ds(WQ_ROW + c, D, stride=12), :] = dwall_ref[c * 128 : (c + 1) * 128, :].T
        extra = extra_ref.shape[0]
        rows_scr[WO_ROW : WO_ROW + extra, :] = extra_ref[...]
        copy = pltpu.make_async_copy(rows_scr, flat_ref, row_sem.at[0])
        copy.start()
        copy.wait()


def whole(shape):
    return pl.BlockSpec(shape, lambda *_: (0,) * len(shape), pipeline_mode=pl.Buffered(1))


def kept(shape):
    return pl.BlockSpec(shape, lambda *_: (0,) * len(shape))


def struct(shape, kind=F32):
    return jax.ShapeDtypeStruct(shape, kind)


def params_for(mib):
    return pltpu.CompilerParams(vmem_limit_bytes=mib * MIB)


def head_forward(tokens, routes_t, segments, wall, gain):
    count = tokens.shape[0]
    steps = count // TB
    across = lambda rows: pl.BlockSpec((rows, TB), lambda b: (0, b))
    down = lambda columns: pl.BlockSpec((TB, columns), lambda b: (b, 0))
    return pl.pallas_call(
        functools.partial(head_forward_kernel, steps),
        grid=(steps,),
        in_specs=[down(D), across(TOPK), whole(segments.shape), whole((ALLW, D)), whole((1, D))],
        out_specs=[
            across(TOPK * H), across(TOPK * H), across(TOPK), across(TOPK), down(2 * H), across(2 * H),
            across(1), whole((1, 128)),
        ],
        scratch_shapes=[
            pltpu.VMEM((ALLW, TB), F32),
            pltpu.VMEM((LEN, H), BF16),
            pltpu.VMEM((H, LEN), BF16),
            pltpu.VMEM((E, TB), F32),
        ],
        out_shape=[
            struct((TOPK * H, count), BF16),
            struct((TOPK * H, count)),
            struct((TOPK, count)),
            struct((TOPK, count)),
            struct((count, 2 * H), BF16),
            struct((2 * H, count), BF16),
            struct((1, count), jnp.int32),
            struct((1, 128)),
        ],
        compiler_params=params_for(56),
        name="head_forward",
        cost_estimate=pl.CostEstimate(flops=10_000_000_000, bytes_accessed=16_000_000, transcendentals=0),
    )(tokens, routes_t, segments, wall, gain)


def middle(shard_size, early, many, tokens, grad_out, gain, tail, land, routes_t, gates, attended):
    count = tokens.shape[0]
    steps = count // TB
    window = land.shape[1]
    rows = (shard_size * (many - 1)) // UNIT * 16 + window - WO_ROW
    across = lambda rows: pl.BlockSpec((rows, TB), lambda b: (0, b))
    down = lambda columns: pl.BlockSpec((TB, columns), lambda b: (b, 0))
    return pl.pallas_call(
        functools.partial(middle_kernel, shard_size, early, many),
        grid=(steps,),
        in_specs=[
            down(D), down(D), whole((1, D)), whole(tail.shape), whole(land.shape),
            across(TOPK), across(TOPK), across(TOPK * H),
        ],
        out_specs=[
            down(D), down(D), across(TOPK * H), across(TOPK), across(E),
            pl.BlockSpec(memory_space=pl.ANY), whole(tail.shape), whole((1, D)),
        ],
        out_shape=[
            struct((count, D), BF16),
            struct((count, D)),
            struct((TOPK * H, count), BF16),
            struct((TOPK, count)),
            struct((E, count)),
            struct((rows, 128)),
            struct(tail.shape),
            struct((1, D)),
        ],
        scratch_shapes=[
            pltpu.VMEM((TOPK * H, TB), F32),
            pltpu.VMEM((QW, TB), F32),
            pltpu.VMEM((QW, TB), BF16),
            pltpu.VMEM((QW, D), F32),
            pltpu.VMEM((D, FF), F32),
            pltpu.VMEM((D, FF), F32),
            pltpu.VMEM((QW, D), BF16),
            pltpu.VMEM((D, FF), BF16),
            pltpu.VMEM((FF, D), BF16),
            pltpu.VMEM((rows, 128), F32),
            pltpu.SemaphoreType.DMA((1,)),
        ],
        compiler_params=params_for(60),
        name="middle",
        cost_estimate=pl.CostEstimate(flops=40_000_000_000, bytes_accessed=32_000_000, transcendentals=0),
    )(tokens, grad_out, gain, tail, land, routes_t, gates, attended)


def head_backward(
    tokens, gain, wall, routes_t, start, queries, datt, lse, delta, kv, kvt, dlogits, dres, dgain_two, extra
):
    count = tokens.shape[0]
    steps = count // TB
    early_rows = WO_ROW + extra.shape[0]

    def place(b):
        return (b // NB) * NB + NB - 1 - b % NB

    across = lambda rows: pl.BlockSpec((rows, TB), lambda b: (0, place(b)))
    down = lambda columns: pl.BlockSpec((TB, columns), lambda b: (place(b), 0))
    return pl.pallas_call(
        head_backward_kernel,
        grid=(steps,),
        in_specs=[
            down(D), whole((1, D)), whole((ALLW, D)), across(TOPK), across(1),
            across(TOPK * H), across(TOPK * H), across(TOPK), across(TOPK),
            pl.BlockSpec((LEN, 2 * H), lambda b: (b // NB, 0)),
            pl.BlockSpec((2 * H, LEN), lambda b: (0, b // NB)),
            across(E), down(D), whole((1, D)), whole(extra.shape),
        ],
        out_specs=[down(D), pl.BlockSpec(memory_space=pl.ANY)],
        scratch_shapes=[
            pltpu.VMEM((LEN, H), F32),
            pltpu.VMEM((LEN, H), F32),
            pltpu.VMEM((TOPK * H, TB), F32),
            pltpu.VMEM((ALLW, TB), BF16),
            pltpu.VMEM((ALLW, D), F32),
            pltpu.VMEM((1, D), F32),
            pltpu.VMEM((early_rows, 128), F32),
            pltpu.SemaphoreType.DMA((1,)),
        ],
        out_shape=[struct((count, D)), struct((early_rows, 128))],
        compiler_params=params_for(56),
        name="head_backward",
        cost_estimate=pl.CostEstimate(flops=30_000_000_000, bytes_accessed=24_000_000, transcendentals=0),
    )(
        tokens, gain, wall, routes_t, start, queries, datt, lse, delta, kv, kvt, dlogits, dres,
        dgain_two, extra,
    )


class Mesh3:
    def __init__(self, shards, over):
        shard = lax.axis_index("dp")
        other = lax.axis_index("fsdp")
        self.over = over
        self.many = shards * over
        self.sizes = {"x": 2, "y": shards // 2, "z": over // 2}
        self.here = {"x": lax.rem(other, 2), "y": lax.div(shard, 2), "z": lax.div(other, 2)}
        self.core = lax.rem(shard, 2)
        self.me = shard * over + other
        self.partner = (shard + 1 - 2 * self.core, other)

    def moved(self, steps):
        return {
            axis: lax.rem(self.here[axis] + steps.get(axis, 0), self.sizes[axis]) for axis in "xyz"
        }

    def device(self, core, steps):
        at = self.moved(steps)
        return (at["y"] * 2 + core, at["z"] * 2 + at["x"])

    def number(self, core, steps):
        shard, other = self.device(core, steps)
        return shard * self.over + other

    def nth(self, number):
        return (lax.div(number, self.over), lax.rem(number, self.over))

    def greet_near(self):
        devices = [
            self.device(self.core, {axis: step})
            for axis in "xyz"
            for step in range(1, self.sizes[axis])
        ] + [self.partner]
        barrier = pltpu.get_barrier_semaphore()
        for device in devices:
            pl.semaphore_signal(barrier, inc=1, device_id=device, device_id_type=MESH)
        pl.semaphore_wait(barrier, len(devices))

    def greet_all(self):
        barrier = pltpu.get_barrier_semaphore()

        def hello(j, carry):
            device = self.nth(lax.rem(self.me + j, self.many))
            pl.semaphore_signal(barrier, inc=1, device_id=device, device_id_type=MESH)
            return carry

        lax.fori_loop(1, self.many, hello, 0)
        pl.semaphore_wait(barrier, self.many - 1)


def along_z(step):
    return {1: (0, 3), 2: (1, 5), 3: (3, 8)}.get(step, (step, 2 * step + 2))


class Kind:
    def __init__(self, mesh, core, axes):
        self.mesh = mesh
        self.core = core
        self.axes = axes
        ranges = [range(mesh.sizes[axis]) for axis in axes]
        self.offsets = list(itertools.product(*ranges))
        self.index = {one: number for number, one in enumerate(self.offsets)}

    def owner(self, offsets):
        return self.mesh.number(self.core, dict(zip(self.axes, offsets)))

    def last(self, offsets):
        return max([i for i in range(3) if offsets[i]], default=-1)

    def turn(self, offsets):
        total = 0
        for axis, step in zip(self.axes, offsets):
            if step:
                total += along_z(step)[1] if axis == "z" else 2
        return total

    def hops(self, offsets):
        for i in range(self.last(offsets) + 1, 3):
            for step in range(1, self.mesh.sizes[self.axes[i]]):
                delay = along_z(step)[0] if self.axes[i] == "z" else 0
                yield i, step, self.turn(offsets) + delay

    def ahead(self, i, step):
        return self.mesh.device(self.core, {self.axes[i]: step})


GATHER_AXES = ("yzx", "zxy")
REDUCE_AXES = ("zxy", "zyx")


def gather_events(mesh, wanted, own_ref, land, send_sem, recv_sem):
    events = []
    many = mesh.many
    kinds = [Kind(mesh, core, GATHER_AXES[core]) for core in range(2)]
    end = max(kind.turn(one) for kind in kinds for one in kind.offsets) + 2

    def copy(owner, device, slot):
        return pltpu.make_async_remote_copy(
            src_ref=land.at[owner],
            dst_ref=land.at[owner],
            send_sem=send_sem.at[slot],
            recv_sem=recv_sem.at[owner],
            device_id=device,
            device_id_type=MESH,
        )

    def event(turn, condition, action):
        events.append((turn, lambda: pl.when(condition)(action)))

    for kind in kinds:
        slots = itertools.count()
        for offsets in kind.offsets:
            owner = kind.owner(offsets)
            ours = (mesh.core == kind.core) & wanted(owner)
            theirs = (mesh.core != kind.core) & wanted(owner)
            slot = next(slots)

            def come(owner=owner, offsets=offsets, slot=slot):
                if any(offsets):
                    copy(owner, mesh.partner, slot).wait_recv()
                else:
                    land[owner] = own_ref[...]
                copy(owner, mesh.partner, slot).start()

            def across(owner=owner, slot=slot):
                copy(owner, mesh.partner, slot).wait_recv()

            def done(owner=owner, slot=slot):
                copy(owner, mesh.partner, slot).wait_send()

            event(kind.turn(offsets), ours, come)
            event(end, theirs, across)
            event(end, ours, done)
            for i, step, turn in kind.hops(offsets):
                slot = next(slots)
                device = kind.ahead(i, step)

                def send(owner=owner, device=device, slot=slot):
                    copy(owner, device, slot).start()

                def sent(owner=owner, device=device, slot=slot):
                    copy(owner, device, slot).wait_send()

                event(turn, ours, send)
                event(end, ours, sent)
    return sorted(events, key=lambda one: one[0])


def reduce_events(mesh, wanted, load, outgo, income, send_sem, recv_sem, finish):
    events = []
    half = mesh.many // 2
    kinds = [Kind(mesh, core, REDUCE_AXES[core]) for core in range(2)]
    end = max(kind.turn(one) for kind in kinds for one in kind.offsets) + 2

    def copy(slot, device):
        return pltpu.make_async_remote_copy(
            src_ref=outgo.at[slot],
            dst_ref=income.at[slot],
            send_sem=send_sem.at[slot],
            recv_sem=recv_sem.at[slot],
            device_id=device,
            device_id_type=MESH,
        )

    def event(turn, condition, action):
        events.append((turn, lambda: pl.when(condition)(action)))

    def sends(slot, device, values):
        outgo[slot] = values.astype(BF16)
        copy(slot, device).start()

    def taken(slot):
        copy(slot, mesh.partner).wait_recv()
        return income[slot].astype(F32)

    for kind in kinds:
        slots = {}
        for offsets in kind.offsets:
            if any(offsets):
                slots[offsets] = half + len(slots)
        for offsets in kind.offsets:
            owner = kind.owner(offsets)
            ours = (mesh.core == kind.core) & wanted(owner)
            theirs = (mesh.core != kind.core) & wanted(owner)
            number = kind.index[offsets]
            axis = kind.last(offsets)
            turn = end - kind.turn(offsets)

            def hand(owner=owner, number=number):
                sends(number, mesh.partner, load(owner))

            def handed(number=number):
                copy(number, mesh.partner).wait_send()

            def onward(owner=owner, offsets=offsets, number=number, axis=axis, kind=kind, slots=slots):
                total = load(owner) + taken(number)
                for i, step, _ in kind.hops(offsets):
                    longer = tuple(step if j == i else o for j, o in enumerate(offsets))
                    total = total + taken(slots[longer])
                if axis < 0:
                    finish(total)
                else:
                    sends(slots[offsets], kind.ahead(axis, offsets[axis]), total)

            event(turn - 2, theirs, hand)
            event(end + 1, theirs, handed)
            event(turn, ours, onward)
            if axis >= 0:

                def passed(slot=slots[offsets]):
                    copy(slot, mesh.partner).wait_send()

                event(end + 1, ours, passed)
    return sorted(events, key=lambda one: one[0])


def at_polls(events, polls):
    last = events[-1][0]
    spread = [[] for _ in range(polls)]
    for turn, action in events:
        spread[turn if last < polls else turn * (polls - 1) // last].append(action)
    return spread


def poll(step, half, spread):
    for number in range(len(spread) // 2):
        actions = spread[2 * number + half]
        if actions:

            @pl.when(step == number)
            def _(actions=actions):
                for action in actions:
                    action()


def window_rows(shard_size, many):
    units = [(shard_size * d) // UNIT for d in range(many + 1)]
    return 16 * (max(b - a for a, b in zip(units, units[1:])) + 1)


def first_row(shard_size, number):
    if isinstance(number, int):
        return number * shard_size // UNIT * 16
    return pl.multiple_of(lax.div(number * shard_size, UNIT) * 16, 16)


def early_owners(shard_size, over):
    group = shard_size * over
    return -(-(WO_ROW * 128) // group) * over


def lay_blocks(shard_size, land, flat, first, last, origin):
    window = land.shape[1]

    def lay(number, carry):
        row = pl.multiple_of(first_row(shard_size, number) - origin, 8)
        flat[pl.ds(row, 16), :] += land[number, 0:16, :].astype(F32)
        flat[pl.ds(row + 16, window - 16), :] = land[number, 16:window, :].astype(F32)
        return carry

    lax.fori_loop(first, last, lay, 0)


def early_matrices(flat, wall_ref, gain_one_ref, gain_two_ref):
    for c in range(D // 128):
        lanes = slice(c * 128, (c + 1) * 128)
        gain_one_ref[:, lanes] = flat[c : c + 1, :]
        gain_two_ref[:, lanes] = flat[4 + c : 5 + c, :]
    for c in range(QW // 128):
        wall_ref[c * 128 : (c + 1) * 128, :] = flat[pl.ds(WQ_ROW + c, D, stride=12), :].T.astype(BF16)
    for first, row in ((KROW, WK_ROW), (VROW, WV_ROW)):
        pair = flat[row : row + 256, :].T.astype(BF16)
        wall_ref[first : first + H, :] = (
            nn(pair[:H], picks(256, 2, 0).astype(BF16)) + nn(pair[H:], picks(256, 2, 1).astype(BF16))
        ).astype(BF16)
    across = jnp.concatenate(
        [flat[pl.ds(WR_ROW + j, 32, stride=3), :] for j in range(3)], axis=1
    ).T.astype(BF16)
    router_t = jnp.zeros((E, D), F32)
    for part in range(16):
        router_t = router_t + nn(across[part * E : (part + 1) * E, :], picks(32, 16, part).astype(BF16))
    wall_ref[RROW:ALLW, :] = jnp.concatenate(
        [router_t, jnp.zeros((ALLW - RROW - E, D), F32)], axis=0
    ).astype(BF16)


def late_matrices(flat, wo_ref, w1_ref, w2_ref):
    for c in range(D // 128):
        lanes = slice(c * 128, (c + 1) * 128)
        wo_ref[:, lanes] = flat[pl.ds(c, QW, stride=4), :].astype(BF16)
        w2_ref[:, lanes] = flat[pl.ds(W2_ROW - WO_ROW + c, FF, stride=4), :].astype(BF16)
    for c in range(FF // 128):
        w1_ref[:, c * 128 : (c + 1) * 128] = flat[
            pl.ds(W1_ROW - WO_ROW + c, D, stride=16), :
        ].astype(BF16)


def gather_kernel(
    mesh, shard_size, early, own_ref,
    wall_ref, gain_one_ref, gain_two_ref, tail_ref,
    land, flat, send_sem, recv_sem,
):
    mesh = mesh()
    mesh.greet_near()
    for _, action in gather_events(mesh, lambda owner: owner < early, own_ref, land, send_sem, recv_sem):
        action()
    flat[0:16, :] = jnp.zeros((16, 128), F32)
    lay_blocks(shard_size, land, flat, 0, early, 0)
    early_matrices(flat, wall_ref, gain_one_ref, gain_two_ref)
    tail_ref[...] = flat[WO_ROW : WO_ROW + tail_ref.shape[0], :]


def gather_early(shards, over, shard_size, own):
    window = own.shape[0]
    early = early_owners(shard_size, over)
    rows = (shard_size * (early - 1)) // UNIT * 16 + window
    vmem = pl.BlockSpec(memory_space=pltpu.VMEM)
    mesh = functools.partial(Mesh3, shards, over)
    return pl.pallas_call(
        functools.partial(gather_kernel, mesh, shard_size, early),
        in_specs=[vmem],
        out_specs=[vmem] * 4,
        out_shape=[
            struct((ALLW, D), BF16),
            struct((1, D)),
            struct((1, D)),
            struct((rows - WO_ROW, 128)),
        ],
        scratch_shapes=[
            pltpu.VMEM((early, window, 128), BF16),
            pltpu.VMEM((rows, 128), F32),
            pltpu.SemaphoreType.DMA((shards * over,)),
            pltpu.SemaphoreType.DMA((early,)),
        ],
        compiler_params=pltpu.CompilerParams(
            collective_id=0, has_side_effects=True, vmem_limit_bytes=56 * MIB
        ),
        name="gather_early",
        cost_estimate=pl.CostEstimate(flops=0, bytes_accessed=60_000_000, transcendentals=0),
    )(own)


def reduce_kernel(
    mesh, shard_size, early, flat_ref, late_ref, count_ref,
    out_ref, total_ref, gain_ref,
    part, outgo, income, stats, gains, part_sem, send_sem, recv_sem, stat_send, stat_recv, gain_send, gain_recv,
):
    mesh = mesh()
    many = mesh.many
    window = out_ref.shape[0]

    def piece(owner):
        row = first_row(shard_size, owner)
        if owner < early:
            source = flat_ref.at[pl.ds(row, window), :]
        else:
            source = late_ref.at[pl.ds(row - WO_ROW, window), :]
        return pltpu.make_async_copy(source, part.at[owner], part_sem.at[owner])

    for owner in range(many):
        piece(owner).start()
    mesh.greet_all()

    def finish(total):
        out_ref[...] = total

    def block(owner):
        pltpu.make_async_copy(
            flat_ref.at[pl.ds(0, window), :], part.at[owner], part_sem.at[owner]
        ).wait()
        return part[owner]

    for _, action in reduce_events(
        mesh, lambda owner: True, block, outgo, income, send_sem, recv_sem, finish
    ):
        action()
    total = out_ref[...]
    begin = mesh.me * shard_size - lax.div(mesh.me * shard_size, UNIT) * UNIT
    at = (
        lax.broadcasted_iota(jnp.int32, (window, 128), 0) * 128
        + lax.broadcasted_iota(jnp.int32, (window, 128), 1)
    )
    inside = jnp.where((at >= begin) & (at < begin + shard_size), total, 0.0)
    squares = jnp.sum(jnp.sum(inside * inside, axis=0, keepdims=True), axis=1, keepdims=True)
    lane = lax.broadcasted_iota(jnp.int32, (1, 128), 1)
    stats[0] = jnp.where(lane == E, squares, count_ref[...])

    def told(j):
        return pltpu.make_async_remote_copy(
            src_ref=stats.at[0],
            dst_ref=stats.at[j],
            send_sem=stat_send.at[j],
            recv_sem=stat_recv.at[j],
            device_id=mesh.nth(lax.rem(mesh.me + j, many)),
            device_id_type=MESH,
        )

    def shown(j):
        return pltpu.make_async_remote_copy(
            src_ref=gains,
            dst_ref=gains,
            send_sem=gain_send.at[j],
            recv_sem=gain_recv.at[0],
            device_id=mesh.nth(lax.rem(mesh.me + j, many)),
            device_id_type=MESH,
        )

    def tell(j, carry):
        told(j).start()
        return carry

    def hear(j, carry):
        told(j).wait()
        return carry

    def show(j, carry):
        shown(j).start()
        return carry

    def showed(j, carry):
        shown(j).wait_send()
        return carry

    lax.fori_loop(1, many, tell, 0)

    @pl.when(mesh.me == 0)
    def _():
        gains[...] = total[0:8, :]
        lax.fori_loop(1, many, show, 0)
        lax.fori_loop(1, many, showed, 0)

    @pl.when(mesh.me != 0)
    def _():
        shown(1).wait_recv()

    lax.fori_loop(1, many, hear, 0)
    total_ref[...] = jnp.sum(stats[...], axis=0)
    gain_ref[...] = gains[...]


def reduce_grads(shards, over, shard_size, window, flat, late, counts):
    vmem = pl.BlockSpec(memory_space=pltpu.VMEM)
    many = shards * over
    early = early_owners(shard_size, over)
    mesh = functools.partial(Mesh3, shards, over)
    return pl.pallas_call(
        functools.partial(reduce_kernel, mesh, shard_size, early),
        in_specs=[pl.BlockSpec(memory_space=pl.ANY), pl.BlockSpec(memory_space=pl.ANY), vmem],
        out_specs=[vmem] * 3,
        out_shape=[struct((window, 128)), struct((1, 128)), struct((8, 128))],
        scratch_shapes=[
            pltpu.VMEM((many, window, 128), F32),
            pltpu.VMEM((many, window, 128), BF16),
            pltpu.VMEM((many, window, 128), BF16),
            pltpu.VMEM((many, 1, 128), F32),
            pltpu.VMEM((8, 128), F32),
            pltpu.SemaphoreType.DMA((many,)),
            pltpu.SemaphoreType.DMA((many,)),
            pltpu.SemaphoreType.DMA((many,)),
            pltpu.SemaphoreType.DMA((many,)),
            pltpu.SemaphoreType.DMA((many,)),
            pltpu.SemaphoreType.DMA((many,)),
            pltpu.SemaphoreType.DMA((1,)),
        ],
        compiler_params=pltpu.CompilerParams(
            collective_id=1, has_side_effects=True, vmem_limit_bytes=56 * MIB
        ),
        name="reduce_grads",
    )(flat, late, counts)


def per_device(
    shards, over, tokens, grad_out, routes, segments, params, first_moment, second_moment, ema_weights
):
    shard_size = params.shape[0]
    window = window_rows(shard_size, shards * over)
    early = early_owners(shard_size, over)
    me = lax.axis_index("dp") * over + lax.axis_index("fsdp")
    begin = lax.rem(me * shard_size, UNIT)
    own = lax.dynamic_slice(
        jnp.pad(params.astype(BF16), (UNIT, window * 128 - shard_size)), (UNIT - begin,), (window * 128,)
    ).reshape(window, 128)
    routes_t = routes.T
    wall, gain_one, gain_two, tail = gather_early(shards, over, shard_size, own)
    land = lax.all_gather(own, ("dp", "fsdp"), axis=0, tiled=True).reshape(-1, window, 128)
    queries, attended, gates, lse, kv, kvt, start, counts = head_forward(
        tokens, routes_t, segments, wall, gain_one
    )
    output, dres, datt, delta, dlogits, late, extra, dgain_two = middle(
        shard_size, early, shards * over, tokens, grad_out, gain_two, tail, land, routes_t, gates, attended
    )
    input_grad, flat = head_backward(
        tokens, gain_one, wall, routes_t, start, queries, datt, lse, delta, kv, kvt, dlogits, dres,
        dgain_two, extra,
    )
    reduced, sums, gain_grads = reduce_grads(shards, over, shard_size, window, flat, late, counts)
    grad_shard = lax.dynamic_slice(reduced.reshape(-1), (begin,), (shard_size,))
    total_tokens = tokens.shape[0] * shards * over
    expert_load = sums[0, :E] * (E / (total_tokens * TOPK))
    grad_norm = jnp.sqrt(sums[0, E])
    clipped = grad_shard * (CLIP_LIMIT / jnp.maximum(grad_norm, CLIP_LIMIT))
    new_first = BETA_FIRST * first_moment + (1.0 - BETA_FIRST) * clipped
    new_second = BETA_SECOND * second_moment + (1.0 - BETA_SECOND) * clipped * clipped
    first_hat = new_first / (1.0 - BETA_FIRST**STEP)
    second_hat = new_second / (1.0 - BETA_SECOND**STEP)
    new_params = params * (1.0 - LEARN_RATE * DECAY_RATE) - LEARN_RATE * first_hat / (
        jnp.sqrt(second_hat) + ADAM_EPS
    )
    new_ema = EMA_KEEP * ema_weights + (1.0 - EMA_KEEP) * new_params
    return (
        output,
        input_grad,
        expert_load,
        grad_norm.reshape(1),
        new_params,
        new_first,
        new_second,
        new_ema,
        gain_grads.reshape(2, D),
    )


def solution(mesh):
    row = P(("dp", "fsdp"), None)
    flat = P(("dp", "fsdp"))
    return jax.shard_map(
        functools.partial(per_device, mesh.shape["dp"], mesh.shape["fsdp"]),
        mesh=mesh,
        in_specs=(row, row, row, row, flat, flat, flat, flat),
        out_specs=(row, row, P(), P(), flat, flat, flat, flat, P()),
        check_vma=False,
    )
```

```python
import functools
import itertools

import jax
import jax.numpy as jnp
from jax import lax
from jax.experimental import pallas as pl
from jax.experimental.pallas import tpu as pltpu
from jax.sharding import PartitionSpec as P

D = 512
E = 24
TOPK = 8
H = 64
FF = 2048
STEP = 10

NORM_EPS = 1e-06
CLIP_LIMIT = 1.0
BETA_FIRST = 0.9
BETA_SECOND = 0.95
LEARN_RATE = 0.1
DECAY_RATE = 0.1
ADAM_EPS = 1e-08
EMA_KEEP = 0.9
NEG_LARGE = -1e30

QW = E * H
KROW = QW
VROW = QW + H
RROW = QW + 2 * H
ALLW = 1696
LEN = 1024
TB = 256
NB = LEN // TB
FC = 512
MIB = 1 << 20

WR_ROW = 8
WK_ROW = 104
WV_ROW = 360
WQ_ROW = 616
WO_ROW = 6760
W1_ROW = 12904
W2_ROW = 21096
ALL_ROWS = 29288
UNIT = 16 * 128
MESH = pl.DeviceIdType.MESH

F32 = jnp.float32
BF16 = jnp.bfloat16


def nn(a, b):
    return lax.dot_general(a, b, (((1,), (0,)), ((), ())), preferred_element_type=F32)


def nt(a, b):
    return lax.dot_general(a, b, (((1,), (1,)), ((), ())), preferred_element_type=F32)


def tn(a, b):
    return lax.dot_general(a, b, (((0,), (0,)), ((), ())), preferred_element_type=F32)


def rms_scale(values):
    return lax.rsqrt(jnp.mean(values * values, axis=-1, keepdims=True) + NORM_EPS)


def slot_of(routes, k, rows):
    return jnp.broadcast_to(routes[k : k + 1, :], (rows, routes.shape[1]))


def pick_heads(route_ref, source_ref, k):
    route = jnp.broadcast_to(route_ref[k : k + 1, :], (H, route_ref.shape[1]))
    taken = source_ref[0:H, :]
    for e in range(1, E):
        taken = jnp.where(route == e, source_ref[e * H : (e + 1) * H, :], taken)
    return taken


def place_heads(route_ref, source_ref, e):
    total = jnp.zeros((H, route_ref.shape[1]), F32)
    for k in range(TOPK):
        route = jnp.broadcast_to(route_ref[k : k + 1, :], (H, route_ref.shape[1]))
        total = jnp.where(route == e, source_ref[k * H : (k + 1) * H, :], total)
    return total


def key_mask(first_key, first_query, rows, start_row):
    keys = lax.broadcasted_iota(jnp.int32, (rows, TB), 0) + first_key
    queries = lax.broadcasted_iota(jnp.int32, (rows, TB), 1) + first_query
    return (keys <= queries) & (keys >= start_row)


def head_forward_kernel(
    steps, x_ref, route_ref, segment_ref, wall_ref, gain_ref,
    q_ref, att_ref, gate_ref, lse_ref, kv_ref, kvt_ref, start_ref, count_ref,
    all_scr, k_scr, vt_scr, count_scr,
):
    step = pl.program_id(0)
    place = lax.rem(step, NB)
    here = pl.multiple_of(place * TB, TB)

    @pl.when(step == 0)
    def _():
        count_scr[...] = jnp.zeros_like(count_scr)

    row = segment_ref[pl.ds(lax.div(step, NB), 1), :]
    segments = segment_ref[pl.ds(lax.div(step, NB), 1), pl.ds(here, TB)]
    start = jnp.zeros((1, TB), jnp.int32)
    for number in range(1, 4):
        below = jnp.sum((row < number).astype(jnp.int32), axis=1, keepdims=True)
        start = jnp.where(segments == number, below, start)
    start_ref[...] = start
    x = x_ref[...].astype(F32)
    normed = (x * rms_scale(x) * gain_ref[...]).astype(BF16)
    all_scr[...] = nt(wall_ref[...], normed)
    kt = all_scr[KROW : KROW + H, :]
    vt = all_scr[VROW : VROW + H, :]
    logits = all_scr[RROW : RROW + E, :]
    kvt = jnp.concatenate([kt, vt], axis=0)
    kv = kvt.T.astype(BF16)
    kv_ref[...] = kv
    kvt_ref[...] = kvt.astype(BF16)
    k_scr[pl.ds(here, TB), :] = kv[:, :H]
    vt_scr[:, pl.ds(here, TB)] = vt.astype(BF16)
    routes = route_ref[...]
    experts = lax.broadcasted_iota(jnp.int32, (E, TB), 0)
    chosen = []
    counts = count_scr[...]
    for k in range(TOPK):
        named = slot_of(routes, k, E) == experts
        chosen.append(jnp.sum(jnp.where(named, logits, 0.0), axis=0, keepdims=True))
        counts = counts + named.astype(F32)
    count_scr[...] = counts
    chosen = jnp.concatenate(chosen, axis=0)
    raised = jnp.exp(chosen - jnp.max(chosen, axis=0, keepdims=True))
    gate_ref[...] = raised / jnp.sum(raised, axis=0, keepdims=True)
    for k in range(TOPK):
        query = pick_heads(route_ref, all_scr, k).astype(BF16)
        q_ref[k * H : (k + 1) * H, :] = query * jnp.asarray(H ** (-0.5), BF16)

    def attend(blocks):
        rows = blocks * TB
        first_key = pl.multiple_of((place - (blocks - 1)) * TB, TB)
        mask = key_mask(first_key, here, rows, start)
        keys = k_scr[pl.ds(first_key, rows), :]
        values = vt_scr[:, pl.ds(first_key, rows)]
        for k in range(TOPK):
            scores = jnp.where(mask, nn(keys, q_ref[k * H : (k + 1) * H, :]), NEG_LARGE)
            top = jnp.max(scores, axis=0, keepdims=True)
            raised = jnp.exp(scores - top)
            total = jnp.sum(raised, axis=0, keepdims=True)
            probs = (raised * (1.0 / total)).astype(BF16)
            att_ref[k * H : (k + 1) * H, :] = nn(values, probs)
            lse_ref[k : k + 1, :] = top + jnp.log(total)

    span = place - lax.div(jnp.min(start), TB) + 1
    for blocks in range(1, min(3, NB) + 1):

        @pl.when(span == blocks)
        def _(blocks=blocks):
            attend(blocks)

    @pl.when(step == steps - 1)
    def _():
        held = jnp.sum(count_scr[...], axis=1, keepdims=True)
        lane = lax.broadcasted_iota(jnp.int32, (E, 128), 1)
        row = lax.broadcasted_iota(jnp.int32, (E, 128), 0)
        count_ref[...] = jnp.sum(jnp.where(lane == row, held, 0.0), axis=0, keepdims=True)


def picks(rows, stride, first):
    at = lax.broadcasted_iota(jnp.int32, (rows, D), 1)
    row = lax.broadcasted_iota(jnp.int32, (rows, D), 0)
    return (at == row * stride + first).astype(F32)


def exact(product, a, b):
    return lax.dot_general(
        a, b, (product, ((), ())), precision=lax.Precision.HIGHEST, preferred_element_type=F32
    )


def gelu_parts(v):
    size = jnp.abs(v) * 0.7071067811865476
    bell = jnp.exp(-(size * size))
    t = 1.0 / (1.0 + 0.3275911 * size)
    series = t * (
        0.254829592
        + t * (-0.284496736 + t * (1.421413741 + t * (-1.453152027 + t * 1.061405429)))
    )
    tail = 0.5 * series * bell
    cdf = jnp.where(v < 0.0, tail, 1.0 - tail)
    return cdf, bell * 0.3989422804014327


def middle_kernel(
    x_ref, dy_ref, gain_ref, wo_ref, w1_ref, w2_ref, route_ref, gate_ref, att_ref,
    out_ref, dres_ref, datt_ref, delta_ref, dlogit_ref, flat_ref, extra_ref, dgain_ref,
    slot_scr, head_scr, mix_scr, dwo_ref, dw1_ref, dw2t_ref, rows_scr, low_scr, row_sem,
):
    step = pl.program_id(0)

    @pl.when(step == 0)
    def _():
        dwo_ref[...] = jnp.zeros_like(dwo_ref)
        dw1_ref[...] = jnp.zeros_like(dw1_ref)
        dw2t_ref[...] = jnp.zeros_like(dw2t_ref)
        dgain_ref[...] = jnp.zeros_like(dgain_ref)

    routes = route_ref[...]
    tokens = routes.shape[1]
    gates = gate_ref[...]
    for k in range(TOPK):
        slot_scr[k * H : (k + 1) * H, :] = gates[k : k + 1, :] * att_ref[k * H : (k + 1) * H, :]
    for e in range(E):
        mix_scr[e * H : (e + 1) * H, :] = place_heads(route_ref, slot_scr, e).astype(BF16)
    x = x_ref[...].astype(F32)
    dy = dy_ref[...]
    mixed = mix_scr[...]
    residual = x + tn(mixed, wo_ref[...])
    scale = rms_scale(residual)
    gain = gain_ref[...]
    second = (residual * scale * gain).astype(BF16)
    second_t = second.T
    dy_t = dy.T
    out = residual
    dsecond = jnp.zeros((tokens, D), F32)
    for c in range(0, FF, FC):
        up = w1_ref[:, c : c + FC]
        down = w2_ref[c : c + FC, :]
        pre = nn(second, up)
        cdf, density = gelu_parts(pre)
        hidden = (pre * cdf).astype(BF16)
        dpre = (nt(dy, down) * (cdf + pre * density)).astype(BF16)
        out = out + nn(hidden, down)
        dsecond = dsecond + nt(dpre, up)
        dw2t_ref[:, c : c + FC] += nn(dy_t, hidden)
        dw1_ref[:, c : c + FC] += nn(second_t, dpre)
    out_ref[...] = out.astype(BF16)
    dgain_ref[...] += jnp.sum(dsecond * residual * scale, axis=0, keepdims=True)
    weighted = gain * dsecond
    dres = (
        dy.astype(F32)
        + scale * weighted
        - residual * (scale * scale * scale) * jnp.mean(weighted * residual, axis=-1, keepdims=True)
    )
    dres_ref[...] = dres
    branch = dres.astype(BF16)
    dwo_ref[...] += nn(mixed, branch)
    head_scr[...] = nt(wo_ref[...], branch).astype(BF16).astype(F32)
    dgates = []
    for k in range(TOPK):
        rows = slice(k * H, (k + 1) * H)
        dslot = pick_heads(route_ref, head_scr, k)
        attended = att_ref[rows, :]
        dgates.append(jnp.sum(dslot * attended, axis=0, keepdims=True))
        datt = (gates[k : k + 1, :] * dslot).astype(BF16)
        datt_ref[rows, :] = datt
        delta_ref[k : k + 1, :] = jnp.sum(datt.astype(F32) * attended, axis=0, keepdims=True)
    dgate = jnp.concatenate(dgates, axis=0)
    dchosen = gates * (dgate - jnp.sum(gates * dgate, axis=0, keepdims=True))
    experts = lax.broadcasted_iota(jnp.int32, (E, tokens), 0)
    dlogits = jnp.zeros((E, tokens), F32)
    for k in range(TOPK):
        dlogits = jnp.where(
            slot_of(routes, k, E) == experts,
            jnp.broadcast_to(dchosen[k : k + 1, :], (E, tokens)),
            dlogits,
        )
    dlogit_ref[...] = dlogits

    @pl.when(step == pl.num_programs(0) - 1)
    def _():
        for c in range(D // 128):
            lanes = slice(c * 128, (c + 1) * 128)
            rows_scr[pl.ds(c, QW, stride=4), :] = dwo_ref[:, lanes]
            rows_scr[pl.ds(W2_ROW - WO_ROW + c, FF, stride=4), :] = dw2t_ref[lanes, :].T
        for c in range(FF // 128):
            rows_scr[pl.ds(W1_ROW - WO_ROW + c, D, stride=16), :] = dw1_ref[:, c * 128 : (c + 1) * 128]
        extra_ref[...] = rows_scr[0:8, :]
        low_scr[...] = rows_scr[8:, :].astype(BF16)
        copy = pltpu.make_async_copy(
            low_scr, flat_ref.at[pl.ds(WO_ROW + 8, low_scr.shape[0]), :], row_sem.at[0]
        )
        copy.start()
        copy.wait()


def head_backward_kernel(
    x_ref, gain_ref, wall_ref, route_ref, start_ref, q_ref, datt_ref,
    lse_ref, delta_ref, kv_ref, kvt_ref, dlogit_ref, dres_ref, dgain_two_ref, extra_ref, flat_in,
    dx_ref, flat_ref,
    dk_scr, dv_scr, dq_scr, dall_scr, dwall_ref, dgain_ref, rows_scr, low_scr, row_sem,
):
    step = pl.program_id(0)
    place = NB - 1 - lax.rem(step, NB)
    here = pl.multiple_of(place * TB, TB)

    @pl.when(step == 0)
    def _():
        dwall_ref[...] = jnp.zeros_like(dwall_ref)
        dgain_ref[...] = jnp.zeros_like(dgain_ref)

    @pl.when(lax.rem(step, NB) == 0)
    def _():
        dk_scr[...] = jnp.zeros_like(dk_scr)
        dv_scr[...] = jnp.zeros_like(dv_scr)

    def attend(blocks):
        rows = blocks * TB
        first_key = pl.multiple_of((place - (blocks - 1)) * TB, TB)
        mask = key_mask(first_key, here, rows, start_ref[...])
        keys = kv_ref[pl.ds(first_key, rows), :H]
        values = kv_ref[pl.ds(first_key, rows), H:]
        keys_t = kvt_ref[:H, pl.ds(first_key, rows)]
        dk = jnp.zeros((rows, H), F32)
        dv = jnp.zeros((rows, H), F32)
        for k in range(TOPK):
            part = slice(k * H, (k + 1) * H)
            query = q_ref[part, :]
            datt = datt_ref[part, :]
            scores = jnp.where(mask, nn(keys, query), NEG_LARGE)
            probs = jnp.exp(scores - lse_ref[k : k + 1, :])
            dscore = (probs * (nn(values, datt) - delta_ref[k : k + 1, :])).astype(BF16)
            dv = dv + nt(probs.astype(BF16), datt)
            dk = dk + nt(dscore, query)
            dq_scr[part, :] = nn(keys_t, dscore) * (H ** (-0.5))
        dk_scr[pl.ds(first_key, rows), :] += dk
        dv_scr[pl.ds(first_key, rows), :] += dv

    span = place - lax.div(jnp.min(start_ref[...]), TB) + 1
    for blocks in range(1, min(3, NB) + 1):

        @pl.when(span == blocks)
        def _(blocks=blocks):
            attend(blocks)

    for e in range(E):
        dall_scr[e * H : (e + 1) * H, :] = place_heads(route_ref, dq_scr, e).astype(BF16)
    dkv = jnp.concatenate([dk_scr[pl.ds(here, TB), :], dv_scr[pl.ds(here, TB), :]], axis=1)
    dall_scr[KROW : KROW + 2 * H, :] = dkv.T.astype(BF16)
    dall_scr[RROW : RROW + 32, :] = jnp.concatenate(
        [dlogit_ref[...], jnp.zeros((32 - E, TB), F32)], axis=0
    ).astype(BF16)
    x = x_ref[...].astype(F32)
    scale = rms_scale(x)
    gain = gain_ref[...]
    normed = (x * scale * gain).astype(BF16)
    dall = dall_scr[...]
    dwall_ref[...] += nn(dall, normed)
    dnormed = tn(dall, wall_ref[...])
    dgain_ref[...] += jnp.sum(dnormed * x * scale, axis=0, keepdims=True)
    weighted = gain * dnormed
    dx_ref[...] = (
        dres_ref[...]
        + scale * weighted
        - x * (scale * scale * scale) * jnp.mean(weighted * x, axis=-1, keepdims=True)
    )

    @pl.when(step == pl.num_programs(0) - 1)
    def _():
        for c in range(D // 128):
            lanes = slice(c * 128, (c + 1) * 128)
            rows_scr[c : c + 1, :] = dgain_ref[:, lanes]
            rows_scr[4 + c : 5 + c, :] = dgain_two_ref[:, lanes]
        router_t = dwall_ref[RROW : RROW + E, :]
        across = jnp.concatenate(
            [exact(((1,), (1,)), router_t, picks(32, 16, b)) for b in range(16)], axis=0
        ).T
        for j in range(3):
            rows_scr[pl.ds(WR_ROW + j, 32, stride=3), :] = across[:, j * 128 : (j + 1) * 128]
        for first, row in ((KROW, WK_ROW), (VROW, WV_ROW)):
            part = dwall_ref[first : first + H, :]
            rows_scr[row : row + 256, :] = jnp.concatenate(
                [exact(((1,), (1,)), picks(256, 2, b), part) for b in range(2)], axis=1
            )
        for c in range(QW // 128):
            rows_scr[pl.ds(WQ_ROW + c, D, stride=12), :] = dwall_ref[c * 128 : (c + 1) * 128, :].T
        rows_scr[WO_ROW : WO_ROW + 8, :] = extra_ref[...]
        low_scr[...] = rows_scr[...].astype(BF16)
        copy = pltpu.make_async_copy(low_scr, flat_ref.at[pl.ds(0, WO_ROW + 8), :], row_sem.at[0])
        copy.start()
        copy.wait()


def whole(shape):
    return pl.BlockSpec(shape, lambda *_: (0,) * len(shape), pipeline_mode=pl.Buffered(1))


def kept(shape):
    return pl.BlockSpec(shape, lambda *_: (0,) * len(shape))


def struct(shape, kind=F32):
    return jax.ShapeDtypeStruct(shape, kind)


def params_for(mib):
    return pltpu.CompilerParams(vmem_limit_bytes=mib * MIB)


def head_forward(tokens, routes_t, segments, wall, gain):
    count = tokens.shape[0]
    steps = count // TB
    across = lambda rows: pl.BlockSpec((rows, TB), lambda b: (0, b))
    down = lambda columns: pl.BlockSpec((TB, columns), lambda b: (b, 0))
    return pl.pallas_call(
        functools.partial(head_forward_kernel, steps),
        grid=(steps,),
        in_specs=[down(D), across(TOPK), whole(segments.shape), whole((ALLW, D)), whole((1, D))],
        out_specs=[
            across(TOPK * H), across(TOPK * H), across(TOPK), across(TOPK), down(2 * H), across(2 * H),
            across(1), whole((1, 128)),
        ],
        scratch_shapes=[
            pltpu.VMEM((ALLW, TB), F32),
            pltpu.VMEM((LEN, H), BF16),
            pltpu.VMEM((H, LEN), BF16),
            pltpu.VMEM((E, TB), F32),
        ],
        out_shape=[
            struct((TOPK * H, count), BF16),
            struct((TOPK * H, count)),
            struct((TOPK, count)),
            struct((TOPK, count)),
            struct((count, 2 * H), BF16),
            struct((2 * H, count), BF16),
            struct((1, count), jnp.int32),
            struct((1, 128)),
        ],
        compiler_params=params_for(56),
        name="head_forward",
        cost_estimate=pl.CostEstimate(flops=10_000_000_000, bytes_accessed=16_000_000, transcendentals=0),
    )(tokens, routes_t, segments, wall, gain)


def middle(flat_rows, tokens, grad_out, gain, wo, w1, w2, routes_t, gates, attended):
    count = tokens.shape[0]
    steps = count // TB
    across = lambda rows: pl.BlockSpec((rows, TB), lambda b: (0, b))
    down = lambda columns: pl.BlockSpec((TB, columns), lambda b: (b, 0))
    return pl.pallas_call(
        middle_kernel,
        grid=(steps,),
        in_specs=[
            down(D), down(D), whole((1, D)), whole((QW, D)), whole((D, FF)), whole((FF, D)),
            across(TOPK), across(TOPK), across(TOPK * H),
        ],
        out_specs=[
            down(D), down(D), across(TOPK * H), across(TOPK), across(E),
            pl.BlockSpec(memory_space=pl.ANY), whole((8, 128)), whole((1, D)),
        ],
        out_shape=[
            struct((count, D), BF16),
            struct((count, D)),
            struct((TOPK * H, count), BF16),
            struct((TOPK, count)),
            struct((E, count)),
            struct((flat_rows, 128), BF16),
            struct((8, 128)),
            struct((1, D)),
        ],
        scratch_shapes=[
            pltpu.VMEM((TOPK * H, TB), F32),
            pltpu.VMEM((QW, TB), F32),
            pltpu.VMEM((QW, TB), BF16),
            pltpu.VMEM((QW, D), F32),
            pltpu.VMEM((D, FF), F32),
            pltpu.VMEM((D, FF), F32),
            pltpu.VMEM((flat_rows - WO_ROW, 128), F32),
            pltpu.VMEM((flat_rows - WO_ROW - 8, 128), BF16),
            pltpu.SemaphoreType.DMA((1,)),
        ],
        compiler_params=params_for(60),
        name="middle",
    )(tokens, grad_out, gain, wo, w1, w2, routes_t, gates, attended)


def head_backward(
    tokens, gain, wall, routes_t, start, queries, datt, lse, delta, kv, kvt, dlogits, dres, dgain_two,
    extra, flat,
):
    count = tokens.shape[0]
    steps = count // TB

    def place(b):
        return (b // NB) * NB + NB - 1 - b % NB

    across = lambda rows: pl.BlockSpec((rows, TB), lambda b: (0, place(b)))
    down = lambda columns: pl.BlockSpec((TB, columns), lambda b: (place(b), 0))
    return pl.pallas_call(
        head_backward_kernel,
        grid=(steps,),
        in_specs=[
            down(D), whole((1, D)), whole((ALLW, D)), across(TOPK), across(1),
            across(TOPK * H), across(TOPK * H), across(TOPK), across(TOPK),
            pl.BlockSpec((LEN, 2 * H), lambda b: (b // NB, 0)),
            pl.BlockSpec((2 * H, LEN), lambda b: (0, b // NB)),
            across(E), down(D), whole((1, D)), whole((8, 128)), pl.BlockSpec(memory_space=pl.ANY),
        ],
        out_specs=[down(D), pl.BlockSpec(memory_space=pl.ANY)],
        scratch_shapes=[
            pltpu.VMEM((LEN, H), F32),
            pltpu.VMEM((LEN, H), F32),
            pltpu.VMEM((TOPK * H, TB), F32),
            pltpu.VMEM((ALLW, TB), BF16),
            pltpu.VMEM((ALLW, D), F32),
            pltpu.VMEM((1, D), F32),
            pltpu.VMEM((WO_ROW + 8, 128), F32),
            pltpu.VMEM((WO_ROW + 8, 128), BF16),
            pltpu.SemaphoreType.DMA((1,)),
        ],
        out_shape=[struct((count, D)), struct(flat.shape, BF16)],
        input_output_aliases={15: 1},
        compiler_params=params_for(56),
        name="head_backward",
        cost_estimate=pl.CostEstimate(flops=30_000_000_000, bytes_accessed=24_000_000, transcendentals=0),
    )(
        tokens, gain, wall, routes_t, start, queries, datt, lse, delta, kv, kvt, dlogits, dres,
        dgain_two, extra, flat,
    )


class Mesh3:
    def __init__(self, shards, over):
        shard = lax.axis_index("dp")
        other = lax.axis_index("fsdp")
        self.over = over
        self.many = shards * over
        self.sizes = {"x": 2, "y": shards // 2, "z": over // 2}
        self.here = {"x": lax.rem(other, 2), "y": lax.div(shard, 2), "z": lax.div(other, 2)}
        self.core = lax.rem(shard, 2)
        self.me = shard * over + other
        self.partner = (shard + 1 - 2 * self.core, other)

    def moved(self, steps):
        return {
            axis: lax.rem(self.here[axis] + steps.get(axis, 0), self.sizes[axis]) for axis in "xyz"
        }

    def device(self, core, steps):
        at = self.moved(steps)
        return (at["y"] * 2 + core, at["z"] * 2 + at["x"])

    def number(self, core, steps):
        shard, other = self.device(core, steps)
        return shard * self.over + other

    def nth(self, number):
        return (lax.div(number, self.over), lax.rem(number, self.over))

    def greet_near(self):
        devices = [
            self.device(self.core, {axis: step})
            for axis in "xyz"
            for step in range(1, self.sizes[axis])
        ] + [self.partner]
        barrier = pltpu.get_barrier_semaphore()
        for device in devices:
            pl.semaphore_signal(barrier, inc=1, device_id=device, device_id_type=MESH)
        pl.semaphore_wait(barrier, len(devices))

    def greet_all(self):
        barrier = pltpu.get_barrier_semaphore()

        def hello(j, carry):
            device = self.nth(lax.rem(self.me + j, self.many))
            pl.semaphore_signal(barrier, inc=1, device_id=device, device_id_type=MESH)
            return carry

        lax.fori_loop(1, self.many, hello, 0)
        pl.semaphore_wait(barrier, self.many - 1)


def along_z(step):
    return {1: (0, 3), 2: (1, 5), 3: (3, 8)}.get(step, (step, 2 * step + 2))


class Kind:
    def __init__(self, mesh, core, axes):
        self.mesh = mesh
        self.core = core
        self.axes = axes
        ranges = [range(mesh.sizes[axis]) for axis in axes]
        self.offsets = list(itertools.product(*ranges))
        self.index = {one: number for number, one in enumerate(self.offsets)}

    def owner(self, offsets):
        return self.mesh.number(self.core, dict(zip(self.axes, offsets)))

    def last(self, offsets):
        return max([i for i in range(3) if offsets[i]], default=-1)

    def turn(self, offsets):
        total = 0
        for axis, step in zip(self.axes, offsets):
            if step:
                total += along_z(step)[1] if axis == "z" else 2
        return total

    def hops(self, offsets):
        for i in range(self.last(offsets) + 1, 3):
            for step in range(1, self.mesh.sizes[self.axes[i]]):
                delay = along_z(step)[0] if self.axes[i] == "z" else 0
                yield i, step, self.turn(offsets) + delay

    def ahead(self, i, step):
        return self.mesh.device(self.core, {self.axes[i]: step})


AXES = ("zxy", "zyx")


def pieces_of(window):
    if window < 512:
        return [(0, window)]
    first = (window // 16 + 1) // 2 * 16
    return [(0, first), (first, window - first)]


def gather_events(mesh, own_ref, land, send_sem, recv_sem, laid):
    events = []
    pieces = pieces_of(own_ref.shape[0])
    kinds = [Kind(mesh, core, AXES[core]) for core in range(2)]
    end = 2 * max(kind.turn(one) for kind in kinds for one in kind.offsets) + 4

    def copy(owner, device, slot, p):
        rows = pl.ds(*pieces[p])
        return pltpu.make_async_remote_copy(
            src_ref=land.at[owner, rows],
            dst_ref=land.at[owner, rows],
            send_sem=send_sem.at[slot, p],
            recv_sem=recv_sem.at[owner, p],
            device_id=device,
            device_id_type=MESH,
        )

    def event(turn, condition, action):
        events.append((turn, lambda: pl.when(condition)(action)))

    for kind in kinds:
        ours = mesh.core == kind.core
        theirs = mesh.core != kind.core
        slots = itertools.count()
        for offsets in kind.offsets:
            owner = kind.owner(offsets)
            slot = next(slots)
            hops = [(i, step, turn, next(slots)) for i, step, turn in kind.hops(offsets)]
            for p in range(len(pieces)):

                def come(owner=owner, offsets=offsets, slot=slot, p=p, kind=kind, hops=hops):
                    if any(offsets):
                        copy(owner, mesh.partner, slot, p).wait_recv()
                    elif p == 0:
                        land[owner] = own_ref[...]
                    for i, step, turn, number in hops:
                        if turn == kind.turn(offsets):
                            copy(owner, kind.ahead(i, step), number, p).start()
                    copy(owner, mesh.partner, slot, p).start()
                    laid(owner, p)

                def across(owner=owner, slot=slot, p=p):
                    copy(owner, mesh.partner, slot, p).wait_recv()
                    laid(owner, p)

                def done(owner=owner, slot=slot, p=p, hops=hops):
                    copy(owner, mesh.partner, slot, p).wait_send()
                    for _, _, _, number in hops:
                        copy(owner, mesh.partner, number, p).wait_send()

                event(2 * kind.turn(offsets) + p, ours, come)
                event(end + kind.turn(offsets) / 100, theirs, across)
                event(end + 1, ours, done)
                for i, step, turn, number in hops:
                    if turn == kind.turn(offsets):
                        continue

                    def send(owner=owner, device=kind.ahead(i, step), number=number, p=p):
                        copy(owner, device, number, p).start()

                    event(2 * turn + p, ours, send)
    return sorted(events, key=lambda one: one[0])


def reduce_events(mesh, source, fetch, part, outgo, income, send_sem, recv_sem, finish):
    events = []
    half = mesh.many // 2
    pieces = pieces_of(outgo.shape[1])
    kinds = [Kind(mesh, core, AXES[core]) for core in range(2)]
    end = 2 * max(kind.turn(one) for kind in kinds for one in kind.offsets) + 4

    def copy(slot, device, p, begin=None):
        rows = pl.ds(*pieces[p])
        return pltpu.make_async_remote_copy(
            src_ref=outgo.at[slot, rows] if begin is None else begin,
            dst_ref=income.at[slot, rows],
            send_sem=send_sem.at[slot, p],
            recv_sem=recv_sem.at[slot, p],
            device_id=device,
            device_id_type=MESH,
        )

    def event(turn, condition, action):
        events.append((turn, lambda: pl.when(condition)(action)))

    def taken(slot, p):
        copy(slot, mesh.partner, p).wait_recv()
        return income[slot, pl.ds(*pieces[p])].astype(F32)

    for kind in kinds:
        ours = mesh.core == kind.core
        theirs = mesh.core != kind.core
        slots = {}
        for offsets in kind.offsets:
            if any(offsets):
                slots[offsets] = half + len(slots)
        for offsets in kind.offsets:
            owner = kind.owner(offsets)
            number = kind.index[offsets]
            axis = kind.last(offsets)
            turn = end - 2 * kind.turn(offsets)
            for p, (first, rows) in enumerate(pieces):

                def hand(owner=owner, number=number, p=p, first=first, rows=rows):
                    copy(number, mesh.partner, p, source(owner, first, rows)).start()

                def onward(
                    owner=owner, offsets=offsets, number=number, axis=axis, kind=kind, slots=slots, p=p
                ):
                    mine = pl.ds(*pieces[p])
                    fetch(owner, number, p).wait()
                    total = part[number, mine].astype(F32) + taken(number, p)
                    for i, step, _ in kind.hops(offsets):
                        longer = tuple(step if j == i else o for j, o in enumerate(offsets))
                        total = total + taken(slots[longer], p)
                    if axis < 0:
                        finish(total, p)
                    else:
                        outgo[slots[offsets], mine] = total.astype(BF16)
                        copy(slots[offsets], kind.ahead(axis, offsets[axis]), p).start()

                def handed(number=number, p=p):
                    copy(number, mesh.partner, p).wait_send()

                event(-1 - kind.turn(offsets) / 100, theirs, hand)
                event(-2, ours, lambda owner=owner, number=number, p=p: fetch(owner, number, p).start())
                event(turn + p, ours, onward)
                event(end + 2, theirs, handed)
                if axis >= 0:

                    def passed(slot=slots[offsets], p=p):
                        copy(slot, mesh.partner, p).wait_send()

                    event(end + 2, ours, passed)
    return sorted(events, key=lambda one: one[0])


def window_rows(shard_size, many):
    units = [(shard_size * d) // UNIT for d in range(many + 1)]
    return 16 * (max(b - a for a, b in zip(units, units[1:])) + 1)


def first_row(shard_size, number):
    if isinstance(number, int):
        return number * shard_size // UNIT * 16
    return pl.multiple_of(lax.div(number * shard_size, UNIT) * 16, 16)


def inner_units(shard_size, many):
    units = [(shard_size * d) // UNIT for d in range(many + 1)]
    return min(b - a for a, b in zip(units, units[1:]))


def lay_inner(shard_size, many, land, flat, owner, first, rows):
    begin = max(first, 16)
    count = min(first + rows, 16 * inner_units(shard_size, many)) - begin
    row = pl.multiple_of(first_row(shard_size, owner) + begin, 16)
    flat[pl.ds(row, count), :] = land[owner, pl.ds(begin, count), :].astype(F32)


def lay_edges(shard_size, many, land, flat):
    inner = 16 * inner_units(shard_size, many)
    flat[0:16, :] = jnp.zeros((16, 128), F32)

    def lay(number, carry):
        row = first_row(shard_size, number)
        after = first_row(shard_size, number + 1)
        flat[pl.ds(row, 16), :] += land[number, 0:16, :].astype(F32)
        tail = land[number, pl.ds(inner, 16), :].astype(F32)
        flat[pl.ds(pl.multiple_of(row + inner, 16), 16), :] = tail
        last = pl.multiple_of(after - row, 16)
        flat[pl.ds(after, 16), :] = land[number, pl.ds(last, 16), :].astype(F32)
        return carry

    lax.fori_loop(0, many, lay, 0)


def early_matrices(flat, wall_ref, gain_one_ref, gain_two_ref):
    for c in range(D // 128):
        lanes = slice(c * 128, (c + 1) * 128)
        gain_one_ref[:, lanes] = flat[c : c + 1, :]
        gain_two_ref[:, lanes] = flat[4 + c : 5 + c, :]
    for c in range(QW // 128):
        wall_ref[c * 128 : (c + 1) * 128, :] = flat[pl.ds(WQ_ROW + c, D, stride=12), :].T.astype(BF16)
    for first, row in ((KROW, WK_ROW), (VROW, WV_ROW)):
        pair = flat[row : row + 256, :].T.astype(BF16)
        wall_ref[first : first + H, :] = (
            nn(pair[:H], picks(256, 2, 0).astype(BF16)) + nn(pair[H:], picks(256, 2, 1).astype(BF16))
        ).astype(BF16)
    across = jnp.concatenate(
        [flat[pl.ds(WR_ROW + j, 32, stride=3), :] for j in range(3)], axis=1
    ).T.astype(BF16)
    router_t = jnp.zeros((E, D), F32)
    for part in range(16):
        router_t = router_t + nn(across[part * E : (part + 1) * E, :], picks(32, 16, part).astype(BF16))
    wall_ref[RROW:ALLW, :] = jnp.concatenate(
        [router_t, jnp.zeros((ALLW - RROW - E, D), F32)], axis=0
    ).astype(BF16)


def gather_kernel(
    mesh, shard_size, own_ref,
    wall_out, gain_one_ref, gain_two_ref, wo_out, w1_out, w2_out,
    land, flat, wall_ref, wo_ref, w1_ref, w2_ref, send_sem, recv_sem, out_sem,
):
    mesh = mesh()
    many = mesh.many
    pieces = pieces_of(own_ref.shape[0])
    mesh.greet_near()

    def laid(owner, p):
        lay_inner(shard_size, many, land, flat, owner, *pieces[p])

    for _, action in gather_events(mesh, own_ref, land, send_sem, recv_sem, laid):
        action()
    lay_edges(shard_size, many, land, flat)
    copies = []

    def leave(matrix, out):
        copy = pltpu.make_async_copy(matrix, out, out_sem.at[len(copies)])
        copy.start()
        copies.append(copy)

    for c in range(D // 128):
        wo_ref[:, c * 128 : (c + 1) * 128] = flat[pl.ds(WO_ROW + c, QW, stride=4), :].astype(BF16)
    leave(wo_ref, wo_out)
    for c in range(D // 128):
        w2_ref[:, c * 128 : (c + 1) * 128] = flat[pl.ds(W2_ROW + c, FF, stride=4), :].astype(BF16)
    leave(w2_ref, w2_out)
    for c in range(FF // 128):
        w1_ref[:, c * 128 : (c + 1) * 128] = flat[pl.ds(W1_ROW + c, D, stride=16), :].astype(BF16)
    leave(w1_ref, w1_out)
    early_matrices(flat, wall_ref, gain_one_ref, gain_two_ref)
    leave(wall_ref, wall_out)
    for copy in copies:
        copy.wait()


def gather_weights(shards, over, shard_size, own):
    window = own.shape[0]
    many = shards * over
    rows = (shard_size * (many - 1)) // UNIT * 16 + window
    vmem = pl.BlockSpec(memory_space=pltpu.VMEM)
    hbm = pl.BlockSpec(memory_space=pl.ANY)
    mesh = functools.partial(Mesh3, shards, over)
    pieces = len(pieces_of(window))
    return pl.pallas_call(
        functools.partial(gather_kernel, mesh, shard_size),
        in_specs=[vmem],
        out_specs=[hbm, vmem, vmem, hbm, hbm, hbm],
        out_shape=[
            struct((ALLW, D), BF16),
            struct((1, D)),
            struct((1, D)),
            struct((QW, D), BF16),
            struct((D, FF), BF16),
            struct((FF, D), BF16),
        ],
        scratch_shapes=[
            pltpu.VMEM((many, window, 128), BF16),
            pltpu.VMEM((rows, 128), F32),
            pltpu.VMEM((ALLW, D), BF16),
            pltpu.VMEM((QW, D), BF16),
            pltpu.VMEM((D, FF), BF16),
            pltpu.VMEM((FF, D), BF16),
            pltpu.SemaphoreType.DMA((many, pieces)),
            pltpu.SemaphoreType.DMA((many, pieces)),
            pltpu.SemaphoreType.DMA((4,)),
        ],
        compiler_params=pltpu.CompilerParams(
            collective_id=0, has_side_effects=True, vmem_limit_bytes=60 * MIB
        ),
        name="gather_weights",
    )(own)


def reduce_kernel(
    mesh, shard_size, flat_ref, count_ref,
    out_ref, total_ref, gain_ref,
    part, outgo, income, stats, gains, part_sem, send_sem, recv_sem, stat_send, stat_recv, gain_send, gain_recv,
):
    mesh = mesh()
    many = mesh.many
    window = out_ref.shape[0]
    pieces = pieces_of(window)

    def source(owner, first, rows):
        row = pl.multiple_of(first_row(shard_size, owner) + first, 16)
        return flat_ref.at[pl.ds(row, rows), :]

    def fetch(owner, number, p):
        return pltpu.make_async_copy(
            source(owner, *pieces[p]), part.at[number, pl.ds(*pieces[p])], part_sem.at[number, p]
        )

    def finish(total, p):
        out_ref[pl.ds(*pieces[p]), :] = total

    mesh.greet_all()
    for _, action in reduce_events(mesh, source, fetch, part, outgo, income, send_sem, recv_sem, finish):
        action()
    total = out_ref[...]
    begin = mesh.me * shard_size - lax.div(mesh.me * shard_size, UNIT) * UNIT
    at = (
        lax.broadcasted_iota(jnp.int32, (window, 128), 0) * 128
        + lax.broadcasted_iota(jnp.int32, (window, 128), 1)
    )
    inside = jnp.where((at >= begin) & (at < begin + shard_size), total, 0.0)
    squares = jnp.sum(jnp.sum(inside * inside, axis=0, keepdims=True), axis=1, keepdims=True)
    lane = lax.broadcasted_iota(jnp.int32, (1, 128), 1)
    stats[0] = jnp.where(lane == E, squares, count_ref[...])

    def told(j):
        return pltpu.make_async_remote_copy(
            src_ref=stats.at[0],
            dst_ref=stats.at[j],
            send_sem=stat_send.at[j],
            recv_sem=stat_recv.at[j],
            device_id=mesh.nth(lax.rem(mesh.me + j, many)),
            device_id_type=MESH,
        )

    def shown(j):
        return pltpu.make_async_remote_copy(
            src_ref=gains,
            dst_ref=gains,
            send_sem=gain_send.at[j],
            recv_sem=gain_recv.at[0],
            device_id=mesh.nth(lax.rem(mesh.me + j, many)),
            device_id_type=MESH,
        )

    def tell(j, carry):
        told(j).start()
        return carry

    def hear(j, carry):
        told(j).wait()
        return carry

    def show(j, carry):
        shown(j).start()
        return carry

    def showed(j, carry):
        shown(j).wait_send()
        return carry

    lax.fori_loop(1, many, tell, 0)

    @pl.when(mesh.me == 0)
    def _():
        gains[...] = total[0:8, :]
        lax.fori_loop(1, many, show, 0)
        lax.fori_loop(1, many, showed, 0)

    @pl.when(mesh.me != 0)
    def _():
        shown(1).wait_recv()

    lax.fori_loop(1, many, hear, 0)
    total_ref[...] = jnp.sum(stats[...], axis=0)
    gain_ref[...] = gains[...]


def reduce_grads(shards, over, shard_size, window, flat, counts):
    vmem = pl.BlockSpec(memory_space=pltpu.VMEM)
    many = shards * over
    mesh = functools.partial(Mesh3, shards, over)
    pieces = len(pieces_of(window))
    return pl.pallas_call(
        functools.partial(reduce_kernel, mesh, shard_size),
        in_specs=[pl.BlockSpec(memory_space=pl.ANY), vmem],
        out_specs=[vmem] * 3,
        out_shape=[struct((window, 128)), struct((1, 128)), struct((8, 128))],
        scratch_shapes=[
            pltpu.VMEM((many // 2, window, 128), BF16),
            pltpu.VMEM((many, window, 128), BF16),
            pltpu.VMEM((many, window, 128), BF16),
            pltpu.VMEM((many, 1, 128), F32),
            pltpu.VMEM((8, 128), F32),
            pltpu.SemaphoreType.DMA((many // 2, pieces)),
            pltpu.SemaphoreType.DMA((many, pieces)),
            pltpu.SemaphoreType.DMA((many, pieces)),
            pltpu.SemaphoreType.DMA((many,)),
            pltpu.SemaphoreType.DMA((many,)),
            pltpu.SemaphoreType.DMA((many,)),
            pltpu.SemaphoreType.DMA((1,)),
        ],
        compiler_params=pltpu.CompilerParams(
            collective_id=1, has_side_effects=True, vmem_limit_bytes=56 * MIB
        ),
        name="reduce_grads",
    )(flat, counts)


def per_device(
    shards, over, tokens, grad_out, routes, segments, params, first_moment, second_moment, ema_weights
):
    shard_size = params.shape[0]
    window = window_rows(shard_size, shards * over)
    flat_rows = (shard_size * (shards * over - 1)) // UNIT * 16 + window
    me = lax.axis_index("dp") * over + lax.axis_index("fsdp")
    begin = lax.rem(me * shard_size, UNIT)
    own = lax.dynamic_slice(
        jnp.pad(params.astype(BF16), (UNIT, window * 128 - shard_size)), (UNIT - begin,), (window * 128,)
    ).reshape(window, 128)
    routes_t = routes.T
    wall, gain_one, gain_two, wo, w1, w2 = gather_weights(shards, over, shard_size, own)
    queries, attended, gates, lse, kv, kvt, start, counts = head_forward(
        tokens, routes_t, segments, wall, gain_one
    )
    output, dres, datt, delta, dlogits, flat, extra, dgain_two = middle(
        flat_rows, tokens, grad_out, gain_two, wo, w1, w2, routes_t, gates, attended
    )
    input_grad, flat = head_backward(
        tokens, gain_one, wall, routes_t, start, queries, datt, lse, delta, kv, kvt, dlogits, dres,
        dgain_two, extra, flat,
    )
    reduced, sums, gain_grads = reduce_grads(shards, over, shard_size, window, flat, counts)
    grad_shard = lax.dynamic_slice(reduced.reshape(-1), (begin,), (shard_size,))
    total_tokens = tokens.shape[0] * shards * over
    expert_load = sums[0, :E] * (E / (total_tokens * TOPK))
    grad_norm = jnp.sqrt(sums[0, E])
    clipped = grad_shard * (CLIP_LIMIT / jnp.maximum(grad_norm, CLIP_LIMIT))
    new_first = BETA_FIRST * first_moment + (1.0 - BETA_FIRST) * clipped
    new_second = BETA_SECOND * second_moment + (1.0 - BETA_SECOND) * clipped * clipped
    first_hat = new_first / (1.0 - BETA_FIRST**STEP)
    second_hat = new_second / (1.0 - BETA_SECOND**STEP)
    new_params = params * (1.0 - LEARN_RATE * DECAY_RATE) - LEARN_RATE * first_hat / (
        jnp.sqrt(second_hat) + ADAM_EPS
    )
    new_ema = EMA_KEEP * ema_weights + (1.0 - EMA_KEEP) * new_params
    return (
        output,
        input_grad,
        expert_load,
        grad_norm.reshape(1),
        new_params,
        new_first,
        new_second,
        new_ema,
        gain_grads.reshape(2, D),
    )


def solution(mesh):
    row = P(("dp", "fsdp"), None)
    flat = P(("dp", "fsdp"))
    return jax.shard_map(
        functools.partial(per_device, mesh.shape["dp"], mesh.shape["fsdp"]),
        mesh=mesh,
        in_specs=(row, row, row, row, flat, flat, flat, flat),
        out_specs=(row, row, P(), P(), flat, flat, flat, flat, P()),
        check_vma=False,
    )
```

```python
import functools
import itertools

import jax
import jax.numpy as jnp
from jax import lax
from jax.experimental import pallas as pl
from jax.experimental.pallas import tpu as pltpu
from jax.sharding import PartitionSpec as P

D = 512
E = 24
TOPK = 8
H = 64
FF = 2048
STEP = 10

NORM_EPS = 1e-06
CLIP_LIMIT = 1.0
BETA_FIRST = 0.9
BETA_SECOND = 0.95
LEARN_RATE = 0.1
DECAY_RATE = 0.1
ADAM_EPS = 1e-08
EMA_KEEP = 0.9
NEG_LARGE = -1e30

QW = E * H
KROW = QW
VROW = QW + H
RROW = QW + 2 * H
ALLW = 1696
LEN = 1024
TB = 256
NB = LEN // TB
QB = 128
MOST = 512 // QB + 1
SORT_STEPS = (
    (0, 1), (2, 3), (4, 5), (6, 7), (0, 2), (1, 3), (4, 6), (5, 7), (1, 2), (5, 6),
    (0, 4), (1, 5), (2, 6), (3, 7), (2, 4), (3, 5), (1, 2), (3, 4), (5, 6),
)
FC = 512
MIB = 1 << 20

WR_ROW = 8
WK_ROW = 104
WV_ROW = 360
WQ_ROW = 616
WO_ROW = 6760
W1_ROW = 12904
W2_ROW = 21096
ALL_ROWS = 29288
UNIT = 16 * 128
MESH = pl.DeviceIdType.MESH

F32 = jnp.float32
BF16 = jnp.bfloat16


def nn(a, b):
    return lax.dot_general(a, b, (((1,), (0,)), ((), ())), preferred_element_type=F32)


def nt(a, b):
    return lax.dot_general(a, b, (((1,), (1,)), ((), ())), preferred_element_type=F32)


def tn(a, b):
    return lax.dot_general(a, b, (((0,), (0,)), ((), ())), preferred_element_type=F32)


def rms_scale(values):
    return lax.rsqrt(jnp.mean(values * values, axis=-1, keepdims=True) + NORM_EPS)


def slot_of(routes, k, rows):
    return jnp.broadcast_to(routes[k : k + 1, :], (rows, routes.shape[1]))


def expert_rows(routes, k):
    return jnp.broadcast_to(routes.astype(jnp.int16)[k : k + 1, :], (16, routes.shape[1]))


def pick_heads(routes, source_ref, k):
    tokens = routes.shape[1]
    route = expert_rows(routes, k)
    taken = source_ref[k * H : (k + 1) * H, :].reshape(H // 16, 16, tokens)
    for e in range(k + 1, k + E - TOPK + 1):
        piece = source_ref[e * H : (e + 1) * H, :].reshape(H // 16, 16, tokens)
        taken = jnp.where((route == jnp.int16(e))[None], piece, taken)
    return taken.reshape(H, tokens)


def place_heads(routes, source_ref, target_ref):
    tokens = routes.shape[1]
    rows = [expert_rows(routes, k) for k in range(TOPK)]
    for e in range(E):
        total = jnp.zeros((H // 16, 16, tokens), BF16)
        for k in range(max(0, e - (E - TOPK)), min(TOPK - 1, e) + 1):
            piece = source_ref[k * H : (k + 1) * H, :].reshape(H // 16, 16, tokens)
            total = jnp.where((rows[k] == jnp.int16(e))[None], piece, total)
        target_ref[e * H : (e + 1) * H, :] = total.reshape(H, tokens)


def sorted_rows(rows):
    rows = list(rows)
    for one, two in SORT_STEPS:
        rows[one], rows[two] = jnp.minimum(rows[one], rows[two]), jnp.maximum(rows[one], rows[two])
    return rows


def key_mask(first_key, first_query, rows, start_row):
    keys = lax.broadcasted_iota(jnp.int32, (rows, QB), 0) + first_key
    queries = lax.broadcasted_iota(jnp.int32, (rows, QB), 1) + first_query
    mask = (keys <= queries) & (keys >= start_row)
    return jnp.concatenate([mask, mask], axis=1)


def pair_of(ref, k, lanes):
    return jnp.concatenate(
        [ref[k * H : (k + 1) * H, lanes], ref[(k + 1) * H : (k + 2) * H, lanes]], axis=1
    )


def row_pair(ref, k, lanes):
    return jnp.concatenate([ref[k : k + 1, lanes], ref[k + 1 : k + 2, lanes]], axis=1)


def by_span(attend, place, start_ref):
    def one(j, carry):
        lanes = pl.ds(pl.multiple_of(j * QB, QB), QB)
        block = place * (TB // QB) + j
        span = block - lax.div(jnp.min(start_ref[:, lanes]), QB) + 1
        for blocks in range(1, MOST + 1):

            @pl.when(span == blocks)
            def _(blocks=blocks):
                attend(lanes, block, blocks)

        return carry

    lax.fori_loop(0, TB // QB, one, 0)


def head_forward_kernel(
    steps, x_ref, route_ref, segment_ref, wall_ref, gain_ref,
    q_ref, att_ref, gate_ref, lse_ref, kv_ref, kvt_ref, start_ref, sorted_ref, count_ref,
    all_scr, low_scr, k_scr, vt_scr, count_scr,
):
    step = pl.program_id(0)
    place = lax.rem(step, NB)
    here = pl.multiple_of(place * TB, TB)

    @pl.when(step == 0)
    def _():
        count_scr[...] = jnp.zeros_like(count_scr)

    row = segment_ref[pl.ds(lax.div(step, NB), 1), :]
    segments = segment_ref[pl.ds(lax.div(step, NB), 1), pl.ds(here, TB)]
    start = jnp.zeros((1, TB), jnp.int32)
    for number in range(1, 4):
        below = jnp.sum((row < number).astype(jnp.int32), axis=1, keepdims=True)
        start = jnp.where(segments == number, below, start)
    start_ref[...] = start
    x = x_ref[...].astype(F32)
    normed = (x * rms_scale(x) * gain_ref[...]).astype(BF16)
    all_scr[...] = nt(wall_ref[...], normed)
    kt = all_scr[KROW : KROW + H, :]
    vt = all_scr[VROW : VROW + H, :]
    logits = all_scr[RROW : RROW + E, :]
    kvt = jnp.concatenate([kt, vt], axis=0)
    kv = kvt.T.astype(BF16)
    kv_ref[...] = kv
    kvt_ref[...] = kvt.astype(BF16)
    k_scr[pl.ds(here, TB), :] = kv[:, :H]
    vt_scr[:, pl.ds(here, TB)] = vt.astype(BF16)
    routes = jnp.concatenate(sorted_rows(route_ref[k : k + 1, :] for k in range(TOPK)), axis=0)
    sorted_ref[...] = routes
    experts = lax.broadcasted_iota(jnp.int32, (E, TB), 0)
    chosen = []
    counts = count_scr[...]
    for k in range(TOPK):
        named = slot_of(routes, k, E) == experts
        chosen.append(jnp.sum(jnp.where(named, logits, 0.0), axis=0, keepdims=True))
        counts = counts + named.astype(F32)
    count_scr[...] = counts
    chosen = jnp.concatenate(chosen, axis=0)
    raised = jnp.exp(chosen - jnp.max(chosen, axis=0, keepdims=True))
    gate_ref[...] = raised / jnp.sum(raised, axis=0, keepdims=True)
    low_scr[...] = all_scr[0:QW, :].astype(BF16)
    for k in range(TOPK):
        q_ref[k * H : (k + 1) * H, :] = pick_heads(routes, low_scr, k) * jnp.asarray(H ** (-0.5), BF16)

    def attend(lanes, block, blocks):
        rows = blocks * QB
        first_key = pl.multiple_of((block - (blocks - 1)) * QB, QB)
        mask = key_mask(first_key, block * QB, rows, start_ref[:, lanes])
        keys = k_scr[pl.ds(first_key, rows), :]
        values = vt_scr[:, pl.ds(first_key, rows)]
        for k in range(0, TOPK, 2):
            scores = jnp.where(mask, nn(keys, pair_of(q_ref, k, lanes)), NEG_LARGE)
            top = jnp.max(scores, axis=0, keepdims=True)
            raised = jnp.exp(scores - top)
            total = jnp.sum(raised, axis=0, keepdims=True)
            out = nn(values, (raised * (1.0 / total)).astype(BF16))
            lse = top + jnp.log(total)
            for side in range(2):
                one = slice(side * QB, (side + 1) * QB)
                att_ref[(k + side) * H : (k + side + 1) * H, lanes] = out[:, one]
                lse_ref[k + side : k + side + 1, lanes] = lse[:, one]

    by_span(attend, place, start_ref)

    @pl.when(step == steps - 1)
    def _():
        held = jnp.sum(count_scr[...], axis=1, keepdims=True)
        lane = lax.broadcasted_iota(jnp.int32, (E, 128), 1)
        row = lax.broadcasted_iota(jnp.int32, (E, 128), 0)
        count_ref[...] = jnp.sum(jnp.where(lane == row, held, 0.0), axis=0, keepdims=True)


def picks(rows, stride, first):
    at = lax.broadcasted_iota(jnp.int32, (rows, D), 1)
    row = lax.broadcasted_iota(jnp.int32, (rows, D), 0)
    return (at == row * stride + first).astype(F32)


def exact(product, a, b):
    return lax.dot_general(
        a, b, (product, ((), ())), precision=lax.Precision.HIGHEST, preferred_element_type=F32
    )


def gelu_parts(v):
    size = jnp.abs(v) * 0.7071067811865476
    bell = jnp.exp(-(size * size))
    t = 1.0 / (1.0 + 0.3275911 * size)
    series = t * (
        0.254829592
        + t * (-0.284496736 + t * (1.421413741 + t * (-1.453152027 + t * 1.061405429)))
    )
    tail = 0.5 * series * bell
    cdf = jnp.where(v < 0.0, tail, 1.0 - tail)
    return cdf, bell * 0.3989422804014327


def middle_kernel(
    x_ref, dy_ref, gain_ref, wo_ref, w1_ref, w2_ref, route_ref, gate_ref, att_ref,
    out_ref, dres_ref, datt_ref, delta_ref, dlogit_ref, flat_ref, extra_ref, dgain_ref,
    slot_scr, head_scr, mix_scr, dwo_ref, dw1_ref, dw2t_ref, rows_scr, low_scr, row_sem,
):
    step = pl.program_id(0)

    @pl.when(step == 0)
    def _():
        dwo_ref[...] = jnp.zeros_like(dwo_ref)
        dw1_ref[...] = jnp.zeros_like(dw1_ref)
        dw2t_ref[...] = jnp.zeros_like(dw2t_ref)
        dgain_ref[...] = jnp.zeros_like(dgain_ref)

    routes = route_ref[...]
    tokens = routes.shape[1]
    gates = gate_ref[...]
    for k in range(TOPK):
        rows = slice(k * H, (k + 1) * H)
        slot_scr[rows, :] = (gates[k : k + 1, :] * att_ref[rows, :]).astype(BF16)
    place_heads(routes, slot_scr, mix_scr)
    x = x_ref[...].astype(F32)
    dy = dy_ref[...]
    mixed = mix_scr[...]
    residual = x + tn(mixed, wo_ref[...])
    scale = rms_scale(residual)
    gain = gain_ref[...]
    second = (residual * scale * gain).astype(BF16)
    second_t = second.T
    dy_t = dy.T
    out = residual
    dsecond = jnp.zeros((tokens, D), F32)
    for c in range(0, FF, FC):
        up = w1_ref[:, c : c + FC]
        down = w2_ref[c : c + FC, :]
        pre = nn(second, up)
        cdf, density = gelu_parts(pre)
        hidden = (pre * cdf).astype(BF16)
        dpre = (nt(dy, down) * (cdf + pre * density)).astype(BF16)
        out = out + nn(hidden, down)
        dsecond = dsecond + nt(dpre, up)
        dw2t_ref[:, c : c + FC] += nn(dy_t, hidden)
        dw1_ref[:, c : c + FC] += nn(second_t, dpre)
    out_ref[...] = out.astype(BF16)
    dgain_ref[...] += jnp.sum(dsecond * residual * scale, axis=0, keepdims=True)
    weighted = gain * dsecond
    dres = (
        dy.astype(F32)
        + scale * weighted
        - residual * (scale * scale * scale) * jnp.mean(weighted * residual, axis=-1, keepdims=True)
    )
    dres_ref[...] = dres
    branch = dres.astype(BF16)
    dwo_ref[...] += nn(mixed, branch)
    head_scr[...] = nt(wo_ref[...], branch).astype(BF16)
    dgates = []
    for k in range(TOPK):
        rows = slice(k * H, (k + 1) * H)
        dslot = pick_heads(routes, head_scr, k).astype(F32)
        attended = att_ref[rows, :]
        dgates.append(jnp.sum(dslot * attended, axis=0, keepdims=True))
        datt = (gates[k : k + 1, :] * dslot).astype(BF16)
        datt_ref[rows, :] = datt
        delta_ref[k : k + 1, :] = jnp.sum(datt.astype(F32) * attended, axis=0, keepdims=True)
    dgate = jnp.concatenate(dgates, axis=0)
    dchosen = gates * (dgate - jnp.sum(gates * dgate, axis=0, keepdims=True))
    experts = lax.broadcasted_iota(jnp.int32, (E, tokens), 0)
    dlogits = jnp.zeros((E, tokens), F32)
    for k in range(TOPK):
        dlogits = jnp.where(
            slot_of(routes, k, E) == experts,
            jnp.broadcast_to(dchosen[k : k + 1, :], (E, tokens)),
            dlogits,
        )
    dlogit_ref[...] = dlogits

    @pl.when(step == pl.num_programs(0) - 1)
    def _():
        for c in range(D // 128):
            lanes = slice(c * 128, (c + 1) * 128)
            rows_scr[pl.ds(c, QW, stride=4), :] = dwo_ref[:, lanes]
            rows_scr[pl.ds(W2_ROW - WO_ROW + c, FF, stride=4), :] = dw2t_ref[lanes, :].T
        for c in range(FF // 128):
            rows_scr[pl.ds(W1_ROW - WO_ROW + c, D, stride=16), :] = dw1_ref[:, c * 128 : (c + 1) * 128]
        extra_ref[...] = rows_scr[0:8, :]
        low_scr[...] = rows_scr[8:, :].astype(BF16)
        copy = pltpu.make_async_copy(
            low_scr, flat_ref.at[pl.ds(WO_ROW + 8, low_scr.shape[0]), :], row_sem.at[0]
        )
        copy.start()
        copy.wait()


def head_backward_kernel(
    x_ref, gain_ref, wall_ref, route_ref, start_ref, q_ref, datt_ref,
    lse_ref, delta_ref, kv_ref, kvt_ref, dlogit_ref, dres_ref, dgain_two_ref, extra_ref, flat_in,
    dx_ref, flat_ref,
    dk_scr, dv_scr, dq_scr, dall_scr, dwall_ref, dgain_ref, rows_scr, low_scr, row_sem,
):
    step = pl.program_id(0)
    place = NB - 1 - lax.rem(step, NB)
    here = pl.multiple_of(place * TB, TB)

    @pl.when(step == 0)
    def _():
        dwall_ref[...] = jnp.zeros_like(dwall_ref)
        dgain_ref[...] = jnp.zeros_like(dgain_ref)

    @pl.when(lax.rem(step, NB) == 0)
    def _():
        dk_scr[...] = jnp.zeros_like(dk_scr)
        dv_scr[...] = jnp.zeros_like(dv_scr)

    def attend(lanes, block, blocks):
        rows = blocks * QB
        first_key = pl.multiple_of((block - (blocks - 1)) * QB, QB)
        mask = key_mask(first_key, block * QB, rows, start_ref[:, lanes])
        keys = kv_ref[pl.ds(first_key, rows), :H]
        values = kv_ref[pl.ds(first_key, rows), H:]
        keys_t = kvt_ref[:H, pl.ds(first_key, rows)]
        dk = jnp.zeros((rows, H), F32)
        dv = jnp.zeros((rows, H), F32)
        for k in range(0, TOPK, 2):
            query = pair_of(q_ref, k, lanes)
            datt = pair_of(datt_ref, k, lanes)
            scores = jnp.where(mask, nn(keys, query), NEG_LARGE)
            probs = jnp.exp(scores - row_pair(lse_ref, k, lanes))
            dscore = (probs * (nn(values, datt) - row_pair(delta_ref, k, lanes))).astype(BF16)
            dv = dv + nt(probs.astype(BF16), datt)
            dk = dk + nt(dscore, query)
            dq = (nn(keys_t, dscore) * (H ** (-0.5))).astype(BF16)
            dq_scr[k * H : (k + 1) * H, lanes] = dq[:, :QB]
            dq_scr[(k + 1) * H : (k + 2) * H, lanes] = dq[:, QB:]
        dk_scr[pl.ds(first_key, rows), :] += dk
        dv_scr[pl.ds(first_key, rows), :] += dv

    by_span(attend, place, start_ref)
    place_heads(route_ref[...], dq_scr, dall_scr)
    dkv = jnp.concatenate([dk_scr[pl.ds(here, TB), :], dv_scr[pl.ds(here, TB), :]], axis=1)
    dall_scr[KROW : KROW + 2 * H, :] = dkv.T.astype(BF16)
    dall_scr[RROW : RROW + 32, :] = jnp.concatenate(
        [dlogit_ref[...], jnp.zeros((32 - E, TB), F32)], axis=0
    ).astype(BF16)
    x = x_ref[...].astype(F32)
    scale = rms_scale(x)
    gain = gain_ref[...]
    normed = (x * scale * gain).astype(BF16)
    dall = dall_scr[...]
    dwall_ref[...] += nn(dall, normed)
    dnormed = tn(dall, wall_ref[...])
    dgain_ref[...] += jnp.sum(dnormed * x * scale, axis=0, keepdims=True)
    weighted = gain * dnormed
    dx_ref[...] = (
        dres_ref[...]
        + scale * weighted
        - x * (scale * scale * scale) * jnp.mean(weighted * x, axis=-1, keepdims=True)
    )

    @pl.when(step == pl.num_programs(0) - 1)
    def _():
        for c in range(D // 128):
            lanes = slice(c * 128, (c + 1) * 128)
            rows_scr[c : c + 1, :] = dgain_ref[:, lanes]
            rows_scr[4 + c : 5 + c, :] = dgain_two_ref[:, lanes]
        router_t = dwall_ref[RROW : RROW + E, :]
        across = jnp.concatenate(
            [exact(((1,), (1,)), router_t, picks(32, 16, b)) for b in range(16)], axis=0
        ).T
        for j in range(3):
            rows_scr[pl.ds(WR_ROW + j, 32, stride=3), :] = across[:, j * 128 : (j + 1) * 128]
        for first, row in ((KROW, WK_ROW), (VROW, WV_ROW)):
            part = dwall_ref[first : first + H, :]
            rows_scr[row : row + 256, :] = jnp.concatenate(
                [exact(((1,), (1,)), picks(256, 2, b), part) for b in range(2)], axis=1
            )
        for c in range(QW // 128):
            rows_scr[pl.ds(WQ_ROW + c, D, stride=12), :] = dwall_ref[c * 128 : (c + 1) * 128, :].T
        rows_scr[WO_ROW : WO_ROW + 8, :] = extra_ref[...]
        low_scr[...] = rows_scr[...].astype(BF16)
        copy = pltpu.make_async_copy(low_scr, flat_ref.at[pl.ds(0, WO_ROW + 8), :], row_sem.at[0])
        copy.start()
        copy.wait()


def whole(shape):
    return pl.BlockSpec(shape, lambda *_: (0,) * len(shape), pipeline_mode=pl.Buffered(1))


def kept(shape):
    return pl.BlockSpec(shape, lambda *_: (0,) * len(shape))


def struct(shape, kind=F32):
    return jax.ShapeDtypeStruct(shape, kind)


def params_for(mib):
    return pltpu.CompilerParams(vmem_limit_bytes=mib * MIB)


def head_forward(tokens, routes_t, segments, wall, gain):
    count = tokens.shape[0]
    steps = count // TB
    across = lambda rows: pl.BlockSpec((rows, TB), lambda b: (0, b))
    down = lambda columns: pl.BlockSpec((TB, columns), lambda b: (b, 0))
    return pl.pallas_call(
        functools.partial(head_forward_kernel, steps),
        grid=(steps,),
        in_specs=[down(D), across(TOPK), whole(segments.shape), whole((ALLW, D)), whole((1, D))],
        out_specs=[
            across(TOPK * H), across(TOPK * H), across(TOPK), across(TOPK), down(2 * H), across(2 * H),
            across(1), across(TOPK), whole((1, 128)),
        ],
        scratch_shapes=[
            pltpu.VMEM((ALLW, TB), F32),
            pltpu.VMEM((QW, TB), BF16),
            pltpu.VMEM((LEN, H), BF16),
            pltpu.VMEM((H, LEN), BF16),
            pltpu.VMEM((E, TB), F32),
        ],
        out_shape=[
            struct((TOPK * H, count), BF16),
            struct((TOPK * H, count)),
            struct((TOPK, count)),
            struct((TOPK, count)),
            struct((count, 2 * H), BF16),
            struct((2 * H, count), BF16),
            struct((1, count), jnp.int32),
            struct((TOPK, count), jnp.int32),
            struct((1, 128)),
        ],
        compiler_params=params_for(56),
        name="head_forward",
        cost_estimate=pl.CostEstimate(flops=10_000_000_000, bytes_accessed=16_000_000, transcendentals=0),
    )(tokens, routes_t, segments, wall, gain)


def middle(flat_rows, tokens, grad_out, gain, wo, w1, w2, routes_t, gates, attended):
    count = tokens.shape[0]
    steps = count // TB
    across = lambda rows: pl.BlockSpec((rows, TB), lambda b: (0, b))
    down = lambda columns: pl.BlockSpec((TB, columns), lambda b: (b, 0))
    return pl.pallas_call(
        middle_kernel,
        grid=(steps,),
        in_specs=[
            down(D), down(D), whole((1, D)), whole((QW, D)), whole((D, FF)), whole((FF, D)),
            across(TOPK), across(TOPK), across(TOPK * H),
        ],
        out_specs=[
            down(D), down(D), across(TOPK * H), across(TOPK), across(E),
            pl.BlockSpec(memory_space=pl.ANY), whole((8, 128)), whole((1, D)),
        ],
        out_shape=[
            struct((count, D), BF16),
            struct((count, D)),
            struct((TOPK * H, count), BF16),
            struct((TOPK, count)),
            struct((E, count)),
            struct((flat_rows, 128), BF16),
            struct((8, 128)),
            struct((1, D)),
        ],
        scratch_shapes=[
            pltpu.VMEM((TOPK * H, TB), BF16),
            pltpu.VMEM((QW, TB), BF16),
            pltpu.VMEM((QW, TB), BF16),
            pltpu.VMEM((QW, D), F32),
            pltpu.VMEM((D, FF), F32),
            pltpu.VMEM((D, FF), F32),
            pltpu.VMEM((flat_rows - WO_ROW, 128), F32),
            pltpu.VMEM((flat_rows - WO_ROW - 8, 128), BF16),
            pltpu.SemaphoreType.DMA((1,)),
        ],
        compiler_params=params_for(60),
        name="middle",
    )(tokens, grad_out, gain, wo, w1, w2, routes_t, gates, attended)


def head_backward(
    tokens, gain, wall, routes_t, start, queries, datt, lse, delta, kv, kvt, dlogits, dres, dgain_two,
    extra, flat,
):
    count = tokens.shape[0]
    steps = count // TB

    def place(b):
        return (b // NB) * NB + NB - 1 - b % NB

    across = lambda rows: pl.BlockSpec((rows, TB), lambda b: (0, place(b)))
    down = lambda columns: pl.BlockSpec((TB, columns), lambda b: (place(b), 0))
    return pl.pallas_call(
        head_backward_kernel,
        grid=(steps,),
        in_specs=[
            down(D), whole((1, D)), whole((ALLW, D)), across(TOPK), across(1),
            across(TOPK * H), across(TOPK * H), across(TOPK), across(TOPK),
            pl.BlockSpec((LEN, 2 * H), lambda b: (b // NB, 0)),
            pl.BlockSpec((2 * H, LEN), lambda b: (0, b // NB)),
            across(E), down(D), whole((1, D)), whole((8, 128)), pl.BlockSpec(memory_space=pl.ANY),
        ],
        out_specs=[down(D), pl.BlockSpec(memory_space=pl.ANY)],
        scratch_shapes=[
            pltpu.VMEM((LEN, H), F32),
            pltpu.VMEM((LEN, H), F32),
            pltpu.VMEM((TOPK * H, TB), BF16),
            pltpu.VMEM((ALLW, TB), BF16),
            pltpu.VMEM((ALLW, D), F32),
            pltpu.VMEM((1, D), F32),
            pltpu.VMEM((WO_ROW + 8, 128), F32),
            pltpu.VMEM((WO_ROW + 8, 128), BF16),
            pltpu.SemaphoreType.DMA((1,)),
        ],
        out_shape=[struct((count, D)), struct(flat.shape, BF16)],
        input_output_aliases={15: 1},
        compiler_params=params_for(56),
        name="head_backward",
        cost_estimate=pl.CostEstimate(flops=30_000_000_000, bytes_accessed=24_000_000, transcendentals=0),
    )(
        tokens, gain, wall, routes_t, start, queries, datt, lse, delta, kv, kvt, dlogits, dres,
        dgain_two, extra, flat,
    )


class Mesh3:
    def __init__(self, shards, over):
        shard = lax.axis_index("dp")
        other = lax.axis_index("fsdp")
        self.over = over
        self.many = shards * over
        self.sizes = {"x": 2, "y": shards // 2, "z": over // 2}
        self.here = {"x": lax.rem(other, 2), "y": lax.div(shard, 2), "z": lax.div(other, 2)}
        self.core = lax.rem(shard, 2)
        self.me = shard * over + other
        self.partner = (shard + 1 - 2 * self.core, other)

    def moved(self, steps):
        return {
            axis: lax.rem(self.here[axis] + steps.get(axis, 0), self.sizes[axis]) for axis in "xyz"
        }

    def device(self, core, steps):
        at = self.moved(steps)
        return (at["y"] * 2 + core, at["z"] * 2 + at["x"])

    def number(self, core, steps):
        shard, other = self.device(core, steps)
        return shard * self.over + other

    def nth(self, number):
        return (lax.div(number, self.over), lax.rem(number, self.over))

    def greet_near(self):
        devices = [
            self.device(self.core, {axis: step})
            for axis in "xyz"
            for step in range(1, self.sizes[axis])
        ] + [self.partner]
        barrier = pltpu.get_barrier_semaphore()
        for device in devices:
            pl.semaphore_signal(barrier, inc=1, device_id=device, device_id_type=MESH)
        pl.semaphore_wait(barrier, len(devices))

    def greet_all(self):
        barrier = pltpu.get_barrier_semaphore()

        def hello(j, carry):
            device = self.nth(lax.rem(self.me + j, self.many))
            pl.semaphore_signal(barrier, inc=1, device_id=device, device_id_type=MESH)
            return carry

        lax.fori_loop(1, self.many, hello, 0)
        pl.semaphore_wait(barrier, self.many - 1)


def along_z(step):
    return {1: (0, 3), 2: (1, 5), 3: (3, 8)}.get(step, (step, 2 * step + 2))


class Kind:
    def __init__(self, mesh, core, axes):
        self.mesh = mesh
        self.core = core
        self.axes = axes
        ranges = [range(mesh.sizes[axis]) for axis in axes]
        self.offsets = list(itertools.product(*ranges))
        self.index = {one: number for number, one in enumerate(self.offsets)}

    def owner(self, offsets):
        return self.mesh.number(self.core, dict(zip(self.axes, offsets)))

    def last(self, offsets):
        return max([i for i in range(3) if offsets[i]], default=-1)

    def turn(self, offsets):
        total = 0
        for axis, step in zip(self.axes, offsets):
            if step:
                total += along_z(step)[1] if axis == "z" else 2
        return total

    def hops(self, offsets):
        for i in range(self.last(offsets) + 1, 3):
            for step in range(1, self.mesh.sizes[self.axes[i]]):
                delay = along_z(step)[0] if self.axes[i] == "z" else 0
                yield i, step, self.turn(offsets) + delay

    def ahead(self, i, step):
        return self.mesh.device(self.core, {self.axes[i]: step})


AXES = ("zxy", "zyx")


def pieces_of(window):
    if window < 512:
        return [(0, window)]
    first = (window // 16 + 1) // 2 * 16
    return [(0, first), (first, window - first)]


def gather_events(mesh, own_ref, land, send_sem, recv_sem, laid):
    events = []
    pieces = pieces_of(own_ref.shape[0])
    kinds = [Kind(mesh, core, AXES[core]) for core in range(2)]
    end = 2 * max(kind.turn(one) for kind in kinds for one in kind.offsets) + 4

    def copy(owner, device, slot, p):
        rows = pl.ds(*pieces[p])
        return pltpu.make_async_remote_copy(
            src_ref=land.at[owner, rows],
            dst_ref=land.at[owner, rows],
            send_sem=send_sem.at[slot, p],
            recv_sem=recv_sem.at[owner, p],
            device_id=device,
            device_id_type=MESH,
        )

    def event(turn, condition, action):
        events.append((turn, lambda: pl.when(condition)(action)))

    for kind in kinds:
        ours = mesh.core == kind.core
        theirs = mesh.core != kind.core
        slots = itertools.count()
        for offsets in kind.offsets:
            owner = kind.owner(offsets)
            slot = next(slots)
            hops = [(i, step, turn, next(slots)) for i, step, turn in kind.hops(offsets)]
            for p in range(len(pieces)):

                def come(owner=owner, offsets=offsets, slot=slot, p=p, kind=kind, hops=hops):
                    if any(offsets):
                        copy(owner, mesh.partner, slot, p).wait_recv()
                    elif p == 0:
                        land[owner] = own_ref[...]
                    for i, step, turn, number in hops:
                        if turn == kind.turn(offsets):
                            copy(owner, kind.ahead(i, step), number, p).start()
                    copy(owner, mesh.partner, slot, p).start()
                    laid(owner, p)

                def across(owner=owner, slot=slot, p=p):
                    copy(owner, mesh.partner, slot, p).wait_recv()
                    laid(owner, p)

                def done(owner=owner, slot=slot, p=p, hops=hops):
                    copy(owner, mesh.partner, slot, p).wait_send()
                    for _, _, _, number in hops:
                        copy(owner, mesh.partner, number, p).wait_send()

                event(2 * kind.turn(offsets) + p, ours, come)
                event(end + kind.turn(offsets) / 100, theirs, across)
                event(end + 1, ours, done)
                for i, step, turn, number in hops:
                    if turn == kind.turn(offsets):
                        continue

                    def send(owner=owner, device=kind.ahead(i, step), number=number, p=p):
                        copy(owner, device, number, p).start()

                    event(2 * turn + p, ours, send)
    return sorted(events, key=lambda one: one[0])


def reduce_events(mesh, source, fetch, part, outgo, income, send_sem, recv_sem, finish):
    events = []
    half = mesh.many // 2
    pieces = pieces_of(outgo.shape[1])
    kinds = [Kind(mesh, core, AXES[core]) for core in range(2)]
    end = 2 * max(kind.turn(one) for kind in kinds for one in kind.offsets) + 4

    def copy(slot, device, p, begin=None):
        rows = pl.ds(*pieces[p])
        return pltpu.make_async_remote_copy(
            src_ref=outgo.at[slot, rows] if begin is None else begin,
            dst_ref=income.at[slot, rows],
            send_sem=send_sem.at[slot, p],
            recv_sem=recv_sem.at[slot, p],
            device_id=device,
            device_id_type=MESH,
        )

    def event(turn, condition, action):
        events.append((turn, lambda: pl.when(condition)(action)))

    def taken(slot, p):
        copy(slot, mesh.partner, p).wait_recv()
        return income[slot, pl.ds(*pieces[p])].astype(F32)

    for kind in kinds:
        ours = mesh.core == kind.core
        theirs = mesh.core != kind.core
        slots = {}
        for offsets in kind.offsets:
            if any(offsets):
                slots[offsets] = half + len(slots)
        for offsets in kind.offsets:
            owner = kind.owner(offsets)
            number = kind.index[offsets]
            axis = kind.last(offsets)
            turn = end - 2 * kind.turn(offsets)
            for p, (first, rows) in enumerate(pieces):

                def hand(owner=owner, number=number, p=p, first=first, rows=rows):
                    copy(number, mesh.partner, p, source(owner, first, rows)).start()

                def onward(
                    owner=owner, offsets=offsets, number=number, axis=axis, kind=kind, slots=slots, p=p
                ):
                    mine = pl.ds(*pieces[p])
                    fetch(owner, number, p).wait()
                    total = part[number, mine].astype(F32) + taken(number, p)
                    for i, step, _ in kind.hops(offsets):
                        longer = tuple(step if j == i else o for j, o in enumerate(offsets))
                        total = total + taken(slots[longer], p)
                    if axis < 0:
                        finish(total, p)
                    else:
                        outgo[slots[offsets], mine] = total.astype(BF16)
                        copy(slots[offsets], kind.ahead(axis, offsets[axis]), p).start()

                def handed(number=number, p=p):
                    copy(number, mesh.partner, p).wait_send()

                event(-1 - kind.turn(offsets) / 100, theirs, hand)
                event(-2, ours, lambda owner=owner, number=number, p=p: fetch(owner, number, p).start())
                event(turn + p, ours, onward)
                event(end + 2, theirs, handed)
                if axis >= 0:

                    def passed(slot=slots[offsets], p=p):
                        copy(slot, mesh.partner, p).wait_send()

                    event(end + 2, ours, passed)
    return sorted(events, key=lambda one: one[0])


def window_rows(shard_size, many):
    units = [(shard_size * d) // UNIT for d in range(many + 1)]
    return 16 * (max(b - a for a, b in zip(units, units[1:])) + 1)


def first_row(shard_size, number):
    if isinstance(number, int):
        return number * shard_size // UNIT * 16
    return pl.multiple_of(lax.div(number * shard_size, UNIT) * 16, 16)


def inner_units(shard_size, many):
    units = [(shard_size * d) // UNIT for d in range(many + 1)]
    return min(b - a for a, b in zip(units, units[1:]))


def lay_inner(shard_size, many, land, flat, owner, first, rows):
    begin = max(first, 16)
    count = min(first + rows, 16 * inner_units(shard_size, many)) - begin
    row = pl.multiple_of(first_row(shard_size, owner) + begin, 16)
    flat[pl.ds(row, count), :] = land[owner, pl.ds(begin, count), :].astype(F32)


def lay_edges(shard_size, many, land, flat):
    inner = 16 * inner_units(shard_size, many)
    flat[0:16, :] = jnp.zeros((16, 128), F32)

    def lay(number, carry):
        row = first_row(shard_size, number)
        after = first_row(shard_size, number + 1)
        flat[pl.ds(row, 16), :] += land[number, 0:16, :].astype(F32)
        tail = land[number, pl.ds(inner, 16), :].astype(F32)
        flat[pl.ds(pl.multiple_of(row + inner, 16), 16), :] = tail
        last = pl.multiple_of(after - row, 16)
        flat[pl.ds(after, 16), :] = land[number, pl.ds(last, 16), :].astype(F32)
        return carry

    lax.fori_loop(0, many, lay, 0)


def early_matrices(flat, wall_ref, gain_one_ref, gain_two_ref):
    for c in range(D // 128):
        lanes = slice(c * 128, (c + 1) * 128)
        gain_one_ref[:, lanes] = flat[c : c + 1, :]
        gain_two_ref[:, lanes] = flat[4 + c : 5 + c, :]
    for c in range(QW // 128):
        wall_ref[c * 128 : (c + 1) * 128, :] = flat[pl.ds(WQ_ROW + c, D, stride=12), :].T.astype(BF16)
    for first, row in ((KROW, WK_ROW), (VROW, WV_ROW)):
        pair = flat[row : row + 256, :].T.astype(BF16)
        wall_ref[first : first + H, :] = (
            nn(pair[:H], picks(256, 2, 0).astype(BF16)) + nn(pair[H:], picks(256, 2, 1).astype(BF16))
        ).astype(BF16)
    across = jnp.concatenate(
        [flat[pl.ds(WR_ROW + j, 32, stride=3), :] for j in range(3)], axis=1
    ).T.astype(BF16)
    router_t = jnp.zeros((E, D), F32)
    for part in range(16):
        router_t = router_t + nn(across[part * E : (part + 1) * E, :], picks(32, 16, part).astype(BF16))
    wall_ref[RROW:ALLW, :] = jnp.concatenate(
        [router_t, jnp.zeros((ALLW - RROW - E, D), F32)], axis=0
    ).astype(BF16)


def gather_kernel(
    mesh, shard_size, own_ref,
    wall_out, gain_one_ref, gain_two_ref, wo_out, w1_out, w2_out,
    land, flat, wall_ref, wo_ref, w1_ref, w2_ref, send_sem, recv_sem, out_sem,
):
    mesh = mesh()
    many = mesh.many
    pieces = pieces_of(own_ref.shape[0])
    mesh.greet_near()

    def laid(owner, p):
        lay_inner(shard_size, many, land, flat, owner, *pieces[p])

    for _, action in gather_events(mesh, own_ref, land, send_sem, recv_sem, laid):
        action()
    lay_edges(shard_size, many, land, flat)
    copies = []

    def leave(matrix, out):
        copy = pltpu.make_async_copy(matrix, out, out_sem.at[len(copies)])
        copy.start()
        copies.append(copy)

    for c in range(D // 128):
        wo_ref[:, c * 128 : (c + 1) * 128] = flat[pl.ds(WO_ROW + c, QW, stride=4), :].astype(BF16)
    leave(wo_ref, wo_out)
    for c in range(D // 128):
        w2_ref[:, c * 128 : (c + 1) * 128] = flat[pl.ds(W2_ROW + c, FF, stride=4), :].astype(BF16)
    leave(w2_ref, w2_out)
    for c in range(FF // 128):
        w1_ref[:, c * 128 : (c + 1) * 128] = flat[pl.ds(W1_ROW + c, D, stride=16), :].astype(BF16)
    leave(w1_ref, w1_out)
    early_matrices(flat, wall_ref, gain_one_ref, gain_two_ref)
    leave(wall_ref, wall_out)
    for copy in copies:
        copy.wait()


def gather_weights(shards, over, shard_size, own):
    window = own.shape[0]
    many = shards * over
    rows = (shard_size * (many - 1)) // UNIT * 16 + window
    vmem = pl.BlockSpec(memory_space=pltpu.VMEM)
    hbm = pl.BlockSpec(memory_space=pl.ANY)
    mesh = functools.partial(Mesh3, shards, over)
    pieces = len(pieces_of(window))
    return pl.pallas_call(
        functools.partial(gather_kernel, mesh, shard_size),
        in_specs=[vmem],
        out_specs=[hbm, vmem, vmem, hbm, hbm, hbm],
        out_shape=[
            struct((ALLW, D), BF16),
            struct((1, D)),
            struct((1, D)),
            struct((QW, D), BF16),
            struct((D, FF), BF16),
            struct((FF, D), BF16),
        ],
        scratch_shapes=[
            pltpu.VMEM((many, window, 128), BF16),
            pltpu.VMEM((rows, 128), F32),
            pltpu.VMEM((ALLW, D), BF16),
            pltpu.VMEM((QW, D), BF16),
            pltpu.VMEM((D, FF), BF16),
            pltpu.VMEM((FF, D), BF16),
            pltpu.SemaphoreType.DMA((many, pieces)),
            pltpu.SemaphoreType.DMA((many, pieces)),
            pltpu.SemaphoreType.DMA((4,)),
        ],
        compiler_params=pltpu.CompilerParams(
            collective_id=0, has_side_effects=True, vmem_limit_bytes=60 * MIB
        ),
        name="gather_weights",
    )(own)


def reduce_kernel(
    mesh, shard_size, flat_ref, count_ref,
    out_ref, total_ref, gain_ref,
    part, outgo, income, stats, gains, part_sem, send_sem, recv_sem, stat_send, stat_recv, gain_send, gain_recv,
):
    mesh = mesh()
    many = mesh.many
    window = out_ref.shape[0]
    pieces = pieces_of(window)

    def source(owner, first, rows):
        row = pl.multiple_of(first_row(shard_size, owner) + first, 16)
        return flat_ref.at[pl.ds(row, rows), :]

    def fetch(owner, number, p):
        return pltpu.make_async_copy(
            source(owner, *pieces[p]), part.at[number, pl.ds(*pieces[p])], part_sem.at[number, p]
        )

    def finish(total, p):
        out_ref[pl.ds(*pieces[p]), :] = total

    mesh.greet_all()
    for _, action in reduce_events(mesh, source, fetch, part, outgo, income, send_sem, recv_sem, finish):
        action()
    total = out_ref[...]
    begin = mesh.me * shard_size - lax.div(mesh.me * shard_size, UNIT) * UNIT
    at = (
        lax.broadcasted_iota(jnp.int32, (window, 128), 0) * 128
        + lax.broadcasted_iota(jnp.int32, (window, 128), 1)
    )
    inside = jnp.where((at >= begin) & (at < begin + shard_size), total, 0.0)
    squares = jnp.sum(jnp.sum(inside * inside, axis=0, keepdims=True), axis=1, keepdims=True)
    lane = lax.broadcasted_iota(jnp.int32, (1, 128), 1)
    stats[0] = jnp.where(lane == E, squares, count_ref[...])

    def told(j):
        return pltpu.make_async_remote_copy(
            src_ref=stats.at[0],
            dst_ref=stats.at[j],
            send_sem=stat_send.at[j],
            recv_sem=stat_recv.at[j],
            device_id=mesh.nth(lax.rem(mesh.me + j, many)),
            device_id_type=MESH,
        )

    def shown(j):
        return pltpu.make_async_remote_copy(
            src_ref=gains,
            dst_ref=gains,
            send_sem=gain_send.at[j],
            recv_sem=gain_recv.at[0],
            device_id=mesh.nth(lax.rem(mesh.me + j, many)),
            device_id_type=MESH,
        )

    def tell(j, carry):
        told(j).start()
        return carry

    def hear(j, carry):
        told(j).wait()
        return carry

    def show(j, carry):
        shown(j).start()
        return carry

    def showed(j, carry):
        shown(j).wait_send()
        return carry

    lax.fori_loop(1, many, tell, 0)

    @pl.when(mesh.me == 0)
    def _():
        gains[...] = total[0:8, :]
        lax.fori_loop(1, many, show, 0)
        lax.fori_loop(1, many, showed, 0)

    @pl.when(mesh.me != 0)
    def _():
        shown(1).wait_recv()

    lax.fori_loop(1, many, hear, 0)
    total_ref[...] = jnp.sum(stats[...], axis=0)
    gain_ref[...] = gains[...]


def reduce_grads(shards, over, shard_size, window, flat, counts):
    vmem = pl.BlockSpec(memory_space=pltpu.VMEM)
    many = shards * over
    mesh = functools.partial(Mesh3, shards, over)
    pieces = len(pieces_of(window))
    return pl.pallas_call(
        functools.partial(reduce_kernel, mesh, shard_size),
        in_specs=[pl.BlockSpec(memory_space=pl.ANY), vmem],
        out_specs=[vmem] * 3,
        out_shape=[struct((window, 128)), struct((1, 128)), struct((8, 128))],
        scratch_shapes=[
            pltpu.VMEM((many // 2, window, 128), BF16),
            pltpu.VMEM((many, window, 128), BF16),
            pltpu.VMEM((many, window, 128), BF16),
            pltpu.VMEM((many, 1, 128), F32),
            pltpu.VMEM((8, 128), F32),
            pltpu.SemaphoreType.DMA((many // 2, pieces)),
            pltpu.SemaphoreType.DMA((many, pieces)),
            pltpu.SemaphoreType.DMA((many, pieces)),
            pltpu.SemaphoreType.DMA((many,)),
            pltpu.SemaphoreType.DMA((many,)),
            pltpu.SemaphoreType.DMA((many,)),
            pltpu.SemaphoreType.DMA((1,)),
        ],
        compiler_params=pltpu.CompilerParams(
            collective_id=1, has_side_effects=True, vmem_limit_bytes=56 * MIB
        ),
        name="reduce_grads",
    )(flat, counts)


def local_step(flat_rows, tokens, grad_out, routes, segments, weights):
    wall, gain_one, gain_two, wo, w1, w2 = weights
    queries, attended, gates, lse, kv, kvt, start, routes_t, counts = head_forward(
        tokens, routes.T, segments, wall, gain_one
    )
    output, dres, datt, delta, dlogits, flat, extra, dgain_two = middle(
        flat_rows, tokens, grad_out, gain_two, wo, w1, w2, routes_t, gates, attended
    )
    input_grad, flat = head_backward(
        tokens, gain_one, wall, routes_t, start, queries, datt, lse, delta, kv, kvt, dlogits, dres,
        dgain_two, extra, flat,
    )
    return output, input_grad, flat, counts


def per_device(
    shards, over, tokens, grad_out, routes, segments, params, first_moment, second_moment, ema_weights
):
    shard_size = params.shape[0]
    window = window_rows(shard_size, shards * over)
    flat_rows = (shard_size * (shards * over - 1)) // UNIT * 16 + window
    me = lax.axis_index("dp") * over + lax.axis_index("fsdp")
    begin = lax.rem(me * shard_size, UNIT)
    own = lax.dynamic_slice(
        jnp.pad(params.astype(BF16), (UNIT, window * 128 - shard_size)), (UNIT - begin,), (window * 128,)
    ).reshape(window, 128)
    wall, gain_one, gain_two, wo, w1, w2 = gather_weights(shards, over, shard_size, own)
    output, input_grad, flat, counts = local_step(
        flat_rows, tokens, grad_out, routes, segments, (wall, gain_one, gain_two, wo, w1, w2)
    )
    reduced, sums, gain_grads = reduce_grads(shards, over, shard_size, window, flat, counts)
    grad_shard = lax.dynamic_slice(reduced.reshape(-1), (begin,), (shard_size,))
    total_tokens = tokens.shape[0] * shards * over
    expert_load = sums[0, :E] * (E / (total_tokens * TOPK))
    grad_norm = jnp.sqrt(sums[0, E])
    clipped = grad_shard * (CLIP_LIMIT / jnp.maximum(grad_norm, CLIP_LIMIT))
    new_first = BETA_FIRST * first_moment + (1.0 - BETA_FIRST) * clipped
    new_second = BETA_SECOND * second_moment + (1.0 - BETA_SECOND) * clipped * clipped
    first_hat = new_first / (1.0 - BETA_FIRST**STEP)
    second_hat = new_second / (1.0 - BETA_SECOND**STEP)
    new_params = params * (1.0 - LEARN_RATE * DECAY_RATE) - LEARN_RATE * first_hat / (
        jnp.sqrt(second_hat) + ADAM_EPS
    )
    new_ema = EMA_KEEP * ema_weights + (1.0 - EMA_KEEP) * new_params
    return (
        output,
        input_grad,
        expert_load,
        grad_norm.reshape(1),
        new_params,
        new_first,
        new_second,
        new_ema,
        gain_grads.reshape(2, D),
    )


def solution(mesh):
    row = P(("dp", "fsdp"), None)
    flat = P(("dp", "fsdp"))
    return jax.shard_map(
        functools.partial(per_device, mesh.shape["dp"], mesh.shape["fsdp"]),
        mesh=mesh,
        in_specs=(row, row, row, row, flat, flat, flat, flat),
        out_specs=(row, row, P(), P(), flat, flat, flat, flat, P()),
        check_vma=False,
    )
```

```python
import functools
import itertools

import jax
import jax.numpy as jnp
from jax import lax
from jax.experimental import pallas as pl
from jax.experimental.pallas import tpu as pltpu
from jax.sharding import PartitionSpec as P

D = 512
E = 24
TOPK = 8
H = 64
FF = 2048
STEP = 10

NORM_EPS = 1e-06
CLIP_LIMIT = 1.0
BETA_FIRST = 0.9
BETA_SECOND = 0.95
LEARN_RATE = 0.1
DECAY_RATE = 0.1
ADAM_EPS = 1e-08
EMA_KEEP = 0.9
NEG_LARGE = -1e30

QW = E * H
KROW = QW
VROW = QW + H
RROW = QW + 2 * H
ALLW = 1696
LEN = 1024
TB = 256
NB = LEN // TB
QB = 128
MOST = 512 // QB + 1
SORT_STEPS = (
    (0, 1), (2, 3), (4, 5), (6, 7), (0, 2), (1, 3), (4, 6), (5, 7), (1, 2), (5, 6),
    (0, 4), (1, 5), (2, 6), (3, 7), (2, 4), (3, 5), (1, 2), (3, 4), (5, 6),
)
FC = 512
MB = 512
MIB = 1 << 20

WR_ROW = 8
WK_ROW = 104
WV_ROW = 360
WQ_ROW = 616
WO_ROW = 6760
W1_ROW = 12904
W2_ROW = 21096
ALL_ROWS = 29288
UNIT = 16 * 128
MESH = pl.DeviceIdType.MESH

F32 = jnp.float32
BF16 = jnp.bfloat16


def nn(a, b):
    return lax.dot_general(a, b, (((1,), (0,)), ((), ())), preferred_element_type=F32)


def nt(a, b):
    return lax.dot_general(a, b, (((1,), (1,)), ((), ())), preferred_element_type=F32)


def tn(a, b):
    return lax.dot_general(a, b, (((0,), (0,)), ((), ())), preferred_element_type=F32)


def rms_scale(values):
    return lax.rsqrt(jnp.mean(values * values, axis=-1, keepdims=True) + NORM_EPS)


def slot_of(routes, k, rows):
    return jnp.broadcast_to(routes[k : k + 1, :], (rows, routes.shape[1]))


def expert_rows(routes, k):
    return jnp.broadcast_to(routes.astype(jnp.int16)[k : k + 1, :], (16, routes.shape[1]))


def pick_heads(routes, source_ref, k):
    tokens = routes.shape[1]
    route = expert_rows(routes, k)
    taken = source_ref[k * H : (k + 1) * H, :].reshape(H // 16, 16, tokens)
    for e in range(k + 1, k + E - TOPK + 1):
        piece = source_ref[e * H : (e + 1) * H, :].reshape(H // 16, 16, tokens)
        taken = jnp.where((route == jnp.int16(e))[None], piece, taken)
    return taken.reshape(H, tokens)


def place_heads(routes, source_ref, target_ref):
    tokens = routes.shape[1]
    rows = [expert_rows(routes, k) for k in range(TOPK)]
    for e in range(E):
        total = jnp.zeros((H // 16, 16, tokens), BF16)
        for k in range(max(0, e - (E - TOPK)), min(TOPK - 1, e) + 1):
            piece = source_ref[k * H : (k + 1) * H, :].reshape(H // 16, 16, tokens)
            total = jnp.where((rows[k] == jnp.int16(e))[None], piece, total)
        target_ref[e * H : (e + 1) * H, :] = total.reshape(H, tokens)


def sorted_rows(rows):
    rows = list(rows)
    for one, two in SORT_STEPS:
        rows[one], rows[two] = jnp.minimum(rows[one], rows[two]), jnp.maximum(rows[one], rows[two])
    return rows


def key_mask(first_key, first_query, rows, start_row):
    keys = lax.broadcasted_iota(jnp.int32, (rows, QB), 0) + first_key
    queries = lax.broadcasted_iota(jnp.int32, (rows, QB), 1) + first_query
    mask = (keys <= queries) & (keys >= start_row)
    return jnp.concatenate([mask, mask], axis=1)


def pair_of(ref, k, lanes):
    return jnp.concatenate(
        [ref[k * H : (k + 1) * H, lanes], ref[(k + 1) * H : (k + 2) * H, lanes]], axis=1
    )


def row_pair(ref, k, lanes):
    return jnp.concatenate([ref[k : k + 1, lanes], ref[k + 1 : k + 2, lanes]], axis=1)


def by_span(attend, row, place, segment_ref):
    def one(j, carry):
        block = place * (TB // QB) + j
        first = block * QB
        span = jnp.int32(1)
        for back in range(MOST - 1):
            last = first - back * QB - 1
            same = segment_ref[row, jnp.maximum(last, 0)] == segment_ref[row, first]
            span = span + jnp.where((last >= 0) & same, 1, 0)
        for blocks in range(1, MOST + 1):

            @pl.when(span == blocks)
            def _(blocks=blocks):
                attend(pl.ds(pl.multiple_of(j * QB, QB), QB), block, blocks)

        return carry

    lax.fori_loop(0, TB // QB, one, 0)


def head_forward_kernel(
    steps, segment_smem, x_ref, route_ref, segment_ref, wall_ref, gain_ref,
    q_ref, att_ref, gate_ref, lse_ref, kv_ref, kvt_ref, start_ref, sorted_ref, count_ref,
    all_scr, low_scr, k_scr, vt_scr, count_scr,
):
    step = pl.program_id(0)
    place = lax.rem(step, NB)
    here = pl.multiple_of(place * TB, TB)

    @pl.when(step == 0)
    def _():
        count_scr[...] = jnp.zeros_like(count_scr)

    row = segment_ref[pl.ds(lax.div(step, NB), 1), :]
    segments = segment_ref[pl.ds(lax.div(step, NB), 1), pl.ds(here, TB)]
    start = jnp.zeros((1, TB), jnp.int32)
    for number in range(1, 4):
        below = jnp.sum((row < number).astype(jnp.int32), axis=1, keepdims=True)
        start = jnp.where(segments == number, below, start)
    start_ref[...] = start
    x = x_ref[...].astype(F32)
    normed = (x * rms_scale(x) * gain_ref[...]).astype(BF16)
    all_scr[...] = nt(wall_ref[...], normed)
    kt = all_scr[KROW : KROW + H, :]
    vt = all_scr[VROW : VROW + H, :]
    logits = all_scr[RROW : RROW + E, :]
    kvt = jnp.concatenate([kt, vt], axis=0)
    kv = kvt.T.astype(BF16)
    kv_ref[...] = kv
    kvt_ref[...] = kvt.astype(BF16)
    k_scr[pl.ds(here, TB), :] = kv[:, :H]
    vt_scr[:, pl.ds(here, TB)] = vt.astype(BF16)
    routes = jnp.concatenate(sorted_rows(route_ref[k : k + 1, :] for k in range(TOPK)), axis=0)
    sorted_ref[...] = routes
    experts = lax.broadcasted_iota(jnp.int32, (E, TB), 0)
    chosen = []
    counts = count_scr[...]
    for k in range(TOPK):
        named = slot_of(routes, k, E) == experts
        chosen.append(jnp.sum(jnp.where(named, logits, 0.0), axis=0, keepdims=True))
        counts = counts + named.astype(F32)
    count_scr[...] = counts
    chosen = jnp.concatenate(chosen, axis=0)
    raised = jnp.exp(chosen - jnp.max(chosen, axis=0, keepdims=True))
    gate_ref[...] = raised / jnp.sum(raised, axis=0, keepdims=True)
    low_scr[...] = all_scr[0:QW, :].astype(BF16)
    for k in range(TOPK):
        q_ref[k * H : (k + 1) * H, :] = pick_heads(routes, low_scr, k) * jnp.asarray(H ** (-0.5), BF16)

    def attend(lanes, block, blocks):
        rows = blocks * QB
        first_key = pl.multiple_of((block - (blocks - 1)) * QB, QB)
        mask = key_mask(first_key, block * QB, rows, start_ref[:, lanes])
        keys = k_scr[pl.ds(first_key, rows), :]
        values = vt_scr[:, pl.ds(first_key, rows)]
        pairs = [nn(keys, pair_of(q_ref, 0, lanes))]
        for k in range(0, TOPK, 2):
            if k + 2 < TOPK:
                pairs.append(nn(keys, pair_of(q_ref, k + 2, lanes)))
            scores = jnp.where(mask, pairs[k // 2], NEG_LARGE)
            top = jnp.max(scores, axis=0, keepdims=True)
            raised = jnp.exp(scores - top)
            total = jnp.sum(raised, axis=0, keepdims=True)
            out = nn(values, (raised * (1.0 / total)).astype(BF16))
            lse = top + jnp.log(total)
            for side in range(2):
                one = slice(side * QB, (side + 1) * QB)
                att_ref[(k + side) * H : (k + side + 1) * H, lanes] = out[:, one]
                lse_ref[k + side : k + side + 1, lanes] = lse[:, one]

    by_span(attend, lax.div(step, NB), place, segment_smem)

    @pl.when(step == steps - 1)
    def _():
        held = jnp.sum(count_scr[...], axis=1, keepdims=True)
        lane = lax.broadcasted_iota(jnp.int32, (E, 128), 1)
        row = lax.broadcasted_iota(jnp.int32, (E, 128), 0)
        count_ref[...] = jnp.sum(jnp.where(lane == row, held, 0.0), axis=0, keepdims=True)


def picks(rows, stride, first):
    at = lax.broadcasted_iota(jnp.int32, (rows, D), 1)
    row = lax.broadcasted_iota(jnp.int32, (rows, D), 0)
    return (at == row * stride + first).astype(F32)


def exact(product, a, b):
    return lax.dot_general(
        a, b, (product, ((), ())), precision=lax.Precision.HIGHEST, preferred_element_type=F32
    )


def gelu_parts(v):
    size = jnp.abs(v) * 0.7071067811865476
    bell = jnp.exp(-(size * size))
    t = 1.0 / (1.0 + 0.3275911 * size)
    series = t * (
        0.254829592
        + t * (-0.284496736 + t * (1.421413741 + t * (-1.453152027 + t * 1.061405429)))
    )
    tail = 0.5 * series * bell
    cdf = jnp.where(v < 0.0, tail, 1.0 - tail)
    return cdf, bell * 0.3989422804014327


def middle_kernel(
    x_ref, dy_ref, gain_ref, wo_ref, w1_ref, w2_ref, route_ref, gate_ref, att_ref,
    out_ref, dres_ref, datt_ref, delta_ref, dlogit_ref, flat_ref, extra_ref, dgain_ref,
    slot_scr, head_scr, mix_scr, dwo_ref, dw1_ref, dw2t_ref, rows_scr, low_scr, row_sem,
):
    step = pl.program_id(0)

    @pl.when(step == 0)
    def _():
        dwo_ref[...] = jnp.zeros_like(dwo_ref)
        dw1_ref[...] = jnp.zeros_like(dw1_ref)
        dw2t_ref[...] = jnp.zeros_like(dw2t_ref)
        dgain_ref[...] = jnp.zeros_like(dgain_ref)

    routes = route_ref[...]
    tokens = routes.shape[1]
    gates = gate_ref[...]
    for k in range(TOPK):
        rows = slice(k * H, (k + 1) * H)
        slot_scr[rows, :] = (gates[k : k + 1, :] * att_ref[rows, :]).astype(BF16)
    place_heads(routes, slot_scr, mix_scr)
    x = x_ref[...].astype(F32)
    dy = dy_ref[...]
    mixed = mix_scr[...]
    residual = x + tn(mixed, wo_ref[...])
    scale = rms_scale(residual)
    gain = gain_ref[...]
    second = (residual * scale * gain).astype(BF16)
    second_t = second.T
    dy_t = dy.T
    out = residual
    dsecond = jnp.zeros((tokens, D), F32)
    for c in range(0, FF, FC):
        up = w1_ref[:, c : c + FC]
        down = w2_ref[c : c + FC, :]
        pre = nn(second, up)
        cdf, density = gelu_parts(pre)
        hidden = (pre * cdf).astype(BF16)
        dpre = (nt(dy, down) * (cdf + pre * density)).astype(BF16)
        out = out + nn(hidden, down)
        dsecond = dsecond + nt(dpre, up)
        dw2t_ref[:, c : c + FC] += nn(dy_t, hidden)
        dw1_ref[:, c : c + FC] += nn(second_t, dpre)
    out_ref[...] = out.astype(BF16)
    dgain_ref[...] += jnp.sum(dsecond * residual * scale, axis=0, keepdims=True)
    weighted = gain * dsecond
    dres = (
        dy.astype(F32)
        + scale * weighted
        - residual * (scale * scale * scale) * jnp.mean(weighted * residual, axis=-1, keepdims=True)
    )
    dres_ref[...] = dres
    branch = dres.astype(BF16)
    dwo_ref[...] += nn(mixed, branch)
    head_scr[...] = nt(wo_ref[...], branch).astype(BF16)
    dgates = []
    for k in range(TOPK):
        rows = slice(k * H, (k + 1) * H)
        dslot = pick_heads(routes, head_scr, k).astype(F32)
        attended = att_ref[rows, :]
        dgates.append(jnp.sum(dslot * attended, axis=0, keepdims=True))
        datt = (gates[k : k + 1, :] * dslot).astype(BF16)
        datt_ref[rows, :] = datt
        delta_ref[k : k + 1, :] = jnp.sum(datt.astype(F32) * attended, axis=0, keepdims=True)
    dgate = jnp.concatenate(dgates, axis=0)
    dchosen = gates * (dgate - jnp.sum(gates * dgate, axis=0, keepdims=True))
    experts = lax.broadcasted_iota(jnp.int32, (E, tokens), 0)
    dlogits = jnp.zeros((E, tokens), F32)
    for k in range(TOPK):
        dlogits = jnp.where(
            slot_of(routes, k, E) == experts,
            jnp.broadcast_to(dchosen[k : k + 1, :], (E, tokens)),
            dlogits,
        )
    dlogit_ref[...] = dlogits

    @pl.when(step == pl.num_programs(0) - 1)
    def _():
        for c in range(D // 128):
            lanes = slice(c * 128, (c + 1) * 128)
            rows_scr[pl.ds(c, QW, stride=4), :] = dwo_ref[:, lanes]
            rows_scr[pl.ds(W2_ROW - WO_ROW + c, FF, stride=4), :] = dw2t_ref[lanes, :].T
        for c in range(FF // 128):
            rows_scr[pl.ds(W1_ROW - WO_ROW + c, D, stride=16), :] = dw1_ref[:, c * 128 : (c + 1) * 128]
        extra_ref[...] = rows_scr[0:8, :]
        low_scr[...] = rows_scr[8:, :].astype(BF16)
        copy = pltpu.make_async_copy(
            low_scr, flat_ref.at[pl.ds(WO_ROW + 8, low_scr.shape[0]), :], row_sem.at[0]
        )
        copy.start()
        copy.wait()


def head_backward_kernel(
    segment_smem, x_ref, gain_ref, wall_ref, route_ref, start_ref, q_ref, datt_ref,
    lse_ref, delta_ref, kv_ref, kvt_ref, dlogit_ref, dres_ref, dgain_two_ref, extra_ref, flat_in,
    dx_ref, flat_ref,
    dk_scr, dv_scr, dq_scr, dall_scr, prob_scr, dscore_scr, dwall_ref, dgain_ref, rows_scr, low_scr, row_sem,
):
    step = pl.program_id(0)
    place = NB - 1 - lax.rem(step, NB)
    here = pl.multiple_of(place * TB, TB)

    @pl.when(step == 0)
    def _():
        dwall_ref[...] = jnp.zeros_like(dwall_ref)
        dgain_ref[...] = jnp.zeros_like(dgain_ref)

    @pl.when(lax.rem(step, NB) == 0)
    def _():
        dk_scr[...] = jnp.zeros_like(dk_scr)
        dv_scr[...] = jnp.zeros_like(dv_scr)

    def attend(lanes, block, blocks):
        rows = blocks * QB
        first_key = pl.multiple_of((block - (blocks - 1)) * QB, QB)
        mask = key_mask(first_key, block * QB, rows, start_ref[:, lanes])
        keys = kv_ref[pl.ds(first_key, rows), :H]
        values = kv_ref[pl.ds(first_key, rows), H:]
        keys_t = kvt_ref[:H, pl.ds(first_key, rows)]
        queries = [pair_of(q_ref, k, lanes) for k in range(0, TOPK, 2)]
        datts = [pair_of(datt_ref, k, lanes) for k in range(0, TOPK, 2)]
        scores = [nn(keys, queries[0])]
        dprobs = [nn(values, datts[0])]
        for i in range(TOPK // 2):
            if i + 1 < TOPK // 2:
                scores.append(nn(keys, queries[i + 1]))
                dprobs.append(nn(values, datts[i + 1]))
            k = 2 * i
            wide = slice(i * 2 * QB, (i + 1) * 2 * QB)
            probs = jnp.exp(jnp.where(mask, scores[i], NEG_LARGE) - row_pair(lse_ref, k, lanes))
            dscore = (probs * (dprobs[i] - row_pair(delta_ref, k, lanes))).astype(BF16)
            prob_scr[0:rows, wide] = probs.astype(BF16)
            dscore_scr[0:rows, wide] = dscore
            dq = (nn(keys_t, dscore) * (H ** (-0.5))).astype(BF16)
            dq_scr[k * H : (k + 1) * H, lanes] = dq[:, :QB]
            dq_scr[(k + 1) * H : (k + 2) * H, lanes] = dq[:, QB:]
        dv_scr[pl.ds(first_key, rows), :] += nt(prob_scr[0:rows, :], jnp.concatenate(datts, axis=1))
        dk_scr[pl.ds(first_key, rows), :] += nt(dscore_scr[0:rows, :], jnp.concatenate(queries, axis=1))

    by_span(attend, lax.div(step, NB), place, segment_smem)
    place_heads(route_ref[...], dq_scr, dall_scr)
    dkv = jnp.concatenate([dk_scr[pl.ds(here, TB), :], dv_scr[pl.ds(here, TB), :]], axis=1)
    dall_scr[KROW : KROW + 2 * H, :] = dkv.T.astype(BF16)
    dall_scr[RROW : RROW + 32, :] = jnp.concatenate(
        [dlogit_ref[...], jnp.zeros((32 - E, TB), F32)], axis=0
    ).astype(BF16)
    x = x_ref[...].astype(F32)
    scale = rms_scale(x)
    gain = gain_ref[...]
    normed = (x * scale * gain).astype(BF16)
    dall = dall_scr[...]
    dwall_ref[...] += nn(dall, normed)
    dnormed = tn(dall, wall_ref[...])
    dgain_ref[...] += jnp.sum(dnormed * x * scale, axis=0, keepdims=True)
    weighted = gain * dnormed
    dx_ref[...] = (
        dres_ref[...]
        + scale * weighted
        - x * (scale * scale * scale) * jnp.mean(weighted * x, axis=-1, keepdims=True)
    )

    @pl.when(step == pl.num_programs(0) - 1)
    def _():
        for c in range(D // 128):
            lanes = slice(c * 128, (c + 1) * 128)
            rows_scr[c : c + 1, :] = dgain_ref[:, lanes]
            rows_scr[4 + c : 5 + c, :] = dgain_two_ref[:, lanes]
        router_t = dwall_ref[RROW : RROW + E, :]
        across = jnp.concatenate(
            [exact(((1,), (1,)), router_t, picks(32, 16, b)) for b in range(16)], axis=0
        ).T
        for j in range(3):
            rows_scr[pl.ds(WR_ROW + j, 32, stride=3), :] = across[:, j * 128 : (j + 1) * 128]
        for first, row in ((KROW, WK_ROW), (VROW, WV_ROW)):
            part = dwall_ref[first : first + H, :]
            rows_scr[row : row + 256, :] = jnp.concatenate(
                [exact(((1,), (1,)), picks(256, 2, b), part) for b in range(2)], axis=1
            )
        for c in range(QW // 128):
            rows_scr[pl.ds(WQ_ROW + c, D, stride=12), :] = dwall_ref[c * 128 : (c + 1) * 128, :].T
        rows_scr[WO_ROW : WO_ROW + 8, :] = extra_ref[...]
        low_scr[...] = rows_scr[...].astype(BF16)
        copy = pltpu.make_async_copy(low_scr, flat_ref.at[pl.ds(0, WO_ROW + 8), :], row_sem.at[0])
        copy.start()
        copy.wait()


def whole(shape):
    return pl.BlockSpec(shape, lambda *_: (0,) * len(shape), pipeline_mode=pl.Buffered(1))


def kept(shape):
    return pl.BlockSpec(shape, lambda *_: (0,) * len(shape))


SMEM = pl.BlockSpec(memory_space=pltpu.SMEM)


def struct(shape, kind=F32):
    return jax.ShapeDtypeStruct(shape, kind)


def params_for(mib):
    return pltpu.CompilerParams(vmem_limit_bytes=mib * MIB)


def head_forward(tokens, routes_t, segments, wall, gain):
    count = tokens.shape[0]
    steps = count // TB
    across = lambda rows: pl.BlockSpec((rows, TB), lambda b: (0, b))
    down = lambda columns: pl.BlockSpec((TB, columns), lambda b: (b, 0))
    return pl.pallas_call(
        functools.partial(head_forward_kernel, steps),
        grid=(steps,),
        in_specs=[SMEM, down(D), across(TOPK), whole(segments.shape), whole((ALLW, D)), whole((1, D))],
        out_specs=[
            across(TOPK * H), across(TOPK * H), across(TOPK), across(TOPK), down(2 * H), across(2 * H),
            across(1), across(TOPK), whole((1, 128)),
        ],
        scratch_shapes=[
            pltpu.VMEM((ALLW, TB), F32),
            pltpu.VMEM((QW, TB), BF16),
            pltpu.VMEM((LEN, H), BF16),
            pltpu.VMEM((H, LEN), BF16),
            pltpu.VMEM((E, TB), F32),
        ],
        out_shape=[
            struct((TOPK * H, count), BF16),
            struct((TOPK * H, count)),
            struct((TOPK, count)),
            struct((TOPK, count)),
            struct((count, 2 * H), BF16),
            struct((2 * H, count), BF16),
            struct((1, count), jnp.int32),
            struct((TOPK, count), jnp.int32),
            struct((1, 128)),
        ],
        compiler_params=params_for(56),
        name="head_forward",
        cost_estimate=pl.CostEstimate(flops=10_000_000_000, bytes_accessed=16_000_000, transcendentals=0),
    )(segments, tokens, routes_t, segments, wall, gain)


def middle(flat_rows, tokens, grad_out, gain, wo, w1, w2, routes_t, gates, attended):
    count = tokens.shape[0]
    steps = count // MB
    across = lambda rows: pl.BlockSpec((rows, MB), lambda b: (0, b))
    down = lambda columns: pl.BlockSpec((MB, columns), lambda b: (b, 0))
    return pl.pallas_call(
        middle_kernel,
        grid=(steps,),
        in_specs=[
            down(D), down(D), whole((1, D)), whole((QW, D)), whole((D, FF)), whole((FF, D)),
            across(TOPK), across(TOPK), across(TOPK * H),
        ],
        out_specs=[
            down(D), down(D), across(TOPK * H), across(TOPK), across(E),
            pl.BlockSpec(memory_space=pl.ANY), whole((8, 128)), whole((1, D)),
        ],
        out_shape=[
            struct((count, D), BF16),
            struct((count, D)),
            struct((TOPK * H, count), BF16),
            struct((TOPK, count)),
            struct((E, count)),
            struct((flat_rows, 128), BF16),
            struct((8, 128)),
            struct((1, D)),
        ],
        scratch_shapes=[
            pltpu.VMEM((TOPK * H, MB), BF16),
            pltpu.VMEM((QW, MB), BF16),
            pltpu.VMEM((QW, MB), BF16),
            pltpu.VMEM((QW, D), F32),
            pltpu.VMEM((D, FF), F32),
            pltpu.VMEM((D, FF), F32),
            pltpu.VMEM((flat_rows - WO_ROW, 128), F32),
            pltpu.VMEM((flat_rows - WO_ROW - 8, 128), BF16),
            pltpu.SemaphoreType.DMA((1,)),
        ],
        compiler_params=params_for(60),
        name="middle",
    )(tokens, grad_out, gain, wo, w1, w2, routes_t, gates, attended)


def head_backward(
    segments, tokens, gain, wall, routes_t, start, queries, datt, lse, delta, kv, kvt, dlogits, dres,
    dgain_two, extra, flat,
):
    count = tokens.shape[0]
    steps = count // TB

    def place(b):
        return (b // NB) * NB + NB - 1 - b % NB

    across = lambda rows: pl.BlockSpec((rows, TB), lambda b: (0, place(b)))
    down = lambda columns: pl.BlockSpec((TB, columns), lambda b: (place(b), 0))
    return pl.pallas_call(
        head_backward_kernel,
        grid=(steps,),
        in_specs=[
            SMEM, down(D), whole((1, D)), whole((ALLW, D)), across(TOPK), across(1),
            across(TOPK * H), across(TOPK * H), across(TOPK), across(TOPK),
            pl.BlockSpec((LEN, 2 * H), lambda b: (b // NB, 0)),
            pl.BlockSpec((2 * H, LEN), lambda b: (0, b // NB)),
            across(E), down(D), whole((1, D)), whole((8, 128)), pl.BlockSpec(memory_space=pl.ANY),
        ],
        out_specs=[down(D), pl.BlockSpec(memory_space=pl.ANY)],
        scratch_shapes=[
            pltpu.VMEM((LEN, H), F32),
            pltpu.VMEM((LEN, H), F32),
            pltpu.VMEM((TOPK * H, TB), BF16),
            pltpu.VMEM((ALLW, TB), BF16),
            pltpu.VMEM((MOST * QB, TOPK * QB), BF16),
            pltpu.VMEM((MOST * QB, TOPK * QB), BF16),
            pltpu.VMEM((ALLW, D), F32),
            pltpu.VMEM((1, D), F32),
            pltpu.VMEM((WO_ROW + 8, 128), F32),
            pltpu.VMEM((WO_ROW + 8, 128), BF16),
            pltpu.SemaphoreType.DMA((1,)),
        ],
        out_shape=[struct((count, D)), struct(flat.shape, BF16)],
        input_output_aliases={16: 1},
        compiler_params=params_for(56),
        name="head_backward",
        cost_estimate=pl.CostEstimate(flops=30_000_000_000, bytes_accessed=24_000_000, transcendentals=0),
    )(
        segments, tokens, gain, wall, routes_t, start, queries, datt, lse, delta, kv, kvt, dlogits, dres,
        dgain_two, extra, flat,
    )


class Mesh3:
    def __init__(self, shards, over):
        shard = lax.axis_index("dp")
        other = lax.axis_index("fsdp")
        self.over = over
        self.many = shards * over
        self.sizes = {"x": 2, "y": shards // 2, "z": over // 2}
        self.here = {"x": lax.rem(other, 2), "y": lax.div(shard, 2), "z": lax.div(other, 2)}
        self.core = lax.rem(shard, 2)
        self.me = shard * over + other
        self.partner = (shard + 1 - 2 * self.core, other)

    def moved(self, steps):
        return {
            axis: lax.rem(self.here[axis] + steps.get(axis, 0), self.sizes[axis]) for axis in "xyz"
        }

    def device(self, core, steps):
        at = self.moved(steps)
        return (at["y"] * 2 + core, at["z"] * 2 + at["x"])

    def number(self, core, steps):
        shard, other = self.device(core, steps)
        return shard * self.over + other

    def nth(self, number):
        return (lax.div(number, self.over), lax.rem(number, self.over))

    def greet_near(self):
        devices = [
            self.device(self.core, {axis: step})
            for axis in "xyz"
            for step in range(1, self.sizes[axis])
        ] + [self.partner]
        barrier = pltpu.get_barrier_semaphore()
        for device in devices:
            pl.semaphore_signal(barrier, inc=1, device_id=device, device_id_type=MESH)
        pl.semaphore_wait(barrier, len(devices))

    def greet_all(self):
        barrier = pltpu.get_barrier_semaphore()

        def hello(j, carry):
            device = self.nth(lax.rem(self.me + j, self.many))
            pl.semaphore_signal(barrier, inc=1, device_id=device, device_id_type=MESH)
            return carry

        lax.fori_loop(1, self.many, hello, 0)
        pl.semaphore_wait(barrier, self.many - 1)


def along_z(step):
    return {1: (0, 3), 2: (1, 5), 3: (3, 8)}.get(step, (step, 2 * step + 2))


class Kind:
    def __init__(self, mesh, core, axes):
        self.mesh = mesh
        self.core = core
        self.axes = axes
        ranges = [range(mesh.sizes[axis]) for axis in axes]
        self.offsets = list(itertools.product(*ranges))
        self.index = {one: number for number, one in enumerate(self.offsets)}

    def owner(self, offsets):
        return self.mesh.number(self.core, dict(zip(self.axes, offsets)))

    def last(self, offsets):
        return max([i for i in range(3) if offsets[i]], default=-1)

    def turn(self, offsets):
        total = 0
        for axis, step in zip(self.axes, offsets):
            if step:
                total += along_z(step)[1] if axis == "z" else 2
        return total

    def hops(self, offsets):
        for i in range(self.last(offsets) + 1, 3):
            for step in range(1, self.mesh.sizes[self.axes[i]]):
                delay = along_z(step)[0] if self.axes[i] == "z" else 0
                yield i, step, self.turn(offsets) + delay

    def ahead(self, i, step):
        return self.mesh.device(self.core, {self.axes[i]: step})


AXES = ("zxy", "zyx")


def pieces_of(window):
    if window < 512:
        return [(0, window)]
    first = (window // 16 + 1) // 2 * 16
    return [(0, first), (first, window - first)]


def gather_events(mesh, own_ref, land, send_sem, recv_sem, laid):
    events = []
    pieces = pieces_of(own_ref.shape[0])
    kinds = [Kind(mesh, core, AXES[core]) for core in range(2)]
    end = 2 * max(kind.turn(one) for kind in kinds for one in kind.offsets) + 4

    def copy(owner, device, slot, p):
        rows = pl.ds(*pieces[p])
        return pltpu.make_async_remote_copy(
            src_ref=land.at[owner, rows],
            dst_ref=land.at[owner, rows],
            send_sem=send_sem.at[slot, p],
            recv_sem=recv_sem.at[owner, p],
            device_id=device,
            device_id_type=MESH,
        )

    def event(turn, condition, action):
        events.append((turn, lambda: pl.when(condition)(action)))

    for kind in kinds:
        ours = mesh.core == kind.core
        theirs = mesh.core != kind.core
        slots = itertools.count()
        for offsets in kind.offsets:
            owner = kind.owner(offsets)
            slot = next(slots)
            hops = [(i, step, turn, next(slots)) for i, step, turn in kind.hops(offsets)]
            for p in range(len(pieces)):

                def come(owner=owner, offsets=offsets, slot=slot, p=p, kind=kind, hops=hops):
                    if any(offsets):
                        copy(owner, mesh.partner, slot, p).wait_recv()
                    elif p == 0:
                        land[owner] = own_ref[...]
                    for i, step, turn, number in hops:
                        if turn == kind.turn(offsets):
                            copy(owner, kind.ahead(i, step), number, p).start()
                    copy(owner, mesh.partner, slot, p).start()
                    laid(owner, p)

                def across(owner=owner, slot=slot, p=p):
                    copy(owner, mesh.partner, slot, p).wait_recv()
                    laid(owner, p)

                def done(owner=owner, slot=slot, p=p, hops=hops):
                    copy(owner, mesh.partner, slot, p).wait_send()
                    for _, _, _, number in hops:
                        copy(owner, mesh.partner, number, p).wait_send()

                event(2 * kind.turn(offsets) + p, ours, come)
                event(end + kind.turn(offsets) / 100, theirs, across)
                event(end + 1, ours, done)
                for i, step, turn, number in hops:
                    if turn == kind.turn(offsets):
                        continue

                    def send(owner=owner, device=kind.ahead(i, step), number=number, p=p):
                        copy(owner, device, number, p).start()

                    event(2 * turn + p, ours, send)
    return sorted(events, key=lambda one: one[0])


def reduce_events(mesh, source, fetch, part, outgo, income, send_sem, recv_sem, finish):
    events = []
    half = mesh.many // 2
    pieces = pieces_of(outgo.shape[1])
    kinds = [Kind(mesh, core, AXES[core]) for core in range(2)]
    end = 2 * max(kind.turn(one) for kind in kinds for one in kind.offsets) + 4

    def copy(slot, device, p, begin=None):
        rows = pl.ds(*pieces[p])
        return pltpu.make_async_remote_copy(
            src_ref=outgo.at[slot, rows] if begin is None else begin,
            dst_ref=income.at[slot, rows],
            send_sem=send_sem.at[slot, p],
            recv_sem=recv_sem.at[slot, p],
            device_id=device,
            device_id_type=MESH,
        )

    def event(turn, condition, action):
        events.append((turn, lambda: pl.when(condition)(action)))

    def taken(slot, p):
        copy(slot, mesh.partner, p).wait_recv()
        return income[slot, pl.ds(*pieces[p])].astype(F32)

    for kind in kinds:
        ours = mesh.core == kind.core
        theirs = mesh.core != kind.core
        slots = {}
        for offsets in kind.offsets:
            if any(offsets):
                slots[offsets] = half + len(slots)
        for offsets in kind.offsets:
            owner = kind.owner(offsets)
            number = kind.index[offsets]
            axis = kind.last(offsets)
            turn = end - 2 * kind.turn(offsets)
            for p, (first, rows) in enumerate(pieces):

                def hand(owner=owner, number=number, p=p, first=first, rows=rows):
                    copy(number, mesh.partner, p, source(owner, first, rows)).start()

                def onward(
                    owner=owner, offsets=offsets, number=number, axis=axis, kind=kind, slots=slots, p=p
                ):
                    mine = pl.ds(*pieces[p])
                    fetch(owner, number, p).wait()
                    total = part[number, mine].astype(F32) + taken(number, p)
                    for i, step, _ in kind.hops(offsets):
                        longer = tuple(step if j == i else o for j, o in enumerate(offsets))
                        total = total + taken(slots[longer], p)
                    if axis < 0:
                        finish(total, p)
                    else:
                        outgo[slots[offsets], mine] = total.astype(BF16)
                        copy(slots[offsets], kind.ahead(axis, offsets[axis]), p).start()

                def handed(number=number, p=p):
                    copy(number, mesh.partner, p).wait_send()

                event(-1 - kind.turn(offsets) / 100, theirs, hand)
                event(-2, ours, lambda owner=owner, number=number, p=p: fetch(owner, number, p).start())
                event(turn + p, ours, onward)
                event(end + 2, theirs, handed)
                if axis >= 0:

                    def passed(slot=slots[offsets], p=p):
                        copy(slot, mesh.partner, p).wait_send()

                    event(end + 2, ours, passed)
    return sorted(events, key=lambda one: one[0])


def window_rows(shard_size, many):
    units = [(shard_size * d) // UNIT for d in range(many + 1)]
    return 16 * (max(b - a for a, b in zip(units, units[1:])) + 1)


def first_row(shard_size, number):
    if isinstance(number, int):
        return number * shard_size // UNIT * 16
    return pl.multiple_of(lax.div(number * shard_size, UNIT) * 16, 16)


def inner_units(shard_size, many):
    units = [(shard_size * d) // UNIT for d in range(many + 1)]
    return min(b - a for a, b in zip(units, units[1:]))


def lay_inner(shard_size, many, land, flat, owner, first, rows):
    begin = max(first, 16)
    count = min(first + rows, 16 * inner_units(shard_size, many)) - begin
    row = pl.multiple_of(first_row(shard_size, owner) + begin, 16)
    flat[pl.ds(row, count), :] = land[owner, pl.ds(begin, count), :].astype(F32)


def lay_edges(shard_size, many, land, flat):
    inner = 16 * inner_units(shard_size, many)
    flat[0:16, :] = jnp.zeros((16, 128), F32)

    def lay(number, carry):
        row = first_row(shard_size, number)
        after = first_row(shard_size, number + 1)
        flat[pl.ds(row, 16), :] += land[number, 0:16, :].astype(F32)
        tail = land[number, pl.ds(inner, 16), :].astype(F32)
        flat[pl.ds(pl.multiple_of(row + inner, 16), 16), :] = tail
        last = pl.multiple_of(after - row, 16)
        flat[pl.ds(after, 16), :] = land[number, pl.ds(last, 16), :].astype(F32)
        return carry

    lax.fori_loop(0, many, lay, 0)


def early_matrices(flat, wall_ref, gain_one_ref, gain_two_ref):
    for c in range(D // 128):
        lanes = slice(c * 128, (c + 1) * 128)
        gain_one_ref[:, lanes] = flat[c : c + 1, :]
        gain_two_ref[:, lanes] = flat[4 + c : 5 + c, :]
    for c in range(QW // 128):
        wall_ref[c * 128 : (c + 1) * 128, :] = flat[pl.ds(WQ_ROW + c, D, stride=12), :].T.astype(BF16)
    for first, row in ((KROW, WK_ROW), (VROW, WV_ROW)):
        pair = flat[row : row + 256, :].T.astype(BF16)
        wall_ref[first : first + H, :] = (
            nn(pair[:H], picks(256, 2, 0).astype(BF16)) + nn(pair[H:], picks(256, 2, 1).astype(BF16))
        ).astype(BF16)
    across = jnp.concatenate(
        [flat[pl.ds(WR_ROW + j, 32, stride=3), :] for j in range(3)], axis=1
    ).T.astype(BF16)
    router_t = jnp.zeros((E, D), F32)
    for part in range(16):
        router_t = router_t + nn(across[part * E : (part + 1) * E, :], picks(32, 16, part).astype(BF16))
    wall_ref[RROW:ALLW, :] = jnp.concatenate(
        [router_t, jnp.zeros((ALLW - RROW - E, D), F32)], axis=0
    ).astype(BF16)


def gather_kernel(
    mesh, shard_size, own_ref,
    wall_out, gain_one_ref, gain_two_ref, wo_out, w1_out, w2_out,
    land, flat, wall_ref, wo_ref, w1_ref, w2_ref, send_sem, recv_sem, out_sem,
):
    mesh = mesh()
    many = mesh.many
    pieces = pieces_of(own_ref.shape[0])
    mesh.greet_near()

    def laid(owner, p):
        lay_inner(shard_size, many, land, flat, owner, *pieces[p])

    for _, action in gather_events(mesh, own_ref, land, send_sem, recv_sem, laid):
        action()
    lay_edges(shard_size, many, land, flat)
    copies = []

    def leave(matrix, out):
        copy = pltpu.make_async_copy(matrix, out, out_sem.at[len(copies)])
        copy.start()
        copies.append(copy)

    for c in range(D // 128):
        wo_ref[:, c * 128 : (c + 1) * 128] = flat[pl.ds(WO_ROW + c, QW, stride=4), :].astype(BF16)
    leave(wo_ref, wo_out)
    for c in range(D // 128):
        w2_ref[:, c * 128 : (c + 1) * 128] = flat[pl.ds(W2_ROW + c, FF, stride=4), :].astype(BF16)
    leave(w2_ref, w2_out)
    for c in range(FF // 128):
        w1_ref[:, c * 128 : (c + 1) * 128] = flat[pl.ds(W1_ROW + c, D, stride=16), :].astype(BF16)
    leave(w1_ref, w1_out)
    early_matrices(flat, wall_ref, gain_one_ref, gain_two_ref)
    leave(wall_ref, wall_out)
    for copy in copies:
        copy.wait()


def gather_weights(shards, over, shard_size, own):
    window = own.shape[0]
    many = shards * over
    rows = (shard_size * (many - 1)) // UNIT * 16 + window
    vmem = pl.BlockSpec(memory_space=pltpu.VMEM)
    hbm = pl.BlockSpec(memory_space=pl.ANY)
    mesh = functools.partial(Mesh3, shards, over)
    pieces = len(pieces_of(window))
    return pl.pallas_call(
        functools.partial(gather_kernel, mesh, shard_size),
        in_specs=[vmem],
        out_specs=[hbm, vmem, vmem, hbm, hbm, hbm],
        out_shape=[
            struct((ALLW, D), BF16),
            struct((1, D)),
            struct((1, D)),
            struct((QW, D), BF16),
            struct((D, FF), BF16),
            struct((FF, D), BF16),
        ],
        scratch_shapes=[
            pltpu.VMEM((many, window, 128), BF16),
            pltpu.VMEM((rows, 128), F32),
            pltpu.VMEM((ALLW, D), BF16),
            pltpu.VMEM((QW, D), BF16),
            pltpu.VMEM((D, FF), BF16),
            pltpu.VMEM((FF, D), BF16),
            pltpu.SemaphoreType.DMA((many, pieces)),
            pltpu.SemaphoreType.DMA((many, pieces)),
            pltpu.SemaphoreType.DMA((4,)),
        ],
        compiler_params=pltpu.CompilerParams(
            collective_id=0, has_side_effects=True, vmem_limit_bytes=60 * MIB
        ),
        name="gather_weights",
    )(own)


def reduce_kernel(
    mesh, shard_size, flat_ref, count_ref,
    out_ref, total_ref, gain_ref,
    part, outgo, income, stats, gains, part_sem, send_sem, recv_sem, stat_send, stat_recv, gain_send, gain_recv,
):
    mesh = mesh()
    many = mesh.many
    window = out_ref.shape[0]
    pieces = pieces_of(window)

    def source(owner, first, rows):
        row = pl.multiple_of(first_row(shard_size, owner) + first, 16)
        return flat_ref.at[pl.ds(row, rows), :]

    def fetch(owner, number, p):
        return pltpu.make_async_copy(
            source(owner, *pieces[p]), part.at[number, pl.ds(*pieces[p])], part_sem.at[number, p]
        )

    def finish(total, p):
        out_ref[pl.ds(*pieces[p]), :] = total

    mesh.greet_all()
    for _, action in reduce_events(mesh, source, fetch, part, outgo, income, send_sem, recv_sem, finish):
        action()
    total = out_ref[...]
    begin = mesh.me * shard_size - lax.div(mesh.me * shard_size, UNIT) * UNIT
    at = (
        lax.broadcasted_iota(jnp.int32, (window, 128), 0) * 128
        + lax.broadcasted_iota(jnp.int32, (window, 128), 1)
    )
    inside = jnp.where((at >= begin) & (at < begin + shard_size), total, 0.0)
    squares = jnp.sum(jnp.sum(inside * inside, axis=0, keepdims=True), axis=1, keepdims=True)
    lane = lax.broadcasted_iota(jnp.int32, (1, 128), 1)
    stats[0] = jnp.where(lane == E, squares, count_ref[...])

    def told(j):
        return pltpu.make_async_remote_copy(
            src_ref=stats.at[0],
            dst_ref=stats.at[j],
            send_sem=stat_send.at[j],
            recv_sem=stat_recv.at[j],
            device_id=mesh.nth(lax.rem(mesh.me + j, many)),
            device_id_type=MESH,
        )

    def shown(j):
        return pltpu.make_async_remote_copy(
            src_ref=gains,
            dst_ref=gains,
            send_sem=gain_send.at[j],
            recv_sem=gain_recv.at[0],
            device_id=mesh.nth(lax.rem(mesh.me + j, many)),
            device_id_type=MESH,
        )

    def tell(j, carry):
        told(j).start()
        return carry

    def hear(j, carry):
        told(j).wait()
        return carry

    def show(j, carry):
        shown(j).start()
        return carry

    def showed(j, carry):
        shown(j).wait_send()
        return carry

    lax.fori_loop(1, many, tell, 0)

    @pl.when(mesh.me == 0)
    def _():
        gains[...] = total[0:8, :]
        lax.fori_loop(1, many, show, 0)
        lax.fori_loop(1, many, showed, 0)

    @pl.when(mesh.me != 0)
    def _():
        shown(1).wait_recv()

    lax.fori_loop(1, many, hear, 0)
    total_ref[...] = jnp.sum(stats[...], axis=0)
    gain_ref[...] = gains[...]


def reduce_grads(shards, over, shard_size, window, flat, counts):
    vmem = pl.BlockSpec(memory_space=pltpu.VMEM)
    many = shards * over
    mesh = functools.partial(Mesh3, shards, over)
    pieces = len(pieces_of(window))
    return pl.pallas_call(
        functools.partial(reduce_kernel, mesh, shard_size),
        in_specs=[pl.BlockSpec(memory_space=pl.ANY), vmem],
        out_specs=[vmem] * 3,
        out_shape=[struct((window, 128)), struct((1, 128)), struct((8, 128))],
        scratch_shapes=[
            pltpu.VMEM((many // 2, window, 128), BF16),
            pltpu.VMEM((many, window, 128), BF16),
            pltpu.VMEM((many, window, 128), BF16),
            pltpu.VMEM((many, 1, 128), F32),
            pltpu.VMEM((8, 128), F32),
            pltpu.SemaphoreType.DMA((many // 2, pieces)),
            pltpu.SemaphoreType.DMA((many, pieces)),
            pltpu.SemaphoreType.DMA((many, pieces)),
            pltpu.SemaphoreType.DMA((many,)),
            pltpu.SemaphoreType.DMA((many,)),
            pltpu.SemaphoreType.DMA((many,)),
            pltpu.SemaphoreType.DMA((1,)),
        ],
        compiler_params=pltpu.CompilerParams(
            collective_id=1, has_side_effects=True, vmem_limit_bytes=56 * MIB
        ),
        name="reduce_grads",
    )(flat, counts)


def local_step(flat_rows, tokens, grad_out, routes, segments, weights):
    wall, gain_one, gain_two, wo, w1, w2 = weights
    queries, attended, gates, lse, kv, kvt, start, routes_t, counts = head_forward(
        tokens, routes.T, segments, wall, gain_one
    )
    output, dres, datt, delta, dlogits, flat, extra, dgain_two = middle(
        flat_rows, tokens, grad_out, gain_two, wo, w1, w2, routes_t, gates, attended
    )
    input_grad, flat = head_backward(
        segments, tokens, gain_one, wall, routes_t, start, queries, datt, lse, delta, kv, kvt, dlogits, dres,
        dgain_two, extra, flat,
    )
    return output, input_grad, flat, counts


def per_device(
    shards, over, tokens, grad_out, routes, segments, params, first_moment, second_moment, ema_weights
):
    shard_size = params.shape[0]
    window = window_rows(shard_size, shards * over)
    flat_rows = (shard_size * (shards * over - 1)) // UNIT * 16 + window
    me = lax.axis_index("dp") * over + lax.axis_index("fsdp")
    begin = lax.rem(me * shard_size, UNIT)
    own = lax.dynamic_slice(
        jnp.pad(params.astype(BF16), (UNIT, window * 128 - shard_size)), (UNIT - begin,), (window * 128,)
    ).reshape(window, 128)
    wall, gain_one, gain_two, wo, w1, w2 = gather_weights(shards, over, shard_size, own)
    output, input_grad, flat, counts = local_step(
        flat_rows, tokens, grad_out, routes, segments, (wall, gain_one, gain_two, wo, w1, w2)
    )
    reduced, sums, gain_grads = reduce_grads(shards, over, shard_size, window, flat, counts)
    grad_shard = lax.dynamic_slice(reduced.reshape(-1), (begin,), (shard_size,))
    total_tokens = tokens.shape[0] * shards * over
    expert_load = sums[0, :E] * (E / (total_tokens * TOPK))
    grad_norm = jnp.sqrt(sums[0, E])
    clipped = grad_shard * (CLIP_LIMIT / jnp.maximum(grad_norm, CLIP_LIMIT))
    new_first = BETA_FIRST * first_moment + (1.0 - BETA_FIRST) * clipped
    new_second = BETA_SECOND * second_moment + (1.0 - BETA_SECOND) * clipped * clipped
    first_hat = new_first / (1.0 - BETA_FIRST**STEP)
    second_hat = new_second / (1.0 - BETA_SECOND**STEP)
    new_params = params * (1.0 - LEARN_RATE * DECAY_RATE) - LEARN_RATE * first_hat / (
        jnp.sqrt(second_hat) + ADAM_EPS
    )
    new_ema = EMA_KEEP * ema_weights + (1.0 - EMA_KEEP) * new_params
    return (
        output,
        input_grad,
        expert_load,
        grad_norm.reshape(1),
        new_params,
        new_first,
        new_second,
        new_ema,
        gain_grads.reshape(2, D),
    )


def solution(mesh):
    row = P(("dp", "fsdp"), None)
    flat = P(("dp", "fsdp"))
    return jax.shard_map(
        functools.partial(per_device, mesh.shape["dp"], mesh.shape["fsdp"]),
        mesh=mesh,
        in_specs=(row, row, row, row, flat, flat, flat, flat),
        out_specs=(row, row, P(), P(), flat, flat, flat, flat, P()),
        check_vma=False,
    )
```

```python
import functools
import itertools

import jax
import jax.numpy as jnp
from jax import lax
from jax.experimental import pallas as pl
from jax.experimental.pallas import tpu as pltpu
from jax.sharding import PartitionSpec as P

D = 512
E = 24
TOPK = 8
H = 64
FF = 2048
STEP = 10

NORM_EPS = 1e-06
CLIP_LIMIT = 1.0
BETA_FIRST = 0.9
BETA_SECOND = 0.95
LEARN_RATE = 0.1
DECAY_RATE = 0.1
ADAM_EPS = 1e-08
EMA_KEEP = 0.9
NEG_LARGE = -1e30

QW = E * H
KROW = QW
VROW = QW + H
RROW = QW + 2 * H
ALLW = 1696
LEN = 1024
TB = 256
NB = LEN // TB
QB = 128
MOST = 512 // QB + 1
SORT_STEPS = (
    (0, 1), (2, 3), (4, 5), (6, 7), (0, 2), (1, 3), (4, 6), (5, 7), (1, 2), (5, 6),
    (0, 4), (1, 5), (2, 6), (3, 7), (2, 4), (3, 5), (1, 2), (3, 4), (5, 6),
)
FC = 512
MB = 512
MIB = 1 << 20

WR_ROW = 8
WK_ROW = 104
WV_ROW = 360
WQ_ROW = 616
WO_ROW = 6760
W1_ROW = 12904
W2_ROW = 21096
ALL_ROWS = 29288
UNIT = 16 * 128
MESH = pl.DeviceIdType.MESH

F32 = jnp.float32
BF16 = jnp.bfloat16


def nn(a, b):
    return lax.dot_general(a, b, (((1,), (0,)), ((), ())), preferred_element_type=F32)


def nt(a, b):
    return lax.dot_general(a, b, (((1,), (1,)), ((), ())), preferred_element_type=F32)


def tn(a, b):
    return lax.dot_general(a, b, (((0,), (0,)), ((), ())), preferred_element_type=F32)


def rms_scale(values):
    return lax.rsqrt(jnp.mean(values * values, axis=-1, keepdims=True) + NORM_EPS)


def slot_of(routes, k, rows):
    return jnp.broadcast_to(routes[k : k + 1, :], (rows, routes.shape[1]))


def expert_rows(routes, k):
    return jnp.broadcast_to(routes.astype(jnp.int16)[k : k + 1, :], (16, routes.shape[1]))


def pick_heads(routes, source_ref, k):
    tokens = routes.shape[1]
    route = expert_rows(routes, k)
    taken = source_ref[k * H : (k + 1) * H, :].reshape(H // 16, 16, tokens)
    for e in range(k + 1, k + E - TOPK + 1):
        piece = source_ref[e * H : (e + 1) * H, :].reshape(H // 16, 16, tokens)
        taken = jnp.where((route == jnp.int16(e))[None], piece, taken)
    return taken.reshape(H, tokens)


def place_heads(routes, source_ref, target_ref):
    tokens = routes.shape[1]
    rows = [expert_rows(routes, k) for k in range(TOPK)]
    for e in range(E):
        total = jnp.zeros((H // 16, 16, tokens), BF16)
        for k in range(max(0, e - (E - TOPK)), min(TOPK - 1, e) + 1):
            piece = source_ref[k * H : (k + 1) * H, :].reshape(H // 16, 16, tokens)
            total = jnp.where((rows[k] == jnp.int16(e))[None], piece, total)
        target_ref[e * H : (e + 1) * H, :] = total.reshape(H, tokens)


def sorted_rows(rows):
    rows = list(rows)
    for one, two in SORT_STEPS:
        rows[one], rows[two] = jnp.minimum(rows[one], rows[two]), jnp.maximum(rows[one], rows[two])
    return rows


def key_mask(first_key, first_query, rows, start_row):
    keys = lax.broadcasted_iota(jnp.int32, (rows, QB), 0) + first_key
    queries = lax.broadcasted_iota(jnp.int32, (rows, QB), 1) + first_query
    mask = (keys <= queries) & (keys >= start_row)
    return jnp.concatenate([mask, mask], axis=1)


def pair_of(ref, k, lanes):
    return jnp.concatenate(
        [ref[k * H : (k + 1) * H, lanes], ref[(k + 1) * H : (k + 2) * H, lanes]], axis=1
    )


def row_pair(ref, k, lanes):
    return jnp.concatenate([ref[k : k + 1, lanes], ref[k + 1 : k + 2, lanes]], axis=1)


def by_span(attend, row, place, segment_ref):
    def one(j, carry):
        block = place * (TB // QB) + j
        first = block * QB
        span = jnp.int32(1)
        for back in range(MOST - 1):
            last = first - back * QB - 1
            same = segment_ref[row, jnp.maximum(last, 0)] == segment_ref[row, first]
            span = span + jnp.where((last >= 0) & same, 1, 0)
        for blocks in range(1, MOST + 1):

            @pl.when(span == blocks)
            def _(blocks=blocks):
                attend(pl.ds(pl.multiple_of(j * QB, QB), QB), block, blocks)

        return carry

    lax.fori_loop(0, TB // QB, one, 0)


def head_forward_kernel(
    steps, segment_smem, x_ref, route_ref, segment_ref, wall_ref, gain_ref,
    q_ref, att_ref, gate_ref, lse_ref, kv_ref, kvt_ref, start_ref, sorted_ref, count_ref,
    all_scr, low_scr, k_scr, vt_scr, count_scr,
):
    step = pl.program_id(0)
    place = lax.rem(step, NB)
    here = pl.multiple_of(place * TB, TB)

    @pl.when(step == 0)
    def _():
        count_scr[...] = jnp.zeros_like(count_scr)

    row = segment_ref[pl.ds(lax.div(step, NB), 1), :]
    segments = segment_ref[pl.ds(lax.div(step, NB), 1), pl.ds(here, TB)]
    start = jnp.zeros((1, TB), jnp.int32)
    for number in range(1, 4):
        below = jnp.sum((row < number).astype(jnp.int32), axis=1, keepdims=True)
        start = jnp.where(segments == number, below, start)
    start_ref[...] = start
    x = x_ref[...].astype(F32)
    normed = (x * rms_scale(x) * gain_ref[...]).astype(BF16)
    all_scr[...] = nt(wall_ref[...], normed)
    kt = all_scr[KROW : KROW + H, :]
    vt = all_scr[VROW : VROW + H, :]
    logits = all_scr[RROW : RROW + E, :]
    kvt = jnp.concatenate([kt, vt], axis=0)
    kv = kvt.T.astype(BF16)
    kv_ref[...] = kv
    kvt_ref[...] = kvt.astype(BF16)
    k_scr[pl.ds(here, TB), :] = kv[:, :H]
    vt_scr[:, pl.ds(here, TB)] = vt.astype(BF16)
    routes = jnp.concatenate(sorted_rows(route_ref[k : k + 1, :] for k in range(TOPK)), axis=0)
    sorted_ref[...] = routes
    experts = lax.broadcasted_iota(jnp.int32, (E, TB), 0)
    chosen = []
    counts = count_scr[...]
    for k in range(TOPK):
        named = slot_of(routes, k, E) == experts
        chosen.append(jnp.sum(jnp.where(named, logits, 0.0), axis=0, keepdims=True))
        counts = counts + named.astype(F32)
    count_scr[...] = counts
    chosen = jnp.concatenate(chosen, axis=0)
    raised = jnp.exp(chosen - jnp.max(chosen, axis=0, keepdims=True))
    gate_ref[...] = raised / jnp.sum(raised, axis=0, keepdims=True)
    low_scr[...] = all_scr[0:QW, :].astype(BF16)
    for k in range(TOPK):
        q_ref[k * H : (k + 1) * H, :] = pick_heads(routes, low_scr, k) * jnp.asarray(H ** (-0.5), BF16)

    def attend(lanes, block, blocks):
        rows = blocks * QB
        first_key = pl.multiple_of((block - (blocks - 1)) * QB, QB)
        mask = key_mask(first_key, block * QB, rows, start_ref[:, lanes])
        keys = k_scr[pl.ds(first_key, rows), :]
        values = vt_scr[:, pl.ds(first_key, rows)]
        pairs = [nn(keys, pair_of(q_ref, 0, lanes))]
        for k in range(0, TOPK, 2):
            if k + 2 < TOPK:
                pairs.append(nn(keys, pair_of(q_ref, k + 2, lanes)))
            scores = jnp.where(mask, pairs[k // 2], NEG_LARGE)
            top = jnp.max(scores, axis=0, keepdims=True)
            raised = jnp.exp(scores - top)
            total = jnp.sum(raised, axis=0, keepdims=True)
            out = nn(values, (raised * (1.0 / total)).astype(BF16))
            lse = top + jnp.log(total)
            for side in range(2):
                one = slice(side * QB, (side + 1) * QB)
                att_ref[(k + side) * H : (k + side + 1) * H, lanes] = out[:, one]
                lse_ref[k + side : k + side + 1, lanes] = lse[:, one]

    by_span(attend, lax.div(step, NB), place, segment_smem)

    @pl.when(step == steps - 1)
    def _():
        held = jnp.sum(count_scr[...], axis=1, keepdims=True)
        lane = lax.broadcasted_iota(jnp.int32, (E, 128), 1)
        row = lax.broadcasted_iota(jnp.int32, (E, 128), 0)
        count_ref[...] = jnp.sum(jnp.where(lane == row, held, 0.0), axis=0, keepdims=True)


def picks(rows, stride, first):
    at = lax.broadcasted_iota(jnp.int32, (rows, D), 1)
    row = lax.broadcasted_iota(jnp.int32, (rows, D), 0)
    return (at == row * stride + first).astype(F32)


def exact(product, a, b):
    return lax.dot_general(
        a, b, (product, ((), ())), precision=lax.Precision.HIGHEST, preferred_element_type=F32
    )


def gelu_parts(v):
    cdf = 0.5 + 0.5 * lax.erf(v * 0.7071067811865476)
    return cdf, jnp.exp(v * v * -0.5) * 0.3989422804014327


def middle_kernel(
    x_ref, dy_ref, gain_ref, wo_ref, w1_ref, w2_ref, route_ref, gate_ref, att_ref,
    out_ref, dres_ref, datt_ref, delta_ref, dlogit_ref, flat_ref, extra_ref, dgain_ref,
    slot_scr, head_scr, mix_scr, dwo_ref, dw1_ref, dw2t_ref, rows_scr, low_scr, row_sem,
):
    step = pl.program_id(0)

    @pl.when(step == 0)
    def _():
        dwo_ref[...] = jnp.zeros_like(dwo_ref)
        dw1_ref[...] = jnp.zeros_like(dw1_ref)
        dw2t_ref[...] = jnp.zeros_like(dw2t_ref)
        dgain_ref[...] = jnp.zeros_like(dgain_ref)

    routes = route_ref[...]
    tokens = routes.shape[1]
    gates = gate_ref[...]
    for k in range(TOPK):
        rows = slice(k * H, (k + 1) * H)
        slot_scr[rows, :] = (gates[k : k + 1, :] * att_ref[rows, :]).astype(BF16)
    place_heads(routes, slot_scr, mix_scr)
    x = x_ref[...].astype(F32)
    dy = dy_ref[...]
    mixed = mix_scr[...]
    residual = x + tn(mixed, wo_ref[...])
    scale = rms_scale(residual)
    gain = gain_ref[...]
    second = (residual * scale * gain).astype(BF16)
    second_t = second.T
    dy_t = dy.T
    out = residual
    dsecond = jnp.zeros((tokens, D), F32)
    for c in range(0, FF, FC):
        up = w1_ref[:, c : c + FC]
        down = w2_ref[c : c + FC, :]
        pre = nn(second, up)
        cdf, density = gelu_parts(pre)
        hidden = (pre * cdf).astype(BF16)
        dpre = (nt(dy, down) * (cdf + pre * density)).astype(BF16)
        out = out + nn(hidden, down)
        dsecond = dsecond + nt(dpre, up)
        dw2t_ref[:, c : c + FC] += nn(dy_t, hidden)
        dw1_ref[:, c : c + FC] += nn(second_t, dpre)
    out_ref[...] = out.astype(BF16)
    dgain_ref[...] += jnp.sum(dsecond * residual * scale, axis=0, keepdims=True)
    weighted = gain * dsecond
    dres = (
        dy.astype(F32)
        + scale * weighted
        - residual * (scale * scale * scale) * jnp.mean(weighted * residual, axis=-1, keepdims=True)
    )
    dres_ref[...] = dres
    branch = dres.astype(BF16)
    dwo_ref[...] += nn(mixed, branch)
    head_scr[...] = nt(wo_ref[...], branch).astype(BF16)
    dgates = []
    for k in range(TOPK):
        rows = slice(k * H, (k + 1) * H)
        dslot = pick_heads(routes, head_scr, k).astype(F32)
        attended = att_ref[rows, :]
        dgates.append(jnp.sum(dslot * attended, axis=0, keepdims=True))
        datt = (gates[k : k + 1, :] * dslot).astype(BF16)
        datt_ref[rows, :] = datt
        delta_ref[k : k + 1, :] = jnp.sum(datt.astype(F32) * attended, axis=0, keepdims=True)
    dgate = jnp.concatenate(dgates, axis=0)
    dchosen = gates * (dgate - jnp.sum(gates * dgate, axis=0, keepdims=True))
    experts = lax.broadcasted_iota(jnp.int32, (E, tokens), 0)
    dlogits = jnp.zeros((E, tokens), F32)
    for k in range(TOPK):
        dlogits = jnp.where(
            slot_of(routes, k, E) == experts,
            jnp.broadcast_to(dchosen[k : k + 1, :], (E, tokens)),
            dlogits,
        )
    dlogit_ref[...] = dlogits

    @pl.when(step == pl.num_programs(0) - 1)
    def _():
        for c in range(D // 128):
            lanes = slice(c * 128, (c + 1) * 128)
            rows_scr[pl.ds(c, QW, stride=4), :] = dwo_ref[:, lanes]
            rows_scr[pl.ds(W2_ROW - WO_ROW + c, FF, stride=4), :] = dw2t_ref[lanes, :].T
        for c in range(FF // 128):
            rows_scr[pl.ds(W1_ROW - WO_ROW + c, D, stride=16), :] = dw1_ref[:, c * 128 : (c + 1) * 128]
        extra_ref[...] = rows_scr[0:8, :]
        low_scr[...] = rows_scr[8:, :].astype(BF16)
        copy = pltpu.make_async_copy(
            low_scr, flat_ref.at[pl.ds(WO_ROW + 8, low_scr.shape[0]), :], row_sem.at[0]
        )
        copy.start()
        copy.wait()


def head_backward_kernel(
    segment_smem, x_ref, gain_ref, wall_ref, route_ref, start_ref, q_ref, datt_ref,
    lse_ref, delta_ref, kv_ref, kvt_ref, dlogit_ref, dres_ref, dgain_two_ref, extra_ref, flat_in,
    dx_ref, flat_ref,
    dk_scr, dv_scr, dq_scr, dall_scr, prob_scr, dscore_scr, dwall_ref, dgain_ref, rows_scr, low_scr, row_sem,
):
    step = pl.program_id(0)
    place = NB - 1 - lax.rem(step, NB)
    here = pl.multiple_of(place * TB, TB)

    @pl.when(step == 0)
    def _():
        dwall_ref[...] = jnp.zeros_like(dwall_ref)
        dgain_ref[...] = jnp.zeros_like(dgain_ref)

    @pl.when(lax.rem(step, NB) == 0)
    def _():
        dk_scr[...] = jnp.zeros_like(dk_scr)
        dv_scr[...] = jnp.zeros_like(dv_scr)

    def attend(lanes, block, blocks):
        rows = blocks * QB
        first_key = pl.multiple_of((block - (blocks - 1)) * QB, QB)
        mask = key_mask(first_key, block * QB, rows, start_ref[:, lanes])
        keys = kv_ref[pl.ds(first_key, rows), :H]
        values = kv_ref[pl.ds(first_key, rows), H:]
        keys_t = kvt_ref[:H, pl.ds(first_key, rows)]
        queries = [pair_of(q_ref, k, lanes) for k in range(0, TOPK, 2)]
        datts = [pair_of(datt_ref, k, lanes) for k in range(0, TOPK, 2)]
        scores = [nn(keys, queries[0])]
        dprobs = [nn(values, datts[0])]
        for i in range(TOPK // 2):
            if i + 1 < TOPK // 2:
                scores.append(nn(keys, queries[i + 1]))
                dprobs.append(nn(values, datts[i + 1]))
            k = 2 * i
            wide = slice(i * 2 * QB, (i + 1) * 2 * QB)
            probs = jnp.exp(jnp.where(mask, scores[i], NEG_LARGE) - row_pair(lse_ref, k, lanes))
            dscore = (probs * (dprobs[i] - row_pair(delta_ref, k, lanes))).astype(BF16)
            prob_scr[0:rows, wide] = probs.astype(BF16)
            dscore_scr[0:rows, wide] = dscore
            dq = (nn(keys_t, dscore) * (H ** (-0.5))).astype(BF16)
            dq_scr[k * H : (k + 1) * H, lanes] = dq[:, :QB]
            dq_scr[(k + 1) * H : (k + 2) * H, lanes] = dq[:, QB:]
        dv_scr[pl.ds(first_key, rows), :] += nt(prob_scr[0:rows, :], jnp.concatenate(datts, axis=1))
        dk_scr[pl.ds(first_key, rows), :] += nt(dscore_scr[0:rows, :], jnp.concatenate(queries, axis=1))

    by_span(attend, lax.div(step, NB), place, segment_smem)
    place_heads(route_ref[...], dq_scr, dall_scr)
    dkv = jnp.concatenate([dk_scr[pl.ds(here, TB), :], dv_scr[pl.ds(here, TB), :]], axis=1)
    dall_scr[KROW : KROW + 2 * H, :] = dkv.T.astype(BF16)
    dall_scr[RROW : RROW + 32, :] = jnp.concatenate(
        [dlogit_ref[...], jnp.zeros((32 - E, TB), F32)], axis=0
    ).astype(BF16)
    x = x_ref[...].astype(F32)
    scale = rms_scale(x)
    gain = gain_ref[...]
    normed = (x * scale * gain).astype(BF16)
    dall = dall_scr[...]
    dwall_ref[...] += nn(dall, normed)
    dnormed = tn(dall, wall_ref[...])
    dgain_ref[...] += jnp.sum(dnormed * x * scale, axis=0, keepdims=True)
    weighted = gain * dnormed
    dx_ref[...] = (
        dres_ref[...]
        + scale * weighted
        - x * (scale * scale * scale) * jnp.mean(weighted * x, axis=-1, keepdims=True)
    )

    @pl.when(step == pl.num_programs(0) - 1)
    def _():
        for c in range(D // 128):
            lanes = slice(c * 128, (c + 1) * 128)
            rows_scr[c : c + 1, :] = dgain_ref[:, lanes]
            rows_scr[4 + c : 5 + c, :] = dgain_two_ref[:, lanes]
        router_t = dwall_ref[RROW : RROW + E, :]
        across = jnp.concatenate(
            [exact(((1,), (1,)), router_t, picks(32, 16, b)) for b in range(16)], axis=0
        ).T
        for j in range(3):
            rows_scr[pl.ds(WR_ROW + j, 32, stride=3), :] = across[:, j * 128 : (j + 1) * 128]
        for first, row in ((KROW, WK_ROW), (VROW, WV_ROW)):
            part = dwall_ref[first : first + H, :]
            rows_scr[row : row + 256, :] = jnp.concatenate(
                [exact(((1,), (1,)), picks(256, 2, b), part) for b in range(2)], axis=1
            )
        for c in range(QW // 128):
            rows_scr[pl.ds(WQ_ROW + c, D, stride=12), :] = dwall_ref[c * 128 : (c + 1) * 128, :].T
        rows_scr[WO_ROW : WO_ROW + 8, :] = extra_ref[...]
        low_scr[...] = rows_scr[...].astype(BF16)
        copy = pltpu.make_async_copy(low_scr, flat_ref.at[pl.ds(0, WO_ROW + 8), :], row_sem.at[0])
        copy.start()
        copy.wait()


def whole(shape):
    return pl.BlockSpec(shape, lambda *_: (0,) * len(shape), pipeline_mode=pl.Buffered(1))


def kept(shape):
    return pl.BlockSpec(shape, lambda *_: (0,) * len(shape))


SMEM = pl.BlockSpec(memory_space=pltpu.SMEM)


def struct(shape, kind=F32):
    return jax.ShapeDtypeStruct(shape, kind)


def params_for(mib):
    return pltpu.CompilerParams(vmem_limit_bytes=mib * MIB)


def head_forward(tokens, routes_t, segments, wall, gain):
    count = tokens.shape[0]
    steps = count // TB
    across = lambda rows: pl.BlockSpec((rows, TB), lambda b: (0, b))
    down = lambda columns: pl.BlockSpec((TB, columns), lambda b: (b, 0))
    return pl.pallas_call(
        functools.partial(head_forward_kernel, steps),
        grid=(steps,),
        in_specs=[SMEM, down(D), across(TOPK), whole(segments.shape), whole((ALLW, D)), whole((1, D))],
        out_specs=[
            across(TOPK * H), across(TOPK * H), across(TOPK), across(TOPK), down(2 * H), across(2 * H),
            across(1), across(TOPK), whole((1, 128)),
        ],
        scratch_shapes=[
            pltpu.VMEM((ALLW, TB), F32),
            pltpu.VMEM((QW, TB), BF16),
            pltpu.VMEM((LEN, H), BF16),
            pltpu.VMEM((H, LEN), BF16),
            pltpu.VMEM((E, TB), F32),
        ],
        out_shape=[
            struct((TOPK * H, count), BF16),
            struct((TOPK * H, count)),
            struct((TOPK, count)),
            struct((TOPK, count)),
            struct((count, 2 * H), BF16),
            struct((2 * H, count), BF16),
            struct((1, count), jnp.int32),
            struct((TOPK, count), jnp.int32),
            struct((1, 128)),
        ],
        compiler_params=params_for(56),
        name="head_forward",
        cost_estimate=pl.CostEstimate(flops=10_000_000_000, bytes_accessed=16_000_000, transcendentals=0),
    )(segments, tokens, routes_t, segments, wall, gain)


def middle(flat_rows, tokens, grad_out, gain, wo, w1, w2, routes_t, gates, attended):
    count = tokens.shape[0]
    steps = count // MB
    across = lambda rows: pl.BlockSpec((rows, MB), lambda b: (0, b))
    down = lambda columns: pl.BlockSpec((MB, columns), lambda b: (b, 0))
    return pl.pallas_call(
        middle_kernel,
        grid=(steps,),
        in_specs=[
            down(D), down(D), whole((1, D)), whole((QW, D)), whole((D, FF)), whole((FF, D)),
            across(TOPK), across(TOPK), across(TOPK * H),
        ],
        out_specs=[
            down(D), down(D), across(TOPK * H), across(TOPK), across(E),
            pl.BlockSpec(memory_space=pl.ANY), whole((8, 128)), whole((1, D)),
        ],
        out_shape=[
            struct((count, D), BF16),
            struct((count, D)),
            struct((TOPK * H, count), BF16),
            struct((TOPK, count)),
            struct((E, count)),
            struct((flat_rows, 128), BF16),
            struct((8, 128)),
            struct((1, D)),
        ],
        scratch_shapes=[
            pltpu.VMEM((TOPK * H, MB), BF16),
            pltpu.VMEM((QW, MB), BF16),
            pltpu.VMEM((QW, MB), BF16),
            pltpu.VMEM((QW, D), F32),
            pltpu.VMEM((D, FF), F32),
            pltpu.VMEM((D, FF), F32),
            pltpu.VMEM((flat_rows - WO_ROW, 128), F32),
            pltpu.VMEM((flat_rows - WO_ROW - 8, 128), BF16),
            pltpu.SemaphoreType.DMA((1,)),
        ],
        compiler_params=params_for(60),
        name="middle",
    )(tokens, grad_out, gain, wo, w1, w2, routes_t, gates, attended)


def head_backward(
    segments, tokens, gain, wall, routes_t, start, queries, datt, lse, delta, kv, kvt, dlogits, dres,
    dgain_two, extra, flat,
):
    count = tokens.shape[0]
    steps = count // TB

    def place(b):
        return (b // NB) * NB + NB - 1 - b % NB

    across = lambda rows: pl.BlockSpec((rows, TB), lambda b: (0, place(b)))
    down = lambda columns: pl.BlockSpec((TB, columns), lambda b: (place(b), 0))
    return pl.pallas_call(
        head_backward_kernel,
        grid=(steps,),
        in_specs=[
            SMEM, down(D), whole((1, D)), whole((ALLW, D)), across(TOPK), across(1),
            across(TOPK * H), across(TOPK * H), across(TOPK), across(TOPK),
            pl.BlockSpec((LEN, 2 * H), lambda b: (b // NB, 0)),
            pl.BlockSpec((2 * H, LEN), lambda b: (0, b // NB)),
            across(E), down(D), whole((1, D)), whole((8, 128)), pl.BlockSpec(memory_space=pl.ANY),
        ],
        out_specs=[down(D), pl.BlockSpec(memory_space=pl.ANY)],
        scratch_shapes=[
            pltpu.VMEM((LEN, H), F32),
            pltpu.VMEM((LEN, H), F32),
            pltpu.VMEM((TOPK * H, TB), BF16),
            pltpu.VMEM((ALLW, TB), BF16),
            pltpu.VMEM((MOST * QB, TOPK * QB), BF16),
            pltpu.VMEM((MOST * QB, TOPK * QB), BF16),
            pltpu.VMEM((ALLW, D), F32),
            pltpu.VMEM((1, D), F32),
            pltpu.VMEM((WO_ROW + 8, 128), F32),
            pltpu.VMEM((WO_ROW + 8, 128), BF16),
            pltpu.SemaphoreType.DMA((1,)),
        ],
        out_shape=[struct((count, D)), struct(flat.shape, BF16)],
        input_output_aliases={16: 1},
        compiler_params=params_for(56),
        name="head_backward",
        cost_estimate=pl.CostEstimate(flops=30_000_000_000, bytes_accessed=24_000_000, transcendentals=0),
    )(
        segments, tokens, gain, wall, routes_t, start, queries, datt, lse, delta, kv, kvt, dlogits, dres,
        dgain_two, extra, flat,
    )


class Mesh3:
    def __init__(self, shards, over):
        shard = lax.axis_index("dp")
        other = lax.axis_index("fsdp")
        self.over = over
        self.many = shards * over
        self.sizes = {"x": 2, "y": shards // 2, "z": over // 2}
        self.here = {"x": lax.rem(other, 2), "y": lax.div(shard, 2), "z": lax.div(other, 2)}
        self.core = lax.rem(shard, 2)
        self.me = shard * over + other
        self.partner = (shard + 1 - 2 * self.core, other)

    def spots(self):
        x, y, z = (self.sizes[axis] for axis in "xyz")
        return list(itertools.product(range(x), range(y), range(1 - z, z)))

    def exists(self, z_steps):
        at = self.here["z"] + z_steps
        return (at >= 0) & (at < self.sizes["z"])

    def device(self, core, spot):
        x = lax.rem(self.here["x"] + spot[0], self.sizes["x"])
        y = lax.rem(self.here["y"] + spot[1], self.sizes["y"])
        return (y * 2 + core, (self.here["z"] + spot[2]) * 2 + x)

    def number(self, core, spot):
        shard, other = self.device(core, spot)
        return shard * self.over + other

    def others(self, axis):
        size = self.sizes[axis]
        return range(1, size) if axis != "z" else [step for step in range(1 - size, size) if step]

    def greet_near(self):
        barrier = pltpu.get_barrier_semaphore()

        def greet(device):
            pl.semaphore_signal(barrier, inc=1, device_id=device, device_id_type=MESH)

        for axis in "xyz":
            for step in self.others(axis):
                device = self.device(self.core, at(axis, step))
                if axis == "z":
                    pl.when(self.exists(step))(functools.partial(greet, device))
                else:
                    greet(device)
        greet(self.partner)
        pl.semaphore_wait(barrier, sum(self.sizes.values()) - 2)


def at(axis, step):
    return tuple(step if one == axis else 0 for one in "xyz")


def last_axis(axes, spot):
    return max([i for i, axis in enumerate(axes) if spot["xyz".index(axis)]], default=-1)


def pieces_of(window):
    if window < 512:
        return [(0, window)]
    first = (window // 16 + 1) // 2 * 16
    return [(0, first), (first, window - first)]


GATHER_AXES = (("zxy", "yzx"), ("zyx", "xzy"))
REDUCE_AXES = ("zxy", "zyx")


def gather_events(mesh, own_ref, land, send_sem, recv_sem, laid):
    events = []
    pieces = pieces_of(own_ref.shape[0])

    def copy(owner, device, slot, p):
        rows = pl.ds(*pieces[p])
        return pltpu.make_async_remote_copy(
            src_ref=land.at[owner, rows],
            dst_ref=land.at[owner, rows],
            send_sem=send_sem.at[slot, p],
            recv_sem=recv_sem.at[owner, p],
            device_id=device,
            device_id_type=MESH,
        )

    def onward(axes, spot):
        last = last_axis(axes, spot)
        steps = []
        if last >= 0 and axes[last] == "z":
            steps.append(("z", -1 if spot[2] > 0 else 1))
        for axis in axes[last + 1 :]:
            steps += [("z", 1), ("z", -1)] if axis == "z" else [(axis, one) for one in mesh.others(axis)]
        return steps

    for core in range(2):
        slots = {}
        for spot in mesh.spots():
            owner = mesh.number(core, spot)
            there = mesh.exists(spot[2])
            turn = 0.5 * abs(spot[2]) + (spot[0] > 0) + (spot[1] > 0) + (0.001 if spot[2] < 0 else 0)
            for p in range(len(pieces)):
                sends = []
                for axis, step in onward(GATHER_AXES[core][p], spot):
                    key = (spot[0], spot[1], spot[2] % mesh.sizes["z"], axis, step)
                    slot = slots.setdefault(key, len(slots))
                    away = mesh.exists(step) if axis == "z" else True
                    sends.append((mesh.device(core, at(axis, step)), slot, away))
                key = (spot[0], spot[1], spot[2] % mesh.sizes["z"])
                sends.append((mesh.partner, slots.setdefault(key, len(slots)), True))

                def come(owner=owner, spot=spot, p=p, sends=sends):
                    if any(spot):
                        copy(owner, mesh.partner, 0, p).wait_recv()
                    elif p == 0:
                        land[owner] = own_ref[...]
                    for device, slot, away in sends:
                        start = copy(owner, device, slot, p).start
                        if away is True:
                            start()
                        else:
                            pl.when(away)(start)
                    laid(owner, p)

                def across(owner=owner, p=p):
                    copy(owner, mesh.partner, 0, p).wait_recv()
                    laid(owner, p)

                def done(owner=owner, p=p, sends=sends):
                    for _, slot, away in sends:
                        wait = copy(owner, mesh.partner, slot, p).wait_send
                        if away is True:
                            wait()
                        else:
                            pl.when(away)(wait)

                ours = (mesh.core == core) & there
                theirs = (mesh.core != core) & there
                events.append((turn + 0.01 * p, ours, come))
                events.append((1000 + turn, theirs, across))
                events.append((2000, ours, done))
    return sorted(events, key=lambda one: one[0])


def reduce_events(mesh, source, fetch, part, outgo, income, send_sem, recv_sem, total_ref):
    events = []
    half = mesh.many // 2
    pieces = pieces_of(outgo.shape[1])
    x_size, y_size, z_size = (mesh.sizes[axis] for axis in "xyz")
    inward = {spot: half + i for i, spot in enumerate(one for one in mesh.spots() if any(one))}

    def held(spot):
        return (spot[0] * y_size + spot[1]) * z_size + spot[2] % z_size

    def copy(src, slot, device, p):
        rows = pl.ds(*pieces[p])
        return pltpu.make_async_remote_copy(
            src_ref=src,
            dst_ref=income.at[slot, rows],
            send_sem=send_sem.at[slot, p],
            recv_sem=recv_sem.at[slot, p],
            device_id=device,
            device_id_type=MESH,
        )

    def sent(spot, p):
        return outgo.at[held(spot), pl.ds(*pieces[p])]

    def taken(slot, p):
        copy(outgo.at[0, pl.ds(*pieces[p])], slot, mesh.partner, p).wait_recv()
        return income[slot, pl.ds(*pieces[p])].astype(F32)

    for core in range(2):
        axes = REDUCE_AXES[core]
        for spot in mesh.spots():
            owner = mesh.number(core, spot)
            there = mesh.exists(spot[2])
            ours = (mesh.core == core) & there
            theirs = (mesh.core != core) & there
            slot = held(spot)
            last = last_axis(axes, spot)
            for p, (first, rows) in enumerate(pieces):
                turn = 0.5 * p - 1.5 * abs(spot[2]) - (spot[0] > 0) - (spot[1] > 0)
                turn += 0.001 if spot[2] < 0 else 0

                def begin(owner=owner, slot=slot, p=p):
                    fetch(owner, slot, p).start()

                def hand(owner=owner, slot=slot, p=p, first=first, rows=rows):
                    copy(source(owner, first, rows), slot, mesh.partner, p).start()

                def handed(owner=owner, slot=slot, p=p, first=first, rows=rows):
                    copy(source(owner, first, rows), slot, mesh.partner, p).wait_send()

                def onward(owner=owner, spot=spot, slot=slot, last=last, axes=axes, core=core, p=p):
                    mine = pl.ds(*pieces[p])
                    fetch(owner, slot, p).wait()
                    total = part[slot, mine].astype(F32) + taken(slot, p)
                    for axis in axes[max(last, 0) + 1 :]:
                        size = mesh.sizes[axis]
                        for step in mesh.others(axis):
                            child = at(axis, size - step)
                            child = tuple(one or other for one, other in zip(spot, child))
                            total = total + taken(inward[child], p)
                    if last < 0:
                        total_ref[mine, :] = total
                        for step in mesh.others("z"):

                            @pl.when(mesh.exists(step))
                            def _(step=step):
                                total_ref[mine, :] += taken(inward[0, 0, -step], p)

                    else:
                        axis = axes[last]
                        outgo[slot, mine] = total.astype(BF16)
                        device = mesh.device(core, at(axis, spot["xyz".index(axis)]))
                        copy(sent(spot, p), inward[spot], device, p).start()

                def passed(spot=spot, p=p):
                    copy(sent(spot, p), inward[spot], mesh.partner, p).wait_send()

                events.append((-100, ours, begin))
                events.append((turn - 1, theirs, hand))
                events.append((turn, ours, onward))
                events.append((100, theirs, handed))
                if last >= 0:
                    events.append((100, ours, passed))
    return sorted(events, key=lambda one: one[0])


def act_all(events):
    for _, condition, action in events:
        pl.when(condition)(action)


def sum_all(mesh, mine, stats, send_sem, recv_sem):
    total = mine
    base = 0
    for axis in ("core", "x", "y", "z"):
        size = 2 if axis == "core" else mesh.sizes[axis]
        here = mesh.core if axis == "core" else mesh.here[axis]
        stats[base + here] = total

        def copy(place, device, base=base, here=here):
            return pltpu.make_async_remote_copy(
                src_ref=stats.at[base + here],
                dst_ref=stats.at[base + here],
                send_sem=send_sem.at[base + place],
                recv_sem=recv_sem.at[base + here],
                device_id=device,
                device_id_type=MESH,
            )

        def come(place, base=base):
            pltpu.make_async_remote_copy(
                src_ref=stats.at[base + place],
                dst_ref=stats.at[base + place],
                send_sem=send_sem.at[base + place],
                recv_sem=recv_sem.at[base + place],
                device_id=mesh.partner,
                device_id_type=MESH,
            ).wait_recv()

        def target(place, axis=axis, here=here, size=size):
            if axis == "core":
                return mesh.partner
            step = place - here
            return mesh.device(mesh.core, at(axis, step if axis == "z" else step + size))

        for place in range(size):

            @pl.when(here != place)
            def _(place=place):
                copy(place, target(place)).start()

        for place in range(size):

            @pl.when(here != place)
            def _(place=place):
                come(place)
                copy(place, target(place)).wait_send()

        total = stats[base]
        for place in range(1, size):
            total = total + stats[base + place]
        base += size
    return total


def window_rows(shard_size, many):
    units = [(shard_size * d) // UNIT for d in range(many + 1)]
    return 16 * (max(b - a for a, b in zip(units, units[1:])) + 1)


def first_row(shard_size, number):
    if isinstance(number, int):
        return number * shard_size // UNIT * 16
    return pl.multiple_of(lax.div(number * shard_size, UNIT) * 16, 16)


def inner_units(shard_size, many):
    units = [(shard_size * d) // UNIT for d in range(many + 1)]
    return min(b - a for a, b in zip(units, units[1:]))


def lay_inner(shard_size, many, land, flat, owner, first, rows):
    begin = max(first, 16)
    count = min(first + rows, 16 * inner_units(shard_size, many)) - begin
    row = pl.multiple_of(first_row(shard_size, owner) + begin, 16)
    flat[pl.ds(row, count), :] = land[owner, pl.ds(begin, count), :].astype(F32)


def lay_edges(shard_size, many, land, flat):
    inner = 16 * inner_units(shard_size, many)
    flat[0:16, :] = jnp.zeros((16, 128), F32)

    def lay(number, carry):
        row = first_row(shard_size, number)
        after = first_row(shard_size, number + 1)
        flat[pl.ds(row, 16), :] += land[number, 0:16, :].astype(F32)
        tail = land[number, pl.ds(inner, 16), :].astype(F32)
        flat[pl.ds(pl.multiple_of(row + inner, 16), 16), :] = tail
        last = pl.multiple_of(after - row, 16)
        flat[pl.ds(after, 16), :] = land[number, pl.ds(last, 16), :].astype(F32)
        return carry

    lax.fori_loop(0, many, lay, 0)


def early_matrices(flat, wall_ref, gain_one_ref, gain_two_ref):
    for c in range(D // 128):
        lanes = slice(c * 128, (c + 1) * 128)
        gain_one_ref[:, lanes] = flat[c : c + 1, :]
        gain_two_ref[:, lanes] = flat[4 + c : 5 + c, :]
    for c in range(QW // 128):
        wall_ref[c * 128 : (c + 1) * 128, :] = flat[pl.ds(WQ_ROW + c, D, stride=12), :].T.astype(BF16)
    for first, row in ((KROW, WK_ROW), (VROW, WV_ROW)):
        pair = flat[row : row + 256, :].T.astype(BF16)
        wall_ref[first : first + H, :] = (
            nn(pair[:H], picks(256, 2, 0).astype(BF16)) + nn(pair[H:], picks(256, 2, 1).astype(BF16))
        ).astype(BF16)
    across = jnp.concatenate(
        [flat[pl.ds(WR_ROW + j, 32, stride=3), :] for j in range(3)], axis=1
    ).T.astype(BF16)
    router_t = jnp.zeros((E, D), F32)
    for part in range(16):
        router_t = router_t + nn(across[part * E : (part + 1) * E, :], picks(32, 16, part).astype(BF16))
    wall_ref[RROW:ALLW, :] = jnp.concatenate(
        [router_t, jnp.zeros((ALLW - RROW - E, D), F32)], axis=0
    ).astype(BF16)


def gather_kernel(
    mesh, shard_size, own_ref,
    wall_out, gain_one_ref, gain_two_ref, wo_out, w1_out, w2_out,
    land, flat, wall_ref, wo_ref, w1_ref, w2_ref, send_sem, recv_sem, out_sem,
):
    mesh = mesh()
    many = mesh.many
    pieces = pieces_of(own_ref.shape[0])
    mesh.greet_near()

    def laid(owner, p):
        lay_inner(shard_size, many, land, flat, owner, *pieces[p])

    act_all(gather_events(mesh, own_ref, land, send_sem, recv_sem, laid))
    lay_edges(shard_size, many, land, flat)
    copies = []

    def leave(matrix, out):
        copy = pltpu.make_async_copy(matrix, out, out_sem.at[len(copies)])
        copy.start()
        copies.append(copy)

    for c in range(D // 128):
        wo_ref[:, c * 128 : (c + 1) * 128] = flat[pl.ds(WO_ROW + c, QW, stride=4), :].astype(BF16)
    leave(wo_ref, wo_out)
    for c in range(D // 128):
        w2_ref[:, c * 128 : (c + 1) * 128] = flat[pl.ds(W2_ROW + c, FF, stride=4), :].astype(BF16)
    leave(w2_ref, w2_out)
    for c in range(FF // 128):
        w1_ref[:, c * 128 : (c + 1) * 128] = flat[pl.ds(W1_ROW + c, D, stride=16), :].astype(BF16)
    leave(w1_ref, w1_out)
    early_matrices(flat, wall_ref, gain_one_ref, gain_two_ref)
    leave(wall_ref, wall_out)
    for copy in copies:
        copy.wait()


def gather_weights(shards, over, shard_size, own):
    window = own.shape[0]
    many = shards * over
    rows = (shard_size * (many - 1)) // UNIT * 16 + window
    vmem = pl.BlockSpec(memory_space=pltpu.VMEM)
    hbm = pl.BlockSpec(memory_space=pl.ANY)
    mesh = functools.partial(Mesh3, shards, over)
    pieces = len(pieces_of(window))
    return pl.pallas_call(
        functools.partial(gather_kernel, mesh, shard_size),
        in_specs=[vmem],
        out_specs=[hbm, vmem, vmem, hbm, hbm, hbm],
        out_shape=[
            struct((ALLW, D), BF16),
            struct((1, D)),
            struct((1, D)),
            struct((QW, D), BF16),
            struct((D, FF), BF16),
            struct((FF, D), BF16),
        ],
        scratch_shapes=[
            pltpu.VMEM((many, window, 128), BF16),
            pltpu.VMEM((rows, 128), F32),
            pltpu.VMEM((ALLW, D), BF16),
            pltpu.VMEM((QW, D), BF16),
            pltpu.VMEM((D, FF), BF16),
            pltpu.VMEM((FF, D), BF16),
            pltpu.SemaphoreType.DMA((5 * many // 2, pieces)),
            pltpu.SemaphoreType.DMA((many, pieces)),
            pltpu.SemaphoreType.DMA((4,)),
        ],
        compiler_params=pltpu.CompilerParams(
            collective_id=0, has_side_effects=True, vmem_limit_bytes=60 * MIB
        ),
        name="gather_weights",
    )(own)


def reduce_kernel(
    mesh, shard_size, flat_ref, count_ref,
    out_ref, total_ref, gain_ref,
    part, outgo, income, stats, part_sem, send_sem, recv_sem, stat_send, stat_recv,
):
    mesh = mesh()
    window = out_ref.shape[0]
    pieces = pieces_of(window)

    def source(owner, first, rows):
        row = pl.multiple_of(first_row(shard_size, owner) + first, 16)
        return flat_ref.at[pl.ds(row, rows), :]

    def fetch(owner, number, p):
        return pltpu.make_async_copy(
            source(owner, *pieces[p]), part.at[number, pl.ds(*pieces[p])], part_sem.at[number, p]
        )

    mesh.greet_near()
    act_all(reduce_events(mesh, source, fetch, part, outgo, income, send_sem, recv_sem, out_ref))
    total = out_ref[...]
    begin = mesh.me * shard_size - lax.div(mesh.me * shard_size, UNIT) * UNIT
    place = (
        lax.broadcasted_iota(jnp.int32, (window, 128), 0) * 128
        + lax.broadcasted_iota(jnp.int32, (window, 128), 1)
    )
    inside = jnp.where((place >= begin) & (place < begin + shard_size), total, 0.0)
    squares = jnp.sum(jnp.sum(inside * inside, axis=0, keepdims=True), axis=1, keepdims=True)
    lane = lax.broadcasted_iota(jnp.int32, (8, 128), 1)
    row = jnp.where(lane == E, squares, count_ref[...])
    gains = jnp.where(mesh.me == 0, total[0:8, :], 0.0)
    summed = sum_all(mesh, jnp.concatenate([row, gains], axis=0), stats, stat_send, stat_recv)
    total_ref[...] = summed[0:1, :]
    gain_ref[...] = summed[8:16, :]


def reduce_grads(shards, over, shard_size, window, flat, counts):
    vmem = pl.BlockSpec(memory_space=pltpu.VMEM)
    many = shards * over
    mesh = functools.partial(Mesh3, shards, over)
    pieces = len(pieces_of(window))
    incomes = many // 2 + 2 * (shards // 2) * (over - 1)
    steps = 4 + shards // 2 + over // 2
    return pl.pallas_call(
        functools.partial(reduce_kernel, mesh, shard_size),
        in_specs=[pl.BlockSpec(memory_space=pl.ANY), vmem],
        out_specs=[vmem] * 3,
        out_shape=[struct((window, 128)), struct((1, 128)), struct((8, 128))],
        scratch_shapes=[
            pltpu.VMEM((many // 2, window, 128), BF16),
            pltpu.VMEM((many // 2, window, 128), BF16),
            pltpu.VMEM((incomes, window, 128), BF16),
            pltpu.VMEM((steps, 16, 128), F32),
            pltpu.SemaphoreType.DMA((many // 2, pieces)),
            pltpu.SemaphoreType.DMA((incomes, pieces)),
            pltpu.SemaphoreType.DMA((incomes, pieces)),
            pltpu.SemaphoreType.DMA((steps,)),
            pltpu.SemaphoreType.DMA((steps,)),
        ],
        compiler_params=pltpu.CompilerParams(
            collective_id=1, has_side_effects=True, vmem_limit_bytes=56 * MIB
        ),
        name="reduce_grads",
    )(flat, counts)


def local_step(flat_rows, tokens, grad_out, routes, segments, weights):
    wall, gain_one, gain_two, wo, w1, w2 = weights
    queries, attended, gates, lse, kv, kvt, start, routes_t, counts = head_forward(
        tokens, routes.T, segments, wall, gain_one
    )
    output, dres, datt, delta, dlogits, flat, extra, dgain_two = middle(
        flat_rows, tokens, grad_out, gain_two, wo, w1, w2, routes_t, gates, attended
    )
    input_grad, flat = head_backward(
        segments, tokens, gain_one, wall, routes_t, start, queries, datt, lse, delta, kv, kvt, dlogits, dres,
        dgain_two, extra, flat,
    )
    return output, input_grad, flat, counts


def per_device(
    shards, over, tokens, grad_out, routes, segments, params, first_moment, second_moment, ema_weights
):
    shard_size = params.shape[0]
    window = window_rows(shard_size, shards * over)
    flat_rows = (shard_size * (shards * over - 1)) // UNIT * 16 + window
    me = lax.axis_index("dp") * over + lax.axis_index("fsdp")
    begin = lax.rem(me * shard_size, UNIT)
    own = lax.dynamic_slice(
        jnp.pad(params.astype(BF16), (UNIT, window * 128 - shard_size)), (UNIT - begin,), (window * 128,)
    ).reshape(window, 128)
    wall, gain_one, gain_two, wo, w1, w2 = gather_weights(shards, over, shard_size, own)
    output, input_grad, flat, counts = local_step(
        flat_rows, tokens, grad_out, routes, segments, (wall, gain_one, gain_two, wo, w1, w2)
    )
    reduced, sums, gain_grads = reduce_grads(shards, over, shard_size, window, flat, counts)
    grad_shard = lax.dynamic_slice(reduced.reshape(-1), (begin,), (shard_size,))
    total_tokens = tokens.shape[0] * shards * over
    expert_load = sums[0, :E] * (E / (total_tokens * TOPK))
    grad_norm = jnp.sqrt(sums[0, E])
    clipped = grad_shard * (CLIP_LIMIT / jnp.maximum(grad_norm, CLIP_LIMIT))
    new_first = BETA_FIRST * first_moment + (1.0 - BETA_FIRST) * clipped
    new_second = BETA_SECOND * second_moment + (1.0 - BETA_SECOND) * clipped * clipped
    first_hat = new_first / (1.0 - BETA_FIRST**STEP)
    second_hat = new_second / (1.0 - BETA_SECOND**STEP)
    new_params = params * (1.0 - LEARN_RATE * DECAY_RATE) - LEARN_RATE * first_hat / (
        jnp.sqrt(second_hat) + ADAM_EPS
    )
    new_ema = EMA_KEEP * ema_weights + (1.0 - EMA_KEEP) * new_params
    return (
        output,
        input_grad,
        expert_load,
        grad_norm.reshape(1),
        new_params,
        new_first,
        new_second,
        new_ema,
        gain_grads.reshape(2, D),
    )


def solution(mesh):
    row = P(("dp", "fsdp"), None)
    flat = P(("dp", "fsdp"))
    return jax.shard_map(
        functools.partial(per_device, mesh.shape["dp"], mesh.shape["fsdp"]),
        mesh=mesh,
        in_specs=(row, row, row, row, flat, flat, flat, flat),
        out_specs=(row, row, P(), P(), flat, flat, flat, flat, P()),
        check_vma=False,
    )
```

```python
import copy
import functools
import itertools

import jax
import jax.numpy as jnp
from jax import lax
from jax.experimental import pallas as pl
from jax.experimental.pallas import tpu as pltpu
from jax.sharding import PartitionSpec as P

D = 512
E = 24
TOPK = 8
H = 64
FF = 2048
STEP = 10

NORM_EPS = 1e-06
CLIP_LIMIT = 1.0
BETA_FIRST = 0.9
BETA_SECOND = 0.95
LEARN_RATE = 0.1
DECAY_RATE = 0.1
ADAM_EPS = 1e-08
EMA_KEEP = 0.9
NEG_LARGE = -1e30

QW = E * H
KROW = QW
VROW = QW + H
RROW = QW + 2 * H
ALLW = 1696
LEN = 1024
TB = 256
NB = LEN // TB
QB = 128
MOST = 512 // QB + 1
SORT_STEPS = (
    (0, 1), (2, 3), (4, 5), (6, 7), (0, 2), (1, 3), (4, 6), (5, 7), (1, 2), (5, 6),
    (0, 4), (1, 5), (2, 6), (3, 7), (2, 4), (3, 5), (1, 2), (3, 4), (5, 6),
)
FC = 512
MB = 512
MIB = 1 << 20

WR_ROW = 8
WK_ROW = 104
WV_ROW = 360
WQ_ROW = 616
WO_ROW = 6760
W1_ROW = 12904
W2_ROW = 21096
ALL_ROWS = 29288
UNIT = 16 * 128
MESH = pl.DeviceIdType.MESH

F32 = jnp.float32
BF16 = jnp.bfloat16


def nn(a, b):
    return lax.dot_general(a, b, (((1,), (0,)), ((), ())), preferred_element_type=F32)


def nt(a, b):
    return lax.dot_general(a, b, (((1,), (1,)), ((), ())), preferred_element_type=F32)


def tn(a, b):
    return lax.dot_general(a, b, (((0,), (0,)), ((), ())), preferred_element_type=F32)


def rms_scale(values):
    return lax.rsqrt(jnp.mean(values * values, axis=-1, keepdims=True) + NORM_EPS)


def slot_of(routes, k, rows):
    return jnp.broadcast_to(routes[k : k + 1, :], (rows, routes.shape[1]))


def expert_rows(routes, k):
    return jnp.broadcast_to(routes.astype(jnp.int16)[k : k + 1, :], (16, routes.shape[1]))


def pick_heads(routes, source_ref, k):
    tokens = routes.shape[1]
    route = expert_rows(routes, k)
    taken = source_ref[k * H : (k + 1) * H, :].reshape(H // 16, 16, tokens)
    for e in range(k + 1, k + E - TOPK + 1):
        piece = source_ref[e * H : (e + 1) * H, :].reshape(H // 16, 16, tokens)
        taken = jnp.where((route == jnp.int16(e))[None], piece, taken)
    return taken.reshape(H, tokens)


def place_heads(routes, source_ref, target_ref):
    tokens = routes.shape[1]
    rows = [expert_rows(routes, k) for k in range(TOPK)]
    for e in range(E):
        total = jnp.zeros((H // 16, 16, tokens), BF16)
        for k in range(max(0, e - (E - TOPK)), min(TOPK - 1, e) + 1):
            piece = source_ref[k * H : (k + 1) * H, :].reshape(H // 16, 16, tokens)
            total = jnp.where((rows[k] == jnp.int16(e))[None], piece, total)
        target_ref[e * H : (e + 1) * H, :] = total.reshape(H, tokens)


def sorted_rows(rows):
    rows = list(rows)
    for one, two in SORT_STEPS:
        rows[one], rows[two] = jnp.minimum(rows[one], rows[two]), jnp.maximum(rows[one], rows[two])
    return rows


def key_mask(first_key, first_query, rows, start_row):
    keys = lax.broadcasted_iota(jnp.int32, (rows, QB), 0) + first_key
    queries = lax.broadcasted_iota(jnp.int32, (rows, QB), 1) + first_query
    mask = (keys <= queries) & (keys >= start_row)
    return jnp.concatenate([mask, mask], axis=1)


def pair_of(ref, k, lanes):
    return jnp.concatenate(
        [ref[k * H : (k + 1) * H, lanes], ref[(k + 1) * H : (k + 2) * H, lanes]], axis=1
    )


def row_pair(ref, k, lanes):
    return jnp.concatenate([ref[k : k + 1, lanes], ref[k + 1 : k + 2, lanes]], axis=1)


def by_span(attend, row, place, segment_ref):
    def one(j, carry):
        block = place * (TB // QB) + j
        first = block * QB
        span = jnp.int32(1)
        for back in range(MOST - 1):
            last = first - back * QB - 1
            same = segment_ref[row, jnp.maximum(last, 0)] == segment_ref[row, first]
            span = span + jnp.where((last >= 0) & same, 1, 0)
        for blocks in range(1, MOST + 1):

            @pl.when(span == blocks)
            def _(blocks=blocks):
                attend(pl.ds(pl.multiple_of(j * QB, QB), QB), block, blocks)

        return carry

    lax.fori_loop(0, TB // QB, one, 0)


def head_forward_kernel(
    steps, segment_smem, x_ref, route_ref, segment_ref, wall_ref, gain_ref,
    q_ref, att_ref, gate_ref, lse_ref, kv_ref, kvt_ref, start_ref, sorted_ref, count_ref,
    all_scr, low_scr, k_scr, vt_scr, count_scr,
):
    step = pl.program_id(0)
    place = lax.rem(step, NB)
    here = pl.multiple_of(place * TB, TB)

    @pl.when(step == 0)
    def _():
        count_scr[...] = jnp.zeros_like(count_scr)

    row = segment_ref[pl.ds(lax.div(step, NB), 1), :]
    segments = segment_ref[pl.ds(lax.div(step, NB), 1), pl.ds(here, TB)]
    start = jnp.zeros((1, TB), jnp.int32)
    for number in range(1, 4):
        below = jnp.sum((row < number).astype(jnp.int32), axis=1, keepdims=True)
        start = jnp.where(segments == number, below, start)
    start_ref[...] = start
    x = x_ref[...].astype(F32)
    normed = (x * rms_scale(x) * gain_ref[...]).astype(BF16)
    all_scr[...] = nt(wall_ref[...], normed)
    kt = all_scr[KROW : KROW + H, :]
    vt = all_scr[VROW : VROW + H, :]
    logits = all_scr[RROW : RROW + E, :]
    kvt = jnp.concatenate([kt, vt], axis=0)
    kv = kvt.T.astype(BF16)
    kv_ref[...] = kv
    kvt_ref[...] = kvt.astype(BF16)
    k_scr[pl.ds(here, TB), :] = kv[:, :H]
    vt_scr[:, pl.ds(here, TB)] = vt.astype(BF16)
    routes = jnp.concatenate(sorted_rows(route_ref[k : k + 1, :] for k in range(TOPK)), axis=0)
    sorted_ref[...] = routes
    experts = lax.broadcasted_iota(jnp.int32, (E, TB), 0)
    chosen = []
    counts = count_scr[...]
    for k in range(TOPK):
        named = slot_of(routes, k, E) == experts
        chosen.append(jnp.sum(jnp.where(named, logits, 0.0), axis=0, keepdims=True))
        counts = counts + named.astype(F32)
    count_scr[...] = counts
    chosen = jnp.concatenate(chosen, axis=0)
    raised = jnp.exp(chosen - jnp.max(chosen, axis=0, keepdims=True))
    gate_ref[...] = raised / jnp.sum(raised, axis=0, keepdims=True)
    low_scr[...] = all_scr[0:QW, :].astype(BF16)
    for k in range(TOPK):
        q_ref[k * H : (k + 1) * H, :] = pick_heads(routes, low_scr, k) * jnp.asarray(H ** (-0.5), BF16)

    def attend(lanes, block, blocks):
        rows = blocks * QB
        first_key = pl.multiple_of((block - (blocks - 1)) * QB, QB)
        mask = key_mask(first_key, block * QB, rows, start_ref[:, lanes])
        keys = k_scr[pl.ds(first_key, rows), :]
        values = vt_scr[:, pl.ds(first_key, rows)]
        pairs = [nn(keys, pair_of(q_ref, 0, lanes))]
        for k in range(0, TOPK, 2):
            if k + 2 < TOPK:
                pairs.append(nn(keys, pair_of(q_ref, k + 2, lanes)))
            scores = jnp.where(mask, pairs[k // 2], NEG_LARGE)
            top = jnp.max(scores, axis=0, keepdims=True)
            raised = jnp.exp(scores - top)
            total = jnp.sum(raised, axis=0, keepdims=True)
            out = nn(values, (raised * (1.0 / total)).astype(BF16))
            lse = top + jnp.log(total)
            for side in range(2):
                one = slice(side * QB, (side + 1) * QB)
                att_ref[(k + side) * H : (k + side + 1) * H, lanes] = out[:, one]
                lse_ref[k + side : k + side + 1, lanes] = lse[:, one]

    by_span(attend, lax.div(step, NB), place, segment_smem)

    @pl.when(step == steps - 1)
    def _():
        held = jnp.sum(count_scr[...], axis=1, keepdims=True)
        lane = lax.broadcasted_iota(jnp.int32, (E, 128), 1)
        row = lax.broadcasted_iota(jnp.int32, (E, 128), 0)
        count_ref[...] = jnp.sum(jnp.where(lane == row, held, 0.0), axis=0, keepdims=True)


def picks(rows, stride, first):
    at = lax.broadcasted_iota(jnp.int32, (rows, D), 1)
    row = lax.broadcasted_iota(jnp.int32, (rows, D), 0)
    return (at == row * stride + first).astype(F32)


def exact(product, a, b):
    return lax.dot_general(
        a, b, (product, ((), ())), precision=lax.Precision.HIGHEST, preferred_element_type=F32
    )


def gelu_parts(v):
    cdf = 0.5 + 0.5 * lax.erf(v * 0.7071067811865476)
    return cdf, jnp.exp(v * v * -0.5) * 0.3989422804014327


def middle_kernel(
    x_ref, dy_ref, gain_ref, wo_ref, w1_ref, w2_ref, route_ref, gate_ref, att_ref,
    out_ref, dres_ref, datt_ref, delta_ref, dlogit_ref, flat_ref, extra_ref, dgain_ref,
    slot_scr, head_scr, mix_scr, dwo_ref, dw1_ref, dw2t_ref, rows_scr, low_scr, row_sem,
):
    step = pl.program_id(0)

    @pl.when(step == 0)
    def _():
        dwo_ref[...] = jnp.zeros_like(dwo_ref)
        dw1_ref[...] = jnp.zeros_like(dw1_ref)
        dw2t_ref[...] = jnp.zeros_like(dw2t_ref)
        dgain_ref[...] = jnp.zeros_like(dgain_ref)

    routes = route_ref[...]
    tokens = routes.shape[1]
    gates = gate_ref[...]
    for k in range(TOPK):
        rows = slice(k * H, (k + 1) * H)
        slot_scr[rows, :] = (gates[k : k + 1, :] * att_ref[rows, :]).astype(BF16)
    place_heads(routes, slot_scr, mix_scr)
    x = x_ref[...].astype(F32)
    dy = dy_ref[...]
    mixed = mix_scr[...]
    residual = x + tn(mixed, wo_ref[...])
    scale = rms_scale(residual)
    gain = gain_ref[...]
    second = (residual * scale * gain).astype(BF16)
    second_t = second.T
    dy_t = dy.T
    out = residual
    dsecond = jnp.zeros((tokens, D), F32)
    for c in range(0, FF, FC):
        up = w1_ref[:, c : c + FC]
        down = w2_ref[c : c + FC, :]
        pre = nn(second, up)
        cdf, density = gelu_parts(pre)
        hidden = (pre * cdf).astype(BF16)
        dpre = (nt(dy, down) * (cdf + pre * density)).astype(BF16)
        out = out + nn(hidden, down)
        dsecond = dsecond + nt(dpre, up)
        dw2t_ref[:, c : c + FC] += nn(dy_t, hidden)
        dw1_ref[:, c : c + FC] += nn(second_t, dpre)
    out_ref[...] = out.astype(BF16)
    dgain_ref[...] += jnp.sum(dsecond * residual * scale, axis=0, keepdims=True)
    weighted = gain * dsecond
    dres = (
        dy.astype(F32)
        + scale * weighted
        - residual * (scale * scale * scale) * jnp.mean(weighted * residual, axis=-1, keepdims=True)
    )
    dres_ref[...] = dres
    branch = dres.astype(BF16)
    dwo_ref[...] += nn(mixed, branch)
    head_scr[...] = nt(wo_ref[...], branch).astype(BF16)
    dgates = []
    for k in range(TOPK):
        rows = slice(k * H, (k + 1) * H)
        dslot = pick_heads(routes, head_scr, k).astype(F32)
        attended = att_ref[rows, :]
        dgates.append(jnp.sum(dslot * attended, axis=0, keepdims=True))
        datt = (gates[k : k + 1, :] * dslot).astype(BF16)
        datt_ref[rows, :] = datt
        delta_ref[k : k + 1, :] = jnp.sum(datt.astype(F32) * attended, axis=0, keepdims=True)
    dgate = jnp.concatenate(dgates, axis=0)
    dchosen = gates * (dgate - jnp.sum(gates * dgate, axis=0, keepdims=True))
    experts = lax.broadcasted_iota(jnp.int32, (E, tokens), 0)
    dlogits = jnp.zeros((E, tokens), F32)
    for k in range(TOPK):
        dlogits = jnp.where(
            slot_of(routes, k, E) == experts,
            jnp.broadcast_to(dchosen[k : k + 1, :], (E, tokens)),
            dlogits,
        )
    dlogit_ref[...] = dlogits

    @pl.when(step == pl.num_programs(0) - 1)
    def _():
        for c in range(D // 128):
            lanes = slice(c * 128, (c + 1) * 128)
            rows_scr[pl.ds(c, QW, stride=4), :] = dwo_ref[:, lanes]
            rows_scr[pl.ds(W2_ROW - WO_ROW + c, FF, stride=4), :] = dw2t_ref[lanes, :].T
        for c in range(FF // 128):
            rows_scr[pl.ds(W1_ROW - WO_ROW + c, D, stride=16), :] = dw1_ref[:, c * 128 : (c + 1) * 128]
        extra_ref[...] = rows_scr[0:8, :]
        low_scr[...] = rows_scr[8:, :].astype(BF16)
        copy = pltpu.make_async_copy(
            low_scr, flat_ref.at[pl.ds(WO_ROW + 8, low_scr.shape[0]), :], row_sem.at[0]
        )
        copy.start()
        copy.wait()


def head_backward_kernel(
    segment_smem, x_ref, gain_ref, wall_ref, route_ref, start_ref, q_ref, datt_ref,
    lse_ref, delta_ref, kv_ref, kvt_ref, dlogit_ref, dres_ref, dgain_two_ref, extra_ref, flat_in,
    dx_ref, flat_ref,
    dk_scr, dv_scr, dq_scr, dall_scr, prob_scr, dscore_scr, dwall_ref, dgain_ref, rows_scr, low_scr, row_sem,
):
    step = pl.program_id(0)
    place = NB - 1 - lax.rem(step, NB)
    here = pl.multiple_of(place * TB, TB)

    @pl.when(step == 0)
    def _():
        dwall_ref[...] = jnp.zeros_like(dwall_ref)
        dgain_ref[...] = jnp.zeros_like(dgain_ref)

    @pl.when(lax.rem(step, NB) == 0)
    def _():
        dk_scr[...] = jnp.zeros_like(dk_scr)
        dv_scr[...] = jnp.zeros_like(dv_scr)

    def attend(lanes, block, blocks):
        rows = blocks * QB
        first_key = pl.multiple_of((block - (blocks - 1)) * QB, QB)
        mask = key_mask(first_key, block * QB, rows, start_ref[:, lanes])
        keys = kv_ref[pl.ds(first_key, rows), :H]
        values = kv_ref[pl.ds(first_key, rows), H:]
        keys_t = kvt_ref[:H, pl.ds(first_key, rows)]
        queries = [pair_of(q_ref, k, lanes) for k in range(0, TOPK, 2)]
        datts = [pair_of(datt_ref, k, lanes) for k in range(0, TOPK, 2)]
        scores = [nn(keys, queries[0])]
        dprobs = [nn(values, datts[0])]
        for i in range(TOPK // 2):
            if i + 1 < TOPK // 2:
                scores.append(nn(keys, queries[i + 1]))
                dprobs.append(nn(values, datts[i + 1]))
            k = 2 * i
            wide = slice(i * 2 * QB, (i + 1) * 2 * QB)
            probs = jnp.exp(jnp.where(mask, scores[i], NEG_LARGE) - row_pair(lse_ref, k, lanes))
            dscore = (probs * (dprobs[i] - row_pair(delta_ref, k, lanes))).astype(BF16)
            prob_scr[0:rows, wide] = probs.astype(BF16)
            dscore_scr[0:rows, wide] = dscore
            dq = (nn(keys_t, dscore) * (H ** (-0.5))).astype(BF16)
            dq_scr[k * H : (k + 1) * H, lanes] = dq[:, :QB]
            dq_scr[(k + 1) * H : (k + 2) * H, lanes] = dq[:, QB:]
        dv_scr[pl.ds(first_key, rows), :] += nt(prob_scr[0:rows, :], jnp.concatenate(datts, axis=1))
        dk_scr[pl.ds(first_key, rows), :] += nt(dscore_scr[0:rows, :], jnp.concatenate(queries, axis=1))

    by_span(attend, lax.div(step, NB), place, segment_smem)
    place_heads(route_ref[...], dq_scr, dall_scr)
    dkv = jnp.concatenate([dk_scr[pl.ds(here, TB), :], dv_scr[pl.ds(here, TB), :]], axis=1)
    dall_scr[KROW : KROW + 2 * H, :] = dkv.T.astype(BF16)
    dall_scr[RROW : RROW + 32, :] = jnp.concatenate(
        [dlogit_ref[...], jnp.zeros((32 - E, TB), F32)], axis=0
    ).astype(BF16)
    x = x_ref[...].astype(F32)
    scale = rms_scale(x)
    gain = gain_ref[...]
    normed = (x * scale * gain).astype(BF16)
    dall = dall_scr[...]
    dwall_ref[...] += nn(dall, normed)
    dnormed = tn(dall, wall_ref[...])
    dgain_ref[...] += jnp.sum(dnormed * x * scale, axis=0, keepdims=True)
    weighted = gain * dnormed
    dx_ref[...] = (
        dres_ref[...]
        + scale * weighted
        - x * (scale * scale * scale) * jnp.mean(weighted * x, axis=-1, keepdims=True)
    )

    @pl.when(step == pl.num_programs(0) - 1)
    def _():
        for c in range(D // 128):
            lanes = slice(c * 128, (c + 1) * 128)
            rows_scr[c : c + 1, :] = dgain_ref[:, lanes]
            rows_scr[4 + c : 5 + c, :] = dgain_two_ref[:, lanes]
        router_t = dwall_ref[RROW : RROW + E, :]
        across = jnp.concatenate(
            [exact(((1,), (1,)), router_t, picks(32, 16, b)) for b in range(16)], axis=0
        ).T
        for j in range(3):
            rows_scr[pl.ds(WR_ROW + j, 32, stride=3), :] = across[:, j * 128 : (j + 1) * 128]
        for first, row in ((KROW, WK_ROW), (VROW, WV_ROW)):
            part = dwall_ref[first : first + H, :]
            rows_scr[row : row + 256, :] = jnp.concatenate(
                [exact(((1,), (1,)), picks(256, 2, b), part) for b in range(2)], axis=1
            )
        for c in range(QW // 128):
            rows_scr[pl.ds(WQ_ROW + c, D, stride=12), :] = dwall_ref[c * 128 : (c + 1) * 128, :].T
        rows_scr[WO_ROW : WO_ROW + 8, :] = extra_ref[...]
        low_scr[...] = rows_scr[...].astype(BF16)
        copy = pltpu.make_async_copy(low_scr, flat_ref.at[pl.ds(0, WO_ROW + 8), :], row_sem.at[0])
        copy.start()
        copy.wait()


def whole(shape):
    return pl.BlockSpec(shape, lambda *_: (0,) * len(shape), pipeline_mode=pl.Buffered(1))


def kept(shape):
    return pl.BlockSpec(shape, lambda *_: (0,) * len(shape))


SMEM = pl.BlockSpec(memory_space=pltpu.SMEM)


def struct(shape, kind=F32):
    return jax.ShapeDtypeStruct(shape, kind)


def params_for(mib):
    return pltpu.CompilerParams(vmem_limit_bytes=mib * MIB)


def head_forward(tokens, routes_t, segments, wall, gain):
    count = tokens.shape[0]
    steps = count // TB
    across = lambda rows: pl.BlockSpec((rows, TB), lambda b: (0, b))
    down = lambda columns: pl.BlockSpec((TB, columns), lambda b: (b, 0))
    return pl.pallas_call(
        functools.partial(head_forward_kernel, steps),
        grid=(steps,),
        in_specs=[SMEM, down(D), across(TOPK), whole(segments.shape), whole((ALLW, D)), whole((1, D))],
        out_specs=[
            across(TOPK * H), across(TOPK * H), across(TOPK), across(TOPK), down(2 * H), across(2 * H),
            across(1), across(TOPK), whole((1, 128)),
        ],
        scratch_shapes=[
            pltpu.VMEM((ALLW, TB), F32),
            pltpu.VMEM((QW, TB), BF16),
            pltpu.VMEM((LEN, H), BF16),
            pltpu.VMEM((H, LEN), BF16),
            pltpu.VMEM((E, TB), F32),
        ],
        out_shape=[
            struct((TOPK * H, count), BF16),
            struct((TOPK * H, count)),
            struct((TOPK, count)),
            struct((TOPK, count)),
            struct((count, 2 * H), BF16),
            struct((2 * H, count), BF16),
            struct((1, count), jnp.int32),
            struct((TOPK, count), jnp.int32),
            struct((1, 128)),
        ],
        compiler_params=params_for(56),
        name="head_forward",
        cost_estimate=pl.CostEstimate(flops=10_000_000_000, bytes_accessed=16_000_000, transcendentals=0),
    )(segments, tokens, routes_t, segments, wall, gain)


def middle(flat_rows, tokens, grad_out, gain, wo, w1, w2, routes_t, gates, attended):
    count = tokens.shape[0]
    steps = count // MB
    across = lambda rows: pl.BlockSpec((rows, MB), lambda b: (0, b))
    down = lambda columns: pl.BlockSpec((MB, columns), lambda b: (b, 0))
    return pl.pallas_call(
        middle_kernel,
        grid=(steps,),
        in_specs=[
            down(D), down(D), whole((1, D)), whole((QW, D)), whole((D, FF)), whole((FF, D)),
            across(TOPK), across(TOPK), across(TOPK * H),
        ],
        out_specs=[
            down(D), down(D), across(TOPK * H), across(TOPK), across(E),
            pl.BlockSpec(memory_space=pl.ANY), whole((8, 128)), whole((1, D)),
        ],
        out_shape=[
            struct((count, D), BF16),
            struct((count, D)),
            struct((TOPK * H, count), BF16),
            struct((TOPK, count)),
            struct((E, count)),
            struct((flat_rows, 128), BF16),
            struct((8, 128)),
            struct((1, D)),
        ],
        scratch_shapes=[
            pltpu.VMEM((TOPK * H, MB), BF16),
            pltpu.VMEM((QW, MB), BF16),
            pltpu.VMEM((QW, MB), BF16),
            pltpu.VMEM((QW, D), F32),
            pltpu.VMEM((D, FF), F32),
            pltpu.VMEM((D, FF), F32),
            pltpu.VMEM((flat_rows - WO_ROW, 128), F32),
            pltpu.VMEM((flat_rows - WO_ROW - 8, 128), BF16),
            pltpu.SemaphoreType.DMA((1,)),
        ],
        compiler_params=params_for(60),
        name="middle",
    )(tokens, grad_out, gain, wo, w1, w2, routes_t, gates, attended)


def head_backward(
    segments, tokens, gain, wall, routes_t, start, queries, datt, lse, delta, kv, kvt, dlogits, dres,
    dgain_two, extra, flat,
):
    count = tokens.shape[0]
    steps = count // TB

    def place(b):
        return (b // NB) * NB + NB - 1 - b % NB

    across = lambda rows: pl.BlockSpec((rows, TB), lambda b: (0, place(b)))
    down = lambda columns: pl.BlockSpec((TB, columns), lambda b: (place(b), 0))
    return pl.pallas_call(
        head_backward_kernel,
        grid=(steps,),
        in_specs=[
            SMEM, down(D), whole((1, D)), whole((ALLW, D)), across(TOPK), across(1),
            across(TOPK * H), across(TOPK * H), across(TOPK), across(TOPK),
            pl.BlockSpec((LEN, 2 * H), lambda b: (b // NB, 0)),
            pl.BlockSpec((2 * H, LEN), lambda b: (0, b // NB)),
            across(E), down(D), whole((1, D)), whole((8, 128)), pl.BlockSpec(memory_space=pl.ANY),
        ],
        out_specs=[down(D), pl.BlockSpec(memory_space=pl.ANY)],
        scratch_shapes=[
            pltpu.VMEM((LEN, H), F32),
            pltpu.VMEM((LEN, H), F32),
            pltpu.VMEM((TOPK * H, TB), BF16),
            pltpu.VMEM((ALLW, TB), BF16),
            pltpu.VMEM((MOST * QB, TOPK * QB), BF16),
            pltpu.VMEM((MOST * QB, TOPK * QB), BF16),
            pltpu.VMEM((ALLW, D), F32),
            pltpu.VMEM((1, D), F32),
            pltpu.VMEM((WO_ROW + 8, 128), F32),
            pltpu.VMEM((WO_ROW + 8, 128), BF16),
            pltpu.SemaphoreType.DMA((1,)),
        ],
        out_shape=[struct((count, D)), struct(flat.shape, BF16)],
        input_output_aliases={16: 1},
        compiler_params=params_for(56),
        name="head_backward",
        cost_estimate=pl.CostEstimate(flops=30_000_000_000, bytes_accessed=24_000_000, transcendentals=0),
    )(
        segments, tokens, gain, wall, routes_t, start, queries, datt, lse, delta, kv, kvt, dlogits, dres,
        dgain_two, extra, flat,
    )


class Mesh3:
    def __init__(self, shards, over):
        shard = lax.axis_index("dp")
        other = lax.axis_index("fsdp")
        self.over = over
        self.many = shards * over
        self.sizes = {"x": 2, "y": shards // 2, "z": over // 2}
        self.here = {"x": lax.rem(other, 2), "y": lax.div(shard, 2), "z": lax.div(other, 2)}
        self.core = lax.rem(shard, 2)
        self.me = shard * over + other
        self.partner = (shard + 1 - 2 * self.core, other)

    def at_z(self, z):
        same = copy.copy(self)
        if z is not None:
            same.here = dict(self.here, z=z)
        return same

    def spots(self):
        x, y, z = (self.sizes[axis] for axis in "xyz")
        return list(itertools.product(range(x), range(y), range(1 - z, z)))

    def round_spots(self):
        return list(itertools.product(*[range(self.sizes[axis]) for axis in "xyz"]))

    def exists(self, z_steps):
        place = self.here["z"] + z_steps
        if isinstance(place, int):
            return 0 <= place < self.sizes["z"]
        return (place >= 0) & (place < self.sizes["z"])

    def device(self, core, spot):
        size = self.sizes["z"]
        x = lax.rem(self.here["x"] + spot[0], self.sizes["x"])
        y = lax.rem(self.here["y"] + spot[1], self.sizes["y"])
        z = self.here["z"] + spot[2]
        z = z % size if isinstance(z, int) else lax.rem(z + size, size)
        return (y * 2 + core, z * 2 + x)

    def number(self, core, spot):
        shard, other = self.device(core, spot)
        return shard * self.over + other

    def greet(self, devices):
        barrier = pltpu.get_barrier_semaphore()
        for device in devices:
            pl.semaphore_signal(barrier, inc=1, device_id=device, device_id_type=MESH)
        pl.semaphore_wait(barrier, len(devices))

    def near(self):
        steps = [at(axis, step) for axis in "xyz" for step in range(1, self.sizes[axis])]
        return [self.device(self.core, step) for step in steps] + [self.partner]

    def column(self):
        steps = [(core, step) for core in range(2) for step in range(self.sizes["z"]) if core or step]
        return [self.device(lax.rem(self.core + core, 2), (0, 0, step)) for core, step in steps]

    def layer(self):
        steps = [(x, y, 0) for x in range(self.sizes["x"]) for y in range(self.sizes["y"]) if x or y]
        return [self.device(self.core, step) for step in steps]


def at(axis, step):
    return tuple(step if one == axis else 0 for one in "xyz")


def last_axis(axes, spot):
    return max([i for i, axis in enumerate(axes) if spot["xyz".index(axis)]], default=-1)


def pieces_of(window):
    if window < 512:
        return [(0, window)]
    first = (window // 16 + 1) // 2 * 16
    return [(0, first), (first, window - first)]


def act(condition, action):
    if condition is True:
        action()
    elif condition is not False:
        pl.when(condition)(action)


GATHER_AXES = (("zxy", "yzx"), ("zyx", "xzy"))
REDUCE_AXES = ("zxy", "zyx")


def gather_own_core(mesh, core, land, send_sem, recv_sem, begin):
    window = land.shape[1]
    pieces = pieces_of(window)
    slots = {}
    events = []

    def moved(owner, device, slot, p):
        rows = pl.ds(*pieces[p])
        return pltpu.make_async_remote_copy(
            src_ref=land.at[owner, rows],
            dst_ref=land.at[owner, rows],
            send_sem=send_sem.at[slot, p],
            recv_sem=recv_sem.at[owner, p],
            device_id=device,
            device_id_type=MESH,
        )

    def onward(axes, spot):
        last = last_axis(axes, spot)
        steps = []
        if last >= 0 and axes[last] == "z":
            steps.append(("z", -1 if spot[2] > 0 else 1))
        for axis in axes[last + 1 :]:
            steps += [("z", 1), ("z", -1)] if axis == "z" else [
                (axis, one) for one in range(1, mesh.sizes[axis])
            ]
        return steps

    for spot in mesh.spots():
        there = mesh.exists(spot[2])
        if there is False:
            continue
        owner = mesh.number(core, spot)
        turn = 0.5 * abs(spot[2]) + (spot[0] > 0) + (spot[1] > 0) + (0.001 if spot[2] < 0 else 0)
        for p in range(len(pieces)):
            sends = []
            for axis, step in onward(GATHER_AXES[core][p], spot):
                key = (spot[0], spot[1], spot[2] % mesh.sizes["z"], axis, step)
                away = mesh.exists(step) if axis == "z" else True
                if away is not False:
                    slot = slots.setdefault(key, len(slots))
                    sends.append((mesh.device(core, at(axis, step)), slot, away))
            key = (spot[0], spot[1], spot[2] % mesh.sizes["z"])
            sends.append((mesh.partner, slots.setdefault(key, len(slots)), True))

            def come(owner=owner, spot=spot, p=p, sends=sends):
                if any(spot):
                    moved(owner, mesh.partner, 0, p).wait_recv()
                for device, slot, away in sends:
                    act(away, moved(owner, device, slot, p).start)

            def done(owner=owner, p=p, sends=sends):
                for _, slot, away in sends:
                    act(away, moved(owner, mesh.partner, slot, p).wait_send)

            events.append((turn + 0.01 * p, there, come if begin else done))
    for _, there, action in sorted(events, key=lambda one: one[0]):
        act(there, action)


def gather_blocks(mesh, land, send_sem, recv_sem, begin):
    known = range(mesh.sizes["z"]) if mesh.sizes["z"] <= 4 else [None]
    for core in range(2):
        for z in known:

            @pl.when((mesh.core == core) & (True if z is None else mesh.here["z"] == z))
            def _(core=core, z=z):
                gather_own_core(mesh.at_z(z), core, land, send_sem, recv_sem, begin)


def each_owner(mesh, core, action):
    def one(number, carry):
        shard = 2 * lax.div(number, mesh.over) + core
        action(shard * mesh.over + lax.rem(number, mesh.over))
        return carry

    lax.fori_loop(0, mesh.many // 2, one, 0)


def reduce_blocks(mesh, core, source, mine, outgo, income, send_sem, recv_sem, total_ref):
    pieces = pieces_of(outgo.shape[1])
    half = mesh.many // 2
    held = {spot: i for i, spot in enumerate(mesh.round_spots())}

    def across(kind, spot):
        slot = held[spot]
        return pltpu.make_async_remote_copy(
            src_ref=source(mesh.number(kind, spot)),
            dst_ref=income.at[slot],
            send_sem=send_sem.at[slot, 0],
            recv_sem=recv_sem.at[slot, 0],
            device_id=mesh.partner,
            device_id_type=MESH,
        )

    def moved(spot, p, device):
        rows = pl.ds(*pieces[p])
        slot = half + held[spot]
        return pltpu.make_async_remote_copy(
            src_ref=outgo.at[held[spot], rows],
            dst_ref=income.at[slot, rows],
            send_sem=send_sem.at[slot, p],
            recv_sem=recv_sem.at[slot, p],
            device_id=device,
            device_id_type=MESH,
        )

    def far(spot):
        z = {0: 0, 1: 3, 2: 5, 3: 8}.get(spot[2], 2 * spot[2] + 2)
        return z + 2 * (spot[0] > 0) + 2 * (spot[1] > 0)

    for spot in sorted(held, key=far, reverse=True):
        across(1 - core, spot).start()
    axes = REDUCE_AXES[core]
    order = sorted(itertools.product(held, range(len(pieces))), key=lambda one: one[1] - 2 * far(one[0]))
    for spot, p in order:
        if p == 0:
            across(core, spot).wait_recv()
        rows = pl.ds(*pieces[p])
        total = mine(mesh.number(core, spot), *pieces[p]) + income[held[spot], rows].astype(F32)
        last = last_axis(axes, spot)
        for axis in axes[last + 1 :]:
            size = mesh.sizes[axis]
            for step in range(1, size):
                child = tuple(one or other for one, other in zip(spot, at(axis, size - step)))
                moved(child, p, mesh.partner).wait_recv()
                total = total + income[half + held[child], rows].astype(F32)
        if last < 0:
            total_ref[rows, :] = total
        else:
            outgo[held[spot], rows] = total.astype(BF16)
            step = spot["xyz".index(axes[last])]
            moved(spot, p, mesh.device(core, at(axes[last], step))).start()
    for spot, p in order:
        if p == 0:
            across(1 - core, spot).wait_send()
        if any(spot):
            moved(spot, p, mesh.partner).wait_send()


def sum_all(mesh, mine, stats, send_sem, recv_sem):
    column = mesh.sizes["z"] * 2
    layer = mesh.sizes["x"] * mesh.sizes["y"]
    groups = (
        (0, column, mesh.here["z"] * 2 + mesh.core, mesh.column()),
        (column, layer, mesh.here["x"] * mesh.sizes["y"] + mesh.here["y"], mesh.layer()),
    )
    total = mine
    for base, size, here, devices in groups:
        stats[base + here] = total

        def sent(j, device, base=base, here=here):
            return pltpu.make_async_remote_copy(
                src_ref=stats.at[base + here],
                dst_ref=stats.at[base + here],
                send_sem=send_sem.at[base + j],
                recv_sem=recv_sem.at[base + here],
                device_id=device,
                device_id_type=MESH,
            )

        def come(place, base=base):
            return pltpu.make_async_remote_copy(
                src_ref=stats.at[base + place],
                dst_ref=stats.at[base + place],
                send_sem=send_sem.at[base],
                recv_sem=recv_sem.at[base + place],
                device_id=mesh.partner,
                device_id_type=MESH,
            )

        for j, device in enumerate(devices):
            sent(j, device).start()
        for j in range(1, size):
            come(lax.rem(here + j, size)).wait_recv()
        for j, device in enumerate(devices):
            sent(j, device).wait_send()
        total = stats[base]
        for place in range(1, size):
            total = total + stats[base + place]
    return total


def window_rows(shard_size, many):
    units = [(shard_size * d) // UNIT for d in range(many + 1)]
    return 16 * (max(b - a for a, b in zip(units, units[1:])) + 1)


def first_row(shard_size, number):
    if isinstance(number, int):
        return number * shard_size // UNIT * 16
    return pl.multiple_of(lax.div(number * shard_size, UNIT) * 16, 16)


def inner_units(shard_size, many):
    units = [(shard_size * d) // UNIT for d in range(many + 1)]
    return min(b - a for a, b in zip(units, units[1:]))


def lay_inner(shard_size, many, land, flat, owner):
    count = 16 * inner_units(shard_size, many) - 16
    row = pl.multiple_of(first_row(shard_size, owner) + 16, 16)
    flat[pl.ds(row, count), :] = land[owner, pl.ds(16, count), :].astype(F32)


def lay_edges(shard_size, many, land, flat):
    inner = 16 * inner_units(shard_size, many)
    flat[0:16, :] = jnp.zeros((16, 128), F32)

    def lay(number, carry):
        row = first_row(shard_size, number)
        after = first_row(shard_size, number + 1)
        flat[pl.ds(row, 16), :] += land[number, 0:16, :].astype(F32)
        tail = land[number, pl.ds(inner, 16), :].astype(F32)
        flat[pl.ds(pl.multiple_of(row + inner, 16), 16), :] = tail
        last = pl.multiple_of(after - row, 16)
        flat[pl.ds(after, 16), :] = land[number, pl.ds(last, 16), :].astype(F32)
        return carry

    lax.fori_loop(0, many, lay, 0)


def early_matrices(flat, wall_ref, gain_one_ref, gain_two_ref):
    for c in range(D // 128):
        lanes = slice(c * 128, (c + 1) * 128)
        gain_one_ref[:, lanes] = flat[c : c + 1, :]
        gain_two_ref[:, lanes] = flat[4 + c : 5 + c, :]
    for c in range(QW // 128):
        wall_ref[c * 128 : (c + 1) * 128, :] = flat[pl.ds(WQ_ROW + c, D, stride=12), :].T.astype(BF16)
    for first, row in ((KROW, WK_ROW), (VROW, WV_ROW)):
        pair = flat[row : row + 256, :].T.astype(BF16)
        wall_ref[first : first + H, :] = (
            nn(pair[:H], picks(256, 2, 0).astype(BF16)) + nn(pair[H:], picks(256, 2, 1).astype(BF16))
        ).astype(BF16)
    across = jnp.concatenate(
        [flat[pl.ds(WR_ROW + j, 32, stride=3), :] for j in range(3)], axis=1
    ).T.astype(BF16)
    router_t = jnp.zeros((E, D), F32)
    for part in range(16):
        router_t = router_t + nn(across[part * E : (part + 1) * E, :], picks(32, 16, part).astype(BF16))
    wall_ref[RROW:ALLW, :] = jnp.concatenate(
        [router_t, jnp.zeros((ALLW - RROW - E, D), F32)], axis=0
    ).astype(BF16)


def gather_kernel(
    mesh, shard_size, own_ref,
    wall_out, gain_one_ref, gain_two_ref, wo_out, w1_out, w2_out,
    land, flat, wall_ref, wo_ref, w1_ref, w2_ref, send_sem, recv_sem, out_sem,
):
    mesh = mesh()
    many = mesh.many
    mesh.greet(mesh.near())
    land[mesh.me] = own_ref[...]
    gather_blocks(mesh, land, send_sem, recv_sem, True)
    each_owner(mesh, mesh.core, functools.partial(lay_inner, shard_size, many, land, flat))

    def arrive(owner):
        for p in range(recv_sem.shape[1]):
            rows = pl.ds(*pieces_of(own_ref.shape[0])[p])
            pltpu.make_async_remote_copy(
                src_ref=land.at[owner, rows],
                dst_ref=land.at[owner, rows],
                send_sem=send_sem.at[0, p],
                recv_sem=recv_sem.at[owner, p],
                device_id=mesh.partner,
                device_id_type=MESH,
            ).wait_recv()
        lay_inner(shard_size, many, land, flat, owner)

    each_owner(mesh, 1 - mesh.core, arrive)
    lay_edges(shard_size, many, land, flat)
    copies = []

    def leave(matrix, out):
        one = pltpu.make_async_copy(matrix, out, out_sem.at[len(copies)])
        one.start()
        copies.append(one)

    for c in range(D // 128):
        wo_ref[:, c * 128 : (c + 1) * 128] = flat[pl.ds(WO_ROW + c, QW, stride=4), :].astype(BF16)
    leave(wo_ref, wo_out)
    for c in range(D // 128):
        w2_ref[:, c * 128 : (c + 1) * 128] = flat[pl.ds(W2_ROW + c, FF, stride=4), :].astype(BF16)
    leave(w2_ref, w2_out)
    for c in range(FF // 128):
        w1_ref[:, c * 128 : (c + 1) * 128] = flat[pl.ds(W1_ROW + c, D, stride=16), :].astype(BF16)
    leave(w1_ref, w1_out)
    early_matrices(flat, wall_ref, gain_one_ref, gain_two_ref)
    leave(wall_ref, wall_out)
    gather_blocks(mesh, land, send_sem, recv_sem, False)
    for one in copies:
        one.wait()


def gather_weights(shards, over, shard_size, own):
    window = own.shape[0]
    many = shards * over
    rows = (shard_size * (many - 1)) // UNIT * 16 + window
    vmem = pl.BlockSpec(memory_space=pltpu.VMEM)
    hbm = pl.BlockSpec(memory_space=pl.ANY)
    mesh = functools.partial(Mesh3, shards, over)
    pieces = len(pieces_of(window))
    return pl.pallas_call(
        functools.partial(gather_kernel, mesh, shard_size),
        in_specs=[vmem],
        out_specs=[hbm, vmem, vmem, hbm, hbm, hbm],
        out_shape=[
            struct((ALLW, D), BF16),
            struct((1, D)),
            struct((1, D)),
            struct((QW, D), BF16),
            struct((D, FF), BF16),
            struct((FF, D), BF16),
        ],
        scratch_shapes=[
            pltpu.VMEM((many, window, 128), BF16),
            pltpu.VMEM((rows, 128), F32),
            pltpu.VMEM((ALLW, D), BF16),
            pltpu.VMEM((QW, D), BF16),
            pltpu.VMEM((D, FF), BF16),
            pltpu.VMEM((FF, D), BF16),
            pltpu.SemaphoreType.DMA((5 * many // 2, pieces)),
            pltpu.SemaphoreType.DMA((many, pieces)),
            pltpu.SemaphoreType.DMA((4,)),
        ],
        compiler_params=pltpu.CompilerParams(
            collective_id=0, has_side_effects=True, vmem_limit_bytes=60 * MIB
        ),
        name="gather_weights",
    )(own)


def reduce_kernel(
    mesh, shard_size, flat_ref, count_ref,
    out_ref, total_ref, gain_ref,
    part, outgo, income, stats, part_sem, send_sem, recv_sem, stat_send, stat_recv,
):
    mesh = mesh()
    window = out_ref.shape[0]
    span = part.shape[1]

    def source(owner):
        return flat_ref.at[pl.ds(first_row(shard_size, owner), window), :]

    def fetch(y):
        first = first_row(shard_size, (2 * y + mesh.core) * mesh.over)
        return pltpu.make_async_copy(flat_ref.at[pl.ds(first, span), :], part.at[y], part_sem.at[y])

    def mine(owner, first, rows):
        shard = lax.div(owner, mesh.over)
        row = first_row(shard_size, owner) - first_row(shard_size, shard * mesh.over) + first
        return part[lax.div(shard, 2), pl.ds(pl.multiple_of(row, 16), rows), :].astype(F32)

    for y in range(mesh.sizes["y"]):
        fetch(y).start()
    mesh.greet(mesh.column() + mesh.layer())
    for y in range(mesh.sizes["y"]):
        fetch(y).wait()
    for core in range(2):

        @pl.when(mesh.core == core)
        def _(core=core):
            reduce_blocks(mesh, core, source, mine, outgo, income, send_sem, recv_sem, out_ref)

    total = out_ref[...]
    begin = mesh.me * shard_size - lax.div(mesh.me * shard_size, UNIT) * UNIT
    place = (
        lax.broadcasted_iota(jnp.int32, (window, 128), 0) * 128
        + lax.broadcasted_iota(jnp.int32, (window, 128), 1)
    )
    inside = jnp.where((place >= begin) & (place < begin + shard_size), total, 0.0)
    squares = jnp.sum(jnp.sum(inside * inside, axis=0, keepdims=True), axis=1, keepdims=True)
    lane = lax.broadcasted_iota(jnp.int32, (8, 128), 1)
    row = jnp.where(lane == E, squares, count_ref[...])
    gains = jnp.where(mesh.me == 0, total[0:8, :], 0.0)
    summed = sum_all(mesh, jnp.concatenate([row, gains], axis=0), stats, stat_send, stat_recv)
    total_ref[...] = summed[0:1, :]
    gain_ref[...] = summed[8:16, :]


def reduce_grads(shards, over, shard_size, window, flat, counts):
    vmem = pl.BlockSpec(memory_space=pltpu.VMEM)
    many = shards * over
    mesh = functools.partial(Mesh3, shards, over)
    pieces = len(pieces_of(window))
    steps = over + shards
    units = [(shard_size * d) // UNIT for d in range(many)]
    span = 16 * max(units[d + over - 1] - units[d] for d in range(0, many, over)) + window
    return pl.pallas_call(
        functools.partial(reduce_kernel, mesh, shard_size),
        in_specs=[pl.BlockSpec(memory_space=pl.ANY), vmem],
        out_specs=[vmem] * 3,
        out_shape=[struct((window, 128)), struct((1, 128)), struct((8, 128))],
        scratch_shapes=[
            pltpu.VMEM((shards // 2, span, 128), BF16),
            pltpu.VMEM((many // 2, window, 128), BF16),
            pltpu.VMEM((many, window, 128), BF16),
            pltpu.VMEM((steps, 16, 128), F32),
            pltpu.SemaphoreType.DMA((shards // 2,)),
            pltpu.SemaphoreType.DMA((many, pieces)),
            pltpu.SemaphoreType.DMA((many, pieces)),
            pltpu.SemaphoreType.DMA((steps,)),
            pltpu.SemaphoreType.DMA((steps,)),
        ],
        compiler_params=pltpu.CompilerParams(
            collective_id=1, has_side_effects=True, vmem_limit_bytes=56 * MIB
        ),
        name="reduce_grads",
    )(flat, counts)


def local_step(flat_rows, tokens, grad_out, routes, segments, weights):
    wall, gain_one, gain_two, wo, w1, w2 = weights
    queries, attended, gates, lse, kv, kvt, start, routes_t, counts = head_forward(
        tokens, routes.T, segments, wall, gain_one
    )
    output, dres, datt, delta, dlogits, flat, extra, dgain_two = middle(
        flat_rows, tokens, grad_out, gain_two, wo, w1, w2, routes_t, gates, attended
    )
    input_grad, flat = head_backward(
        segments, tokens, gain_one, wall, routes_t, start, queries, datt, lse, delta, kv, kvt, dlogits, dres,
        dgain_two, extra, flat,
    )
    return output, input_grad, flat, counts


def per_device(
    shards, over, tokens, grad_out, routes, segments, params, first_moment, second_moment, ema_weights
):
    shard_size = params.shape[0]
    window = window_rows(shard_size, shards * over)
    flat_rows = (shard_size * (shards * over - 1)) // UNIT * 16 + window + 16
    me = lax.axis_index("dp") * over + lax.axis_index("fsdp")
    begin = lax.rem(me * shard_size, UNIT)
    own = lax.dynamic_slice(
        jnp.pad(params.astype(BF16), (UNIT, window * 128 - shard_size)), (UNIT - begin,), (window * 128,)
    ).reshape(window, 128)
    wall, gain_one, gain_two, wo, w1, w2 = gather_weights(shards, over, shard_size, own)
    output, input_grad, flat, counts = local_step(
        flat_rows, tokens, grad_out, routes, segments, (wall, gain_one, gain_two, wo, w1, w2)
    )
    reduced, sums, gain_grads = reduce_grads(shards, over, shard_size, window, flat, counts)
    grad_shard = lax.dynamic_slice(reduced.reshape(-1), (begin,), (shard_size,))
    total_tokens = tokens.shape[0] * shards * over
    expert_load = sums[0, :E] * (E / (total_tokens * TOPK))
    grad_norm = jnp.sqrt(sums[0, E])
    clipped = grad_shard * (CLIP_LIMIT / jnp.maximum(grad_norm, CLIP_LIMIT))
    new_first = BETA_FIRST * first_moment + (1.0 - BETA_FIRST) * clipped
    new_second = BETA_SECOND * second_moment + (1.0 - BETA_SECOND) * clipped * clipped
    first_hat = new_first / (1.0 - BETA_FIRST**STEP)
    second_hat = new_second / (1.0 - BETA_SECOND**STEP)
    new_params = params * (1.0 - LEARN_RATE * DECAY_RATE) - LEARN_RATE * first_hat / (
        jnp.sqrt(second_hat) + ADAM_EPS
    )
    new_ema = EMA_KEEP * ema_weights + (1.0 - EMA_KEEP) * new_params
    return (
        output,
        input_grad,
        expert_load,
        grad_norm.reshape(1),
        new_params,
        new_first,
        new_second,
        new_ema,
        gain_grads.reshape(2, D),
    )


def solution(mesh):
    row = P(("dp", "fsdp"), None)
    flat = P(("dp", "fsdp"))
    return jax.shard_map(
        functools.partial(per_device, mesh.shape["dp"], mesh.shape["fsdp"]),
        mesh=mesh,
        in_specs=(row, row, row, row, flat, flat, flat, flat),
        out_specs=(row, row, P(), P(), flat, flat, flat, flat, P()),
        check_vma=False,
    )
```

```python
import copy
import functools
import itertools

import jax
import jax.numpy as jnp
from jax import lax
from jax.experimental import pallas as pl
from jax.experimental.pallas import tpu as pltpu
from jax.sharding import PartitionSpec as P

D = 512
E = 24
TOPK = 8
H = 64
FF = 2048
STEP = 10

NORM_EPS = 1e-06
CLIP_LIMIT = 1.0
BETA_FIRST = 0.9
BETA_SECOND = 0.95
LEARN_RATE = 0.1
DECAY_RATE = 0.1
ADAM_EPS = 1e-08
EMA_KEEP = 0.9
NEG_LARGE = -1e30

QW = E * H
KROW = QW
VROW = QW + H
RROW = QW + 2 * H
ALLW = 1696
LEN = 1024
TB = 256
NB = LEN // TB
QB = 128
MOST = 512 // QB + 1
SORT_STEPS = (
    (0, 1), (2, 3), (4, 5), (6, 7), (0, 2), (1, 3), (4, 6), (5, 7), (1, 2), (5, 6),
    (0, 4), (1, 5), (2, 6), (3, 7), (2, 4), (3, 5), (1, 2), (3, 4), (5, 6),
)
FC = 512
MB = 512
MIB = 1 << 20

WR_ROW = 8
WK_ROW = 104
WV_ROW = 360
WQ_ROW = 616
WO_ROW = 6760
W1_ROW = 12904
W2_ROW = 21096
ALL_ROWS = 29288
UNIT = 16 * 128
MESH = pl.DeviceIdType.MESH

F32 = jnp.float32
BF16 = jnp.bfloat16


def nn(a, b):
    return lax.dot_general(a, b, (((1,), (0,)), ((), ())), preferred_element_type=F32)


def nt(a, b):
    return lax.dot_general(a, b, (((1,), (1,)), ((), ())), preferred_element_type=F32)


def tn(a, b):
    return lax.dot_general(a, b, (((0,), (0,)), ((), ())), preferred_element_type=F32)


def rms_scale(values):
    return lax.rsqrt(jnp.mean(values * values, axis=-1, keepdims=True) + NORM_EPS)


def slot_of(routes, k, rows):
    return jnp.broadcast_to(routes[k : k + 1, :], (rows, routes.shape[1]))


def expert_rows(routes, k):
    return jnp.broadcast_to(routes.astype(jnp.int16)[k : k + 1, :], (16, routes.shape[1]))


def pick_heads(routes, source_ref, k):
    tokens = routes.shape[1]
    route = expert_rows(routes, k)
    taken = source_ref[k * H : (k + 1) * H, :].reshape(H // 16, 16, tokens)
    for e in range(k + 1, k + E - TOPK + 1):
        piece = source_ref[e * H : (e + 1) * H, :].reshape(H // 16, 16, tokens)
        taken = jnp.where((route == jnp.int16(e))[None], piece, taken)
    return taken.reshape(H, tokens)


def place_heads(routes, source_ref, target_ref):
    tokens = routes.shape[1]
    rows = [expert_rows(routes, k) for k in range(TOPK)]
    for e in range(E):
        total = jnp.zeros((H // 16, 16, tokens), BF16)
        for k in range(max(0, e - (E - TOPK)), min(TOPK - 1, e) + 1):
            piece = source_ref[k * H : (k + 1) * H, :].reshape(H // 16, 16, tokens)
            total = jnp.where((rows[k] == jnp.int16(e))[None], piece, total)
        target_ref[e * H : (e + 1) * H, :] = total.reshape(H, tokens)


def sorted_rows(rows):
    rows = list(rows)
    for one, two in SORT_STEPS:
        rows[one], rows[two] = jnp.minimum(rows[one], rows[two]), jnp.maximum(rows[one], rows[two])
    return rows


def key_mask(first_key, first_query, rows, start_row):
    keys = lax.broadcasted_iota(jnp.int32, (rows, QB), 0) + first_key
    queries = lax.broadcasted_iota(jnp.int32, (rows, QB), 1) + first_query
    mask = (keys <= queries) & (keys >= start_row)
    return jnp.concatenate([mask, mask], axis=1)


def pair_of(ref, k, lanes):
    return jnp.concatenate(
        [ref[k * H : (k + 1) * H, lanes], ref[(k + 1) * H : (k + 2) * H, lanes]], axis=1
    )


def row_pair(ref, k, lanes):
    return jnp.concatenate([ref[k : k + 1, lanes], ref[k + 1 : k + 2, lanes]], axis=1)


def by_span(attend, row, place, segment_ref):
    def one(j, carry):
        block = place * (TB // QB) + j
        first = block * QB
        span = jnp.int32(1)
        for back in range(MOST - 1):
            last = first - back * QB - 1
            same = segment_ref[row, jnp.maximum(last, 0)] == segment_ref[row, first]
            span = span + jnp.where((last >= 0) & same, 1, 0)
        for blocks in range(1, MOST + 1):

            @pl.when(span == blocks)
            def _(blocks=blocks):
                attend(pl.ds(pl.multiple_of(j * QB, QB), QB), block, blocks)

        return carry

    lax.fori_loop(0, TB // QB, one, 0)


def head_forward_kernel(
    steps, segment_smem, x_ref, route_ref, segment_ref, wall_ref, gain_ref,
    q_ref, att_ref, gate_ref, lse_ref, kv_ref, kvt_ref, start_ref, sorted_ref, count_ref,
    all_scr, low_scr, k_scr, vt_scr, count_scr,
):
    step = pl.program_id(0)
    place = lax.rem(step, NB)
    here = pl.multiple_of(place * TB, TB)

    @pl.when(step == 0)
    def _():
        count_scr[...] = jnp.zeros_like(count_scr)

    row = segment_ref[pl.ds(lax.div(step, NB), 1), :]
    segments = segment_ref[pl.ds(lax.div(step, NB), 1), pl.ds(here, TB)]
    start = jnp.zeros((1, TB), jnp.int32)
    for number in range(1, 4):
        below = jnp.sum((row < number).astype(jnp.int32), axis=1, keepdims=True)
        start = jnp.where(segments == number, below, start)
    start_ref[...] = start
    x = x_ref[...].astype(F32)
    normed = (x * rms_scale(x) * gain_ref[...]).astype(BF16)
    all_scr[...] = nt(wall_ref[...], normed)
    kt = all_scr[KROW : KROW + H, :]
    vt = all_scr[VROW : VROW + H, :]
    logits = all_scr[RROW : RROW + E, :]
    kvt = jnp.concatenate([kt, vt], axis=0)
    kv = kvt.T.astype(BF16)
    kv_ref[...] = kv
    kvt_ref[...] = kvt.astype(BF16)
    k_scr[pl.ds(here, TB), :] = kv[:, :H]
    vt_scr[:, pl.ds(here, TB)] = vt.astype(BF16)
    routes = jnp.concatenate(sorted_rows(route_ref[k : k + 1, :] for k in range(TOPK)), axis=0)
    sorted_ref[...] = routes
    experts = lax.broadcasted_iota(jnp.int32, (E, TB), 0)
    chosen = []
    counts = count_scr[...]
    for k in range(TOPK):
        named = slot_of(routes, k, E) == experts
        chosen.append(jnp.sum(jnp.where(named, logits, 0.0), axis=0, keepdims=True))
        counts = counts + named.astype(F32)
    count_scr[...] = counts
    chosen = jnp.concatenate(chosen, axis=0)
    raised = jnp.exp(chosen - jnp.max(chosen, axis=0, keepdims=True))
    gate_ref[...] = raised / jnp.sum(raised, axis=0, keepdims=True)
    low_scr[...] = all_scr[0:QW, :].astype(BF16)
    for k in range(TOPK):
        q_ref[k * H : (k + 1) * H, :] = pick_heads(routes, low_scr, k) * jnp.asarray(H ** (-0.5), BF16)

    def attend(lanes, block, blocks):
        rows = blocks * QB
        first_key = pl.multiple_of((block - (blocks - 1)) * QB, QB)
        mask = key_mask(first_key, block * QB, rows, start_ref[:, lanes])
        keys = k_scr[pl.ds(first_key, rows), :]
        values = vt_scr[:, pl.ds(first_key, rows)]
        pairs = [nn(keys, pair_of(q_ref, 0, lanes))]
        for k in range(0, TOPK, 2):
            if k + 2 < TOPK:
                pairs.append(nn(keys, pair_of(q_ref, k + 2, lanes)))
            scores = jnp.where(mask, pairs[k // 2], NEG_LARGE)
            top = jnp.max(scores, axis=0, keepdims=True)
            raised = jnp.exp(scores - top)
            total = jnp.sum(raised, axis=0, keepdims=True)
            out = nn(values, (raised * (1.0 / total)).astype(BF16))
            lse = top + jnp.log(total)
            for side in range(2):
                one = slice(side * QB, (side + 1) * QB)
                att_ref[(k + side) * H : (k + side + 1) * H, lanes] = out[:, one]
                lse_ref[k + side : k + side + 1, lanes] = lse[:, one]

    by_span(attend, lax.div(step, NB), place, segment_smem)

    @pl.when(step == steps - 1)
    def _():
        held = jnp.sum(count_scr[...], axis=1, keepdims=True)
        lane = lax.broadcasted_iota(jnp.int32, (E, 128), 1)
        row = lax.broadcasted_iota(jnp.int32, (E, 128), 0)
        count_ref[...] = jnp.sum(jnp.where(lane == row, held, 0.0), axis=0, keepdims=True)


def picks(rows, stride, first):
    at = lax.broadcasted_iota(jnp.int32, (rows, D), 1)
    row = lax.broadcasted_iota(jnp.int32, (rows, D), 0)
    return (at == row * stride + first).astype(F32)


def exact(product, a, b):
    return lax.dot_general(
        a, b, (product, ((), ())), precision=lax.Precision.HIGHEST, preferred_element_type=F32
    )


def gelu_parts(v):
    cdf = 0.5 + 0.5 * lax.erf(v * 0.7071067811865476)
    return cdf, jnp.exp(v * v * -0.5) * 0.3989422804014327


def middle_kernel(
    x_ref, dy_ref, gain_ref, wo_ref, w1_ref, w2_ref, route_ref, gate_ref, att_ref,
    out_ref, dres_ref, datt_ref, delta_ref, dlogit_ref, dgain_ref,
    mix_ref, branch_ref, second_t_ref, dpre_ref, dy_t_ref, hidden_ref,
    slot_scr, head_scr,
):
    @pl.when(pl.program_id(0) == 0)
    def _():
        dgain_ref[...] = jnp.zeros_like(dgain_ref)

    routes = route_ref[...]
    tokens = routes.shape[1]
    gates = gate_ref[...]
    for k in range(TOPK):
        rows = slice(k * H, (k + 1) * H)
        slot_scr[rows, :] = (gates[k : k + 1, :] * att_ref[rows, :]).astype(BF16)
    place_heads(routes, slot_scr, mix_ref)
    x = x_ref[...].astype(F32)
    dy = dy_ref[...]
    residual = x + tn(mix_ref[...], wo_ref[...])
    scale = rms_scale(residual)
    gain = gain_ref[...]
    second = (residual * scale * gain).astype(BF16)
    second_t_ref[...] = second.T
    dy_t_ref[...] = dy.T
    out = residual
    dsecond = jnp.zeros((tokens, D), F32)
    for c in range(0, FF, FC):
        up = w1_ref[:, c : c + FC]
        down = w2_ref[c : c + FC, :]
        pre = nn(second, up)
        cdf, density = gelu_parts(pre)
        hidden = (pre * cdf).astype(BF16)
        dpre = (nt(dy, down) * (cdf + pre * density)).astype(BF16)
        out = out + nn(hidden, down)
        dsecond = dsecond + nt(dpre, up)
        hidden_ref[:, c : c + FC] = hidden
        dpre_ref[:, c : c + FC] = dpre
    out_ref[...] = out.astype(BF16)
    dgain_ref[...] += jnp.sum(dsecond * residual * scale, axis=0, keepdims=True)
    weighted = gain * dsecond
    dres = (
        dy.astype(F32)
        + scale * weighted
        - residual * (scale * scale * scale) * jnp.mean(weighted * residual, axis=-1, keepdims=True)
    )
    dres_ref[...] = dres
    branch = dres.astype(BF16)
    branch_ref[...] = branch
    head_scr[...] = nt(wo_ref[...], branch).astype(BF16)
    dgates = []
    for k in range(TOPK):
        rows = slice(k * H, (k + 1) * H)
        dslot = pick_heads(routes, head_scr, k).astype(F32)
        attended = att_ref[rows, :]
        dgates.append(jnp.sum(dslot * attended, axis=0, keepdims=True))
        datt = (gates[k : k + 1, :] * dslot).astype(BF16)
        datt_ref[rows, :] = datt
        delta_ref[k : k + 1, :] = jnp.sum(datt.astype(F32) * attended, axis=0, keepdims=True)
    dgate = jnp.concatenate(dgates, axis=0)
    dchosen = gates * (dgate - jnp.sum(gates * dgate, axis=0, keepdims=True))
    experts = lax.broadcasted_iota(jnp.int32, (E, tokens), 0)
    dlogits = jnp.zeros((E, tokens), F32)
    for k in range(TOPK):
        dlogits = jnp.where(
            slot_of(routes, k, E) == experts,
            jnp.broadcast_to(dchosen[k : k + 1, :], (E, tokens)),
            dlogits,
        )
    dlogit_ref[...] = dlogits


def head_backward_kernel(
    segment_smem, x_ref, gain_ref, wall_ref, route_ref, start_ref, q_ref, datt_ref,
    lse_ref, delta_ref, kv_ref, kvt_ref, dlogit_ref, dres_ref,
    dx_ref, dgain_ref, dquery_ref, drest_ref, normed_ref,
    dk_scr, dv_scr, dq_scr, prob_scr, dscore_scr,
):
    step = pl.program_id(0)
    place = NB - 1 - lax.rem(step, NB)
    here = pl.multiple_of(place * TB, TB)

    @pl.when(step == 0)
    def _():
        dgain_ref[...] = jnp.zeros_like(dgain_ref)

    @pl.when(lax.rem(step, NB) == 0)
    def _():
        dk_scr[...] = jnp.zeros_like(dk_scr)
        dv_scr[...] = jnp.zeros_like(dv_scr)

    def attend(lanes, block, blocks):
        rows = blocks * QB
        first_key = pl.multiple_of((block - (blocks - 1)) * QB, QB)
        mask = key_mask(first_key, block * QB, rows, start_ref[:, lanes])
        keys = kv_ref[pl.ds(first_key, rows), :H]
        values = kv_ref[pl.ds(first_key, rows), H:]
        keys_t = kvt_ref[:H, pl.ds(first_key, rows)]
        queries = [pair_of(q_ref, k, lanes) for k in range(0, TOPK, 2)]
        datts = [pair_of(datt_ref, k, lanes) for k in range(0, TOPK, 2)]
        scores = [nn(keys, queries[0])]
        dprobs = [nn(values, datts[0])]
        for i in range(TOPK // 2):
            if i + 1 < TOPK // 2:
                scores.append(nn(keys, queries[i + 1]))
                dprobs.append(nn(values, datts[i + 1]))
            k = 2 * i
            wide = slice(i * 2 * QB, (i + 1) * 2 * QB)
            probs = jnp.exp(jnp.where(mask, scores[i], NEG_LARGE) - row_pair(lse_ref, k, lanes))
            dscore = (probs * (dprobs[i] - row_pair(delta_ref, k, lanes))).astype(BF16)
            prob_scr[0:rows, wide] = probs.astype(BF16)
            dscore_scr[0:rows, wide] = dscore
            dq = (nn(keys_t, dscore) * (H ** (-0.5))).astype(BF16)
            dq_scr[k * H : (k + 1) * H, lanes] = dq[:, :QB]
            dq_scr[(k + 1) * H : (k + 2) * H, lanes] = dq[:, QB:]
        dv_scr[pl.ds(first_key, rows), :] += nt(prob_scr[0:rows, :], jnp.concatenate(datts, axis=1))
        dk_scr[pl.ds(first_key, rows), :] += nt(dscore_scr[0:rows, :], jnp.concatenate(queries, axis=1))

    by_span(attend, lax.div(step, NB), place, segment_smem)
    place_heads(route_ref[...], dq_scr, dquery_ref)
    dkv = jnp.concatenate([dk_scr[pl.ds(here, TB), :], dv_scr[pl.ds(here, TB), :]], axis=1)
    drest_ref[0 : 2 * H, :] = dkv.T.astype(BF16)
    drest_ref[2 * H :, :] = jnp.concatenate(
        [dlogit_ref[...], jnp.zeros((32 - E, TB), F32)], axis=0
    ).astype(BF16)
    x = x_ref[...].astype(F32)
    scale = rms_scale(x)
    gain = gain_ref[...]
    normed = (x * scale * gain).astype(BF16)
    normed_ref[...] = normed
    dnormed = tn(dquery_ref[...], wall_ref[:QW, :]) + tn(drest_ref[...], wall_ref[QW:, :])
    dgain_ref[...] += jnp.sum(dnormed * x * scale, axis=0, keepdims=True)
    weighted = gain * dnormed
    dx_ref[...] = (
        dres_ref[...]
        + scale * weighted
        - x * (scale * scale * scale) * jnp.mean(weighted * x, axis=-1, keepdims=True)
    )


def weight_grad_kernel(
    dgain_one_ref, dgain_two_ref, drest_ref, dquery_ref, normed_ref, mix_ref, branch_hbm, second_hbm,
    dpre_ref, dy_hbm, hidden_ref,
    flat_ref,
    branch, second_t, dy_t, rows_scr, low_scr, in_sem, out_sem,
):
    step = pl.program_id(0)
    early = [
        pltpu.make_async_copy(source, target, in_sem.at[i])
        for i, (source, target) in enumerate(((branch_hbm, branch), (second_hbm, second_t), (dy_hbm, dy_t)))
    ]
    ends = (0, WO_ROW // 16 * 16, W1_ROW // 16 * 16, W2_ROW // 16 * 16, -(-ALL_ROWS // 16) * 16)

    def out(number):
        rows = pl.ds(ends[number], ends[number + 1] - ends[number])
        return pltpu.make_async_copy(low_scr.at[rows, :], flat_ref.at[rows, :], out_sem.at[number])

    def leave(number):
        rows = pl.ds(ends[number], ends[number + 1] - ends[number])
        low_scr[rows, :] = rows_scr[rows, :].astype(BF16)
        out(number).start()

    @pl.when(step == 0)
    def _():
        for copy in early:
            copy.start()
        for c in range(D // 128):
            lanes = slice(c * 128, (c + 1) * 128)
            rows_scr[c : c + 1, :] = dgain_one_ref[:, lanes]
            rows_scr[4 + c : 5 + c, :] = dgain_two_ref[:, lanes]
        rest = nn(drest_ref[...], normed_ref[...])
        across = jnp.concatenate(
            [exact(((1,), (1,)), rest[2 * H : 2 * H + E, :], picks(32, 16, b)) for b in range(16)], axis=0
        ).T
        for j in range(3):
            rows_scr[pl.ds(WR_ROW + j, 32, stride=3), :] = across[:, j * 128 : (j + 1) * 128]
        for first, row in ((0, WK_ROW), (H, WV_ROW)):
            part = rest[first : first + H, :]
            rows_scr[row : row + 256, :] = jnp.concatenate(
                [exact(((1,), (1,)), picks(256, 2, b), part) for b in range(2)], axis=1
            )

    @pl.when((step >= 1) & (step < 4))
    def _():
        part = nn(dquery_ref[...], normed_ref[...])
        for c in range(4):
            rows_scr[pl.ds(WQ_ROW + 4 * (step - 1) + c, D, stride=12), :] = part[
                c * 128 : (c + 1) * 128, :
            ].T

        @pl.when(step == 3)
        def _():
            leave(0)

    @pl.when((step >= 4) & (step < 7))
    def _():
        pl.when(step == 4)(early[0].wait)
        part = nn(mix_ref[...], branch[...])
        for c in range(4):
            rows_scr[pl.ds(WO_ROW + 2048 * (step - 4) + c, 512, stride=4), :] = part[
                :, c * 128 : (c + 1) * 128
            ]

        @pl.when(step == 6)
        def _():
            leave(1)

    @pl.when((step >= 7) & (step < 11))
    def _():
        pl.when(step == 7)(early[1].wait)
        part = nn(second_t[...], dpre_ref[...])
        for c in range(4):
            rows_scr[pl.ds(W1_ROW + 4 * (step - 7) + c, D, stride=16), :] = part[
                :, c * 128 : (c + 1) * 128
            ]

        @pl.when(step == 10)
        def _():
            leave(2)

    @pl.when(step >= 11)
    def _():
        pl.when(step == 11)(early[2].wait)
        part = nn(dy_t[...], hidden_ref[...])
        for c in range(4):
            rows_scr[pl.ds(W2_ROW + 2048 * (step - 11) + c, 512, stride=4), :] = part[
                c * 128 : (c + 1) * 128, :
            ].T

        @pl.when(step == 14)
        def _():
            leave(3)
            for number in range(4):
                out(number).wait()


def whole(shape):
    return pl.BlockSpec(shape, lambda *_: (0,) * len(shape), pipeline_mode=pl.Buffered(1))


def kept(shape):
    return pl.BlockSpec(shape, lambda *_: (0,) * len(shape))


SMEM = pl.BlockSpec(memory_space=pltpu.SMEM)


def struct(shape, kind=F32):
    return jax.ShapeDtypeStruct(shape, kind)


def params_for(mib):
    return pltpu.CompilerParams(vmem_limit_bytes=mib * MIB)


def head_forward(tokens, routes_t, segments, wall, gain):
    count = tokens.shape[0]
    steps = count // TB
    across = lambda rows: pl.BlockSpec((rows, TB), lambda b: (0, b))
    down = lambda columns: pl.BlockSpec((TB, columns), lambda b: (b, 0))
    return pl.pallas_call(
        functools.partial(head_forward_kernel, steps),
        grid=(steps,),
        in_specs=[SMEM, down(D), across(TOPK), whole(segments.shape), whole((ALLW, D)), whole((1, D))],
        out_specs=[
            across(TOPK * H), across(TOPK * H), across(TOPK), across(TOPK), down(2 * H), across(2 * H),
            across(1), across(TOPK), whole((1, 128)),
        ],
        scratch_shapes=[
            pltpu.VMEM((ALLW, TB), F32),
            pltpu.VMEM((QW, TB), BF16),
            pltpu.VMEM((LEN, H), BF16),
            pltpu.VMEM((H, LEN), BF16),
            pltpu.VMEM((E, TB), F32),
        ],
        out_shape=[
            struct((TOPK * H, count), BF16),
            struct((TOPK * H, count)),
            struct((TOPK, count)),
            struct((TOPK, count)),
            struct((count, 2 * H), BF16),
            struct((2 * H, count), BF16),
            struct((1, count), jnp.int32),
            struct((TOPK, count), jnp.int32),
            struct((1, 128)),
        ],
        compiler_params=params_for(56),
        name="head_forward",
        cost_estimate=pl.CostEstimate(flops=10_000_000_000, bytes_accessed=16_000_000, transcendentals=0),
    )(segments, tokens, routes_t, segments, wall, gain)


def middle(tokens, grad_out, gain, wo, w1, w2, routes_t, gates, attended):
    count = tokens.shape[0]
    steps = count // MB
    across = lambda rows: pl.BlockSpec((rows, MB), lambda b: (0, b))
    down = lambda columns: pl.BlockSpec((MB, columns), lambda b: (b, 0))
    return pl.pallas_call(
        middle_kernel,
        grid=(steps,),
        in_specs=[
            down(D), down(D), whole((1, D)), whole((QW, D)), whole((D, FF)), whole((FF, D)),
            across(TOPK), across(TOPK), across(TOPK * H),
        ],
        out_specs=[
            down(D), down(D), across(TOPK * H), across(TOPK), across(E), whole((1, D)),
            across(QW), down(D), across(D), down(FF), across(D), down(FF),
        ],
        out_shape=[
            struct((count, D), BF16),
            struct((count, D)),
            struct((TOPK * H, count), BF16),
            struct((TOPK, count)),
            struct((E, count)),
            struct((1, D)),
            struct((QW, count), BF16),
            struct((count, D), BF16),
            struct((D, count), BF16),
            struct((count, FF), BF16),
            struct((D, count), BF16),
            struct((count, FF), BF16),
        ],
        scratch_shapes=[
            pltpu.VMEM((TOPK * H, MB), BF16),
            pltpu.VMEM((QW, MB), BF16),
        ],
        compiler_params=params_for(60),
        name="middle",
    )(tokens, grad_out, gain, wo, w1, w2, routes_t, gates, attended)


def head_backward(
    segments, tokens, gain, wall, routes_t, start, queries, datt, lse, delta, kv, kvt, dlogits, dres
):
    count = tokens.shape[0]
    steps = count // TB

    def place(b):
        return (b // NB) * NB + NB - 1 - b % NB

    across = lambda rows: pl.BlockSpec((rows, TB), lambda b: (0, place(b)))
    down = lambda columns: pl.BlockSpec((TB, columns), lambda b: (place(b), 0))
    return pl.pallas_call(
        head_backward_kernel,
        grid=(steps,),
        in_specs=[
            SMEM, down(D), whole((1, D)), whole((ALLW, D)), across(TOPK), across(1),
            across(TOPK * H), across(TOPK * H), across(TOPK), across(TOPK),
            pl.BlockSpec((LEN, 2 * H), lambda b: (b // NB, 0)),
            pl.BlockSpec((2 * H, LEN), lambda b: (0, b // NB)),
            across(E), down(D),
        ],
        out_specs=[down(D), whole((1, D)), across(QW), across(ALLW - QW), down(D)],
        scratch_shapes=[
            pltpu.VMEM((LEN, H), F32),
            pltpu.VMEM((LEN, H), F32),
            pltpu.VMEM((TOPK * H, TB), BF16),
            pltpu.VMEM((MOST * QB, TOPK * QB), BF16),
            pltpu.VMEM((MOST * QB, TOPK * QB), BF16),
        ],
        out_shape=[
            struct((count, D)),
            struct((1, D)),
            struct((QW, count), BF16),
            struct((ALLW - QW, count), BF16),
            struct((count, D), BF16),
        ],
        compiler_params=params_for(56),
        name="head_backward",
    )(segments, tokens, gain, wall, routes_t, start, queries, datt, lse, delta, kv, kvt, dlogits, dres)


def weight_grads(flat_rows, dgain_one, dgain_two, drest, dquery, normed, mix, branch, second_t, dpre, dy_t, hidden):
    count = normed.shape[0]
    hbm = pl.BlockSpec(memory_space=pl.ANY)
    rows_from = lambda first, last: pl.BlockSpec((512, count), lambda b: (jnp.clip(b - first, 0, last), 0))
    columns_from = lambda first, last: pl.BlockSpec((count, 512), lambda b: (0, jnp.clip(b - first, 0, last)))
    return pl.pallas_call(
        weight_grad_kernel,
        grid=(15,),
        in_specs=[
            whole((1, D)), whole((1, D)), whole(drest.shape), rows_from(1, 2), whole(normed.shape),
            rows_from(4, 2), hbm, hbm, columns_from(7, 3), hbm, columns_from(11, 3),
        ],
        out_specs=hbm,
        out_shape=struct((flat_rows, 128), BF16),
        scratch_shapes=[
            pltpu.VMEM(branch.shape, BF16),
            pltpu.VMEM(second_t.shape, BF16),
            pltpu.VMEM(dy_t.shape, BF16),
            pltpu.VMEM((flat_rows, 128), F32),
            pltpu.VMEM((flat_rows, 128), BF16),
            pltpu.SemaphoreType.DMA((3,)),
            pltpu.SemaphoreType.DMA((4,)),
        ],
        compiler_params=params_for(60),
        name="weight_grads",
    )(dgain_one, dgain_two, drest, dquery, normed, mix, branch, second_t, dpre, dy_t, hidden)


class Mesh3:
    def __init__(self, shards, over):
        shard = lax.axis_index("dp")
        other = lax.axis_index("fsdp")
        self.over = over
        self.many = shards * over
        self.sizes = {"x": 2, "y": shards // 2, "z": over // 2}
        self.here = {"x": lax.rem(other, 2), "y": lax.div(shard, 2), "z": lax.div(other, 2)}
        self.core = lax.rem(shard, 2)
        self.me = shard * over + other
        self.partner = (shard + 1 - 2 * self.core, other)

    def at_z(self, z):
        same = copy.copy(self)
        if z is not None:
            same.here = dict(self.here, z=z)
        return same

    def spots(self):
        x, y, z = (self.sizes[axis] for axis in "xyz")
        return list(itertools.product(range(x), range(y), range(1 - z, z)))

    def round_spots(self):
        return list(itertools.product(*[range(self.sizes[axis]) for axis in "xyz"]))

    def exists(self, z_steps):
        place = self.here["z"] + z_steps
        if isinstance(place, int):
            return 0 <= place < self.sizes["z"]
        return (place >= 0) & (place < self.sizes["z"])

    def device(self, core, spot):
        size = self.sizes["z"]
        x = lax.rem(self.here["x"] + spot[0], self.sizes["x"])
        y = lax.rem(self.here["y"] + spot[1], self.sizes["y"])
        z = self.here["z"] + spot[2]
        z = z % size if isinstance(z, int) else lax.rem(z + size, size)
        return (y * 2 + core, z * 2 + x)

    def number(self, core, spot):
        shard, other = self.device(core, spot)
        return shard * self.over + other

    def greet(self, devices):
        barrier = pltpu.get_barrier_semaphore()
        for device in devices:
            pl.semaphore_signal(barrier, inc=1, device_id=device, device_id_type=MESH)
        pl.semaphore_wait(barrier, len(devices))

    def near(self):
        steps = [at(axis, step) for axis in "xyz" for step in range(1, self.sizes[axis])]
        return [self.device(self.core, step) for step in steps] + [self.partner]

    def column(self):
        steps = [(core, step) for core in range(2) for step in range(self.sizes["z"]) if core or step]
        return [self.device(lax.rem(self.core + core, 2), (0, 0, step)) for core, step in steps]

    def layer(self):
        steps = [(x, y, 0) for x in range(self.sizes["x"]) for y in range(self.sizes["y"]) if x or y]
        return [self.device(self.core, step) for step in steps]


def at(axis, step):
    return tuple(step if one == axis else 0 for one in "xyz")


def last_axis(axes, spot):
    return max([i for i, axis in enumerate(axes) if spot["xyz".index(axis)]], default=-1)


def pieces_of(window):
    if window < 512:
        return [(0, window)]
    first = (window // 16 + 1) // 2 * 16
    return [(0, first), (first, window - first)]


def act(condition, action):
    if condition is True:
        action()
    elif condition is not False:
        pl.when(condition)(action)


GATHER_AXES = (("zxy", "yzx"), ("zyx", "xzy"))
REDUCE_AXES = ("zxy", "zyx")


def gather_own_core(mesh, core, land, send_sem, recv_sem, begin):
    window = land.shape[1]
    pieces = pieces_of(window)
    slots = {}
    events = []

    def moved(owner, device, slot, p):
        rows = pl.ds(*pieces[p])
        return pltpu.make_async_remote_copy(
            src_ref=land.at[owner, rows],
            dst_ref=land.at[owner, rows],
            send_sem=send_sem.at[slot, p],
            recv_sem=recv_sem.at[owner, p],
            device_id=device,
            device_id_type=MESH,
        )

    def onward(axes, spot):
        last = last_axis(axes, spot)
        steps = []
        if last >= 0 and axes[last] == "z":
            steps.append(("z", -1 if spot[2] > 0 else 1))
        for axis in axes[last + 1 :]:
            steps += [("z", 1), ("z", -1)] if axis == "z" else [
                (axis, one) for one in range(1, mesh.sizes[axis])
            ]
        return steps

    for spot in mesh.spots():
        there = mesh.exists(spot[2])
        if there is False:
            continue
        owner = mesh.number(core, spot)
        turn = 0.5 * abs(spot[2]) + (spot[0] > 0) + (spot[1] > 0) + (0.001 if spot[2] < 0 else 0)
        for p in range(len(pieces)):
            sends = []
            for axis, step in onward(GATHER_AXES[core][p], spot):
                key = (spot[0], spot[1], spot[2] % mesh.sizes["z"], axis, step)
                away = mesh.exists(step) if axis == "z" else True
                if away is not False:
                    slot = slots.setdefault(key, len(slots))
                    sends.append((mesh.device(core, at(axis, step)), slot, away))
            key = (spot[0], spot[1], spot[2] % mesh.sizes["z"])
            sends.append((mesh.partner, slots.setdefault(key, len(slots)), True))

            def come(owner=owner, spot=spot, p=p, sends=sends):
                if any(spot):
                    moved(owner, mesh.partner, 0, p).wait_recv()
                for device, slot, away in sends:
                    act(away, moved(owner, device, slot, p).start)

            def done(owner=owner, p=p, sends=sends):
                for _, slot, away in sends:
                    act(away, moved(owner, mesh.partner, slot, p).wait_send)

            events.append((turn + 0.01 * p, there, come if begin else done))
    for _, there, action in sorted(events, key=lambda one: one[0]):
        act(there, action)


def gather_blocks(mesh, land, send_sem, recv_sem, begin):
    known = range(mesh.sizes["z"]) if mesh.sizes["z"] <= 4 else [None]
    for core in range(2):
        for z in known:

            @pl.when((mesh.core == core) & (True if z is None else mesh.here["z"] == z))
            def _(core=core, z=z):
                gather_own_core(mesh.at_z(z), core, land, send_sem, recv_sem, begin)


def each_owner(mesh, core, action):
    def one(number, carry):
        shard = 2 * lax.div(number, mesh.over) + core
        action(shard * mesh.over + lax.rem(number, mesh.over))
        return carry

    lax.fori_loop(0, mesh.many // 2, one, 0)


def reduce_blocks(mesh, core, source, mine, outgo, income, send_sem, recv_sem, total_ref):
    pieces = pieces_of(outgo.shape[1])
    half = mesh.many // 2
    held = {spot: i for i, spot in enumerate(mesh.round_spots())}

    def across(kind, spot):
        slot = held[spot]
        return pltpu.make_async_remote_copy(
            src_ref=source(mesh.number(kind, spot)),
            dst_ref=income.at[slot],
            send_sem=send_sem.at[slot, 0],
            recv_sem=recv_sem.at[slot, 0],
            device_id=mesh.partner,
            device_id_type=MESH,
        )

    def moved(spot, p, device):
        rows = pl.ds(*pieces[p])
        slot = half + held[spot]
        return pltpu.make_async_remote_copy(
            src_ref=outgo.at[held[spot], rows],
            dst_ref=income.at[slot, rows],
            send_sem=send_sem.at[slot, p],
            recv_sem=recv_sem.at[slot, p],
            device_id=device,
            device_id_type=MESH,
        )

    def far(spot):
        z = {0: 0, 1: 3, 2: 5, 3: 8}.get(spot[2], 2 * spot[2] + 2)
        return z + 2 * (spot[0] > 0) + 2 * (spot[1] > 0)

    for spot in sorted(held, key=far, reverse=True):
        across(1 - core, spot).start()
    axes = REDUCE_AXES[core]
    order = sorted(itertools.product(held, range(len(pieces))), key=lambda one: one[1] - 2 * far(one[0]))
    for spot, p in order:
        if p == 0:
            across(core, spot).wait_recv()
        rows = pl.ds(*pieces[p])
        total = mine(mesh.number(core, spot), *pieces[p]) + income[held[spot], rows].astype(F32)
        last = last_axis(axes, spot)
        for axis in axes[last + 1 :]:
            size = mesh.sizes[axis]
            for step in range(1, size):
                child = tuple(one or other for one, other in zip(spot, at(axis, size - step)))
                moved(child, p, mesh.partner).wait_recv()
                total = total + income[half + held[child], rows].astype(F32)
        if last < 0:
            total_ref[rows, :] = total
        else:
            outgo[held[spot], rows] = total.astype(BF16)
            step = spot["xyz".index(axes[last])]
            moved(spot, p, mesh.device(core, at(axes[last], step))).start()
    for spot, p in order:
        if p == 0:
            across(1 - core, spot).wait_send()
        if any(spot):
            moved(spot, p, mesh.partner).wait_send()


def sum_all(mesh, mine, stats, send_sem, recv_sem):
    column = mesh.sizes["z"] * 2
    layer = mesh.sizes["x"] * mesh.sizes["y"]
    groups = (
        (0, column, mesh.here["z"] * 2 + mesh.core, mesh.column()),
        (column, layer, mesh.here["x"] * mesh.sizes["y"] + mesh.here["y"], mesh.layer()),
    )
    total = mine
    for base, size, here, devices in groups:
        stats[base + here] = total

        def sent(j, device, base=base, here=here):
            return pltpu.make_async_remote_copy(
                src_ref=stats.at[base + here],
                dst_ref=stats.at[base + here],
                send_sem=send_sem.at[base + j],
                recv_sem=recv_sem.at[base + here],
                device_id=device,
                device_id_type=MESH,
            )

        def come(place, base=base):
            return pltpu.make_async_remote_copy(
                src_ref=stats.at[base + place],
                dst_ref=stats.at[base + place],
                send_sem=send_sem.at[base],
                recv_sem=recv_sem.at[base + place],
                device_id=mesh.partner,
                device_id_type=MESH,
            )

        for j, device in enumerate(devices):
            sent(j, device).start()
        for j in range(1, size):
            come(lax.rem(here + j, size)).wait_recv()
        for j, device in enumerate(devices):
            sent(j, device).wait_send()
        total = stats[base]
        for place in range(1, size):
            total = total + stats[base + place]
    return total


def window_rows(shard_size, many):
    units = [(shard_size * d) // UNIT for d in range(many + 1)]
    return 16 * (max(b - a for a, b in zip(units, units[1:])) + 1)


def first_row(shard_size, number):
    if isinstance(number, int):
        return number * shard_size // UNIT * 16
    return pl.multiple_of(lax.div(number * shard_size, UNIT) * 16, 16)


def inner_units(shard_size, many):
    units = [(shard_size * d) // UNIT for d in range(many + 1)]
    return min(b - a for a, b in zip(units, units[1:]))


def lay_inner(shard_size, many, land, flat, owner):
    count = 16 * inner_units(shard_size, many) - 16
    row = pl.multiple_of(first_row(shard_size, owner) + 16, 16)
    flat[pl.ds(row, count), :] = land[owner, pl.ds(16, count), :].astype(F32)


def lay_edges(shard_size, many, land, flat):
    inner = 16 * inner_units(shard_size, many)
    flat[0:16, :] = jnp.zeros((16, 128), F32)

    def lay(number, carry):
        row = first_row(shard_size, number)
        after = first_row(shard_size, number + 1)
        flat[pl.ds(row, 16), :] += land[number, 0:16, :].astype(F32)
        tail = land[number, pl.ds(inner, 16), :].astype(F32)
        flat[pl.ds(pl.multiple_of(row + inner, 16), 16), :] = tail
        last = pl.multiple_of(after - row, 16)
        flat[pl.ds(after, 16), :] = land[number, pl.ds(last, 16), :].astype(F32)
        return carry

    lax.fori_loop(0, many, lay, 0)


def early_matrices(flat, wall_ref, gain_one_ref, gain_two_ref):
    for c in range(D // 128):
        lanes = slice(c * 128, (c + 1) * 128)
        gain_one_ref[:, lanes] = flat[c : c + 1, :]
        gain_two_ref[:, lanes] = flat[4 + c : 5 + c, :]
    for c in range(QW // 128):
        wall_ref[c * 128 : (c + 1) * 128, :] = flat[pl.ds(WQ_ROW + c, D, stride=12), :].T.astype(BF16)
    for first, row in ((KROW, WK_ROW), (VROW, WV_ROW)):
        pair = flat[row : row + 256, :].T.astype(BF16)
        wall_ref[first : first + H, :] = (
            nn(pair[:H], picks(256, 2, 0).astype(BF16)) + nn(pair[H:], picks(256, 2, 1).astype(BF16))
        ).astype(BF16)
    across = jnp.concatenate(
        [flat[pl.ds(WR_ROW + j, 32, stride=3), :] for j in range(3)], axis=1
    ).T.astype(BF16)
    router_t = jnp.zeros((E, D), F32)
    for part in range(16):
        router_t = router_t + nn(across[part * E : (part + 1) * E, :], picks(32, 16, part).astype(BF16))
    wall_ref[RROW:ALLW, :] = jnp.concatenate(
        [router_t, jnp.zeros((ALLW - RROW - E, D), F32)], axis=0
    ).astype(BF16)


def gather_kernel(
    mesh, shard_size, own_ref,
    wall_out, gain_one_ref, gain_two_ref, wo_out, w1_out, w2_out,
    land, flat, wall_ref, wo_ref, w1_ref, w2_ref, send_sem, recv_sem, out_sem,
):
    mesh = mesh()
    many = mesh.many
    mesh.greet(mesh.near())
    land[mesh.me] = own_ref[...]
    gather_blocks(mesh, land, send_sem, recv_sem, True)
    each_owner(mesh, mesh.core, functools.partial(lay_inner, shard_size, many, land, flat))

    def arrive(owner):
        for p in range(recv_sem.shape[1]):
            rows = pl.ds(*pieces_of(own_ref.shape[0])[p])
            pltpu.make_async_remote_copy(
                src_ref=land.at[owner, rows],
                dst_ref=land.at[owner, rows],
                send_sem=send_sem.at[0, p],
                recv_sem=recv_sem.at[owner, p],
                device_id=mesh.partner,
                device_id_type=MESH,
            ).wait_recv()
        lay_inner(shard_size, many, land, flat, owner)

    each_owner(mesh, 1 - mesh.core, arrive)
    lay_edges(shard_size, many, land, flat)
    copies = []

    def leave(matrix, out):
        one = pltpu.make_async_copy(matrix, out, out_sem.at[len(copies)])
        one.start()
        copies.append(one)

    for c in range(D // 128):
        wo_ref[:, c * 128 : (c + 1) * 128] = flat[pl.ds(WO_ROW + c, QW, stride=4), :].astype(BF16)
    leave(wo_ref, wo_out)
    for c in range(D // 128):
        w2_ref[:, c * 128 : (c + 1) * 128] = flat[pl.ds(W2_ROW + c, FF, stride=4), :].astype(BF16)
    leave(w2_ref, w2_out)
    for c in range(FF // 128):
        w1_ref[:, c * 128 : (c + 1) * 128] = flat[pl.ds(W1_ROW + c, D, stride=16), :].astype(BF16)
    leave(w1_ref, w1_out)
    early_matrices(flat, wall_ref, gain_one_ref, gain_two_ref)
    leave(wall_ref, wall_out)
    gather_blocks(mesh, land, send_sem, recv_sem, False)
    for one in copies:
        one.wait()


def gather_weights(shards, over, shard_size, own):
    window = own.shape[0]
    many = shards * over
    rows = (shard_size * (many - 1)) // UNIT * 16 + window
    vmem = pl.BlockSpec(memory_space=pltpu.VMEM)
    hbm = pl.BlockSpec(memory_space=pl.ANY)
    mesh = functools.partial(Mesh3, shards, over)
    pieces = len(pieces_of(window))
    return pl.pallas_call(
        functools.partial(gather_kernel, mesh, shard_size),
        in_specs=[vmem],
        out_specs=[hbm, vmem, vmem, hbm, hbm, hbm],
        out_shape=[
            struct((ALLW, D), BF16),
            struct((1, D)),
            struct((1, D)),
            struct((QW, D), BF16),
            struct((D, FF), BF16),
            struct((FF, D), BF16),
        ],
        scratch_shapes=[
            pltpu.VMEM((many, window, 128), BF16),
            pltpu.VMEM((rows, 128), F32),
            pltpu.VMEM((ALLW, D), BF16),
            pltpu.VMEM((QW, D), BF16),
            pltpu.VMEM((D, FF), BF16),
            pltpu.VMEM((FF, D), BF16),
            pltpu.SemaphoreType.DMA((5 * many // 2, pieces)),
            pltpu.SemaphoreType.DMA((many, pieces)),
            pltpu.SemaphoreType.DMA((4,)),
        ],
        compiler_params=pltpu.CompilerParams(
            collective_id=0, has_side_effects=True, vmem_limit_bytes=60 * MIB
        ),
        name="gather_weights",
    )(own)


def reduce_kernel(
    mesh, shard_size, flat_ref, count_ref,
    out_ref, total_ref, gain_ref,
    part, outgo, income, stats, part_sem, send_sem, recv_sem, stat_send, stat_recv,
):
    mesh = mesh()
    window = out_ref.shape[0]
    span = part.shape[1]

    def source(owner):
        return flat_ref.at[pl.ds(first_row(shard_size, owner), window), :]

    def fetch(y):
        first = first_row(shard_size, (2 * y + mesh.core) * mesh.over)
        return pltpu.make_async_copy(flat_ref.at[pl.ds(first, span), :], part.at[y], part_sem.at[y])

    def mine(owner, first, rows):
        shard = lax.div(owner, mesh.over)
        row = first_row(shard_size, owner) - first_row(shard_size, shard * mesh.over) + first
        return part[lax.div(shard, 2), pl.ds(pl.multiple_of(row, 16), rows), :].astype(F32)

    for y in range(mesh.sizes["y"]):
        fetch(y).start()
    mesh.greet(mesh.column() + mesh.layer())
    for y in range(mesh.sizes["y"]):
        fetch(y).wait()
    for core in range(2):

        @pl.when(mesh.core == core)
        def _(core=core):
            reduce_blocks(mesh, core, source, mine, outgo, income, send_sem, recv_sem, out_ref)

    total = out_ref[...]
    begin = mesh.me * shard_size - lax.div(mesh.me * shard_size, UNIT) * UNIT
    place = (
        lax.broadcasted_iota(jnp.int32, (window, 128), 0) * 128
        + lax.broadcasted_iota(jnp.int32, (window, 128), 1)
    )
    inside = jnp.where((place >= begin) & (place < begin + shard_size), total, 0.0)
    squares = jnp.sum(jnp.sum(inside * inside, axis=0, keepdims=True), axis=1, keepdims=True)
    lane = lax.broadcasted_iota(jnp.int32, (8, 128), 1)
    row = jnp.where(lane == E, squares, count_ref[...])
    gains = jnp.where(mesh.me == 0, total[0:8, :], 0.0)
    summed = sum_all(mesh, jnp.concatenate([row, gains], axis=0), stats, stat_send, stat_recv)
    total_ref[...] = summed[0:1, :]
    gain_ref[...] = summed[8:16, :]


def reduce_grads(shards, over, shard_size, window, flat, counts):
    vmem = pl.BlockSpec(memory_space=pltpu.VMEM)
    many = shards * over
    mesh = functools.partial(Mesh3, shards, over)
    pieces = len(pieces_of(window))
    steps = over + shards
    units = [(shard_size * d) // UNIT for d in range(many)]
    span = 16 * max(units[d + over - 1] - units[d] for d in range(0, many, over)) + window
    return pl.pallas_call(
        functools.partial(reduce_kernel, mesh, shard_size),
        in_specs=[pl.BlockSpec(memory_space=pl.ANY), vmem],
        out_specs=[vmem] * 3,
        out_shape=[struct((window, 128)), struct((1, 128)), struct((8, 128))],
        scratch_shapes=[
            pltpu.VMEM((shards // 2, span, 128), BF16),
            pltpu.VMEM((many // 2, window, 128), BF16),
            pltpu.VMEM((many, window, 128), BF16),
            pltpu.VMEM((steps, 16, 128), F32),
            pltpu.SemaphoreType.DMA((shards // 2,)),
            pltpu.SemaphoreType.DMA((many, pieces)),
            pltpu.SemaphoreType.DMA((many, pieces)),
            pltpu.SemaphoreType.DMA((steps,)),
            pltpu.SemaphoreType.DMA((steps,)),
        ],
        compiler_params=pltpu.CompilerParams(
            collective_id=1, has_side_effects=True, vmem_limit_bytes=56 * MIB
        ),
        name="reduce_grads",
    )(flat, counts)


def local_step(flat_rows, tokens, grad_out, routes, segments, weights):
    wall, gain_one, gain_two, wo, w1, w2 = weights
    queries, attended, gates, lse, kv, kvt, start, routes_t, counts = head_forward(
        tokens, routes.T, segments, wall, gain_one
    )
    (
        output, dres, datt, delta, dlogits, dgain_two, mix, branch, second_t, dpre, dy_t, hidden
    ) = middle(tokens, grad_out, gain_two, wo, w1, w2, routes_t, gates, attended)
    input_grad, dgain_one, dquery, drest, normed = head_backward(
        segments, tokens, gain_one, wall, routes_t, start, queries, datt, lse, delta, kv, kvt, dlogits, dres
    )
    flat = weight_grads(
        flat_rows, dgain_one, dgain_two, drest, dquery, normed, mix, branch, second_t, dpre, dy_t, hidden
    )
    return output, input_grad, flat, counts


def per_device(
    shards, over, tokens, grad_out, routes, segments, params, first_moment, second_moment, ema_weights
):
    shard_size = params.shape[0]
    window = window_rows(shard_size, shards * over)
    flat_rows = (shard_size * (shards * over - 1)) // UNIT * 16 + window + 16
    me = lax.axis_index("dp") * over + lax.axis_index("fsdp")
    begin = lax.rem(me * shard_size, UNIT)
    own = lax.dynamic_slice(
        jnp.pad(params.astype(BF16), (UNIT, window * 128 - shard_size)), (UNIT - begin,), (window * 128,)
    ).reshape(window, 128)
    wall, gain_one, gain_two, wo, w1, w2 = gather_weights(shards, over, shard_size, own)
    output, input_grad, flat, counts = local_step(
        flat_rows, tokens, grad_out, routes, segments, (wall, gain_one, gain_two, wo, w1, w2)
    )
    reduced, sums, gain_grads = reduce_grads(shards, over, shard_size, window, flat, counts)
    grad_shard = lax.dynamic_slice(reduced.reshape(-1), (begin,), (shard_size,))
    total_tokens = tokens.shape[0] * shards * over
    expert_load = sums[0, :E] * (E / (total_tokens * TOPK))
    grad_norm = jnp.sqrt(sums[0, E])
    clipped = grad_shard * (CLIP_LIMIT / jnp.maximum(grad_norm, CLIP_LIMIT))
    new_first = BETA_FIRST * first_moment + (1.0 - BETA_FIRST) * clipped
    new_second = BETA_SECOND * second_moment + (1.0 - BETA_SECOND) * clipped * clipped
    first_hat = new_first / (1.0 - BETA_FIRST**STEP)
    second_hat = new_second / (1.0 - BETA_SECOND**STEP)
    new_params = params * (1.0 - LEARN_RATE * DECAY_RATE) - LEARN_RATE * first_hat / (
        jnp.sqrt(second_hat) + ADAM_EPS
    )
    new_ema = EMA_KEEP * ema_weights + (1.0 - EMA_KEEP) * new_params
    return (
        output,
        input_grad,
        expert_load,
        grad_norm.reshape(1),
        new_params,
        new_first,
        new_second,
        new_ema,
        gain_grads.reshape(2, D),
    )


def solution(mesh):
    row = P(("dp", "fsdp"), None)
    flat = P(("dp", "fsdp"))
    return jax.shard_map(
        functools.partial(per_device, mesh.shape["dp"], mesh.shape["fsdp"]),
        mesh=mesh,
        in_specs=(row, row, row, row, flat, flat, flat, flat),
        out_specs=(row, row, P(), P(), flat, flat, flat, flat, P()),
        check_vma=False,
    )
```

```python
import copy
import functools
import itertools

import jax
import jax.numpy as jnp
from jax import lax
from jax.experimental import pallas as pl
from jax.experimental.pallas import tpu as pltpu
from jax.sharding import PartitionSpec as P

D = 512
E = 24
TOPK = 8
H = 64
FF = 2048
STEP = 10

NORM_EPS = 1e-06
CLIP_LIMIT = 1.0
BETA_FIRST = 0.9
BETA_SECOND = 0.95
LEARN_RATE = 0.1
DECAY_RATE = 0.1
ADAM_EPS = 1e-08
EMA_KEEP = 0.9
NEG_LARGE = -1e30

QW = E * H
KROW = QW
VROW = QW + H
RROW = QW + 2 * H
ALLW = 1696
LEN = 1024
TB = 512
NB = LEN // TB
QB = 128
MOST = 512 // QB + 1
SORT_STEPS = (
    (0, 1), (2, 3), (4, 5), (6, 7), (0, 2), (1, 3), (4, 6), (5, 7), (1, 2), (5, 6),
    (0, 4), (1, 5), (2, 6), (3, 7), (2, 4), (3, 5), (1, 2), (3, 4), (5, 6),
)
FC = 512
MB = 512
MIB = 1 << 20

WR_ROW = 8
WK_ROW = 104
WV_ROW = 360
WQ_ROW = 616
WO_ROW = 6760
W1_ROW = 12904
W2_ROW = 21096
ALL_ROWS = 29288
UNIT = 16 * 128
MESH = pl.DeviceIdType.MESH

F32 = jnp.float32
BF16 = jnp.bfloat16


def nn(a, b):
    return lax.dot_general(a, b, (((1,), (0,)), ((), ())), preferred_element_type=F32)


def nt(a, b):
    return lax.dot_general(a, b, (((1,), (1,)), ((), ())), preferred_element_type=F32)


def tn(a, b):
    return lax.dot_general(a, b, (((0,), (0,)), ((), ())), preferred_element_type=F32)


def rms_scale(values):
    return lax.rsqrt(jnp.mean(values * values, axis=-1, keepdims=True) + NORM_EPS)


def slot_of(routes, k, rows):
    return jnp.broadcast_to(routes[k : k + 1, :], (rows, routes.shape[1]))


def expert_rows(routes, k):
    return jnp.broadcast_to(routes.astype(jnp.int16)[k : k + 1, :], (16, routes.shape[1]))


def pick_heads(routes, source_ref, k):
    tokens = routes.shape[1]
    route = expert_rows(routes, k)
    taken = source_ref[k * H : (k + 1) * H, :].reshape(H // 16, 16, tokens)
    for e in range(k + 1, k + E - TOPK + 1):
        piece = source_ref[e * H : (e + 1) * H, :].reshape(H // 16, 16, tokens)
        taken = jnp.where((route == jnp.int16(e))[None], piece, taken)
    return taken.reshape(H, tokens)


def place_heads(routes, source_ref, target_ref):
    tokens = routes.shape[1]
    rows = [expert_rows(routes, k) for k in range(TOPK)]
    for e in range(E):
        total = jnp.zeros((H // 16, 16, tokens), BF16)
        for k in range(max(0, e - (E - TOPK)), min(TOPK - 1, e) + 1):
            piece = source_ref[k * H : (k + 1) * H, :].reshape(H // 16, 16, tokens)
            total = jnp.where((rows[k] == jnp.int16(e))[None], piece, total)
        target_ref[e * H : (e + 1) * H, :] = total.reshape(H, tokens)


def sorted_rows(rows):
    rows = list(rows)
    for one, two in SORT_STEPS:
        rows[one], rows[two] = jnp.minimum(rows[one], rows[two]), jnp.maximum(rows[one], rows[two])
    return rows


def key_mask(first_key, first_query, rows, start_row):
    keys = lax.broadcasted_iota(jnp.int32, (rows, QB), 0) + first_key
    queries = lax.broadcasted_iota(jnp.int32, (rows, QB), 1) + first_query
    mask = (keys <= queries) & (keys >= start_row)
    return jnp.concatenate([mask, mask], axis=1)


def pair_of(ref, k, lanes):
    return jnp.concatenate(
        [ref[k * H : (k + 1) * H, lanes], ref[(k + 1) * H : (k + 2) * H, lanes]], axis=1
    )


def row_pair(ref, k, lanes):
    return jnp.concatenate([ref[k : k + 1, lanes], ref[k + 1 : k + 2, lanes]], axis=1)


def by_span(attend, row, place, segment_ref):
    def one(j, carry):
        block = place * (TB // QB) + j
        first = block * QB
        span = jnp.int32(1)
        for back in range(MOST - 1):
            last = first - back * QB - 1
            same = segment_ref[row, jnp.maximum(last, 0)] == segment_ref[row, first]
            span = span + jnp.where((last >= 0) & same, 1, 0)
        for blocks in range(1, MOST + 1):

            @pl.when(span == blocks)
            def _(blocks=blocks):
                attend(pl.ds(pl.multiple_of(j * QB, QB), QB), block, blocks)

        return carry

    lax.fori_loop(0, TB // QB, one, 0)


def head_forward_kernel(
    steps, segment_smem, x_ref, route_ref, segment_ref, wall_ref, gain_ref,
    q_ref, att_ref, gate_ref, lse_ref, kv_ref, kvt_ref, start_ref, sorted_ref, count_ref,
    all_scr, low_scr, k_scr, vt_scr, count_scr,
):
    step = pl.program_id(0)
    place = lax.rem(step, NB)
    here = pl.multiple_of(place * TB, TB)

    @pl.when(step == 0)
    def _():
        count_scr[...] = jnp.zeros_like(count_scr)

    row = segment_ref[pl.ds(lax.div(step, NB), 1), :]
    segments = segment_ref[pl.ds(lax.div(step, NB), 1), pl.ds(here, TB)]
    start = jnp.zeros((1, TB), jnp.int32)
    for number in range(1, 4):
        below = jnp.sum((row < number).astype(jnp.int32), axis=1, keepdims=True)
        start = jnp.where(segments == number, below, start)
    start_ref[...] = start
    x = x_ref[...].astype(F32)
    normed = (x * rms_scale(x) * gain_ref[...]).astype(BF16)
    all_scr[...] = nt(wall_ref[...], normed)
    kt = all_scr[KROW : KROW + H, :]
    vt = all_scr[VROW : VROW + H, :]
    logits = all_scr[RROW : RROW + E, :]
    kvt = jnp.concatenate([kt, vt], axis=0)
    kv = kvt.T.astype(BF16)
    kv_ref[...] = kv
    kvt_ref[...] = kvt.astype(BF16)
    k_scr[pl.ds(here, TB), :] = kv[:, :H]
    vt_scr[:, pl.ds(here, TB)] = vt.astype(BF16)
    routes = jnp.concatenate(sorted_rows(route_ref[k : k + 1, :] for k in range(TOPK)), axis=0)
    sorted_ref[...] = routes
    experts = lax.broadcasted_iota(jnp.int32, (E, TB), 0)
    chosen = []
    counts = count_scr[...]
    for k in range(TOPK):
        named = slot_of(routes, k, E) == experts
        chosen.append(jnp.sum(jnp.where(named, logits, 0.0), axis=0, keepdims=True))
        counts = counts + named.astype(F32)
    count_scr[...] = counts
    chosen = jnp.concatenate(chosen, axis=0)
    raised = jnp.exp(chosen - jnp.max(chosen, axis=0, keepdims=True))
    gate_ref[...] = raised / jnp.sum(raised, axis=0, keepdims=True)
    low_scr[...] = all_scr[0:QW, :].astype(BF16)
    for k in range(TOPK):
        q_ref[k * H : (k + 1) * H, :] = pick_heads(routes, low_scr, k) * jnp.asarray(H ** (-0.5), BF16)

    def attend(lanes, block, blocks):
        rows = blocks * QB
        first_key = pl.multiple_of((block - (blocks - 1)) * QB, QB)
        mask = key_mask(first_key, block * QB, rows, start_ref[:, lanes])
        keys = k_scr[pl.ds(first_key, rows), :]
        values = vt_scr[:, pl.ds(first_key, rows)]
        pairs = [nn(keys, pair_of(q_ref, 0, lanes))]
        for k in range(0, TOPK, 2):
            if k + 2 < TOPK:
                pairs.append(nn(keys, pair_of(q_ref, k + 2, lanes)))
            scores = jnp.where(mask, pairs[k // 2], NEG_LARGE)
            top = jnp.max(scores, axis=0, keepdims=True)
            raised = jnp.exp(scores - top)
            total = jnp.sum(raised, axis=0, keepdims=True)
            out = nn(values, (raised * (1.0 / total)).astype(BF16))
            lse = top + jnp.log(total)
            for side in range(2):
                one = slice(side * QB, (side + 1) * QB)
                att_ref[(k + side) * H : (k + side + 1) * H, lanes] = out[:, one]
                lse_ref[k + side : k + side + 1, lanes] = lse[:, one]

    by_span(attend, lax.div(step, NB), place, segment_smem)

    @pl.when(step == steps - 1)
    def _():
        held = jnp.sum(count_scr[...], axis=1, keepdims=True)
        lane = lax.broadcasted_iota(jnp.int32, (E, 128), 1)
        row = lax.broadcasted_iota(jnp.int32, (E, 128), 0)
        count_ref[...] = jnp.sum(jnp.where(lane == row, held, 0.0), axis=0, keepdims=True)


def picks(rows, stride, first):
    at = lax.broadcasted_iota(jnp.int32, (rows, D), 1)
    row = lax.broadcasted_iota(jnp.int32, (rows, D), 0)
    return (at == row * stride + first).astype(F32)


def exact(product, a, b):
    return lax.dot_general(
        a, b, (product, ((), ())), precision=lax.Precision.HIGHEST, preferred_element_type=F32
    )


def gelu_parts(v):
    cdf = 0.5 + 0.5 * lax.erf(v * 0.7071067811865476)
    return cdf, jnp.exp(v * v * -0.5) * 0.3989422804014327


def middle_kernel(
    x_ref, dy_ref, gain_ref, wo_ref, w1_ref, w2_ref, route_ref, gate_ref, att_ref,
    out_ref, dres_ref, datt_ref, delta_ref, dlogit_ref, flat_ref, extra_ref, dgain_ref,
    slot_scr, head_scr, mix_scr, dwo_ref, dw1_ref, dw2t_ref, rows_scr, low_scr, row_sem,
):
    step = pl.program_id(0)

    @pl.when(step == 0)
    def _():
        dwo_ref[...] = jnp.zeros_like(dwo_ref)
        dw1_ref[...] = jnp.zeros_like(dw1_ref)
        dw2t_ref[...] = jnp.zeros_like(dw2t_ref)
        dgain_ref[...] = jnp.zeros_like(dgain_ref)

    routes = route_ref[...]
    tokens = routes.shape[1]
    gates = gate_ref[...]
    for k in range(TOPK):
        rows = slice(k * H, (k + 1) * H)
        slot_scr[rows, :] = (gates[k : k + 1, :] * att_ref[rows, :]).astype(BF16)
    place_heads(routes, slot_scr, mix_scr)
    x = x_ref[...].astype(F32)
    dy = dy_ref[...]
    mixed = mix_scr[...]
    residual = x + tn(mixed, wo_ref[...])
    scale = rms_scale(residual)
    gain = gain_ref[...]
    second = (residual * scale * gain).astype(BF16)
    second_t = second.T
    dy_t = dy.T
    out = residual
    dsecond = jnp.zeros((tokens, D), F32)
    for c in range(0, FF, FC):
        up = w1_ref[:, c : c + FC]
        down = w2_ref[c : c + FC, :]
        pre = nn(second, up)
        cdf, density = gelu_parts(pre)
        hidden = (pre * cdf).astype(BF16)
        dpre = (nt(dy, down) * (cdf + pre * density)).astype(BF16)
        out = out + nn(hidden, down)
        dsecond = dsecond + nt(dpre, up)
        dw2t_ref[:, c : c + FC] += nn(dy_t, hidden)
        dw1_ref[:, c : c + FC] += nn(second_t, dpre)
    out_ref[...] = out.astype(BF16)
    dgain_ref[...] += jnp.sum(dsecond * residual * scale, axis=0, keepdims=True)
    weighted = gain * dsecond
    dres = (
        dy.astype(F32)
        + scale * weighted
        - residual * (scale * scale * scale) * jnp.mean(weighted * residual, axis=-1, keepdims=True)
    )
    dres_ref[...] = dres
    branch = dres.astype(BF16)
    dwo_ref[...] += nn(mixed, branch)
    head_scr[...] = nt(wo_ref[...], branch).astype(BF16)
    dgates = []
    for k in range(TOPK):
        rows = slice(k * H, (k + 1) * H)
        dslot = pick_heads(routes, head_scr, k).astype(F32)
        attended = att_ref[rows, :]
        dgates.append(jnp.sum(dslot * attended, axis=0, keepdims=True))
        datt = (gates[k : k + 1, :] * dslot).astype(BF16)
        datt_ref[rows, :] = datt
        delta_ref[k : k + 1, :] = jnp.sum(datt.astype(F32) * attended, axis=0, keepdims=True)
    dgate = jnp.concatenate(dgates, axis=0)
    dchosen = gates * (dgate - jnp.sum(gates * dgate, axis=0, keepdims=True))
    experts = lax.broadcasted_iota(jnp.int32, (E, tokens), 0)
    dlogits = jnp.zeros((E, tokens), F32)
    for k in range(TOPK):
        dlogits = jnp.where(
            slot_of(routes, k, E) == experts,
            jnp.broadcast_to(dchosen[k : k + 1, :], (E, tokens)),
            dlogits,
        )
    dlogit_ref[...] = dlogits

    @pl.when(step == pl.num_programs(0) - 1)
    def _():
        for c in range(D // 128):
            lanes = slice(c * 128, (c + 1) * 128)
            rows_scr[pl.ds(c, QW, stride=4), :] = dwo_ref[:, lanes]
            rows_scr[pl.ds(W2_ROW - WO_ROW + c, FF, stride=4), :] = dw2t_ref[lanes, :].T
        for c in range(FF // 128):
            rows_scr[pl.ds(W1_ROW - WO_ROW + c, D, stride=16), :] = dw1_ref[:, c * 128 : (c + 1) * 128]
        extra_ref[...] = rows_scr[0:8, :]
        low_scr[...] = rows_scr[8:, :].astype(BF16)
        copy = pltpu.make_async_copy(
            low_scr, flat_ref.at[pl.ds(WO_ROW + 8, low_scr.shape[0]), :], row_sem.at[0]
        )
        copy.start()
        copy.wait()


def head_backward_kernel(
    segment_smem, x_ref, gain_ref, wall_ref, route_ref, start_ref, q_ref, datt_ref,
    lse_ref, delta_ref, kv_ref, kvt_ref, dlogit_ref, dres_ref, dgain_two_ref, extra_ref, flat_in,
    dx_ref, flat_ref,
    dk_scr, dv_scr, dq_scr, dall_scr, prob_scr, dscore_scr, dwall_ref, dgain_ref, rows_scr, low_scr, row_sem,
):
    step = pl.program_id(0)
    place = NB - 1 - lax.rem(step, NB)
    here = pl.multiple_of(place * TB, TB)

    @pl.when(step == 0)
    def _():
        dwall_ref[...] = jnp.zeros_like(dwall_ref)
        dgain_ref[...] = jnp.zeros_like(dgain_ref)

    @pl.when(lax.rem(step, NB) == 0)
    def _():
        dk_scr[...] = jnp.zeros_like(dk_scr)
        dv_scr[...] = jnp.zeros_like(dv_scr)

    def attend(lanes, block, blocks):
        rows = blocks * QB
        first_key = pl.multiple_of((block - (blocks - 1)) * QB, QB)
        mask = key_mask(first_key, block * QB, rows, start_ref[:, lanes])
        keys = kv_ref[pl.ds(first_key, rows), :H]
        values = kv_ref[pl.ds(first_key, rows), H:]
        keys_t = kvt_ref[:H, pl.ds(first_key, rows)]
        queries = [pair_of(q_ref, k, lanes) for k in range(0, TOPK, 2)]
        datts = [pair_of(datt_ref, k, lanes) for k in range(0, TOPK, 2)]
        scores = [nn(keys, queries[0])]
        dprobs = [nn(values, datts[0])]
        for i in range(TOPK // 2):
            if i + 1 < TOPK // 2:
                scores.append(nn(keys, queries[i + 1]))
                dprobs.append(nn(values, datts[i + 1]))
            k = 2 * i
            wide = slice(i * 2 * QB, (i + 1) * 2 * QB)
            probs = jnp.exp(jnp.where(mask, scores[i], NEG_LARGE) - row_pair(lse_ref, k, lanes))
            dscore = (probs * (dprobs[i] - row_pair(delta_ref, k, lanes))).astype(BF16)
            prob_scr[0:rows, wide] = probs.astype(BF16)
            dscore_scr[0:rows, wide] = dscore
            dq = (nn(keys_t, dscore) * (H ** (-0.5))).astype(BF16)
            dq_scr[k * H : (k + 1) * H, lanes] = dq[:, :QB]
            dq_scr[(k + 1) * H : (k + 2) * H, lanes] = dq[:, QB:]
        dv_scr[pl.ds(first_key, rows), :] += nt(prob_scr[0:rows, :], jnp.concatenate(datts, axis=1))
        dk_scr[pl.ds(first_key, rows), :] += nt(dscore_scr[0:rows, :], jnp.concatenate(queries, axis=1))

    by_span(attend, lax.div(step, NB), place, segment_smem)
    place_heads(route_ref[...], dq_scr, dall_scr)
    dkv = jnp.concatenate([dk_scr[pl.ds(here, TB), :], dv_scr[pl.ds(here, TB), :]], axis=1)
    dall_scr[KROW : KROW + 2 * H, :] = dkv.T.astype(BF16)
    dall_scr[RROW : RROW + 32, :] = jnp.concatenate(
        [dlogit_ref[...], jnp.zeros((32 - E, TB), F32)], axis=0
    ).astype(BF16)
    x = x_ref[...].astype(F32)
    scale = rms_scale(x)
    gain = gain_ref[...]
    normed = (x * scale * gain).astype(BF16)
    dall = dall_scr[...]
    dwall_ref[...] += nn(dall, normed)
    dnormed = tn(dall, wall_ref[...])
    dgain_ref[...] += jnp.sum(dnormed * x * scale, axis=0, keepdims=True)
    weighted = gain * dnormed
    dx_ref[...] = (
        dres_ref[...]
        + scale * weighted
        - x * (scale * scale * scale) * jnp.mean(weighted * x, axis=-1, keepdims=True)
    )

    @pl.when(step == pl.num_programs(0) - 1)
    def _():
        for c in range(D // 128):
            lanes = slice(c * 128, (c + 1) * 128)
            rows_scr[c : c + 1, :] = dgain_ref[:, lanes]
            rows_scr[4 + c : 5 + c, :] = dgain_two_ref[:, lanes]
        router_t = dwall_ref[RROW : RROW + E, :]
        across = jnp.concatenate(
            [exact(((1,), (1,)), router_t, picks(32, 16, b)) for b in range(16)], axis=0
        ).T
        for j in range(3):
            rows_scr[pl.ds(WR_ROW + j, 32, stride=3), :] = across[:, j * 128 : (j + 1) * 128]
        for first, row in ((KROW, WK_ROW), (VROW, WV_ROW)):
            part = dwall_ref[first : first + H, :]
            rows_scr[row : row + 256, :] = jnp.concatenate(
                [exact(((1,), (1,)), picks(256, 2, b), part) for b in range(2)], axis=1
            )
        for c in range(QW // 128):
            rows_scr[pl.ds(WQ_ROW + c, D, stride=12), :] = dwall_ref[c * 128 : (c + 1) * 128, :].T
        rows_scr[WO_ROW : WO_ROW + 8, :] = extra_ref[...]
        low_scr[...] = rows_scr[...].astype(BF16)
        copy = pltpu.make_async_copy(low_scr, flat_ref.at[pl.ds(0, WO_ROW + 8), :], row_sem.at[0])
        copy.start()
        copy.wait()


def whole(shape):
    return pl.BlockSpec(shape, lambda *_: (0,) * len(shape), pipeline_mode=pl.Buffered(1))


def kept(shape):
    return pl.BlockSpec(shape, lambda *_: (0,) * len(shape))


SMEM = pl.BlockSpec(memory_space=pltpu.SMEM)


def struct(shape, kind=F32):
    return jax.ShapeDtypeStruct(shape, kind)


def params_for(mib):
    return pltpu.CompilerParams(vmem_limit_bytes=mib * MIB)


def head_forward(tokens, routes_t, segments, wall, gain):
    count = tokens.shape[0]
    steps = count // TB
    across = lambda rows: pl.BlockSpec((rows, TB), lambda b: (0, b))
    down = lambda columns: pl.BlockSpec((TB, columns), lambda b: (b, 0))
    return pl.pallas_call(
        functools.partial(head_forward_kernel, steps),
        grid=(steps,),
        in_specs=[SMEM, down(D), across(TOPK), whole(segments.shape), whole((ALLW, D)), whole((1, D))],
        out_specs=[
            across(TOPK * H), across(TOPK * H), across(TOPK), across(TOPK), down(2 * H), across(2 * H),
            across(1), across(TOPK), whole((1, 128)),
        ],
        scratch_shapes=[
            pltpu.VMEM((ALLW, TB), F32),
            pltpu.VMEM((QW, TB), BF16),
            pltpu.VMEM((LEN, H), BF16),
            pltpu.VMEM((H, LEN), BF16),
            pltpu.VMEM((E, TB), F32),
        ],
        out_shape=[
            struct((TOPK * H, count), BF16),
            struct((TOPK * H, count)),
            struct((TOPK, count)),
            struct((TOPK, count)),
            struct((count, 2 * H), BF16),
            struct((2 * H, count), BF16),
            struct((1, count), jnp.int32),
            struct((TOPK, count), jnp.int32),
            struct((1, 128)),
        ],
        compiler_params=params_for(56),
        name="head_forward",
        cost_estimate=pl.CostEstimate(flops=10_000_000_000, bytes_accessed=16_000_000, transcendentals=0),
    )(segments, tokens, routes_t, segments, wall, gain)


def middle(flat_rows, tokens, grad_out, gain, wo, w1, w2, routes_t, gates, attended):
    count = tokens.shape[0]
    steps = count // MB
    across = lambda rows: pl.BlockSpec((rows, MB), lambda b: (0, b))
    down = lambda columns: pl.BlockSpec((MB, columns), lambda b: (b, 0))
    return pl.pallas_call(
        middle_kernel,
        grid=(steps,),
        in_specs=[
            down(D), down(D), whole((1, D)), whole((QW, D)), whole((D, FF)), whole((FF, D)),
            across(TOPK), across(TOPK), across(TOPK * H),
        ],
        out_specs=[
            down(D), down(D), across(TOPK * H), across(TOPK), across(E),
            pl.BlockSpec(memory_space=pl.ANY), whole((8, 128)), whole((1, D)),
        ],
        out_shape=[
            struct((count, D), BF16),
            struct((count, D)),
            struct((TOPK * H, count), BF16),
            struct((TOPK, count)),
            struct((E, count)),
            struct((flat_rows, 128), BF16),
            struct((8, 128)),
            struct((1, D)),
        ],
        scratch_shapes=[
            pltpu.VMEM((TOPK * H, MB), BF16),
            pltpu.VMEM((QW, MB), BF16),
            pltpu.VMEM((QW, MB), BF16),
            pltpu.VMEM((QW, D), F32),
            pltpu.VMEM((D, FF), F32),
            pltpu.VMEM((D, FF), F32),
            pltpu.VMEM((flat_rows - WO_ROW, 128), F32),
            pltpu.VMEM((flat_rows - WO_ROW - 8, 128), BF16),
            pltpu.SemaphoreType.DMA((1,)),
        ],
        compiler_params=params_for(60),
        name="middle",
    )(tokens, grad_out, gain, wo, w1, w2, routes_t, gates, attended)


def head_backward(
    segments, tokens, gain, wall, routes_t, start, queries, datt, lse, delta, kv, kvt, dlogits, dres,
    dgain_two, extra, flat,
):
    count = tokens.shape[0]
    steps = count // TB

    def place(b):
        return (b // NB) * NB + NB - 1 - b % NB

    across = lambda rows: pl.BlockSpec((rows, TB), lambda b: (0, place(b)))
    down = lambda columns: pl.BlockSpec((TB, columns), lambda b: (place(b), 0))
    return pl.pallas_call(
        head_backward_kernel,
        grid=(steps,),
        in_specs=[
            SMEM, down(D), whole((1, D)), whole((ALLW, D)), across(TOPK), across(1),
            across(TOPK * H), across(TOPK * H), across(TOPK), across(TOPK),
            pl.BlockSpec((LEN, 2 * H), lambda b: (b // NB, 0)),
            pl.BlockSpec((2 * H, LEN), lambda b: (0, b // NB)),
            across(E), down(D), whole((1, D)), whole((8, 128)), pl.BlockSpec(memory_space=pl.ANY),
        ],
        out_specs=[down(D), pl.BlockSpec(memory_space=pl.ANY)],
        scratch_shapes=[
            pltpu.VMEM((LEN, H), F32),
            pltpu.VMEM((LEN, H), F32),
            pltpu.VMEM((TOPK * H, TB), BF16),
            pltpu.VMEM((ALLW, TB), BF16),
            pltpu.VMEM((MOST * QB, TOPK * QB), BF16),
            pltpu.VMEM((MOST * QB, TOPK * QB), BF16),
            pltpu.VMEM((ALLW, D), F32),
            pltpu.VMEM((1, D), F32),
            pltpu.VMEM((WO_ROW + 8, 128), F32),
            pltpu.VMEM((WO_ROW + 8, 128), BF16),
            pltpu.SemaphoreType.DMA((1,)),
        ],
        out_shape=[struct((count, D)), struct(flat.shape, BF16)],
        input_output_aliases={16: 1},
        compiler_params=params_for(56),
        name="head_backward",
        cost_estimate=pl.CostEstimate(flops=30_000_000_000, bytes_accessed=24_000_000, transcendentals=0),
    )(
        segments, tokens, gain, wall, routes_t, start, queries, datt, lse, delta, kv, kvt, dlogits, dres,
        dgain_two, extra, flat,
    )


class Mesh3:
    def __init__(self, shards, over):
        shard = lax.axis_index("dp")
        other = lax.axis_index("fsdp")
        self.over = over
        self.many = shards * over
        self.sizes = {"x": 2, "y": shards // 2, "z": over // 2}
        self.here = {"x": lax.rem(other, 2), "y": lax.div(shard, 2), "z": lax.div(other, 2)}
        self.core = lax.rem(shard, 2)
        self.me = shard * over + other
        self.partner = (shard + 1 - 2 * self.core, other)

    def at_z(self, z):
        same = copy.copy(self)
        if z is not None:
            same.here = dict(self.here, z=z)
        return same

    def spots(self):
        x, y, z = (self.sizes[axis] for axis in "xyz")
        return list(itertools.product(range(x), range(y), range(1 - z, z)))

    def round_spots(self):
        return list(itertools.product(*[range(self.sizes[axis]) for axis in "xyz"]))

    def exists(self, z_steps):
        place = self.here["z"] + z_steps
        if isinstance(place, int):
            return 0 <= place < self.sizes["z"]
        return (place >= 0) & (place < self.sizes["z"])

    def device(self, core, spot):
        size = self.sizes["z"]
        x = lax.rem(self.here["x"] + spot[0], self.sizes["x"])
        y = lax.rem(self.here["y"] + spot[1], self.sizes["y"])
        z = self.here["z"] + spot[2]
        z = z % size if isinstance(z, int) else lax.rem(z + size, size)
        return (y * 2 + core, z * 2 + x)

    def number(self, core, spot):
        shard, other = self.device(core, spot)
        return shard * self.over + other

    def greet(self, devices):
        barrier = pltpu.get_barrier_semaphore()
        for device in devices:
            pl.semaphore_signal(barrier, inc=1, device_id=device, device_id_type=MESH)
        pl.semaphore_wait(barrier, len(devices))

    def near(self):
        steps = [at(axis, step) for axis in "xyz" for step in range(1, self.sizes[axis])]
        return [self.device(self.core, step) for step in steps] + [self.partner]

    def column(self):
        steps = [(core, step) for core in range(2) for step in range(self.sizes["z"]) if core or step]
        return [self.device(lax.rem(self.core + core, 2), (0, 0, step)) for core, step in steps]

    def layer(self):
        steps = [(x, y, 0) for x in range(self.sizes["x"]) for y in range(self.sizes["y"]) if x or y]
        return [self.device(self.core, step) for step in steps]


def at(axis, step):
    return tuple(step if one == axis else 0 for one in "xyz")


def last_axis(axes, spot):
    return max([i for i, axis in enumerate(axes) if spot["xyz".index(axis)]], default=-1)


def pieces_of(window):
    if window < 512:
        return [(0, window)]
    first = (window // 16 + 1) // 2 * 16
    return [(0, first), (first, window - first)]


def act(condition, action):
    if condition is True:
        action()
    elif condition is not False:
        pl.when(condition)(action)


GATHER_AXES = (("zxy", "yzx"), ("zyx", "xzy"))
REDUCE_AXES = ("zxy", "zyx")


def gather_own_core(mesh, core, land, send_sem, recv_sem, begin):
    window = land.shape[1]
    pieces = pieces_of(window)
    slots = {}
    events = []

    def moved(owner, device, slot, p):
        rows = pl.ds(*pieces[p])
        return pltpu.make_async_remote_copy(
            src_ref=land.at[owner, rows],
            dst_ref=land.at[owner, rows],
            send_sem=send_sem.at[slot, p],
            recv_sem=recv_sem.at[owner, p],
            device_id=device,
            device_id_type=MESH,
        )

    def onward(axes, spot):
        last = last_axis(axes, spot)
        steps = []
        if last >= 0 and axes[last] == "z":
            steps.append(("z", -1 if spot[2] > 0 else 1))
        for axis in axes[last + 1 :]:
            steps += [("z", 1), ("z", -1)] if axis == "z" else [
                (axis, one) for one in range(1, mesh.sizes[axis])
            ]
        return steps

    for spot in mesh.spots():
        there = mesh.exists(spot[2])
        if there is False:
            continue
        owner = mesh.number(core, spot)
        turn = 0.5 * abs(spot[2]) + (spot[0] > 0) + (spot[1] > 0) + (0.001 if spot[2] < 0 else 0)
        for p in range(len(pieces)):
            sends = []
            for axis, step in onward(GATHER_AXES[core][p], spot):
                key = (spot[0], spot[1], spot[2] % mesh.sizes["z"], axis, step)
                away = mesh.exists(step) if axis == "z" else True
                if away is not False:
                    slot = slots.setdefault(key, len(slots))
                    sends.append((mesh.device(core, at(axis, step)), slot, away))
            key = (spot[0], spot[1], spot[2] % mesh.sizes["z"])
            sends.append((mesh.partner, slots.setdefault(key, len(slots)), True))

            def come(owner=owner, spot=spot, p=p, sends=sends):
                if any(spot):
                    moved(owner, mesh.partner, 0, p).wait_recv()
                for device, slot, away in sends:
                    act(away, moved(owner, device, slot, p).start)

            def done(owner=owner, p=p, sends=sends):
                for _, slot, away in sends:
                    act(away, moved(owner, mesh.partner, slot, p).wait_send)

            events.append((turn + 0.01 * p, there, come if begin else done))
    for _, there, action in sorted(events, key=lambda one: one[0]):
        act(there, action)


def gather_blocks(mesh, land, send_sem, recv_sem, begin):
    known = range(mesh.sizes["z"]) if mesh.sizes["z"] <= 4 else [None]
    for core in range(2):
        for z in known:

            @pl.when((mesh.core == core) & (True if z is None else mesh.here["z"] == z))
            def _(core=core, z=z):
                gather_own_core(mesh.at_z(z), core, land, send_sem, recv_sem, begin)


def each_owner(mesh, core, action):
    def one(number, carry):
        shard = 2 * lax.div(number, mesh.over) + core
        action(shard * mesh.over + lax.rem(number, mesh.over))
        return carry

    lax.fori_loop(0, mesh.many // 2, one, 0)


def reduce_blocks(mesh, core, source, mine, outgo, income, send_sem, recv_sem, total_ref):
    pieces = pieces_of(outgo.shape[1])
    half = mesh.many // 2
    held = {spot: i for i, spot in enumerate(mesh.round_spots())}

    def across(kind, spot):
        slot = held[spot]
        return pltpu.make_async_remote_copy(
            src_ref=source(mesh.number(kind, spot)),
            dst_ref=income.at[slot],
            send_sem=send_sem.at[slot, 0],
            recv_sem=recv_sem.at[slot, 0],
            device_id=mesh.partner,
            device_id_type=MESH,
        )

    def moved(spot, p, device):
        rows = pl.ds(*pieces[p])
        slot = half + held[spot]
        return pltpu.make_async_remote_copy(
            src_ref=outgo.at[held[spot], rows],
            dst_ref=income.at[slot, rows],
            send_sem=send_sem.at[slot, p],
            recv_sem=recv_sem.at[slot, p],
            device_id=device,
            device_id_type=MESH,
        )

    def far(spot):
        z = {0: 0, 1: 3, 2: 5, 3: 8}.get(spot[2], 2 * spot[2] + 2)
        return z + 2 * (spot[0] > 0) + 2 * (spot[1] > 0)

    for spot in sorted(held, key=far, reverse=True):
        across(1 - core, spot).start()
    axes = REDUCE_AXES[core]
    order = sorted(itertools.product(held, range(len(pieces))), key=lambda one: one[1] - 2 * far(one[0]))
    for spot, p in order:
        if p == 0:
            across(core, spot).wait_recv()
        rows = pl.ds(*pieces[p])
        total = mine(mesh.number(core, spot), *pieces[p]) + income[held[spot], rows].astype(F32)
        last = last_axis(axes, spot)
        for axis in axes[last + 1 :]:
            size = mesh.sizes[axis]
            for step in range(1, size):
                child = tuple(one or other for one, other in zip(spot, at(axis, size - step)))
                moved(child, p, mesh.partner).wait_recv()
                total = total + income[half + held[child], rows].astype(F32)
        if last < 0:
            total_ref[rows, :] = total
        else:
            outgo[held[spot], rows] = total.astype(BF16)
            step = spot["xyz".index(axes[last])]
            moved(spot, p, mesh.device(core, at(axes[last], step))).start()
    for spot, p in order:
        if p == 0:
            across(1 - core, spot).wait_send()
        if any(spot):
            moved(spot, p, mesh.partner).wait_send()


def sum_all(mesh, mine, stats, send_sem, recv_sem):
    column = mesh.sizes["z"] * 2
    layer = mesh.sizes["x"] * mesh.sizes["y"]
    groups = (
        (0, column, mesh.here["z"] * 2 + mesh.core, mesh.column()),
        (column, layer, mesh.here["x"] * mesh.sizes["y"] + mesh.here["y"], mesh.layer()),
    )
    total = mine
    for base, size, here, devices in groups:
        stats[base + here] = total

        def sent(j, device, base=base, here=here):
            return pltpu.make_async_remote_copy(
                src_ref=stats.at[base + here],
                dst_ref=stats.at[base + here],
                send_sem=send_sem.at[base + j],
                recv_sem=recv_sem.at[base + here],
                device_id=device,
                device_id_type=MESH,
            )

        def come(place, base=base):
            return pltpu.make_async_remote_copy(
                src_ref=stats.at[base + place],
                dst_ref=stats.at[base + place],
                send_sem=send_sem.at[base],
                recv_sem=recv_sem.at[base + place],
                device_id=mesh.partner,
                device_id_type=MESH,
            )

        for j, device in enumerate(devices):
            sent(j, device).start()
        for j in range(1, size):
            come(lax.rem(here + j, size)).wait_recv()
        for j, device in enumerate(devices):
            sent(j, device).wait_send()
        total = stats[base]
        for place in range(1, size):
            total = total + stats[base + place]
    return total


def window_rows(shard_size, many):
    units = [(shard_size * d) // UNIT for d in range(many + 1)]
    return 16 * (max(b - a for a, b in zip(units, units[1:])) + 1)


def first_row(shard_size, number):
    if isinstance(number, int):
        return number * shard_size // UNIT * 16
    return pl.multiple_of(lax.div(number * shard_size, UNIT) * 16, 16)


def inner_units(shard_size, many):
    units = [(shard_size * d) // UNIT for d in range(many + 1)]
    return min(b - a for a, b in zip(units, units[1:]))


def lay_inner(shard_size, many, land, flat, owner):
    count = 16 * inner_units(shard_size, many) - 16
    row = pl.multiple_of(first_row(shard_size, owner) + 16, 16)
    flat[pl.ds(row, count), :] = land[owner, pl.ds(16, count), :].astype(F32)


def lay_edges(shard_size, many, land, flat):
    inner = 16 * inner_units(shard_size, many)
    flat[0:16, :] = jnp.zeros((16, 128), F32)

    def lay(number, carry):
        row = first_row(shard_size, number)
        after = first_row(shard_size, number + 1)
        flat[pl.ds(row, 16), :] += land[number, 0:16, :].astype(F32)
        tail = land[number, pl.ds(inner, 16), :].astype(F32)
        flat[pl.ds(pl.multiple_of(row + inner, 16), 16), :] = tail
        last = pl.multiple_of(after - row, 16)
        flat[pl.ds(after, 16), :] = land[number, pl.ds(last, 16), :].astype(F32)
        return carry

    lax.fori_loop(0, many, lay, 0)


def early_matrices(flat, wall_ref, gain_one_ref, gain_two_ref):
    for c in range(D // 128):
        lanes = slice(c * 128, (c + 1) * 128)
        gain_one_ref[:, lanes] = flat[c : c + 1, :]
        gain_two_ref[:, lanes] = flat[4 + c : 5 + c, :]
    for c in range(QW // 128):
        wall_ref[c * 128 : (c + 1) * 128, :] = flat[pl.ds(WQ_ROW + c, D, stride=12), :].T.astype(BF16)
    for first, row in ((KROW, WK_ROW), (VROW, WV_ROW)):
        pair = flat[row : row + 256, :].T.astype(BF16)
        wall_ref[first : first + H, :] = (
            nn(pair[:H], picks(256, 2, 0).astype(BF16)) + nn(pair[H:], picks(256, 2, 1).astype(BF16))
        ).astype(BF16)
    across = jnp.concatenate(
        [flat[pl.ds(WR_ROW + j, 32, stride=3), :] for j in range(3)], axis=1
    ).T.astype(BF16)
    router_t = jnp.zeros((E, D), F32)
    for part in range(16):
        router_t = router_t + nn(across[part * E : (part + 1) * E, :], picks(32, 16, part).astype(BF16))
    wall_ref[RROW:ALLW, :] = jnp.concatenate(
        [router_t, jnp.zeros((ALLW - RROW - E, D), F32)], axis=0
    ).astype(BF16)


def gather_kernel(
    mesh, shard_size, own_ref,
    wall_out, gain_one_ref, gain_two_ref, wo_out, w1_out, w2_out,
    land, flat, wall_ref, wo_ref, w1_ref, w2_ref, send_sem, recv_sem, out_sem,
):
    mesh = mesh()
    many = mesh.many
    mesh.greet(mesh.near())
    land[mesh.me] = own_ref[...]
    gather_blocks(mesh, land, send_sem, recv_sem, True)
    each_owner(mesh, mesh.core, functools.partial(lay_inner, shard_size, many, land, flat))

    def arrive(owner):
        for p in range(recv_sem.shape[1]):
            rows = pl.ds(*pieces_of(own_ref.shape[0])[p])
            pltpu.make_async_remote_copy(
                src_ref=land.at[owner, rows],
                dst_ref=land.at[owner, rows],
                send_sem=send_sem.at[0, p],
                recv_sem=recv_sem.at[owner, p],
                device_id=mesh.partner,
                device_id_type=MESH,
            ).wait_recv()
        lay_inner(shard_size, many, land, flat, owner)

    each_owner(mesh, 1 - mesh.core, arrive)
    lay_edges(shard_size, many, land, flat)
    copies = []

    def leave(matrix, out):
        one = pltpu.make_async_copy(matrix, out, out_sem.at[len(copies)])
        one.start()
        copies.append(one)

    for c in range(D // 128):
        wo_ref[:, c * 128 : (c + 1) * 128] = flat[pl.ds(WO_ROW + c, QW, stride=4), :].astype(BF16)
    leave(wo_ref, wo_out)
    for c in range(D // 128):
        w2_ref[:, c * 128 : (c + 1) * 128] = flat[pl.ds(W2_ROW + c, FF, stride=4), :].astype(BF16)
    leave(w2_ref, w2_out)
    for c in range(FF // 128):
        w1_ref[:, c * 128 : (c + 1) * 128] = flat[pl.ds(W1_ROW + c, D, stride=16), :].astype(BF16)
    leave(w1_ref, w1_out)
    early_matrices(flat, wall_ref, gain_one_ref, gain_two_ref)
    leave(wall_ref, wall_out)
    gather_blocks(mesh, land, send_sem, recv_sem, False)
    for one in copies:
        one.wait()


def gather_weights(shards, over, shard_size, own):
    window = own.shape[0]
    many = shards * over
    rows = (shard_size * (many - 1)) // UNIT * 16 + window
    vmem = pl.BlockSpec(memory_space=pltpu.VMEM)
    hbm = pl.BlockSpec(memory_space=pl.ANY)
    mesh = functools.partial(Mesh3, shards, over)
    pieces = len(pieces_of(window))
    return pl.pallas_call(
        functools.partial(gather_kernel, mesh, shard_size),
        in_specs=[vmem],
        out_specs=[hbm, vmem, vmem, hbm, hbm, hbm],
        out_shape=[
            struct((ALLW, D), BF16),
            struct((1, D)),
            struct((1, D)),
            struct((QW, D), BF16),
            struct((D, FF), BF16),
            struct((FF, D), BF16),
        ],
        scratch_shapes=[
            pltpu.VMEM((many, window, 128), BF16),
            pltpu.VMEM((rows, 128), F32),
            pltpu.VMEM((ALLW, D), BF16),
            pltpu.VMEM((QW, D), BF16),
            pltpu.VMEM((D, FF), BF16),
            pltpu.VMEM((FF, D), BF16),
            pltpu.SemaphoreType.DMA((5 * many // 2, pieces)),
            pltpu.SemaphoreType.DMA((many, pieces)),
            pltpu.SemaphoreType.DMA((4,)),
        ],
        compiler_params=pltpu.CompilerParams(
            collective_id=0, has_side_effects=True, vmem_limit_bytes=60 * MIB
        ),
        name="gather_weights",
    )(own)


def reduce_kernel(
    mesh, shard_size, flat_ref, count_ref,
    out_ref, total_ref, gain_ref,
    part, outgo, income, stats, part_sem, send_sem, recv_sem, stat_send, stat_recv,
):
    mesh = mesh()
    window = out_ref.shape[0]
    span = part.shape[1]

    def source(owner):
        return flat_ref.at[pl.ds(first_row(shard_size, owner), window), :]

    def fetch(y):
        first = first_row(shard_size, (2 * y + mesh.core) * mesh.over)
        return pltpu.make_async_copy(flat_ref.at[pl.ds(first, span), :], part.at[y], part_sem.at[y])

    def mine(owner, first, rows):
        shard = lax.div(owner, mesh.over)
        row = first_row(shard_size, owner) - first_row(shard_size, shard * mesh.over) + first
        return part[lax.div(shard, 2), pl.ds(pl.multiple_of(row, 16), rows), :].astype(F32)

    for y in range(mesh.sizes["y"]):
        fetch(y).start()
    mesh.greet(mesh.column() + mesh.layer())
    for y in range(mesh.sizes["y"]):
        fetch(y).wait()
    for core in range(2):

        @pl.when(mesh.core == core)
        def _(core=core):
            reduce_blocks(mesh, core, source, mine, outgo, income, send_sem, recv_sem, out_ref)

    total = out_ref[...]
    begin = mesh.me * shard_size - lax.div(mesh.me * shard_size, UNIT) * UNIT
    place = (
        lax.broadcasted_iota(jnp.int32, (window, 128), 0) * 128
        + lax.broadcasted_iota(jnp.int32, (window, 128), 1)
    )
    inside = jnp.where((place >= begin) & (place < begin + shard_size), total, 0.0)
    squares = jnp.sum(jnp.sum(inside * inside, axis=0, keepdims=True), axis=1, keepdims=True)
    lane = lax.broadcasted_iota(jnp.int32, (8, 128), 1)
    row = jnp.where(lane == E, squares, count_ref[...])
    gains = jnp.where(mesh.me == 0, total[0:8, :], 0.0)
    summed = sum_all(mesh, jnp.concatenate([row, gains], axis=0), stats, stat_send, stat_recv)
    total_ref[...] = summed[0:1, :]
    gain_ref[...] = summed[8:16, :]


def reduce_grads(shards, over, shard_size, window, flat, counts):
    vmem = pl.BlockSpec(memory_space=pltpu.VMEM)
    many = shards * over
    mesh = functools.partial(Mesh3, shards, over)
    pieces = len(pieces_of(window))
    steps = over + shards
    units = [(shard_size * d) // UNIT for d in range(many)]
    span = 16 * max(units[d + over - 1] - units[d] for d in range(0, many, over)) + window
    return pl.pallas_call(
        functools.partial(reduce_kernel, mesh, shard_size),
        in_specs=[pl.BlockSpec(memory_space=pl.ANY), vmem],
        out_specs=[vmem] * 3,
        out_shape=[struct((window, 128)), struct((1, 128)), struct((8, 128))],
        scratch_shapes=[
            pltpu.VMEM((shards // 2, span, 128), BF16),
            pltpu.VMEM((many // 2, window, 128), BF16),
            pltpu.VMEM((many, window, 128), BF16),
            pltpu.VMEM((steps, 16, 128), F32),
            pltpu.SemaphoreType.DMA((shards // 2,)),
            pltpu.SemaphoreType.DMA((many, pieces)),
            pltpu.SemaphoreType.DMA((many, pieces)),
            pltpu.SemaphoreType.DMA((steps,)),
            pltpu.SemaphoreType.DMA((steps,)),
        ],
        compiler_params=pltpu.CompilerParams(
            collective_id=1, has_side_effects=True, vmem_limit_bytes=56 * MIB
        ),
        name="reduce_grads",
    )(flat, counts)


def local_step(flat_rows, tokens, grad_out, routes, segments, weights):
    wall, gain_one, gain_two, wo, w1, w2 = weights
    queries, attended, gates, lse, kv, kvt, start, routes_t, counts = head_forward(
        tokens, routes.T, segments, wall, gain_one
    )
    output, dres, datt, delta, dlogits, flat, extra, dgain_two = middle(
        flat_rows, tokens, grad_out, gain_two, wo, w1, w2, routes_t, gates, attended
    )
    input_grad, flat = head_backward(
        segments, tokens, gain_one, wall, routes_t, start, queries, datt, lse, delta, kv, kvt, dlogits, dres,
        dgain_two, extra, flat,
    )
    return output, input_grad, flat, counts


def per_device(
    shards, over, tokens, grad_out, routes, segments, params, first_moment, second_moment, ema_weights
):
    shard_size = params.shape[0]
    window = window_rows(shard_size, shards * over)
    flat_rows = (shard_size * (shards * over - 1)) // UNIT * 16 + window + 16
    me = lax.axis_index("dp") * over + lax.axis_index("fsdp")
    begin = lax.rem(me * shard_size, UNIT)
    own = lax.dynamic_slice(
        jnp.pad(params.astype(BF16), (UNIT, window * 128 - shard_size)), (UNIT - begin,), (window * 128,)
    ).reshape(window, 128)
    wall, gain_one, gain_two, wo, w1, w2 = gather_weights(shards, over, shard_size, own)
    output, input_grad, flat, counts = local_step(
        flat_rows, tokens, grad_out, routes, segments, (wall, gain_one, gain_two, wo, w1, w2)
    )
    reduced, sums, gain_grads = reduce_grads(shards, over, shard_size, window, flat, counts)
    grad_shard = lax.dynamic_slice(reduced.reshape(-1), (begin,), (shard_size,))
    total_tokens = tokens.shape[0] * shards * over
    expert_load = sums[0, :E] * (E / (total_tokens * TOPK))
    grad_norm = jnp.sqrt(sums[0, E])
    clipped = grad_shard * (CLIP_LIMIT / jnp.maximum(grad_norm, CLIP_LIMIT))
    new_first = BETA_FIRST * first_moment + (1.0 - BETA_FIRST) * clipped
    new_second = BETA_SECOND * second_moment + (1.0 - BETA_SECOND) * clipped * clipped
    first_hat = new_first / (1.0 - BETA_FIRST**STEP)
    second_hat = new_second / (1.0 - BETA_SECOND**STEP)
    new_params = params * (1.0 - LEARN_RATE * DECAY_RATE) - LEARN_RATE * first_hat / (
        jnp.sqrt(second_hat) + ADAM_EPS
    )
    new_ema = EMA_KEEP * ema_weights + (1.0 - EMA_KEEP) * new_params
    return (
        output,
        input_grad,
        expert_load,
        grad_norm.reshape(1),
        new_params,
        new_first,
        new_second,
        new_ema,
        gain_grads.reshape(2, D),
    )


def solution(mesh):
    row = P(("dp", "fsdp"), None)
    flat = P(("dp", "fsdp"))
    return jax.shard_map(
        functools.partial(per_device, mesh.shape["dp"], mesh.shape["fsdp"]),
        mesh=mesh,
        in_specs=(row, row, row, row, flat, flat, flat, flat),
        out_specs=(row, row, P(), P(), flat, flat, flat, flat, P()),
        check_vma=False,
    )
```

```python
import copy
import functools
import itertools

import jax
import jax.numpy as jnp
from jax import lax
from jax.experimental import pallas as pl
from jax.experimental.pallas import tpu as pltpu
from jax.sharding import PartitionSpec as P

D = 512
E = 24
TOPK = 8
H = 64
FF = 2048
STEP = 10

NORM_EPS = 1e-06
CLIP_LIMIT = 1.0
BETA_FIRST = 0.9
BETA_SECOND = 0.95
LEARN_RATE = 0.1
DECAY_RATE = 0.1
ADAM_EPS = 1e-08
EMA_KEEP = 0.9
NEG_LARGE = -1e30

QW = E * H
KROW = QW
VROW = QW + H
RROW = QW + 2 * H
ALLW = 1696
LEN = 1024
TB = 512
NB = LEN // TB
QB = 128
SIDE = 4
MOST = 512 // QB + 1
SORT_STEPS = (
    (0, 1), (2, 3), (4, 5), (6, 7), (0, 2), (1, 3), (4, 6), (5, 7), (1, 2), (5, 6),
    (0, 4), (1, 5), (2, 6), (3, 7), (2, 4), (3, 5), (1, 2), (3, 4), (5, 6),
)
FC = 512
MB = 512
MIB = 1 << 20

WR_ROW = 8
WK_ROW = 104
WV_ROW = 360
WQ_ROW = 616
WO_ROW = 6760
W1_ROW = 12904
W2_ROW = 21096
ALL_ROWS = 29288
UNIT = 16 * 128
MESH = pl.DeviceIdType.MESH

F32 = jnp.float32
BF16 = jnp.bfloat16


def nn(a, b):
    return lax.dot_general(a, b, (((1,), (0,)), ((), ())), preferred_element_type=F32)


def nt(a, b):
    return lax.dot_general(a, b, (((1,), (1,)), ((), ())), preferred_element_type=F32)


def tn(a, b):
    return lax.dot_general(a, b, (((0,), (0,)), ((), ())), preferred_element_type=F32)


def rms_scale(values):
    return lax.rsqrt(jnp.mean(values * values, axis=-1, keepdims=True) + NORM_EPS)


def slot_of(routes, k, rows):
    return jnp.broadcast_to(routes[k : k + 1, :], (rows, routes.shape[1]))


def expert_rows(routes, k):
    return jnp.broadcast_to(routes.astype(jnp.int16)[k : k + 1, :], (16, routes.shape[1]))


def pick_heads(routes, source_ref, k):
    tokens = routes.shape[1]
    route = expert_rows(routes, k)
    taken = source_ref[k * H : (k + 1) * H, :].reshape(H // 16, 16, tokens)
    for e in range(k + 1, k + E - TOPK + 1):
        piece = source_ref[e * H : (e + 1) * H, :].reshape(H // 16, 16, tokens)
        taken = jnp.where((route == jnp.int16(e))[None], piece, taken)
    return taken.reshape(H, tokens)


def place_heads(routes, source_ref, target_ref):
    tokens = routes.shape[1]
    rows = [expert_rows(routes, k) for k in range(TOPK)]
    for e in range(E):
        total = jnp.zeros((H // 16, 16, tokens), BF16)
        for k in range(max(0, e - (E - TOPK)), min(TOPK - 1, e) + 1):
            piece = source_ref[k * H : (k + 1) * H, :].reshape(H // 16, 16, tokens)
            total = jnp.where((rows[k] == jnp.int16(e))[None], piece, total)
        target_ref[e * H : (e + 1) * H, :] = total.reshape(H, tokens)


def sorted_rows(rows):
    rows = list(rows)
    for one, two in SORT_STEPS:
        rows[one], rows[two] = jnp.minimum(rows[one], rows[two]), jnp.maximum(rows[one], rows[two])
    return rows


def key_mask(first_key, first_query, rows, start_row):
    keys = lax.broadcasted_iota(jnp.int32, (rows, QB), 0) + first_key
    queries = lax.broadcasted_iota(jnp.int32, (rows, QB), 1) + first_query
    mask = (keys <= queries) & (keys >= start_row)
    return jnp.concatenate([mask] * SIDE, axis=1)


def group_of(ref, k, lanes):
    return jnp.concatenate([ref[i * H : (i + 1) * H, lanes] for i in range(k, k + SIDE)], axis=1)


def row_group(ref, k, lanes):
    return jnp.concatenate([ref[i : i + 1, lanes] for i in range(k, k + SIDE)], axis=1)


def by_span(attend, row, place, segment_ref):
    def one(j, carry):
        block = place * (TB // QB) + j
        first = block * QB
        span = jnp.int32(1)
        for back in range(MOST - 1):
            last = first - back * QB - 1
            same = segment_ref[row, jnp.maximum(last, 0)] == segment_ref[row, first]
            span = span + jnp.where((last >= 0) & same, 1, 0)
        for blocks in range(1, MOST + 1):

            @pl.when(span == blocks)
            def _(blocks=blocks):
                attend(pl.ds(pl.multiple_of(j * QB, QB), QB), block, blocks)

        return carry

    lax.fori_loop(0, TB // QB, one, 0)


def head_forward_kernel(
    steps, segment_smem, x_ref, route_ref, segment_ref, wall_ref, gain_ref,
    q_ref, att_ref, gate_ref, lse_ref, kv_ref, kvt_ref, start_ref, sorted_ref, count_ref,
    all_scr, low_scr, k_scr, vt_scr, count_scr,
):
    step = pl.program_id(0)
    place = lax.rem(step, NB)
    here = pl.multiple_of(place * TB, TB)

    @pl.when(step == 0)
    def _():
        count_scr[...] = jnp.zeros_like(count_scr)

    row = segment_ref[pl.ds(lax.div(step, NB), 1), :]
    segments = segment_ref[pl.ds(lax.div(step, NB), 1), pl.ds(here, TB)]
    start = jnp.zeros((1, TB), jnp.int32)
    for number in range(1, 4):
        below = jnp.sum((row < number).astype(jnp.int32), axis=1, keepdims=True)
        start = jnp.where(segments == number, below, start)
    start_ref[...] = start
    x = x_ref[...].astype(F32)
    normed = (x * rms_scale(x) * gain_ref[...]).astype(BF16)
    all_scr[...] = nt(wall_ref[...], normed)
    kt = all_scr[KROW : KROW + H, :]
    vt = all_scr[VROW : VROW + H, :]
    logits = all_scr[RROW : RROW + E, :]
    kvt = jnp.concatenate([kt, vt], axis=0)
    kv = kvt.T.astype(BF16)
    kv_ref[...] = kv
    kvt_ref[...] = kvt.astype(BF16)
    k_scr[pl.ds(here, TB), :] = kv[:, :H]
    vt_scr[:, pl.ds(here, TB)] = vt.astype(BF16)
    routes = jnp.concatenate(sorted_rows(route_ref[k : k + 1, :] for k in range(TOPK)), axis=0)
    sorted_ref[...] = routes
    experts = lax.broadcasted_iota(jnp.int32, (E, TB), 0)
    chosen = []
    counts = count_scr[...]
    for k in range(TOPK):
        named = slot_of(routes, k, E) == experts
        chosen.append(jnp.sum(jnp.where(named, logits, 0.0), axis=0, keepdims=True))
        counts = counts + named.astype(F32)
    count_scr[...] = counts
    chosen = jnp.concatenate(chosen, axis=0)
    raised = jnp.exp(chosen - jnp.max(chosen, axis=0, keepdims=True))
    gate_ref[...] = raised / jnp.sum(raised, axis=0, keepdims=True)
    low_scr[...] = all_scr[0:QW, :].astype(BF16)
    for k in range(TOPK):
        q_ref[k * H : (k + 1) * H, :] = pick_heads(routes, low_scr, k) * jnp.asarray(H ** (-0.5), BF16)

    def attend(lanes, block, blocks):
        rows = blocks * QB
        first_key = pl.multiple_of((block - (blocks - 1)) * QB, QB)
        mask = key_mask(first_key, block * QB, rows, start_ref[:, lanes])
        keys = k_scr[pl.ds(first_key, rows), :]
        values = vt_scr[:, pl.ds(first_key, rows)]
        groups = [nn(keys, group_of(q_ref, 0, lanes))]
        for k in range(0, TOPK, SIDE):
            if k + SIDE < TOPK:
                groups.append(nn(keys, group_of(q_ref, k + SIDE, lanes)))
            scores = jnp.where(mask, groups[k // SIDE], NEG_LARGE)
            top = jnp.max(scores, axis=0, keepdims=True)
            raised = jnp.exp(scores - top)
            total = jnp.sum(raised, axis=0, keepdims=True)
            out = nn(values, (raised * (1.0 / total)).astype(BF16))
            lse = top + jnp.log(total)
            for side in range(SIDE):
                one = slice(side * QB, (side + 1) * QB)
                att_ref[(k + side) * H : (k + side + 1) * H, lanes] = out[:, one]
                lse_ref[k + side : k + side + 1, lanes] = lse[:, one]

    by_span(attend, lax.div(step, NB), place, segment_smem)

    @pl.when(step == steps - 1)
    def _():
        held = jnp.sum(count_scr[...], axis=1, keepdims=True)
        lane = lax.broadcasted_iota(jnp.int32, (E, 128), 1)
        row = lax.broadcasted_iota(jnp.int32, (E, 128), 0)
        count_ref[...] = jnp.sum(jnp.where(lane == row, held, 0.0), axis=0, keepdims=True)


def picks(rows, stride, first):
    at = lax.broadcasted_iota(jnp.int32, (rows, D), 1)
    row = lax.broadcasted_iota(jnp.int32, (rows, D), 0)
    return (at == row * stride + first).astype(F32)


def exact(product, a, b):
    return lax.dot_general(
        a, b, (product, ((), ())), precision=lax.Precision.HIGHEST, preferred_element_type=F32
    )


def gelu_parts(v):
    cdf = 0.5 + 0.5 * lax.erf(v * 0.7071067811865476)
    return cdf, jnp.exp(v * v * -0.5) * 0.3989422804014327


def middle_kernel(
    x_ref, dy_ref, gain_ref, wo_ref, w1_ref, w2_ref, route_ref, gate_ref, att_ref,
    out_ref, dres_ref, datt_ref, delta_ref, dlogit_ref, flat_ref, extra_ref, dgain_ref,
    slot_scr, head_scr, mix_scr, dwo_ref, dw1_ref, dw2t_ref, rows_scr, low_scr, row_sem,
):
    step = pl.program_id(0)

    @pl.when(step == 0)
    def _():
        dwo_ref[...] = jnp.zeros_like(dwo_ref)
        dw1_ref[...] = jnp.zeros_like(dw1_ref)
        dw2t_ref[...] = jnp.zeros_like(dw2t_ref)
        dgain_ref[...] = jnp.zeros_like(dgain_ref)

    routes = route_ref[...]
    tokens = routes.shape[1]
    gates = gate_ref[...]
    for k in range(TOPK):
        rows = slice(k * H, (k + 1) * H)
        slot_scr[rows, :] = (gates[k : k + 1, :] * att_ref[rows, :]).astype(BF16)
    place_heads(routes, slot_scr, mix_scr)
    x = x_ref[...].astype(F32)
    dy = dy_ref[...]
    mixed = mix_scr[...]
    residual = x + tn(mixed, wo_ref[...])
    scale = rms_scale(residual)
    gain = gain_ref[...]
    second = (residual * scale * gain).astype(BF16)
    second_t = second.T
    dy_t = dy.T
    out = residual
    dsecond = jnp.zeros((tokens, D), F32)
    for c in range(0, FF, FC):
        up = w1_ref[:, c : c + FC]
        down = w2_ref[c : c + FC, :]
        pre = nn(second, up)
        cdf, density = gelu_parts(pre)
        hidden = (pre * cdf).astype(BF16)
        dpre = (nt(dy, down) * (cdf + pre * density)).astype(BF16)
        out = out + nn(hidden, down)
        dsecond = dsecond + nt(dpre, up)
        dw2t_ref[:, c : c + FC] += nn(dy_t, hidden)
        dw1_ref[:, c : c + FC] += nn(second_t, dpre)
    out_ref[...] = out.astype(BF16)
    dgain_ref[...] += jnp.sum(dsecond * residual * scale, axis=0, keepdims=True)
    weighted = gain * dsecond
    dres = (
        dy.astype(F32)
        + scale * weighted
        - residual * (scale * scale * scale) * jnp.mean(weighted * residual, axis=-1, keepdims=True)
    )
    dres_ref[...] = dres
    branch = dres.astype(BF16)
    dwo_ref[...] += nn(mixed, branch)
    head_scr[...] = nt(wo_ref[...], branch).astype(BF16)
    dgates = []
    for k in range(TOPK):
        rows = slice(k * H, (k + 1) * H)
        dslot = pick_heads(routes, head_scr, k).astype(F32)
        attended = att_ref[rows, :]
        dgates.append(jnp.sum(dslot * attended, axis=0, keepdims=True))
        datt = (gates[k : k + 1, :] * dslot).astype(BF16)
        datt_ref[rows, :] = datt
        delta_ref[k : k + 1, :] = jnp.sum(datt.astype(F32) * attended, axis=0, keepdims=True)
    dgate = jnp.concatenate(dgates, axis=0)
    dchosen = gates * (dgate - jnp.sum(gates * dgate, axis=0, keepdims=True))
    experts = lax.broadcasted_iota(jnp.int32, (E, tokens), 0)
    dlogits = jnp.zeros((E, tokens), F32)
    for k in range(TOPK):
        dlogits = jnp.where(
            slot_of(routes, k, E) == experts,
            jnp.broadcast_to(dchosen[k : k + 1, :], (E, tokens)),
            dlogits,
        )
    dlogit_ref[...] = dlogits

    @pl.when(step == pl.num_programs(0) - 1)
    def _():
        for c in range(D // 128):
            lanes = slice(c * 128, (c + 1) * 128)
            rows_scr[pl.ds(c, QW, stride=4), :] = dwo_ref[:, lanes]
            rows_scr[pl.ds(W2_ROW - WO_ROW + c, FF, stride=4), :] = dw2t_ref[lanes, :].T
        for c in range(FF // 128):
            rows_scr[pl.ds(W1_ROW - WO_ROW + c, D, stride=16), :] = dw1_ref[:, c * 128 : (c + 1) * 128]
        extra_ref[...] = rows_scr[0:8, :]
        low_scr[...] = rows_scr[8:, :].astype(BF16)
        copy = pltpu.make_async_copy(
            low_scr, flat_ref.at[pl.ds(WO_ROW + 8, low_scr.shape[0]), :], row_sem.at[0]
        )
        copy.start()
        copy.wait()


def head_backward_kernel(
    segment_smem, x_ref, gain_ref, wall_ref, route_ref, start_ref, q_ref, datt_ref,
    lse_ref, delta_ref, kv_ref, kvt_ref, dlogit_ref, dres_ref, dgain_two_ref, extra_ref, flat_in,
    dx_ref, flat_ref,
    dk_scr, dv_scr, dq_scr, dall_scr, prob_scr, dscore_scr, dwall_ref, dgain_ref, rows_scr, low_scr, row_sem,
):
    step = pl.program_id(0)
    place = NB - 1 - lax.rem(step, NB)
    here = pl.multiple_of(place * TB, TB)

    @pl.when(step == 0)
    def _():
        dwall_ref[...] = jnp.zeros_like(dwall_ref)
        dgain_ref[...] = jnp.zeros_like(dgain_ref)

    @pl.when(lax.rem(step, NB) == 0)
    def _():
        dk_scr[...] = jnp.zeros_like(dk_scr)
        dv_scr[...] = jnp.zeros_like(dv_scr)

    def attend(lanes, block, blocks):
        rows = blocks * QB
        first_key = pl.multiple_of((block - (blocks - 1)) * QB, QB)
        mask = key_mask(first_key, block * QB, rows, start_ref[:, lanes])
        keys = kv_ref[pl.ds(first_key, rows), :H]
        values = kv_ref[pl.ds(first_key, rows), H:]
        keys_t = kvt_ref[:H, pl.ds(first_key, rows)]
        queries = [group_of(q_ref, k, lanes) for k in range(0, TOPK, SIDE)]
        datts = [group_of(datt_ref, k, lanes) for k in range(0, TOPK, SIDE)]
        scores = [nn(keys, queries[0])]
        dprobs = [nn(values, datts[0])]
        for i in range(TOPK // SIDE):
            if i + 1 < TOPK // SIDE:
                scores.append(nn(keys, queries[i + 1]))
                dprobs.append(nn(values, datts[i + 1]))
            k = i * SIDE
            wide = slice(k * QB, (k + SIDE) * QB)
            probs = jnp.exp(jnp.where(mask, scores[i], NEG_LARGE) - row_group(lse_ref, k, lanes))
            dscore = (probs * (dprobs[i] - row_group(delta_ref, k, lanes))).astype(BF16)
            prob_scr[0:rows, wide] = probs.astype(BF16)
            dscore_scr[0:rows, wide] = dscore
            dq = (nn(keys_t, dscore) * (H ** (-0.5))).astype(BF16)
            for side in range(SIDE):
                dq_scr[(k + side) * H : (k + side + 1) * H, lanes] = dq[:, side * QB : (side + 1) * QB]
        dv_scr[pl.ds(first_key, rows), :] += nt(prob_scr[0:rows, :], jnp.concatenate(datts, axis=1))
        dk_scr[pl.ds(first_key, rows), :] += nt(dscore_scr[0:rows, :], jnp.concatenate(queries, axis=1))

    by_span(attend, lax.div(step, NB), place, segment_smem)
    place_heads(route_ref[...], dq_scr, dall_scr)
    dkv = jnp.concatenate([dk_scr[pl.ds(here, TB), :], dv_scr[pl.ds(here, TB), :]], axis=1)
    dall_scr[KROW : KROW + 2 * H, :] = dkv.T.astype(BF16)
    dall_scr[RROW : RROW + 32, :] = jnp.concatenate(
        [dlogit_ref[...], jnp.zeros((32 - E, TB), F32)], axis=0
    ).astype(BF16)
    x = x_ref[...].astype(F32)
    scale = rms_scale(x)
    gain = gain_ref[...]
    normed = (x * scale * gain).astype(BF16)
    dall = dall_scr[...]
    dwall_ref[...] += nn(dall, normed)
    dnormed = tn(dall, wall_ref[...])
    dgain_ref[...] += jnp.sum(dnormed * x * scale, axis=0, keepdims=True)
    weighted = gain * dnormed
    dx_ref[...] = (
        dres_ref[...]
        + scale * weighted
        - x * (scale * scale * scale) * jnp.mean(weighted * x, axis=-1, keepdims=True)
    )

    @pl.when(step == pl.num_programs(0) - 1)
    def _():
        for c in range(D // 128):
            lanes = slice(c * 128, (c + 1) * 128)
            rows_scr[c : c + 1, :] = dgain_ref[:, lanes]
            rows_scr[4 + c : 5 + c, :] = dgain_two_ref[:, lanes]
        router_t = dwall_ref[RROW : RROW + E, :]
        across = jnp.concatenate(
            [exact(((1,), (1,)), router_t, picks(32, 16, b)) for b in range(16)], axis=0
        ).T
        for j in range(3):
            rows_scr[pl.ds(WR_ROW + j, 32, stride=3), :] = across[:, j * 128 : (j + 1) * 128]
        for first, row in ((KROW, WK_ROW), (VROW, WV_ROW)):
            part = dwall_ref[first : first + H, :]
            rows_scr[row : row + 256, :] = jnp.concatenate(
                [exact(((1,), (1,)), picks(256, 2, b), part) for b in range(2)], axis=1
            )
        for c in range(QW // 128):
            rows_scr[pl.ds(WQ_ROW + c, D, stride=12), :] = dwall_ref[c * 128 : (c + 1) * 128, :].T
        rows_scr[WO_ROW : WO_ROW + 8, :] = extra_ref[...]
        low_scr[...] = rows_scr[...].astype(BF16)
        copy = pltpu.make_async_copy(low_scr, flat_ref.at[pl.ds(0, WO_ROW + 8), :], row_sem.at[0])
        copy.start()
        copy.wait()


def whole(shape):
    return pl.BlockSpec(shape, lambda *_: (0,) * len(shape), pipeline_mode=pl.Buffered(1))


def kept(shape):
    return pl.BlockSpec(shape, lambda *_: (0,) * len(shape))


SMEM = pl.BlockSpec(memory_space=pltpu.SMEM)


def struct(shape, kind=F32):
    return jax.ShapeDtypeStruct(shape, kind)


def params_for(mib):
    return pltpu.CompilerParams(vmem_limit_bytes=mib * MIB)


def head_forward(tokens, routes_t, segments, wall, gain):
    count = tokens.shape[0]
    steps = count // TB
    across = lambda rows: pl.BlockSpec((rows, TB), lambda b: (0, b))
    down = lambda columns: pl.BlockSpec((TB, columns), lambda b: (b, 0))
    return pl.pallas_call(
        functools.partial(head_forward_kernel, steps),
        grid=(steps,),
        in_specs=[SMEM, down(D), across(TOPK), whole(segments.shape), whole((ALLW, D)), whole((1, D))],
        out_specs=[
            across(TOPK * H), across(TOPK * H), across(TOPK), across(TOPK), down(2 * H), across(2 * H),
            across(1), across(TOPK), whole((1, 128)),
        ],
        scratch_shapes=[
            pltpu.VMEM((ALLW, TB), F32),
            pltpu.VMEM((QW, TB), BF16),
            pltpu.VMEM((LEN, H), BF16),
            pltpu.VMEM((H, LEN), BF16),
            pltpu.VMEM((E, TB), F32),
        ],
        out_shape=[
            struct((TOPK * H, count), BF16),
            struct((TOPK * H, count)),
            struct((TOPK, count)),
            struct((TOPK, count)),
            struct((count, 2 * H), BF16),
            struct((2 * H, count), BF16),
            struct((1, count), jnp.int32),
            struct((TOPK, count), jnp.int32),
            struct((1, 128)),
        ],
        compiler_params=params_for(56),
        name="head_forward",
        cost_estimate=pl.CostEstimate(flops=10_000_000_000, bytes_accessed=16_000_000, transcendentals=0),
    )(segments, tokens, routes_t, segments, wall, gain)


def middle(flat_rows, tokens, grad_out, gain, wo, w1, w2, routes_t, gates, attended):
    count = tokens.shape[0]
    steps = count // MB
    across = lambda rows: pl.BlockSpec((rows, MB), lambda b: (0, b))
    down = lambda columns: pl.BlockSpec((MB, columns), lambda b: (b, 0))
    return pl.pallas_call(
        middle_kernel,
        grid=(steps,),
        in_specs=[
            down(D), down(D), whole((1, D)), whole((QW, D)), whole((D, FF)), whole((FF, D)),
            across(TOPK), across(TOPK), across(TOPK * H),
        ],
        out_specs=[
            down(D), down(D), across(TOPK * H), across(TOPK), across(E),
            pl.BlockSpec(memory_space=pl.ANY), whole((8, 128)), whole((1, D)),
        ],
        out_shape=[
            struct((count, D), BF16),
            struct((count, D)),
            struct((TOPK * H, count), BF16),
            struct((TOPK, count)),
            struct((E, count)),
            struct((flat_rows, 128), BF16),
            struct((8, 128)),
            struct((1, D)),
        ],
        scratch_shapes=[
            pltpu.VMEM((TOPK * H, MB), BF16),
            pltpu.VMEM((QW, MB), BF16),
            pltpu.VMEM((QW, MB), BF16),
            pltpu.VMEM((QW, D), F32),
            pltpu.VMEM((D, FF), F32),
            pltpu.VMEM((D, FF), F32),
            pltpu.VMEM((flat_rows - WO_ROW, 128), F32),
            pltpu.VMEM((flat_rows - WO_ROW - 8, 128), BF16),
            pltpu.SemaphoreType.DMA((1,)),
        ],
        compiler_params=params_for(60),
        name="middle",
    )(tokens, grad_out, gain, wo, w1, w2, routes_t, gates, attended)


def head_backward(
    segments, tokens, gain, wall, routes_t, start, queries, datt, lse, delta, kv, kvt, dlogits, dres,
    dgain_two, extra, flat,
):
    count = tokens.shape[0]
    steps = count // TB

    def place(b):
        return (b // NB) * NB + NB - 1 - b % NB

    across = lambda rows: pl.BlockSpec((rows, TB), lambda b: (0, place(b)))
    down = lambda columns: pl.BlockSpec((TB, columns), lambda b: (place(b), 0))
    return pl.pallas_call(
        head_backward_kernel,
        grid=(steps,),
        in_specs=[
            SMEM, down(D), whole((1, D)), whole((ALLW, D)), across(TOPK), across(1),
            across(TOPK * H), across(TOPK * H), across(TOPK), across(TOPK),
            pl.BlockSpec((LEN, 2 * H), lambda b: (b // NB, 0)),
            pl.BlockSpec((2 * H, LEN), lambda b: (0, b // NB)),
            across(E), down(D), whole((1, D)), whole((8, 128)), pl.BlockSpec(memory_space=pl.ANY),
        ],
        out_specs=[down(D), pl.BlockSpec(memory_space=pl.ANY)],
        scratch_shapes=[
            pltpu.VMEM((LEN, H), F32),
            pltpu.VMEM((LEN, H), F32),
            pltpu.VMEM((TOPK * H, TB), BF16),
            pltpu.VMEM((ALLW, TB), BF16),
            pltpu.VMEM((MOST * QB, TOPK * QB), BF16),
            pltpu.VMEM((MOST * QB, TOPK * QB), BF16),
            pltpu.VMEM((ALLW, D), F32),
            pltpu.VMEM((1, D), F32),
            pltpu.VMEM((WO_ROW + 8, 128), F32),
            pltpu.VMEM((WO_ROW + 8, 128), BF16),
            pltpu.SemaphoreType.DMA((1,)),
        ],
        out_shape=[struct((count, D)), struct(flat.shape, BF16)],
        input_output_aliases={16: 1},
        compiler_params=params_for(56),
        name="head_backward",
        cost_estimate=pl.CostEstimate(flops=30_000_000_000, bytes_accessed=24_000_000, transcendentals=0),
    )(
        segments, tokens, gain, wall, routes_t, start, queries, datt, lse, delta, kv, kvt, dlogits, dres,
        dgain_two, extra, flat,
    )


class Mesh3:
    def __init__(self, shards, over):
        shard = lax.axis_index("dp")
        other = lax.axis_index("fsdp")
        self.over = over
        self.many = shards * over
        self.sizes = {"x": 2, "y": shards // 2, "z": over // 2}
        self.here = {"x": lax.rem(other, 2), "y": lax.div(shard, 2), "z": lax.div(other, 2)}
        self.core = lax.rem(shard, 2)
        self.me = shard * over + other
        self.partner = (shard + 1 - 2 * self.core, other)

    def at_z(self, z):
        same = copy.copy(self)
        if z is not None:
            same.here = dict(self.here, z=z)
        return same

    def spots(self):
        x, y, z = (self.sizes[axis] for axis in "xyz")
        return list(itertools.product(range(x), range(y), range(1 - z, z)))

    def round_spots(self):
        return list(itertools.product(*[range(self.sizes[axis]) for axis in "xyz"]))

    def exists(self, z_steps):
        place = self.here["z"] + z_steps
        if isinstance(place, int):
            return 0 <= place < self.sizes["z"]
        return (place >= 0) & (place < self.sizes["z"])

    def device(self, core, spot):
        size = self.sizes["z"]
        x = lax.rem(self.here["x"] + spot[0], self.sizes["x"])
        y = lax.rem(self.here["y"] + spot[1], self.sizes["y"])
        z = self.here["z"] + spot[2]
        z = z % size if isinstance(z, int) else lax.rem(z + size, size)
        return (y * 2 + core, z * 2 + x)

    def number(self, core, spot):
        shard, other = self.device(core, spot)
        return shard * self.over + other

    def greet(self, devices):
        barrier = pltpu.get_barrier_semaphore()
        for device in devices:
            pl.semaphore_signal(barrier, inc=1, device_id=device, device_id_type=MESH)
        pl.semaphore_wait(barrier, len(devices))

    def near(self):
        steps = [at(axis, step) for axis in "xyz" for step in range(1, self.sizes[axis])]
        return [self.device(self.core, step) for step in steps] + [self.partner]

    def column(self):
        steps = [(core, step) for core in range(2) for step in range(self.sizes["z"]) if core or step]
        return [self.device(lax.rem(self.core + core, 2), (0, 0, step)) for core, step in steps]

    def layer(self):
        steps = [(x, y, 0) for x in range(self.sizes["x"]) for y in range(self.sizes["y"]) if x or y]
        return [self.device(self.core, step) for step in steps]


def at(axis, step):
    return tuple(step if one == axis else 0 for one in "xyz")


def last_axis(axes, spot):
    return max([i for i, axis in enumerate(axes) if spot["xyz".index(axis)]], default=-1)


def pieces_of(window):
    if window < 512:
        return [(0, window)]
    first = (window // 16 + 1) // 2 * 16
    return [(0, first), (first, window - first)]


def act(condition, action):
    if condition is True:
        action()
    elif condition is not False:
        pl.when(condition)(action)


GATHER_AXES = (("zxy", "yzx"), ("zyx", "xzy"))
REDUCE_AXES = ("zxy", "zyx")


def onward(mesh, axes, spot):
    last = last_axis(axes, spot)
    steps = []
    if last >= 0 and axes[last] == "z":
        steps.append(("z", -1 if spot[2] > 0 else 1))
    for axis in axes[last + 1 :]:
        steps += [("z", 1), ("z", -1)] if axis == "z" else [
            (axis, one) for one in range(1, mesh.sizes[axis])
        ]
    return steps


def gather_own_core(mesh, core, land, send_sem, recv_sem, begin):
    window = land.shape[1]
    pieces = pieces_of(window)
    slots = {}
    events = []

    def moved(owner, device, slot, p):
        rows = pl.ds(*pieces[p])
        return pltpu.make_async_remote_copy(
            src_ref=land.at[owner, rows],
            dst_ref=land.at[owner, rows],
            send_sem=send_sem.at[slot, p],
            recv_sem=recv_sem.at[owner, p],
            device_id=device,
            device_id_type=MESH,
        )

    for spot in mesh.spots():
        there = mesh.exists(spot[2])
        if there is False:
            continue
        owner = mesh.number(core, spot)
        turn = 0.5 * abs(spot[2]) + (spot[0] > 0) + (spot[1] > 0) + (0.001 if spot[2] < 0 else 0)
        for p in range(len(pieces)):
            sends = []
            for axis, step in onward(mesh, GATHER_AXES[core][p], spot):
                key = (spot[0], spot[1], spot[2] % mesh.sizes["z"], axis, step)
                away = mesh.exists(step) if axis == "z" else True
                if away is not False:
                    slot = slots.setdefault(key, len(slots))
                    sends.append((mesh.device(core, at(axis, step)), slot, away))
            key = (spot[0], spot[1], spot[2] % mesh.sizes["z"])
            sends.append((mesh.partner, slots.setdefault(key, len(slots)), True))

            def come(owner=owner, spot=spot, p=p, sends=sends):
                if any(spot):
                    moved(owner, mesh.partner, 0, p).wait_recv()
                for device, slot, away in sends:
                    act(away, moved(owner, device, slot, p).start)

            def done(owner=owner, p=p, sends=sends):
                for _, slot, away in sends:
                    act(away, moved(owner, mesh.partner, slot, p).wait_send)

            events.append((turn + 0.01 * p, there, come if begin else done))
    for _, there, action in sorted(events, key=lambda one: one[0]):
        act(there, action)


def gather_blocks(mesh, land, send_sem, recv_sem, begin):
    known = range(mesh.sizes["z"]) if mesh.sizes["z"] <= 4 else [None]
    for core in range(2):
        for z in known:

            @pl.when((mesh.core == core) & (True if z is None else mesh.here["z"] == z))
            def _(core=core, z=z):
                gather_own_core(mesh.at_z(z), core, land, send_sem, recv_sem, begin)


def each_owner(mesh, core, action):
    def one(number, carry):
        shard = 2 * lax.div(number, mesh.over) + core
        action(shard * mesh.over + lax.rem(number, mesh.over))
        return carry

    lax.fori_loop(0, mesh.many // 2, one, 0)


def reduce_blocks(mesh, core, source, mine, outgo, income, send_sem, recv_sem, total_ref):
    pieces = pieces_of(outgo.shape[1])
    half = mesh.many // 2
    held = {spot: i for i, spot in enumerate(mesh.round_spots())}

    def across(kind, spot):
        slot = held[spot]
        return pltpu.make_async_remote_copy(
            src_ref=source(mesh.number(kind, spot)),
            dst_ref=income.at[slot],
            send_sem=send_sem.at[slot, 0],
            recv_sem=recv_sem.at[slot, 0],
            device_id=mesh.partner,
            device_id_type=MESH,
        )

    def moved(spot, p, device):
        rows = pl.ds(*pieces[p])
        slot = half + held[spot]
        return pltpu.make_async_remote_copy(
            src_ref=outgo.at[held[spot], rows],
            dst_ref=income.at[slot, rows],
            send_sem=send_sem.at[slot, p],
            recv_sem=recv_sem.at[slot, p],
            device_id=device,
            device_id_type=MESH,
        )

    def far(spot):
        z = {0: 0, 1: 3, 2: 5, 3: 8}.get(spot[2], 2 * spot[2] + 2)
        return z + 2 * (spot[0] > 0) + 2 * (spot[1] > 0)

    for spot in sorted(held, key=far, reverse=True):
        across(1 - core, spot).start()
    axes = REDUCE_AXES[core]
    order = sorted(itertools.product(held, range(len(pieces))), key=lambda one: one[1] - 2 * far(one[0]))
    for spot, p in order:
        if p == 0:
            across(core, spot).wait_recv()
        rows = pl.ds(*pieces[p])
        total = mine(mesh.number(core, spot), *pieces[p]) + income[held[spot], rows].astype(F32)
        last = last_axis(axes, spot)
        for axis in axes[last + 1 :]:
            size = mesh.sizes[axis]
            for step in range(1, size):
                child = tuple(one or other for one, other in zip(spot, at(axis, size - step)))
                moved(child, p, mesh.partner).wait_recv()
                total = total + income[half + held[child], rows].astype(F32)
        if last < 0:
            total_ref[rows, :] = total
        else:
            outgo[held[spot], rows] = total.astype(BF16)
            step = spot["xyz".index(axes[last])]
            moved(spot, p, mesh.device(core, at(axes[last], step))).start()
    for spot, p in order:
        if p == 0:
            across(1 - core, spot).wait_send()
        if any(spot):
            moved(spot, p, mesh.partner).wait_send()


def reduce_line(mesh, core, source, mine, outgo, income, send_sem, recv_sem, total_ref):
    window = outgo.shape[1]
    pieces = pieces_of(window)
    half = mesh.many // 2
    spots = [spot for spot in mesh.spots() if mesh.exists(spot[2])]
    around = {spot: i for i, spot in enumerate(mesh.round_spots())}
    held = {spot: around[spot[0], spot[1], spot[2] % mesh.sizes["z"]] for spot in spots}
    inward = {spot: half + i for i, spot in enumerate(one for one in mesh.spots() if any(one))}

    def across(kind, spot):
        slot = held[spot]
        return pltpu.make_async_remote_copy(
            src_ref=source(mesh.number(kind, spot)),
            dst_ref=income.at[slot],
            send_sem=send_sem.at[slot, 0],
            recv_sem=recv_sem.at[slot, 0],
            device_id=mesh.partner,
            device_id_type=MESH,
        )

    def moved(src, spot, p, device):
        rows = pl.ds(*pieces[p])
        slot = inward[spot]
        return pltpu.make_async_remote_copy(
            src_ref=outgo.at[src, rows],
            dst_ref=income.at[slot, rows],
            send_sem=send_sem.at[slot, p],
            recv_sem=recv_sem.at[slot, p],
            device_id=device,
            device_id_type=MESH,
        )

    def far(one):
        spot, p = one
        return 0.75 * abs(spot[2]) + (spot[0] > 0) + (spot[1] > 0) + 0.3 * p

    order = sorted(itertools.product(spots, range(len(pieces))), key=far, reverse=True)
    for spot, p in order:
        if p == 0:
            across(1 - core, spot).start()
    ready = set()
    for spot, p in order:
        if spot not in ready:
            ready.add(spot)
            across(core, spot).wait_recv()
        rows = pl.ds(*pieces[p])
        axes = GATHER_AXES[core][p]
        total = mine(mesh.number(core, spot), *pieces[p]) + income[held[spot], rows].astype(F32)
        for axis, step in onward(mesh, axes, spot):
            if axis == "z":
                if not mesh.exists(step):
                    continue
                child = (spot[0], spot[1], spot[2] - step)
            else:
                back = at(axis, mesh.sizes[axis] - step)
                child = tuple(one or other for one, other in zip(spot, back))
            moved(0, child, p, mesh.partner).wait_recv()
            total = total + income[inward[child], rows].astype(F32)
        last = last_axis(axes, spot)
        if last < 0:
            total_ref[rows, :] = total
            continue
        outgo[held[spot], rows] = total.astype(BF16)
        step = spot["xyz".index(axes[last])]
        if axes[last] == "z":
            step = 1 if step > 0 else -1
        moved(held[spot], spot, p, mesh.device(core, at(axes[last], step))).start()
    for spot, p in order:
        if p == 0:
            across(1 - core, spot).wait_send()
        if any(spot):
            moved(held[spot], spot, p, mesh.partner).wait_send()


def sum_all(mesh, mine, stats, send_sem, recv_sem):
    column = mesh.sizes["z"] * 2
    layer = mesh.sizes["x"] * mesh.sizes["y"]
    groups = (
        (0, column, mesh.here["z"] * 2 + mesh.core, mesh.column()),
        (column, layer, mesh.here["x"] * mesh.sizes["y"] + mesh.here["y"], mesh.layer()),
    )
    total = mine
    for base, size, here, devices in groups:
        stats[base + here] = total

        def sent(j, device, base=base, here=here):
            return pltpu.make_async_remote_copy(
                src_ref=stats.at[base + here],
                dst_ref=stats.at[base + here],
                send_sem=send_sem.at[base + j],
                recv_sem=recv_sem.at[base + here],
                device_id=device,
                device_id_type=MESH,
            )

        def come(place, base=base):
            return pltpu.make_async_remote_copy(
                src_ref=stats.at[base + place],
                dst_ref=stats.at[base + place],
                send_sem=send_sem.at[base],
                recv_sem=recv_sem.at[base + place],
                device_id=mesh.partner,
                device_id_type=MESH,
            )

        for j, device in enumerate(devices):
            sent(j, device).start()
        for j in range(1, size):
            come(lax.rem(here + j, size)).wait_recv()
        for j, device in enumerate(devices):
            sent(j, device).wait_send()
        total = stats[base]
        for place in range(1, size):
            total = total + stats[base + place]
    return total


def window_rows(shard_size, many):
    units = [(shard_size * d) // UNIT for d in range(many + 1)]
    return 16 * (max(b - a for a, b in zip(units, units[1:])) + 1)


def first_row(shard_size, number):
    if isinstance(number, int):
        return number * shard_size // UNIT * 16
    return pl.multiple_of(lax.div(number * shard_size, UNIT) * 16, 16)


def inner_units(shard_size, many):
    units = [(shard_size * d) // UNIT for d in range(many + 1)]
    return min(b - a for a, b in zip(units, units[1:]))


def lay_inner(shard_size, many, land, flat, owner):
    count = 16 * inner_units(shard_size, many) - 16
    row = pl.multiple_of(first_row(shard_size, owner) + 16, 16)
    flat[pl.ds(row, count), :] = land[owner, pl.ds(16, count), :].astype(F32)


def lay_edges(shard_size, many, land, flat):
    inner = 16 * inner_units(shard_size, many)
    flat[0:16, :] = jnp.zeros((16, 128), F32)

    def lay(number, carry):
        row = first_row(shard_size, number)
        after = first_row(shard_size, number + 1)
        flat[pl.ds(row, 16), :] += land[number, 0:16, :].astype(F32)
        tail = land[number, pl.ds(inner, 16), :].astype(F32)
        flat[pl.ds(pl.multiple_of(row + inner, 16), 16), :] = tail
        last = pl.multiple_of(after - row, 16)
        flat[pl.ds(after, 16), :] = land[number, pl.ds(last, 16), :].astype(F32)
        return carry

    lax.fori_loop(0, many, lay, 0)


def early_matrices(flat, wall_ref, gain_one_ref, gain_two_ref):
    for c in range(D // 128):
        lanes = slice(c * 128, (c + 1) * 128)
        gain_one_ref[:, lanes] = flat[c : c + 1, :]
        gain_two_ref[:, lanes] = flat[4 + c : 5 + c, :]
    for c in range(QW // 128):
        wall_ref[c * 128 : (c + 1) * 128, :] = flat[pl.ds(WQ_ROW + c, D, stride=12), :].T.astype(BF16)
    for first, row in ((KROW, WK_ROW), (VROW, WV_ROW)):
        pair = flat[row : row + 256, :].T.astype(BF16)
        wall_ref[first : first + H, :] = (
            nn(pair[:H], picks(256, 2, 0).astype(BF16)) + nn(pair[H:], picks(256, 2, 1).astype(BF16))
        ).astype(BF16)
    across = jnp.concatenate(
        [flat[pl.ds(WR_ROW + j, 32, stride=3), :] for j in range(3)], axis=1
    ).T.astype(BF16)
    router_t = jnp.zeros((E, D), F32)
    for part in range(16):
        router_t = router_t + nn(across[part * E : (part + 1) * E, :], picks(32, 16, part).astype(BF16))
    wall_ref[RROW:ALLW, :] = jnp.concatenate(
        [router_t, jnp.zeros((ALLW - RROW - E, D), F32)], axis=0
    ).astype(BF16)


def gather_kernel(
    mesh, shard_size, own_ref,
    wall_out, gain_one_ref, gain_two_ref, wo_out, w1_out, w2_out,
    land, flat, wall_ref, wo_ref, w1_ref, w2_ref, send_sem, recv_sem, out_sem,
):
    mesh = mesh()
    many = mesh.many
    mesh.greet(mesh.near())
    land[mesh.me] = own_ref[...]
    gather_blocks(mesh, land, send_sem, recv_sem, True)
    each_owner(mesh, mesh.core, functools.partial(lay_inner, shard_size, many, land, flat))

    def arrive(owner):
        for p in range(recv_sem.shape[1]):
            rows = pl.ds(*pieces_of(own_ref.shape[0])[p])
            pltpu.make_async_remote_copy(
                src_ref=land.at[owner, rows],
                dst_ref=land.at[owner, rows],
                send_sem=send_sem.at[0, p],
                recv_sem=recv_sem.at[owner, p],
                device_id=mesh.partner,
                device_id_type=MESH,
            ).wait_recv()
        lay_inner(shard_size, many, land, flat, owner)

    each_owner(mesh, 1 - mesh.core, arrive)
    lay_edges(shard_size, many, land, flat)
    copies = []

    def leave(matrix, out):
        one = pltpu.make_async_copy(matrix, out, out_sem.at[len(copies)])
        one.start()
        copies.append(one)

    for c in range(D // 128):
        wo_ref[:, c * 128 : (c + 1) * 128] = flat[pl.ds(WO_ROW + c, QW, stride=4), :].astype(BF16)
    leave(wo_ref, wo_out)
    for c in range(D // 128):
        w2_ref[:, c * 128 : (c + 1) * 128] = flat[pl.ds(W2_ROW + c, FF, stride=4), :].astype(BF16)
    leave(w2_ref, w2_out)
    for c in range(FF // 128):
        w1_ref[:, c * 128 : (c + 1) * 128] = flat[pl.ds(W1_ROW + c, D, stride=16), :].astype(BF16)
    leave(w1_ref, w1_out)
    early_matrices(flat, wall_ref, gain_one_ref, gain_two_ref)
    leave(wall_ref, wall_out)
    gather_blocks(mesh, land, send_sem, recv_sem, False)
    for one in copies:
        one.wait()


def gather_weights(shards, over, shard_size, own):
    window = own.shape[0]
    many = shards * over
    rows = (shard_size * (many - 1)) // UNIT * 16 + window
    vmem = pl.BlockSpec(memory_space=pltpu.VMEM)
    hbm = pl.BlockSpec(memory_space=pl.ANY)
    mesh = functools.partial(Mesh3, shards, over)
    pieces = len(pieces_of(window))
    return pl.pallas_call(
        functools.partial(gather_kernel, mesh, shard_size),
        in_specs=[vmem],
        out_specs=[hbm, vmem, vmem, hbm, hbm, hbm],
        out_shape=[
            struct((ALLW, D), BF16),
            struct((1, D)),
            struct((1, D)),
            struct((QW, D), BF16),
            struct((D, FF), BF16),
            struct((FF, D), BF16),
        ],
        scratch_shapes=[
            pltpu.VMEM((many, window, 128), BF16),
            pltpu.VMEM((rows, 128), F32),
            pltpu.VMEM((ALLW, D), BF16),
            pltpu.VMEM((QW, D), BF16),
            pltpu.VMEM((D, FF), BF16),
            pltpu.VMEM((FF, D), BF16),
            pltpu.SemaphoreType.DMA((5 * many // 2, pieces)),
            pltpu.SemaphoreType.DMA((many, pieces)),
            pltpu.SemaphoreType.DMA((4,)),
        ],
        compiler_params=pltpu.CompilerParams(
            collective_id=0, has_side_effects=True, vmem_limit_bytes=60 * MIB
        ),
        name="gather_weights",
    )(own)


def reduce_kernel(
    mesh, shard_size, flat_ref, count_ref,
    out_ref, total_ref, gain_ref,
    part, outgo, income, stats, part_sem, send_sem, recv_sem, stat_send, stat_recv,
):
    mesh = mesh()
    window = out_ref.shape[0]
    span = part.shape[1]

    def source(owner):
        return flat_ref.at[pl.ds(first_row(shard_size, owner), window), :]

    def fetch(y):
        first = first_row(shard_size, (2 * y + mesh.core) * mesh.over)
        return pltpu.make_async_copy(flat_ref.at[pl.ds(first, span), :], part.at[y], part_sem.at[y])

    def mine(owner, first, rows):
        shard = lax.div(owner, mesh.over)
        row = first_row(shard_size, owner) - first_row(shard_size, shard * mesh.over) + first
        return part[lax.div(shard, 2), pl.ds(pl.multiple_of(row, 16), rows), :].astype(F32)

    for y in range(mesh.sizes["y"]):
        fetch(y).start()
    mesh.greet(mesh.column() + mesh.layer())
    for y in range(mesh.sizes["y"]):
        fetch(y).wait()
    buffers = (source, mine, outgo, income, send_sem, recv_sem, out_ref)
    for core in range(2):
        if mesh.sizes["z"] > 4:
            pl.when(mesh.core == core)(functools.partial(reduce_blocks, mesh, core, *buffers))
            continue
        for z in range(mesh.sizes["z"]):
            pl.when((mesh.core == core) & (mesh.here["z"] == z))(
                functools.partial(reduce_line, mesh.at_z(z), core, *buffers)
            )

    total = out_ref[...]
    begin = mesh.me * shard_size - lax.div(mesh.me * shard_size, UNIT) * UNIT
    place = (
        lax.broadcasted_iota(jnp.int32, (window, 128), 0) * 128
        + lax.broadcasted_iota(jnp.int32, (window, 128), 1)
    )
    inside = jnp.where((place >= begin) & (place < begin + shard_size), total, 0.0)
    squares = jnp.sum(jnp.sum(inside * inside, axis=0, keepdims=True), axis=1, keepdims=True)
    lane = lax.broadcasted_iota(jnp.int32, (8, 128), 1)
    row = jnp.where(lane == E, squares, count_ref[...])
    gains = jnp.where(mesh.me == 0, total[0:8, :], 0.0)
    summed = sum_all(mesh, jnp.concatenate([row, gains], axis=0), stats, stat_send, stat_recv)
    total_ref[...] = summed[0:1, :]
    gain_ref[...] = summed[8:16, :]


def reduce_grads(shards, over, shard_size, window, flat, counts):
    vmem = pl.BlockSpec(memory_space=pltpu.VMEM)
    many = shards * over
    mesh = functools.partial(Mesh3, shards, over)
    pieces = len(pieces_of(window))
    incomes = many // 2 + 2 * (shards // 2) * (over - 1)
    steps = over + shards
    units = [(shard_size * d) // UNIT for d in range(many)]
    span = 16 * max(units[d + over - 1] - units[d] for d in range(0, many, over)) + window
    return pl.pallas_call(
        functools.partial(reduce_kernel, mesh, shard_size),
        in_specs=[pl.BlockSpec(memory_space=pl.ANY), vmem],
        out_specs=[vmem] * 3,
        out_shape=[struct((window, 128)), struct((1, 128)), struct((8, 128))],
        scratch_shapes=[
            pltpu.VMEM((shards // 2, span, 128), BF16),
            pltpu.VMEM((many // 2, window, 128), BF16),
            pltpu.VMEM((incomes, window, 128), BF16),
            pltpu.VMEM((steps, 16, 128), F32),
            pltpu.SemaphoreType.DMA((shards // 2,)),
            pltpu.SemaphoreType.DMA((incomes, pieces)),
            pltpu.SemaphoreType.DMA((incomes, pieces)),
            pltpu.SemaphoreType.DMA((steps,)),
            pltpu.SemaphoreType.DMA((steps,)),
        ],
        compiler_params=pltpu.CompilerParams(
            collective_id=1, has_side_effects=True, vmem_limit_bytes=56 * MIB
        ),
        name="reduce_grads",
    )(flat, counts)


def local_step(flat_rows, tokens, grad_out, routes, segments, weights):
    wall, gain_one, gain_two, wo, w1, w2 = weights
    queries, attended, gates, lse, kv, kvt, start, routes_t, counts = head_forward(
        tokens, routes.T, segments, wall, gain_one
    )
    output, dres, datt, delta, dlogits, flat, extra, dgain_two = middle(
        flat_rows, tokens, grad_out, gain_two, wo, w1, w2, routes_t, gates, attended
    )
    input_grad, flat = head_backward(
        segments, tokens, gain_one, wall, routes_t, start, queries, datt, lse, delta, kv, kvt, dlogits, dres,
        dgain_two, extra, flat,
    )
    return output, input_grad, flat, counts


def per_device(
    shards, over, tokens, grad_out, routes, segments, params, first_moment, second_moment, ema_weights
):
    shard_size = params.shape[0]
    window = window_rows(shard_size, shards * over)
    flat_rows = (shard_size * (shards * over - 1)) // UNIT * 16 + window + 16
    me = lax.axis_index("dp") * over + lax.axis_index("fsdp")
    begin = lax.rem(me * shard_size, UNIT)
    own = lax.dynamic_slice(
        jnp.pad(params.astype(BF16), (UNIT, window * 128 - shard_size)), (UNIT - begin,), (window * 128,)
    ).reshape(window, 128)
    wall, gain_one, gain_two, wo, w1, w2 = gather_weights(shards, over, shard_size, own)
    output, input_grad, flat, counts = local_step(
        flat_rows, tokens, grad_out, routes, segments, (wall, gain_one, gain_two, wo, w1, w2)
    )
    reduced, sums, gain_grads = reduce_grads(shards, over, shard_size, window, flat, counts)
    grad_shard = lax.dynamic_slice(reduced.reshape(-1), (begin,), (shard_size,))
    total_tokens = tokens.shape[0] * shards * over
    expert_load = sums[0, :E] * (E / (total_tokens * TOPK))
    grad_norm = jnp.sqrt(sums[0, E])
    clipped = grad_shard * (CLIP_LIMIT / jnp.maximum(grad_norm, CLIP_LIMIT))
    new_first = BETA_FIRST * first_moment + (1.0 - BETA_FIRST) * clipped
    new_second = BETA_SECOND * second_moment + (1.0 - BETA_SECOND) * clipped * clipped
    first_hat = new_first / (1.0 - BETA_FIRST**STEP)
    second_hat = new_second / (1.0 - BETA_SECOND**STEP)
    new_params = params * (1.0 - LEARN_RATE * DECAY_RATE) - LEARN_RATE * first_hat / (
        jnp.sqrt(second_hat) + ADAM_EPS
    )
    new_ema = EMA_KEEP * ema_weights + (1.0 - EMA_KEEP) * new_params
    return (
        output,
        input_grad,
        expert_load,
        grad_norm.reshape(1),
        new_params,
        new_first,
        new_second,
        new_ema,
        gain_grads.reshape(2, D),
    )


def solution(mesh):
    row = P(("dp", "fsdp"), None)
    flat = P(("dp", "fsdp"))
    return jax.shard_map(
        functools.partial(per_device, mesh.shape["dp"], mesh.shape["fsdp"]),
        mesh=mesh,
        in_specs=(row, row, row, row, flat, flat, flat, flat),
        out_specs=(row, row, P(), P(), flat, flat, flat, flat, P()),
        check_vma=False,
    )
```

```python
import copy
import functools
import itertools

import jax
import jax.numpy as jnp
from jax import lax
from jax.experimental import pallas as pl
from jax.experimental.pallas import tpu as pltpu
from jax.sharding import PartitionSpec as P

D = 512
E = 24
TOPK = 8
H = 64
FF = 2048
STEP = 10

NORM_EPS = 1e-06
CLIP_LIMIT = 1.0
BETA_FIRST = 0.9
BETA_SECOND = 0.95
LEARN_RATE = 0.1
DECAY_RATE = 0.1
ADAM_EPS = 1e-08
EMA_KEEP = 0.9
NEG_LARGE = -1e30

QW = E * H
KROW = QW
VROW = QW + H
RROW = QW + 2 * H
ALLW = 1696
LEN = 1024
TB = 512
NB = LEN // TB
QB = 128
SIDE = 8
MOST = 512 // QB + 1
SORT_STEPS = (
    (0, 1), (2, 3), (4, 5), (6, 7), (0, 2), (1, 3), (4, 6), (5, 7), (1, 2), (5, 6),
    (0, 4), (1, 5), (2, 6), (3, 7), (2, 4), (3, 5), (1, 2), (3, 4), (5, 6),
)
FC = 512
MB = 512
MIB = 1 << 20

WR_ROW = 8
WK_ROW = 104
WV_ROW = 360
WQ_ROW = 616
WO_ROW = 6760
W1_ROW = 12904
W2_ROW = 21096
ALL_ROWS = 29288
UNIT = 16 * 128
MESH = pl.DeviceIdType.MESH

F32 = jnp.float32
BF16 = jnp.bfloat16


def nn(a, b):
    return lax.dot_general(a, b, (((1,), (0,)), ((), ())), preferred_element_type=F32)


def nt(a, b):
    return lax.dot_general(a, b, (((1,), (1,)), ((), ())), preferred_element_type=F32)


def tn(a, b):
    return lax.dot_general(a, b, (((0,), (0,)), ((), ())), preferred_element_type=F32)


def rms_scale(values):
    return lax.rsqrt(jnp.mean(values * values, axis=-1, keepdims=True) + NORM_EPS)


def slot_of(routes, k, rows):
    return jnp.broadcast_to(routes[k : k + 1, :], (rows, routes.shape[1]))


def expert_rows(routes, k):
    return jnp.broadcast_to(routes.astype(jnp.int16)[k : k + 1, :], (16, routes.shape[1]))


def pick_heads(routes, source_ref, k):
    tokens = routes.shape[1]
    route = expert_rows(routes, k)
    taken = source_ref[k * H : (k + 1) * H, :].reshape(H // 16, 16, tokens)
    for e in range(k + 1, k + E - TOPK + 1):
        piece = source_ref[e * H : (e + 1) * H, :].reshape(H // 16, 16, tokens)
        taken = jnp.where((route == jnp.int16(e))[None], piece, taken)
    return taken.reshape(H, tokens)


def place_heads(routes, source_ref, target_ref):
    tokens = routes.shape[1]
    rows = [expert_rows(routes, k) for k in range(TOPK)]
    for e in range(E):
        total = jnp.zeros((H // 16, 16, tokens), BF16)
        for k in range(max(0, e - (E - TOPK)), min(TOPK - 1, e) + 1):
            piece = source_ref[k * H : (k + 1) * H, :].reshape(H // 16, 16, tokens)
            total = jnp.where((rows[k] == jnp.int16(e))[None], piece, total)
        target_ref[e * H : (e + 1) * H, :] = total.reshape(H, tokens)


def sorted_rows(rows):
    rows = list(rows)
    for one, two in SORT_STEPS:
        rows[one], rows[two] = jnp.minimum(rows[one], rows[two]), jnp.maximum(rows[one], rows[two])
    return rows


def key_mask(first_key, first_query, rows, start_row):
    keys = lax.broadcasted_iota(jnp.int32, (rows, QB), 0) + first_key
    queries = lax.broadcasted_iota(jnp.int32, (rows, QB), 1) + first_query
    mask = (keys <= queries) & (keys >= start_row)
    return jnp.concatenate([mask] * SIDE, axis=1)


def group_of(ref, k, lanes):
    return jnp.concatenate([ref[i * H : (i + 1) * H, lanes] for i in range(k, k + SIDE)], axis=1)


def row_group(ref, k, lanes):
    return jnp.concatenate([ref[i : i + 1, lanes] for i in range(k, k + SIDE)], axis=1)


def by_span(attend, row, place, segment_ref):
    def one(j, carry):
        block = place * (TB // QB) + j
        first = block * QB
        span = jnp.int32(1)
        for back in range(MOST - 1):
            last = first - back * QB - 1
            same = segment_ref[row, jnp.maximum(last, 0)] == segment_ref[row, first]
            span = span + jnp.where((last >= 0) & same, 1, 0)
        for blocks in range(1, MOST + 1):

            @pl.when(span == blocks)
            def _(blocks=blocks):
                attend(pl.ds(pl.multiple_of(j * QB, QB), QB), block, blocks)

        return carry

    lax.fori_loop(0, TB // QB, one, 0)


def head_forward_kernel(
    steps, segment_smem, x_ref, route_ref, segment_ref, wall_ref, gain_ref,
    q_ref, att_ref, gate_ref, lse_ref, kv_ref, kvt_ref, start_ref, sorted_ref, count_ref,
    all_scr, low_scr, k_scr, vt_scr, count_scr,
):
    step = pl.program_id(0)
    place = lax.rem(step, NB)
    here = pl.multiple_of(place * TB, TB)

    @pl.when(step == 0)
    def _():
        count_scr[...] = jnp.zeros_like(count_scr)

    row = segment_ref[pl.ds(lax.div(step, NB), 1), :]
    segments = segment_ref[pl.ds(lax.div(step, NB), 1), pl.ds(here, TB)]
    start = jnp.zeros((1, TB), jnp.int32)
    for number in range(1, 4):
        below = jnp.sum((row < number).astype(jnp.int32), axis=1, keepdims=True)
        start = jnp.where(segments == number, below, start)
    start_ref[...] = start
    x = x_ref[...].astype(F32)
    normed = (x * rms_scale(x) * gain_ref[...]).astype(BF16)
    all_scr[...] = nt(wall_ref[...], normed)
    kt = all_scr[KROW : KROW + H, :]
    vt = all_scr[VROW : VROW + H, :]
    logits = all_scr[RROW : RROW + E, :]
    kvt = jnp.concatenate([kt, vt], axis=0)
    kv = kvt.T.astype(BF16)
    kv_ref[...] = kv
    kvt_ref[...] = kvt.astype(BF16)
    k_scr[pl.ds(here, TB), :] = kv[:, :H]
    vt_scr[:, pl.ds(here, TB)] = vt.astype(BF16)
    routes = jnp.concatenate(sorted_rows(route_ref[k : k + 1, :] for k in range(TOPK)), axis=0)
    sorted_ref[...] = routes
    experts = lax.broadcasted_iota(jnp.int32, (E, TB), 0)
    chosen = []
    counts = count_scr[...]
    for k in range(TOPK):
        named = slot_of(routes, k, E) == experts
        chosen.append(jnp.sum(jnp.where(named, logits, 0.0), axis=0, keepdims=True))
        counts = counts + named.astype(F32)
    count_scr[...] = counts
    chosen = jnp.concatenate(chosen, axis=0)
    raised = jnp.exp(chosen - jnp.max(chosen, axis=0, keepdims=True))
    gate_ref[...] = raised / jnp.sum(raised, axis=0, keepdims=True)
    low_scr[...] = all_scr[0:QW, :].astype(BF16)
    for k in range(TOPK):
        q_ref[k * H : (k + 1) * H, :] = pick_heads(routes, low_scr, k) * jnp.asarray(H ** (-0.5), BF16)

    def attend(lanes, block, blocks):
        rows = blocks * QB
        first_key = pl.multiple_of((block - (blocks - 1)) * QB, QB)
        mask = key_mask(first_key, block * QB, rows, start_ref[:, lanes])
        keys = k_scr[pl.ds(first_key, rows), :]
        values = vt_scr[:, pl.ds(first_key, rows)]
        groups = [nn(keys, group_of(q_ref, 0, lanes))]
        for k in range(0, TOPK, SIDE):
            if k + SIDE < TOPK:
                groups.append(nn(keys, group_of(q_ref, k + SIDE, lanes)))
            scores = jnp.where(mask, groups[k // SIDE], NEG_LARGE)
            top = jnp.max(scores, axis=0, keepdims=True)
            raised = jnp.exp(scores - top)
            total = jnp.sum(raised, axis=0, keepdims=True)
            out = nn(values, (raised * (1.0 / total)).astype(BF16))
            lse = top + jnp.log(total)
            for side in range(SIDE):
                one = slice(side * QB, (side + 1) * QB)
                att_ref[(k + side) * H : (k + side + 1) * H, lanes] = out[:, one]
                lse_ref[k + side : k + side + 1, lanes] = lse[:, one]

    by_span(attend, lax.div(step, NB), place, segment_smem)

    @pl.when(step == steps - 1)
    def _():
        held = jnp.sum(count_scr[...], axis=1, keepdims=True)
        lane = lax.broadcasted_iota(jnp.int32, (E, 128), 1)
        row = lax.broadcasted_iota(jnp.int32, (E, 128), 0)
        count_ref[...] = jnp.sum(jnp.where(lane == row, held, 0.0), axis=0, keepdims=True)


def picks(rows, stride, first):
    at = lax.broadcasted_iota(jnp.int32, (rows, D), 1)
    row = lax.broadcasted_iota(jnp.int32, (rows, D), 0)
    return (at == row * stride + first).astype(F32)


def exact(product, a, b):
    return lax.dot_general(
        a, b, (product, ((), ())), precision=lax.Precision.HIGHEST, preferred_element_type=F32
    )


def gelu_parts(v):
    cdf = 0.5 + 0.5 * lax.erf(v * 0.7071067811865476)
    return cdf, jnp.exp(v * v * -0.5) * 0.3989422804014327


def middle_kernel(
    x_ref, dy_ref, gain_ref, wo_ref, w1_ref, w2_ref, route_ref, gate_ref, att_ref,
    out_ref, dres_ref, datt_ref, delta_ref, dlogit_ref, flat_ref, extra_ref, dgain_ref,
    slot_scr, head_scr, mix_scr, hidden_scr, dpre_scr, dwo_ref, dw1_ref, dw2t_ref, rows_scr, low_scr, row_sem,
):
    step = pl.program_id(0)

    @pl.when(step == 0)
    def _():
        dwo_ref[...] = jnp.zeros_like(dwo_ref)
        dw1_ref[...] = jnp.zeros_like(dw1_ref)
        dw2t_ref[...] = jnp.zeros_like(dw2t_ref)
        dgain_ref[...] = jnp.zeros_like(dgain_ref)

    routes = route_ref[...]
    tokens = routes.shape[1]
    gates = gate_ref[...]
    for k in range(TOPK):
        rows = slice(k * H, (k + 1) * H)
        slot_scr[rows, :] = (gates[k : k + 1, :] * att_ref[rows, :]).astype(BF16)
    place_heads(routes, slot_scr, mix_scr)
    x = x_ref[...].astype(F32)
    dy = dy_ref[...]
    mixed = mix_scr[...]
    residual = x + tn(mixed, wo_ref[...])
    scale = rms_scale(residual)
    gain = gain_ref[...]
    second = (residual * scale * gain).astype(BF16)
    second_t = second.T
    dy_t = dy.T
    pre = [nn(second, w1_ref[:, 0:FC])]
    back = [nt(dy, w2_ref[0:FC, :])]
    for i in range(FF // FC):
        here = slice(i * FC, (i + 1) * FC)
        if i + 1 < FF // FC:
            after = slice((i + 1) * FC, (i + 2) * FC)
            pre.append(nn(second, w1_ref[:, after]))
            back.append(nt(dy, w2_ref[after, :]))
        cdf, density = gelu_parts(pre[i])
        hidden_scr[:, here] = (pre[i] * cdf).astype(BF16)
        dpre_scr[:, here] = (back[i] * (cdf + pre[i] * density)).astype(BF16)
    dsecond = nt(dpre_scr[...], w1_ref[...])
    out_ref[...] = (residual + nn(hidden_scr[...], w2_ref[...])).astype(BF16)
    dw1_ref[...] += nn(second_t, dpre_scr[...])
    dw2t_ref[...] += nn(dy_t, hidden_scr[...])
    dgain_ref[...] += jnp.sum(dsecond * residual * scale, axis=0, keepdims=True)
    weighted = gain * dsecond
    dres = (
        dy.astype(F32)
        + scale * weighted
        - residual * (scale * scale * scale) * jnp.mean(weighted * residual, axis=-1, keepdims=True)
    )
    dres_ref[...] = dres
    branch = dres.astype(BF16)
    dwo_ref[...] += nn(mixed, branch)
    head_scr[...] = nt(wo_ref[...], branch).astype(BF16)
    dgates = []
    for k in range(TOPK):
        rows = slice(k * H, (k + 1) * H)
        dslot = pick_heads(routes, head_scr, k).astype(F32)
        attended = att_ref[rows, :]
        dgates.append(jnp.sum(dslot * attended, axis=0, keepdims=True))
        datt = (gates[k : k + 1, :] * dslot).astype(BF16)
        datt_ref[rows, :] = datt
        delta_ref[k : k + 1, :] = jnp.sum(datt.astype(F32) * attended, axis=0, keepdims=True)
    dgate = jnp.concatenate(dgates, axis=0)
    dchosen = gates * (dgate - jnp.sum(gates * dgate, axis=0, keepdims=True))
    experts = lax.broadcasted_iota(jnp.int32, (E, tokens), 0)
    dlogits = jnp.zeros((E, tokens), F32)
    for k in range(TOPK):
        dlogits = jnp.where(
            slot_of(routes, k, E) == experts,
            jnp.broadcast_to(dchosen[k : k + 1, :], (E, tokens)),
            dlogits,
        )
    dlogit_ref[...] = dlogits

    @pl.when(step == pl.num_programs(0) - 1)
    def _():
        for c in range(D // 128):
            lanes = slice(c * 128, (c + 1) * 128)
            rows_scr[pl.ds(c, QW, stride=4), :] = dwo_ref[:, lanes]
            rows_scr[pl.ds(W2_ROW - WO_ROW + c, FF, stride=4), :] = dw2t_ref[lanes, :].T
        for c in range(FF // 128):
            rows_scr[pl.ds(W1_ROW - WO_ROW + c, D, stride=16), :] = dw1_ref[:, c * 128 : (c + 1) * 128]
        extra_ref[...] = rows_scr[0:8, :]
        low_scr[...] = rows_scr[8:, :].astype(BF16)
        copy = pltpu.make_async_copy(
            low_scr, flat_ref.at[pl.ds(WO_ROW + 8, low_scr.shape[0]), :], row_sem.at[0]
        )
        copy.start()
        copy.wait()


def head_backward_kernel(
    segment_smem, x_ref, gain_ref, wall_ref, route_ref, start_ref, q_ref, datt_ref,
    lse_ref, delta_ref, kv_ref, kvt_ref, dlogit_ref, dres_ref, dgain_two_ref, extra_ref, flat_in,
    dx_ref, flat_ref,
    dk_scr, dv_scr, dq_scr, dall_scr, prob_scr, dscore_scr, dwall_ref, dgain_ref, rows_scr, low_scr, row_sem,
):
    step = pl.program_id(0)
    place = NB - 1 - lax.rem(step, NB)
    here = pl.multiple_of(place * TB, TB)

    @pl.when(step == 0)
    def _():
        dwall_ref[...] = jnp.zeros_like(dwall_ref)
        dgain_ref[...] = jnp.zeros_like(dgain_ref)

    @pl.when(lax.rem(step, NB) == 0)
    def _():
        dk_scr[...] = jnp.zeros_like(dk_scr)
        dv_scr[...] = jnp.zeros_like(dv_scr)

    def attend(lanes, block, blocks):
        rows = blocks * QB
        first_key = pl.multiple_of((block - (blocks - 1)) * QB, QB)
        mask = key_mask(first_key, block * QB, rows, start_ref[:, lanes])
        keys = kv_ref[pl.ds(first_key, rows), :H]
        values = kv_ref[pl.ds(first_key, rows), H:]
        keys_t = kvt_ref[:H, pl.ds(first_key, rows)]
        queries = [group_of(q_ref, k, lanes) for k in range(0, TOPK, SIDE)]
        datts = [group_of(datt_ref, k, lanes) for k in range(0, TOPK, SIDE)]
        scores = [nn(keys, queries[0])]
        dprobs = [nn(values, datts[0])]
        for i in range(TOPK // SIDE):
            if i + 1 < TOPK // SIDE:
                scores.append(nn(keys, queries[i + 1]))
                dprobs.append(nn(values, datts[i + 1]))
            k = i * SIDE
            wide = slice(k * QB, (k + SIDE) * QB)
            probs = jnp.exp(jnp.where(mask, scores[i], NEG_LARGE) - row_group(lse_ref, k, lanes))
            dscore = (probs * (dprobs[i] - row_group(delta_ref, k, lanes))).astype(BF16)
            prob_scr[0:rows, wide] = probs.astype(BF16)
            dscore_scr[0:rows, wide] = dscore
            dq = (nn(keys_t, dscore) * (H ** (-0.5))).astype(BF16)
            for side in range(SIDE):
                dq_scr[(k + side) * H : (k + side + 1) * H, lanes] = dq[:, side * QB : (side + 1) * QB]
        dv_scr[pl.ds(first_key, rows), :] += nt(prob_scr[0:rows, :], jnp.concatenate(datts, axis=1))
        dk_scr[pl.ds(first_key, rows), :] += nt(dscore_scr[0:rows, :], jnp.concatenate(queries, axis=1))

    by_span(attend, lax.div(step, NB), place, segment_smem)
    place_heads(route_ref[...], dq_scr, dall_scr)
    dkv = jnp.concatenate([dk_scr[pl.ds(here, TB), :], dv_scr[pl.ds(here, TB), :]], axis=1)
    dall_scr[KROW : KROW + 2 * H, :] = dkv.T.astype(BF16)
    dall_scr[RROW : RROW + 32, :] = jnp.concatenate(
        [dlogit_ref[...], jnp.zeros((32 - E, TB), F32)], axis=0
    ).astype(BF16)
    x = x_ref[...].astype(F32)
    scale = rms_scale(x)
    gain = gain_ref[...]
    normed = (x * scale * gain).astype(BF16)
    dall = dall_scr[...]
    dwall_ref[...] += nn(dall, normed)
    dnormed = tn(dall, wall_ref[...])
    dgain_ref[...] += jnp.sum(dnormed * x * scale, axis=0, keepdims=True)
    weighted = gain * dnormed
    dx_ref[...] = (
        dres_ref[...]
        + scale * weighted
        - x * (scale * scale * scale) * jnp.mean(weighted * x, axis=-1, keepdims=True)
    )

    @pl.when(step == pl.num_programs(0) - 1)
    def _():
        for c in range(D // 128):
            lanes = slice(c * 128, (c + 1) * 128)
            rows_scr[c : c + 1, :] = dgain_ref[:, lanes]
            rows_scr[4 + c : 5 + c, :] = dgain_two_ref[:, lanes]
        router_t = dwall_ref[RROW : RROW + E, :]
        across = jnp.concatenate(
            [exact(((1,), (1,)), router_t, picks(32, 16, b)) for b in range(16)], axis=0
        ).T
        for j in range(3):
            rows_scr[pl.ds(WR_ROW + j, 32, stride=3), :] = across[:, j * 128 : (j + 1) * 128]
        for first, row in ((KROW, WK_ROW), (VROW, WV_ROW)):
            part = dwall_ref[first : first + H, :]
            rows_scr[row : row + 256, :] = jnp.concatenate(
                [exact(((1,), (1,)), picks(256, 2, b), part) for b in range(2)], axis=1
            )
        for c in range(QW // 128):
            rows_scr[pl.ds(WQ_ROW + c, D, stride=12), :] = dwall_ref[c * 128 : (c + 1) * 128, :].T
        rows_scr[WO_ROW : WO_ROW + 8, :] = extra_ref[...]
        low_scr[...] = rows_scr[...].astype(BF16)
        copy = pltpu.make_async_copy(low_scr, flat_ref.at[pl.ds(0, WO_ROW + 8), :], row_sem.at[0])
        copy.start()
        copy.wait()


def whole(shape):
    return pl.BlockSpec(shape, lambda *_: (0,) * len(shape), pipeline_mode=pl.Buffered(1))


def kept(shape):
    return pl.BlockSpec(shape, lambda *_: (0,) * len(shape))


SMEM = pl.BlockSpec(memory_space=pltpu.SMEM)


def struct(shape, kind=F32):
    return jax.ShapeDtypeStruct(shape, kind)


def params_for(mib):
    return pltpu.CompilerParams(vmem_limit_bytes=mib * MIB)


def head_forward(tokens, routes_t, segments, wall, gain):
    count = tokens.shape[0]
    steps = count // TB
    across = lambda rows: pl.BlockSpec((rows, TB), lambda b: (0, b))
    down = lambda columns: pl.BlockSpec((TB, columns), lambda b: (b, 0))
    return pl.pallas_call(
        functools.partial(head_forward_kernel, steps),
        grid=(steps,),
        in_specs=[SMEM, down(D), across(TOPK), whole(segments.shape), whole((ALLW, D)), whole((1, D))],
        out_specs=[
            across(TOPK * H), across(TOPK * H), across(TOPK), across(TOPK), down(2 * H), across(2 * H),
            across(1), across(TOPK), whole((1, 128)),
        ],
        scratch_shapes=[
            pltpu.VMEM((ALLW, TB), F32),
            pltpu.VMEM((QW, TB), BF16),
            pltpu.VMEM((LEN, H), BF16),
            pltpu.VMEM((H, LEN), BF16),
            pltpu.VMEM((E, TB), F32),
        ],
        out_shape=[
            struct((TOPK * H, count), BF16),
            struct((TOPK * H, count)),
            struct((TOPK, count)),
            struct((TOPK, count)),
            struct((count, 2 * H), BF16),
            struct((2 * H, count), BF16),
            struct((1, count), jnp.int32),
            struct((TOPK, count), jnp.int32),
            struct((1, 128)),
        ],
        compiler_params=params_for(56),
        name="head_forward",
        cost_estimate=pl.CostEstimate(flops=10_000_000_000, bytes_accessed=16_000_000, transcendentals=0),
    )(segments, tokens, routes_t, segments, wall, gain)


def middle(flat_rows, tokens, grad_out, gain, wo, w1, w2, routes_t, gates, attended):
    count = tokens.shape[0]
    steps = count // MB
    across = lambda rows: pl.BlockSpec((rows, MB), lambda b: (0, b))
    down = lambda columns: pl.BlockSpec((MB, columns), lambda b: (b, 0))
    return pl.pallas_call(
        middle_kernel,
        grid=(steps,),
        in_specs=[
            down(D), down(D), whole((1, D)), whole((QW, D)), whole((D, FF)), whole((FF, D)),
            across(TOPK), across(TOPK), across(TOPK * H),
        ],
        out_specs=[
            down(D), down(D), across(TOPK * H), across(TOPK), across(E),
            pl.BlockSpec(memory_space=pl.ANY), whole((8, 128)), whole((1, D)),
        ],
        out_shape=[
            struct((count, D), BF16),
            struct((count, D)),
            struct((TOPK * H, count), BF16),
            struct((TOPK, count)),
            struct((E, count)),
            struct((flat_rows, 128), BF16),
            struct((8, 128)),
            struct((1, D)),
        ],
        scratch_shapes=[
            pltpu.VMEM((TOPK * H, MB), BF16),
            pltpu.VMEM((QW, MB), BF16),
            pltpu.VMEM((QW, MB), BF16),
            pltpu.VMEM((MB, FF), BF16),
            pltpu.VMEM((MB, FF), BF16),
            pltpu.VMEM((QW, D), F32),
            pltpu.VMEM((D, FF), F32),
            pltpu.VMEM((D, FF), F32),
            pltpu.VMEM((flat_rows - WO_ROW, 128), F32),
            pltpu.VMEM((flat_rows - WO_ROW - 8, 128), BF16),
            pltpu.SemaphoreType.DMA((1,)),
        ],
        compiler_params=params_for(60),
        name="middle",
    )(tokens, grad_out, gain, wo, w1, w2, routes_t, gates, attended)


def head_backward(
    segments, tokens, gain, wall, routes_t, start, queries, datt, lse, delta, kv, kvt, dlogits, dres,
    dgain_two, extra, flat,
):
    count = tokens.shape[0]
    steps = count // TB

    def place(b):
        return (b // NB) * NB + NB - 1 - b % NB

    across = lambda rows: pl.BlockSpec((rows, TB), lambda b: (0, place(b)))
    down = lambda columns: pl.BlockSpec((TB, columns), lambda b: (place(b), 0))
    return pl.pallas_call(
        head_backward_kernel,
        grid=(steps,),
        in_specs=[
            SMEM, down(D), whole((1, D)), whole((ALLW, D)), across(TOPK), across(1),
            across(TOPK * H), across(TOPK * H), across(TOPK), across(TOPK),
            pl.BlockSpec((LEN, 2 * H), lambda b: (b // NB, 0)),
            pl.BlockSpec((2 * H, LEN), lambda b: (0, b // NB)),
            across(E), down(D), whole((1, D)), whole((8, 128)), pl.BlockSpec(memory_space=pl.ANY),
        ],
        out_specs=[down(D), pl.BlockSpec(memory_space=pl.ANY)],
        scratch_shapes=[
            pltpu.VMEM((LEN, H), F32),
            pltpu.VMEM((LEN, H), F32),
            pltpu.VMEM((TOPK * H, TB), BF16),
            pltpu.VMEM((ALLW, TB), BF16),
            pltpu.VMEM((MOST * QB, TOPK * QB), BF16),
            pltpu.VMEM((MOST * QB, TOPK * QB), BF16),
            pltpu.VMEM((ALLW, D), F32),
            pltpu.VMEM((1, D), F32),
            pltpu.VMEM((WO_ROW + 8, 128), F32),
            pltpu.VMEM((WO_ROW + 8, 128), BF16),
            pltpu.SemaphoreType.DMA((1,)),
        ],
        out_shape=[struct((count, D)), struct(flat.shape, BF16)],
        input_output_aliases={16: 1},
        compiler_params=params_for(56),
        name="head_backward",
        cost_estimate=pl.CostEstimate(flops=30_000_000_000, bytes_accessed=24_000_000, transcendentals=0),
    )(
        segments, tokens, gain, wall, routes_t, start, queries, datt, lse, delta, kv, kvt, dlogits, dres,
        dgain_two, extra, flat,
    )


class Mesh3:
    def __init__(self, shards, over):
        shard = lax.axis_index("dp")
        other = lax.axis_index("fsdp")
        self.over = over
        self.many = shards * over
        self.sizes = {"x": 2, "y": shards // 2, "z": over // 2}
        self.here = {"x": lax.rem(other, 2), "y": lax.div(shard, 2), "z": lax.div(other, 2)}
        self.core = lax.rem(shard, 2)
        self.me = shard * over + other
        self.partner = (shard + 1 - 2 * self.core, other)

    def at_z(self, z):
        same = copy.copy(self)
        if z is not None:
            same.here = dict(self.here, z=z)
        return same

    def spots(self):
        x, y, z = (self.sizes[axis] for axis in "xyz")
        return list(itertools.product(range(x), range(y), range(1 - z, z)))

    def round_spots(self):
        return list(itertools.product(*[range(self.sizes[axis]) for axis in "xyz"]))

    def exists(self, z_steps):
        place = self.here["z"] + z_steps
        if isinstance(place, int):
            return 0 <= place < self.sizes["z"]
        return (place >= 0) & (place < self.sizes["z"])

    def device(self, core, spot):
        size = self.sizes["z"]
        x = lax.rem(self.here["x"] + spot[0], self.sizes["x"])
        y = lax.rem(self.here["y"] + spot[1], self.sizes["y"])
        z = self.here["z"] + spot[2]
        z = z % size if isinstance(z, int) else lax.rem(z + size, size)
        return (y * 2 + core, z * 2 + x)

    def number(self, core, spot):
        shard, other = self.device(core, spot)
        return shard * self.over + other

    def greet(self, devices):
        barrier = pltpu.get_barrier_semaphore()
        for device in devices:
            pl.semaphore_signal(barrier, inc=1, device_id=device, device_id_type=MESH)
        pl.semaphore_wait(barrier, len(devices))

    def near(self):
        steps = [at(axis, step) for axis in "xyz" for step in range(1, self.sizes[axis])]
        return [self.device(self.core, step) for step in steps] + [self.partner]

    def column(self):
        steps = [(core, step) for core in range(2) for step in range(self.sizes["z"]) if core or step]
        return [self.device(lax.rem(self.core + core, 2), (0, 0, step)) for core, step in steps]

    def layer(self):
        steps = [(x, y, 0) for x in range(self.sizes["x"]) for y in range(self.sizes["y"]) if x or y]
        return [self.device(self.core, step) for step in steps]


def at(axis, step):
    return tuple(step if one == axis else 0 for one in "xyz")


def last_axis(axes, spot):
    return max([i for i, axis in enumerate(axes) if spot["xyz".index(axis)]], default=-1)


def pieces_of(window):
    if window < 512:
        return [(0, window)]
    first = (window // 16 + 1) // 2 * 16
    return [(0, first), (first, window - first)]


def act(condition, action):
    if condition is True:
        action()
    elif condition is not False:
        pl.when(condition)(action)


GATHER_AXES = (("zxy", "yzx"), ("zyx", "xzy"))
REDUCE_AXES = ("zxy", "zyx")


def onward(mesh, axes, spot):
    last = last_axis(axes, spot)
    steps = []
    if last >= 0 and axes[last] == "z":
        steps.append(("z", -1 if spot[2] > 0 else 1))
    for axis in axes[last + 1 :]:
        steps += [("z", 1), ("z", -1)] if axis == "z" else [
            (axis, one) for one in range(1, mesh.sizes[axis])
        ]
    return steps


def gather_own_core(mesh, core, land, send_sem, recv_sem, begin):
    window = land.shape[1]
    pieces = pieces_of(window)
    slots = {}
    events = []

    def moved(owner, device, slot, p):
        rows = pl.ds(*pieces[p])
        return pltpu.make_async_remote_copy(
            src_ref=land.at[owner, rows],
            dst_ref=land.at[owner, rows],
            send_sem=send_sem.at[slot, p],
            recv_sem=recv_sem.at[owner, p],
            device_id=device,
            device_id_type=MESH,
        )

    for spot in mesh.spots():
        there = mesh.exists(spot[2])
        if there is False:
            continue
        owner = mesh.number(core, spot)
        turn = 0.5 * abs(spot[2]) + (spot[0] > 0) + (spot[1] > 0) + (0.001 if spot[2] < 0 else 0)
        for p in range(len(pieces)):
            sends = []
            for axis, step in onward(mesh, GATHER_AXES[core][p], spot):
                key = (spot[0], spot[1], spot[2] % mesh.sizes["z"], axis, step)
                away = mesh.exists(step) if axis == "z" else True
                if away is not False:
                    slot = slots.setdefault(key, len(slots))
                    sends.append((mesh.device(core, at(axis, step)), slot, away))
            key = (spot[0], spot[1], spot[2] % mesh.sizes["z"])
            sends.append((mesh.partner, slots.setdefault(key, len(slots)), True))

            def come(owner=owner, spot=spot, p=p, sends=sends):
                if any(spot):
                    moved(owner, mesh.partner, 0, p).wait_recv()
                for device, slot, away in sends:
                    act(away, moved(owner, device, slot, p).start)

            def done(owner=owner, p=p, sends=sends):
                for _, slot, away in sends:
                    act(away, moved(owner, mesh.partner, slot, p).wait_send)

            events.append((turn + 0.01 * p, there, come if begin else done))
    for _, there, action in sorted(events, key=lambda one: one[0]):
        act(there, action)


def gather_blocks(mesh, land, send_sem, recv_sem, begin):
    known = range(mesh.sizes["z"]) if mesh.sizes["z"] <= 4 else [None]
    for core in range(2):
        for z in known:

            @pl.when((mesh.core == core) & (True if z is None else mesh.here["z"] == z))
            def _(core=core, z=z):
                gather_own_core(mesh.at_z(z), core, land, send_sem, recv_sem, begin)


def each_owner(mesh, core, action):
    def one(number, carry):
        shard = 2 * lax.div(number, mesh.over) + core
        action(shard * mesh.over + lax.rem(number, mesh.over))
        return carry

    lax.fori_loop(0, mesh.many // 2, one, 0)


def reduce_blocks(mesh, core, source, mine, outgo, income, send_sem, recv_sem, total_ref):
    pieces = pieces_of(outgo.shape[1])
    half = mesh.many // 2
    held = {spot: i for i, spot in enumerate(mesh.round_spots())}

    def across(kind, spot):
        slot = held[spot]
        return pltpu.make_async_remote_copy(
            src_ref=source(mesh.number(kind, spot)),
            dst_ref=income.at[slot],
            send_sem=send_sem.at[slot, 0],
            recv_sem=recv_sem.at[slot, 0],
            device_id=mesh.partner,
            device_id_type=MESH,
        )

    def moved(spot, p, device):
        rows = pl.ds(*pieces[p])
        slot = half + held[spot]
        return pltpu.make_async_remote_copy(
            src_ref=outgo.at[held[spot], rows],
            dst_ref=income.at[slot, rows],
            send_sem=send_sem.at[slot, p],
            recv_sem=recv_sem.at[slot, p],
            device_id=device,
            device_id_type=MESH,
        )

    def far(spot):
        z = {0: 0, 1: 3, 2: 5, 3: 8}.get(spot[2], 2 * spot[2] + 2)
        return z + 2 * (spot[0] > 0) + 2 * (spot[1] > 0)

    for spot in sorted(held, key=far, reverse=True):
        across(1 - core, spot).start()
    axes = REDUCE_AXES[core]
    order = sorted(itertools.product(held, range(len(pieces))), key=lambda one: one[1] - 2 * far(one[0]))
    for spot, p in order:
        if p == 0:
            across(core, spot).wait_recv()
        rows = pl.ds(*pieces[p])
        total = mine(mesh.number(core, spot), *pieces[p]) + income[held[spot], rows].astype(F32)
        last = last_axis(axes, spot)
        for axis in axes[last + 1 :]:
            size = mesh.sizes[axis]
            for step in range(1, size):
                child = tuple(one or other for one, other in zip(spot, at(axis, size - step)))
                moved(child, p, mesh.partner).wait_recv()
                total = total + income[half + held[child], rows].astype(F32)
        if last < 0:
            total_ref[rows, :] = total
        else:
            outgo[held[spot], rows] = total.astype(BF16)
            step = spot["xyz".index(axes[last])]
            moved(spot, p, mesh.device(core, at(axes[last], step))).start()
    for spot, p in order:
        if p == 0:
            across(1 - core, spot).wait_send()
        if any(spot):
            moved(spot, p, mesh.partner).wait_send()


def sum_all(mesh, mine, stats, send_sem, recv_sem):
    column = mesh.sizes["z"] * 2
    layer = mesh.sizes["x"] * mesh.sizes["y"]
    groups = (
        (0, column, mesh.here["z"] * 2 + mesh.core, mesh.column()),
        (column, layer, mesh.here["x"] * mesh.sizes["y"] + mesh.here["y"], mesh.layer()),
    )
    total = mine
    for base, size, here, devices in groups:
        stats[base + here] = total

        def sent(j, device, base=base, here=here):
            return pltpu.make_async_remote_copy(
                src_ref=stats.at[base + here],
                dst_ref=stats.at[base + here],
                send_sem=send_sem.at[base + j],
                recv_sem=recv_sem.at[base + here],
                device_id=device,
                device_id_type=MESH,
            )

        def come(place, base=base):
            return pltpu.make_async_remote_copy(
                src_ref=stats.at[base + place],
                dst_ref=stats.at[base + place],
                send_sem=send_sem.at[base],
                recv_sem=recv_sem.at[base + place],
                device_id=mesh.partner,
                device_id_type=MESH,
            )

        for j, device in enumerate(devices):
            sent(j, device).start()
        for j in range(1, size):
            come(lax.rem(here + j, size)).wait_recv()
        for j, device in enumerate(devices):
            sent(j, device).wait_send()
        total = stats[base]
        for place in range(1, size):
            total = total + stats[base + place]
    return total


def window_rows(shard_size, many):
    units = [(shard_size * d) // UNIT for d in range(many + 1)]
    return 16 * (max(b - a for a, b in zip(units, units[1:])) + 1)


def first_row(shard_size, number):
    if isinstance(number, int):
        return number * shard_size // UNIT * 16
    return pl.multiple_of(lax.div(number * shard_size, UNIT) * 16, 16)


def inner_units(shard_size, many):
    units = [(shard_size * d) // UNIT for d in range(many + 1)]
    return min(b - a for a, b in zip(units, units[1:]))


def lay_inner(shard_size, many, land, flat, owner):
    count = 16 * inner_units(shard_size, many) - 16
    row = pl.multiple_of(first_row(shard_size, owner) + 16, 16)
    flat[pl.ds(row, count), :] = land[owner, pl.ds(16, count), :].astype(F32)


def lay_edges(shard_size, many, land, flat):
    inner = 16 * inner_units(shard_size, many)
    flat[0:16, :] = jnp.zeros((16, 128), F32)

    def lay(number, carry):
        row = first_row(shard_size, number)
        after = first_row(shard_size, number + 1)
        flat[pl.ds(row, 16), :] += land[number, 0:16, :].astype(F32)
        tail = land[number, pl.ds(inner, 16), :].astype(F32)
        flat[pl.ds(pl.multiple_of(row + inner, 16), 16), :] = tail
        last = pl.multiple_of(after - row, 16)
        flat[pl.ds(after, 16), :] = land[number, pl.ds(last, 16), :].astype(F32)
        return carry

    lax.fori_loop(0, many, lay, 0)


def early_matrices(flat, wall_ref, gain_one_ref, gain_two_ref):
    for c in range(D // 128):
        lanes = slice(c * 128, (c + 1) * 128)
        gain_one_ref[:, lanes] = flat[c : c + 1, :]
        gain_two_ref[:, lanes] = flat[4 + c : 5 + c, :]
    for c in range(QW // 128):
        wall_ref[c * 128 : (c + 1) * 128, :] = flat[pl.ds(WQ_ROW + c, D, stride=12), :].T.astype(BF16)
    for first, row in ((KROW, WK_ROW), (VROW, WV_ROW)):
        pair = flat[row : row + 256, :].T.astype(BF16)
        wall_ref[first : first + H, :] = (
            nn(pair[:H], picks(256, 2, 0).astype(BF16)) + nn(pair[H:], picks(256, 2, 1).astype(BF16))
        ).astype(BF16)
    across = jnp.concatenate(
        [flat[pl.ds(WR_ROW + j, 32, stride=3), :] for j in range(3)], axis=1
    ).T.astype(BF16)
    router_t = jnp.zeros((E, D), F32)
    for part in range(16):
        router_t = router_t + nn(across[part * E : (part + 1) * E, :], picks(32, 16, part).astype(BF16))
    wall_ref[RROW:ALLW, :] = jnp.concatenate(
        [router_t, jnp.zeros((ALLW - RROW - E, D), F32)], axis=0
    ).astype(BF16)


def gather_kernel(
    mesh, shard_size, own_ref,
    wall_out, gain_one_ref, gain_two_ref, wo_out, w1_out, w2_out,
    land, flat, wall_ref, wo_ref, w1_ref, w2_ref, send_sem, recv_sem, out_sem,
):
    mesh = mesh()
    many = mesh.many
    mesh.greet(mesh.near())
    land[mesh.me] = own_ref[...]
    gather_blocks(mesh, land, send_sem, recv_sem, True)
    each_owner(mesh, mesh.core, functools.partial(lay_inner, shard_size, many, land, flat))

    def arrive(owner):
        for p in range(recv_sem.shape[1]):
            rows = pl.ds(*pieces_of(own_ref.shape[0])[p])
            pltpu.make_async_remote_copy(
                src_ref=land.at[owner, rows],
                dst_ref=land.at[owner, rows],
                send_sem=send_sem.at[0, p],
                recv_sem=recv_sem.at[owner, p],
                device_id=mesh.partner,
                device_id_type=MESH,
            ).wait_recv()
        lay_inner(shard_size, many, land, flat, owner)

    each_owner(mesh, 1 - mesh.core, arrive)
    lay_edges(shard_size, many, land, flat)
    copies = []

    def leave(matrix, out):
        one = pltpu.make_async_copy(matrix, out, out_sem.at[len(copies)])
        one.start()
        copies.append(one)

    for c in range(D // 128):
        wo_ref[:, c * 128 : (c + 1) * 128] = flat[pl.ds(WO_ROW + c, QW, stride=4), :].astype(BF16)
    leave(wo_ref, wo_out)
    for c in range(D // 128):
        w2_ref[:, c * 128 : (c + 1) * 128] = flat[pl.ds(W2_ROW + c, FF, stride=4), :].astype(BF16)
    leave(w2_ref, w2_out)
    for c in range(FF // 128):
        w1_ref[:, c * 128 : (c + 1) * 128] = flat[pl.ds(W1_ROW + c, D, stride=16), :].astype(BF16)
    leave(w1_ref, w1_out)
    early_matrices(flat, wall_ref, gain_one_ref, gain_two_ref)
    leave(wall_ref, wall_out)
    gather_blocks(mesh, land, send_sem, recv_sem, False)
    for one in copies:
        one.wait()


def gather_weights(shards, over, shard_size, own):
    window = own.shape[0]
    many = shards * over
    rows = (shard_size * (many - 1)) // UNIT * 16 + window
    vmem = pl.BlockSpec(memory_space=pltpu.VMEM)
    hbm = pl.BlockSpec(memory_space=pl.ANY)
    mesh = functools.partial(Mesh3, shards, over)
    pieces = len(pieces_of(window))
    return pl.pallas_call(
        functools.partial(gather_kernel, mesh, shard_size),
        in_specs=[vmem],
        out_specs=[hbm, vmem, vmem, hbm, hbm, hbm],
        out_shape=[
            struct((ALLW, D), BF16),
            struct((1, D)),
            struct((1, D)),
            struct((QW, D), BF16),
            struct((D, FF), BF16),
            struct((FF, D), BF16),
        ],
        scratch_shapes=[
            pltpu.VMEM((many, window, 128), BF16),
            pltpu.VMEM((rows, 128), F32),
            pltpu.VMEM((ALLW, D), BF16),
            pltpu.VMEM((QW, D), BF16),
            pltpu.VMEM((D, FF), BF16),
            pltpu.VMEM((FF, D), BF16),
            pltpu.SemaphoreType.DMA((5 * many // 2, pieces)),
            pltpu.SemaphoreType.DMA((many, pieces)),
            pltpu.SemaphoreType.DMA((4,)),
        ],
        compiler_params=pltpu.CompilerParams(
            collective_id=0, has_side_effects=True, vmem_limit_bytes=60 * MIB
        ),
        name="gather_weights",
    )(own)


def reduce_kernel(
    mesh, shard_size, flat_ref, count_ref,
    out_ref, total_ref, gain_ref,
    part, outgo, income, stats, part_sem, send_sem, recv_sem, stat_send, stat_recv,
):
    mesh = mesh()
    window = out_ref.shape[0]
    span = part.shape[1]

    def source(owner):
        return flat_ref.at[pl.ds(first_row(shard_size, owner), window), :]

    def fetch(y):
        first = first_row(shard_size, (2 * y + mesh.core) * mesh.over)
        return pltpu.make_async_copy(flat_ref.at[pl.ds(first, span), :], part.at[y], part_sem.at[y])

    def mine(owner, first, rows):
        shard = lax.div(owner, mesh.over)
        row = first_row(shard_size, owner) - first_row(shard_size, shard * mesh.over) + first
        return part[lax.div(shard, 2), pl.ds(pl.multiple_of(row, 16), rows), :].astype(F32)

    for y in range(mesh.sizes["y"]):
        fetch(y).start()
    mesh.greet(mesh.column() + mesh.layer())
    for y in range(mesh.sizes["y"]):
        fetch(y).wait()
    buffers = (source, mine, outgo, income, send_sem, recv_sem, out_ref)
    for core in range(2):
        pl.when(mesh.core == core)(functools.partial(reduce_blocks, mesh, core, *buffers))

    total = out_ref[...]
    begin = mesh.me * shard_size - lax.div(mesh.me * shard_size, UNIT) * UNIT
    place = (
        lax.broadcasted_iota(jnp.int32, (window, 128), 0) * 128
        + lax.broadcasted_iota(jnp.int32, (window, 128), 1)
    )
    inside = jnp.where((place >= begin) & (place < begin + shard_size), total, 0.0)
    squares = jnp.sum(jnp.sum(inside * inside, axis=0, keepdims=True), axis=1, keepdims=True)
    lane = lax.broadcasted_iota(jnp.int32, (8, 128), 1)
    row = jnp.where(lane == E, squares, count_ref[...])
    gains = jnp.where(mesh.me == 0, total[0:8, :], 0.0)
    summed = sum_all(mesh, jnp.concatenate([row, gains], axis=0), stats, stat_send, stat_recv)
    total_ref[...] = summed[0:1, :]
    gain_ref[...] = summed[8:16, :]


def reduce_grads(shards, over, shard_size, window, flat, counts):
    vmem = pl.BlockSpec(memory_space=pltpu.VMEM)
    many = shards * over
    mesh = functools.partial(Mesh3, shards, over)
    pieces = len(pieces_of(window))
    steps = over + shards
    units = [(shard_size * d) // UNIT for d in range(many)]
    span = 16 * max(units[d + over - 1] - units[d] for d in range(0, many, over)) + window
    return pl.pallas_call(
        functools.partial(reduce_kernel, mesh, shard_size),
        in_specs=[pl.BlockSpec(memory_space=pl.ANY), vmem],
        out_specs=[vmem] * 3,
        out_shape=[struct((window, 128)), struct((1, 128)), struct((8, 128))],
        scratch_shapes=[
            pltpu.VMEM((shards // 2, span, 128), BF16),
            pltpu.VMEM((many // 2, window, 128), BF16),
            pltpu.VMEM((many, window, 128), BF16),
            pltpu.VMEM((steps, 16, 128), F32),
            pltpu.SemaphoreType.DMA((shards // 2,)),
            pltpu.SemaphoreType.DMA((many, pieces)),
            pltpu.SemaphoreType.DMA((many, pieces)),
            pltpu.SemaphoreType.DMA((steps,)),
            pltpu.SemaphoreType.DMA((steps,)),
        ],
        compiler_params=pltpu.CompilerParams(
            collective_id=1, has_side_effects=True, vmem_limit_bytes=56 * MIB
        ),
        name="reduce_grads",
    )(flat, counts)


def local_step(flat_rows, tokens, grad_out, routes, segments, weights):
    wall, gain_one, gain_two, wo, w1, w2 = weights
    queries, attended, gates, lse, kv, kvt, start, routes_t, counts = head_forward(
        tokens, routes.T, segments, wall, gain_one
    )
    output, dres, datt, delta, dlogits, flat, extra, dgain_two = middle(
        flat_rows, tokens, grad_out, gain_two, wo, w1, w2, routes_t, gates, attended
    )
    input_grad, flat = head_backward(
        segments, tokens, gain_one, wall, routes_t, start, queries, datt, lse, delta, kv, kvt, dlogits, dres,
        dgain_two, extra, flat,
    )
    return output, input_grad, flat, counts


def per_device(
    shards, over, tokens, grad_out, routes, segments, params, first_moment, second_moment, ema_weights
):
    shard_size = params.shape[0]
    window = window_rows(shard_size, shards * over)
    flat_rows = (shard_size * (shards * over - 1)) // UNIT * 16 + window + 16
    me = lax.axis_index("dp") * over + lax.axis_index("fsdp")
    begin = lax.rem(me * shard_size, UNIT)
    own = lax.dynamic_slice(
        jnp.pad(params.astype(BF16), (UNIT, window * 128 - shard_size)), (UNIT - begin,), (window * 128,)
    ).reshape(window, 128)
    wall, gain_one, gain_two, wo, w1, w2 = gather_weights(shards, over, shard_size, own)
    output, input_grad, flat, counts = local_step(
        flat_rows, tokens, grad_out, routes, segments, (wall, gain_one, gain_two, wo, w1, w2)
    )
    reduced, sums, gain_grads = reduce_grads(shards, over, shard_size, window, flat, counts)
    grad_shard = lax.dynamic_slice(reduced.reshape(-1), (begin,), (shard_size,))
    total_tokens = tokens.shape[0] * shards * over
    expert_load = sums[0, :E] * (E / (total_tokens * TOPK))
    grad_norm = jnp.sqrt(sums[0, E])
    clipped = grad_shard * (CLIP_LIMIT / jnp.maximum(grad_norm, CLIP_LIMIT))
    new_first = BETA_FIRST * first_moment + (1.0 - BETA_FIRST) * clipped
    new_second = BETA_SECOND * second_moment + (1.0 - BETA_SECOND) * clipped * clipped
    first_hat = new_first / (1.0 - BETA_FIRST**STEP)
    second_hat = new_second / (1.0 - BETA_SECOND**STEP)
    new_params = params * (1.0 - LEARN_RATE * DECAY_RATE) - LEARN_RATE * first_hat / (
        jnp.sqrt(second_hat) + ADAM_EPS
    )
    new_ema = EMA_KEEP * ema_weights + (1.0 - EMA_KEEP) * new_params
    return (
        output,
        input_grad,
        expert_load,
        grad_norm.reshape(1),
        new_params,
        new_first,
        new_second,
        new_ema,
        gain_grads.reshape(2, D),
    )


def solution(mesh):
    row = P(("dp", "fsdp"), None)
    flat = P(("dp", "fsdp"))
    return jax.shard_map(
        functools.partial(per_device, mesh.shape["dp"], mesh.shape["fsdp"]),
        mesh=mesh,
        in_specs=(row, row, row, row, flat, flat, flat, flat),
        out_specs=(row, row, P(), P(), flat, flat, flat, flat, P()),
        check_vma=False,
    )
```

```python
import copy
import functools
import itertools

import jax
import jax.numpy as jnp
from jax import lax
from jax.experimental import pallas as pl
from jax.experimental.pallas import tpu as pltpu
from jax.sharding import PartitionSpec as P

D = 512
E = 24
TOPK = 8
H = 64
FF = 2048
STEP = 10

NORM_EPS = 1e-06
CLIP_LIMIT = 1.0
BETA_FIRST = 0.9
BETA_SECOND = 0.95
LEARN_RATE = 0.1
DECAY_RATE = 0.1
ADAM_EPS = 1e-08
EMA_KEEP = 0.9
NEG_LARGE = -1e30

QW = E * H
KROW = QW
VROW = QW + H
RROW = QW + 2 * H
ALLW = 1696
LEN = 1024
TB = 512
NB = LEN // TB
QB = 128
SIDE = 4
MOST = 512 // QB + 1
SORT_STEPS = (
    (0, 1), (2, 3), (4, 5), (6, 7), (0, 2), (1, 3), (4, 6), (5, 7), (1, 2), (5, 6),
    (0, 4), (1, 5), (2, 6), (3, 7), (2, 4), (3, 5), (1, 2), (3, 4), (5, 6),
)
FC = 256
MB = 512
MIB = 1 << 20

WR_ROW = 8
WK_ROW = 104
WV_ROW = 360
WQ_ROW = 616
WO_ROW = 6760
W1_ROW = 12904
W2_ROW = 21096
ALL_ROWS = 29288
UNIT = 16 * 128
MESH = pl.DeviceIdType.MESH

F32 = jnp.float32
BF16 = jnp.bfloat16


def nn(a, b):
    return lax.dot_general(a, b, (((1,), (0,)), ((), ())), preferred_element_type=F32)


def nt(a, b):
    return lax.dot_general(a, b, (((1,), (1,)), ((), ())), preferred_element_type=F32)


def tn(a, b):
    return lax.dot_general(a, b, (((0,), (0,)), ((), ())), preferred_element_type=F32)


def rms_scale(values):
    return lax.rsqrt(jnp.mean(values * values, axis=-1, keepdims=True) + NORM_EPS)


def slot_of(routes, k, rows):
    return jnp.broadcast_to(routes[k : k + 1, :], (rows, routes.shape[1]))


def expert_rows(routes, k):
    return jnp.broadcast_to(routes.astype(jnp.int16)[k : k + 1, :], (16, routes.shape[1]))


def pick_heads(routes, source_ref, k):
    tokens = routes.shape[1]
    route = expert_rows(routes, k)
    taken = source_ref[k * H : (k + 1) * H, :].reshape(H // 16, 16, tokens)
    for e in range(k + 1, k + E - TOPK + 1):
        piece = source_ref[e * H : (e + 1) * H, :].reshape(H // 16, 16, tokens)
        taken = jnp.where((route == jnp.int16(e))[None], piece, taken)
    return taken.reshape(H, tokens)


def place_heads(routes, source_ref, target_ref):
    tokens = routes.shape[1]
    rows = [expert_rows(routes, k) for k in range(TOPK)]
    for e in range(E):
        total = jnp.zeros((H // 16, 16, tokens), BF16)
        for k in range(max(0, e - (E - TOPK)), min(TOPK - 1, e) + 1):
            piece = source_ref[k * H : (k + 1) * H, :].reshape(H // 16, 16, tokens)
            total = jnp.where((rows[k] == jnp.int16(e))[None], piece, total)
        target_ref[e * H : (e + 1) * H, :] = total.reshape(H, tokens)


def sorted_rows(rows):
    rows = list(rows)
    for one, two in SORT_STEPS:
        rows[one], rows[two] = jnp.minimum(rows[one], rows[two]), jnp.maximum(rows[one], rows[two])
    return rows


def key_mask(first_key, first_query, rows, start_row):
    keys = lax.broadcasted_iota(jnp.int32, (rows, QB), 0) + first_key
    queries = lax.broadcasted_iota(jnp.int32, (rows, QB), 1) + first_query
    mask = (keys <= queries) & (keys >= start_row)
    return jnp.concatenate([mask] * SIDE, axis=1)


def group_of(ref, k, lanes):
    return jnp.concatenate([ref[i * H : (i + 1) * H, lanes] for i in range(k, k + SIDE)], axis=1)


def row_group(ref, k, lanes):
    return jnp.concatenate([ref[i : i + 1, lanes] for i in range(k, k + SIDE)], axis=1)


def by_span(attend, row, place, segment_ref):
    def one(j, carry):
        block = place * (TB // QB) + j
        first = block * QB
        span = jnp.int32(1)
        for back in range(MOST - 1):
            last = first - back * QB - 1
            same = segment_ref[row, jnp.maximum(last, 0)] == segment_ref[row, first]
            span = span + jnp.where((last >= 0) & same, 1, 0)
        for blocks in range(1, MOST + 1):

            @pl.when(span == blocks)
            def _(blocks=blocks):
                attend(pl.ds(pl.multiple_of(j * QB, QB), QB), block, blocks)

        return carry

    lax.fori_loop(0, TB // QB, one, 0)


def head_forward_kernel(
    steps, segment_smem, x_ref, route_ref, segment_ref, wall_ref, gain_ref,
    q_ref, att_ref, gate_ref, lse_ref, kv_ref, kvt_ref, start_ref, sorted_ref, count_ref,
    all_scr, low_scr, k_scr, vt_scr, count_scr,
):
    step = pl.program_id(0)
    place = lax.rem(step, NB)
    here = pl.multiple_of(place * TB, TB)

    @pl.when(step == 0)
    def _():
        count_scr[...] = jnp.zeros_like(count_scr)

    row = segment_ref[pl.ds(lax.div(step, NB), 1), :]
    segments = segment_ref[pl.ds(lax.div(step, NB), 1), pl.ds(here, TB)]
    start = jnp.zeros((1, TB), jnp.int32)
    for number in range(1, 4):
        below = jnp.sum((row < number).astype(jnp.int32), axis=1, keepdims=True)
        start = jnp.where(segments == number, below, start)
    start_ref[...] = start
    x = x_ref[...].astype(F32)
    normed = (x * rms_scale(x) * gain_ref[...]).astype(BF16)
    all_scr[...] = nt(wall_ref[...], normed)
    kt = all_scr[KROW : KROW + H, :]
    vt = all_scr[VROW : VROW + H, :]
    logits = all_scr[RROW : RROW + E, :]
    kvt = jnp.concatenate([kt, vt], axis=0)
    kv = kvt.T.astype(BF16)
    kv_ref[...] = kv
    kvt_ref[...] = kvt.astype(BF16)
    k_scr[pl.ds(here, TB), :] = kv[:, :H]
    vt_scr[:, pl.ds(here, TB)] = vt.astype(BF16)
    routes = jnp.concatenate(sorted_rows(route_ref[k : k + 1, :] for k in range(TOPK)), axis=0)
    sorted_ref[...] = routes
    experts = lax.broadcasted_iota(jnp.int32, (E, TB), 0)
    chosen = []
    counts = count_scr[...]
    for k in range(TOPK):
        named = slot_of(routes, k, E) == experts
        chosen.append(jnp.sum(jnp.where(named, logits, 0.0), axis=0, keepdims=True))
        counts = counts + named.astype(F32)
    count_scr[...] = counts
    chosen = jnp.concatenate(chosen, axis=0)
    raised = jnp.exp(chosen - jnp.max(chosen, axis=0, keepdims=True))
    gate_ref[...] = raised / jnp.sum(raised, axis=0, keepdims=True)
    low_scr[...] = all_scr[0:QW, :].astype(BF16)
    for k in range(TOPK):
        q_ref[k * H : (k + 1) * H, :] = pick_heads(routes, low_scr, k) * jnp.asarray(H ** (-0.5), BF16)

    def attend(lanes, block, blocks):
        rows = blocks * QB
        first_key = pl.multiple_of((block - (blocks - 1)) * QB, QB)
        mask = key_mask(first_key, block * QB, rows, start_ref[:, lanes])
        keys = k_scr[pl.ds(first_key, rows), :]
        values = vt_scr[:, pl.ds(first_key, rows)]
        groups = [nn(keys, group_of(q_ref, 0, lanes))]
        for k in range(0, TOPK, SIDE):
            if k + SIDE < TOPK:
                groups.append(nn(keys, group_of(q_ref, k + SIDE, lanes)))
            scores = jnp.where(mask, groups[k // SIDE], NEG_LARGE)
            top = jnp.max(scores, axis=0, keepdims=True)
            raised = jnp.exp(scores - top)
            total = jnp.sum(raised, axis=0, keepdims=True)
            out = nn(values, (raised * (1.0 / total)).astype(BF16))
            lse = top + jnp.log(total)
            for side in range(SIDE):
                one = slice(side * QB, (side + 1) * QB)
                att_ref[(k + side) * H : (k + side + 1) * H, lanes] = out[:, one]
                lse_ref[k + side : k + side + 1, lanes] = lse[:, one]

    by_span(attend, lax.div(step, NB), place, segment_smem)

    @pl.when(step == steps - 1)
    def _():
        held = jnp.sum(count_scr[...], axis=1, keepdims=True)
        lane = lax.broadcasted_iota(jnp.int32, (E, 128), 1)
        row = lax.broadcasted_iota(jnp.int32, (E, 128), 0)
        count_ref[...] = jnp.sum(jnp.where(lane == row, held, 0.0), axis=0, keepdims=True)


def picks(rows, stride, first):
    at = lax.broadcasted_iota(jnp.int32, (rows, D), 1)
    row = lax.broadcasted_iota(jnp.int32, (rows, D), 0)
    return (at == row * stride + first).astype(F32)


def exact(product, a, b):
    return lax.dot_general(
        a, b, (product, ((), ())), precision=lax.Precision.HIGHEST, preferred_element_type=F32
    )


def gelu_parts(v):
    cdf = 0.5 + 0.5 * lax.erf(v * 0.7071067811865476)
    return cdf, jnp.exp(v * v * -0.5) * 0.3989422804014327


def middle_kernel(
    x_ref, dy_ref, gain_ref, wo_ref, w1_ref, w2_ref, route_ref, gate_ref, att_ref,
    out_ref, dres_ref, datt_ref, delta_ref, dlogit_ref, flat_ref, extra_ref, dgain_ref,
    slot_scr, head_scr, mix_scr, hidden_scr, dpre_scr, dwo_ref, dw1_ref, dw2t_ref, rows_scr, low_scr, row_sem,
):
    step = pl.program_id(0)

    @pl.when(step == 0)
    def _():
        dwo_ref[...] = jnp.zeros_like(dwo_ref)
        dw1_ref[...] = jnp.zeros_like(dw1_ref)
        dw2t_ref[...] = jnp.zeros_like(dw2t_ref)
        dgain_ref[...] = jnp.zeros_like(dgain_ref)

    routes = route_ref[...]
    tokens = routes.shape[1]
    gates = gate_ref[...]
    for k in range(TOPK):
        rows = slice(k * H, (k + 1) * H)
        slot_scr[rows, :] = (gates[k : k + 1, :] * att_ref[rows, :]).astype(BF16)
    place_heads(routes, slot_scr, mix_scr)
    x = x_ref[...].astype(F32)
    dy = dy_ref[...]
    mixed = mix_scr[...]
    residual = x + tn(mixed, wo_ref[...])
    scale = rms_scale(residual)
    gain = gain_ref[...]
    second = (residual * scale * gain).astype(BF16)
    second_t = second.T
    dy_t = dy.T
    pre = [nn(second, w1_ref[:, 0:FC])]
    back = [nt(dy, w2_ref[0:FC, :])]
    for i in range(FF // FC):
        here = slice(i * FC, (i + 1) * FC)
        if i + 1 < FF // FC:
            after = slice((i + 1) * FC, (i + 2) * FC)
            pre.append(nn(second, w1_ref[:, after]))
            back.append(nt(dy, w2_ref[after, :]))
        cdf, density = gelu_parts(pre[i])
        hidden_scr[:, here] = (pre[i] * cdf).astype(BF16)
        dpre_scr[:, here] = (back[i] * (cdf + pre[i] * density)).astype(BF16)
    dsecond = nt(dpre_scr[...], w1_ref[...])
    out_ref[...] = (residual + nn(hidden_scr[...], w2_ref[...])).astype(BF16)
    dw1_ref[...] += nn(second_t, dpre_scr[...])
    dw2t_ref[...] += nn(dy_t, hidden_scr[...])
    dgain_ref[...] += jnp.sum(dsecond * residual * scale, axis=0, keepdims=True)
    weighted = gain * dsecond
    dres = (
        dy.astype(F32)
        + scale * weighted
        - residual * (scale * scale * scale) * jnp.mean(weighted * residual, axis=-1, keepdims=True)
    )
    dres_ref[...] = dres
    branch = dres.astype(BF16)
    dwo_ref[...] += nn(mixed, branch)
    head_scr[...] = nt(wo_ref[...], branch).astype(BF16)
    dgates = []
    for k in range(TOPK):
        rows = slice(k * H, (k + 1) * H)
        dslot = pick_heads(routes, head_scr, k).astype(F32)
        attended = att_ref[rows, :]
        dgates.append(jnp.sum(dslot * attended, axis=0, keepdims=True))
        datt = (gates[k : k + 1, :] * dslot).astype(BF16)
        datt_ref[rows, :] = datt
        delta_ref[k : k + 1, :] = jnp.sum(datt.astype(F32) * attended, axis=0, keepdims=True)
    dgate = jnp.concatenate(dgates, axis=0)
    dchosen = gates * (dgate - jnp.sum(gates * dgate, axis=0, keepdims=True))
    experts = lax.broadcasted_iota(jnp.int32, (E, tokens), 0)
    dlogits = jnp.zeros((E, tokens), F32)
    for k in range(TOPK):
        dlogits = jnp.where(
            slot_of(routes, k, E) == experts,
            jnp.broadcast_to(dchosen[k : k + 1, :], (E, tokens)),
            dlogits,
        )
    dlogit_ref[...] = dlogits

    @pl.when(step == pl.num_programs(0) - 1)
    def _():
        for c in range(D // 128):
            lanes = slice(c * 128, (c + 1) * 128)
            rows_scr[pl.ds(c, QW, stride=4), :] = dwo_ref[:, lanes]
            rows_scr[pl.ds(W2_ROW - WO_ROW + c, FF, stride=4), :] = dw2t_ref[lanes, :].T
        for c in range(FF // 128):
            rows_scr[pl.ds(W1_ROW - WO_ROW + c, D, stride=16), :] = dw1_ref[:, c * 128 : (c + 1) * 128]
        extra_ref[...] = rows_scr[0:8, :]
        low_scr[...] = rows_scr[8:, :].astype(BF16)
        copy = pltpu.make_async_copy(
            low_scr, flat_ref.at[pl.ds(WO_ROW + 8, low_scr.shape[0]), :], row_sem.at[0]
        )
        copy.start()
        copy.wait()


def head_backward_kernel(
    segment_smem, x_ref, gain_ref, wall_ref, route_ref, start_ref, q_ref, datt_ref,
    lse_ref, delta_ref, kv_ref, kvt_ref, dlogit_ref, dres_ref, dgain_two_ref, extra_ref, flat_in,
    dx_ref, flat_ref,
    dk_scr, dv_scr, dq_scr, dall_scr, prob_scr, dscore_scr, dwall_ref, dgain_ref, rows_scr, low_scr, row_sem,
):
    step = pl.program_id(0)
    place = NB - 1 - lax.rem(step, NB)
    here = pl.multiple_of(place * TB, TB)

    @pl.when(step == 0)
    def _():
        dwall_ref[...] = jnp.zeros_like(dwall_ref)
        dgain_ref[...] = jnp.zeros_like(dgain_ref)

    @pl.when(lax.rem(step, NB) == 0)
    def _():
        dk_scr[...] = jnp.zeros_like(dk_scr)
        dv_scr[...] = jnp.zeros_like(dv_scr)

    def attend(lanes, block, blocks):
        rows = blocks * QB
        first_key = pl.multiple_of((block - (blocks - 1)) * QB, QB)
        mask = key_mask(first_key, block * QB, rows, start_ref[:, lanes])
        keys = kv_ref[pl.ds(first_key, rows), :H]
        values = kv_ref[pl.ds(first_key, rows), H:]
        keys_t = kvt_ref[:H, pl.ds(first_key, rows)]
        queries = [group_of(q_ref, k, lanes) for k in range(0, TOPK, SIDE)]
        datts = [group_of(datt_ref, k, lanes) for k in range(0, TOPK, SIDE)]
        scores = [nn(keys, queries[0])]
        dprobs = [nn(values, datts[0])]
        for i in range(TOPK // SIDE):
            if i + 1 < TOPK // SIDE:
                scores.append(nn(keys, queries[i + 1]))
                dprobs.append(nn(values, datts[i + 1]))
            k = i * SIDE
            wide = slice(k * QB, (k + SIDE) * QB)
            probs = jnp.exp(jnp.where(mask, scores[i], NEG_LARGE) - row_group(lse_ref, k, lanes))
            dscore = (probs * (dprobs[i] - row_group(delta_ref, k, lanes))).astype(BF16)
            prob_scr[0:rows, wide] = probs.astype(BF16)
            dscore_scr[0:rows, wide] = dscore
            dq = (nn(keys_t, dscore) * (H ** (-0.5))).astype(BF16)
            for side in range(SIDE):
                dq_scr[(k + side) * H : (k + side + 1) * H, lanes] = dq[:, side * QB : (side + 1) * QB]
        dv_scr[pl.ds(first_key, rows), :] += nt(prob_scr[0:rows, :], jnp.concatenate(datts, axis=1))
        dk_scr[pl.ds(first_key, rows), :] += nt(dscore_scr[0:rows, :], jnp.concatenate(queries, axis=1))

    by_span(attend, lax.div(step, NB), place, segment_smem)
    place_heads(route_ref[...], dq_scr, dall_scr)
    dkv = jnp.concatenate([dk_scr[pl.ds(here, TB), :], dv_scr[pl.ds(here, TB), :]], axis=1)
    dall_scr[KROW : KROW + 2 * H, :] = dkv.T.astype(BF16)
    dall_scr[RROW : RROW + 32, :] = jnp.concatenate(
        [dlogit_ref[...], jnp.zeros((32 - E, TB), F32)], axis=0
    ).astype(BF16)
    x = x_ref[...].astype(F32)
    scale = rms_scale(x)
    gain = gain_ref[...]
    normed = (x * scale * gain).astype(BF16)
    dall = dall_scr[...]
    dwall_ref[...] += nn(dall, normed)
    dnormed = tn(dall, wall_ref[...])
    dgain_ref[...] += jnp.sum(dnormed * x * scale, axis=0, keepdims=True)
    weighted = gain * dnormed
    dx_ref[...] = (
        dres_ref[...]
        + scale * weighted
        - x * (scale * scale * scale) * jnp.mean(weighted * x, axis=-1, keepdims=True)
    )

    @pl.when(step == pl.num_programs(0) - 1)
    def _():
        for c in range(D // 128):
            lanes = slice(c * 128, (c + 1) * 128)
            rows_scr[c : c + 1, :] = dgain_ref[:, lanes]
            rows_scr[4 + c : 5 + c, :] = dgain_two_ref[:, lanes]
        router_t = dwall_ref[RROW : RROW + E, :]
        across = jnp.concatenate(
            [exact(((1,), (1,)), router_t, picks(32, 16, b)) for b in range(16)], axis=0
        ).T
        for j in range(3):
            rows_scr[pl.ds(WR_ROW + j, 32, stride=3), :] = across[:, j * 128 : (j + 1) * 128]
        for first, row in ((KROW, WK_ROW), (VROW, WV_ROW)):
            part = dwall_ref[first : first + H, :]
            rows_scr[row : row + 256, :] = jnp.concatenate(
                [exact(((1,), (1,)), picks(256, 2, b), part) for b in range(2)], axis=1
            )
        for c in range(QW // 128):
            rows_scr[pl.ds(WQ_ROW + c, D, stride=12), :] = dwall_ref[c * 128 : (c + 1) * 128, :].T
        rows_scr[WO_ROW : WO_ROW + 8, :] = extra_ref[...]
        low_scr[...] = rows_scr[...].astype(BF16)
        copy = pltpu.make_async_copy(low_scr, flat_ref.at[pl.ds(0, WO_ROW + 8), :], row_sem.at[0])
        copy.start()
        copy.wait()


def whole(shape):
    return pl.BlockSpec(shape, lambda *_: (0,) * len(shape), pipeline_mode=pl.Buffered(1))


def kept(shape):
    return pl.BlockSpec(shape, lambda *_: (0,) * len(shape))


SMEM = pl.BlockSpec(memory_space=pltpu.SMEM)


def struct(shape, kind=F32):
    return jax.ShapeDtypeStruct(shape, kind)


def params_for(mib):
    return pltpu.CompilerParams(vmem_limit_bytes=mib * MIB)


def head_forward(tokens, routes_t, segments, wall, gain):
    count = tokens.shape[0]
    steps = count // TB
    across = lambda rows: pl.BlockSpec((rows, TB), lambda b: (0, b))
    down = lambda columns: pl.BlockSpec((TB, columns), lambda b: (b, 0))
    return pl.pallas_call(
        functools.partial(head_forward_kernel, steps),
        grid=(steps,),
        in_specs=[SMEM, down(D), across(TOPK), whole(segments.shape), whole((ALLW, D)), whole((1, D))],
        out_specs=[
            across(TOPK * H), across(TOPK * H), across(TOPK), across(TOPK), down(2 * H), across(2 * H),
            across(1), across(TOPK), whole((1, 128)),
        ],
        scratch_shapes=[
            pltpu.VMEM((ALLW, TB), F32),
            pltpu.VMEM((QW, TB), BF16),
            pltpu.VMEM((LEN, H), BF16),
            pltpu.VMEM((H, LEN), BF16),
            pltpu.VMEM((E, TB), F32),
        ],
        out_shape=[
            struct((TOPK * H, count), BF16),
            struct((TOPK * H, count)),
            struct((TOPK, count)),
            struct((TOPK, count)),
            struct((count, 2 * H), BF16),
            struct((2 * H, count), BF16),
            struct((1, count), jnp.int32),
            struct((TOPK, count), jnp.int32),
            struct((1, 128)),
        ],
        compiler_params=params_for(56),
        name="head_forward",
        cost_estimate=pl.CostEstimate(flops=10_000_000_000, bytes_accessed=16_000_000, transcendentals=0),
    )(segments, tokens, routes_t, segments, wall, gain)


def middle(flat_rows, tokens, grad_out, gain, wo, w1, w2, routes_t, gates, attended):
    count = tokens.shape[0]
    steps = count // MB
    across = lambda rows: pl.BlockSpec((rows, MB), lambda b: (0, b))
    down = lambda columns: pl.BlockSpec((MB, columns), lambda b: (b, 0))
    return pl.pallas_call(
        middle_kernel,
        grid=(steps,),
        in_specs=[
            down(D), down(D), whole((1, D)), whole((QW, D)), whole((D, FF)), whole((FF, D)),
            across(TOPK), across(TOPK), across(TOPK * H),
        ],
        out_specs=[
            down(D), down(D), across(TOPK * H), across(TOPK), across(E),
            pl.BlockSpec(memory_space=pl.ANY), whole((8, 128)), whole((1, D)),
        ],
        out_shape=[
            struct((count, D), BF16),
            struct((count, D)),
            struct((TOPK * H, count), BF16),
            struct((TOPK, count)),
            struct((E, count)),
            struct((flat_rows, 128), BF16),
            struct((8, 128)),
            struct((1, D)),
        ],
        scratch_shapes=[
            pltpu.VMEM((TOPK * H, MB), BF16),
            pltpu.VMEM((QW, MB), BF16),
            pltpu.VMEM((QW, MB), BF16),
            pltpu.VMEM((MB, FF), BF16),
            pltpu.VMEM((MB, FF), BF16),
            pltpu.VMEM((QW, D), F32),
            pltpu.VMEM((D, FF), F32),
            pltpu.VMEM((D, FF), F32),
            pltpu.VMEM((flat_rows - WO_ROW, 128), F32),
            pltpu.VMEM((flat_rows - WO_ROW - 8, 128), BF16),
            pltpu.SemaphoreType.DMA((1,)),
        ],
        compiler_params=params_for(60),
        name="middle",
    )(tokens, grad_out, gain, wo, w1, w2, routes_t, gates, attended)


def head_backward(
    segments, tokens, gain, wall, routes_t, start, queries, datt, lse, delta, kv, kvt, dlogits, dres,
    dgain_two, extra, flat,
):
    count = tokens.shape[0]
    steps = count // TB

    def place(b):
        return (b // NB) * NB + NB - 1 - b % NB

    across = lambda rows: pl.BlockSpec((rows, TB), lambda b: (0, place(b)))
    down = lambda columns: pl.BlockSpec((TB, columns), lambda b: (place(b), 0))
    return pl.pallas_call(
        head_backward_kernel,
        grid=(steps,),
        in_specs=[
            SMEM, down(D), whole((1, D)), whole((ALLW, D)), across(TOPK), across(1),
            across(TOPK * H), across(TOPK * H), across(TOPK), across(TOPK),
            pl.BlockSpec((LEN, 2 * H), lambda b: (b // NB, 0)),
            pl.BlockSpec((2 * H, LEN), lambda b: (0, b // NB)),
            across(E), down(D), whole((1, D)), whole((8, 128)), pl.BlockSpec(memory_space=pl.ANY),
        ],
        out_specs=[down(D), pl.BlockSpec(memory_space=pl.ANY)],
        scratch_shapes=[
            pltpu.VMEM((LEN, H), F32),
            pltpu.VMEM((LEN, H), F32),
            pltpu.VMEM((TOPK * H, TB), BF16),
            pltpu.VMEM((ALLW, TB), BF16),
            pltpu.VMEM((MOST * QB, TOPK * QB), BF16),
            pltpu.VMEM((MOST * QB, TOPK * QB), BF16),
            pltpu.VMEM((ALLW, D), F32),
            pltpu.VMEM((1, D), F32),
            pltpu.VMEM((WO_ROW + 8, 128), F32),
            pltpu.VMEM((WO_ROW + 8, 128), BF16),
            pltpu.SemaphoreType.DMA((1,)),
        ],
        out_shape=[struct((count, D)), struct(flat.shape, BF16)],
        input_output_aliases={16: 1},
        compiler_params=params_for(56),
        name="head_backward",
        cost_estimate=pl.CostEstimate(flops=30_000_000_000, bytes_accessed=24_000_000, transcendentals=0),
    )(
        segments, tokens, gain, wall, routes_t, start, queries, datt, lse, delta, kv, kvt, dlogits, dres,
        dgain_two, extra, flat,
    )


class Mesh3:
    def __init__(self, shards, over):
        shard = lax.axis_index("dp")
        other = lax.axis_index("fsdp")
        self.over = over
        self.many = shards * over
        self.sizes = {"x": 2, "y": shards // 2, "z": over // 2}
        self.here = {"x": lax.rem(other, 2), "y": lax.div(shard, 2), "z": lax.div(other, 2)}
        self.core = lax.rem(shard, 2)
        self.me = shard * over + other
        self.partner = (shard + 1 - 2 * self.core, other)

    def at_z(self, z):
        same = copy.copy(self)
        if z is not None:
            same.here = dict(self.here, z=z)
        return same

    def spots(self):
        x, y, z = (self.sizes[axis] for axis in "xyz")
        return list(itertools.product(range(x), range(y), range(1 - z, z)))

    def round_spots(self):
        return list(itertools.product(*[range(self.sizes[axis]) for axis in "xyz"]))

    def exists(self, z_steps):
        place = self.here["z"] + z_steps
        if isinstance(place, int):
            return 0 <= place < self.sizes["z"]
        return (place >= 0) & (place < self.sizes["z"])

    def device(self, core, spot):
        size = self.sizes["z"]
        x = lax.rem(self.here["x"] + spot[0], self.sizes["x"])
        y = lax.rem(self.here["y"] + spot[1], self.sizes["y"])
        z = self.here["z"] + spot[2]
        z = z % size if isinstance(z, int) else lax.rem(z + size, size)
        return (y * 2 + core, z * 2 + x)

    def number(self, core, spot):
        shard, other = self.device(core, spot)
        return shard * self.over + other

    def greet(self, devices):
        barrier = pltpu.get_barrier_semaphore()
        for device in devices:
            pl.semaphore_signal(barrier, inc=1, device_id=device, device_id_type=MESH)
        pl.semaphore_wait(barrier, len(devices))

    def near(self):
        steps = [at(axis, step) for axis in "xyz" for step in range(1, self.sizes[axis])]
        return [self.device(self.core, step) for step in steps] + [self.partner]

    def column(self):
        steps = [(core, step) for core in range(2) for step in range(self.sizes["z"]) if core or step]
        return [self.device(lax.rem(self.core + core, 2), (0, 0, step)) for core, step in steps]

    def layer(self):
        steps = [(x, y, 0) for x in range(self.sizes["x"]) for y in range(self.sizes["y"]) if x or y]
        return [self.device(self.core, step) for step in steps]


def at(axis, step):
    return tuple(step if one == axis else 0 for one in "xyz")


def last_axis(axes, spot):
    return max([i for i, axis in enumerate(axes) if spot["xyz".index(axis)]], default=-1)


def pieces_of(window, count=2):
    if window < 512:
        return [(0, window)]
    ends = [window // 16 * i // count * 16 for i in range(count)] + [window]
    return [(first, last - first) for first, last in zip(ends, ends[1:])]


def act(condition, action):
    if condition is True:
        action()
    elif condition is not False:
        pl.when(condition)(action)


GATHER_AXES = (("zxy", "yzx"), ("zyx", "xzy"))
REDUCE_PIECES = 3
REDUCE_AXES = ("zxy", "zyx")


def onward(mesh, axes, spot):
    last = last_axis(axes, spot)
    steps = []
    if last >= 0 and axes[last] == "z":
        steps.append(("z", -1 if spot[2] > 0 else 1))
    for axis in axes[last + 1 :]:
        steps += [("z", 1), ("z", -1)] if axis == "z" else [
            (axis, one) for one in range(1, mesh.sizes[axis])
        ]
    return steps


def gather_own_core(mesh, core, land, send_sem, recv_sem, begin):
    window = land.shape[1]
    pieces = pieces_of(window)
    slots = {}
    events = []

    def moved(owner, device, slot, p):
        rows = pl.ds(*pieces[p])
        return pltpu.make_async_remote_copy(
            src_ref=land.at[owner, rows],
            dst_ref=land.at[owner, rows],
            send_sem=send_sem.at[slot, p],
            recv_sem=recv_sem.at[owner, p],
            device_id=device,
            device_id_type=MESH,
        )

    for spot in mesh.spots():
        there = mesh.exists(spot[2])
        if there is False:
            continue
        owner = mesh.number(core, spot)
        turn = 0.5 * abs(spot[2]) + (spot[0] > 0) + (spot[1] > 0) + (0.001 if spot[2] < 0 else 0)
        for p in range(len(pieces)):
            sends = []
            for axis, step in onward(mesh, GATHER_AXES[core][p], spot):
                key = (spot[0], spot[1], spot[2] % mesh.sizes["z"], axis, step)
                away = mesh.exists(step) if axis == "z" else True
                if away is not False:
                    slot = slots.setdefault(key, len(slots))
                    sends.append((mesh.device(core, at(axis, step)), slot, away))
            key = (spot[0], spot[1], spot[2] % mesh.sizes["z"])
            sends.append((mesh.partner, slots.setdefault(key, len(slots)), True))

            def come(owner=owner, spot=spot, p=p, sends=sends):
                if any(spot):
                    moved(owner, mesh.partner, 0, p).wait_recv()
                for device, slot, away in sends:
                    act(away, moved(owner, device, slot, p).start)

            def done(owner=owner, p=p, sends=sends):
                for _, slot, away in sends:
                    act(away, moved(owner, mesh.partner, slot, p).wait_send)

            events.append((turn + 0.01 * p, there, come if begin else done))
    for _, there, action in sorted(events, key=lambda one: one[0]):
        act(there, action)


def gather_blocks(mesh, land, send_sem, recv_sem, begin):
    known = range(mesh.sizes["z"]) if mesh.sizes["z"] <= 4 else [None]
    for core in range(2):
        for z in known:

            @pl.when((mesh.core == core) & (True if z is None else mesh.here["z"] == z))
            def _(core=core, z=z):
                gather_own_core(mesh.at_z(z), core, land, send_sem, recv_sem, begin)


def each_owner(mesh, core, action):
    def one(number, carry):
        shard = 2 * lax.div(number, mesh.over) + core
        action(shard * mesh.over + lax.rem(number, mesh.over))
        return carry

    lax.fori_loop(0, mesh.many // 2, one, 0)


def reduce_blocks(mesh, core, source, mine, outgo, income, send_sem, recv_sem, total_ref):
    pieces = pieces_of(outgo.shape[1], REDUCE_PIECES)
    half = mesh.many // 2
    held = {spot: i for i, spot in enumerate(mesh.round_spots())}

    def across(kind, spot):
        slot = held[spot]
        return pltpu.make_async_remote_copy(
            src_ref=source(mesh.number(kind, spot)),
            dst_ref=income.at[slot],
            send_sem=send_sem.at[slot, 0],
            recv_sem=recv_sem.at[slot, 0],
            device_id=mesh.partner,
            device_id_type=MESH,
        )

    def moved(spot, p, device):
        rows = pl.ds(*pieces[p])
        slot = half + held[spot]
        return pltpu.make_async_remote_copy(
            src_ref=outgo.at[held[spot], rows],
            dst_ref=income.at[slot, rows],
            send_sem=send_sem.at[slot, p],
            recv_sem=recv_sem.at[slot, p],
            device_id=device,
            device_id_type=MESH,
        )

    def far(spot):
        z = {0: 0, 1: 3, 2: 5, 3: 8}.get(spot[2], 2 * spot[2] + 2)
        return z + 2 * (spot[0] > 0) + 2 * (spot[1] > 0)

    for spot in sorted(held, key=far, reverse=True):
        across(1 - core, spot).start()
    axes = REDUCE_AXES[core]
    order = sorted(
        itertools.product(held, range(len(pieces))), key=lambda one: 2 * one[1] / len(pieces) - 2 * far(one[0])
    )
    for spot, p in order:
        if p == 0:
            across(core, spot).wait_recv()
        rows = pl.ds(*pieces[p])
        total = mine(mesh.number(core, spot), *pieces[p]) + income[held[spot], rows].astype(F32)
        last = last_axis(axes, spot)
        for axis in axes[last + 1 :]:
            size = mesh.sizes[axis]
            for step in range(1, size):
                child = tuple(one or other for one, other in zip(spot, at(axis, size - step)))
                moved(child, p, mesh.partner).wait_recv()
                total = total + income[half + held[child], rows].astype(F32)
        if last < 0:
            total_ref[rows, :] = total
        else:
            outgo[held[spot], rows] = total.astype(BF16)
            step = spot["xyz".index(axes[last])]
            moved(spot, p, mesh.device(core, at(axes[last], step))).start()
    for spot, p in order:
        if p == 0:
            across(1 - core, spot).wait_send()
        if any(spot):
            moved(spot, p, mesh.partner).wait_send()


def sum_all(mesh, mine, stats, send_sem, recv_sem):
    column = mesh.sizes["z"] * 2
    layer = mesh.sizes["x"] * mesh.sizes["y"]
    groups = (
        (0, column, mesh.here["z"] * 2 + mesh.core, mesh.column()),
        (column, layer, mesh.here["x"] * mesh.sizes["y"] + mesh.here["y"], mesh.layer()),
    )
    total = mine
    for base, size, here, devices in groups:
        stats[base + here] = total

        def sent(j, device, base=base, here=here):
            return pltpu.make_async_remote_copy(
                src_ref=stats.at[base + here],
                dst_ref=stats.at[base + here],
                send_sem=send_sem.at[base + j],
                recv_sem=recv_sem.at[base + here],
                device_id=device,
                device_id_type=MESH,
            )

        def come(place, base=base):
            return pltpu.make_async_remote_copy(
                src_ref=stats.at[base + place],
                dst_ref=stats.at[base + place],
                send_sem=send_sem.at[base],
                recv_sem=recv_sem.at[base + place],
                device_id=mesh.partner,
                device_id_type=MESH,
            )

        for j, device in enumerate(devices):
            sent(j, device).start()
        for j in range(1, size):
            come(lax.rem(here + j, size)).wait_recv()
        for j, device in enumerate(devices):
            sent(j, device).wait_send()
        total = stats[base]
        for place in range(1, size):
            total = total + stats[base + place]
    return total


def window_rows(shard_size, many):
    units = [(shard_size * d) // UNIT for d in range(many + 1)]
    return 16 * (max(b - a for a, b in zip(units, units[1:])) + 1)


def first_row(shard_size, number):
    if isinstance(number, int):
        return number * shard_size // UNIT * 16
    return pl.multiple_of(lax.div(number * shard_size, UNIT) * 16, 16)


def inner_units(shard_size, many):
    units = [(shard_size * d) // UNIT for d in range(many + 1)]
    return min(b - a for a, b in zip(units, units[1:]))


def lay_inner(shard_size, many, land, flat, owner):
    count = 16 * inner_units(shard_size, many) - 16
    row = pl.multiple_of(first_row(shard_size, owner) + 16, 16)
    flat[pl.ds(row, count), :] = land[owner, pl.ds(16, count), :].astype(F32)


def lay_edges(shard_size, many, land, flat):
    inner = 16 * inner_units(shard_size, many)
    flat[0:16, :] = jnp.zeros((16, 128), F32)

    def lay(number, carry):
        row = first_row(shard_size, number)
        after = first_row(shard_size, number + 1)
        flat[pl.ds(row, 16), :] += land[number, 0:16, :].astype(F32)
        tail = land[number, pl.ds(inner, 16), :].astype(F32)
        flat[pl.ds(pl.multiple_of(row + inner, 16), 16), :] = tail
        last = pl.multiple_of(after - row, 16)
        flat[pl.ds(after, 16), :] = land[number, pl.ds(last, 16), :].astype(F32)
        return carry

    lax.fori_loop(0, many, lay, 0)


def early_matrices(flat, wall_ref, gain_one_ref, gain_two_ref):
    for c in range(D // 128):
        lanes = slice(c * 128, (c + 1) * 128)
        gain_one_ref[:, lanes] = flat[c : c + 1, :]
        gain_two_ref[:, lanes] = flat[4 + c : 5 + c, :]
    for c in range(QW // 128):
        wall_ref[c * 128 : (c + 1) * 128, :] = flat[pl.ds(WQ_ROW + c, D, stride=12), :].T.astype(BF16)
    for first, row in ((KROW, WK_ROW), (VROW, WV_ROW)):
        pair = flat[row : row + 256, :].T.astype(BF16)
        wall_ref[first : first + H, :] = (
            nn(pair[:H], picks(256, 2, 0).astype(BF16)) + nn(pair[H:], picks(256, 2, 1).astype(BF16))
        ).astype(BF16)
    across = jnp.concatenate(
        [flat[pl.ds(WR_ROW + j, 32, stride=3), :] for j in range(3)], axis=1
    ).T.astype(BF16)
    router_t = jnp.zeros((E, D), F32)
    for part in range(16):
        router_t = router_t + nn(across[part * E : (part + 1) * E, :], picks(32, 16, part).astype(BF16))
    wall_ref[RROW:ALLW, :] = jnp.concatenate(
        [router_t, jnp.zeros((ALLW - RROW - E, D), F32)], axis=0
    ).astype(BF16)


def gather_kernel(
    mesh, shard_size, own_ref,
    wall_out, gain_one_ref, gain_two_ref, wo_out, w1_out, w2_out,
    land, flat, wall_ref, wo_ref, w1_ref, w2_ref, send_sem, recv_sem, out_sem,
):
    mesh = mesh()
    many = mesh.many
    mesh.greet(mesh.near())
    land[mesh.me] = own_ref[...].astype(BF16)
    gather_blocks(mesh, land, send_sem, recv_sem, True)
    each_owner(mesh, mesh.core, functools.partial(lay_inner, shard_size, many, land, flat))

    def arrive(owner):
        for p in range(recv_sem.shape[1]):
            rows = pl.ds(*pieces_of(own_ref.shape[0])[p])
            pltpu.make_async_remote_copy(
                src_ref=land.at[owner, rows],
                dst_ref=land.at[owner, rows],
                send_sem=send_sem.at[0, p],
                recv_sem=recv_sem.at[owner, p],
                device_id=mesh.partner,
                device_id_type=MESH,
            ).wait_recv()
        lay_inner(shard_size, many, land, flat, owner)

    each_owner(mesh, 1 - mesh.core, arrive)
    lay_edges(shard_size, many, land, flat)
    copies = []

    def leave(matrix, out):
        one = pltpu.make_async_copy(matrix, out, out_sem.at[len(copies)])
        one.start()
        copies.append(one)

    for c in range(D // 128):
        wo_ref[:, c * 128 : (c + 1) * 128] = flat[pl.ds(WO_ROW + c, QW, stride=4), :].astype(BF16)
    leave(wo_ref, wo_out)
    for c in range(D // 128):
        w2_ref[:, c * 128 : (c + 1) * 128] = flat[pl.ds(W2_ROW + c, FF, stride=4), :].astype(BF16)
    leave(w2_ref, w2_out)
    for c in range(FF // 128):
        w1_ref[:, c * 128 : (c + 1) * 128] = flat[pl.ds(W1_ROW + c, D, stride=16), :].astype(BF16)
    leave(w1_ref, w1_out)
    early_matrices(flat, wall_ref, gain_one_ref, gain_two_ref)
    leave(wall_ref, wall_out)
    gather_blocks(mesh, land, send_sem, recv_sem, False)
    for one in copies:
        one.wait()


def gather_weights(shards, over, shard_size, own):
    window = own.shape[0]
    many = shards * over
    rows = (shard_size * (many - 1)) // UNIT * 16 + window
    vmem = pl.BlockSpec(memory_space=pltpu.VMEM)
    hbm = pl.BlockSpec(memory_space=pl.ANY)
    mesh = functools.partial(Mesh3, shards, over)
    pieces = len(pieces_of(window))
    return pl.pallas_call(
        functools.partial(gather_kernel, mesh, shard_size),
        in_specs=[vmem],
        out_specs=[hbm, vmem, vmem, hbm, hbm, hbm],
        out_shape=[
            struct((ALLW, D), BF16),
            struct((1, D)),
            struct((1, D)),
            struct((QW, D), BF16),
            struct((D, FF), BF16),
            struct((FF, D), BF16),
        ],
        scratch_shapes=[
            pltpu.VMEM((many, window, 128), BF16),
            pltpu.VMEM((rows, 128), F32),
            pltpu.VMEM((ALLW, D), BF16),
            pltpu.VMEM((QW, D), BF16),
            pltpu.VMEM((D, FF), BF16),
            pltpu.VMEM((FF, D), BF16),
            pltpu.SemaphoreType.DMA((5 * many // 2, pieces)),
            pltpu.SemaphoreType.DMA((many, pieces)),
            pltpu.SemaphoreType.DMA((4,)),
        ],
        compiler_params=pltpu.CompilerParams(
            collective_id=0, has_side_effects=True, vmem_limit_bytes=60 * MIB
        ),
        name="gather_weights",
    )(own)


def reduce_kernel(
    mesh, shard_size, flat_ref, count_ref,
    out_ref, total_ref, gain_ref,
    part, outgo, income, whole_scr, stats, part_sem, send_sem, recv_sem, stat_send, stat_recv,
):
    mesh = mesh()
    window = outgo.shape[1]
    span = part.shape[1]

    def source(owner):
        return flat_ref.at[pl.ds(first_row(shard_size, owner), window), :]

    def fetch(y):
        first = first_row(shard_size, (2 * y + mesh.core) * mesh.over)
        return pltpu.make_async_copy(flat_ref.at[pl.ds(first, span), :], part.at[y], part_sem.at[y])

    def mine(owner, first, rows):
        shard = lax.div(owner, mesh.over)
        row = first_row(shard_size, owner) - first_row(shard_size, shard * mesh.over) + first
        return part[lax.div(shard, 2), pl.ds(pl.multiple_of(row, 16), rows), :].astype(F32)

    for y in range(mesh.sizes["y"]):
        fetch(y).start()
    mesh.greet(mesh.column() + mesh.layer())
    for y in range(mesh.sizes["y"]):
        fetch(y).wait()
    buffers = (source, mine, outgo, income, send_sem, recv_sem, whole_scr)
    for core in range(2):
        pl.when(mesh.core == core)(functools.partial(reduce_blocks, mesh, core, *buffers))

    begin = mesh.me * shard_size - lax.div(mesh.me * shard_size, UNIT) * UNIT
    rows = out_ref.shape[0]
    row, lane = lax.div(begin, 128), lax.rem(begin, 128)
    back = lax.rem(128 - lane, 128)
    first = pltpu.roll(whole_scr[pl.ds(row, rows), :], back, 1)
    second = pltpu.roll(whole_scr[pl.ds(row + 1, rows), :], back, 1)
    at_lane = lax.broadcasted_iota(jnp.int32, (rows, 128), 1)
    place = lax.broadcasted_iota(jnp.int32, (rows, 128), 0) * 128 + at_lane
    total = jnp.where(at_lane < 128 - lane, first, second)
    out_ref[...] = total
    inside = jnp.where(place < shard_size, total, 0.0)
    squares = jnp.sum(jnp.sum(inside * inside, axis=0, keepdims=True), axis=1, keepdims=True)
    lane = lax.broadcasted_iota(jnp.int32, (8, 128), 1)
    row = jnp.where(lane == E, squares, count_ref[...])
    gains = jnp.where(mesh.me == 0, total[0:8, :], 0.0)
    summed = sum_all(mesh, jnp.concatenate([row, gains], axis=0), stats, stat_send, stat_recv)
    total_ref[...] = summed[0:1, :]
    for c in range(D // 128):
        lanes = slice(c * 128, (c + 1) * 128)
        gain_ref[0:1, lanes] = summed[8 + c : 9 + c, :]
        gain_ref[1:2, lanes] = summed[12 + c : 13 + c, :]


def reduce_grads(shards, over, shard_size, window, flat, counts):
    vmem = pl.BlockSpec(memory_space=pltpu.VMEM)
    many = shards * over
    mesh = functools.partial(Mesh3, shards, over)
    pieces = len(pieces_of(window, REDUCE_PIECES))
    steps = over + shards
    units = [(shard_size * d) // UNIT for d in range(many)]
    span = 16 * max(units[d + over - 1] - units[d] for d in range(0, many, over)) + window
    return pl.pallas_call(
        functools.partial(reduce_kernel, mesh, shard_size),
        in_specs=[pl.BlockSpec(memory_space=pl.ANY), vmem],
        out_specs=[vmem] * 3,
        out_shape=[struct((-(-shard_size // 128), 128)), struct((1, 128)), struct((2, D))],
        scratch_shapes=[
            pltpu.VMEM((shards // 2, span, 128), BF16),
            pltpu.VMEM((many // 2, window, 128), BF16),
            pltpu.VMEM((many, window, 128), BF16),
            pltpu.VMEM((window + 16, 128), F32),
            pltpu.VMEM((steps, 16, 128), F32),
            pltpu.SemaphoreType.DMA((shards // 2,)),
            pltpu.SemaphoreType.DMA((many, pieces)),
            pltpu.SemaphoreType.DMA((many, pieces)),
            pltpu.SemaphoreType.DMA((steps,)),
            pltpu.SemaphoreType.DMA((steps,)),
        ],
        compiler_params=pltpu.CompilerParams(
            collective_id=1, has_side_effects=True, vmem_limit_bytes=56 * MIB
        ),
        name="reduce_grads",
    )(flat, counts)


def local_step(flat_rows, tokens, grad_out, routes, segments, weights):
    wall, gain_one, gain_two, wo, w1, w2 = weights
    queries, attended, gates, lse, kv, kvt, start, routes_t, counts = head_forward(
        tokens, routes.T, segments, wall, gain_one
    )
    output, dres, datt, delta, dlogits, flat, extra, dgain_two = middle(
        flat_rows, tokens, grad_out, gain_two, wo, w1, w2, routes_t, gates, attended
    )
    input_grad, flat = head_backward(
        segments, tokens, gain_one, wall, routes_t, start, queries, datt, lse, delta, kv, kvt, dlogits, dres,
        dgain_two, extra, flat,
    )
    return output, input_grad, flat, counts


def per_device(
    shards, over, tokens, grad_out, routes, segments, params, first_moment, second_moment, ema_weights
):
    shard_size = params.shape[0]
    window = window_rows(shard_size, shards * over)
    flat_rows = (shard_size * (shards * over - 1)) // UNIT * 16 + window + 16
    me = lax.axis_index("dp") * over + lax.axis_index("fsdp")
    begin = lax.rem(me * shard_size, UNIT)
    own = lax.dynamic_slice(
        jnp.pad(params, (UNIT, window * 128 - shard_size)), (UNIT - begin,), (window * 128,)
    ).reshape(window, 128)
    wall, gain_one, gain_two, wo, w1, w2 = gather_weights(shards, over, shard_size, own)
    output, input_grad, flat, counts = local_step(
        flat_rows, tokens, grad_out, routes, segments, (wall, gain_one, gain_two, wo, w1, w2)
    )
    reduced, sums, gain_grads = reduce_grads(shards, over, shard_size, window, flat, counts)
    grad_shard = reduced.reshape(-1)[:shard_size]
    total_tokens = tokens.shape[0] * shards * over
    expert_load = sums[0, :E] * (E / (total_tokens * TOPK))
    grad_norm = jnp.sqrt(sums[0, E])
    clipped = grad_shard * (CLIP_LIMIT / jnp.maximum(grad_norm, CLIP_LIMIT))
    new_first = BETA_FIRST * first_moment + (1.0 - BETA_FIRST) * clipped
    new_second = BETA_SECOND * second_moment + (1.0 - BETA_SECOND) * clipped * clipped
    first_hat = new_first / (1.0 - BETA_FIRST**STEP)
    second_hat = new_second / (1.0 - BETA_SECOND**STEP)
    new_params = params * (1.0 - LEARN_RATE * DECAY_RATE) - LEARN_RATE * first_hat / (
        jnp.sqrt(second_hat) + ADAM_EPS
    )
    new_ema = EMA_KEEP * ema_weights + (1.0 - EMA_KEEP) * new_params
    return (
        output,
        input_grad,
        expert_load,
        grad_norm.reshape(1),
        new_params,
        new_first,
        new_second,
        new_ema,
        gain_grads,
    )


def solution(mesh):
    row = P(("dp", "fsdp"), None)
    flat = P(("dp", "fsdp"))
    return jax.shard_map(
        functools.partial(per_device, mesh.shape["dp"], mesh.shape["fsdp"]),
        mesh=mesh,
        in_specs=(row, row, row, row, flat, flat, flat, flat),
        out_specs=(row, row, P(), P(), flat, flat, flat, flat, P()),
        check_vma=False,
    )
```

```python
import copy
import functools
import itertools

import jax
import jax.numpy as jnp
from jax import lax
from jax.experimental import pallas as pl
from jax.experimental.pallas import tpu as pltpu
from jax.sharding import PartitionSpec as P

D = 512
E = 24
TOPK = 8
H = 64
FF = 2048
STEP = 10

NORM_EPS = 1e-06
CLIP_LIMIT = 1.0
BETA_FIRST = 0.9
BETA_SECOND = 0.95
LEARN_RATE = 0.1
DECAY_RATE = 0.1
ADAM_EPS = 1e-08
EMA_KEEP = 0.9
NEG_LARGE = -1e30

QW = E * H
KROW = QW
VROW = QW + H
RROW = QW + 2 * H
ALLW = 1696
LEN = 1024
TB = 512
NB = LEN // TB
QB = 128
SIDE = 4
MOST = 512 // QB + 1
SORT_STEPS = (
    (0, 1), (2, 3), (4, 5), (6, 7), (0, 2), (1, 3), (4, 6), (5, 7), (1, 2), (5, 6),
    (0, 4), (1, 5), (2, 6), (3, 7), (2, 4), (3, 5), (1, 2), (3, 4), (5, 6),
)
FC = 256
MB = 512
MIB = 1 << 20

WR_ROW = 8
WK_ROW = 104
WV_ROW = 360
WQ_ROW = 616
WO_ROW = 6760
W1_ROW = 12904
W2_ROW = 21096
ALL_ROWS = 29288
UNIT = 16 * 128
MESH = pl.DeviceIdType.MESH

F32 = jnp.float32
BF16 = jnp.bfloat16


def nn(a, b):
    return lax.dot_general(a, b, (((1,), (0,)), ((), ())), preferred_element_type=F32)


def nt(a, b):
    return lax.dot_general(a, b, (((1,), (1,)), ((), ())), preferred_element_type=F32)


def tn(a, b):
    return lax.dot_general(a, b, (((0,), (0,)), ((), ())), preferred_element_type=F32)


def rms_scale(values):
    return lax.rsqrt(jnp.mean(values * values, axis=-1, keepdims=True) + NORM_EPS)


def slot_of(routes, k, rows):
    return jnp.broadcast_to(routes[k : k + 1, :], (rows, routes.shape[1]))


def expert_rows(routes, k):
    return jnp.broadcast_to(routes.astype(jnp.int16)[k : k + 1, :], (16, routes.shape[1]))


def pick_heads(routes, source_ref, k):
    tokens = routes.shape[1]
    route = expert_rows(routes, k)
    taken = source_ref[k * H : (k + 1) * H, :].reshape(H // 16, 16, tokens)
    for e in range(k + 1, k + E - TOPK + 1):
        piece = source_ref[e * H : (e + 1) * H, :].reshape(H // 16, 16, tokens)
        taken = jnp.where((route == jnp.int16(e))[None], piece, taken)
    return taken.reshape(H, tokens)


def place_heads(routes, source_ref, target_ref, experts):
    tokens = routes.shape[1]
    rows = [expert_rows(routes, k) for k in range(TOPK)]
    for e in experts:
        total = jnp.zeros((H // 16, 16, tokens), BF16)
        for k in range(max(0, e - (E - TOPK)), min(TOPK - 1, e) + 1):
            piece = source_ref[k * H : (k + 1) * H, :].reshape(H // 16, 16, tokens)
            total = jnp.where((rows[k] == jnp.int16(e))[None], piece, total)
        target_ref[e * H : (e + 1) * H, :] = total.reshape(H, tokens)


def sorted_rows(rows):
    rows = list(rows)
    for one, two in SORT_STEPS:
        rows[one], rows[two] = jnp.minimum(rows[one], rows[two]), jnp.maximum(rows[one], rows[two])
    return rows


def key_mask(first_key, first_query, rows, start_row):
    keys = lax.broadcasted_iota(jnp.int32, (rows, QB), 0) + first_key
    queries = lax.broadcasted_iota(jnp.int32, (rows, QB), 1) + first_query
    mask = (keys <= queries) & (keys >= start_row)
    return jnp.concatenate([mask] * SIDE, axis=1)


def group_of(ref, k, lanes):
    return jnp.concatenate([ref[i * H : (i + 1) * H, lanes] for i in range(k, k + SIDE)], axis=1)


def row_group(ref, k, lanes):
    return jnp.concatenate([ref[i : i + 1, lanes] for i in range(k, k + SIDE)], axis=1)


def by_span(attend, row, place, segment_ref):
    def one(j, carry):
        block = place * (TB // QB) + j
        first = block * QB
        span = jnp.int32(1)
        for back in range(MOST - 1):
            last = first - back * QB - 1
            same = segment_ref[row, jnp.maximum(last, 0)] == segment_ref[row, first]
            span = span + jnp.where((last >= 0) & same, 1, 0)
        for blocks in range(1, MOST + 1):

            @pl.when(span == blocks)
            def _(blocks=blocks):
                attend(pl.ds(pl.multiple_of(j * QB, QB), QB), block, blocks)

        return carry

    lax.fori_loop(0, TB // QB, one, 0)


def head_forward_kernel(
    steps, segment_smem, x_ref, route_ref, segment_ref, wall_ref, gain_ref,
    q_ref, att_ref, gate_ref, lse_ref, kv_ref, kvt_ref, start_ref, sorted_ref, count_ref,
    all_scr, low_scr, k_scr, vt_scr, count_scr,
):
    step = pl.program_id(0)
    place = lax.rem(step, NB)
    here = pl.multiple_of(place * TB, TB)

    @pl.when(step == 0)
    def _():
        count_scr[...] = jnp.zeros_like(count_scr)

    row = segment_ref[pl.ds(lax.div(step, NB), 1), :]
    segments = segment_ref[pl.ds(lax.div(step, NB), 1), pl.ds(here, TB)]
    start = jnp.zeros((1, TB), jnp.int32)
    for number in range(1, 4):
        below = jnp.sum((row < number).astype(jnp.int32), axis=1, keepdims=True)
        start = jnp.where(segments == number, below, start)
    start_ref[...] = start
    x = x_ref[...].astype(F32)
    normed = (x * rms_scale(x) * gain_ref[...]).astype(BF16)
    all_scr[KROW:, :] = nt(wall_ref[KROW:, :], normed)
    soon = (E - TOPK + 1) * H
    low_scr[0:soon, :] = nt(wall_ref[0:soon, :], normed).astype(BF16)
    kt = all_scr[KROW : KROW + H, :]
    vt = all_scr[VROW : VROW + H, :]
    logits = all_scr[RROW : RROW + E, :]
    kvt = jnp.concatenate([kt, vt], axis=0)
    kv = kvt.T.astype(BF16)
    kv_ref[...] = kv
    kvt_ref[...] = kvt.astype(BF16)
    k_scr[pl.ds(here, TB), :] = kv[:, :H]
    vt_scr[:, pl.ds(here, TB)] = vt.astype(BF16)
    routes = jnp.concatenate(sorted_rows(route_ref[k : k + 1, :] for k in range(TOPK)), axis=0)
    sorted_ref[...] = routes
    experts = lax.broadcasted_iota(jnp.int32, (E, TB), 0)
    chosen = []
    counts = count_scr[...]
    for k in range(TOPK):
        named = slot_of(routes, k, E) == experts
        chosen.append(jnp.sum(jnp.where(named, logits, 0.0), axis=0, keepdims=True))
        counts = counts + named.astype(F32)
    count_scr[...] = counts
    chosen = jnp.concatenate(chosen, axis=0)
    raised = jnp.exp(chosen - jnp.max(chosen, axis=0, keepdims=True))
    gate_ref[...] = raised / jnp.sum(raised, axis=0, keepdims=True)
    for k in range(TOPK):
        if k + 1 < TOPK:
            after = slice(soon + k * H, soon + (k + 1) * H)
            low_scr[after, :] = nt(wall_ref[after, :], normed).astype(BF16)
        q_ref[k * H : (k + 1) * H, :] = pick_heads(routes, low_scr, k) * jnp.asarray(H ** (-0.5), BF16)

    def attend(lanes, block, blocks):
        rows = blocks * QB
        first_key = pl.multiple_of((block - (blocks - 1)) * QB, QB)
        mask = key_mask(first_key, block * QB, rows, start_ref[:, lanes])
        keys = k_scr[pl.ds(first_key, rows), :]
        values = vt_scr[:, pl.ds(first_key, rows)]
        groups = [nn(keys, group_of(q_ref, 0, lanes))]
        for k in range(0, TOPK, SIDE):
            if k + SIDE < TOPK:
                groups.append(nn(keys, group_of(q_ref, k + SIDE, lanes)))
            scores = jnp.where(mask, groups[k // SIDE], NEG_LARGE)
            top = jnp.max(scores, axis=0, keepdims=True)
            raised = jnp.exp(scores - top)
            total = jnp.sum(raised, axis=0, keepdims=True)
            out = nn(values, (raised * (1.0 / total)).astype(BF16))
            lse = top + jnp.log(total)
            for side in range(SIDE):
                one = slice(side * QB, (side + 1) * QB)
                att_ref[(k + side) * H : (k + side + 1) * H, lanes] = out[:, one]
                lse_ref[k + side : k + side + 1, lanes] = lse[:, one]

    by_span(attend, lax.div(step, NB), place, segment_smem)

    @pl.when(step == steps - 1)
    def _():
        held = jnp.sum(count_scr[...], axis=1, keepdims=True)
        lane = lax.broadcasted_iota(jnp.int32, (E, 128), 1)
        row = lax.broadcasted_iota(jnp.int32, (E, 128), 0)
        count_ref[...] = jnp.sum(jnp.where(lane == row, held, 0.0), axis=0, keepdims=True)


def picks(rows, stride, first):
    at = lax.broadcasted_iota(jnp.int32, (rows, D), 1)
    row = lax.broadcasted_iota(jnp.int32, (rows, D), 0)
    return (at == row * stride + first).astype(F32)


def exact(product, a, b):
    return lax.dot_general(
        a, b, (product, ((), ())), precision=lax.Precision.HIGHEST, preferred_element_type=F32
    )


def gelu_parts(v):
    cdf = 0.5 + 0.5 * lax.erf(v * 0.7071067811865476)
    return cdf, jnp.exp(v * v * -0.5) * 0.3989422804014327


def middle_kernel(
    x_ref, dy_ref, gain_ref, wo_ref, w1_ref, w2_ref, route_ref, gate_ref, att_ref,
    out_ref, dres_ref, datt_ref, delta_ref, dlogit_ref, flat_ref, extra_ref, dgain_ref,
    slot_scr, head_scr, mix_scr, hidden_scr, dpre_scr, branch_scr, dwo_ref, dw1_ref, dw2t_ref, rows_scr, low_scr, row_sem,
):
    step = pl.program_id(0)

    @pl.when(step == 0)
    def _():
        dwo_ref[...] = jnp.zeros_like(dwo_ref)
        dw1_ref[...] = jnp.zeros_like(dw1_ref)
        dw2t_ref[...] = jnp.zeros_like(dw2t_ref)
        dgain_ref[...] = jnp.zeros_like(dgain_ref)

    routes = route_ref[...]
    tokens = routes.shape[1]
    gates = gate_ref[...]
    for k in range(TOPK):
        rows = slice(k * H, (k + 1) * H)
        slot_scr[rows, :] = (gates[k : k + 1, :] * att_ref[rows, :]).astype(BF16)
    x = x_ref[...].astype(F32)
    dy = dy_ref[...]
    chunks = [slice(c, c + FC) for c in range(0, FF, FC)]
    share = E // len(chunks)
    back = []
    for i, here in enumerate(chunks):
        place_heads(routes, slot_scr, mix_scr, range(i * share, (i + 1) * share))
        back.append(nt(dy, w2_ref[here, :]))
    residual = x + tn(mix_scr[...], wo_ref[...])
    scale = rms_scale(residual)
    gain = gain_ref[...]
    second = (residual * scale * gain).astype(BF16)
    second_t = second.T
    dy_t = dy.T

    def weight_sums(here):
        dw1_ref[:, here] += nn(second_t, dpre_scr[:, here])
        dw2t_ref[:, here] += nn(dy_t, hidden_scr[:, here])

    pre = [nn(second, w1_ref[:, chunks[0]])]
    for i, here in enumerate(chunks):
        if i + 1 < len(chunks):
            pre.append(nn(second, w1_ref[:, chunks[i + 1]]))
        cdf, density = gelu_parts(pre[i])
        hidden_scr[:, here] = (pre[i] * cdf).astype(BF16)
        dpre_scr[:, here] = (back[i] * (cdf + pre[i] * density)).astype(BF16)
        if i > 0:
            weight_sums(chunks[i - 1])
    dsecond = nt(dpre_scr[...], w1_ref[...])
    weight_sums(chunks[-1])
    dgain = jnp.zeros((1, D), F32)
    for first in range(0, tokens, 128):
        part = slice(first, first + 128)
        res, dsec, rms = residual[part], dsecond[part], scale[part]
        out_ref[part, :] = (res + nn(hidden_scr[part, :], w2_ref[...])).astype(BF16)
        dgain = dgain + jnp.sum(dsec * res * rms, axis=0, keepdims=True)
        weighted = gain * dsec
        dres = (
            dy[part].astype(F32)
            + rms * weighted
            - res * (rms * rms * rms) * jnp.mean(weighted * res, axis=-1, keepdims=True)
        )
        dres_ref[part, :] = dres
        branch_scr[part, :] = dres.astype(BF16)
    dgain_ref[...] += dgain
    branch = branch_scr[...]
    head_scr[...] = nt(wo_ref[...], branch).astype(BF16)
    dgates = []
    share = QW // TOPK
    for k in range(TOPK):
        rows = slice(k * H, (k + 1) * H)
        dslot = pick_heads(routes, head_scr, k).astype(F32)
        attended = att_ref[rows, :]
        dgates.append(jnp.sum(dslot * attended, axis=0, keepdims=True))
        datt = (gates[k : k + 1, :] * dslot).astype(BF16)
        datt_ref[rows, :] = datt
        delta_ref[k : k + 1, :] = jnp.sum(datt.astype(F32) * attended, axis=0, keepdims=True)
        wide = slice(k * share, (k + 1) * share)
        dwo_ref[wide, :] += nn(mix_scr[wide, :], branch)
    dgate = jnp.concatenate(dgates, axis=0)
    dchosen = gates * (dgate - jnp.sum(gates * dgate, axis=0, keepdims=True))
    experts = lax.broadcasted_iota(jnp.int32, (E, tokens), 0)
    dlogits = jnp.zeros((E, tokens), F32)
    for k in range(TOPK):
        dlogits = jnp.where(
            slot_of(routes, k, E) == experts,
            jnp.broadcast_to(dchosen[k : k + 1, :], (E, tokens)),
            dlogits,
        )
    dlogit_ref[...] = dlogits

    @pl.when(step == pl.num_programs(0) - 1)
    def _():
        for c in range(D // 128):
            lanes = slice(c * 128, (c + 1) * 128)
            rows_scr[pl.ds(c, QW, stride=4), :] = dwo_ref[:, lanes]
            rows_scr[pl.ds(W2_ROW - WO_ROW + c, FF, stride=4), :] = dw2t_ref[lanes, :].T
        for c in range(FF // 128):
            rows_scr[pl.ds(W1_ROW - WO_ROW + c, D, stride=16), :] = dw1_ref[:, c * 128 : (c + 1) * 128]
        extra_ref[...] = rows_scr[0:8, :]
        low_scr[...] = rows_scr[8:, :].astype(BF16)
        copy = pltpu.make_async_copy(
            low_scr, flat_ref.at[pl.ds(WO_ROW + 8, low_scr.shape[0]), :], row_sem.at[0]
        )
        copy.start()
        copy.wait()


def head_backward_kernel(
    segment_smem, x_ref, gain_ref, wall_ref, route_ref, start_ref, q_ref, datt_ref,
    lse_ref, delta_ref, kv_ref, kvt_ref, dlogit_ref, dres_ref, dgain_two_ref, extra_ref, flat_in,
    dx_ref, flat_ref,
    dk_scr, dv_scr, dq_scr, dall_scr, prob_scr, dscore_scr, dwall_ref, dgain_ref, rows_scr, low_scr, row_sem,
):
    step = pl.program_id(0)
    place = NB - 1 - lax.rem(step, NB)
    here = pl.multiple_of(place * TB, TB)

    @pl.when(step == 0)
    def _():
        dwall_ref[...] = jnp.zeros_like(dwall_ref)
        dgain_ref[...] = jnp.zeros_like(dgain_ref)

    @pl.when(lax.rem(step, NB) == 0)
    def _():
        dk_scr[...] = jnp.zeros_like(dk_scr)
        dv_scr[...] = jnp.zeros_like(dv_scr)

    def attend(lanes, block, blocks):
        rows = blocks * QB
        first_key = pl.multiple_of((block - (blocks - 1)) * QB, QB)
        mask = key_mask(first_key, block * QB, rows, start_ref[:, lanes])
        keys = kv_ref[pl.ds(first_key, rows), :H]
        values = kv_ref[pl.ds(first_key, rows), H:]
        keys_t = kvt_ref[:H, pl.ds(first_key, rows)]
        queries = [group_of(q_ref, k, lanes) for k in range(0, TOPK, SIDE)]
        datts = [group_of(datt_ref, k, lanes) for k in range(0, TOPK, SIDE)]
        scores = [nn(keys, queries[0])]
        dprobs = [nn(values, datts[0])]
        for i in range(TOPK // SIDE):
            if i + 1 < TOPK // SIDE:
                scores.append(nn(keys, queries[i + 1]))
                dprobs.append(nn(values, datts[i + 1]))
            k = i * SIDE
            wide = slice(k * QB, (k + SIDE) * QB)
            probs = jnp.exp(jnp.where(mask, scores[i], NEG_LARGE) - row_group(lse_ref, k, lanes))
            dscore = (probs * (dprobs[i] - row_group(delta_ref, k, lanes))).astype(BF16)
            prob_scr[0:rows, wide] = probs.astype(BF16)
            dscore_scr[0:rows, wide] = dscore
            dq = (nn(keys_t, dscore) * (H ** (-0.5))).astype(BF16)
            for side in range(SIDE):
                dq_scr[(k + side) * H : (k + side + 1) * H, lanes] = dq[:, side * QB : (side + 1) * QB]
        dv_scr[pl.ds(first_key, rows), :] += nt(prob_scr[0:rows, :], jnp.concatenate(datts, axis=1))
        dk_scr[pl.ds(first_key, rows), :] += nt(dscore_scr[0:rows, :], jnp.concatenate(queries, axis=1))

    by_span(attend, lax.div(step, NB), place, segment_smem)
    dkv = jnp.concatenate([dk_scr[pl.ds(here, TB), :], dv_scr[pl.ds(here, TB), :]], axis=1)
    dall_scr[KROW : KROW + 2 * H, :] = dkv.T.astype(BF16)
    dall_scr[RROW : RROW + 32, :] = jnp.concatenate(
        [dlogit_ref[...], jnp.zeros((32 - E, TB), F32)], axis=0
    ).astype(BF16)
    x = x_ref[...].astype(F32)
    scale = rms_scale(x)
    gain = gain_ref[...]
    normed = (x * scale * gain).astype(BF16)
    for e in range(0, E, 4):
        place_heads(route_ref[...], dq_scr, dall_scr, range(e, e + 4))
        rows = slice(e * H, (e + 4) * H)
        dwall_ref[rows, :] += nn(dall_scr[rows, :], normed)
    dwall_ref[KROW:, :] += nn(dall_scr[KROW:, :], normed)
    dnormed = tn(dall_scr[...], wall_ref[...])
    dgain_ref[...] += jnp.sum(dnormed * x * scale, axis=0, keepdims=True)
    weighted = gain * dnormed
    dx_ref[...] = (
        dres_ref[...]
        + scale * weighted
        - x * (scale * scale * scale) * jnp.mean(weighted * x, axis=-1, keepdims=True)
    )

    @pl.when(step == pl.num_programs(0) - 1)
    def _():
        for c in range(D // 128):
            lanes = slice(c * 128, (c + 1) * 128)
            rows_scr[c : c + 1, :] = dgain_ref[:, lanes]
            rows_scr[4 + c : 5 + c, :] = dgain_two_ref[:, lanes]
        router_t = dwall_ref[RROW : RROW + E, :]
        across = jnp.concatenate(
            [exact(((1,), (1,)), router_t, picks(32, 16, b)) for b in range(16)], axis=0
        ).T
        for j in range(3):
            rows_scr[pl.ds(WR_ROW + j, 32, stride=3), :] = across[:, j * 128 : (j + 1) * 128]
        for first, row in ((KROW, WK_ROW), (VROW, WV_ROW)):
            part = dwall_ref[first : first + H, :]
            rows_scr[row : row + 256, :] = jnp.concatenate(
                [exact(((1,), (1,)), picks(256, 2, b), part) for b in range(2)], axis=1
            )
        for c in range(QW // 128):
            rows_scr[pl.ds(WQ_ROW + c, D, stride=12), :] = dwall_ref[c * 128 : (c + 1) * 128, :].T
        rows_scr[WO_ROW : WO_ROW + 8, :] = extra_ref[...]
        low_scr[...] = rows_scr[...].astype(BF16)
        copy = pltpu.make_async_copy(low_scr, flat_ref.at[pl.ds(0, WO_ROW + 8), :], row_sem.at[0])
        copy.start()
        copy.wait()


def whole(shape):
    return pl.BlockSpec(shape, lambda *_: (0,) * len(shape), pipeline_mode=pl.Buffered(1))


def kept(shape):
    return pl.BlockSpec(shape, lambda *_: (0,) * len(shape))


SMEM = pl.BlockSpec(memory_space=pltpu.SMEM)


def struct(shape, kind=F32):
    return jax.ShapeDtypeStruct(shape, kind)


def params_for(mib):
    return pltpu.CompilerParams(vmem_limit_bytes=mib * MIB)


def head_forward(tokens, routes_t, segments, wall, gain):
    count = tokens.shape[0]
    steps = count // TB
    across = lambda rows: pl.BlockSpec((rows, TB), lambda b: (0, b))
    down = lambda columns: pl.BlockSpec((TB, columns), lambda b: (b, 0))
    return pl.pallas_call(
        functools.partial(head_forward_kernel, steps),
        grid=(steps,),
        in_specs=[SMEM, down(D), across(TOPK), whole(segments.shape), whole((ALLW, D)), whole((1, D))],
        out_specs=[
            across(TOPK * H), across(TOPK * H), across(TOPK), across(TOPK), down(2 * H), across(2 * H),
            across(1), across(TOPK), whole((1, 128)),
        ],
        scratch_shapes=[
            pltpu.VMEM((ALLW, TB), F32),
            pltpu.VMEM((QW, TB), BF16),
            pltpu.VMEM((LEN, H), BF16),
            pltpu.VMEM((H, LEN), BF16),
            pltpu.VMEM((E, TB), F32),
        ],
        out_shape=[
            struct((TOPK * H, count), BF16),
            struct((TOPK * H, count)),
            struct((TOPK, count)),
            struct((TOPK, count)),
            struct((count, 2 * H), BF16),
            struct((2 * H, count), BF16),
            struct((1, count), jnp.int32),
            struct((TOPK, count), jnp.int32),
            struct((1, 128)),
        ],
        compiler_params=params_for(56),
        name="head_forward",
        cost_estimate=pl.CostEstimate(flops=10_000_000_000, bytes_accessed=16_000_000, transcendentals=0),
    )(segments, tokens, routes_t, segments, wall, gain)


def middle(flat_rows, tokens, grad_out, gain, wo, w1, w2, routes_t, gates, attended):
    count = tokens.shape[0]
    steps = count // MB
    across = lambda rows: pl.BlockSpec((rows, MB), lambda b: (0, b))
    down = lambda columns: pl.BlockSpec((MB, columns), lambda b: (b, 0))
    return pl.pallas_call(
        middle_kernel,
        grid=(steps,),
        in_specs=[
            down(D), down(D), whole((1, D)), whole((QW, D)), whole((D, FF)), whole((FF, D)),
            across(TOPK), across(TOPK), across(TOPK * H),
        ],
        out_specs=[
            down(D), down(D), across(TOPK * H), across(TOPK), across(E),
            pl.BlockSpec(memory_space=pl.ANY), whole((8, 128)), whole((1, D)),
        ],
        out_shape=[
            struct((count, D), BF16),
            struct((count, D)),
            struct((TOPK * H, count), BF16),
            struct((TOPK, count)),
            struct((E, count)),
            struct((flat_rows, 128), BF16),
            struct((8, 128)),
            struct((1, D)),
        ],
        scratch_shapes=[
            pltpu.VMEM((TOPK * H, MB), BF16),
            pltpu.VMEM((QW, MB), BF16),
            pltpu.VMEM((QW, MB), BF16),
            pltpu.VMEM((MB, FF), BF16),
            pltpu.VMEM((MB, FF), BF16),
            pltpu.VMEM((MB, D), BF16),
            pltpu.VMEM((QW, D), F32),
            pltpu.VMEM((D, FF), F32),
            pltpu.VMEM((D, FF), F32),
            pltpu.VMEM((flat_rows - WO_ROW, 128), F32),
            pltpu.VMEM((flat_rows - WO_ROW - 8, 128), BF16),
            pltpu.SemaphoreType.DMA((1,)),
        ],
        compiler_params=params_for(60),
        name="middle",
    )(tokens, grad_out, gain, wo, w1, w2, routes_t, gates, attended)


def head_backward(
    segments, tokens, gain, wall, routes_t, start, queries, datt, lse, delta, kv, kvt, dlogits, dres,
    dgain_two, extra, flat,
):
    count = tokens.shape[0]
    steps = count // TB

    def place(b):
        return (b // NB) * NB + NB - 1 - b % NB

    across = lambda rows: pl.BlockSpec((rows, TB), lambda b: (0, place(b)))
    down = lambda columns: pl.BlockSpec((TB, columns), lambda b: (place(b), 0))
    return pl.pallas_call(
        head_backward_kernel,
        grid=(steps,),
        in_specs=[
            SMEM, down(D), whole((1, D)), whole((ALLW, D)), across(TOPK), across(1),
            across(TOPK * H), across(TOPK * H), across(TOPK), across(TOPK),
            pl.BlockSpec((LEN, 2 * H), lambda b: (b // NB, 0)),
            pl.BlockSpec((2 * H, LEN), lambda b: (0, b // NB)),
            across(E), down(D), whole((1, D)), whole((8, 128)), pl.BlockSpec(memory_space=pl.ANY),
        ],
        out_specs=[down(D), pl.BlockSpec(memory_space=pl.ANY)],
        scratch_shapes=[
            pltpu.VMEM((LEN, H), F32),
            pltpu.VMEM((LEN, H), F32),
            pltpu.VMEM((TOPK * H, TB), BF16),
            pltpu.VMEM((ALLW, TB), BF16),
            pltpu.VMEM((MOST * QB, TOPK * QB), BF16),
            pltpu.VMEM((MOST * QB, TOPK * QB), BF16),
            pltpu.VMEM((ALLW, D), F32),
            pltpu.VMEM((1, D), F32),
            pltpu.VMEM((WO_ROW + 8, 128), F32),
            pltpu.VMEM((WO_ROW + 8, 128), BF16),
            pltpu.SemaphoreType.DMA((1,)),
        ],
        out_shape=[struct((count, D)), struct(flat.shape, BF16)],
        input_output_aliases={16: 1},
        compiler_params=params_for(56),
        name="head_backward",
        cost_estimate=pl.CostEstimate(flops=30_000_000_000, bytes_accessed=24_000_000, transcendentals=0),
    )(
        segments, tokens, gain, wall, routes_t, start, queries, datt, lse, delta, kv, kvt, dlogits, dres,
        dgain_two, extra, flat,
    )


class Mesh3:
    def __init__(self, shards, over):
        shard = lax.axis_index("dp")
        other = lax.axis_index("fsdp")
        self.over = over
        self.many = shards * over
        self.sizes = {"x": 2, "y": shards // 2, "z": over // 2}
        self.here = {"x": lax.rem(other, 2), "y": lax.div(shard, 2), "z": lax.div(other, 2)}
        self.core = lax.rem(shard, 2)
        self.me = shard * over + other
        self.partner = (shard + 1 - 2 * self.core, other)

    def at_z(self, z):
        same = copy.copy(self)
        if z is not None:
            same.here = dict(self.here, z=z)
        return same

    def spots(self):
        x, y, z = (self.sizes[axis] for axis in "xyz")
        return list(itertools.product(range(x), range(y), range(1 - z, z)))

    def round_spots(self):
        return list(itertools.product(*[range(self.sizes[axis]) for axis in "xyz"]))

    def exists(self, z_steps):
        place = self.here["z"] + z_steps
        if isinstance(place, int):
            return 0 <= place < self.sizes["z"]
        return (place >= 0) & (place < self.sizes["z"])

    def device(self, core, spot):
        size = self.sizes["z"]
        x = lax.rem(self.here["x"] + spot[0], self.sizes["x"])
        y = lax.rem(self.here["y"] + spot[1], self.sizes["y"])
        z = self.here["z"] + spot[2]
        z = z % size if isinstance(z, int) else lax.rem(z + size, size)
        return (y * 2 + core, z * 2 + x)

    def number(self, core, spot):
        shard, other = self.device(core, spot)
        return shard * self.over + other

    def greet(self, devices):
        barrier = pltpu.get_barrier_semaphore()
        for device in devices:
            pl.semaphore_signal(barrier, inc=1, device_id=device, device_id_type=MESH)
        pl.semaphore_wait(barrier, len(devices))

    def near(self):
        steps = [at(axis, step) for axis in "xyz" for step in range(1, self.sizes[axis])]
        return [self.device(self.core, step) for step in steps] + [self.partner]

    def column(self):
        steps = [(core, step) for core in range(2) for step in range(self.sizes["z"]) if core or step]
        return [self.device(lax.rem(self.core + core, 2), (0, 0, step)) for core, step in steps]

    def layer(self):
        steps = [(x, y, 0) for x in range(self.sizes["x"]) for y in range(self.sizes["y"]) if x or y]
        return [self.device(self.core, step) for step in steps]


def at(axis, step):
    return tuple(step if one == axis else 0 for one in "xyz")


def last_axis(axes, spot):
    return max([i for i, axis in enumerate(axes) if spot["xyz".index(axis)]], default=-1)


def pieces_of(window, count=2):
    if window < 512:
        return [(0, window)]
    ends = [window // 16 * i // count * 16 for i in range(count)] + [window]
    return [(first, last - first) for first, last in zip(ends, ends[1:])]


def act(condition, action):
    if condition is True:
        action()
    elif condition is not False:
        pl.when(condition)(action)


GATHER_AXES = (("zxy", "yzx"), ("zyx", "xzy"))
REDUCE_PIECES = 3
REDUCE_AXES = ("zxy", "zyx")


def onward(mesh, axes, spot):
    last = last_axis(axes, spot)
    steps = []
    if last >= 0 and axes[last] == "z":
        steps.append(("z", -1 if spot[2] > 0 else 1))
    for axis in axes[last + 1 :]:
        steps += [("z", 1), ("z", -1)] if axis == "z" else [
            (axis, one) for one in range(1, mesh.sizes[axis])
        ]
    return steps


def gather_own_core(mesh, core, land, send_sem, recv_sem, begin):
    window = land.shape[1]
    pieces = pieces_of(window)
    slots = {}
    events = []

    def moved(owner, device, slot, p):
        rows = pl.ds(*pieces[p])
        return pltpu.make_async_remote_copy(
            src_ref=land.at[owner, rows],
            dst_ref=land.at[owner, rows],
            send_sem=send_sem.at[slot, p],
            recv_sem=recv_sem.at[owner, p],
            device_id=device,
            device_id_type=MESH,
        )

    for spot in mesh.spots():
        there = mesh.exists(spot[2])
        if there is False:
            continue
        owner = mesh.number(core, spot)
        turn = 0.5 * abs(spot[2]) + (spot[0] > 0) + (spot[1] > 0) + (0.001 if spot[2] < 0 else 0)
        for p in range(len(pieces)):
            sends = []
            for axis, step in onward(mesh, GATHER_AXES[core][p], spot):
                key = (spot[0], spot[1], spot[2] % mesh.sizes["z"], axis, step)
                away = mesh.exists(step) if axis == "z" else True
                if away is not False:
                    slot = slots.setdefault(key, len(slots))
                    sends.append((mesh.device(core, at(axis, step)), slot, away))
            key = (spot[0], spot[1], spot[2] % mesh.sizes["z"])
            sends.append((mesh.partner, slots.setdefault(key, len(slots)), True))

            def come(owner=owner, spot=spot, p=p, sends=sends):
                if any(spot):
                    moved(owner, mesh.partner, 0, p).wait_recv()
                for device, slot, away in sends:
                    act(away, moved(owner, device, slot, p).start)

            def done(owner=owner, p=p, sends=sends):
                for _, slot, away in sends:
                    act(away, moved(owner, mesh.partner, slot, p).wait_send)

            events.append((turn + 0.01 * p, there, come if begin else done))
    for _, there, action in sorted(events, key=lambda one: one[0]):
        act(there, action)


def gather_blocks(mesh, land, send_sem, recv_sem, begin):
    known = range(mesh.sizes["z"]) if mesh.sizes["z"] <= 4 else [None]
    for core in range(2):
        for z in known:

            @pl.when((mesh.core == core) & (True if z is None else mesh.here["z"] == z))
            def _(core=core, z=z):
                gather_own_core(mesh.at_z(z), core, land, send_sem, recv_sem, begin)


def each_owner(mesh, core, action):
    def one(number, carry):
        shard = 2 * lax.div(number, mesh.over) + core
        action(shard * mesh.over + lax.rem(number, mesh.over))
        return carry

    lax.fori_loop(0, mesh.many // 2, one, 0)


def reduce_blocks(mesh, core, source, mine, outgo, income, send_sem, recv_sem, total_ref):
    pieces = pieces_of(outgo.shape[1], REDUCE_PIECES)
    half = mesh.many // 2
    held = {spot: i for i, spot in enumerate(mesh.round_spots())}

    def across(kind, spot):
        slot = held[spot]
        return pltpu.make_async_remote_copy(
            src_ref=source(mesh.number(kind, spot)),
            dst_ref=income.at[slot],
            send_sem=send_sem.at[slot, 0],
            recv_sem=recv_sem.at[slot, 0],
            device_id=mesh.partner,
            device_id_type=MESH,
        )

    def moved(spot, p, device):
        rows = pl.ds(*pieces[p])
        slot = half + held[spot]
        return pltpu.make_async_remote_copy(
            src_ref=outgo.at[held[spot], rows],
            dst_ref=income.at[slot, rows],
            send_sem=send_sem.at[slot, p],
            recv_sem=recv_sem.at[slot, p],
            device_id=device,
            device_id_type=MESH,
        )

    def far(spot):
        z = {0: 0, 1: 3, 2: 5, 3: 8}.get(spot[2], 2 * spot[2] + 2)
        return z + 2 * (spot[0] > 0) + 2 * (spot[1] > 0)

    for spot in sorted(held, key=far, reverse=True):
        across(1 - core, spot).start()
    axes = REDUCE_AXES[core]
    order = sorted(
        itertools.product(held, range(len(pieces))), key=lambda one: 2 * one[1] / len(pieces) - 2 * far(one[0])
    )
    for spot, p in order:
        if p == 0:
            across(core, spot).wait_recv()
        rows = pl.ds(*pieces[p])
        total = mine(mesh.number(core, spot), *pieces[p]) + income[held[spot], rows].astype(F32)
        last = last_axis(axes, spot)
        for axis in axes[last + 1 :]:
            size = mesh.sizes[axis]
            for step in range(1, size):
                child = tuple(one or other for one, other in zip(spot, at(axis, size - step)))
                moved(child, p, mesh.partner).wait_recv()
                total = total + income[half + held[child], rows].astype(F32)
        if last < 0:
            total_ref[rows, :] = total
        else:
            outgo[held[spot], rows] = total.astype(BF16)
            step = spot["xyz".index(axes[last])]
            moved(spot, p, mesh.device(core, at(axes[last], step))).start()
    for spot, p in order:
        if p == 0:
            across(1 - core, spot).wait_send()
        if any(spot):
            moved(spot, p, mesh.partner).wait_send()


def sum_all(mesh, mine, stats, send_sem, recv_sem):
    column = mesh.sizes["z"] * 2
    layer = mesh.sizes["x"] * mesh.sizes["y"]
    groups = (
        (0, column, mesh.here["z"] * 2 + mesh.core, mesh.column()),
        (column, layer, mesh.here["x"] * mesh.sizes["y"] + mesh.here["y"], mesh.layer()),
    )
    total = mine
    for base, size, here, devices in groups:
        stats[base + here] = total

        def sent(j, device, base=base, here=here):
            return pltpu.make_async_remote_copy(
                src_ref=stats.at[base + here],
                dst_ref=stats.at[base + here],
                send_sem=send_sem.at[base + j],
                recv_sem=recv_sem.at[base + here],
                device_id=device,
                device_id_type=MESH,
            )

        def come(place, base=base):
            return pltpu.make_async_remote_copy(
                src_ref=stats.at[base + place],
                dst_ref=stats.at[base + place],
                send_sem=send_sem.at[base],
                recv_sem=recv_sem.at[base + place],
                device_id=mesh.partner,
                device_id_type=MESH,
            )

        for j, device in enumerate(devices):
            sent(j, device).start()
        for j in range(1, size):
            come(lax.rem(here + j, size)).wait_recv()
        for j, device in enumerate(devices):
            sent(j, device).wait_send()
        total = stats[base]
        for place in range(1, size):
            total = total + stats[base + place]
    return total


def window_rows(shard_size, many):
    units = [(shard_size * d) // UNIT for d in range(many + 1)]
    return 16 * (max(b - a for a, b in zip(units, units[1:])) + 1)


def first_row(shard_size, number):
    if isinstance(number, int):
        return number * shard_size // UNIT * 16
    return pl.multiple_of(lax.div(number * shard_size, UNIT) * 16, 16)


def inner_units(shard_size, many):
    units = [(shard_size * d) // UNIT for d in range(many + 1)]
    return min(b - a for a, b in zip(units, units[1:]))


def lay_inner(shard_size, many, land, flat, owner):
    count = 16 * inner_units(shard_size, many) - 16
    row = pl.multiple_of(first_row(shard_size, owner) + 16, 16)
    flat[pl.ds(row, count), :] = land[owner, pl.ds(16, count), :].astype(F32)


def lay_edges(shard_size, many, land, flat):
    inner = 16 * inner_units(shard_size, many)
    flat[0:16, :] = jnp.zeros((16, 128), F32)

    def lay(number, carry):
        row = first_row(shard_size, number)
        after = first_row(shard_size, number + 1)
        flat[pl.ds(row, 16), :] += land[number, 0:16, :].astype(F32)
        tail = land[number, pl.ds(inner, 16), :].astype(F32)
        flat[pl.ds(pl.multiple_of(row + inner, 16), 16), :] = tail
        last = pl.multiple_of(after - row, 16)
        flat[pl.ds(after, 16), :] = land[number, pl.ds(last, 16), :].astype(F32)
        return carry

    lax.fori_loop(0, many, lay, 0)


def early_matrices(flat, wall_ref, gain_one_ref, gain_two_ref):
    for c in range(D // 128):
        lanes = slice(c * 128, (c + 1) * 128)
        gain_one_ref[:, lanes] = flat[c : c + 1, :]
        gain_two_ref[:, lanes] = flat[4 + c : 5 + c, :]
    for c in range(QW // 128):
        wall_ref[c * 128 : (c + 1) * 128, :] = flat[pl.ds(WQ_ROW + c, D, stride=12), :].T.astype(BF16)
    for first, row in ((KROW, WK_ROW), (VROW, WV_ROW)):
        pair = flat[row : row + 256, :].T.astype(BF16)
        wall_ref[first : first + H, :] = (
            nn(pair[:H], picks(256, 2, 0).astype(BF16)) + nn(pair[H:], picks(256, 2, 1).astype(BF16))
        ).astype(BF16)
    across = jnp.concatenate(
        [flat[pl.ds(WR_ROW + j, 32, stride=3), :] for j in range(3)], axis=1
    ).T.astype(BF16)
    router_t = jnp.zeros((E, D), F32)
    for part in range(16):
        router_t = router_t + nn(across[part * E : (part + 1) * E, :], picks(32, 16, part).astype(BF16))
    wall_ref[RROW:ALLW, :] = jnp.concatenate(
        [router_t, jnp.zeros((ALLW - RROW - E, D), F32)], axis=0
    ).astype(BF16)


def gather_kernel(
    mesh, shard_size, own_ref,
    wall_out, gain_one_ref, gain_two_ref, wo_out, w1_out, w2_out,
    land, flat, wall_ref, wo_ref, w1_ref, w2_ref, send_sem, recv_sem, out_sem,
):
    mesh = mesh()
    many = mesh.many
    mesh.greet(mesh.near())
    land[mesh.me] = own_ref[...].astype(BF16)
    gather_blocks(mesh, land, send_sem, recv_sem, True)
    each_owner(mesh, mesh.core, functools.partial(lay_inner, shard_size, many, land, flat))

    def arrive(owner):
        for p in range(recv_sem.shape[1]):
            rows = pl.ds(*pieces_of(own_ref.shape[0])[p])
            pltpu.make_async_remote_copy(
                src_ref=land.at[owner, rows],
                dst_ref=land.at[owner, rows],
                send_sem=send_sem.at[0, p],
                recv_sem=recv_sem.at[owner, p],
                device_id=mesh.partner,
                device_id_type=MESH,
            ).wait_recv()
        lay_inner(shard_size, many, land, flat, owner)

    each_owner(mesh, 1 - mesh.core, arrive)
    lay_edges(shard_size, many, land, flat)
    copies = []

    def leave(matrix, out):
        one = pltpu.make_async_copy(matrix, out, out_sem.at[len(copies)])
        one.start()
        copies.append(one)

    for c in range(D // 128):
        wo_ref[:, c * 128 : (c + 1) * 128] = flat[pl.ds(WO_ROW + c, QW, stride=4), :].astype(BF16)
    leave(wo_ref, wo_out)
    for c in range(D // 128):
        w2_ref[:, c * 128 : (c + 1) * 128] = flat[pl.ds(W2_ROW + c, FF, stride=4), :].astype(BF16)
    leave(w2_ref, w2_out)
    for c in range(FF // 128):
        w1_ref[:, c * 128 : (c + 1) * 128] = flat[pl.ds(W1_ROW + c, D, stride=16), :].astype(BF16)
    leave(w1_ref, w1_out)
    early_matrices(flat, wall_ref, gain_one_ref, gain_two_ref)
    leave(wall_ref, wall_out)
    gather_blocks(mesh, land, send_sem, recv_sem, False)
    for one in copies:
        one.wait()


def gather_weights(shards, over, shard_size, own):
    window = own.shape[0]
    many = shards * over
    rows = (shard_size * (many - 1)) // UNIT * 16 + window
    vmem = pl.BlockSpec(memory_space=pltpu.VMEM)
    hbm = pl.BlockSpec(memory_space=pl.ANY)
    mesh = functools.partial(Mesh3, shards, over)
    pieces = len(pieces_of(window))
    return pl.pallas_call(
        functools.partial(gather_kernel, mesh, shard_size),
        in_specs=[vmem],
        out_specs=[hbm, vmem, vmem, hbm, hbm, hbm],
        out_shape=[
            struct((ALLW, D), BF16),
            struct((1, D)),
            struct((1, D)),
            struct((QW, D), BF16),
            struct((D, FF), BF16),
            struct((FF, D), BF16),
        ],
        scratch_shapes=[
            pltpu.VMEM((many, window, 128), BF16),
            pltpu.VMEM((rows, 128), F32),
            pltpu.VMEM((ALLW, D), BF16),
            pltpu.VMEM((QW, D), BF16),
            pltpu.VMEM((D, FF), BF16),
            pltpu.VMEM((FF, D), BF16),
            pltpu.SemaphoreType.DMA((5 * many // 2, pieces)),
            pltpu.SemaphoreType.DMA((many, pieces)),
            pltpu.SemaphoreType.DMA((4,)),
        ],
        compiler_params=pltpu.CompilerParams(
            collective_id=0, has_side_effects=True, vmem_limit_bytes=60 * MIB
        ),
        name="gather_weights",
    )(own)


def reduce_kernel(
    mesh, shard_size, flat_ref, count_ref,
    out_ref, total_ref, gain_ref,
    part, outgo, income, whole_scr, stats, part_sem, send_sem, recv_sem, stat_send, stat_recv,
):
    mesh = mesh()
    window = outgo.shape[1]
    span = part.shape[1]

    def source(owner):
        return flat_ref.at[pl.ds(first_row(shard_size, owner), window), :]

    def fetch(y):
        first = first_row(shard_size, (2 * y + mesh.core) * mesh.over)
        return pltpu.make_async_copy(flat_ref.at[pl.ds(first, span), :], part.at[y], part_sem.at[y])

    def mine(owner, first, rows):
        shard = lax.div(owner, mesh.over)
        row = first_row(shard_size, owner) - first_row(shard_size, shard * mesh.over) + first
        return part[lax.div(shard, 2), pl.ds(pl.multiple_of(row, 16), rows), :].astype(F32)

    for y in range(mesh.sizes["y"]):
        fetch(y).start()
    mesh.greet(mesh.column() + mesh.layer())
    for y in range(mesh.sizes["y"]):
        fetch(y).wait()
    buffers = (source, mine, outgo, income, send_sem, recv_sem, whole_scr)
    for core in range(2):
        pl.when(mesh.core == core)(functools.partial(reduce_blocks, mesh, core, *buffers))

    begin = mesh.me * shard_size - lax.div(mesh.me * shard_size, UNIT) * UNIT
    rows = out_ref.shape[0]
    row, lane = lax.div(begin, 128), lax.rem(begin, 128)
    back = lax.rem(128 - lane, 128)
    first = pltpu.roll(whole_scr[pl.ds(row, rows), :], back, 1)
    second = pltpu.roll(whole_scr[pl.ds(row + 1, rows), :], back, 1)
    at_lane = lax.broadcasted_iota(jnp.int32, (rows, 128), 1)
    place = lax.broadcasted_iota(jnp.int32, (rows, 128), 0) * 128 + at_lane
    total = jnp.where(at_lane < 128 - lane, first, second)
    out_ref[...] = total
    inside = jnp.where(place < shard_size, total, 0.0)
    squares = jnp.sum(jnp.sum(inside * inside, axis=0, keepdims=True), axis=1, keepdims=True)
    lane = lax.broadcasted_iota(jnp.int32, (8, 128), 1)
    row = jnp.where(lane == E, squares, count_ref[...])
    gains = jnp.where(mesh.me == 0, total[0:8, :], 0.0)
    summed = sum_all(mesh, jnp.concatenate([row, gains], axis=0), stats, stat_send, stat_recv)
    total_ref[...] = summed[0:1, :]
    for c in range(D // 128):
        lanes = slice(c * 128, (c + 1) * 128)
        gain_ref[0:1, lanes] = summed[8 + c : 9 + c, :]
        gain_ref[1:2, lanes] = summed[12 + c : 13 + c, :]


def reduce_grads(shards, over, shard_size, window, flat, counts):
    vmem = pl.BlockSpec(memory_space=pltpu.VMEM)
    many = shards * over
    mesh = functools.partial(Mesh3, shards, over)
    pieces = len(pieces_of(window, REDUCE_PIECES))
    steps = over + shards
    units = [(shard_size * d) // UNIT for d in range(many)]
    span = 16 * max(units[d + over - 1] - units[d] for d in range(0, many, over)) + window
    return pl.pallas_call(
        functools.partial(reduce_kernel, mesh, shard_size),
        in_specs=[pl.BlockSpec(memory_space=pl.ANY), vmem],
        out_specs=[vmem] * 3,
        out_shape=[struct((-(-shard_size // 128), 128)), struct((1, 128)), struct((2, D))],
        scratch_shapes=[
            pltpu.VMEM((shards // 2, span, 128), BF16),
            pltpu.VMEM((many // 2, window, 128), BF16),
            pltpu.VMEM((many, window, 128), BF16),
            pltpu.VMEM((window + 16, 128), F32),
            pltpu.VMEM((steps, 16, 128), F32),
            pltpu.SemaphoreType.DMA((shards // 2,)),
            pltpu.SemaphoreType.DMA((many, pieces)),
            pltpu.SemaphoreType.DMA((many, pieces)),
            pltpu.SemaphoreType.DMA((steps,)),
            pltpu.SemaphoreType.DMA((steps,)),
        ],
        compiler_params=pltpu.CompilerParams(
            collective_id=1, has_side_effects=True, vmem_limit_bytes=56 * MIB
        ),
        name="reduce_grads",
    )(flat, counts)


def local_step(flat_rows, tokens, grad_out, routes, segments, weights):
    wall, gain_one, gain_two, wo, w1, w2 = weights
    queries, attended, gates, lse, kv, kvt, start, routes_t, counts = head_forward(
        tokens, routes.T, segments, wall, gain_one
    )
    output, dres, datt, delta, dlogits, flat, extra, dgain_two = middle(
        flat_rows, tokens, grad_out, gain_two, wo, w1, w2, routes_t, gates, attended
    )
    input_grad, flat = head_backward(
        segments, tokens, gain_one, wall, routes_t, start, queries, datt, lse, delta, kv, kvt, dlogits, dres,
        dgain_two, extra, flat,
    )
    return output, input_grad, flat, counts


def per_device(
    shards, over, tokens, grad_out, routes, segments, params, first_moment, second_moment, ema_weights
):
    shard_size = params.shape[0]
    window = window_rows(shard_size, shards * over)
    flat_rows = (shard_size * (shards * over - 1)) // UNIT * 16 + window + 16
    me = lax.axis_index("dp") * over + lax.axis_index("fsdp")
    begin = lax.rem(me * shard_size, UNIT)
    own = lax.dynamic_slice(
        jnp.pad(params, (UNIT, window * 128 - shard_size)), (UNIT - begin,), (window * 128,)
    ).reshape(window, 128)
    wall, gain_one, gain_two, wo, w1, w2 = gather_weights(shards, over, shard_size, own)
    output, input_grad, flat, counts = local_step(
        flat_rows, tokens, grad_out, routes, segments, (wall, gain_one, gain_two, wo, w1, w2)
    )
    reduced, sums, gain_grads = reduce_grads(shards, over, shard_size, window, flat, counts)
    grad_shard = reduced.reshape(-1)[:shard_size]
    total_tokens = tokens.shape[0] * shards * over
    expert_load = sums[0, :E] * (E / (total_tokens * TOPK))
    grad_norm = jnp.sqrt(sums[0, E])
    clipped = grad_shard * (CLIP_LIMIT / jnp.maximum(grad_norm, CLIP_LIMIT))
    new_first = BETA_FIRST * first_moment + (1.0 - BETA_FIRST) * clipped
    new_second = BETA_SECOND * second_moment + (1.0 - BETA_SECOND) * clipped * clipped
    first_hat = new_first / (1.0 - BETA_FIRST**STEP)
    second_hat = new_second / (1.0 - BETA_SECOND**STEP)
    new_params = params * (1.0 - LEARN_RATE * DECAY_RATE) - LEARN_RATE * first_hat / (
        jnp.sqrt(second_hat) + ADAM_EPS
    )
    new_ema = EMA_KEEP * ema_weights + (1.0 - EMA_KEEP) * new_params
    return (
        output,
        input_grad,
        expert_load,
        grad_norm.reshape(1),
        new_params,
        new_first,
        new_second,
        new_ema,
        gain_grads,
    )


def solution(mesh):
    row = P(("dp", "fsdp"), None)
    flat = P(("dp", "fsdp"))
    return jax.shard_map(
        functools.partial(per_device, mesh.shape["dp"], mesh.shape["fsdp"]),
        mesh=mesh,
        in_specs=(row, row, row, row, flat, flat, flat, flat),
        out_specs=(row, row, P(), P(), flat, flat, flat, flat, P()),
        check_vma=False,
    )
```

```python
import copy
import functools
import itertools

import jax
import jax.numpy as jnp
from jax import lax
from jax.experimental import pallas as pl
from jax.experimental.pallas import tpu as pltpu
from jax.sharding import PartitionSpec as P

D = 512
E = 24
TOPK = 8
H = 64
FF = 2048
STEP = 10

NORM_EPS = 1e-06
CLIP_LIMIT = 1.0
BETA_FIRST = 0.9
BETA_SECOND = 0.95
LEARN_RATE = 0.1
DECAY_RATE = 0.1
ADAM_EPS = 1e-08
EMA_KEEP = 0.9
NEG_LARGE = -1e30

QW = E * H
KROW = QW
VROW = QW + H
RROW = QW + 2 * H
ALLW = 1696
LEN = 1024
TB = 512
NB = LEN // TB
QB = 128
SIDE = 4
MOST = 512 // QB + 1
SORT_STEPS = (
    (0, 1), (2, 3), (4, 5), (6, 7), (0, 2), (1, 3), (4, 6), (5, 7), (1, 2), (5, 6),
    (0, 4), (1, 5), (2, 6), (3, 7), (2, 4), (3, 5), (1, 2), (3, 4), (5, 6),
)
FC = 256
MB = 512
MIB = 1 << 20

WR_ROW = 8
WK_ROW = 104
WV_ROW = 360
WQ_ROW = 616
WO_ROW = 6760
W1_ROW = 12904
W2_ROW = 21096
ALL_ROWS = 29288
UNIT = 16 * 128
MESH = pl.DeviceIdType.MESH

F32 = jnp.float32
BF16 = jnp.bfloat16


def nn(a, b):
    return lax.dot_general(a, b, (((1,), (0,)), ((), ())), preferred_element_type=F32)


def nt(a, b):
    return lax.dot_general(a, b, (((1,), (1,)), ((), ())), preferred_element_type=F32)


def tn(a, b):
    return lax.dot_general(a, b, (((0,), (0,)), ((), ())), preferred_element_type=F32)


def rms_scale(values):
    return lax.rsqrt(jnp.mean(values * values, axis=-1, keepdims=True) + NORM_EPS)


def slot_of(routes, k, rows):
    return jnp.broadcast_to(routes[k : k + 1, :], (rows, routes.shape[1]))


def expert_rows(routes, k):
    return jnp.broadcast_to(routes.astype(jnp.int16)[k : k + 1, :], (16, routes.shape[1]))


def pick_heads(routes, source_ref, k):
    tokens = routes.shape[1]
    route = expert_rows(routes, k)
    taken = source_ref[k * H : (k + 1) * H, :].reshape(H // 16, 16, tokens)
    for e in range(k + 1, k + E - TOPK + 1):
        piece = source_ref[e * H : (e + 1) * H, :].reshape(H // 16, 16, tokens)
        taken = jnp.where((route == jnp.int16(e))[None], piece, taken)
    return taken.reshape(H, tokens)


def place_heads(routes, source_ref, target_ref):
    tokens = routes.shape[1]
    rows = [expert_rows(routes, k) for k in range(TOPK)]
    for e in range(E):
        total = jnp.zeros((H // 16, 16, tokens), BF16)
        for k in range(max(0, e - (E - TOPK)), min(TOPK - 1, e) + 1):
            piece = source_ref[k * H : (k + 1) * H, :].reshape(H // 16, 16, tokens)
            total = jnp.where((rows[k] == jnp.int16(e))[None], piece, total)
        target_ref[e * H : (e + 1) * H, :] = total.reshape(H, tokens)


def sorted_rows(rows):
    rows = list(rows)
    for one, two in SORT_STEPS:
        rows[one], rows[two] = jnp.minimum(rows[one], rows[two]), jnp.maximum(rows[one], rows[two])
    return rows


def key_mask(first_key, first_query, rows, start_row):
    keys = lax.broadcasted_iota(jnp.int32, (rows, QB), 0) + first_key
    queries = lax.broadcasted_iota(jnp.int32, (rows, QB), 1) + first_query
    mask = (keys <= queries) & (keys >= start_row)
    return jnp.concatenate([mask] * SIDE, axis=1)


def group_of(ref, k, lanes):
    return jnp.concatenate([ref[i * H : (i + 1) * H, lanes] for i in range(k, k + SIDE)], axis=1)


def row_group(ref, k, lanes):
    return jnp.concatenate([ref[i : i + 1, lanes] for i in range(k, k + SIDE)], axis=1)


def by_span(attend, row, place, segment_ref):
    def one(j, carry):
        block = place * (TB // QB) + j
        first = block * QB
        span = jnp.int32(1)
        for back in range(MOST - 1):
            last = first - back * QB - 1
            same = segment_ref[row, jnp.maximum(last, 0)] == segment_ref[row, first]
            span = span + jnp.where((last >= 0) & same, 1, 0)
        for blocks in range(1, MOST + 1):

            @pl.when(span == blocks)
            def _(blocks=blocks):
                attend(pl.ds(pl.multiple_of(j * QB, QB), QB), block, blocks)

        return carry

    lax.fori_loop(0, TB // QB, one, 0)


def head_forward_kernel(
    steps, segment_smem, x_ref, route_ref, segment_ref, wall_ref, gain_ref,
    q_ref, att_ref, gate_ref, lse_ref, kv_ref, kvt_ref, start_ref, sorted_ref, count_ref,
    all_scr, low_scr, k_scr, vt_scr, count_scr,
):
    step = pl.program_id(0)
    place = lax.rem(step, NB)
    here = pl.multiple_of(place * TB, TB)

    @pl.when(step == 0)
    def _():
        count_scr[...] = jnp.zeros_like(count_scr)

    row = segment_ref[pl.ds(lax.div(step, NB), 1), :]
    segments = segment_ref[pl.ds(lax.div(step, NB), 1), pl.ds(here, TB)]
    start = jnp.zeros((1, TB), jnp.int32)
    for number in range(1, 4):
        below = jnp.sum((row < number).astype(jnp.int32), axis=1, keepdims=True)
        start = jnp.where(segments == number, below, start)
    start_ref[...] = start
    x = x_ref[...].astype(F32)
    normed = (x * rms_scale(x) * gain_ref[...]).astype(BF16)
    all_scr[...] = nt(wall_ref[...], normed)
    kt = all_scr[KROW : KROW + H, :]
    vt = all_scr[VROW : VROW + H, :]
    logits = all_scr[RROW : RROW + E, :]
    kvt = jnp.concatenate([kt, vt], axis=0)
    kv = kvt.T.astype(BF16)
    kv_ref[...] = kv
    kvt_ref[...] = kvt.astype(BF16)
    k_scr[pl.ds(here, TB), :] = kv[:, :H]
    vt_scr[:, pl.ds(here, TB)] = vt.astype(BF16)
    routes = jnp.concatenate(sorted_rows(route_ref[k : k + 1, :] for k in range(TOPK)), axis=0)
    sorted_ref[...] = routes
    experts = lax.broadcasted_iota(jnp.int32, (E, TB), 0)
    chosen = []
    counts = count_scr[...]
    for k in range(TOPK):
        named = slot_of(routes, k, E) == experts
        chosen.append(jnp.sum(jnp.where(named, logits, 0.0), axis=0, keepdims=True))
        counts = counts + named.astype(F32)
    count_scr[...] = counts
    chosen = jnp.concatenate(chosen, axis=0)
    raised = jnp.exp(chosen - jnp.max(chosen, axis=0, keepdims=True))
    gate_ref[...] = raised / jnp.sum(raised, axis=0, keepdims=True)
    low_scr[...] = all_scr[0:QW, :].astype(BF16)
    for k in range(TOPK):
        q_ref[k * H : (k + 1) * H, :] = pick_heads(routes, low_scr, k) * jnp.asarray(H ** (-0.5), BF16)

    def attend(lanes, block, blocks):
        rows = blocks * QB
        first_key = pl.multiple_of((block - (blocks - 1)) * QB, QB)
        mask = key_mask(first_key, block * QB, rows, start_ref[:, lanes])
        keys = k_scr[pl.ds(first_key, rows), :]
        values = vt_scr[:, pl.ds(first_key, rows)]
        groups = [nn(keys, group_of(q_ref, 0, lanes))]
        for k in range(0, TOPK, SIDE):
            if k + SIDE < TOPK:
                groups.append(nn(keys, group_of(q_ref, k + SIDE, lanes)))
            scores = jnp.where(mask, groups[k // SIDE], NEG_LARGE)
            top = jnp.max(scores, axis=0, keepdims=True)
            raised = jnp.exp(scores - top)
            total = jnp.sum(raised, axis=0, keepdims=True)
            out = nn(values, (raised * (1.0 / total)).astype(BF16))
            lse = top + jnp.log(total)
            for side in range(SIDE):
                one = slice(side * QB, (side + 1) * QB)
                att_ref[(k + side) * H : (k + side + 1) * H, lanes] = out[:, one]
                lse_ref[k + side : k + side + 1, lanes] = lse[:, one]

    by_span(attend, lax.div(step, NB), place, segment_smem)

    @pl.when(step == steps - 1)
    def _():
        held = jnp.sum(count_scr[...], axis=1, keepdims=True)
        lane = lax.broadcasted_iota(jnp.int32, (E, 128), 1)
        row = lax.broadcasted_iota(jnp.int32, (E, 128), 0)
        count_ref[...] = jnp.sum(jnp.where(lane == row, held, 0.0), axis=0, keepdims=True)


def picks(rows, stride, first):
    at = lax.broadcasted_iota(jnp.int32, (rows, D), 1)
    row = lax.broadcasted_iota(jnp.int32, (rows, D), 0)
    return (at == row * stride + first).astype(F32)


def exact(product, a, b):
    return lax.dot_general(
        a, b, (product, ((), ())), precision=lax.Precision.HIGHEST, preferred_element_type=F32
    )


def gelu_parts(v):
    cdf = 0.5 + 0.5 * lax.erf(v * 0.7071067811865476)
    return cdf, jnp.exp(v * v * -0.5) * 0.3989422804014327


def middle_kernel(
    x_ref, dy_ref, gain_ref, wo_ref, w1_ref, w2_ref, route_ref, gate_ref, att_ref,
    out_ref, dres_ref, datt_ref, delta_ref, dlogit_ref, flat_ref, extra_ref, dgain_ref,
    slot_scr, head_scr, mix_scr, hidden_scr, dpre_scr, w1t_scr, w2t_scr, dwo_ref, dw1_ref, dw2t_ref, rows_scr, low_scr, row_sem,
):
    step = pl.program_id(0)

    @pl.when(step == 0)
    def _():
        dwo_ref[...] = jnp.zeros_like(dwo_ref)
        dw1_ref[...] = jnp.zeros_like(dw1_ref)
        dw2t_ref[...] = jnp.zeros_like(dw2t_ref)
        for first in range(0, FF, 512):
            part = slice(first, first + 512)
            w1t_scr[part, :] = w1_ref[:, part].T
            w2t_scr[:, part] = w2_ref[part, :].T
        dgain_ref[...] = jnp.zeros_like(dgain_ref)

    routes = route_ref[...]
    tokens = routes.shape[1]
    gates = gate_ref[...]
    for k in range(TOPK):
        rows = slice(k * H, (k + 1) * H)
        slot_scr[rows, :] = (gates[k : k + 1, :] * att_ref[rows, :]).astype(BF16)
    place_heads(routes, slot_scr, mix_scr)
    x = x_ref[...].astype(F32)
    dy = dy_ref[...]
    mixed = mix_scr[...]
    residual = x + tn(mixed, wo_ref[...])
    scale = rms_scale(residual)
    gain = gain_ref[...]
    second = (residual * scale * gain).astype(BF16)
    second_t = second.T
    dy_t = dy.T
    pre = [nn(second, w1_ref[:, 0:FC])]
    back = [nn(dy, w2t_scr[:, 0:FC])]
    for i in range(FF // FC):
        here = slice(i * FC, (i + 1) * FC)
        if i + 1 < FF // FC:
            after = slice((i + 1) * FC, (i + 2) * FC)
            pre.append(nn(second, w1_ref[:, after]))
            back.append(nn(dy, w2t_scr[:, after]))
        cdf, density = gelu_parts(pre[i])
        hidden_scr[:, here] = (pre[i] * cdf).astype(BF16)
        dpre_scr[:, here] = (back[i] * (cdf + pre[i] * density)).astype(BF16)
    dsecond = nn(dpre_scr[...], w1t_scr[...])
    out_ref[...] = (residual + nn(hidden_scr[...], w2_ref[...])).astype(BF16)
    dw1_ref[...] += nn(second_t, dpre_scr[...])
    dw2t_ref[...] += nn(dy_t, hidden_scr[...])
    dgain_ref[...] += jnp.sum(dsecond * residual * scale, axis=0, keepdims=True)
    weighted = gain * dsecond
    dres = (
        dy.astype(F32)
        + scale * weighted
        - residual * (scale * scale * scale) * jnp.mean(weighted * residual, axis=-1, keepdims=True)
    )
    dres_ref[...] = dres
    branch = dres.astype(BF16)
    dwo_ref[...] += nn(mixed, branch)
    head_scr[...] = nt(wo_ref[...], branch).astype(BF16)
    dgates = []
    for k in range(TOPK):
        rows = slice(k * H, (k + 1) * H)
        dslot = pick_heads(routes, head_scr, k).astype(F32)
        attended = att_ref[rows, :]
        dgates.append(jnp.sum(dslot * attended, axis=0, keepdims=True))
        datt = (gates[k : k + 1, :] * dslot).astype(BF16)
        datt_ref[rows, :] = datt
        delta_ref[k : k + 1, :] = jnp.sum(datt.astype(F32) * attended, axis=0, keepdims=True)
    dgate = jnp.concatenate(dgates, axis=0)
    dchosen = gates * (dgate - jnp.sum(gates * dgate, axis=0, keepdims=True))
    experts = lax.broadcasted_iota(jnp.int32, (E, tokens), 0)
    dlogits = jnp.zeros((E, tokens), F32)
    for k in range(TOPK):
        dlogits = jnp.where(
            slot_of(routes, k, E) == experts,
            jnp.broadcast_to(dchosen[k : k + 1, :], (E, tokens)),
            dlogits,
        )
    dlogit_ref[...] = dlogits

    @pl.when(step == pl.num_programs(0) - 1)
    def _():
        last = low_scr.shape[0]
        ends = (0, (W1_ROW - WO_ROW - 8) // 16 * 16, (W2_ROW - WO_ROW - 8) // 16 * 16, last)

        def out(number):
            first, count = ends[number], ends[number + 1] - ends[number]
            return pltpu.make_async_copy(
                low_scr.at[pl.ds(first, count), :],
                flat_ref.at[pl.ds(WO_ROW + 8 + first, count), :],
                row_sem.at[number],
            )

        def leave(number):
            first, count = ends[number], ends[number + 1] - ends[number]
            low_scr[pl.ds(first, count), :] = rows_scr[pl.ds(first + 8, count), :].astype(BF16)
            out(number).start()

        for c in range(D // 128):
            rows_scr[pl.ds(c, QW, stride=4), :] = dwo_ref[:, c * 128 : (c + 1) * 128]
        extra_ref[...] = rows_scr[0:8, :]
        leave(0)
        for c in range(FF // 128):
            rows_scr[pl.ds(W1_ROW - WO_ROW + c, D, stride=16), :] = dw1_ref[:, c * 128 : (c + 1) * 128]
        leave(1)
        for c in range(D // 128):
            rows_scr[pl.ds(W2_ROW - WO_ROW + c, FF, stride=4), :] = dw2t_ref[c * 128 : (c + 1) * 128, :].T
        leave(2)
        for number in range(3):
            out(number).wait()


def head_backward_kernel(
    segment_smem, x_ref, gain_ref, wall_ref, route_ref, start_ref, q_ref, datt_ref,
    lse_ref, delta_ref, kv_ref, kvt_ref, dlogit_ref, dres_ref, dgain_two_ref, extra_ref, flat_in,
    dx_ref, flat_ref,
    dk_scr, dv_scr, dq_scr, dall_scr, prob_scr, dscore_scr, dwall_ref, dgain_ref, rows_scr, low_scr, row_sem,
):
    step = pl.program_id(0)
    place = NB - 1 - lax.rem(step, NB)
    here = pl.multiple_of(place * TB, TB)

    @pl.when(step == 0)
    def _():
        dwall_ref[...] = jnp.zeros_like(dwall_ref)
        dgain_ref[...] = jnp.zeros_like(dgain_ref)

    @pl.when(lax.rem(step, NB) == 0)
    def _():
        dk_scr[...] = jnp.zeros_like(dk_scr)
        dv_scr[...] = jnp.zeros_like(dv_scr)

    def attend(lanes, block, blocks):
        rows = blocks * QB
        first_key = pl.multiple_of((block - (blocks - 1)) * QB, QB)
        mask = key_mask(first_key, block * QB, rows, start_ref[:, lanes])
        keys = kv_ref[pl.ds(first_key, rows), :H]
        values = kv_ref[pl.ds(first_key, rows), H:]
        keys_t = kvt_ref[:H, pl.ds(first_key, rows)]
        queries = [group_of(q_ref, k, lanes) for k in range(0, TOPK, SIDE)]
        datts = [group_of(datt_ref, k, lanes) for k in range(0, TOPK, SIDE)]
        scores = [nn(keys, queries[0])]
        dprobs = [nn(values, datts[0])]
        for i in range(TOPK // SIDE):
            if i + 1 < TOPK // SIDE:
                scores.append(nn(keys, queries[i + 1]))
                dprobs.append(nn(values, datts[i + 1]))
            k = i * SIDE
            wide = slice(k * QB, (k + SIDE) * QB)
            probs = jnp.exp(jnp.where(mask, scores[i], NEG_LARGE) - row_group(lse_ref, k, lanes))
            dscore = (probs * (dprobs[i] - row_group(delta_ref, k, lanes))).astype(BF16)
            prob_scr[0:rows, wide] = probs.astype(BF16)
            dscore_scr[0:rows, wide] = dscore
            dq = (nn(keys_t, dscore) * (H ** (-0.5))).astype(BF16)
            for side in range(SIDE):
                dq_scr[(k + side) * H : (k + side + 1) * H, lanes] = dq[:, side * QB : (side + 1) * QB]
        dv_scr[pl.ds(first_key, rows), :] += nt(prob_scr[0:rows, :], jnp.concatenate(datts, axis=1))
        dk_scr[pl.ds(first_key, rows), :] += nt(dscore_scr[0:rows, :], jnp.concatenate(queries, axis=1))

    by_span(attend, lax.div(step, NB), place, segment_smem)
    place_heads(route_ref[...], dq_scr, dall_scr)
    dkv = jnp.concatenate([dk_scr[pl.ds(here, TB), :], dv_scr[pl.ds(here, TB), :]], axis=1)
    dall_scr[KROW : KROW + 2 * H, :] = dkv.T.astype(BF16)
    dall_scr[RROW : RROW + 32, :] = jnp.concatenate(
        [dlogit_ref[...], jnp.zeros((32 - E, TB), F32)], axis=0
    ).astype(BF16)
    x = x_ref[...].astype(F32)
    scale = rms_scale(x)
    gain = gain_ref[...]
    normed = (x * scale * gain).astype(BF16)
    dall = dall_scr[...]
    dwall_ref[...] += nn(dall, normed)
    dnormed = tn(dall, wall_ref[...])
    dgain_ref[...] += jnp.sum(dnormed * x * scale, axis=0, keepdims=True)
    weighted = gain * dnormed
    dx_ref[...] = (
        dres_ref[...]
        + scale * weighted
        - x * (scale * scale * scale) * jnp.mean(weighted * x, axis=-1, keepdims=True)
    )

    @pl.when(step == pl.num_programs(0) - 1)
    def _():
        for c in range(D // 128):
            lanes = slice(c * 128, (c + 1) * 128)
            rows_scr[c : c + 1, :] = dgain_ref[:, lanes]
            rows_scr[4 + c : 5 + c, :] = dgain_two_ref[:, lanes]
        router_t = dwall_ref[RROW : RROW + E, :]
        across = jnp.concatenate(
            [exact(((1,), (1,)), router_t, picks(32, 16, b)) for b in range(16)], axis=0
        ).T
        for j in range(3):
            rows_scr[pl.ds(WR_ROW + j, 32, stride=3), :] = across[:, j * 128 : (j + 1) * 128]
        for first, row in ((KROW, WK_ROW), (VROW, WV_ROW)):
            part = dwall_ref[first : first + H, :]
            rows_scr[row : row + 256, :] = jnp.concatenate(
                [exact(((1,), (1,)), picks(256, 2, b), part) for b in range(2)], axis=1
            )
        for c in range(QW // 128):
            rows_scr[pl.ds(WQ_ROW + c, D, stride=12), :] = dwall_ref[c * 128 : (c + 1) * 128, :].T
        rows_scr[WO_ROW : WO_ROW + 8, :] = extra_ref[...]
        low_scr[...] = rows_scr[...].astype(BF16)
        copy = pltpu.make_async_copy(low_scr, flat_ref.at[pl.ds(0, WO_ROW + 8), :], row_sem.at[0])
        copy.start()
        copy.wait()


def whole(shape):
    return pl.BlockSpec(shape, lambda *_: (0,) * len(shape), pipeline_mode=pl.Buffered(1))


def kept(shape):
    return pl.BlockSpec(shape, lambda *_: (0,) * len(shape))


SMEM = pl.BlockSpec(memory_space=pltpu.SMEM)


def struct(shape, kind=F32):
    return jax.ShapeDtypeStruct(shape, kind)


def params_for(mib):
    return pltpu.CompilerParams(vmem_limit_bytes=mib * MIB)


def head_forward(tokens, routes_t, segments, wall, gain):
    count = tokens.shape[0]
    steps = count // TB
    across = lambda rows: pl.BlockSpec((rows, TB), lambda b: (0, b))
    down = lambda columns: pl.BlockSpec((TB, columns), lambda b: (b, 0))
    return pl.pallas_call(
        functools.partial(head_forward_kernel, steps),
        grid=(steps,),
        in_specs=[SMEM, down(D), across(TOPK), whole(segments.shape), whole((ALLW, D)), whole((1, D))],
        out_specs=[
            across(TOPK * H), across(TOPK * H), across(TOPK), across(TOPK), down(2 * H), across(2 * H),
            across(1), across(TOPK), whole((1, 128)),
        ],
        scratch_shapes=[
            pltpu.VMEM((ALLW, TB), F32),
            pltpu.VMEM((QW, TB), BF16),
            pltpu.VMEM((LEN, H), BF16),
            pltpu.VMEM((H, LEN), BF16),
            pltpu.VMEM((E, TB), F32),
        ],
        out_shape=[
            struct((TOPK * H, count), BF16),
            struct((TOPK * H, count)),
            struct((TOPK, count)),
            struct((TOPK, count)),
            struct((count, 2 * H), BF16),
            struct((2 * H, count), BF16),
            struct((1, count), jnp.int32),
            struct((TOPK, count), jnp.int32),
            struct((1, 128)),
        ],
        compiler_params=params_for(56),
        name="head_forward",
        cost_estimate=pl.CostEstimate(flops=10_000_000_000, bytes_accessed=16_000_000, transcendentals=0),
    )(segments, tokens, routes_t, segments, wall, gain)


def middle(flat_rows, tokens, grad_out, gain, wo, w1, w2, routes_t, gates, attended):
    count = tokens.shape[0]
    steps = count // MB
    across = lambda rows: pl.BlockSpec((rows, MB), lambda b: (0, b))
    down = lambda columns: pl.BlockSpec((MB, columns), lambda b: (b, 0))
    return pl.pallas_call(
        middle_kernel,
        grid=(steps,),
        in_specs=[
            down(D), down(D), whole((1, D)), whole((QW, D)), whole((D, FF)), whole((FF, D)),
            across(TOPK), across(TOPK), across(TOPK * H),
        ],
        out_specs=[
            down(D), down(D), across(TOPK * H), across(TOPK), across(E),
            pl.BlockSpec(memory_space=pl.ANY), whole((8, 128)), whole((1, D)),
        ],
        out_shape=[
            struct((count, D), BF16),
            struct((count, D)),
            struct((TOPK * H, count), BF16),
            struct((TOPK, count)),
            struct((E, count)),
            struct((flat_rows, 128), BF16),
            struct((8, 128)),
            struct((1, D)),
        ],
        scratch_shapes=[
            pltpu.VMEM((TOPK * H, MB), BF16),
            pltpu.VMEM((QW, MB), BF16),
            pltpu.VMEM((QW, MB), BF16),
            pltpu.VMEM((MB, FF), BF16),
            pltpu.VMEM((MB, FF), BF16),
            pltpu.VMEM((FF, D), BF16),
            pltpu.VMEM((D, FF), BF16),
            pltpu.VMEM((QW, D), F32),
            pltpu.VMEM((D, FF), F32),
            pltpu.VMEM((D, FF), F32),
            pltpu.VMEM((flat_rows - WO_ROW, 128), F32),
            pltpu.VMEM((flat_rows - WO_ROW - 8, 128), BF16),
            pltpu.SemaphoreType.DMA((3,)),
        ],
        compiler_params=params_for(60),
        name="middle",
    )(tokens, grad_out, gain, wo, w1, w2, routes_t, gates, attended)


def head_backward(
    segments, tokens, gain, wall, routes_t, start, queries, datt, lse, delta, kv, kvt, dlogits, dres,
    dgain_two, extra, flat,
):
    count = tokens.shape[0]
    steps = count // TB

    def place(b):
        return (b // NB) * NB + NB - 1 - b % NB

    across = lambda rows: pl.BlockSpec((rows, TB), lambda b: (0, place(b)))
    down = lambda columns: pl.BlockSpec((TB, columns), lambda b: (place(b), 0))
    return pl.pallas_call(
        head_backward_kernel,
        grid=(steps,),
        in_specs=[
            SMEM, down(D), whole((1, D)), whole((ALLW, D)), across(TOPK), across(1),
            across(TOPK * H), across(TOPK * H), across(TOPK), across(TOPK),
            pl.BlockSpec((LEN, 2 * H), lambda b: (b // NB, 0)),
            pl.BlockSpec((2 * H, LEN), lambda b: (0, b // NB)),
            across(E), down(D), whole((1, D)), whole((8, 128)), pl.BlockSpec(memory_space=pl.ANY),
        ],
        out_specs=[down(D), pl.BlockSpec(memory_space=pl.ANY)],
        scratch_shapes=[
            pltpu.VMEM((LEN, H), F32),
            pltpu.VMEM((LEN, H), F32),
            pltpu.VMEM((TOPK * H, TB), BF16),
            pltpu.VMEM((ALLW, TB), BF16),
            pltpu.VMEM((MOST * QB, TOPK * QB), BF16),
            pltpu.VMEM((MOST * QB, TOPK * QB), BF16),
            pltpu.VMEM((ALLW, D), F32),
            pltpu.VMEM((1, D), F32),
            pltpu.VMEM((WO_ROW + 8, 128), F32),
            pltpu.VMEM((WO_ROW + 8, 128), BF16),
            pltpu.SemaphoreType.DMA((1,)),
        ],
        out_shape=[struct((count, D)), struct(flat.shape, BF16)],
        input_output_aliases={16: 1},
        compiler_params=params_for(56),
        name="head_backward",
        cost_estimate=pl.CostEstimate(flops=30_000_000_000, bytes_accessed=24_000_000, transcendentals=0),
    )(
        segments, tokens, gain, wall, routes_t, start, queries, datt, lse, delta, kv, kvt, dlogits, dres,
        dgain_two, extra, flat,
    )


class Mesh3:
    def __init__(self, shards, over):
        shard = lax.axis_index("dp")
        other = lax.axis_index("fsdp")
        self.over = over
        self.many = shards * over
        self.sizes = {"x": 2, "y": shards // 2, "z": over // 2}
        self.here = {"x": lax.rem(other, 2), "y": lax.div(shard, 2), "z": lax.div(other, 2)}
        self.core = lax.rem(shard, 2)
        self.me = shard * over + other
        self.partner = (shard + 1 - 2 * self.core, other)

    def at_z(self, z):
        same = copy.copy(self)
        if z is not None:
            same.here = dict(self.here, z=z)
        return same

    def spots(self):
        x, y, z = (self.sizes[axis] for axis in "xyz")
        return list(itertools.product(range(x), range(y), range(1 - z, z)))

    def round_spots(self):
        return list(itertools.product(*[range(self.sizes[axis]) for axis in "xyz"]))

    def exists(self, z_steps):
        place = self.here["z"] + z_steps
        if isinstance(place, int):
            return 0 <= place < self.sizes["z"]
        return (place >= 0) & (place < self.sizes["z"])

    def device(self, core, spot):
        size = self.sizes["z"]
        x = lax.rem(self.here["x"] + spot[0], self.sizes["x"])
        y = lax.rem(self.here["y"] + spot[1], self.sizes["y"])
        z = self.here["z"] + spot[2]
        z = z % size if isinstance(z, int) else lax.rem(z + size, size)
        return (y * 2 + core, z * 2 + x)

    def number(self, core, spot):
        shard, other = self.device(core, spot)
        return shard * self.over + other

    def greet(self, devices):
        barrier = pltpu.get_barrier_semaphore()
        for device in devices:
            pl.semaphore_signal(barrier, inc=1, device_id=device, device_id_type=MESH)
        pl.semaphore_wait(barrier, len(devices))

    def near(self):
        steps = [at(axis, step) for axis in "xyz" for step in range(1, self.sizes[axis])]
        return [self.device(self.core, step) for step in steps] + [self.partner]

    def column(self):
        steps = [(core, step) for core in range(2) for step in range(self.sizes["z"]) if core or step]
        return [self.device(lax.rem(self.core + core, 2), (0, 0, step)) for core, step in steps]

    def layer(self):
        steps = [(x, y, 0) for x in range(self.sizes["x"]) for y in range(self.sizes["y"]) if x or y]
        return [self.device(self.core, step) for step in steps]


def at(axis, step):
    return tuple(step if one == axis else 0 for one in "xyz")


def last_axis(axes, spot):
    return max([i for i, axis in enumerate(axes) if spot["xyz".index(axis)]], default=-1)


def pieces_of(window, count=2):
    if window < 512:
        return [(0, window)]
    ends = [window // 16 * i // count * 16 for i in range(count)] + [window]
    return [(first, last - first) for first, last in zip(ends, ends[1:])]


def act(condition, action):
    if condition is True:
        action()
    elif condition is not False:
        pl.when(condition)(action)


GATHER_AXES = (("zxy", "yzx"), ("zyx", "xzy"))
REDUCE_PIECES = 3
REDUCE_AXES = ("zxy", "zyx")


def onward(mesh, axes, spot):
    last = last_axis(axes, spot)
    steps = []
    if last >= 0 and axes[last] == "z":
        steps.append(("z", -1 if spot[2] > 0 else 1))
    for axis in axes[last + 1 :]:
        steps += [("z", 1), ("z", -1)] if axis == "z" else [
            (axis, one) for one in range(1, mesh.sizes[axis])
        ]
    return steps


def gather_own_core(mesh, core, land, send_sem, recv_sem, begin):
    window = land.shape[1]
    pieces = pieces_of(window)
    slots = {}
    events = []

    def moved(owner, device, slot, p):
        rows = pl.ds(*pieces[p])
        return pltpu.make_async_remote_copy(
            src_ref=land.at[owner, rows],
            dst_ref=land.at[owner, rows],
            send_sem=send_sem.at[slot, p],
            recv_sem=recv_sem.at[owner, p],
            device_id=device,
            device_id_type=MESH,
        )

    for spot in mesh.spots():
        there = mesh.exists(spot[2])
        if there is False:
            continue
        owner = mesh.number(core, spot)
        turn = 0.5 * abs(spot[2]) + (spot[0] > 0) + (spot[1] > 0) + (0.001 if spot[2] < 0 else 0)
        for p in range(len(pieces)):
            sends = []
            for axis, step in onward(mesh, GATHER_AXES[core][p], spot):
                key = (spot[0], spot[1], spot[2] % mesh.sizes["z"], axis, step)
                away = mesh.exists(step) if axis == "z" else True
                if away is not False:
                    slot = slots.setdefault(key, len(slots))
                    sends.append((mesh.device(core, at(axis, step)), slot, away))
            key = (spot[0], spot[1], spot[2] % mesh.sizes["z"])
            sends.append((mesh.partner, slots.setdefault(key, len(slots)), True))

            def come(owner=owner, spot=spot, p=p, sends=sends):
                if any(spot):
                    moved(owner, mesh.partner, 0, p).wait_recv()
                for device, slot, away in sends:
                    act(away, moved(owner, device, slot, p).start)

            def done(owner=owner, p=p, sends=sends):
                for _, slot, away in sends:
                    act(away, moved(owner, mesh.partner, slot, p).wait_send)

            events.append((turn + 0.01 * p, there, come if begin else done))
    for _, there, action in sorted(events, key=lambda one: one[0]):
        act(there, action)


def gather_blocks(mesh, land, send_sem, recv_sem, begin):
    known = range(mesh.sizes["z"]) if mesh.sizes["z"] <= 4 else [None]
    for core in range(2):
        for z in known:

            @pl.when((mesh.core == core) & (True if z is None else mesh.here["z"] == z))
            def _(core=core, z=z):
                gather_own_core(mesh.at_z(z), core, land, send_sem, recv_sem, begin)


def each_owner(mesh, core, action):
    def one(number, carry):
        shard = 2 * lax.div(number, mesh.over) + core
        action(shard * mesh.over + lax.rem(number, mesh.over))
        return carry

    lax.fori_loop(0, mesh.many // 2, one, 0)


def reduce_blocks(mesh, core, source, mine, outgo, income, send_sem, recv_sem, total_ref):
    pieces = pieces_of(outgo.shape[1], REDUCE_PIECES)
    half = mesh.many // 2
    held = {spot: i for i, spot in enumerate(mesh.round_spots())}

    def across(kind, spot):
        slot = held[spot]
        return pltpu.make_async_remote_copy(
            src_ref=source(mesh.number(kind, spot)),
            dst_ref=income.at[slot],
            send_sem=send_sem.at[slot, 0],
            recv_sem=recv_sem.at[slot, 0],
            device_id=mesh.partner,
            device_id_type=MESH,
        )

    def moved(spot, p, device):
        rows = pl.ds(*pieces[p])
        slot = half + held[spot]
        return pltpu.make_async_remote_copy(
            src_ref=outgo.at[held[spot], rows],
            dst_ref=income.at[slot, rows],
            send_sem=send_sem.at[slot, p],
            recv_sem=recv_sem.at[slot, p],
            device_id=device,
            device_id_type=MESH,
        )

    def far(spot):
        z = {0: 0, 1: 3, 2: 5, 3: 8}.get(spot[2], 2 * spot[2] + 2)
        return z + 2 * (spot[0] > 0) + 2 * (spot[1] > 0)

    for spot in sorted(held, key=far, reverse=True):
        across(1 - core, spot).start()
    axes = REDUCE_AXES[core]
    order = sorted(
        itertools.product(held, range(len(pieces))), key=lambda one: 2 * one[1] / len(pieces) - 2 * far(one[0])
    )
    for spot, p in order:
        if p == 0:
            across(core, spot).wait_recv()
        rows = pl.ds(*pieces[p])
        total = mine(mesh.number(core, spot), *pieces[p]) + income[held[spot], rows].astype(F32)
        last = last_axis(axes, spot)
        for axis in axes[last + 1 :]:
            size = mesh.sizes[axis]
            for step in range(1, size):
                child = tuple(one or other for one, other in zip(spot, at(axis, size - step)))
                moved(child, p, mesh.partner).wait_recv()
                total = total + income[half + held[child], rows].astype(F32)
        if last < 0:
            total_ref[rows, :] = total
        else:
            outgo[held[spot], rows] = total.astype(BF16)
            step = spot["xyz".index(axes[last])]
            moved(spot, p, mesh.device(core, at(axes[last], step))).start()
    for spot, p in order:
        if p == 0:
            across(1 - core, spot).wait_send()
        if any(spot):
            moved(spot, p, mesh.partner).wait_send()


def sum_all(mesh, mine, stats, send_sem, recv_sem):
    column = mesh.sizes["z"] * 2
    layer = mesh.sizes["x"] * mesh.sizes["y"]
    groups = (
        (0, column, mesh.here["z"] * 2 + mesh.core, mesh.column()),
        (column, layer, mesh.here["x"] * mesh.sizes["y"] + mesh.here["y"], mesh.layer()),
    )
    total = mine
    for base, size, here, devices in groups:
        stats[base + here] = total

        def sent(j, device, base=base, here=here):
            return pltpu.make_async_remote_copy(
                src_ref=stats.at[base + here],
                dst_ref=stats.at[base + here],
                send_sem=send_sem.at[base + j],
                recv_sem=recv_sem.at[base + here],
                device_id=device,
                device_id_type=MESH,
            )

        def come(place, base=base):
            return pltpu.make_async_remote_copy(
                src_ref=stats.at[base + place],
                dst_ref=stats.at[base + place],
                send_sem=send_sem.at[base],
                recv_sem=recv_sem.at[base + place],
                device_id=mesh.partner,
                device_id_type=MESH,
            )

        for j, device in enumerate(devices):
            sent(j, device).start()
        for j in range(1, size):
            come(lax.rem(here + j, size)).wait_recv()
        for j, device in enumerate(devices):
            sent(j, device).wait_send()
        total = stats[base]
        for place in range(1, size):
            total = total + stats[base + place]
    return total


def window_rows(shard_size, many):
    units = [(shard_size * d) // UNIT for d in range(many + 1)]
    return 16 * (max(b - a for a, b in zip(units, units[1:])) + 1)


def first_row(shard_size, number):
    if isinstance(number, int):
        return number * shard_size // UNIT * 16
    return pl.multiple_of(lax.div(number * shard_size, UNIT) * 16, 16)


def inner_units(shard_size, many):
    units = [(shard_size * d) // UNIT for d in range(many + 1)]
    return min(b - a for a, b in zip(units, units[1:]))


def lay_inner(shard_size, many, land, flat, owner):
    count = 16 * inner_units(shard_size, many) - 16
    row = pl.multiple_of(first_row(shard_size, owner) + 16, 16)
    flat[pl.ds(row, count), :] = land[owner, pl.ds(16, count), :].astype(F32)


def lay_edges(shard_size, many, land, flat):
    inner = 16 * inner_units(shard_size, many)
    flat[0:16, :] = jnp.zeros((16, 128), F32)

    def lay(number, carry):
        row = first_row(shard_size, number)
        after = first_row(shard_size, number + 1)
        flat[pl.ds(row, 16), :] += land[number, 0:16, :].astype(F32)
        tail = land[number, pl.ds(inner, 16), :].astype(F32)
        flat[pl.ds(pl.multiple_of(row + inner, 16), 16), :] = tail
        last = pl.multiple_of(after - row, 16)
        flat[pl.ds(after, 16), :] = land[number, pl.ds(last, 16), :].astype(F32)
        return carry

    lax.fori_loop(0, many, lay, 0)


def early_matrices(flat, wall_ref, gain_one_ref, gain_two_ref):
    for c in range(D // 128):
        lanes = slice(c * 128, (c + 1) * 128)
        gain_one_ref[:, lanes] = flat[c : c + 1, :]
        gain_two_ref[:, lanes] = flat[4 + c : 5 + c, :]
    for c in range(QW // 128):
        wall_ref[c * 128 : (c + 1) * 128, :] = flat[pl.ds(WQ_ROW + c, D, stride=12), :].T.astype(BF16)
    for first, row in ((KROW, WK_ROW), (VROW, WV_ROW)):
        pair = flat[row : row + 256, :].T.astype(BF16)
        wall_ref[first : first + H, :] = (
            nn(pair[:H], picks(256, 2, 0).astype(BF16)) + nn(pair[H:], picks(256, 2, 1).astype(BF16))
        ).astype(BF16)
    across = jnp.concatenate(
        [flat[pl.ds(WR_ROW + j, 32, stride=3), :] for j in range(3)], axis=1
    ).T.astype(BF16)
    router_t = jnp.zeros((E, D), F32)
    for part in range(16):
        router_t = router_t + nn(across[part * E : (part + 1) * E, :], picks(32, 16, part).astype(BF16))
    wall_ref[RROW:ALLW, :] = jnp.concatenate(
        [router_t, jnp.zeros((ALLW - RROW - E, D), F32)], axis=0
    ).astype(BF16)


def gather_kernel(
    mesh, shard_size, own_ref,
    wall_out, gain_one_ref, gain_two_ref, wo_out, w1_out, w2_out,
    land, flat, wall_ref, wo_ref, w1_ref, w2_ref, send_sem, recv_sem, out_sem,
):
    mesh = mesh()
    many = mesh.many
    mesh.greet(mesh.near())
    land[mesh.me] = own_ref[...].astype(BF16)
    gather_blocks(mesh, land, send_sem, recv_sem, True)
    each_owner(mesh, mesh.core, functools.partial(lay_inner, shard_size, many, land, flat))

    def arrive(owner):
        for p in range(recv_sem.shape[1]):
            rows = pl.ds(*pieces_of(own_ref.shape[0])[p])
            pltpu.make_async_remote_copy(
                src_ref=land.at[owner, rows],
                dst_ref=land.at[owner, rows],
                send_sem=send_sem.at[0, p],
                recv_sem=recv_sem.at[owner, p],
                device_id=mesh.partner,
                device_id_type=MESH,
            ).wait_recv()
        lay_inner(shard_size, many, land, flat, owner)

    each_owner(mesh, 1 - mesh.core, arrive)
    lay_edges(shard_size, many, land, flat)
    copies = []

    def leave(matrix, out):
        one = pltpu.make_async_copy(matrix, out, out_sem.at[len(copies)])
        one.start()
        copies.append(one)

    for c in range(D // 128):
        wo_ref[:, c * 128 : (c + 1) * 128] = flat[pl.ds(WO_ROW + c, QW, stride=4), :].astype(BF16)
    leave(wo_ref, wo_out)
    for c in range(D // 128):
        w2_ref[:, c * 128 : (c + 1) * 128] = flat[pl.ds(W2_ROW + c, FF, stride=4), :].astype(BF16)
    leave(w2_ref, w2_out)
    for c in range(FF // 128):
        w1_ref[:, c * 128 : (c + 1) * 128] = flat[pl.ds(W1_ROW + c, D, stride=16), :].astype(BF16)
    leave(w1_ref, w1_out)
    early_matrices(flat, wall_ref, gain_one_ref, gain_two_ref)
    leave(wall_ref, wall_out)
    gather_blocks(mesh, land, send_sem, recv_sem, False)
    for one in copies:
        one.wait()


def gather_weights(shards, over, shard_size, own):
    window = own.shape[0]
    many = shards * over
    rows = (shard_size * (many - 1)) // UNIT * 16 + window
    vmem = pl.BlockSpec(memory_space=pltpu.VMEM)
    hbm = pl.BlockSpec(memory_space=pl.ANY)
    mesh = functools.partial(Mesh3, shards, over)
    pieces = len(pieces_of(window))
    return pl.pallas_call(
        functools.partial(gather_kernel, mesh, shard_size),
        in_specs=[vmem],
        out_specs=[hbm, vmem, vmem, hbm, hbm, hbm],
        out_shape=[
            struct((ALLW, D), BF16),
            struct((1, D)),
            struct((1, D)),
            struct((QW, D), BF16),
            struct((D, FF), BF16),
            struct((FF, D), BF16),
        ],
        scratch_shapes=[
            pltpu.VMEM((many, window, 128), BF16),
            pltpu.VMEM((rows, 128), F32),
            pltpu.VMEM((ALLW, D), BF16),
            pltpu.VMEM((QW, D), BF16),
            pltpu.VMEM((D, FF), BF16),
            pltpu.VMEM((FF, D), BF16),
            pltpu.SemaphoreType.DMA((5 * many // 2, pieces)),
            pltpu.SemaphoreType.DMA((many, pieces)),
            pltpu.SemaphoreType.DMA((4,)),
        ],
        compiler_params=pltpu.CompilerParams(
            collective_id=0, has_side_effects=True, vmem_limit_bytes=60 * MIB
        ),
        name="gather_weights",
    )(own)


def reduce_kernel(
    mesh, shard_size, flat_ref, count_ref,
    out_ref, total_ref, gain_ref,
    part, outgo, income, whole_scr, stats, part_sem, send_sem, recv_sem, stat_send, stat_recv,
):
    mesh = mesh()
    window = outgo.shape[1]
    span = part.shape[1]

    def source(owner):
        return flat_ref.at[pl.ds(first_row(shard_size, owner), window), :]

    def fetch(y):
        first = first_row(shard_size, (2 * y + mesh.core) * mesh.over)
        return pltpu.make_async_copy(flat_ref.at[pl.ds(first, span), :], part.at[y], part_sem.at[y])

    def mine(owner, first, rows):
        shard = lax.div(owner, mesh.over)
        row = first_row(shard_size, owner) - first_row(shard_size, shard * mesh.over) + first
        return part[lax.div(shard, 2), pl.ds(pl.multiple_of(row, 16), rows), :].astype(F32)

    for y in range(mesh.sizes["y"]):
        fetch(y).start()
    mesh.greet(mesh.column() + mesh.layer())
    for y in range(mesh.sizes["y"]):
        fetch(y).wait()
    buffers = (source, mine, outgo, income, send_sem, recv_sem, whole_scr)
    for core in range(2):
        pl.when(mesh.core == core)(functools.partial(reduce_blocks, mesh, core, *buffers))

    begin = mesh.me * shard_size - lax.div(mesh.me * shard_size, UNIT) * UNIT
    rows = out_ref.shape[0]
    row, lane = lax.div(begin, 128), lax.rem(begin, 128)
    back = lax.rem(128 - lane, 128)
    first = pltpu.roll(whole_scr[pl.ds(row, rows), :], back, 1)
    second = pltpu.roll(whole_scr[pl.ds(row + 1, rows), :], back, 1)
    at_lane = lax.broadcasted_iota(jnp.int32, (rows, 128), 1)
    place = lax.broadcasted_iota(jnp.int32, (rows, 128), 0) * 128 + at_lane
    total = jnp.where(at_lane < 128 - lane, first, second)
    out_ref[...] = total
    inside = jnp.where(place < shard_size, total, 0.0)
    squares = jnp.sum(jnp.sum(inside * inside, axis=0, keepdims=True), axis=1, keepdims=True)
    lane = lax.broadcasted_iota(jnp.int32, (8, 128), 1)
    row = jnp.where(lane == E, squares, count_ref[...])
    gains = jnp.where(mesh.me == 0, total[0:8, :], 0.0)
    summed = sum_all(mesh, jnp.concatenate([row, gains], axis=0), stats, stat_send, stat_recv)
    total_ref[...] = summed[0:1, :]
    for c in range(D // 128):
        lanes = slice(c * 128, (c + 1) * 128)
        gain_ref[0:1, lanes] = summed[8 + c : 9 + c, :]
        gain_ref[1:2, lanes] = summed[12 + c : 13 + c, :]


def reduce_grads(shards, over, shard_size, window, flat, counts):
    vmem = pl.BlockSpec(memory_space=pltpu.VMEM)
    many = shards * over
    mesh = functools.partial(Mesh3, shards, over)
    pieces = len(pieces_of(window, REDUCE_PIECES))
    steps = over + shards
    units = [(shard_size * d) // UNIT for d in range(many)]
    span = 16 * max(units[d + over - 1] - units[d] for d in range(0, many, over)) + window
    return pl.pallas_call(
        functools.partial(reduce_kernel, mesh, shard_size),
        in_specs=[pl.BlockSpec(memory_space=pl.ANY), vmem],
        out_specs=[vmem] * 3,
        out_shape=[struct((-(-shard_size // 128), 128)), struct((1, 128)), struct((2, D))],
        scratch_shapes=[
            pltpu.VMEM((shards // 2, span, 128), BF16),
            pltpu.VMEM((many // 2, window, 128), BF16),
            pltpu.VMEM((many, window, 128), BF16),
            pltpu.VMEM((window + 16, 128), F32),
            pltpu.VMEM((steps, 16, 128), F32),
            pltpu.SemaphoreType.DMA((shards // 2,)),
            pltpu.SemaphoreType.DMA((many, pieces)),
            pltpu.SemaphoreType.DMA((many, pieces)),
            pltpu.SemaphoreType.DMA((steps,)),
            pltpu.SemaphoreType.DMA((steps,)),
        ],
        compiler_params=pltpu.CompilerParams(
            collective_id=1, has_side_effects=True, vmem_limit_bytes=56 * MIB
        ),
        name="reduce_grads",
    )(flat, counts)


def local_step(flat_rows, tokens, grad_out, routes, segments, weights):
    wall, gain_one, gain_two, wo, w1, w2 = weights
    queries, attended, gates, lse, kv, kvt, start, routes_t, counts = head_forward(
        tokens, routes.T, segments, wall, gain_one
    )
    output, dres, datt, delta, dlogits, flat, extra, dgain_two = middle(
        flat_rows, tokens, grad_out, gain_two, wo, w1, w2, routes_t, gates, attended
    )
    input_grad, flat = head_backward(
        segments, tokens, gain_one, wall, routes_t, start, queries, datt, lse, delta, kv, kvt, dlogits, dres,
        dgain_two, extra, flat,
    )
    return output, input_grad, flat, counts


def per_device(
    shards, over, tokens, grad_out, routes, segments, params, first_moment, second_moment, ema_weights
):
    shard_size = params.shape[0]
    window = window_rows(shard_size, shards * over)
    flat_rows = (shard_size * (shards * over - 1)) // UNIT * 16 + window + 16
    me = lax.axis_index("dp") * over + lax.axis_index("fsdp")
    begin = lax.rem(me * shard_size, UNIT)
    own = lax.dynamic_slice(
        jnp.pad(params, (UNIT, window * 128 - shard_size)), (UNIT - begin,), (window * 128,)
    ).reshape(window, 128)
    wall, gain_one, gain_two, wo, w1, w2 = gather_weights(shards, over, shard_size, own)
    output, input_grad, flat, counts = local_step(
        flat_rows, tokens, grad_out, routes, segments, (wall, gain_one, gain_two, wo, w1, w2)
    )
    reduced, sums, gain_grads = reduce_grads(shards, over, shard_size, window, flat, counts)
    grad_shard = reduced.reshape(-1)[:shard_size]
    total_tokens = tokens.shape[0] * shards * over
    expert_load = sums[0, :E] * (E / (total_tokens * TOPK))
    grad_norm = jnp.sqrt(sums[0, E])
    clipped = grad_shard * (CLIP_LIMIT / jnp.maximum(grad_norm, CLIP_LIMIT))
    new_first = BETA_FIRST * first_moment + (1.0 - BETA_FIRST) * clipped
    new_second = BETA_SECOND * second_moment + (1.0 - BETA_SECOND) * clipped * clipped
    first_hat = new_first / (1.0 - BETA_FIRST**STEP)
    second_hat = new_second / (1.0 - BETA_SECOND**STEP)
    new_params = params * (1.0 - LEARN_RATE * DECAY_RATE) - LEARN_RATE * first_hat / (
        jnp.sqrt(second_hat) + ADAM_EPS
    )
    new_ema = EMA_KEEP * ema_weights + (1.0 - EMA_KEEP) * new_params
    return (
        output,
        input_grad,
        expert_load,
        grad_norm.reshape(1),
        new_params,
        new_first,
        new_second,
        new_ema,
        gain_grads,
    )


def solution(mesh):
    row = P(("dp", "fsdp"), None)
    flat = P(("dp", "fsdp"))
    return jax.shard_map(
        functools.partial(per_device, mesh.shape["dp"], mesh.shape["fsdp"]),
        mesh=mesh,
        in_specs=(row, row, row, row, flat, flat, flat, flat),
        out_specs=(row, row, P(), P(), flat, flat, flat, flat, P()),
        check_vma=False,
    )
```

```python
import copy
import functools
import itertools

import jax
import jax.numpy as jnp
from jax import lax
from jax.experimental import pallas as pl
from jax.experimental.pallas import tpu as pltpu
from jax.sharding import PartitionSpec as P

D = 512
E = 24
TOPK = 8
H = 64
FF = 2048
STEP = 10

NORM_EPS = 1e-06
CLIP_LIMIT = 1.0
BETA_FIRST = 0.9
BETA_SECOND = 0.95
LEARN_RATE = 0.1
DECAY_RATE = 0.1
ADAM_EPS = 1e-08
EMA_KEEP = 0.9
NEG_LARGE = -1e30

QW = E * H
KROW = QW
VROW = QW + H
RROW = QW + 2 * H
ALLW = 1696
LEN = 1024
TB = 512
NB = LEN // TB
QB = 128
SIDE = 4
MOST = 512 // QB + 1
SORT_STEPS = (
    (0, 1), (2, 3), (4, 5), (6, 7), (0, 2), (1, 3), (4, 6), (5, 7), (1, 2), (5, 6),
    (0, 4), (1, 5), (2, 6), (3, 7), (2, 4), (3, 5), (1, 2), (3, 4), (5, 6),
)
FC = 256
MB = 512
MIB = 1 << 20

WR_ROW = 8
WK_ROW = 104
WV_ROW = 360
WQ_ROW = 616
WO_ROW = 6760
W1_ROW = 12904
W2_ROW = 21096
ALL_ROWS = 29288
UNIT = 16 * 128
MESH = pl.DeviceIdType.MESH

F32 = jnp.float32
BF16 = jnp.bfloat16


def nn(a, b):
    return lax.dot_general(a, b, (((1,), (0,)), ((), ())), preferred_element_type=F32)


def nt(a, b):
    return lax.dot_general(a, b, (((1,), (1,)), ((), ())), preferred_element_type=F32)


def tn(a, b):
    return lax.dot_general(a, b, (((0,), (0,)), ((), ())), preferred_element_type=F32)


def rms_scale(values):
    return lax.rsqrt(jnp.mean(values * values, axis=-1, keepdims=True) + NORM_EPS)


def slot_of(routes, k, rows):
    return jnp.broadcast_to(routes[k : k + 1, :], (rows, routes.shape[1]))


def expert_rows(routes, k):
    return jnp.broadcast_to(routes.astype(jnp.int16)[k : k + 1, :], (16, routes.shape[1]))


def pick_heads(routes, source_ref, k):
    tokens = routes.shape[1]
    route = expert_rows(routes, k)
    taken = source_ref[k * H : (k + 1) * H, :].reshape(H // 16, 16, tokens)
    for e in range(k + 1, k + E - TOPK + 1):
        piece = source_ref[e * H : (e + 1) * H, :].reshape(H // 16, 16, tokens)
        taken = jnp.where((route == jnp.int16(e))[None], piece, taken)
    return taken.reshape(H, tokens)


def place_heads(routes, source_ref, target_ref):
    tokens = routes.shape[1]
    rows = [expert_rows(routes, k) for k in range(TOPK)]
    for e in range(E):
        total = jnp.zeros((H // 16, 16, tokens), BF16)
        for k in range(max(0, e - (E - TOPK)), min(TOPK - 1, e) + 1):
            piece = source_ref[k * H : (k + 1) * H, :].reshape(H // 16, 16, tokens)
            total = jnp.where((rows[k] == jnp.int16(e))[None], piece, total)
        target_ref[e * H : (e + 1) * H, :] = total.reshape(H, tokens)


def sorted_rows(rows):
    rows = list(rows)
    for one, two in SORT_STEPS:
        rows[one], rows[two] = jnp.minimum(rows[one], rows[two]), jnp.maximum(rows[one], rows[two])
    return rows


def key_mask(first_key, first_query, rows, start_row):
    keys = lax.broadcasted_iota(jnp.int32, (rows, QB), 0) + first_key
    queries = lax.broadcasted_iota(jnp.int32, (rows, QB), 1) + first_query
    mask = (keys <= queries) & (keys >= start_row)
    return jnp.concatenate([mask] * SIDE, axis=1)


def group_of(ref, k, lanes):
    return jnp.concatenate([ref[i * H : (i + 1) * H, lanes] for i in range(k, k + SIDE)], axis=1)


def row_group(ref, k, lanes):
    return jnp.concatenate([ref[i : i + 1, lanes] for i in range(k, k + SIDE)], axis=1)


def by_span(attend, row, place, segment_ref):
    def one(j, carry):
        block = place * (TB // QB) + j
        first = block * QB
        span = jnp.int32(1)
        for back in range(MOST - 1):
            last = first - back * QB - 1
            same = segment_ref[row, jnp.maximum(last, 0)] == segment_ref[row, first]
            span = span + jnp.where((last >= 0) & same, 1, 0)
        for blocks in range(1, MOST + 1):

            @pl.when(span == blocks)
            def _(blocks=blocks):
                attend(pl.ds(pl.multiple_of(j * QB, QB), QB), block, blocks)

        return carry

    lax.fori_loop(0, TB // QB, one, 0)


def head_forward_kernel(
    steps, segment_smem, x_ref, route_ref, segment_ref, wall_ref, gain_ref,
    q_ref, att_ref, gate_ref, lse_ref, kv_ref, kvt_ref, start_ref, sorted_ref, count_ref,
    all_scr, low_scr, k_scr, vt_scr, count_scr,
):
    step = pl.program_id(0)
    place = lax.rem(step, NB)
    here = pl.multiple_of(place * TB, TB)

    @pl.when(step == 0)
    def _():
        count_scr[...] = jnp.zeros_like(count_scr)

    row = segment_ref[pl.ds(lax.div(step, NB), 1), :]
    segments = segment_ref[pl.ds(lax.div(step, NB), 1), pl.ds(here, TB)]
    start = jnp.zeros((1, TB), jnp.int32)
    for number in range(1, 4):
        below = jnp.sum((row < number).astype(jnp.int32), axis=1, keepdims=True)
        start = jnp.where(segments == number, below, start)
    start_ref[...] = start
    x = x_ref[...].astype(F32)
    normed = (x * rms_scale(x) * gain_ref[...]).astype(BF16)
    all_scr[...] = nt(wall_ref[...], normed)
    kt = all_scr[KROW : KROW + H, :]
    vt = all_scr[VROW : VROW + H, :]
    logits = all_scr[RROW : RROW + E, :]
    kvt = jnp.concatenate([kt, vt], axis=0)
    kv = kvt.T.astype(BF16)
    kv_ref[...] = kv
    kvt_ref[...] = kvt.astype(BF16)
    k_scr[pl.ds(here, TB), :] = kv[:, :H]
    vt_scr[:, pl.ds(here, TB)] = vt.astype(BF16)
    routes = jnp.concatenate(sorted_rows(route_ref[k : k + 1, :] for k in range(TOPK)), axis=0)
    sorted_ref[...] = routes
    experts = lax.broadcasted_iota(jnp.int32, (E, TB), 0)
    chosen = []
    counts = count_scr[...]
    for k in range(TOPK):
        named = slot_of(routes, k, E) == experts
        chosen.append(jnp.sum(jnp.where(named, logits, 0.0), axis=0, keepdims=True))
        counts = counts + named.astype(F32)
    count_scr[...] = counts
    chosen = jnp.concatenate(chosen, axis=0)
    raised = jnp.exp(chosen - jnp.max(chosen, axis=0, keepdims=True))
    gate_ref[...] = raised / jnp.sum(raised, axis=0, keepdims=True)
    low_scr[...] = all_scr[0:QW, :].astype(BF16)
    for k in range(TOPK):
        q_ref[k * H : (k + 1) * H, :] = pick_heads(routes, low_scr, k) * jnp.asarray(H ** (-0.5), BF16)

    def attend(lanes, block, blocks):
        rows = blocks * QB
        first_key = pl.multiple_of((block - (blocks - 1)) * QB, QB)
        mask = key_mask(first_key, block * QB, rows, start_ref[:, lanes])
        keys = k_scr[pl.ds(first_key, rows), :]
        values = vt_scr[:, pl.ds(first_key, rows)]
        groups = [nn(keys, group_of(q_ref, 0, lanes))]
        for k in range(0, TOPK, SIDE):
            if k + SIDE < TOPK:
                groups.append(nn(keys, group_of(q_ref, k + SIDE, lanes)))
            scores = jnp.where(mask, groups[k // SIDE], NEG_LARGE)
            top = jnp.max(scores, axis=0, keepdims=True)
            raised = jnp.exp(scores - top)
            total = jnp.sum(raised, axis=0, keepdims=True)
            out = nn(values, (raised * (1.0 / total)).astype(BF16))
            lse = top + jnp.log(total)
            for side in range(SIDE):
                one = slice(side * QB, (side + 1) * QB)
                att_ref[(k + side) * H : (k + side + 1) * H, lanes] = out[:, one]
                lse_ref[k + side : k + side + 1, lanes] = lse[:, one]

    by_span(attend, lax.div(step, NB), place, segment_smem)

    @pl.when(step == steps - 1)
    def _():
        held = jnp.sum(count_scr[...], axis=1, keepdims=True)
        lane = lax.broadcasted_iota(jnp.int32, (E, 128), 1)
        row = lax.broadcasted_iota(jnp.int32, (E, 128), 0)
        count_ref[...] = jnp.sum(jnp.where(lane == row, held, 0.0), axis=0, keepdims=True)


def picks(rows, stride, first):
    at = lax.broadcasted_iota(jnp.int32, (rows, D), 1)
    row = lax.broadcasted_iota(jnp.int32, (rows, D), 0)
    return (at == row * stride + first).astype(F32)


def exact(product, a, b):
    return lax.dot_general(
        a, b, (product, ((), ())), precision=lax.Precision.HIGHEST, preferred_element_type=F32
    )


def gelu_parts(v):
    cdf = 0.5 + 0.5 * lax.erf(v * 0.7071067811865476)
    return cdf, jnp.exp(v * v * -0.5) * 0.3989422804014327


def middle_kernel(
    x_ref, dy_ref, gain_ref, wo_ref, w1_ref, w2_ref, route_ref, gate_ref, att_ref,
    out_ref, dres_ref, datt_ref, delta_ref, dlogit_ref, flat_ref, extra_ref, dgain_ref,
    slot_scr, head_scr, mix_scr, hidden_scr, dpre_scr, dwo_ref, dw1_ref, dw2t_ref, rows_scr, low_scr, row_sem,
):
    step = pl.program_id(0)

    @pl.when(step == 0)
    def _():
        dwo_ref[...] = jnp.zeros_like(dwo_ref)
        dw1_ref[...] = jnp.zeros_like(dw1_ref)
        dw2t_ref[...] = jnp.zeros_like(dw2t_ref)
        dgain_ref[...] = jnp.zeros_like(dgain_ref)

    routes = route_ref[...]
    tokens = routes.shape[1]
    gates = gate_ref[...]
    for k in range(TOPK):
        rows = slice(k * H, (k + 1) * H)
        slot_scr[rows, :] = (gates[k : k + 1, :] * att_ref[rows, :]).astype(BF16)
    place_heads(routes, slot_scr, mix_scr)
    x = x_ref[...].astype(F32)
    dy = dy_ref[...]
    mixed = mix_scr[...]
    residual = x + tn(mixed, wo_ref[...])
    scale = rms_scale(residual)
    gain = gain_ref[...]
    second = (residual * scale * gain).astype(BF16)
    second_t = second.T
    dy_t = dy.T
    pre = [nn(second, w1_ref[:, 0:FC])]
    back = [nt(dy, w2_ref[0:FC, :])]
    for i in range(FF // FC):
        here = slice(i * FC, (i + 1) * FC)
        if i + 1 < FF // FC:
            after = slice((i + 1) * FC, (i + 2) * FC)
            pre.append(nn(second, w1_ref[:, after]))
            back.append(nt(dy, w2_ref[after, :]))
        cdf, density = gelu_parts(pre[i])
        hidden_scr[:, here] = (pre[i] * cdf).astype(BF16)
        dpre_scr[:, here] = (back[i] * (cdf + pre[i] * density)).astype(BF16)
    dsecond = nt(dpre_scr[...], w1_ref[...])
    out_ref[...] = (residual + nn(hidden_scr[...], w2_ref[...])).astype(BF16)
    dw1_ref[...] += nn(second_t, dpre_scr[...])
    dw2t_ref[...] += nn(dy_t, hidden_scr[...])
    dgain_ref[...] += jnp.sum(dsecond * residual * scale, axis=0, keepdims=True)
    weighted = gain * dsecond
    dres = (
        dy.astype(F32)
        + scale * weighted
        - residual * (scale * scale * scale) * jnp.mean(weighted * residual, axis=-1, keepdims=True)
    )
    dres_ref[...] = dres
    branch = dres.astype(BF16)
    dwo_ref[...] += nn(mixed, branch)
    head_scr[...] = nt(wo_ref[...], branch).astype(BF16)
    dgates = []
    for k in range(TOPK):
        rows = slice(k * H, (k + 1) * H)
        dslot = pick_heads(routes, head_scr, k).astype(F32)
        attended = att_ref[rows, :]
        dgates.append(jnp.sum(dslot * attended, axis=0, keepdims=True))
        datt = (gates[k : k + 1, :] * dslot).astype(BF16)
        datt_ref[rows, :] = datt
        delta_ref[k : k + 1, :] = jnp.sum(datt.astype(F32) * attended, axis=0, keepdims=True)
    dgate = jnp.concatenate(dgates, axis=0)
    dchosen = gates * (dgate - jnp.sum(gates * dgate, axis=0, keepdims=True))
    experts = lax.broadcasted_iota(jnp.int32, (E, tokens), 0)
    dlogits = jnp.zeros((E, tokens), F32)
    for k in range(TOPK):
        dlogits = jnp.where(
            slot_of(routes, k, E) == experts,
            jnp.broadcast_to(dchosen[k : k + 1, :], (E, tokens)),
            dlogits,
        )
    dlogit_ref[...] = dlogits

    @pl.when(step == pl.num_programs(0) - 1)
    def _():
        last = low_scr.shape[0]
        ends = (0, (W1_ROW - WO_ROW - 8) // 16 * 16, (W2_ROW - WO_ROW - 8) // 16 * 16, last)

        def out(number):
            first, count = ends[number], ends[number + 1] - ends[number]
            return pltpu.make_async_copy(
                low_scr.at[pl.ds(first, count), :],
                flat_ref.at[pl.ds(WO_ROW + 8 + first, count), :],
                row_sem.at[number],
            )

        def leave(number):
            first, count = ends[number], ends[number + 1] - ends[number]
            low_scr[pl.ds(first, count), :] = rows_scr[pl.ds(first + 8, count), :].astype(BF16)
            out(number).start()

        for c in range(D // 128):
            rows_scr[pl.ds(c, QW, stride=4), :] = dwo_ref[:, c * 128 : (c + 1) * 128]
        extra_ref[...] = rows_scr[0:8, :]
        leave(0)
        for c in range(FF // 128):
            rows_scr[pl.ds(W1_ROW - WO_ROW + c, D, stride=16), :] = dw1_ref[:, c * 128 : (c + 1) * 128]
        leave(1)
        for c in range(D // 128):
            rows_scr[pl.ds(W2_ROW - WO_ROW + c, FF, stride=4), :] = dw2t_ref[c * 128 : (c + 1) * 128, :].T
        leave(2)
        for number in range(3):
            out(number).wait()


def head_backward_kernel(
    segment_smem, x_ref, gain_ref, wall_ref, route_ref, start_ref, q_ref, datt_ref,
    lse_ref, delta_ref, kv_ref, kvt_ref, dlogit_ref, dres_ref, dgain_two_ref, extra_ref, flat_in,
    dx_ref, flat_ref,
    dk_scr, dv_scr, dq_scr, dall_scr, prob_scr, dscore_scr, dwall_ref, dgain_ref, rows_scr, low_scr, row_sem,
):
    step = pl.program_id(0)
    place = NB - 1 - lax.rem(step, NB)
    here = pl.multiple_of(place * TB, TB)

    @pl.when(step == 0)
    def _():
        dwall_ref[...] = jnp.zeros_like(dwall_ref)
        dgain_ref[...] = jnp.zeros_like(dgain_ref)

    @pl.when(lax.rem(step, NB) == 0)
    def _():
        dk_scr[...] = jnp.zeros_like(dk_scr)
        dv_scr[...] = jnp.zeros_like(dv_scr)

    def attend(lanes, block, blocks):
        rows = blocks * QB
        first_key = pl.multiple_of((block - (blocks - 1)) * QB, QB)
        mask = key_mask(first_key, block * QB, rows, start_ref[:, lanes])
        keys = kv_ref[pl.ds(first_key, rows), :H]
        values = kv_ref[pl.ds(first_key, rows), H:]
        keys_t = kvt_ref[:H, pl.ds(first_key, rows)]
        queries = [group_of(q_ref, k, lanes) for k in range(0, TOPK, SIDE)]
        datts = [group_of(datt_ref, k, lanes) for k in range(0, TOPK, SIDE)]
        scores = [nn(keys, queries[0])]
        dprobs = [nn(values, datts[0])]
        for i in range(TOPK // SIDE):
            if i + 1 < TOPK // SIDE:
                scores.append(nn(keys, queries[i + 1]))
                dprobs.append(nn(values, datts[i + 1]))
            k = i * SIDE
            wide = slice(k * QB, (k + SIDE) * QB)
            probs = jnp.exp(jnp.where(mask, scores[i], NEG_LARGE) - row_group(lse_ref, k, lanes))
            dscore = (probs * (dprobs[i] - row_group(delta_ref, k, lanes))).astype(BF16)
            prob_scr[0:rows, wide] = probs.astype(BF16)
            dscore_scr[0:rows, wide] = dscore
            dq = (nn(keys_t, dscore) * (H ** (-0.5))).astype(BF16)
            for side in range(SIDE):
                dq_scr[(k + side) * H : (k + side + 1) * H, lanes] = dq[:, side * QB : (side + 1) * QB]
        dv_scr[pl.ds(first_key, rows), :] += nt(prob_scr[0:rows, :], jnp.concatenate(datts, axis=1))
        dk_scr[pl.ds(first_key, rows), :] += nt(dscore_scr[0:rows, :], jnp.concatenate(queries, axis=1))

    by_span(attend, lax.div(step, NB), place, segment_smem)
    place_heads(route_ref[...], dq_scr, dall_scr)
    dkv = jnp.concatenate([dk_scr[pl.ds(here, TB), :], dv_scr[pl.ds(here, TB), :]], axis=1)
    dall_scr[KROW : KROW + 2 * H, :] = dkv.T.astype(BF16)
    dall_scr[RROW : RROW + 32, :] = jnp.concatenate(
        [dlogit_ref[...], jnp.zeros((32 - E, TB), F32)], axis=0
    ).astype(BF16)
    x = x_ref[...].astype(F32)
    scale = rms_scale(x)
    gain = gain_ref[...]
    normed = (x * scale * gain).astype(BF16)
    dall = dall_scr[...]
    dwall_ref[...] += nn(dall, normed)
    dnormed = tn(dall, wall_ref[...])
    dgain_ref[...] += jnp.sum(dnormed * x * scale, axis=0, keepdims=True)
    weighted = gain * dnormed
    dx_ref[...] = (
        dres_ref[...]
        + scale * weighted
        - x * (scale * scale * scale) * jnp.mean(weighted * x, axis=-1, keepdims=True)
    )

    @pl.when(step == pl.num_programs(0) - 1)
    def _():
        for c in range(D // 128):
            lanes = slice(c * 128, (c + 1) * 128)
            rows_scr[c : c + 1, :] = dgain_ref[:, lanes]
            rows_scr[4 + c : 5 + c, :] = dgain_two_ref[:, lanes]
        router_t = dwall_ref[RROW : RROW + E, :]
        across = jnp.concatenate(
            [exact(((1,), (1,)), router_t, picks(32, 16, b)) for b in range(16)], axis=0
        ).T
        for j in range(3):
            rows_scr[pl.ds(WR_ROW + j, 32, stride=3), :] = across[:, j * 128 : (j + 1) * 128]
        for first, row in ((KROW, WK_ROW), (VROW, WV_ROW)):
            part = dwall_ref[first : first + H, :]
            rows_scr[row : row + 256, :] = jnp.concatenate(
                [exact(((1,), (1,)), picks(256, 2, b), part) for b in range(2)], axis=1
            )
        for c in range(QW // 128):
            rows_scr[pl.ds(WQ_ROW + c, D, stride=12), :] = dwall_ref[c * 128 : (c + 1) * 128, :].T
        rows_scr[WO_ROW : WO_ROW + 8, :] = extra_ref[...]
        low_scr[...] = rows_scr[...].astype(BF16)
        copy = pltpu.make_async_copy(low_scr, flat_ref.at[pl.ds(0, WO_ROW + 8), :], row_sem.at[0])
        copy.start()
        copy.wait()


def whole(shape):
    return pl.BlockSpec(shape, lambda *_: (0,) * len(shape), pipeline_mode=pl.Buffered(1))


def kept(shape):
    return pl.BlockSpec(shape, lambda *_: (0,) * len(shape))


SMEM = pl.BlockSpec(memory_space=pltpu.SMEM)


def struct(shape, kind=F32):
    return jax.ShapeDtypeStruct(shape, kind)


def params_for(mib):
    return pltpu.CompilerParams(vmem_limit_bytes=mib * MIB)


def head_forward(tokens, routes_t, segments, wall, gain):
    count = tokens.shape[0]
    steps = count // TB
    across = lambda rows: pl.BlockSpec((rows, TB), lambda b: (0, b))
    down = lambda columns: pl.BlockSpec((TB, columns), lambda b: (b, 0))
    return pl.pallas_call(
        functools.partial(head_forward_kernel, steps),
        grid=(steps,),
        in_specs=[SMEM, down(D), across(TOPK), whole(segments.shape), whole((ALLW, D)), whole((1, D))],
        out_specs=[
            across(TOPK * H), across(TOPK * H), across(TOPK), across(TOPK), down(2 * H), across(2 * H),
            across(1), across(TOPK), whole((1, 128)),
        ],
        scratch_shapes=[
            pltpu.VMEM((ALLW, TB), F32),
            pltpu.VMEM((QW, TB), BF16),
            pltpu.VMEM((LEN, H), BF16),
            pltpu.VMEM((H, LEN), BF16),
            pltpu.VMEM((E, TB), F32),
        ],
        out_shape=[
            struct((TOPK * H, count), BF16),
            struct((TOPK * H, count)),
            struct((TOPK, count)),
            struct((TOPK, count)),
            struct((count, 2 * H), BF16),
            struct((2 * H, count), BF16),
            struct((1, count), jnp.int32),
            struct((TOPK, count), jnp.int32),
            struct((1, 128)),
        ],
        compiler_params=params_for(56),
        name="head_forward",
        cost_estimate=pl.CostEstimate(flops=10_000_000_000, bytes_accessed=16_000_000, transcendentals=0),
    )(segments, tokens, routes_t, segments, wall, gain)


def middle(flat_rows, tokens, grad_out, gain, wo, w1, w2, routes_t, gates, attended):
    count = tokens.shape[0]
    steps = count // MB
    across = lambda rows: pl.BlockSpec((rows, MB), lambda b: (0, b))
    down = lambda columns: pl.BlockSpec((MB, columns), lambda b: (b, 0))
    return pl.pallas_call(
        middle_kernel,
        grid=(steps,),
        in_specs=[
            down(D), down(D), whole((1, D)), whole((QW, D)), whole((D, FF)), whole((FF, D)),
            across(TOPK), across(TOPK), across(TOPK * H),
        ],
        out_specs=[
            down(D), down(D), across(TOPK * H), across(TOPK), across(E),
            pl.BlockSpec(memory_space=pl.ANY), whole((8, 128)), whole((1, D)),
        ],
        out_shape=[
            struct((count, D), BF16),
            struct((count, D)),
            struct((TOPK * H, count), BF16),
            struct((TOPK, count)),
            struct((E, count)),
            struct((flat_rows, 128), BF16),
            struct((8, 128)),
            struct((1, D)),
        ],
        scratch_shapes=[
            pltpu.VMEM((TOPK * H, MB), BF16),
            pltpu.VMEM((QW, MB), BF16),
            pltpu.VMEM((QW, MB), BF16),
            pltpu.VMEM((MB, FF), BF16),
            pltpu.VMEM((MB, FF), BF16),
            pltpu.VMEM((QW, D), F32),
            pltpu.VMEM((D, FF), F32),
            pltpu.VMEM((D, FF), F32),
            pltpu.VMEM((flat_rows - WO_ROW, 128), F32),
            pltpu.VMEM((flat_rows - WO_ROW - 8, 128), BF16),
            pltpu.SemaphoreType.DMA((3,)),
        ],
        compiler_params=params_for(60),
        name="middle",
    )(tokens, grad_out, gain, wo, w1, w2, routes_t, gates, attended)


def head_backward(
    segments, tokens, gain, wall, routes_t, start, queries, datt, lse, delta, kv, kvt, dlogits, dres,
    dgain_two, extra, flat,
):
    count = tokens.shape[0]
    steps = count // TB

    def place(b):
        return (b // NB) * NB + NB - 1 - b % NB

    across = lambda rows: pl.BlockSpec((rows, TB), lambda b: (0, place(b)))
    down = lambda columns: pl.BlockSpec((TB, columns), lambda b: (place(b), 0))
    return pl.pallas_call(
        head_backward_kernel,
        grid=(steps,),
        in_specs=[
            SMEM, down(D), whole((1, D)), whole((ALLW, D)), across(TOPK), across(1),
            across(TOPK * H), across(TOPK * H), across(TOPK), across(TOPK),
            pl.BlockSpec((LEN, 2 * H), lambda b: (b // NB, 0)),
            pl.BlockSpec((2 * H, LEN), lambda b: (0, b // NB)),
            across(E), down(D), whole((1, D)), whole((8, 128)), pl.BlockSpec(memory_space=pl.ANY),
        ],
        out_specs=[down(D), pl.BlockSpec(memory_space=pl.ANY)],
        scratch_shapes=[
            pltpu.VMEM((LEN, H), F32),
            pltpu.VMEM((LEN, H), F32),
            pltpu.VMEM((TOPK * H, TB), BF16),
            pltpu.VMEM((ALLW, TB), BF16),
            pltpu.VMEM((MOST * QB, TOPK * QB), BF16),
            pltpu.VMEM((MOST * QB, TOPK * QB), BF16),
            pltpu.VMEM((ALLW, D), F32),
            pltpu.VMEM((1, D), F32),
            pltpu.VMEM((WO_ROW + 8, 128), F32),
            pltpu.VMEM((WO_ROW + 8, 128), BF16),
            pltpu.SemaphoreType.DMA((1,)),
        ],
        out_shape=[struct((count, D)), struct(flat.shape, BF16)],
        input_output_aliases={16: 1},
        compiler_params=params_for(56),
        name="head_backward",
        cost_estimate=pl.CostEstimate(flops=30_000_000_000, bytes_accessed=24_000_000, transcendentals=0),
    )(
        segments, tokens, gain, wall, routes_t, start, queries, datt, lse, delta, kv, kvt, dlogits, dres,
        dgain_two, extra, flat,
    )


class Mesh3:
    def __init__(self, shards, over):
        shard = lax.axis_index("dp")
        other = lax.axis_index("fsdp")
        self.over = over
        self.many = shards * over
        self.sizes = {"x": 2, "y": shards // 2, "z": over // 2}
        self.here = {"x": lax.rem(other, 2), "y": lax.div(shard, 2), "z": lax.div(other, 2)}
        self.core = lax.rem(shard, 2)
        self.me = shard * over + other
        self.partner = (shard + 1 - 2 * self.core, other)

    def at_z(self, z):
        same = copy.copy(self)
        if z is not None:
            same.here = dict(self.here, z=z)
        return same

    def spots(self):
        x, y, z = (self.sizes[axis] for axis in "xyz")
        return list(itertools.product(range(x), range(y), range(1 - z, z)))

    def round_spots(self):
        return list(itertools.product(*[range(self.sizes[axis]) for axis in "xyz"]))

    def exists(self, z_steps):
        place = self.here["z"] + z_steps
        if isinstance(place, int):
            return 0 <= place < self.sizes["z"]
        return (place >= 0) & (place < self.sizes["z"])

    def device(self, core, spot):
        size = self.sizes["z"]
        x = lax.rem(self.here["x"] + spot[0], self.sizes["x"])
        y = lax.rem(self.here["y"] + spot[1], self.sizes["y"])
        z = self.here["z"] + spot[2]
        z = z % size if isinstance(z, int) else lax.rem(z + size, size)
        return (y * 2 + core, z * 2 + x)

    def number(self, core, spot):
        shard, other = self.device(core, spot)
        return shard * self.over + other

    def greet(self, devices):
        barrier = pltpu.get_barrier_semaphore()
        for device in devices:
            pl.semaphore_signal(barrier, inc=1, device_id=device, device_id_type=MESH)
        pl.semaphore_wait(barrier, len(devices))

    def near(self):
        steps = [at(axis, step) for axis in "xyz" for step in range(1, self.sizes[axis])]
        return [self.device(self.core, step) for step in steps] + [self.partner]

    def column(self):
        steps = [(core, step) for core in range(2) for step in range(self.sizes["z"]) if core or step]
        return [self.device(lax.rem(self.core + core, 2), (0, 0, step)) for core, step in steps]

    def layer(self):
        steps = [(x, y, 0) for x in range(self.sizes["x"]) for y in range(self.sizes["y"]) if x or y]
        return [self.device(self.core, step) for step in steps]


def at(axis, step):
    return tuple(step if one == axis else 0 for one in "xyz")


def last_axis(axes, spot):
    return max([i for i, axis in enumerate(axes) if spot["xyz".index(axis)]], default=-1)


def pieces_of(window, count=2):
    if window < 512:
        return [(0, window)]
    ends = [window // 16 * i // count * 16 for i in range(count)] + [window]
    return [(first, last - first) for first, last in zip(ends, ends[1:])]


def act(condition, action):
    if condition is True:
        action()
    elif condition is not False:
        pl.when(condition)(action)


GATHER_AXES = (("zxy", "yzx"), ("zyx", "xzy"))
REDUCE_PIECES = 3
REDUCE_AXES = ("zxy", "zyx")


def onward(mesh, axes, spot):
    last = last_axis(axes, spot)
    steps = []
    if last >= 0 and axes[last] == "z":
        steps.append(("z", -1 if spot[2] > 0 else 1))
    for axis in axes[last + 1 :]:
        steps += [("z", 1), ("z", -1)] if axis == "z" else [
            (axis, one) for one in range(1, mesh.sizes[axis])
        ]
    return steps


def gather_own_core(mesh, core, land, send_sem, recv_sem, begin):
    window = land.shape[1]
    pieces = pieces_of(window)
    slots = {}
    events = []

    def moved(owner, device, slot, p):
        rows = pl.ds(*pieces[p])
        return pltpu.make_async_remote_copy(
            src_ref=land.at[owner, rows],
            dst_ref=land.at[owner, rows],
            send_sem=send_sem.at[slot, p],
            recv_sem=recv_sem.at[owner, p],
            device_id=device,
            device_id_type=MESH,
        )

    for spot in mesh.spots():
        there = mesh.exists(spot[2])
        if there is False:
            continue
        owner = mesh.number(core, spot)
        turn = 0.5 * abs(spot[2]) + (spot[0] > 0) + (spot[1] > 0) + (0.001 if spot[2] < 0 else 0)
        for p in range(len(pieces)):
            sends = []
            for axis, step in onward(mesh, GATHER_AXES[core][p], spot):
                key = (spot[0], spot[1], spot[2] % mesh.sizes["z"], axis, step)
                away = mesh.exists(step) if axis == "z" else True
                if away is not False:
                    slot = slots.setdefault(key, len(slots))
                    sends.append((mesh.device(core, at(axis, step)), slot, away))
            key = (spot[0], spot[1], spot[2] % mesh.sizes["z"])
            sends.append((mesh.partner, slots.setdefault(key, len(slots)), True))

            def come(owner=owner, spot=spot, p=p, sends=sends):
                if any(spot):
                    moved(owner, mesh.partner, 0, p).wait_recv()
                for device, slot, away in sends:
                    act(away, moved(owner, device, slot, p).start)

            def done(owner=owner, p=p, sends=sends):
                for _, slot, away in sends:
                    act(away, moved(owner, mesh.partner, slot, p).wait_send)

            events.append((turn + 0.01 * p, there, come if begin else done))
    for _, there, action in sorted(events, key=lambda one: one[0]):
        act(there, action)


def gather_blocks(mesh, land, send_sem, recv_sem, begin):
    known = range(mesh.sizes["z"]) if mesh.sizes["z"] <= 4 else [None]
    for core in range(2):
        for z in known:

            @pl.when((mesh.core == core) & (True if z is None else mesh.here["z"] == z))
            def _(core=core, z=z):
                gather_own_core(mesh.at_z(z), core, land, send_sem, recv_sem, begin)


def each_owner(mesh, core, action):
    def one(number, carry):
        shard = 2 * lax.div(number, mesh.over) + core
        action(shard * mesh.over + lax.rem(number, mesh.over))
        return carry

    lax.fori_loop(0, mesh.many // 2, one, 0)


def reduce_blocks(mesh, core, source, mine, outgo, income, send_sem, recv_sem, total_ref):
    pieces = pieces_of(outgo.shape[1], REDUCE_PIECES)
    half = mesh.many // 2
    held = {spot: i for i, spot in enumerate(mesh.round_spots())}

    def across(kind, spot, p):
        slot = held[spot]
        return pltpu.make_async_remote_copy(
            src_ref=source(mesh.number(kind, spot), *pieces[p]),
            dst_ref=income.at[slot, pl.ds(*pieces[p])],
            send_sem=send_sem.at[slot, p],
            recv_sem=recv_sem.at[slot, p],
            device_id=mesh.partner,
            device_id_type=MESH,
        )

    def moved(spot, p, device):
        rows = pl.ds(*pieces[p])
        slot = half + held[spot]
        return pltpu.make_async_remote_copy(
            src_ref=outgo.at[held[spot], rows],
            dst_ref=income.at[slot, rows],
            send_sem=send_sem.at[slot, p],
            recv_sem=recv_sem.at[slot, p],
            device_id=device,
            device_id_type=MESH,
        )

    def far(spot):
        z = {0: 0, 1: 3, 2: 5, 3: 8}.get(spot[2], 2 * spot[2] + 2)
        return z + 2 * (spot[0] > 0) + 2 * (spot[1] > 0)

    axes = REDUCE_AXES[core]

    def hand(spot, p):
        across(1 - core, spot, p).start()

    def pass_on(spot, p):
        rows = pl.ds(*pieces[p])
        across(core, spot, p).wait_recv()
        total = mine(mesh.number(core, spot), *pieces[p]) + income[held[spot], rows].astype(F32)
        last = last_axis(axes, spot)
        for axis in axes[last + 1 :]:
            size = mesh.sizes[axis]
            for step in range(1, size):
                child = tuple(one or other for one, other in zip(spot, at(axis, size - step)))
                moved(child, p, mesh.partner).wait_recv()
                total = total + income[half + held[child], rows].astype(F32)
        if last < 0:
            total_ref[rows, :] = total
        else:
            outgo[held[spot], rows] = total.astype(BF16)
            step = spot["xyz".index(axes[last])]
            moved(spot, p, mesh.device(core, at(axes[last], step))).start()

    every = list(itertools.product(held, range(len(pieces))))
    events = [(-2 * far(spot) - 4 + 0.01 * p, 0, hand, spot, p) for spot, p in every]
    events += [(-2 * far(spot) + 2 * p / len(pieces), 1, pass_on, spot, p) for spot, p in every]
    for _, _, action, spot, p in sorted(events, key=lambda one: one[:2]):
        action(spot, p)
    for spot, p in every:
        across(1 - core, spot, p).wait_send()
        if any(spot):
            moved(spot, p, mesh.partner).wait_send()


def sum_all(mesh, mine, stats, send_sem, recv_sem):
    column = mesh.sizes["z"] * 2
    layer = mesh.sizes["x"] * mesh.sizes["y"]
    groups = (
        (0, column, mesh.here["z"] * 2 + mesh.core, mesh.column()),
        (column, layer, mesh.here["x"] * mesh.sizes["y"] + mesh.here["y"], mesh.layer()),
    )
    total = mine
    for base, size, here, devices in groups:
        stats[base + here] = total

        def sent(j, device, base=base, here=here):
            return pltpu.make_async_remote_copy(
                src_ref=stats.at[base + here],
                dst_ref=stats.at[base + here],
                send_sem=send_sem.at[base + j],
                recv_sem=recv_sem.at[base + here],
                device_id=device,
                device_id_type=MESH,
            )

        def come(place, base=base):
            return pltpu.make_async_remote_copy(
                src_ref=stats.at[base + place],
                dst_ref=stats.at[base + place],
                send_sem=send_sem.at[base],
                recv_sem=recv_sem.at[base + place],
                device_id=mesh.partner,
                device_id_type=MESH,
            )

        for j, device in enumerate(devices):
            sent(j, device).start()
        for j in range(1, size):
            come(lax.rem(here + j, size)).wait_recv()
        for j, device in enumerate(devices):
            sent(j, device).wait_send()
        total = stats[base]
        for place in range(1, size):
            total = total + stats[base + place]
    return total


def window_rows(shard_size, many):
    units = [(shard_size * d) // UNIT for d in range(many + 1)]
    return 16 * (max(b - a for a, b in zip(units, units[1:])) + 1)


def first_row(shard_size, number):
    if isinstance(number, int):
        return number * shard_size // UNIT * 16
    return pl.multiple_of(lax.div(number * shard_size, UNIT) * 16, 16)


def inner_units(shard_size, many):
    units = [(shard_size * d) // UNIT for d in range(many + 1)]
    return min(b - a for a, b in zip(units, units[1:]))


def lay_inner(shard_size, many, land, flat, owner):
    count = 16 * inner_units(shard_size, many) - 16
    row = pl.multiple_of(first_row(shard_size, owner) + 16, 16)
    flat[pl.ds(row, count), :] = land[owner, pl.ds(16, count), :].astype(F32)


def lay_edges(shard_size, many, land, flat):
    inner = 16 * inner_units(shard_size, many)
    flat[0:16, :] = jnp.zeros((16, 128), F32)

    def lay(number, carry):
        row = first_row(shard_size, number)
        after = first_row(shard_size, number + 1)
        flat[pl.ds(row, 16), :] += land[number, 0:16, :].astype(F32)
        tail = land[number, pl.ds(inner, 16), :].astype(F32)
        flat[pl.ds(pl.multiple_of(row + inner, 16), 16), :] = tail
        last = pl.multiple_of(after - row, 16)
        flat[pl.ds(after, 16), :] = land[number, pl.ds(last, 16), :].astype(F32)
        return carry

    lax.fori_loop(0, many, lay, 0)


def early_matrices(flat, wall_ref, gain_one_ref, gain_two_ref):
    for c in range(D // 128):
        lanes = slice(c * 128, (c + 1) * 128)
        gain_one_ref[:, lanes] = flat[c : c + 1, :]
        gain_two_ref[:, lanes] = flat[4 + c : 5 + c, :]
    for c in range(QW // 128):
        wall_ref[c * 128 : (c + 1) * 128, :] = flat[pl.ds(WQ_ROW + c, D, stride=12), :].T.astype(BF16)
    for first, row in ((KROW, WK_ROW), (VROW, WV_ROW)):
        pair = flat[row : row + 256, :].T.astype(BF16)
        wall_ref[first : first + H, :] = (
            nn(pair[:H], picks(256, 2, 0).astype(BF16)) + nn(pair[H:], picks(256, 2, 1).astype(BF16))
        ).astype(BF16)
    across = jnp.concatenate(
        [flat[pl.ds(WR_ROW + j, 32, stride=3), :] for j in range(3)], axis=1
    ).T.astype(BF16)
    router_t = jnp.zeros((E, D), F32)
    for part in range(16):
        router_t = router_t + nn(across[part * E : (part + 1) * E, :], picks(32, 16, part).astype(BF16))
    wall_ref[RROW:ALLW, :] = jnp.concatenate(
        [router_t, jnp.zeros((ALLW - RROW - E, D), F32)], axis=0
    ).astype(BF16)


def gather_kernel(
    mesh, shard_size, own_ref,
    wall_out, gain_one_ref, gain_two_ref, wo_out, w1_out, w2_out,
    land, flat, wall_ref, wo_ref, w1_ref, w2_ref, send_sem, recv_sem, out_sem,
):
    mesh = mesh()
    many = mesh.many
    mesh.greet(mesh.near())
    land[mesh.me] = own_ref[...].astype(BF16)
    gather_blocks(mesh, land, send_sem, recv_sem, True)
    each_owner(mesh, mesh.core, functools.partial(lay_inner, shard_size, many, land, flat))

    def arrive(owner):
        for p in range(recv_sem.shape[1]):
            rows = pl.ds(*pieces_of(own_ref.shape[0])[p])
            pltpu.make_async_remote_copy(
                src_ref=land.at[owner, rows],
                dst_ref=land.at[owner, rows],
                send_sem=send_sem.at[0, p],
                recv_sem=recv_sem.at[owner, p],
                device_id=mesh.partner,
                device_id_type=MESH,
            ).wait_recv()
        lay_inner(shard_size, many, land, flat, owner)

    each_owner(mesh, 1 - mesh.core, arrive)
    lay_edges(shard_size, many, land, flat)
    copies = []

    def leave(matrix, out):
        one = pltpu.make_async_copy(matrix, out, out_sem.at[len(copies)])
        one.start()
        copies.append(one)

    for c in range(D // 128):
        wo_ref[:, c * 128 : (c + 1) * 128] = flat[pl.ds(WO_ROW + c, QW, stride=4), :].astype(BF16)
    leave(wo_ref, wo_out)
    for c in range(D // 128):
        w2_ref[:, c * 128 : (c + 1) * 128] = flat[pl.ds(W2_ROW + c, FF, stride=4), :].astype(BF16)
    leave(w2_ref, w2_out)
    for c in range(FF // 128):
        w1_ref[:, c * 128 : (c + 1) * 128] = flat[pl.ds(W1_ROW + c, D, stride=16), :].astype(BF16)
    leave(w1_ref, w1_out)
    early_matrices(flat, wall_ref, gain_one_ref, gain_two_ref)
    leave(wall_ref, wall_out)
    gather_blocks(mesh, land, send_sem, recv_sem, False)
    for one in copies:
        one.wait()


def gather_weights(shards, over, shard_size, own):
    window = own.shape[0]
    many = shards * over
    rows = (shard_size * (many - 1)) // UNIT * 16 + window
    vmem = pl.BlockSpec(memory_space=pltpu.VMEM)
    hbm = pl.BlockSpec(memory_space=pl.ANY)
    mesh = functools.partial(Mesh3, shards, over)
    pieces = len(pieces_of(window))
    return pl.pallas_call(
        functools.partial(gather_kernel, mesh, shard_size),
        in_specs=[vmem],
        out_specs=[hbm, vmem, vmem, hbm, hbm, hbm],
        out_shape=[
            struct((ALLW, D), BF16),
            struct((1, D)),
            struct((1, D)),
            struct((QW, D), BF16),
            struct((D, FF), BF16),
            struct((FF, D), BF16),
        ],
        scratch_shapes=[
            pltpu.VMEM((many, window, 128), BF16),
            pltpu.VMEM((rows, 128), F32),
            pltpu.VMEM((ALLW, D), BF16),
            pltpu.VMEM((QW, D), BF16),
            pltpu.VMEM((D, FF), BF16),
            pltpu.VMEM((FF, D), BF16),
            pltpu.SemaphoreType.DMA((5 * many // 2, pieces)),
            pltpu.SemaphoreType.DMA((many, pieces)),
            pltpu.SemaphoreType.DMA((4,)),
        ],
        compiler_params=pltpu.CompilerParams(
            collective_id=0, has_side_effects=True, vmem_limit_bytes=60 * MIB
        ),
        name="gather_weights",
    )(own)


def reduce_kernel(
    mesh, shard_size, flat_ref, count_ref,
    out_ref, total_ref, gain_ref,
    part, outgo, income, whole_scr, stats, part_sem, send_sem, recv_sem, stat_send, stat_recv,
):
    mesh = mesh()
    window = outgo.shape[1]
    span = part.shape[1]

    def source(owner, first, rows):
        row = pl.multiple_of(first_row(shard_size, owner) + first, 16)
        return flat_ref.at[pl.ds(row, rows), :]

    def fetch(y):
        first = first_row(shard_size, (2 * y + mesh.core) * mesh.over)
        return pltpu.make_async_copy(flat_ref.at[pl.ds(first, span), :], part.at[y], part_sem.at[y])

    def mine(owner, first, rows):
        shard = lax.div(owner, mesh.over)
        row = first_row(shard_size, owner) - first_row(shard_size, shard * mesh.over) + first
        return part[lax.div(shard, 2), pl.ds(pl.multiple_of(row, 16), rows), :].astype(F32)

    for y in range(mesh.sizes["y"]):
        fetch(y).start()
    mesh.greet(mesh.column() + mesh.layer())
    for y in range(mesh.sizes["y"]):
        fetch(y).wait()
    buffers = (source, mine, outgo, income, send_sem, recv_sem, whole_scr)
    for core in range(2):
        pl.when(mesh.core == core)(functools.partial(reduce_blocks, mesh, core, *buffers))

    begin = mesh.me * shard_size - lax.div(mesh.me * shard_size, UNIT) * UNIT
    rows = out_ref.shape[0]
    row, lane = lax.div(begin, 128), lax.rem(begin, 128)
    back = lax.rem(128 - lane, 128)
    first = pltpu.roll(whole_scr[pl.ds(row, rows), :], back, 1)
    second = pltpu.roll(whole_scr[pl.ds(row + 1, rows), :], back, 1)
    at_lane = lax.broadcasted_iota(jnp.int32, (rows, 128), 1)
    place = lax.broadcasted_iota(jnp.int32, (rows, 128), 0) * 128 + at_lane
    total = jnp.where(at_lane < 128 - lane, first, second)
    out_ref[...] = total
    inside = jnp.where(place < shard_size, total, 0.0)
    squares = jnp.sum(jnp.sum(inside * inside, axis=0, keepdims=True), axis=1, keepdims=True)
    lane = lax.broadcasted_iota(jnp.int32, (8, 128), 1)
    row = jnp.where(lane == E, squares, count_ref[...])
    gains = jnp.where(mesh.me == 0, total[0:8, :], 0.0)
    summed = sum_all(mesh, jnp.concatenate([row, gains], axis=0), stats, stat_send, stat_recv)
    total_ref[...] = summed[0:1, :]
    for c in range(D // 128):
        lanes = slice(c * 128, (c + 1) * 128)
        gain_ref[0:1, lanes] = summed[8 + c : 9 + c, :]
        gain_ref[1:2, lanes] = summed[12 + c : 13 + c, :]


def reduce_grads(shards, over, shard_size, window, flat, counts):
    vmem = pl.BlockSpec(memory_space=pltpu.VMEM)
    many = shards * over
    mesh = functools.partial(Mesh3, shards, over)
    pieces = len(pieces_of(window, REDUCE_PIECES))
    steps = over + shards
    units = [(shard_size * d) // UNIT for d in range(many)]
    span = 16 * max(units[d + over - 1] - units[d] for d in range(0, many, over)) + window
    return pl.pallas_call(
        functools.partial(reduce_kernel, mesh, shard_size),
        in_specs=[pl.BlockSpec(memory_space=pl.ANY), vmem],
        out_specs=[vmem] * 3,
        out_shape=[struct((-(-shard_size // 128), 128)), struct((1, 128)), struct((2, D))],
        scratch_shapes=[
            pltpu.VMEM((shards // 2, span, 128), BF16),
            pltpu.VMEM((many // 2, window, 128), BF16),
            pltpu.VMEM((many, window, 128), BF16),
            pltpu.VMEM((window + 16, 128), F32),
            pltpu.VMEM((steps, 16, 128), F32),
            pltpu.SemaphoreType.DMA((shards // 2,)),
            pltpu.SemaphoreType.DMA((many, pieces)),
            pltpu.SemaphoreType.DMA((many, pieces)),
            pltpu.SemaphoreType.DMA((steps,)),
            pltpu.SemaphoreType.DMA((steps,)),
        ],
        compiler_params=pltpu.CompilerParams(
            collective_id=1, has_side_effects=True, vmem_limit_bytes=56 * MIB
        ),
        name="reduce_grads",
    )(flat, counts)


def local_step(flat_rows, tokens, grad_out, routes, segments, weights):
    wall, gain_one, gain_two, wo, w1, w2 = weights
    queries, attended, gates, lse, kv, kvt, start, routes_t, counts = head_forward(
        tokens, routes.T, segments, wall, gain_one
    )
    output, dres, datt, delta, dlogits, flat, extra, dgain_two = middle(
        flat_rows, tokens, grad_out, gain_two, wo, w1, w2, routes_t, gates, attended
    )
    input_grad, flat = head_backward(
        segments, tokens, gain_one, wall, routes_t, start, queries, datt, lse, delta, kv, kvt, dlogits, dres,
        dgain_two, extra, flat,
    )
    return output, input_grad, flat, counts


def per_device(
    shards, over, tokens, grad_out, routes, segments, params, first_moment, second_moment, ema_weights
):
    shard_size = params.shape[0]
    window = window_rows(shard_size, shards * over)
    flat_rows = (shard_size * (shards * over - 1)) // UNIT * 16 + window + 16
    me = lax.axis_index("dp") * over + lax.axis_index("fsdp")
    begin = lax.rem(me * shard_size, UNIT)
    own = lax.dynamic_slice(
        jnp.pad(params, (UNIT, window * 128 - shard_size)), (UNIT - begin,), (window * 128,)
    ).reshape(window, 128)
    wall, gain_one, gain_two, wo, w1, w2 = gather_weights(shards, over, shard_size, own)
    output, input_grad, flat, counts = local_step(
        flat_rows, tokens, grad_out, routes, segments, (wall, gain_one, gain_two, wo, w1, w2)
    )
    reduced, sums, gain_grads = reduce_grads(shards, over, shard_size, window, flat, counts)
    grad_shard = reduced.reshape(-1)[:shard_size]
    total_tokens = tokens.shape[0] * shards * over
    expert_load = sums[0, :E] * (E / (total_tokens * TOPK))
    grad_norm = jnp.sqrt(sums[0, E])
    clipped = grad_shard * (CLIP_LIMIT / jnp.maximum(grad_norm, CLIP_LIMIT))
    new_first = BETA_FIRST * first_moment + (1.0 - BETA_FIRST) * clipped
    new_second = BETA_SECOND * second_moment + (1.0 - BETA_SECOND) * clipped * clipped
    first_hat = new_first / (1.0 - BETA_FIRST**STEP)
    second_hat = new_second / (1.0 - BETA_SECOND**STEP)
    new_params = params * (1.0 - LEARN_RATE * DECAY_RATE) - LEARN_RATE * first_hat / (
        jnp.sqrt(second_hat) + ADAM_EPS
    )
    new_ema = EMA_KEEP * ema_weights + (1.0 - EMA_KEEP) * new_params
    return (
        output,
        input_grad,
        expert_load,
        grad_norm.reshape(1),
        new_params,
        new_first,
        new_second,
        new_ema,
        gain_grads,
    )


def solution(mesh):
    row = P(("dp", "fsdp"), None)
    flat = P(("dp", "fsdp"))
    return jax.shard_map(
        functools.partial(per_device, mesh.shape["dp"], mesh.shape["fsdp"]),
        mesh=mesh,
        in_specs=(row, row, row, row, flat, flat, flat, flat),
        out_specs=(row, row, P(), P(), flat, flat, flat, flat, P()),
        check_vma=False,
    )
```

```python
import copy
import functools
import itertools

import jax
import jax.numpy as jnp
from jax import lax
from jax.experimental import pallas as pl
from jax.experimental.pallas import tpu as pltpu
from jax.sharding import PartitionSpec as P

D = 512
E = 24
TOPK = 8
H = 64
FF = 2048
STEP = 10

NORM_EPS = 1e-06
CLIP_LIMIT = 1.0
BETA_FIRST = 0.9
BETA_SECOND = 0.95
LEARN_RATE = 0.1
DECAY_RATE = 0.1
ADAM_EPS = 1e-08
EMA_KEEP = 0.9
NEG_LARGE = -1e30

QW = E * H
KROW = QW
VROW = QW + H
RROW = QW + 2 * H
ALLW = 1696
LEN = 1024
TB = 512
NB = LEN // TB
QB = 128
SIDE = 4
MOST = 512 // QB + 1
SORT_STEPS = (
    (0, 1), (2, 3), (4, 5), (6, 7), (0, 2), (1, 3), (4, 6), (5, 7), (1, 2), (5, 6),
    (0, 4), (1, 5), (2, 6), (3, 7), (2, 4), (3, 5), (1, 2), (3, 4), (5, 6),
)
FC = 256
MB = 512
MIB = 1 << 20

WR_ROW = 8
WK_ROW = 104
WV_ROW = 360
WQ_ROW = 616
WO_ROW = 6760
W1_ROW = 12904
W2_ROW = 21096
ALL_ROWS = 29288
UNIT = 16 * 128
MESH = pl.DeviceIdType.MESH

F32 = jnp.float32
BF16 = jnp.bfloat16


def nn(a, b):
    return lax.dot_general(a, b, (((1,), (0,)), ((), ())), preferred_element_type=F32)


def nt(a, b):
    return lax.dot_general(a, b, (((1,), (1,)), ((), ())), preferred_element_type=F32)


def tn(a, b):
    return lax.dot_general(a, b, (((0,), (0,)), ((), ())), preferred_element_type=F32)


def rms_scale(values):
    return lax.rsqrt(jnp.mean(values * values, axis=-1, keepdims=True) + NORM_EPS)


def slot_of(routes, k, rows):
    return jnp.broadcast_to(routes[k : k + 1, :], (rows, routes.shape[1]))


def expert_rows(routes, k):
    return jnp.broadcast_to(routes.astype(jnp.int16)[k : k + 1, :], (16, routes.shape[1]))


def pick_heads(routes, source_ref, k):
    tokens = routes.shape[1]
    route = expert_rows(routes, k)
    taken = source_ref[k * H : (k + 1) * H, :].reshape(H // 16, 16, tokens)
    for e in range(k + 1, k + E - TOPK + 1):
        piece = source_ref[e * H : (e + 1) * H, :].reshape(H // 16, 16, tokens)
        taken = jnp.where((route == jnp.int16(e))[None], piece, taken)
    return taken.reshape(H, tokens)


def place_heads(routes, source_ref, target_ref):
    tokens = routes.shape[1]
    rows = [expert_rows(routes, k) for k in range(TOPK)]
    for e in range(E):
        total = jnp.zeros((H // 16, 16, tokens), BF16)
        for k in range(max(0, e - (E - TOPK)), min(TOPK - 1, e) + 1):
            piece = source_ref[k * H : (k + 1) * H, :].reshape(H // 16, 16, tokens)
            total = jnp.where((rows[k] == jnp.int16(e))[None], piece, total)
        target_ref[e * H : (e + 1) * H, :] = total.reshape(H, tokens)


def sorted_rows(rows):
    rows = list(rows)
    for one, two in SORT_STEPS:
        rows[one], rows[two] = jnp.minimum(rows[one], rows[two]), jnp.maximum(rows[one], rows[two])
    return rows


def key_mask(first_key, first_query, rows, start_row):
    keys = lax.broadcasted_iota(jnp.int32, (rows, QB), 0) + first_key
    queries = lax.broadcasted_iota(jnp.int32, (rows, QB), 1) + first_query
    mask = (keys <= queries) & (keys >= start_row)
    return jnp.concatenate([mask] * SIDE, axis=1)


def group_of(ref, k, lanes):
    return jnp.concatenate([ref[i * H : (i + 1) * H, lanes] for i in range(k, k + SIDE)], axis=1)


def row_group(ref, k, lanes):
    return jnp.concatenate([ref[i : i + 1, lanes] for i in range(k, k + SIDE)], axis=1)


def by_span(attend, row, place, segment_ref):
    def one(j, carry):
        block = place * (TB // QB) + j
        first = block * QB
        span = jnp.int32(1)
        for back in range(MOST - 1):
            last = first - back * QB - 1
            same = segment_ref[row, jnp.maximum(last, 0)] == segment_ref[row, first]
            span = span + jnp.where((last >= 0) & same, 1, 0)
        for blocks in range(1, MOST + 1):

            @pl.when(span == blocks)
            def _(blocks=blocks):
                attend(pl.ds(pl.multiple_of(j * QB, QB), QB), block, blocks)

        return carry

    lax.fori_loop(0, TB // QB, one, 0)


def head_forward_kernel(
    steps, segment_smem, x_ref, route_ref, segment_ref, wall_ref, gain_ref,
    wo_rows, w1_rows, w2_rows,
    q_ref, att_ref, gate_ref, lse_ref, kv_ref, kvt_ref, start_ref, sorted_ref, count_ref,
    wo_ref, w1_ref, w2_ref,
    all_scr, low_scr, k_scr, vt_scr, count_scr,
):
    step = pl.program_id(0)
    place = lax.rem(step, NB)
    here = pl.multiple_of(place * TB, TB)

    @pl.when(step == 0)
    def _():
        count_scr[...] = jnp.zeros_like(count_scr)

    row = segment_ref[pl.ds(lax.div(step, NB), 1), :]
    segments = segment_ref[pl.ds(lax.div(step, NB), 1), pl.ds(here, TB)]
    start = jnp.zeros((1, TB), jnp.int32)
    for number in range(1, 4):
        below = jnp.sum((row < number).astype(jnp.int32), axis=1, keepdims=True)
        start = jnp.where(segments == number, below, start)
    start_ref[...] = start
    x = x_ref[...].astype(F32)
    normed = (x * rms_scale(x) * gain_ref[...]).astype(BF16)
    all_scr[...] = nt(wall_ref[...], normed)
    for rows, target in ((wo_rows, wo_ref), (w1_rows, w1_ref), (w2_rows, w2_ref)):
        wide = target.shape[1] // 128
        for c in range(wide):
            target[:, c * 128 : (c + 1) * 128] = rows[
                pl.ds(c, target.shape[0], stride=wide), :
            ].astype(BF16)
    kt = all_scr[KROW : KROW + H, :]
    vt = all_scr[VROW : VROW + H, :]
    logits = all_scr[RROW : RROW + E, :]
    kvt = jnp.concatenate([kt, vt], axis=0)
    kv = kvt.T.astype(BF16)
    kv_ref[...] = kv
    kvt_ref[...] = kvt.astype(BF16)
    k_scr[pl.ds(here, TB), :] = kv[:, :H]
    vt_scr[:, pl.ds(here, TB)] = vt.astype(BF16)
    routes = jnp.concatenate(sorted_rows(route_ref[k : k + 1, :] for k in range(TOPK)), axis=0)
    sorted_ref[...] = routes
    experts = lax.broadcasted_iota(jnp.int32, (E, TB), 0)
    chosen = []
    counts = count_scr[...]
    for k in range(TOPK):
        named = slot_of(routes, k, E) == experts
        chosen.append(jnp.sum(jnp.where(named, logits, 0.0), axis=0, keepdims=True))
        counts = counts + named.astype(F32)
    count_scr[...] = counts
    chosen = jnp.concatenate(chosen, axis=0)
    raised = jnp.exp(chosen - jnp.max(chosen, axis=0, keepdims=True))
    gate_ref[...] = raised / jnp.sum(raised, axis=0, keepdims=True)
    low_scr[...] = all_scr[0:QW, :].astype(BF16)
    for k in range(TOPK):
        q_ref[k * H : (k + 1) * H, :] = pick_heads(routes, low_scr, k) * jnp.asarray(H ** (-0.5), BF16)

    def attend(lanes, block, blocks):
        rows = blocks * QB
        first_key = pl.multiple_of((block - (blocks - 1)) * QB, QB)
        mask = key_mask(first_key, block * QB, rows, start_ref[:, lanes])
        keys = k_scr[pl.ds(first_key, rows), :]
        values = vt_scr[:, pl.ds(first_key, rows)]
        groups = [nn(keys, group_of(q_ref, 0, lanes))]
        for k in range(0, TOPK, SIDE):
            if k + SIDE < TOPK:
                groups.append(nn(keys, group_of(q_ref, k + SIDE, lanes)))
            scores = jnp.where(mask, groups[k // SIDE], NEG_LARGE)
            top = jnp.max(scores, axis=0, keepdims=True)
            raised = jnp.exp(scores - top)
            total = jnp.sum(raised, axis=0, keepdims=True)
            out = nn(values, (raised * (1.0 / total)).astype(BF16))
            lse = top + jnp.log(total)
            for side in range(SIDE):
                one = slice(side * QB, (side + 1) * QB)
                att_ref[(k + side) * H : (k + side + 1) * H, lanes] = out[:, one]
                lse_ref[k + side : k + side + 1, lanes] = lse[:, one]

    by_span(attend, lax.div(step, NB), place, segment_smem)

    @pl.when(step == steps - 1)
    def _():
        held = jnp.sum(count_scr[...], axis=1, keepdims=True)
        lane = lax.broadcasted_iota(jnp.int32, (E, 128), 1)
        row = lax.broadcasted_iota(jnp.int32, (E, 128), 0)
        count_ref[...] = jnp.sum(jnp.where(lane == row, held, 0.0), axis=0, keepdims=True)


def picks(rows, stride, first):
    at = lax.broadcasted_iota(jnp.int32, (rows, D), 1)
    row = lax.broadcasted_iota(jnp.int32, (rows, D), 0)
    return (at == row * stride + first).astype(F32)


def exact(product, a, b):
    return lax.dot_general(
        a, b, (product, ((), ())), precision=lax.Precision.HIGHEST, preferred_element_type=F32
    )


def gelu_parts(v):
    cdf = 0.5 + 0.5 * lax.erf(v * 0.7071067811865476)
    return cdf, jnp.exp(v * v * -0.5) * 0.3989422804014327


def middle_kernel(
    x_ref, dy_ref, gain_ref, wo_ref, w1_ref, w2_ref, route_ref, gate_ref, att_ref,
    out_ref, dres_ref, datt_ref, delta_ref, dlogit_ref, flat_ref, extra_ref, dgain_ref,
    slot_scr, head_scr, mix_scr, hidden_scr, dpre_scr, dwo_ref, dw1_ref, dw2t_ref, rows_scr, low_scr, row_sem,
):
    step = pl.program_id(0)

    @pl.when(step == 0)
    def _():
        dwo_ref[...] = jnp.zeros_like(dwo_ref)
        dw1_ref[...] = jnp.zeros_like(dw1_ref)
        dw2t_ref[...] = jnp.zeros_like(dw2t_ref)
        dgain_ref[...] = jnp.zeros_like(dgain_ref)

    routes = route_ref[...]
    tokens = routes.shape[1]
    gates = gate_ref[...]
    for k in range(TOPK):
        rows = slice(k * H, (k + 1) * H)
        slot_scr[rows, :] = (gates[k : k + 1, :] * att_ref[rows, :]).astype(BF16)
    place_heads(routes, slot_scr, mix_scr)
    x = x_ref[...].astype(F32)
    dy = dy_ref[...]
    mixed = mix_scr[...]
    residual = x + tn(mixed, wo_ref[...])
    scale = rms_scale(residual)
    gain = gain_ref[...]
    second = (residual * scale * gain).astype(BF16)
    second_t = second.T
    dy_t = dy.T
    pre = [nn(second, w1_ref[:, 0:FC])]
    back = [nt(dy, w2_ref[0:FC, :])]
    for i in range(FF // FC):
        here = slice(i * FC, (i + 1) * FC)
        if i + 1 < FF // FC:
            after = slice((i + 1) * FC, (i + 2) * FC)
            pre.append(nn(second, w1_ref[:, after]))
            back.append(nt(dy, w2_ref[after, :]))
        cdf, density = gelu_parts(pre[i])
        hidden_scr[:, here] = (pre[i] * cdf).astype(BF16)
        dpre_scr[:, here] = (back[i] * (cdf + pre[i] * density)).astype(BF16)
    dsecond = nt(dpre_scr[...], w1_ref[...])
    out_ref[...] = (residual + nn(hidden_scr[...], w2_ref[...])).astype(BF16)
    dw1_ref[...] += nn(second_t, dpre_scr[...])
    dw2t_ref[...] += nn(dy_t, hidden_scr[...])
    dgain_ref[...] += jnp.sum(dsecond * residual * scale, axis=0, keepdims=True)
    weighted = gain * dsecond
    dres = (
        dy.astype(F32)
        + scale * weighted
        - residual * (scale * scale * scale) * jnp.mean(weighted * residual, axis=-1, keepdims=True)
    )
    dres_ref[...] = dres
    branch = dres.astype(BF16)
    dwo_ref[...] += nn(mixed, branch)
    head_scr[...] = nt(wo_ref[...], branch).astype(BF16)
    dgates = []
    for k in range(TOPK):
        rows = slice(k * H, (k + 1) * H)
        dslot = pick_heads(routes, head_scr, k).astype(F32)
        attended = att_ref[rows, :]
        dgates.append(jnp.sum(dslot * attended, axis=0, keepdims=True))
        datt = (gates[k : k + 1, :] * dslot).astype(BF16)
        datt_ref[rows, :] = datt
        delta_ref[k : k + 1, :] = jnp.sum(datt.astype(F32) * attended, axis=0, keepdims=True)
    dgate = jnp.concatenate(dgates, axis=0)
    dchosen = gates * (dgate - jnp.sum(gates * dgate, axis=0, keepdims=True))
    experts = lax.broadcasted_iota(jnp.int32, (E, tokens), 0)
    dlogits = jnp.zeros((E, tokens), F32)
    for k in range(TOPK):
        dlogits = jnp.where(
            slot_of(routes, k, E) == experts,
            jnp.broadcast_to(dchosen[k : k + 1, :], (E, tokens)),
            dlogits,
        )
    dlogit_ref[...] = dlogits

    @pl.when(step == pl.num_programs(0) - 1)
    def _():
        last = low_scr.shape[0]
        ends = (0, (W1_ROW - WO_ROW - 8) // 16 * 16, (W2_ROW - WO_ROW - 8) // 16 * 16, last)

        def out(number):
            first, count = ends[number], ends[number + 1] - ends[number]
            return pltpu.make_async_copy(
                low_scr.at[pl.ds(first, count), :],
                flat_ref.at[pl.ds(WO_ROW + 8 + first, count), :],
                row_sem.at[number],
            )

        def leave(number):
            first, count = ends[number], ends[number + 1] - ends[number]
            low_scr[pl.ds(first, count), :] = rows_scr[pl.ds(first + 8, count), :].astype(BF16)
            out(number).start()

        for c in range(D // 128):
            rows_scr[pl.ds(c, QW, stride=4), :] = dwo_ref[:, c * 128 : (c + 1) * 128]
        extra_ref[...] = rows_scr[0:8, :]
        leave(0)
        for c in range(FF // 128):
            rows_scr[pl.ds(W1_ROW - WO_ROW + c, D, stride=16), :] = dw1_ref[:, c * 128 : (c + 1) * 128]
        leave(1)
        for c in range(D // 128):
            rows_scr[pl.ds(W2_ROW - WO_ROW + c, FF, stride=4), :] = dw2t_ref[c * 128 : (c + 1) * 128, :].T
        leave(2)
        for number in range(3):
            out(number).wait()


def head_backward_kernel(
    segment_smem, x_ref, gain_ref, wall_ref, route_ref, start_ref, q_ref, datt_ref,
    lse_ref, delta_ref, kv_ref, kvt_ref, dlogit_ref, dres_ref, dgain_two_ref, extra_ref, flat_in,
    dx_ref, flat_ref,
    dk_scr, dv_scr, dq_scr, dall_scr, prob_scr, dscore_scr, dquery_ref, drest_ref, dgain_ref, rows_scr, low_scr, row_sem,
):
    step = pl.program_id(0)
    place = NB - 1 - lax.rem(step, NB)
    here = pl.multiple_of(place * TB, TB)

    @pl.when(step == 0)
    def _():
        dquery_ref[...] = jnp.zeros_like(dquery_ref)
        drest_ref[...] = jnp.zeros_like(drest_ref)
        dgain_ref[...] = jnp.zeros_like(dgain_ref)

    @pl.when(lax.rem(step, NB) == 0)
    def _():
        dk_scr[...] = jnp.zeros_like(dk_scr)
        dv_scr[...] = jnp.zeros_like(dv_scr)

    def attend(lanes, block, blocks):
        rows = blocks * QB
        first_key = pl.multiple_of((block - (blocks - 1)) * QB, QB)
        mask = key_mask(first_key, block * QB, rows, start_ref[:, lanes])
        keys = kv_ref[pl.ds(first_key, rows), :H]
        values = kv_ref[pl.ds(first_key, rows), H:]
        keys_t = kvt_ref[:H, pl.ds(first_key, rows)]
        queries = [group_of(q_ref, k, lanes) for k in range(0, TOPK, SIDE)]
        datts = [group_of(datt_ref, k, lanes) for k in range(0, TOPK, SIDE)]
        scores = [nn(keys, queries[0])]
        dprobs = [nn(values, datts[0])]
        for i in range(TOPK // SIDE):
            if i + 1 < TOPK // SIDE:
                scores.append(nn(keys, queries[i + 1]))
                dprobs.append(nn(values, datts[i + 1]))
            k = i * SIDE
            wide = slice(k * QB, (k + SIDE) * QB)
            probs = jnp.exp(jnp.where(mask, scores[i], NEG_LARGE) - row_group(lse_ref, k, lanes))
            dscore = (probs * (dprobs[i] - row_group(delta_ref, k, lanes))).astype(BF16)
            prob_scr[0:rows, wide] = probs.astype(BF16)
            dscore_scr[0:rows, wide] = dscore
            dq = (nn(keys_t, dscore) * (H ** (-0.5))).astype(BF16)
            for side in range(SIDE):
                dq_scr[(k + side) * H : (k + side + 1) * H, lanes] = dq[:, side * QB : (side + 1) * QB]
        dv_scr[pl.ds(first_key, rows), :] += nt(prob_scr[0:rows, :], jnp.concatenate(datts, axis=1))
        dk_scr[pl.ds(first_key, rows), :] += nt(dscore_scr[0:rows, :], jnp.concatenate(queries, axis=1))

    by_span(attend, lax.div(step, NB), place, segment_smem)
    place_heads(route_ref[...], dq_scr, dall_scr)
    dkv = jnp.concatenate([dk_scr[pl.ds(here, TB), :], dv_scr[pl.ds(here, TB), :]], axis=1)
    dall_scr[KROW : KROW + 2 * H, :] = dkv.T.astype(BF16)
    dall_scr[RROW : RROW + 32, :] = jnp.concatenate(
        [dlogit_ref[...], jnp.zeros((32 - E, TB), F32)], axis=0
    ).astype(BF16)
    x = x_ref[...].astype(F32)
    scale = rms_scale(x)
    gain = gain_ref[...]
    normed = (x * scale * gain).astype(BF16)
    dall = dall_scr[...]
    dquery_ref[...] += nt(normed.T, dall_scr[:QW, :])
    drest_ref[...] += nn(dall_scr[QW:, :], normed)
    dnormed = tn(dall, wall_ref[...])
    dgain_ref[...] += jnp.sum(dnormed * x * scale, axis=0, keepdims=True)
    weighted = gain * dnormed
    dx_ref[...] = (
        dres_ref[...]
        + scale * weighted
        - x * (scale * scale * scale) * jnp.mean(weighted * x, axis=-1, keepdims=True)
    )

    @pl.when(step == pl.num_programs(0) - 1)
    def _():
        for c in range(D // 128):
            lanes = slice(c * 128, (c + 1) * 128)
            rows_scr[c : c + 1, :] = dgain_ref[:, lanes]
            rows_scr[4 + c : 5 + c, :] = dgain_two_ref[:, lanes]
        router_t = drest_ref[2 * H : 2 * H + E, :]
        across = jnp.concatenate(
            [exact(((1,), (1,)), router_t, picks(32, 16, b)) for b in range(16)], axis=0
        ).T
        for j in range(3):
            rows_scr[pl.ds(WR_ROW + j, 32, stride=3), :] = across[:, j * 128 : (j + 1) * 128]
        for first, row in ((0, WK_ROW), (H, WV_ROW)):
            part = drest_ref[first : first + H, :]
            rows_scr[row : row + 256, :] = jnp.concatenate(
                [exact(((1,), (1,)), picks(256, 2, b), part) for b in range(2)], axis=1
            )
        for c in range(QW // 128):
            rows_scr[pl.ds(WQ_ROW + c, D, stride=12), :] = dquery_ref[:, c * 128 : (c + 1) * 128]
        rows_scr[WO_ROW : WO_ROW + 8, :] = extra_ref[...]
        low_scr[...] = rows_scr[...].astype(BF16)
        copy = pltpu.make_async_copy(low_scr, flat_ref.at[pl.ds(0, WO_ROW + 8), :], row_sem.at[0])
        copy.start()
        copy.wait()


def whole(shape):
    return pl.BlockSpec(shape, lambda *_: (0,) * len(shape), pipeline_mode=pl.Buffered(1))


def kept(shape):
    return pl.BlockSpec(shape, lambda *_: (0,) * len(shape))


SMEM = pl.BlockSpec(memory_space=pltpu.SMEM)


def struct(shape, kind=F32):
    return jax.ShapeDtypeStruct(shape, kind)


def params_for(mib):
    return pltpu.CompilerParams(vmem_limit_bytes=mib * MIB)


def head_forward(tokens, routes_t, segments, wall, gain, wo, w1, w2):
    count = tokens.shape[0]
    steps = count // TB
    part = lambda rows, columns: pl.BlockSpec((rows // steps, columns), lambda b: (b, 0))
    across = lambda rows: pl.BlockSpec((rows, TB), lambda b: (0, b))
    down = lambda columns: pl.BlockSpec((TB, columns), lambda b: (b, 0))
    return pl.pallas_call(
        functools.partial(head_forward_kernel, steps),
        grid=(steps,),
        in_specs=[
            SMEM, down(D), across(TOPK), whole(segments.shape), whole((ALLW, D)), whole((1, D)),
            part(wo.shape[0], 128), part(w1.shape[0], 128), part(w2.shape[0], 128),
        ],
        out_specs=[
            across(TOPK * H), across(TOPK * H), across(TOPK), across(TOPK), down(2 * H), across(2 * H),
            across(1), across(TOPK), whole((1, 128)),
            part(QW, D), part(D, FF), part(FF, D),
        ],
        scratch_shapes=[
            pltpu.VMEM((ALLW, TB), F32),
            pltpu.VMEM((QW, TB), BF16),
            pltpu.VMEM((LEN, H), BF16),
            pltpu.VMEM((H, LEN), BF16),
            pltpu.VMEM((E, TB), F32),
        ],
        out_shape=[
            struct((TOPK * H, count), BF16),
            struct((TOPK * H, count)),
            struct((TOPK, count)),
            struct((TOPK, count)),
            struct((count, 2 * H), BF16),
            struct((2 * H, count), BF16),
            struct((1, count), jnp.int32),
            struct((TOPK, count), jnp.int32),
            struct((1, 128)),
            struct((QW, D), BF16),
            struct((D, FF), BF16),
            struct((FF, D), BF16),
        ],
        compiler_params=params_for(56),
        name="head_forward",
        cost_estimate=pl.CostEstimate(flops=10_000_000_000, bytes_accessed=16_000_000, transcendentals=0),
    )(segments, tokens, routes_t, segments, wall, gain, wo, w1, w2)


def middle(flat_rows, tokens, grad_out, gain, wo, w1, w2, routes_t, gates, attended):
    count = tokens.shape[0]
    steps = count // MB
    across = lambda rows: pl.BlockSpec((rows, MB), lambda b: (0, b))
    down = lambda columns: pl.BlockSpec((MB, columns), lambda b: (b, 0))
    return pl.pallas_call(
        middle_kernel,
        grid=(steps,),
        in_specs=[
            down(D), down(D), whole((1, D)), whole((QW, D)), whole((D, FF)), whole((FF, D)),
            across(TOPK), across(TOPK), across(TOPK * H),
        ],
        out_specs=[
            down(D), down(D), across(TOPK * H), across(TOPK), across(E),
            pl.BlockSpec(memory_space=pl.ANY), whole((8, 128)), whole((1, D)),
        ],
        out_shape=[
            struct((count, D), BF16),
            struct((count, D)),
            struct((TOPK * H, count), BF16),
            struct((TOPK, count)),
            struct((E, count)),
            struct((flat_rows, 128), BF16),
            struct((8, 128)),
            struct((1, D)),
        ],
        scratch_shapes=[
            pltpu.VMEM((TOPK * H, MB), BF16),
            pltpu.VMEM((QW, MB), BF16),
            pltpu.VMEM((QW, MB), BF16),
            pltpu.VMEM((MB, FF), BF16),
            pltpu.VMEM((MB, FF), BF16),
            pltpu.VMEM((QW, D), F32),
            pltpu.VMEM((D, FF), F32),
            pltpu.VMEM((D, FF), F32),
            pltpu.VMEM((flat_rows - WO_ROW, 128), F32),
            pltpu.VMEM((flat_rows - WO_ROW - 8, 128), BF16),
            pltpu.SemaphoreType.DMA((3,)),
        ],
        compiler_params=params_for(60),
        name="middle",
    )(tokens, grad_out, gain, wo, w1, w2, routes_t, gates, attended)


def head_backward(
    segments, tokens, gain, wall, routes_t, start, queries, datt, lse, delta, kv, kvt, dlogits, dres,
    dgain_two, extra, flat,
):
    count = tokens.shape[0]
    steps = count // TB

    def place(b):
        return (b // NB) * NB + NB - 1 - b % NB

    across = lambda rows: pl.BlockSpec((rows, TB), lambda b: (0, place(b)))
    down = lambda columns: pl.BlockSpec((TB, columns), lambda b: (place(b), 0))
    return pl.pallas_call(
        head_backward_kernel,
        grid=(steps,),
        in_specs=[
            SMEM, down(D), whole((1, D)), whole((ALLW, D)), across(TOPK), across(1),
            across(TOPK * H), across(TOPK * H), across(TOPK), across(TOPK),
            pl.BlockSpec((LEN, 2 * H), lambda b: (b // NB, 0)),
            pl.BlockSpec((2 * H, LEN), lambda b: (0, b // NB)),
            across(E), down(D), whole((1, D)), whole((8, 128)), pl.BlockSpec(memory_space=pl.ANY),
        ],
        out_specs=[down(D), pl.BlockSpec(memory_space=pl.ANY)],
        scratch_shapes=[
            pltpu.VMEM((LEN, H), F32),
            pltpu.VMEM((LEN, H), F32),
            pltpu.VMEM((TOPK * H, TB), BF16),
            pltpu.VMEM((ALLW, TB), BF16),
            pltpu.VMEM((MOST * QB, TOPK * QB), BF16),
            pltpu.VMEM((MOST * QB, TOPK * QB), BF16),
            pltpu.VMEM((D, QW), F32),
            pltpu.VMEM((ALLW - QW, D), F32),
            pltpu.VMEM((1, D), F32),
            pltpu.VMEM((WO_ROW + 8, 128), F32),
            pltpu.VMEM((WO_ROW + 8, 128), BF16),
            pltpu.SemaphoreType.DMA((1,)),
        ],
        out_shape=[struct((count, D)), struct(flat.shape, BF16)],
        input_output_aliases={16: 1},
        compiler_params=params_for(56),
        name="head_backward",
        cost_estimate=pl.CostEstimate(flops=30_000_000_000, bytes_accessed=24_000_000, transcendentals=0),
    )(
        segments, tokens, gain, wall, routes_t, start, queries, datt, lse, delta, kv, kvt, dlogits, dres,
        dgain_two, extra, flat,
    )


class Mesh3:
    def __init__(self, shards, over):
        shard = lax.axis_index("dp")
        other = lax.axis_index("fsdp")
        self.over = over
        self.many = shards * over
        self.sizes = {"x": 2, "y": shards // 2, "z": over // 2}
        self.here = {"x": lax.rem(other, 2), "y": lax.div(shard, 2), "z": lax.div(other, 2)}
        self.core = lax.rem(shard, 2)
        self.me = shard * over + other
        self.partner = (shard + 1 - 2 * self.core, other)

    def at_z(self, z):
        same = copy.copy(self)
        if z is not None:
            same.here = dict(self.here, z=z)
        return same

    def spots(self):
        x, y, z = (self.sizes[axis] for axis in "xyz")
        return list(itertools.product(range(x), range(y), range(1 - z, z)))

    def round_spots(self):
        return list(itertools.product(*[range(self.sizes[axis]) for axis in "xyz"]))

    def exists(self, z_steps):
        place = self.here["z"] + z_steps
        if isinstance(place, int):
            return 0 <= place < self.sizes["z"]
        return (place >= 0) & (place < self.sizes["z"])

    def device(self, core, spot):
        size = self.sizes["z"]
        x = lax.rem(self.here["x"] + spot[0], self.sizes["x"])
        y = lax.rem(self.here["y"] + spot[1], self.sizes["y"])
        z = self.here["z"] + spot[2]
        z = z % size if isinstance(z, int) else lax.rem(z + size, size)
        return (y * 2 + core, z * 2 + x)

    def number(self, core, spot):
        shard, other = self.device(core, spot)
        return shard * self.over + other

    def greet(self, devices):
        barrier = pltpu.get_barrier_semaphore()
        for device in devices:
            pl.semaphore_signal(barrier, inc=1, device_id=device, device_id_type=MESH)
        pl.semaphore_wait(barrier, len(devices))

    def near(self):
        steps = [at(axis, step) for axis in "xyz" for step in range(1, self.sizes[axis])]
        return [self.device(self.core, step) for step in steps] + [self.partner]

    def column(self):
        steps = [(core, step) for core in range(2) for step in range(self.sizes["z"]) if core or step]
        return [self.device(lax.rem(self.core + core, 2), (0, 0, step)) for core, step in steps]

    def layer(self):
        steps = [(x, y, 0) for x in range(self.sizes["x"]) for y in range(self.sizes["y"]) if x or y]
        return [self.device(self.core, step) for step in steps]


def at(axis, step):
    return tuple(step if one == axis else 0 for one in "xyz")


def last_axis(axes, spot):
    return max([i for i, axis in enumerate(axes) if spot["xyz".index(axis)]], default=-1)


def pieces_of(window, count=2):
    if window < 512:
        return [(0, window)]
    ends = [window // 16 * i // count * 16 for i in range(count)] + [window]
    return [(first, last - first) for first, last in zip(ends, ends[1:])]


def act(condition, action):
    if condition is True:
        action()
    elif condition is not False:
        pl.when(condition)(action)


GATHER_AXES = (("zxy", "yzx"), ("zyx", "xzy"))
REDUCE_PIECES = 3
REDUCE_AXES = ("zxy", "zyx")


def onward(mesh, axes, spot):
    last = last_axis(axes, spot)
    steps = []
    if last >= 0 and axes[last] == "z":
        steps.append(("z", -1 if spot[2] > 0 else 1))
    for axis in axes[last + 1 :]:
        steps += [("z", 1), ("z", -1)] if axis == "z" else [
            (axis, one) for one in range(1, mesh.sizes[axis])
        ]
    return steps


def gather_own_core(mesh, core, land, send_sem, recv_sem, begin):
    window = land.shape[1]
    pieces = pieces_of(window)
    slots = {}
    events = []

    def moved(owner, device, slot, p):
        rows = pl.ds(*pieces[p])
        return pltpu.make_async_remote_copy(
            src_ref=land.at[owner, rows],
            dst_ref=land.at[owner, rows],
            send_sem=send_sem.at[slot, p],
            recv_sem=recv_sem.at[owner, p],
            device_id=device,
            device_id_type=MESH,
        )

    for spot in mesh.spots():
        there = mesh.exists(spot[2])
        if there is False:
            continue
        owner = mesh.number(core, spot)
        turn = 0.5 * abs(spot[2]) + (spot[0] > 0) + (spot[1] > 0) + (0.001 if spot[2] < 0 else 0)
        for p in range(len(pieces)):
            sends = []
            for axis, step in onward(mesh, GATHER_AXES[core][p], spot):
                key = (spot[0], spot[1], spot[2] % mesh.sizes["z"], axis, step)
                away = mesh.exists(step) if axis == "z" else True
                if away is not False:
                    slot = slots.setdefault(key, len(slots))
                    sends.append((mesh.device(core, at(axis, step)), slot, away))
            key = (spot[0], spot[1], spot[2] % mesh.sizes["z"])
            sends.append((mesh.partner, slots.setdefault(key, len(slots)), True))

            def come(owner=owner, spot=spot, p=p, sends=sends):
                if any(spot):
                    moved(owner, mesh.partner, 0, p).wait_recv()
                for device, slot, away in sends:
                    act(away, moved(owner, device, slot, p).start)

            def done(owner=owner, p=p, sends=sends):
                for _, slot, away in sends:
                    act(away, moved(owner, mesh.partner, slot, p).wait_send)

            events.append((turn + 0.01 * p, there, come if begin else done))
    for _, there, action in sorted(events, key=lambda one: one[0]):
        act(there, action)


def gather_blocks(mesh, land, send_sem, recv_sem, begin):
    known = range(mesh.sizes["z"]) if mesh.sizes["z"] <= 4 else [None]
    for core in range(2):
        for z in known:

            @pl.when((mesh.core == core) & (True if z is None else mesh.here["z"] == z))
            def _(core=core, z=z):
                gather_own_core(mesh.at_z(z), core, land, send_sem, recv_sem, begin)


def each_owner(mesh, core, action):
    def one(number, carry):
        shard = 2 * lax.div(number, mesh.over) + core
        action(shard * mesh.over + lax.rem(number, mesh.over))
        return carry

    lax.fori_loop(0, mesh.many // 2, one, 0)


def reduce_blocks(mesh, core, source, mine, outgo, income, send_sem, recv_sem, total_ref):
    pieces = pieces_of(outgo.shape[1], REDUCE_PIECES)
    half = mesh.many // 2
    held = {spot: i for i, spot in enumerate(mesh.round_spots())}

    def across(kind, spot, p):
        slot = held[spot]
        return pltpu.make_async_remote_copy(
            src_ref=source(mesh.number(kind, spot), *pieces[p]),
            dst_ref=income.at[slot, pl.ds(*pieces[p])],
            send_sem=send_sem.at[slot, p],
            recv_sem=recv_sem.at[slot, p],
            device_id=mesh.partner,
            device_id_type=MESH,
        )

    def moved(spot, p, device):
        rows = pl.ds(*pieces[p])
        slot = half + held[spot]
        return pltpu.make_async_remote_copy(
            src_ref=outgo.at[held[spot], rows],
            dst_ref=income.at[slot, rows],
            send_sem=send_sem.at[slot, p],
            recv_sem=recv_sem.at[slot, p],
            device_id=device,
            device_id_type=MESH,
        )

    def far(spot):
        z = {0: 0, 1: 3, 2: 5, 3: 8}.get(spot[2], 2 * spot[2] + 2)
        return z + 2 * (spot[0] > 0) + 2 * (spot[1] > 0)

    axes = REDUCE_AXES[core]

    def hand(spot, p):
        across(1 - core, spot, p).start()

    def pass_on(spot, p):
        rows = pl.ds(*pieces[p])
        across(core, spot, p).wait_recv()
        total = mine(mesh.number(core, spot), *pieces[p]) + income[held[spot], rows].astype(F32)
        last = last_axis(axes, spot)
        for axis in axes[last + 1 :]:
            size = mesh.sizes[axis]
            for step in range(1, size):
                child = tuple(one or other for one, other in zip(spot, at(axis, size - step)))
                moved(child, p, mesh.partner).wait_recv()
                total = total + income[half + held[child], rows].astype(F32)
        if last < 0:
            total_ref[rows, :] = total
        else:
            outgo[held[spot], rows] = total.astype(BF16)
            step = spot["xyz".index(axes[last])]
            moved(spot, p, mesh.device(core, at(axes[last], step))).start()

    every = list(itertools.product(held, range(len(pieces))))
    events = [(-2 * far(spot) - 4 + 0.01 * p, 0, hand, spot, p) for spot, p in every]
    events += [(-2 * far(spot) + 2 * p / len(pieces), 1, pass_on, spot, p) for spot, p in every]
    for _, _, action, spot, p in sorted(events, key=lambda one: one[:2]):
        action(spot, p)
    for spot, p in every:
        across(1 - core, spot, p).wait_send()
        if any(spot):
            moved(spot, p, mesh.partner).wait_send()


def sum_all(mesh, mine, stats, send_sem, recv_sem):
    column = mesh.sizes["z"] * 2
    layer = mesh.sizes["x"] * mesh.sizes["y"]
    groups = (
        (0, column, mesh.here["z"] * 2 + mesh.core, mesh.column()),
        (column, layer, mesh.here["x"] * mesh.sizes["y"] + mesh.here["y"], mesh.layer()),
    )
    total = mine
    for base, size, here, devices in groups:
        stats[base + here] = total

        def sent(j, device, base=base, here=here):
            return pltpu.make_async_remote_copy(
                src_ref=stats.at[base + here],
                dst_ref=stats.at[base + here],
                send_sem=send_sem.at[base + j],
                recv_sem=recv_sem.at[base + here],
                device_id=device,
                device_id_type=MESH,
            )

        def come(place, base=base):
            return pltpu.make_async_remote_copy(
                src_ref=stats.at[base + place],
                dst_ref=stats.at[base + place],
                send_sem=send_sem.at[base],
                recv_sem=recv_sem.at[base + place],
                device_id=mesh.partner,
                device_id_type=MESH,
            )

        for j, device in enumerate(devices):
            sent(j, device).start()
        for j in range(1, size):
            come(lax.rem(here + j, size)).wait_recv()
        for j, device in enumerate(devices):
            sent(j, device).wait_send()
        total = stats[base]
        for place in range(1, size):
            total = total + stats[base + place]
    return total


def window_rows(shard_size, many):
    units = [(shard_size * d) // UNIT for d in range(many + 1)]
    return 16 * (max(b - a for a, b in zip(units, units[1:])) + 1)


def first_row(shard_size, number):
    if isinstance(number, int):
        return number * shard_size // UNIT * 16
    return pl.multiple_of(lax.div(number * shard_size, UNIT) * 16, 16)


def inner_units(shard_size, many):
    units = [(shard_size * d) // UNIT for d in range(many + 1)]
    return min(b - a for a, b in zip(units, units[1:]))


def lay_inner(shard_size, many, land, flat, owner):
    count = 16 * inner_units(shard_size, many) - 16
    row = pl.multiple_of(first_row(shard_size, owner) + 16, 16)
    flat[pl.ds(row, count), :] = land[owner, pl.ds(16, count), :].astype(F32)


def lay_edges(shard_size, many, land, flat):
    inner = 16 * inner_units(shard_size, many)
    flat[0:16, :] = jnp.zeros((16, 128), F32)

    def lay(number, carry):
        row = first_row(shard_size, number)
        after = first_row(shard_size, number + 1)
        flat[pl.ds(row, 16), :] += land[number, 0:16, :].astype(F32)
        tail = land[number, pl.ds(inner, 16), :].astype(F32)
        flat[pl.ds(pl.multiple_of(row + inner, 16), 16), :] = tail
        last = pl.multiple_of(after - row, 16)
        flat[pl.ds(after, 16), :] = land[number, pl.ds(last, 16), :].astype(F32)
        return carry

    lax.fori_loop(0, many, lay, 0)


def early_matrices(flat, wall_ref, gain_one_ref, gain_two_ref):
    for c in range(D // 128):
        lanes = slice(c * 128, (c + 1) * 128)
        gain_one_ref[:, lanes] = flat[c : c + 1, :]
        gain_two_ref[:, lanes] = flat[4 + c : 5 + c, :]
    for c in range(QW // 128):
        wall_ref[c * 128 : (c + 1) * 128, :] = flat[pl.ds(WQ_ROW + c, D, stride=12), :].T.astype(BF16)
    for first, row in ((KROW, WK_ROW), (VROW, WV_ROW)):
        pair = flat[row : row + 256, :].T.astype(BF16)
        wall_ref[first : first + H, :] = (
            nn(pair[:H], picks(256, 2, 0).astype(BF16)) + nn(pair[H:], picks(256, 2, 1).astype(BF16))
        ).astype(BF16)
    across = jnp.concatenate(
        [flat[pl.ds(WR_ROW + j, 32, stride=3), :] for j in range(3)], axis=1
    ).T.astype(BF16)
    router_t = jnp.zeros((E, D), F32)
    for part in range(16):
        router_t = router_t + nn(across[part * E : (part + 1) * E, :], picks(32, 16, part).astype(BF16))
    wall_ref[RROW:ALLW, :] = jnp.concatenate(
        [router_t, jnp.zeros((ALLW - RROW - E, D), F32)], axis=0
    ).astype(BF16)


def gather_kernel(
    mesh, shard_size, own_ref,
    wall_out, gain_one_ref, gain_two_ref, wo_out, w1_out, w2_out,
    land, flat, wall_ref, send_sem, recv_sem, out_sem,
):
    mesh = mesh()
    many = mesh.many
    mesh.greet(mesh.near())
    land[mesh.me] = own_ref[...].astype(BF16)
    gather_blocks(mesh, land, send_sem, recv_sem, True)
    each_owner(mesh, mesh.core, functools.partial(lay_inner, shard_size, many, land, flat))

    def arrive(owner):
        for p in range(recv_sem.shape[1]):
            rows = pl.ds(*pieces_of(own_ref.shape[0])[p])
            pltpu.make_async_remote_copy(
                src_ref=land.at[owner, rows],
                dst_ref=land.at[owner, rows],
                send_sem=send_sem.at[0, p],
                recv_sem=recv_sem.at[owner, p],
                device_id=mesh.partner,
                device_id_type=MESH,
            ).wait_recv()
        lay_inner(shard_size, many, land, flat, owner)

    each_owner(mesh, 1 - mesh.core, arrive)
    lay_edges(shard_size, many, land, flat)
    copies = []

    def leave(matrix, out):
        one = pltpu.make_async_copy(matrix, out, out_sem.at[len(copies)])
        one.start()
        copies.append(one)

    for row, out in ((WO_ROW, wo_out), (W1_ROW, w1_out), (W2_ROW, w2_out)):
        leave(flat.at[pl.ds(row, out.shape[0]), :], out)
    early_matrices(flat, wall_ref, gain_one_ref, gain_two_ref)
    leave(wall_ref, wall_out)
    gather_blocks(mesh, land, send_sem, recv_sem, False)
    for one in copies:
        one.wait()


def gather_weights(shards, over, shard_size, own):
    window = own.shape[0]
    many = shards * over
    rows = (shard_size * (many - 1)) // UNIT * 16 + window
    vmem = pl.BlockSpec(memory_space=pltpu.VMEM)
    hbm = pl.BlockSpec(memory_space=pl.ANY)
    mesh = functools.partial(Mesh3, shards, over)
    pieces = len(pieces_of(window))
    return pl.pallas_call(
        functools.partial(gather_kernel, mesh, shard_size),
        in_specs=[vmem],
        out_specs=[hbm, vmem, vmem, hbm, hbm, hbm],
        out_shape=[
            struct((ALLW, D), BF16),
            struct((1, D)),
            struct((1, D)),
            struct((W1_ROW - WO_ROW, 128)),
            struct((W2_ROW - W1_ROW, 128)),
            struct((ALL_ROWS - W2_ROW, 128)),
        ],
        scratch_shapes=[
            pltpu.VMEM((many, window, 128), BF16),
            pltpu.VMEM((rows, 128), F32),
            pltpu.VMEM((ALLW, D), BF16),
            pltpu.SemaphoreType.DMA((5 * many // 2, pieces)),
            pltpu.SemaphoreType.DMA((many, pieces)),
            pltpu.SemaphoreType.DMA((4,)),
        ],
        compiler_params=pltpu.CompilerParams(
            collective_id=0, has_side_effects=True, vmem_limit_bytes=60 * MIB
        ),
        name="gather_weights",
    )(own)


def reduce_kernel(
    mesh, shard_size, flat_ref, count_ref,
    out_ref, total_ref, gain_ref,
    part, outgo, income, whole_scr, stats, part_sem, send_sem, recv_sem, stat_send, stat_recv,
):
    mesh = mesh()
    window = outgo.shape[1]
    span = part.shape[1]

    def source(owner, first, rows):
        row = pl.multiple_of(first_row(shard_size, owner) + first, 16)
        return flat_ref.at[pl.ds(row, rows), :]

    def fetch(y):
        first = first_row(shard_size, (2 * y + mesh.core) * mesh.over)
        return pltpu.make_async_copy(flat_ref.at[pl.ds(first, span), :], part.at[y], part_sem.at[y])

    def mine(owner, first, rows):
        shard = lax.div(owner, mesh.over)
        row = first_row(shard_size, owner) - first_row(shard_size, shard * mesh.over) + first
        return part[lax.div(shard, 2), pl.ds(pl.multiple_of(row, 16), rows), :].astype(F32)

    for y in range(mesh.sizes["y"]):
        fetch(y).start()
    mesh.greet(mesh.column() + mesh.layer())
    for y in range(mesh.sizes["y"]):
        fetch(y).wait()
    buffers = (source, mine, outgo, income, send_sem, recv_sem, whole_scr)
    for core in range(2):
        pl.when(mesh.core == core)(functools.partial(reduce_blocks, mesh, core, *buffers))

    begin = mesh.me * shard_size - lax.div(mesh.me * shard_size, UNIT) * UNIT
    rows = out_ref.shape[0]
    row, lane = lax.div(begin, 128), lax.rem(begin, 128)
    back = lax.rem(128 - lane, 128)
    first = pltpu.roll(whole_scr[pl.ds(row, rows), :], back, 1)
    second = pltpu.roll(whole_scr[pl.ds(row + 1, rows), :], back, 1)
    at_lane = lax.broadcasted_iota(jnp.int32, (rows, 128), 1)
    place = lax.broadcasted_iota(jnp.int32, (rows, 128), 0) * 128 + at_lane
    total = jnp.where(at_lane < 128 - lane, first, second)
    out_ref[...] = total
    inside = jnp.where(place < shard_size, total, 0.0)
    squares = jnp.sum(jnp.sum(inside * inside, axis=0, keepdims=True), axis=1, keepdims=True)
    lane = lax.broadcasted_iota(jnp.int32, (8, 128), 1)
    row = jnp.where(lane == E, squares, count_ref[...])
    gains = jnp.where(mesh.me == 0, total[0:8, :], 0.0)
    summed = sum_all(mesh, jnp.concatenate([row, gains], axis=0), stats, stat_send, stat_recv)
    total_ref[...] = summed[0:1, :]
    for c in range(D // 128):
        lanes = slice(c * 128, (c + 1) * 128)
        gain_ref[0:1, lanes] = summed[8 + c : 9 + c, :]
        gain_ref[1:2, lanes] = summed[12 + c : 13 + c, :]


def reduce_grads(shards, over, shard_size, window, flat, counts):
    vmem = pl.BlockSpec(memory_space=pltpu.VMEM)
    many = shards * over
    mesh = functools.partial(Mesh3, shards, over)
    pieces = len(pieces_of(window, REDUCE_PIECES))
    steps = over + shards
    units = [(shard_size * d) // UNIT for d in range(many)]
    span = 16 * max(units[d + over - 1] - units[d] for d in range(0, many, over)) + window
    return pl.pallas_call(
        functools.partial(reduce_kernel, mesh, shard_size),
        in_specs=[pl.BlockSpec(memory_space=pl.ANY), vmem],
        out_specs=[vmem] * 3,
        out_shape=[struct((-(-shard_size // 128), 128)), struct((1, 128)), struct((2, D))],
        scratch_shapes=[
            pltpu.VMEM((shards // 2, span, 128), BF16),
            pltpu.VMEM((many // 2, window, 128), BF16),
            pltpu.VMEM((many, window, 128), BF16),
            pltpu.VMEM((window + 16, 128), F32),
            pltpu.VMEM((steps, 16, 128), F32),
            pltpu.SemaphoreType.DMA((shards // 2,)),
            pltpu.SemaphoreType.DMA((many, pieces)),
            pltpu.SemaphoreType.DMA((many, pieces)),
            pltpu.SemaphoreType.DMA((steps,)),
            pltpu.SemaphoreType.DMA((steps,)),
        ],
        compiler_params=pltpu.CompilerParams(
            collective_id=1, has_side_effects=True, vmem_limit_bytes=56 * MIB
        ),
        name="reduce_grads",
    )(flat, counts)


def local_step(flat_rows, tokens, grad_out, routes, segments, weights):
    wall, gain_one, gain_two, wo, w1, w2 = weights
    queries, attended, gates, lse, kv, kvt, start, routes_t, counts, wo, w1, w2 = head_forward(
        tokens, routes.T, segments, wall, gain_one, wo, w1, w2
    )
    output, dres, datt, delta, dlogits, flat, extra, dgain_two = middle(
        flat_rows, tokens, grad_out, gain_two, wo, w1, w2, routes_t, gates, attended
    )
    input_grad, flat = head_backward(
        segments, tokens, gain_one, wall, routes_t, start, queries, datt, lse, delta, kv, kvt, dlogits, dres,
        dgain_two, extra, flat,
    )
    return output, input_grad, flat, counts


def per_device(
    shards, over, tokens, grad_out, routes, segments, params, first_moment, second_moment, ema_weights
):
    shard_size = params.shape[0]
    window = window_rows(shard_size, shards * over)
    flat_rows = (shard_size * (shards * over - 1)) // UNIT * 16 + window + 16
    me = lax.axis_index("dp") * over + lax.axis_index("fsdp")
    begin = lax.rem(me * shard_size, UNIT)
    own = lax.dynamic_slice(
        jnp.pad(params, (UNIT, window * 128 - shard_size)), (UNIT - begin,), (window * 128,)
    ).reshape(window, 128)
    wall, gain_one, gain_two, wo, w1, w2 = gather_weights(shards, over, shard_size, own)
    output, input_grad, flat, counts = local_step(
        flat_rows, tokens, grad_out, routes, segments, (wall, gain_one, gain_two, wo, w1, w2)
    )
    reduced, sums, gain_grads = reduce_grads(shards, over, shard_size, window, flat, counts)
    grad_shard = reduced.reshape(-1)[:shard_size]
    total_tokens = tokens.shape[0] * shards * over
    expert_load = sums[0, :E] * (E / (total_tokens * TOPK))
    grad_norm = jnp.sqrt(sums[0, E])
    clipped = grad_shard * (CLIP_LIMIT / jnp.maximum(grad_norm, CLIP_LIMIT))
    new_first = BETA_FIRST * first_moment + (1.0 - BETA_FIRST) * clipped
    new_second = BETA_SECOND * second_moment + (1.0 - BETA_SECOND) * clipped * clipped
    first_hat = new_first / (1.0 - BETA_FIRST**STEP)
    second_hat = new_second / (1.0 - BETA_SECOND**STEP)
    new_params = params * (1.0 - LEARN_RATE * DECAY_RATE) - LEARN_RATE * first_hat / (
        jnp.sqrt(second_hat) + ADAM_EPS
    )
    new_ema = EMA_KEEP * ema_weights + (1.0 - EMA_KEEP) * new_params
    return (
        output,
        input_grad,
        expert_load,
        grad_norm.reshape(1),
        new_params,
        new_first,
        new_second,
        new_ema,
        gain_grads,
    )


def solution(mesh):
    row = P(("dp", "fsdp"), None)
    flat = P(("dp", "fsdp"))
    return jax.shard_map(
        functools.partial(per_device, mesh.shape["dp"], mesh.shape["fsdp"]),
        mesh=mesh,
        in_specs=(row, row, row, row, flat, flat, flat, flat),
        out_specs=(row, row, P(), P(), flat, flat, flat, flat, P()),
        check_vma=False,
    )
```

```python
import copy
import functools
import itertools

import jax
import jax.numpy as jnp
from jax import lax
from jax.experimental import pallas as pl
from jax.experimental.pallas import tpu as pltpu
from jax.sharding import PartitionSpec as P

D = 512
E = 24
TOPK = 8
H = 64
FF = 2048
STEP = 10

NORM_EPS = 1e-06
CLIP_LIMIT = 1.0
BETA_FIRST = 0.9
BETA_SECOND = 0.95
LEARN_RATE = 0.1
DECAY_RATE = 0.1
ADAM_EPS = 1e-08
EMA_KEEP = 0.9
NEG_LARGE = -1e30

QW = E * H
KROW = QW
VROW = QW + H
RROW = QW + 2 * H
ALLW = 1696
LEN = 1024
TB = 512
NB = LEN // TB
QB = 128
SIDE = 4
MOST = 512 // QB + 1
SORT_STEPS = (
    (0, 1), (2, 3), (4, 5), (6, 7), (0, 2), (1, 3), (4, 6), (5, 7), (1, 2), (5, 6),
    (0, 4), (1, 5), (2, 6), (3, 7), (2, 4), (3, 5), (1, 2), (3, 4), (5, 6),
)
FC = 256
MB = 512
MIB = 1 << 20

WR_ROW = 8
WK_ROW = 104
WV_ROW = 360
WQ_ROW = 616
WO_ROW = 6760
W1_ROW = 12904
W2_ROW = 21096
ALL_ROWS = 29288
UNIT = 16 * 128
MESH = pl.DeviceIdType.MESH

F32 = jnp.float32
BF16 = jnp.bfloat16


def nn(a, b):
    return lax.dot_general(a, b, (((1,), (0,)), ((), ())), preferred_element_type=F32)


def nt(a, b):
    return lax.dot_general(a, b, (((1,), (1,)), ((), ())), preferred_element_type=F32)


def tn(a, b):
    return lax.dot_general(a, b, (((0,), (0,)), ((), ())), preferred_element_type=F32)


def rms_scale(values):
    return lax.rsqrt(jnp.mean(values * values, axis=-1, keepdims=True) + NORM_EPS)


def slot_of(routes, k, rows):
    return jnp.broadcast_to(routes[k : k + 1, :], (rows, routes.shape[1]))


def expert_rows(routes, k):
    return jnp.broadcast_to(routes.astype(jnp.int16)[k : k + 1, :], (16, routes.shape[1]))


def pick_heads(routes, source_ref, k):
    tokens = routes.shape[1]
    route = expert_rows(routes, k)
    taken = source_ref[k * H : (k + 1) * H, :].reshape(H // 16, 16, tokens)
    for e in range(k + 1, k + E - TOPK + 1):
        piece = source_ref[e * H : (e + 1) * H, :].reshape(H // 16, 16, tokens)
        taken = jnp.where((route == jnp.int16(e))[None], piece, taken)
    return taken.reshape(H, tokens)


def place_heads(routes, source_ref, target_ref):
    tokens = routes.shape[1]
    rows = [expert_rows(routes, k) for k in range(TOPK)]
    for e in range(E):
        total = jnp.zeros((H // 16, 16, tokens), BF16)
        for k in range(max(0, e - (E - TOPK)), min(TOPK - 1, e) + 1):
            piece = source_ref[k * H : (k + 1) * H, :].reshape(H // 16, 16, tokens)
            total = jnp.where((rows[k] == jnp.int16(e))[None], piece, total)
        target_ref[e * H : (e + 1) * H, :] = total.reshape(H, tokens)


def sorted_rows(rows):
    rows = list(rows)
    for one, two in SORT_STEPS:
        rows[one], rows[two] = jnp.minimum(rows[one], rows[two]), jnp.maximum(rows[one], rows[two])
    return rows


def key_mask(first_key, first_query, rows, start_row):
    keys = lax.broadcasted_iota(jnp.int32, (rows, QB), 0) + first_key
    queries = lax.broadcasted_iota(jnp.int32, (rows, QB), 1) + first_query
    mask = (keys <= queries) & (keys >= start_row)
    return jnp.concatenate([mask] * SIDE, axis=1)


def group_of(ref, k, lanes):
    return jnp.concatenate([ref[i * H : (i + 1) * H, lanes] for i in range(k, k + SIDE)], axis=1)


def row_group(ref, k, lanes):
    return jnp.concatenate([ref[i : i + 1, lanes] for i in range(k, k + SIDE)], axis=1)


def by_span(attend, row, place, segment_ref):
    def one(j, carry):
        block = place * (TB // QB) + j
        first = block * QB
        span = jnp.int32(1)
        for back in range(MOST - 1):
            last = first - back * QB - 1
            same = segment_ref[row, jnp.maximum(last, 0)] == segment_ref[row, first]
            span = span + jnp.where((last >= 0) & same, 1, 0)
        for blocks in range(1, MOST + 1):

            @pl.when(span == blocks)
            def _(blocks=blocks):
                attend(pl.ds(pl.multiple_of(j * QB, QB), QB), block, blocks)

        return carry

    lax.fori_loop(0, TB // QB, one, 0)


def head_forward_kernel(
    steps, segment_smem, x_ref, route_ref, segment_ref, wall_ref, gain_ref,
    q_ref, att_ref, gate_ref, lse_ref, kv_ref, kvt_ref, start_ref, sorted_ref, count_ref,
    all_scr, low_scr, k_scr, vt_scr, count_scr,
):
    step = pl.program_id(0)
    place = lax.rem(step, NB)
    here = pl.multiple_of(place * TB, TB)

    @pl.when(step == 0)
    def _():
        count_scr[...] = jnp.zeros_like(count_scr)

    row = segment_ref[pl.ds(lax.div(step, NB), 1), :]
    segments = segment_ref[pl.ds(lax.div(step, NB), 1), pl.ds(here, TB)]
    start = jnp.zeros((1, TB), jnp.int32)
    for number in range(1, 4):
        below = jnp.sum((row < number).astype(jnp.int32), axis=1, keepdims=True)
        start = jnp.where(segments == number, below, start)
    start_ref[...] = start
    x = x_ref[...].astype(F32)
    normed = (x * rms_scale(x) * gain_ref[...]).astype(BF16)
    all_scr[...] = nt(wall_ref[...], normed)
    kt = all_scr[KROW : KROW + H, :]
    vt = all_scr[VROW : VROW + H, :]
    logits = all_scr[RROW : RROW + E, :]
    kvt = jnp.concatenate([kt, vt], axis=0)
    kv = kvt.T.astype(BF16)
    kv_ref[...] = kv
    kvt_ref[...] = kvt.astype(BF16)
    k_scr[pl.ds(here, TB), :] = kv[:, :H]
    vt_scr[:, pl.ds(here, TB)] = vt.astype(BF16)
    routes = jnp.concatenate(sorted_rows(route_ref[k : k + 1, :] for k in range(TOPK)), axis=0)
    sorted_ref[...] = routes
    experts = lax.broadcasted_iota(jnp.int32, (E, TB), 0)
    chosen = []
    counts = count_scr[...]
    for k in range(TOPK):
        named = slot_of(routes, k, E) == experts
        chosen.append(jnp.sum(jnp.where(named, logits, 0.0), axis=0, keepdims=True))
        counts = counts + named.astype(F32)
    count_scr[...] = counts
    chosen = jnp.concatenate(chosen, axis=0)
    raised = jnp.exp(chosen - jnp.max(chosen, axis=0, keepdims=True))
    gate_ref[...] = raised / jnp.sum(raised, axis=0, keepdims=True)
    low_scr[...] = all_scr[0:QW, :].astype(BF16)
    for k in range(TOPK):
        q_ref[k * H : (k + 1) * H, :] = pick_heads(routes, low_scr, k) * jnp.asarray(H ** (-0.5), BF16)

    def attend(lanes, block, blocks):
        rows = blocks * QB
        first_key = pl.multiple_of((block - (blocks - 1)) * QB, QB)
        mask = key_mask(first_key, block * QB, rows, start_ref[:, lanes])
        keys = k_scr[pl.ds(first_key, rows), :]
        values = vt_scr[:, pl.ds(first_key, rows)]
        groups = [nn(keys, group_of(q_ref, 0, lanes))]
        for k in range(0, TOPK, SIDE):
            if k + SIDE < TOPK:
                groups.append(nn(keys, group_of(q_ref, k + SIDE, lanes)))
            scores = jnp.where(mask, groups[k // SIDE], NEG_LARGE)
            top = jnp.max(scores, axis=0, keepdims=True)
            raised = jnp.exp(scores - top)
            total = jnp.sum(raised, axis=0, keepdims=True)
            out = nn(values, (raised * (1.0 / total)).astype(BF16))
            lse = top + jnp.log(total)
            for side in range(SIDE):
                one = slice(side * QB, (side + 1) * QB)
                att_ref[(k + side) * H : (k + side + 1) * H, lanes] = out[:, one]
                lse_ref[k + side : k + side + 1, lanes] = lse[:, one]

    by_span(attend, lax.div(step, NB), place, segment_smem)

    @pl.when(step == steps - 1)
    def _():
        held = jnp.sum(count_scr[...], axis=1, keepdims=True)
        lane = lax.broadcasted_iota(jnp.int32, (E, 128), 1)
        row = lax.broadcasted_iota(jnp.int32, (E, 128), 0)
        count_ref[...] = jnp.sum(jnp.where(lane == row, held, 0.0), axis=0, keepdims=True)


def picks(rows, stride, first):
    at = lax.broadcasted_iota(jnp.int32, (rows, D), 1)
    row = lax.broadcasted_iota(jnp.int32, (rows, D), 0)
    return (at == row * stride + first).astype(F32)


def exact(product, a, b):
    return lax.dot_general(
        a, b, (product, ((), ())), precision=lax.Precision.HIGHEST, preferred_element_type=F32
    )


def gelu_parts(v):
    cdf = 0.5 + 0.5 * lax.erf(v * 0.7071067811865476)
    return cdf, jnp.exp(v * v * -0.5) * 0.3989422804014327


def middle_kernel(
    x_ref, dy_ref, gain_ref, wo_hbm, w1_hbm, w2_hbm, route_ref, gate_ref, att_ref,
    out_ref, dres_ref, datt_ref, delta_ref, dlogit_ref, flat_ref, extra_ref, dgain_ref,
    slot_scr, head_scr, mix_scr, hidden_scr, dpre_scr, dwo_ref, dw1_ref, dw2t_ref, rows_scr, low_scr, row_sem,
    wo_ref, w1_ref, w2_ref, weight_sem,
):
    step = pl.program_id(0)
    weights = [
        pltpu.make_async_copy(source, target, weight_sem.at[i])
        for i, (source, target) in enumerate(((wo_hbm, wo_ref), (w2_hbm, w2_ref), (w1_hbm, w1_ref)))
    ]

    @pl.when(step == 0)
    def _():
        for copy in weights:
            copy.start()
        dwo_ref[...] = jnp.zeros_like(dwo_ref)
        dw1_ref[...] = jnp.zeros_like(dw1_ref)
        dw2t_ref[...] = jnp.zeros_like(dw2t_ref)
        dgain_ref[...] = jnp.zeros_like(dgain_ref)

    routes = route_ref[...]
    tokens = routes.shape[1]
    gates = gate_ref[...]
    for k in range(TOPK):
        rows = slice(k * H, (k + 1) * H)
        slot_scr[rows, :] = (gates[k : k + 1, :] * att_ref[rows, :]).astype(BF16)
    place_heads(routes, slot_scr, mix_scr)
    x = x_ref[...].astype(F32)
    dy = dy_ref[...]
    mixed = mix_scr[...]

    @pl.when(step == 0)
    def _():
        for copy in weights:
            copy.wait()

    residual = x + tn(mixed, wo_ref[...])
    scale = rms_scale(residual)
    gain = gain_ref[...]
    second = (residual * scale * gain).astype(BF16)
    second_t = second.T
    dy_t = dy.T
    pre = [nn(second, w1_ref[:, 0:FC])]
    back = [nt(dy, w2_ref[0:FC, :])]
    for i in range(FF // FC):
        here = slice(i * FC, (i + 1) * FC)
        if i + 1 < FF // FC:
            after = slice((i + 1) * FC, (i + 2) * FC)
            pre.append(nn(second, w1_ref[:, after]))
            back.append(nt(dy, w2_ref[after, :]))
        cdf, density = gelu_parts(pre[i])
        hidden_scr[:, here] = (pre[i] * cdf).astype(BF16)
        dpre_scr[:, here] = (back[i] * (cdf + pre[i] * density)).astype(BF16)
    dsecond = nt(dpre_scr[...], w1_ref[...])
    out_ref[...] = (residual + nn(hidden_scr[...], w2_ref[...])).astype(BF16)
    dw1_ref[...] += nn(second_t, dpre_scr[...])
    dw2t_ref[...] += nn(dy_t, hidden_scr[...])
    dgain_ref[...] += jnp.sum(dsecond * residual * scale, axis=0, keepdims=True)
    weighted = gain * dsecond
    dres = (
        dy.astype(F32)
        + scale * weighted
        - residual * (scale * scale * scale) * jnp.mean(weighted * residual, axis=-1, keepdims=True)
    )
    dres_ref[...] = dres
    branch = dres.astype(BF16)
    dwo_ref[...] += nn(mixed, branch)
    head_scr[...] = nt(wo_ref[...], branch).astype(BF16)
    dgates = []
    for k in range(TOPK):
        rows = slice(k * H, (k + 1) * H)
        dslot = pick_heads(routes, head_scr, k).astype(F32)
        attended = att_ref[rows, :]
        dgates.append(jnp.sum(dslot * attended, axis=0, keepdims=True))
        datt = (gates[k : k + 1, :] * dslot).astype(BF16)
        datt_ref[rows, :] = datt
        delta_ref[k : k + 1, :] = jnp.sum(datt.astype(F32) * attended, axis=0, keepdims=True)
    dgate = jnp.concatenate(dgates, axis=0)
    dchosen = gates * (dgate - jnp.sum(gates * dgate, axis=0, keepdims=True))
    experts = lax.broadcasted_iota(jnp.int32, (E, tokens), 0)
    dlogits = jnp.zeros((E, tokens), F32)
    for k in range(TOPK):
        dlogits = jnp.where(
            slot_of(routes, k, E) == experts,
            jnp.broadcast_to(dchosen[k : k + 1, :], (E, tokens)),
            dlogits,
        )
    dlogit_ref[...] = dlogits

    @pl.when(step == pl.num_programs(0) - 1)
    def _():
        last = low_scr.shape[0]
        ends = (0, (W1_ROW - WO_ROW - 8) // 16 * 16, (W2_ROW - WO_ROW - 8) // 16 * 16, last)

        def out(number):
            first, count = ends[number], ends[number + 1] - ends[number]
            return pltpu.make_async_copy(
                low_scr.at[pl.ds(first, count), :],
                flat_ref.at[pl.ds(WO_ROW + 8 + first, count), :],
                row_sem.at[number],
            )

        def leave(number):
            first, count = ends[number], ends[number + 1] - ends[number]
            low_scr[pl.ds(first, count), :] = rows_scr[pl.ds(first + 8, count), :].astype(BF16)
            out(number).start()

        for c in range(D // 128):
            rows_scr[pl.ds(c, QW, stride=4), :] = dwo_ref[:, c * 128 : (c + 1) * 128]
        extra_ref[...] = rows_scr[0:8, :]
        leave(0)
        for c in range(FF // 128):
            rows_scr[pl.ds(W1_ROW - WO_ROW + c, D, stride=16), :] = dw1_ref[:, c * 128 : (c + 1) * 128]
        leave(1)
        for c in range(D // 128):
            rows_scr[pl.ds(W2_ROW - WO_ROW + c, FF, stride=4), :] = dw2t_ref[c * 128 : (c + 1) * 128, :].T
        leave(2)
        for number in range(3):
            out(number).wait()


def head_backward_kernel(
    segment_smem, x_ref, gain_ref, wall_ref, route_ref, start_ref, q_ref, datt_ref,
    lse_ref, delta_ref, kv_ref, kvt_ref, dlogit_ref, dres_ref, dgain_two_ref, extra_ref, flat_in,
    dx_ref, flat_ref,
    dk_scr, dv_scr, dq_scr, dall_scr, prob_scr, dscore_scr, dwall_ref, dgain_ref, rows_scr, low_scr, row_sem,
):
    step = pl.program_id(0)
    place = NB - 1 - lax.rem(step, NB)
    here = pl.multiple_of(place * TB, TB)

    @pl.when(step == 0)
    def _():
        dwall_ref[...] = jnp.zeros_like(dwall_ref)
        dgain_ref[...] = jnp.zeros_like(dgain_ref)

    @pl.when(lax.rem(step, NB) == 0)
    def _():
        dk_scr[...] = jnp.zeros_like(dk_scr)
        dv_scr[...] = jnp.zeros_like(dv_scr)

    def attend(lanes, block, blocks):
        rows = blocks * QB
        first_key = pl.multiple_of((block - (blocks - 1)) * QB, QB)
        mask = key_mask(first_key, block * QB, rows, start_ref[:, lanes])
        keys = kv_ref[pl.ds(first_key, rows), :H]
        values = kv_ref[pl.ds(first_key, rows), H:]
        keys_t = kvt_ref[:H, pl.ds(first_key, rows)]
        queries = [group_of(q_ref, k, lanes) for k in range(0, TOPK, SIDE)]
        datts = [group_of(datt_ref, k, lanes) for k in range(0, TOPK, SIDE)]
        scores = [nn(keys, queries[0])]
        dprobs = [nn(values, datts[0])]
        for i in range(TOPK // SIDE):
            if i + 1 < TOPK // SIDE:
                scores.append(nn(keys, queries[i + 1]))
                dprobs.append(nn(values, datts[i + 1]))
            k = i * SIDE
            wide = slice(k * QB, (k + SIDE) * QB)
            probs = jnp.exp(jnp.where(mask, scores[i], NEG_LARGE) - row_group(lse_ref, k, lanes))
            dscore = (probs * (dprobs[i] - row_group(delta_ref, k, lanes))).astype(BF16)
            prob_scr[0:rows, wide] = probs.astype(BF16)
            dscore_scr[0:rows, wide] = dscore
            dq = (nn(keys_t, dscore) * (H ** (-0.5))).astype(BF16)
            for side in range(SIDE):
                dq_scr[(k + side) * H : (k + side + 1) * H, lanes] = dq[:, side * QB : (side + 1) * QB]
        dv_scr[pl.ds(first_key, rows), :] += nt(prob_scr[0:rows, :], jnp.concatenate(datts, axis=1))
        dk_scr[pl.ds(first_key, rows), :] += nt(dscore_scr[0:rows, :], jnp.concatenate(queries, axis=1))

    by_span(attend, lax.div(step, NB), place, segment_smem)
    place_heads(route_ref[...], dq_scr, dall_scr)
    dkv = jnp.concatenate([dk_scr[pl.ds(here, TB), :], dv_scr[pl.ds(here, TB), :]], axis=1)
    dall_scr[KROW : KROW + 2 * H, :] = dkv.T.astype(BF16)
    dall_scr[RROW : RROW + 32, :] = jnp.concatenate(
        [dlogit_ref[...], jnp.zeros((32 - E, TB), F32)], axis=0
    ).astype(BF16)
    x = x_ref[...].astype(F32)
    scale = rms_scale(x)
    gain = gain_ref[...]
    normed = (x * scale * gain).astype(BF16)
    dall = dall_scr[...]
    dwall_ref[...] += nn(dall, normed)
    dnormed = tn(dall, wall_ref[...])
    dgain_ref[...] += jnp.sum(dnormed * x * scale, axis=0, keepdims=True)
    weighted = gain * dnormed
    dx_ref[...] = (
        dres_ref[...]
        + scale * weighted
        - x * (scale * scale * scale) * jnp.mean(weighted * x, axis=-1, keepdims=True)
    )

    @pl.when(step == pl.num_programs(0) - 1)
    def _():
        for c in range(D // 128):
            lanes = slice(c * 128, (c + 1) * 128)
            rows_scr[c : c + 1, :] = dgain_ref[:, lanes]
            rows_scr[4 + c : 5 + c, :] = dgain_two_ref[:, lanes]
        router_t = dwall_ref[RROW : RROW + E, :]
        across = jnp.concatenate(
            [exact(((1,), (1,)), router_t, picks(32, 16, b)) for b in range(16)], axis=0
        ).T
        for j in range(3):
            rows_scr[pl.ds(WR_ROW + j, 32, stride=3), :] = across[:, j * 128 : (j + 1) * 128]
        for first, row in ((KROW, WK_ROW), (VROW, WV_ROW)):
            part = dwall_ref[first : first + H, :]
            rows_scr[row : row + 256, :] = jnp.concatenate(
                [exact(((1,), (1,)), picks(256, 2, b), part) for b in range(2)], axis=1
            )
        for c in range(QW // 128):
            rows_scr[pl.ds(WQ_ROW + c, D, stride=12), :] = dwall_ref[c * 128 : (c + 1) * 128, :].T
        rows_scr[WO_ROW : WO_ROW + 8, :] = extra_ref[...]
        low_scr[...] = rows_scr[...].astype(BF16)
        copy = pltpu.make_async_copy(low_scr, flat_ref.at[pl.ds(0, WO_ROW + 8), :], row_sem.at[0])
        copy.start()
        copy.wait()


def whole(shape):
    return pl.BlockSpec(shape, lambda *_: (0,) * len(shape), pipeline_mode=pl.Buffered(1))


def kept(shape):
    return pl.BlockSpec(shape, lambda *_: (0,) * len(shape))


SMEM = pl.BlockSpec(memory_space=pltpu.SMEM)
HBM = pl.BlockSpec(memory_space=pl.ANY)


def struct(shape, kind=F32):
    return jax.ShapeDtypeStruct(shape, kind)


def params_for(mib):
    return pltpu.CompilerParams(vmem_limit_bytes=mib * MIB)


def head_forward(tokens, routes_t, segments, wall, gain):
    count = tokens.shape[0]
    steps = count // TB
    across = lambda rows: pl.BlockSpec((rows, TB), lambda b: (0, b))
    down = lambda columns: pl.BlockSpec((TB, columns), lambda b: (b, 0))
    return pl.pallas_call(
        functools.partial(head_forward_kernel, steps),
        grid=(steps,),
        in_specs=[SMEM, down(D), across(TOPK), whole(segments.shape), whole((ALLW, D)), whole((1, D))],
        out_specs=[
            across(TOPK * H), across(TOPK * H), across(TOPK), across(TOPK), down(2 * H), across(2 * H),
            across(1), across(TOPK), whole((1, 128)),
        ],
        scratch_shapes=[
            pltpu.VMEM((ALLW, TB), F32),
            pltpu.VMEM((QW, TB), BF16),
            pltpu.VMEM((LEN, H), BF16),
            pltpu.VMEM((H, LEN), BF16),
            pltpu.VMEM((E, TB), F32),
        ],
        out_shape=[
            struct((TOPK * H, count), BF16),
            struct((TOPK * H, count)),
            struct((TOPK, count)),
            struct((TOPK, count)),
            struct((count, 2 * H), BF16),
            struct((2 * H, count), BF16),
            struct((1, count), jnp.int32),
            struct((TOPK, count), jnp.int32),
            struct((1, 128)),
        ],
        compiler_params=params_for(56),
        name="head_forward",
        cost_estimate=pl.CostEstimate(flops=10_000_000_000, bytes_accessed=16_000_000, transcendentals=0),
    )(segments, tokens, routes_t, segments, wall, gain)


def middle(flat_rows, tokens, grad_out, gain, wo, w1, w2, routes_t, gates, attended):
    count = tokens.shape[0]
    steps = count // MB
    across = lambda rows: pl.BlockSpec((rows, MB), lambda b: (0, b))
    down = lambda columns: pl.BlockSpec((MB, columns), lambda b: (b, 0))
    return pl.pallas_call(
        middle_kernel,
        grid=(steps,),
        in_specs=[
            down(D), down(D), whole((1, D)), HBM, HBM, HBM, across(TOPK), across(TOPK), across(TOPK * H),
        ],
        out_specs=[
            down(D), down(D), across(TOPK * H), across(TOPK), across(E),
            pl.BlockSpec(memory_space=pl.ANY), whole((8, 128)), whole((1, D)),
        ],
        out_shape=[
            struct((count, D), BF16),
            struct((count, D)),
            struct((TOPK * H, count), BF16),
            struct((TOPK, count)),
            struct((E, count)),
            struct((flat_rows, 128), BF16),
            struct((8, 128)),
            struct((1, D)),
        ],
        scratch_shapes=[
            pltpu.VMEM((TOPK * H, MB), BF16),
            pltpu.VMEM((QW, MB), BF16),
            pltpu.VMEM((QW, MB), BF16),
            pltpu.VMEM((MB, FF), BF16),
            pltpu.VMEM((MB, FF), BF16),
            pltpu.VMEM((QW, D), F32),
            pltpu.VMEM((D, FF), F32),
            pltpu.VMEM((D, FF), F32),
            pltpu.VMEM((flat_rows - WO_ROW, 128), F32),
            pltpu.VMEM((flat_rows - WO_ROW - 8, 128), BF16),
            pltpu.SemaphoreType.DMA((3,)),
            pltpu.VMEM((QW, D), BF16),
            pltpu.VMEM((D, FF), BF16),
            pltpu.VMEM((FF, D), BF16),
            pltpu.SemaphoreType.DMA((3,)),
        ],
        compiler_params=params_for(60),
        name="middle",
    )(tokens, grad_out, gain, wo, w1, w2, routes_t, gates, attended)


def head_backward(
    segments, tokens, gain, wall, routes_t, start, queries, datt, lse, delta, kv, kvt, dlogits, dres,
    dgain_two, extra, flat,
):
    count = tokens.shape[0]
    steps = count // TB

    def place(b):
        return (b // NB) * NB + NB - 1 - b % NB

    across = lambda rows: pl.BlockSpec((rows, TB), lambda b: (0, place(b)))
    down = lambda columns: pl.BlockSpec((TB, columns), lambda b: (place(b), 0))
    return pl.pallas_call(
        head_backward_kernel,
        grid=(steps,),
        in_specs=[
            SMEM, down(D), whole((1, D)), whole((ALLW, D)), across(TOPK), across(1),
            across(TOPK * H), across(TOPK * H), across(TOPK), across(TOPK),
            pl.BlockSpec((LEN, 2 * H), lambda b: (b // NB, 0)),
            pl.BlockSpec((2 * H, LEN), lambda b: (0, b // NB)),
            across(E), down(D), whole((1, D)), whole((8, 128)), pl.BlockSpec(memory_space=pl.ANY),
        ],
        out_specs=[down(D), pl.BlockSpec(memory_space=pl.ANY)],
        scratch_shapes=[
            pltpu.VMEM((LEN, H), F32),
            pltpu.VMEM((LEN, H), F32),
            pltpu.VMEM((TOPK * H, TB), BF16),
            pltpu.VMEM((ALLW, TB), BF16),
            pltpu.VMEM((MOST * QB, TOPK * QB), BF16),
            pltpu.VMEM((MOST * QB, TOPK * QB), BF16),
            pltpu.VMEM((ALLW, D), F32),
            pltpu.VMEM((1, D), F32),
            pltpu.VMEM((WO_ROW + 8, 128), F32),
            pltpu.VMEM((WO_ROW + 8, 128), BF16),
            pltpu.SemaphoreType.DMA((1,)),
        ],
        out_shape=[struct((count, D)), struct(flat.shape, BF16)],
        input_output_aliases={16: 1},
        compiler_params=params_for(56),
        name="head_backward",
        cost_estimate=pl.CostEstimate(flops=30_000_000_000, bytes_accessed=24_000_000, transcendentals=0),
    )(
        segments, tokens, gain, wall, routes_t, start, queries, datt, lse, delta, kv, kvt, dlogits, dres,
        dgain_two, extra, flat,
    )


class Mesh3:
    def __init__(self, shards, over):
        shard = lax.axis_index("dp")
        other = lax.axis_index("fsdp")
        self.over = over
        self.many = shards * over
        self.sizes = {"x": 2, "y": shards // 2, "z": over // 2}
        self.here = {"x": lax.rem(other, 2), "y": lax.div(shard, 2), "z": lax.div(other, 2)}
        self.core = lax.rem(shard, 2)
        self.me = shard * over + other
        self.partner = (shard + 1 - 2 * self.core, other)

    def at_z(self, z):
        same = copy.copy(self)
        if z is not None:
            same.here = dict(self.here, z=z)
        return same

    def spots(self):
        x, y, z = (self.sizes[axis] for axis in "xyz")
        return list(itertools.product(range(x), range(y), range(1 - z, z)))

    def round_spots(self):
        return list(itertools.product(*[range(self.sizes[axis]) for axis in "xyz"]))

    def exists(self, z_steps):
        place = self.here["z"] + z_steps
        if isinstance(place, int):
            return 0 <= place < self.sizes["z"]
        return (place >= 0) & (place < self.sizes["z"])

    def device(self, core, spot):
        size = self.sizes["z"]
        x = lax.rem(self.here["x"] + spot[0], self.sizes["x"])
        y = lax.rem(self.here["y"] + spot[1], self.sizes["y"])
        z = self.here["z"] + spot[2]
        z = z % size if isinstance(z, int) else lax.rem(z + size, size)
        return (y * 2 + core, z * 2 + x)

    def number(self, core, spot):
        shard, other = self.device(core, spot)
        return shard * self.over + other

    def greet(self, devices):
        barrier = pltpu.get_barrier_semaphore()
        for device in devices:
            pl.semaphore_signal(barrier, inc=1, device_id=device, device_id_type=MESH)
        pl.semaphore_wait(barrier, len(devices))

    def near(self):
        steps = [at(axis, step) for axis in "xyz" for step in range(1, self.sizes[axis])]
        return [self.device(self.core, step) for step in steps] + [self.partner]

    def column(self):
        steps = [(core, step) for core in range(2) for step in range(self.sizes["z"]) if core or step]
        return [self.device(lax.rem(self.core + core, 2), (0, 0, step)) for core, step in steps]

    def layer(self):
        steps = [(x, y, 0) for x in range(self.sizes["x"]) for y in range(self.sizes["y"]) if x or y]
        return [self.device(self.core, step) for step in steps]


def at(axis, step):
    return tuple(step if one == axis else 0 for one in "xyz")


def last_axis(axes, spot):
    return max([i for i, axis in enumerate(axes) if spot["xyz".index(axis)]], default=-1)


def pieces_of(window, count=2):
    if window < 512:
        return [(0, window)]
    ends = [window // 16 * i // count * 16 for i in range(count)] + [window]
    return [(first, last - first) for first, last in zip(ends, ends[1:])]


def act(condition, action):
    if condition is True:
        action()
    elif condition is not False:
        pl.when(condition)(action)


GATHER_AXES = (("zxy", "yzx"), ("zyx", "xzy"))
REDUCE_PIECES = 3
REDUCE_AXES = ("zxy", "zyx")


def onward(mesh, axes, spot):
    last = last_axis(axes, spot)
    steps = []
    if last >= 0 and axes[last] == "z":
        steps.append(("z", -1 if spot[2] > 0 else 1))
    for axis in axes[last + 1 :]:
        steps += [("z", 1), ("z", -1)] if axis == "z" else [
            (axis, one) for one in range(1, mesh.sizes[axis])
        ]
    return steps


def gather_own_core(mesh, core, land, send_sem, recv_sem, begin):
    window = land.shape[1]
    pieces = pieces_of(window)
    slots = {}
    events = []

    def moved(owner, device, slot, p):
        rows = pl.ds(*pieces[p])
        return pltpu.make_async_remote_copy(
            src_ref=land.at[owner, rows],
            dst_ref=land.at[owner, rows],
            send_sem=send_sem.at[slot, p],
            recv_sem=recv_sem.at[owner, p],
            device_id=device,
            device_id_type=MESH,
        )

    for spot in mesh.spots():
        there = mesh.exists(spot[2])
        if there is False:
            continue
        owner = mesh.number(core, spot)
        turn = 0.5 * abs(spot[2]) + (spot[0] > 0) + (spot[1] > 0) + (0.001 if spot[2] < 0 else 0)
        for p in range(len(pieces)):
            sends = []
            for axis, step in onward(mesh, GATHER_AXES[core][p], spot):
                key = (spot[0], spot[1], spot[2] % mesh.sizes["z"], axis, step)
                away = mesh.exists(step) if axis == "z" else True
                if away is not False:
                    slot = slots.setdefault(key, len(slots))
                    sends.append((mesh.device(core, at(axis, step)), slot, away))
            key = (spot[0], spot[1], spot[2] % mesh.sizes["z"])
            sends.append((mesh.partner, slots.setdefault(key, len(slots)), True))

            def come(owner=owner, spot=spot, p=p, sends=sends):
                if any(spot):
                    moved(owner, mesh.partner, 0, p).wait_recv()
                for device, slot, away in sends:
                    act(away, moved(owner, device, slot, p).start)

            def done(owner=owner, p=p, sends=sends):
                for _, slot, away in sends:
                    act(away, moved(owner, mesh.partner, slot, p).wait_send)

            events.append((turn + 0.01 * p, there, come if begin else done))
    for _, there, action in sorted(events, key=lambda one: one[0]):
        act(there, action)


def gather_blocks(mesh, land, send_sem, recv_sem, begin):
    known = range(mesh.sizes["z"]) if mesh.sizes["z"] <= 4 else [None]
    for core in range(2):
        for z in known:

            @pl.when((mesh.core == core) & (True if z is None else mesh.here["z"] == z))
            def _(core=core, z=z):
                gather_own_core(mesh.at_z(z), core, land, send_sem, recv_sem, begin)


def each_owner(mesh, core, action):
    def one(number, carry):
        shard = 2 * lax.div(number, mesh.over) + core
        action(shard * mesh.over + lax.rem(number, mesh.over))
        return carry

    lax.fori_loop(0, mesh.many // 2, one, 0)


def reduce_blocks(mesh, core, source, mine, outgo, income, send_sem, recv_sem, total_ref, closing):
    pieces = pieces_of(outgo.shape[1], REDUCE_PIECES)
    half = mesh.many // 2
    held = {spot: i for i, spot in enumerate(mesh.round_spots())}

    def across(kind, spot, p):
        slot = held[spot]
        return pltpu.make_async_remote_copy(
            src_ref=source(mesh.number(kind, spot), *pieces[p]),
            dst_ref=income.at[slot, pl.ds(*pieces[p])],
            send_sem=send_sem.at[slot, p],
            recv_sem=recv_sem.at[slot, p],
            device_id=mesh.partner,
            device_id_type=MESH,
        )

    def moved(spot, p, device):
        rows = pl.ds(*pieces[p])
        slot = half + held[spot]
        return pltpu.make_async_remote_copy(
            src_ref=outgo.at[held[spot], rows],
            dst_ref=income.at[slot, rows],
            send_sem=send_sem.at[slot, p],
            recv_sem=recv_sem.at[slot, p],
            device_id=device,
            device_id_type=MESH,
        )

    def far(spot):
        z = {0: 0, 1: 3, 2: 5, 3: 8}.get(spot[2], 2 * spot[2] + 2)
        return z + 2 * (spot[0] > 0) + 2 * (spot[1] > 0)

    axes = REDUCE_AXES[core]

    def hand(spot, p):
        across(1 - core, spot, p).start()

    def pass_on(spot, p):
        rows = pl.ds(*pieces[p])
        across(core, spot, p).wait_recv()
        total = mine(mesh.number(core, spot), *pieces[p]) + income[held[spot], rows].astype(F32)
        last = last_axis(axes, spot)
        for axis in axes[last + 1 :]:
            size = mesh.sizes[axis]
            for step in range(1, size):
                child = tuple(one or other for one, other in zip(spot, at(axis, size - step)))
                moved(child, p, mesh.partner).wait_recv()
                total = total + income[half + held[child], rows].astype(F32)
        if last < 0:
            total_ref[rows, :] = total
        else:
            outgo[held[spot], rows] = total.astype(BF16)
            step = spot["xyz".index(axes[last])]
            moved(spot, p, mesh.device(core, at(axes[last], step))).start()

    every = list(itertools.product(held, range(len(pieces))))
    events = [(-2 * far(spot) - 4 + 0.01 * p, 0, hand, spot, p) for spot, p in every]
    events += [(-2 * far(spot) + 2 * p / len(pieces), 1, pass_on, spot, p) for spot, p in every]
    for _, _, action, spot, p in sorted(events, key=lambda one: one[:2]):
        if not closing:
            action(spot, p)
    for spot, p in every if closing else ():
        across(1 - core, spot, p).wait_send()
        if any(spot):
            moved(spot, p, mesh.partner).wait_send()


def sum_all(mesh, mine, stats, send_sem, recv_sem, meanwhile):
    column = mesh.sizes["z"] * 2
    layer = mesh.sizes["x"] * mesh.sizes["y"]
    groups = (
        (0, column, mesh.here["z"] * 2 + mesh.core, mesh.column()),
        (column, layer, mesh.here["x"] * mesh.sizes["y"] + mesh.here["y"], mesh.layer()),
    )
    total = mine
    for base, size, here, devices in groups:
        stats[base + here] = total

        def sent(j, device, base=base, here=here):
            return pltpu.make_async_remote_copy(
                src_ref=stats.at[base + here],
                dst_ref=stats.at[base + here],
                send_sem=send_sem.at[base + j],
                recv_sem=recv_sem.at[base + here],
                device_id=device,
                device_id_type=MESH,
            )

        def come(place, base=base):
            return pltpu.make_async_remote_copy(
                src_ref=stats.at[base + place],
                dst_ref=stats.at[base + place],
                send_sem=send_sem.at[base],
                recv_sem=recv_sem.at[base + place],
                device_id=mesh.partner,
                device_id_type=MESH,
            )

        for j, device in enumerate(devices):
            sent(j, device).start()
        if not base:
            meanwhile()
        for j in range(1, size):
            come(lax.rem(here + j, size)).wait_recv()
        for j, device in enumerate(devices):
            sent(j, device).wait_send()
        total = stats[base]
        for place in range(1, size):
            total = total + stats[base + place]
    return total


def window_rows(shard_size, many):
    units = [(shard_size * d) // UNIT for d in range(many + 1)]
    return 16 * (max(b - a for a, b in zip(units, units[1:])) + 1)


def first_row(shard_size, number):
    if isinstance(number, int):
        return number * shard_size // UNIT * 16
    return pl.multiple_of(lax.div(number * shard_size, UNIT) * 16, 16)


def inner_units(shard_size, many):
    units = [(shard_size * d) // UNIT for d in range(many + 1)]
    return min(b - a for a, b in zip(units, units[1:]))


def lay_inner(shard_size, many, land, flat, owner):
    count = 16 * inner_units(shard_size, many) - 16
    row = pl.multiple_of(first_row(shard_size, owner) + 16, 16)
    flat[pl.ds(row, count), :] = land[owner, pl.ds(16, count), :].astype(F32)


def lay_edges(shard_size, many, land, flat):
    inner = 16 * inner_units(shard_size, many)
    flat[0:16, :] = jnp.zeros((16, 128), F32)

    def lay(number, carry):
        row = first_row(shard_size, number)
        after = first_row(shard_size, number + 1)
        flat[pl.ds(row, 16), :] += land[number, 0:16, :].astype(F32)
        tail = land[number, pl.ds(inner, 16), :].astype(F32)
        flat[pl.ds(pl.multiple_of(row + inner, 16), 16), :] = tail
        last = pl.multiple_of(after - row, 16)
        flat[pl.ds(after, 16), :] = land[number, pl.ds(last, 16), :].astype(F32)
        return carry

    lax.fori_loop(0, many, lay, 0)


def early_matrices(flat, wall_ref, gain_one_ref, gain_two_ref):
    for c in range(D // 128):
        lanes = slice(c * 128, (c + 1) * 128)
        gain_one_ref[:, lanes] = flat[c : c + 1, :]
        gain_two_ref[:, lanes] = flat[4 + c : 5 + c, :]
    for c in range(QW // 128):
        wall_ref[c * 128 : (c + 1) * 128, :] = flat[pl.ds(WQ_ROW + c, D, stride=12), :].T.astype(BF16)
    for first, row in ((KROW, WK_ROW), (VROW, WV_ROW)):
        pair = flat[row : row + 256, :].T.astype(BF16)
        wall_ref[first : first + H, :] = (
            nn(pair[:H], picks(256, 2, 0).astype(BF16)) + nn(pair[H:], picks(256, 2, 1).astype(BF16))
        ).astype(BF16)
    across = jnp.concatenate(
        [flat[pl.ds(WR_ROW + j, 32, stride=3), :] for j in range(3)], axis=1
    ).T.astype(BF16)
    router_t = jnp.zeros((E, D), F32)
    for part in range(16):
        router_t = router_t + nn(across[part * E : (part + 1) * E, :], picks(32, 16, part).astype(BF16))
    wall_ref[RROW:ALLW, :] = jnp.concatenate(
        [router_t, jnp.zeros((ALLW - RROW - E, D), F32)], axis=0
    ).astype(BF16)


def gather_kernel(
    mesh, shard_size, own_ref,
    wall_out, gain_one_ref, gain_two_ref, wo_out, w1_out, w2_out,
    land, flat, wall_ref, wo_ref, w1_ref, w2_ref, send_sem, recv_sem, out_sem,
):
    mesh = mesh()
    many = mesh.many
    window = land.shape[1]
    begin = mesh.me * shard_size - lax.div(mesh.me * shard_size, UNIT) * UNIT
    row, lane = lax.div(begin, 128), lax.rem(begin, 128)
    flat[0 : window + 48, :] = jnp.zeros((window + 48, 128), F32)
    flat[24 : 24 + own_ref.shape[0], :] = own_ref[...]
    first = pltpu.roll(flat[pl.ds(24 - row, window), :], lane, 1)
    second = pltpu.roll(flat[pl.ds(23 - row, window), :], lane, 1)
    at_lane = lax.broadcasted_iota(jnp.int32, (window, 128), 1)
    land[mesh.me] = jnp.where(at_lane >= lane, first, second).astype(BF16)
    mesh.greet(mesh.near())
    gather_blocks(mesh, land, send_sem, recv_sem, True)
    each_owner(mesh, mesh.core, functools.partial(lay_inner, shard_size, many, land, flat))

    def arrive(owner):
        for p in range(recv_sem.shape[1]):
            rows = pl.ds(*pieces_of(window)[p])
            pltpu.make_async_remote_copy(
                src_ref=land.at[owner, rows],
                dst_ref=land.at[owner, rows],
                send_sem=send_sem.at[0, p],
                recv_sem=recv_sem.at[owner, p],
                device_id=mesh.partner,
                device_id_type=MESH,
            ).wait_recv()
        lay_inner(shard_size, many, land, flat, owner)

    each_owner(mesh, 1 - mesh.core, arrive)
    lay_edges(shard_size, many, land, flat)
    copies = []

    def leave(matrix, out):
        one = pltpu.make_async_copy(matrix, out, out_sem.at[len(copies)])
        one.start()
        copies.append(one)

    for c in range(D // 128):
        wo_ref[:, c * 128 : (c + 1) * 128] = flat[pl.ds(WO_ROW + c, QW, stride=4), :].astype(BF16)
    leave(wo_ref, wo_out)
    for c in range(D // 128):
        w2_ref[:, c * 128 : (c + 1) * 128] = flat[pl.ds(W2_ROW + c, FF, stride=4), :].astype(BF16)
    leave(w2_ref, w2_out)
    for c in range(FF // 128):
        w1_ref[:, c * 128 : (c + 1) * 128] = flat[pl.ds(W1_ROW + c, D, stride=16), :].astype(BF16)
    leave(w1_ref, w1_out)
    early_matrices(flat, wall_ref, gain_one_ref, gain_two_ref)
    leave(wall_ref, wall_out)
    gather_blocks(mesh, land, send_sem, recv_sem, False)
    for one in copies:
        one.wait()


def gather_weights(shards, over, shard_size, window, own):
    many = shards * over
    rows = (shard_size * (many - 1)) // UNIT * 16 + window
    vmem = pl.BlockSpec(memory_space=pltpu.VMEM)
    hbm = pl.BlockSpec(memory_space=pl.ANY)
    mesh = functools.partial(Mesh3, shards, over)
    pieces = len(pieces_of(window))
    return pl.pallas_call(
        functools.partial(gather_kernel, mesh, shard_size),
        in_specs=[vmem],
        out_specs=[hbm, vmem, vmem, hbm, hbm, hbm],
        out_shape=[
            struct((ALLW, D), BF16),
            struct((1, D)),
            struct((1, D)),
            struct((QW, D), BF16),
            struct((D, FF), BF16),
            struct((FF, D), BF16),
        ],
        scratch_shapes=[
            pltpu.VMEM((many, window, 128), BF16),
            pltpu.VMEM((rows, 128), F32),
            pltpu.VMEM((ALLW, D), BF16),
            pltpu.VMEM((QW, D), BF16),
            pltpu.VMEM((D, FF), BF16),
            pltpu.VMEM((FF, D), BF16),
            pltpu.SemaphoreType.DMA((5 * many // 2, pieces)),
            pltpu.SemaphoreType.DMA((many, pieces)),
            pltpu.SemaphoreType.DMA((4,)),
        ],
        compiler_params=pltpu.CompilerParams(
            collective_id=0, has_side_effects=True, vmem_limit_bytes=60 * MIB
        ),
        name="gather_weights",
    )(own)


def reduce_kernel(
    mesh, shard_size, flat_ref, count_ref,
    out_ref, total_ref, gain_ref,
    part, outgo, income, whole_scr, stats, part_sem, send_sem, recv_sem, stat_send, stat_recv,
):
    mesh = mesh()
    window = outgo.shape[1]
    span = part.shape[1]

    def source(owner, first, rows):
        row = pl.multiple_of(first_row(shard_size, owner) + first, 16)
        return flat_ref.at[pl.ds(row, rows), :]

    def fetch(y):
        first = first_row(shard_size, (2 * y + mesh.core) * mesh.over)
        return pltpu.make_async_copy(flat_ref.at[pl.ds(first, span), :], part.at[y], part_sem.at[y])

    def mine(owner, first, rows):
        shard = lax.div(owner, mesh.over)
        row = first_row(shard_size, owner) - first_row(shard_size, shard * mesh.over) + first
        return part[lax.div(shard, 2), pl.ds(pl.multiple_of(row, 16), rows), :].astype(F32)

    for y in range(mesh.sizes["y"]):
        fetch(y).start()
    mesh.greet(mesh.column() + mesh.layer())
    for y in range(mesh.sizes["y"]):
        fetch(y).wait()
    buffers = (source, mine, outgo, income, send_sem, recv_sem, whole_scr)

    def reduce_all(closing):
        for core in range(2):
            pl.when(mesh.core == core)(
                functools.partial(reduce_blocks, mesh, core, *buffers, closing=closing)
            )

    reduce_all(False)

    begin = mesh.me * shard_size - lax.div(mesh.me * shard_size, UNIT) * UNIT
    rows = out_ref.shape[0]
    row, lane = lax.div(begin, 128), lax.rem(begin, 128)
    back = lax.rem(128 - lane, 128)
    first = pltpu.roll(whole_scr[pl.ds(row, rows), :], back, 1)
    second = pltpu.roll(whole_scr[pl.ds(row + 1, rows), :], back, 1)
    at_lane = lax.broadcasted_iota(jnp.int32, (rows, 128), 1)
    place = lax.broadcasted_iota(jnp.int32, (rows, 128), 0) * 128 + at_lane
    total = jnp.where(at_lane < 128 - lane, first, second)
    out_ref[...] = total
    inside = jnp.where(place < shard_size, total, 0.0)
    squares = jnp.sum(jnp.sum(inside * inside, axis=0, keepdims=True), axis=1, keepdims=True)
    lane = lax.broadcasted_iota(jnp.int32, (8, 128), 1)
    row = jnp.where(lane == E, squares, count_ref[...])
    gains = jnp.where(mesh.me == 0, total[0:8, :], 0.0)
    summed = sum_all(
        mesh, jnp.concatenate([row, gains], axis=0), stats, stat_send, stat_recv,
        lambda: reduce_all(True),
    )
    total_ref[...] = summed[0:1, :]
    for c in range(D // 128):
        lanes = slice(c * 128, (c + 1) * 128)
        gain_ref[0:1, lanes] = summed[8 + c : 9 + c, :]
        gain_ref[1:2, lanes] = summed[12 + c : 13 + c, :]


def reduce_grads(shards, over, shard_size, window, flat, counts):
    vmem = pl.BlockSpec(memory_space=pltpu.VMEM)
    many = shards * over
    mesh = functools.partial(Mesh3, shards, over)
    pieces = len(pieces_of(window, REDUCE_PIECES))
    steps = over + shards
    units = [(shard_size * d) // UNIT for d in range(many)]
    span = 16 * max(units[d + over - 1] - units[d] for d in range(0, many, over)) + window
    return pl.pallas_call(
        functools.partial(reduce_kernel, mesh, shard_size),
        in_specs=[pl.BlockSpec(memory_space=pl.ANY), vmem],
        out_specs=[vmem] * 3,
        out_shape=[struct((-(-shard_size // 128), 128)), struct((1, 128)), struct((2, D))],
        scratch_shapes=[
            pltpu.VMEM((shards // 2, span, 128), BF16),
            pltpu.VMEM((many // 2, window, 128), BF16),
            pltpu.VMEM((many, window, 128), BF16),
            pltpu.VMEM((window + 16, 128), F32),
            pltpu.VMEM((steps, 16, 128), F32),
            pltpu.SemaphoreType.DMA((shards // 2,)),
            pltpu.SemaphoreType.DMA((many, pieces)),
            pltpu.SemaphoreType.DMA((many, pieces)),
            pltpu.SemaphoreType.DMA((steps,)),
            pltpu.SemaphoreType.DMA((steps,)),
        ],
        compiler_params=pltpu.CompilerParams(
            collective_id=1, has_side_effects=True, vmem_limit_bytes=56 * MIB
        ),
        name="reduce_grads",
    )(flat, counts)


def local_step(flat_rows, tokens, grad_out, routes, segments, weights):
    wall, gain_one, gain_two, wo, w1, w2 = weights
    queries, attended, gates, lse, kv, kvt, start, routes_t, counts = head_forward(
        tokens, routes.T, segments, wall, gain_one
    )
    output, dres, datt, delta, dlogits, flat, extra, dgain_two = middle(
        flat_rows, tokens, grad_out, gain_two, wo, w1, w2, routes_t, gates, attended
    )
    input_grad, flat = head_backward(
        segments, tokens, gain_one, wall, routes_t, start, queries, datt, lse, delta, kv, kvt, dlogits, dres,
        dgain_two, extra, flat,
    )
    return output, input_grad, flat, counts


def per_device(
    shards, over, tokens, grad_out, routes, segments, params, first_moment, second_moment, ema_weights
):
    shard_size = params.shape[0]
    window = window_rows(shard_size, shards * over)
    flat_rows = (shard_size * (shards * over - 1)) // UNIT * 16 + window + 16
    own_rows = -(-shard_size // 1024) * 8
    own = jnp.pad(params, (0, own_rows * 128 - shard_size)).reshape(own_rows, 128)
    wall, gain_one, gain_two, wo, w1, w2 = gather_weights(shards, over, shard_size, window, own)
    output, input_grad, flat, counts = local_step(
        flat_rows, tokens, grad_out, routes, segments, (wall, gain_one, gain_two, wo, w1, w2)
    )
    reduced, sums, gain_grads = reduce_grads(shards, over, shard_size, window, flat, counts)
    grad_shard = reduced.reshape(-1)[:shard_size]
    total_tokens = tokens.shape[0] * shards * over
    expert_load = sums[0, :E] * (E / (total_tokens * TOPK))
    grad_norm = jnp.sqrt(sums[0, E])
    clipped = grad_shard * (CLIP_LIMIT / jnp.maximum(grad_norm, CLIP_LIMIT))
    new_first = BETA_FIRST * first_moment + (1.0 - BETA_FIRST) * clipped
    new_second = BETA_SECOND * second_moment + (1.0 - BETA_SECOND) * clipped * clipped
    first_hat = new_first / (1.0 - BETA_FIRST**STEP)
    second_hat = new_second / (1.0 - BETA_SECOND**STEP)
    new_params = params * (1.0 - LEARN_RATE * DECAY_RATE) - LEARN_RATE * first_hat / (
        jnp.sqrt(second_hat) + ADAM_EPS
    )
    new_ema = EMA_KEEP * ema_weights + (1.0 - EMA_KEEP) * new_params
    return (
        output,
        input_grad,
        expert_load,
        grad_norm.reshape(1),
        new_params,
        new_first,
        new_second,
        new_ema,
        gain_grads,
    )


def solution(mesh):
    row = P(("dp", "fsdp"), None)
    flat = P(("dp", "fsdp"))
    return jax.shard_map(
        functools.partial(per_device, mesh.shape["dp"], mesh.shape["fsdp"]),
        mesh=mesh,
        in_specs=(row, row, row, row, flat, flat, flat, flat),
        out_specs=(row, row, P(), P(), flat, flat, flat, flat, P()),
        check_vma=False,
    )
```

```python
import copy
import functools
import itertools

import jax
import jax.numpy as jnp
from jax import lax
from jax.experimental import pallas as pl
from jax.experimental.pallas import tpu as pltpu
from jax.sharding import PartitionSpec as P

D = 512
E = 24
TOPK = 8
H = 64
FF = 2048
STEP = 10

NORM_EPS = 1e-06
CLIP_LIMIT = 1.0
BETA_FIRST = 0.9
BETA_SECOND = 0.95
LEARN_RATE = 0.1
DECAY_RATE = 0.1
ADAM_EPS = 1e-08
EMA_KEEP = 0.9
NEG_LARGE = -1e30

QW = E * H
KROW = QW
VROW = QW + H
RROW = QW + 2 * H
ALLW = 1696
LEN = 1024
TB = 512
NB = LEN // TB
QB = 128
SIDE = 4
MOST = 512 // QB + 1
SORT_STEPS = (
    (0, 1), (2, 3), (4, 5), (6, 7), (0, 2), (1, 3), (4, 6), (5, 7), (1, 2), (5, 6),
    (0, 4), (1, 5), (2, 6), (3, 7), (2, 4), (3, 5), (1, 2), (3, 4), (5, 6),
)
FC = 256
MB = 512
MIB = 1 << 20

WR_ROW = 8
WK_ROW = 104
WV_ROW = 360
WQ_ROW = 616
WO_ROW = 6760
W1_ROW = 12904
W2_ROW = 21096
ALL_ROWS = 29288
UNIT = 16 * 128
MESH = pl.DeviceIdType.MESH

F32 = jnp.float32
BF16 = jnp.bfloat16


def nn(a, b):
    return lax.dot_general(a, b, (((1,), (0,)), ((), ())), preferred_element_type=F32)


def nt(a, b):
    return lax.dot_general(a, b, (((1,), (1,)), ((), ())), preferred_element_type=F32)


def tn(a, b):
    return lax.dot_general(a, b, (((0,), (0,)), ((), ())), preferred_element_type=F32)


def rms_scale(values):
    return lax.rsqrt(jnp.mean(values * values, axis=-1, keepdims=True) + NORM_EPS)


def slot_of(routes, k, rows):
    return jnp.broadcast_to(routes[k : k + 1, :], (rows, routes.shape[1]))


def expert_rows(routes, k):
    return jnp.broadcast_to(routes.astype(jnp.int16)[k : k + 1, :], (16, routes.shape[1]))


def pick_heads(routes, source_ref, k):
    tokens = routes.shape[1]
    route = expert_rows(routes, k)
    taken = source_ref[k * H : (k + 1) * H, :].reshape(H // 16, 16, tokens)
    for e in range(k + 1, k + E - TOPK + 1):
        piece = source_ref[e * H : (e + 1) * H, :].reshape(H // 16, 16, tokens)
        taken = jnp.where((route == jnp.int16(e))[None], piece, taken)
    return taken.reshape(H, tokens)


def place_heads(routes, source_ref, target_ref):
    tokens = routes.shape[1]
    rows = [expert_rows(routes, k) for k in range(TOPK)]
    for e in range(E):
        total = jnp.zeros((H // 16, 16, tokens), BF16)
        for k in range(max(0, e - (E - TOPK)), min(TOPK - 1, e) + 1):
            piece = source_ref[k * H : (k + 1) * H, :].reshape(H // 16, 16, tokens)
            total = jnp.where((rows[k] == jnp.int16(e))[None], piece, total)
        target_ref[e * H : (e + 1) * H, :] = total.reshape(H, tokens)


def sorted_rows(rows):
    rows = list(rows)
    for one, two in SORT_STEPS:
        rows[one], rows[two] = jnp.minimum(rows[one], rows[two]), jnp.maximum(rows[one], rows[two])
    return rows


def key_mask(first_key, first_query, rows, start_row):
    keys = lax.broadcasted_iota(jnp.int32, (rows, QB), 0) + first_key
    queries = lax.broadcasted_iota(jnp.int32, (rows, QB), 1) + first_query
    mask = (keys <= queries) & (keys >= start_row)
    return jnp.concatenate([mask] * SIDE, axis=1)


def group_of(ref, k, lanes):
    return jnp.concatenate([ref[i * H : (i + 1) * H, lanes] for i in range(k, k + SIDE)], axis=1)


def row_group(ref, k, lanes):
    return jnp.concatenate([ref[i : i + 1, lanes] for i in range(k, k + SIDE)], axis=1)


def by_span(attend, row, place, segment_ref):
    def one(j, carry):
        block = place * (TB // QB) + j
        first = block * QB
        span = jnp.int32(1)
        for back in range(MOST - 1):
            last = first - back * QB - 1
            same = segment_ref[row, jnp.maximum(last, 0)] == segment_ref[row, first]
            span = span + jnp.where((last >= 0) & same, 1, 0)
        for blocks in range(1, MOST + 1):

            @pl.when(span == blocks)
            def _(blocks=blocks):
                attend(pl.ds(pl.multiple_of(j * QB, QB), QB), block, blocks)

        return carry

    lax.fori_loop(0, TB // QB, one, 0)


def head_forward_kernel(
    steps, segment_smem, x_ref, route_ref, segment_ref, wall_ref, gain_ref,
    q_ref, att_ref, gate_ref, lse_ref, kv_ref, kvt_ref, start_ref, sorted_ref, count_ref,
    all_scr, low_scr, k_scr, vt_scr, count_scr,
):
    step = pl.program_id(0)
    place = lax.rem(step, NB)
    here = pl.multiple_of(place * TB, TB)

    @pl.when(step == 0)
    def _():
        count_scr[...] = jnp.zeros_like(count_scr)

    row = segment_ref[pl.ds(lax.div(step, NB), 1), :]
    segments = segment_ref[pl.ds(lax.div(step, NB), 1), pl.ds(here, TB)]
    start = jnp.zeros((1, TB), jnp.int32)
    for number in range(1, 4):
        below = jnp.sum((row < number).astype(jnp.int32), axis=1, keepdims=True)
        start = jnp.where(segments == number, below, start)
    start_ref[...] = start
    x = x_ref[...].astype(F32)
    normed = (x * rms_scale(x) * gain_ref[...]).astype(BF16)
    all_scr[...] = nt(wall_ref[...], normed)
    kt = all_scr[KROW : KROW + H, :]
    vt = all_scr[VROW : VROW + H, :]
    logits = all_scr[RROW : RROW + E, :]
    kvt = jnp.concatenate([kt, vt], axis=0)
    kv = kvt.T.astype(BF16)
    kv_ref[...] = kv
    kvt_ref[...] = kvt.astype(BF16)
    k_scr[pl.ds(here, TB), :] = kv[:, :H]
    vt_scr[:, pl.ds(here, TB)] = vt.astype(BF16)
    routes = jnp.concatenate(sorted_rows(route_ref[k : k + 1, :] for k in range(TOPK)), axis=0)
    sorted_ref[...] = routes
    experts = lax.broadcasted_iota(jnp.int32, (E, TB), 0)
    chosen = []
    counts = count_scr[...]
    for k in range(TOPK):
        named = slot_of(routes, k, E) == experts
        chosen.append(jnp.sum(jnp.where(named, logits, 0.0), axis=0, keepdims=True))
        counts = counts + named.astype(F32)
    count_scr[...] = counts
    chosen = jnp.concatenate(chosen, axis=0)
    raised = jnp.exp(chosen - jnp.max(chosen, axis=0, keepdims=True))
    gate_ref[...] = raised / jnp.sum(raised, axis=0, keepdims=True)
    low_scr[...] = all_scr[0:QW, :].astype(BF16)
    for k in range(TOPK):
        q_ref[k * H : (k + 1) * H, :] = pick_heads(routes, low_scr, k) * jnp.asarray(H ** (-0.5), BF16)

    def attend(lanes, block, blocks):
        rows = blocks * QB
        first_key = pl.multiple_of((block - (blocks - 1)) * QB, QB)
        mask = key_mask(first_key, block * QB, rows, start_ref[:, lanes])
        keys = k_scr[pl.ds(first_key, rows), :]
        values = vt_scr[:, pl.ds(first_key, rows)]
        groups = [nn(keys, group_of(q_ref, 0, lanes))]
        for k in range(0, TOPK, SIDE):
            if k + SIDE < TOPK:
                groups.append(nn(keys, group_of(q_ref, k + SIDE, lanes)))
            scores = jnp.where(mask, groups[k // SIDE], NEG_LARGE)
            top = jnp.max(scores, axis=0, keepdims=True)
            raised = jnp.exp(scores - top)
            total = jnp.sum(raised, axis=0, keepdims=True)
            out = nn(values, (raised * (1.0 / total)).astype(BF16))
            lse = top + jnp.log(total)
            for side in range(SIDE):
                one = slice(side * QB, (side + 1) * QB)
                att_ref[(k + side) * H : (k + side + 1) * H, lanes] = out[:, one]
                lse_ref[k + side : k + side + 1, lanes] = lse[:, one]

    by_span(attend, lax.div(step, NB), place, segment_smem)

    @pl.when(step == steps - 1)
    def _():
        held = jnp.sum(count_scr[...], axis=1, keepdims=True)
        lane = lax.broadcasted_iota(jnp.int32, (E, 128), 1)
        row = lax.broadcasted_iota(jnp.int32, (E, 128), 0)
        count_ref[...] = jnp.sum(jnp.where(lane == row, held, 0.0), axis=0, keepdims=True)


def picks(rows, stride, first):
    at = lax.broadcasted_iota(jnp.int32, (rows, D), 1)
    row = lax.broadcasted_iota(jnp.int32, (rows, D), 0)
    return (at == row * stride + first).astype(F32)


def exact(product, a, b):
    return lax.dot_general(
        a, b, (product, ((), ())), precision=lax.Precision.HIGHEST, preferred_element_type=F32
    )


def gelu_parts(v):
    cdf = 0.5 + 0.5 * lax.erf(v * 0.7071067811865476)
    return cdf, jnp.exp(v * v * -0.5) * 0.3989422804014327


def middle_kernel(
    x_ref, dy_ref, gain_ref, wo_ref, w1_ref, w2_ref, route_ref, gate_ref, att_ref,
    out_ref, dres_ref, datt_ref, delta_ref, dlogit_ref, flat_ref, extra_ref, dgain_ref,
    slot_scr, head_scr, mix_scr, hidden_scr, dpre_scr, dwo_ref, dw1_ref, dw2t_ref, rows_scr, low_scr, row_sem,
):
    step = pl.program_id(0)

    @pl.when(step == 0)
    def _():
        dwo_ref[...] = jnp.zeros_like(dwo_ref)
        dw1_ref[...] = jnp.zeros_like(dw1_ref)
        dw2t_ref[...] = jnp.zeros_like(dw2t_ref)
        dgain_ref[...] = jnp.zeros_like(dgain_ref)

    routes = route_ref[...]
    tokens = routes.shape[1]
    gates = gate_ref[...]
    for k in range(TOPK):
        rows = slice(k * H, (k + 1) * H)
        slot_scr[rows, :] = (gates[k : k + 1, :] * att_ref[rows, :]).astype(BF16)
    place_heads(routes, slot_scr, mix_scr)
    x = x_ref[...].astype(F32)
    dy = dy_ref[...]
    mixed = mix_scr[...]
    residual = x + tn(mixed, wo_ref[...])
    scale = rms_scale(residual)
    gain = gain_ref[...]
    second = (residual * scale * gain).astype(BF16)
    second_t = second.T
    dy_t = dy.T
    pre = [nn(second, w1_ref[:, 0:FC])]
    back = [nt(dy, w2_ref[0:FC, :])]
    for i in range(FF // FC):
        here = slice(i * FC, (i + 1) * FC)
        if i + 1 < FF // FC:
            after = slice((i + 1) * FC, (i + 2) * FC)
            pre.append(nn(second, w1_ref[:, after]))
            back.append(nt(dy, w2_ref[after, :]))
        cdf, density = gelu_parts(pre[i])
        hidden_scr[:, here] = (pre[i] * cdf).astype(BF16)
        dpre_scr[:, here] = (back[i] * (cdf + pre[i] * density)).astype(BF16)
    dsecond = nt(dpre_scr[...], w1_ref[...])
    out_ref[...] = (residual + nn(hidden_scr[...], w2_ref[...])).astype(BF16)
    dw1_ref[...] += nn(second_t, dpre_scr[...])
    dw2t_ref[...] += nn(dy_t, hidden_scr[...])
    dgain_ref[...] += jnp.sum(dsecond * residual * scale, axis=0, keepdims=True)
    weighted = gain * dsecond
    dres = (
        dy.astype(F32)
        + scale * weighted
        - residual * (scale * scale * scale) * jnp.mean(weighted * residual, axis=-1, keepdims=True)
    )
    dres_ref[...] = dres
    branch = dres.astype(BF16)
    dwo_ref[...] += nn(mixed, branch)
    head_scr[...] = nt(wo_ref[...], branch).astype(BF16)
    dgates = []
    for k in range(TOPK):
        rows = slice(k * H, (k + 1) * H)
        dslot = pick_heads(routes, head_scr, k).astype(F32)
        attended = att_ref[rows, :]
        dgates.append(jnp.sum(dslot * attended, axis=0, keepdims=True))
        datt = (gates[k : k + 1, :] * dslot).astype(BF16)
        datt_ref[rows, :] = datt
        delta_ref[k : k + 1, :] = jnp.sum(datt.astype(F32) * attended, axis=0, keepdims=True)
    dgate = jnp.concatenate(dgates, axis=0)
    dchosen = gates * (dgate - jnp.sum(gates * dgate, axis=0, keepdims=True))
    experts = lax.broadcasted_iota(jnp.int32, (E, tokens), 0)
    dlogits = jnp.zeros((E, tokens), F32)
    for k in range(TOPK):
        dlogits = jnp.where(
            slot_of(routes, k, E) == experts,
            jnp.broadcast_to(dchosen[k : k + 1, :], (E, tokens)),
            dlogits,
        )
    dlogit_ref[...] = dlogits

    @pl.when(step == pl.num_programs(0) - 1)
    def _():
        last = low_scr.shape[0]
        ends = (0, (W1_ROW - WO_ROW - 8) // 16 * 16, (W2_ROW - WO_ROW - 8) // 16 * 16, last)

        def out(number):
            first, count = ends[number], ends[number + 1] - ends[number]
            return pltpu.make_async_copy(
                low_scr.at[pl.ds(first, count), :],
                flat_ref.at[pl.ds(WO_ROW + 8 + first, count), :],
                row_sem.at[number],
            )

        def leave(number):
            first, count = ends[number], ends[number + 1] - ends[number]
            low_scr[pl.ds(first, count), :] = rows_scr[pl.ds(first + 8, count), :].astype(BF16)
            out(number).start()

        for c in range(D // 128):
            rows_scr[pl.ds(c, QW, stride=4), :] = dwo_ref[:, c * 128 : (c + 1) * 128]
        extra_ref[...] = rows_scr[0:8, :]
        leave(0)
        for c in range(FF // 128):
            rows_scr[pl.ds(W1_ROW - WO_ROW + c, D, stride=16), :] = dw1_ref[:, c * 128 : (c + 1) * 128]
        leave(1)
        for c in range(D // 128):
            rows_scr[pl.ds(W2_ROW - WO_ROW + c, FF, stride=4), :] = dw2t_ref[c * 128 : (c + 1) * 128, :].T
        leave(2)
        for number in range(3):
            out(number).wait()


def head_backward_kernel(
    segment_smem, x_ref, gain_ref, wall_ref, route_ref, start_ref, q_ref, datt_ref,
    lse_ref, delta_ref, kv_ref, kvt_ref, dlogit_ref, dres_ref, dgain_two_ref, extra_ref, flat_in,
    dx_ref, flat_ref,
    dk_scr, dv_scr, dq_scr, dall_scr, prob_scr, dscore_scr, dwall_ref, dgain_ref, rows_scr, low_scr, row_sem,
):
    step = pl.program_id(0)
    place = NB - 1 - lax.rem(step, NB)
    here = pl.multiple_of(place * TB, TB)

    @pl.when(step == 0)
    def _():
        dwall_ref[...] = jnp.zeros_like(dwall_ref)
        dgain_ref[...] = jnp.zeros_like(dgain_ref)

    @pl.when(lax.rem(step, NB) == 0)
    def _():
        dk_scr[...] = jnp.zeros_like(dk_scr)
        dv_scr[...] = jnp.zeros_like(dv_scr)

    def attend(lanes, block, blocks):
        rows = blocks * QB
        first_key = pl.multiple_of((block - (blocks - 1)) * QB, QB)
        mask = key_mask(first_key, block * QB, rows, start_ref[:, lanes])
        keys = kv_ref[pl.ds(first_key, rows), :H]
        values = kv_ref[pl.ds(first_key, rows), H:]
        keys_t = kvt_ref[:H, pl.ds(first_key, rows)]
        queries = [group_of(q_ref, k, lanes) for k in range(0, TOPK, SIDE)]
        datts = [group_of(datt_ref, k, lanes) for k in range(0, TOPK, SIDE)]
        scores = [nn(keys, queries[0])]
        dprobs = [nn(values, datts[0])]
        for i in range(TOPK // SIDE):
            if i + 1 < TOPK // SIDE:
                scores.append(nn(keys, queries[i + 1]))
                dprobs.append(nn(values, datts[i + 1]))
            k = i * SIDE
            wide = slice(k * QB, (k + SIDE) * QB)
            probs = jnp.exp(jnp.where(mask, scores[i], NEG_LARGE) - row_group(lse_ref, k, lanes))
            dscore = (probs * (dprobs[i] - row_group(delta_ref, k, lanes))).astype(BF16)
            prob_scr[0:rows, wide] = probs.astype(BF16)
            dscore_scr[0:rows, wide] = dscore
            dq = (nn(keys_t, dscore) * (H ** (-0.5))).astype(BF16)
            for side in range(SIDE):
                dq_scr[(k + side) * H : (k + side + 1) * H, lanes] = dq[:, side * QB : (side + 1) * QB]
        dv_scr[pl.ds(first_key, rows), :] += nt(prob_scr[0:rows, :], jnp.concatenate(datts, axis=1))
        dk_scr[pl.ds(first_key, rows), :] += nt(dscore_scr[0:rows, :], jnp.concatenate(queries, axis=1))

    by_span(attend, lax.div(step, NB), place, segment_smem)
    place_heads(route_ref[...], dq_scr, dall_scr)
    dkv = jnp.concatenate([dk_scr[pl.ds(here, TB), :], dv_scr[pl.ds(here, TB), :]], axis=1)
    dall_scr[KROW : KROW + 2 * H, :] = dkv.T.astype(BF16)
    dall_scr[RROW : RROW + 32, :] = jnp.concatenate(
        [dlogit_ref[...], jnp.zeros((32 - E, TB), F32)], axis=0
    ).astype(BF16)
    x = x_ref[...].astype(F32)
    scale = rms_scale(x)
    gain = gain_ref[...]
    normed = (x * scale * gain).astype(BF16)
    dall = dall_scr[...]
    dwall_ref[...] += nn(dall, normed)
    dnormed = tn(dall, wall_ref[...])
    dgain_ref[...] += jnp.sum(dnormed * x * scale, axis=0, keepdims=True)
    weighted = gain * dnormed
    dx_ref[...] = (
        dres_ref[...]
        + scale * weighted
        - x * (scale * scale * scale) * jnp.mean(weighted * x, axis=-1, keepdims=True)
    )

    @pl.when(step == pl.num_programs(0) - 1)
    def _():
        for c in range(D // 128):
            lanes = slice(c * 128, (c + 1) * 128)
            rows_scr[c : c + 1, :] = dgain_ref[:, lanes]
            rows_scr[4 + c : 5 + c, :] = dgain_two_ref[:, lanes]
        router_t = dwall_ref[RROW : RROW + E, :]
        across = jnp.concatenate(
            [exact(((1,), (1,)), router_t, picks(32, 16, b)) for b in range(16)], axis=0
        ).T
        for j in range(3):
            rows_scr[pl.ds(WR_ROW + j, 32, stride=3), :] = across[:, j * 128 : (j + 1) * 128]
        for first, row in ((KROW, WK_ROW), (VROW, WV_ROW)):
            part = dwall_ref[first : first + H, :]
            rows_scr[row : row + 256, :] = jnp.concatenate(
                [exact(((1,), (1,)), picks(256, 2, b), part) for b in range(2)], axis=1
            )
        for c in range(QW // 128):
            rows_scr[pl.ds(WQ_ROW + c, D, stride=12), :] = dwall_ref[c * 128 : (c + 1) * 128, :].T
        rows_scr[WO_ROW : WO_ROW + 8, :] = extra_ref[...]
        low_scr[...] = rows_scr[...].astype(BF16)
        copy = pltpu.make_async_copy(low_scr, flat_ref.at[pl.ds(0, WO_ROW + 8), :], row_sem.at[0])
        copy.start()
        copy.wait()


def whole(shape):
    return pl.BlockSpec(shape, lambda *_: (0,) * len(shape), pipeline_mode=pl.Buffered(1))


def kept(shape):
    return pl.BlockSpec(shape, lambda *_: (0,) * len(shape))


SMEM = pl.BlockSpec(memory_space=pltpu.SMEM)


def struct(shape, kind=F32):
    return jax.ShapeDtypeStruct(shape, kind)


def params_for(mib):
    return pltpu.CompilerParams(vmem_limit_bytes=mib * MIB)


def head_forward(tokens, routes_t, segments, wall, gain):
    count = tokens.shape[0]
    steps = count // TB
    across = lambda rows: pl.BlockSpec((rows, TB), lambda b: (0, b))
    down = lambda columns: pl.BlockSpec((TB, columns), lambda b: (b, 0))
    return pl.pallas_call(
        functools.partial(head_forward_kernel, steps),
        grid=(steps,),
        in_specs=[SMEM, down(D), across(TOPK), whole(segments.shape), whole((ALLW, D)), whole((1, D))],
        out_specs=[
            across(TOPK * H), across(TOPK * H), across(TOPK), across(TOPK), down(2 * H), across(2 * H),
            across(1), across(TOPK), whole((1, 128)),
        ],
        scratch_shapes=[
            pltpu.VMEM((ALLW, TB), F32),
            pltpu.VMEM((QW, TB), BF16),
            pltpu.VMEM((LEN, H), BF16),
            pltpu.VMEM((H, LEN), BF16),
            pltpu.VMEM((E, TB), F32),
        ],
        out_shape=[
            struct((TOPK * H, count), BF16),
            struct((TOPK * H, count)),
            struct((TOPK, count)),
            struct((TOPK, count)),
            struct((count, 2 * H), BF16),
            struct((2 * H, count), BF16),
            struct((1, count), jnp.int32),
            struct((TOPK, count), jnp.int32),
            struct((1, 128)),
        ],
        compiler_params=params_for(56),
        name="head_forward",
        cost_estimate=pl.CostEstimate(flops=10_000_000_000, bytes_accessed=16_000_000, transcendentals=0),
    )(segments, tokens, routes_t, segments, wall, gain)


def middle(flat_rows, tokens, grad_out, gain, wo, w1, w2, routes_t, gates, attended):
    count = tokens.shape[0]
    steps = count // MB
    across = lambda rows: pl.BlockSpec((rows, MB), lambda b: (0, b))
    down = lambda columns: pl.BlockSpec((MB, columns), lambda b: (b, 0))
    return pl.pallas_call(
        middle_kernel,
        grid=(steps,),
        in_specs=[
            down(D), down(D), whole((1, D)), whole((QW, D)), whole((D, FF)), whole((FF, D)),
            across(TOPK), across(TOPK), across(TOPK * H),
        ],
        out_specs=[
            down(D), down(D), across(TOPK * H), across(TOPK), across(E),
            pl.BlockSpec(memory_space=pl.ANY), whole((8, 128)), whole((1, D)),
        ],
        out_shape=[
            struct((count, D), BF16),
            struct((count, D)),
            struct((TOPK * H, count), BF16),
            struct((TOPK, count)),
            struct((E, count)),
            struct((flat_rows, 128), BF16),
            struct((8, 128)),
            struct((1, D)),
        ],
        scratch_shapes=[
            pltpu.VMEM((TOPK * H, MB), BF16),
            pltpu.VMEM((QW, MB), BF16),
            pltpu.VMEM((QW, MB), BF16),
            pltpu.VMEM((MB, FF), BF16),
            pltpu.VMEM((MB, FF), BF16),
            pltpu.VMEM((QW, D), F32),
            pltpu.VMEM((D, FF), F32),
            pltpu.VMEM((D, FF), F32),
            pltpu.VMEM((flat_rows - WO_ROW, 128), F32),
            pltpu.VMEM((flat_rows - WO_ROW - 8, 128), BF16),
            pltpu.SemaphoreType.DMA((3,)),
        ],
        compiler_params=params_for(60),
        name="middle",
    )(tokens, grad_out, gain, wo, w1, w2, routes_t, gates, attended)


def head_backward(
    segments, tokens, gain, wall, routes_t, start, queries, datt, lse, delta, kv, kvt, dlogits, dres,
    dgain_two, extra, flat,
):
    count = tokens.shape[0]
    steps = count // TB

    def place(b):
        return (b // NB) * NB + NB - 1 - b % NB

    across = lambda rows: pl.BlockSpec((rows, TB), lambda b: (0, place(b)))
    down = lambda columns: pl.BlockSpec((TB, columns), lambda b: (place(b), 0))
    return pl.pallas_call(
        head_backward_kernel,
        grid=(steps,),
        in_specs=[
            SMEM, down(D), whole((1, D)), whole((ALLW, D)), across(TOPK), across(1),
            across(TOPK * H), across(TOPK * H), across(TOPK), across(TOPK),
            pl.BlockSpec((LEN, 2 * H), lambda b: (b // NB, 0)),
            pl.BlockSpec((2 * H, LEN), lambda b: (0, b // NB)),
            across(E), down(D), whole((1, D)), whole((8, 128)), pl.BlockSpec(memory_space=pl.ANY),
        ],
        out_specs=[down(D), pl.BlockSpec(memory_space=pl.ANY)],
        scratch_shapes=[
            pltpu.VMEM((LEN, H), F32),
            pltpu.VMEM((LEN, H), F32),
            pltpu.VMEM((TOPK * H, TB), BF16),
            pltpu.VMEM((ALLW, TB), BF16),
            pltpu.VMEM((MOST * QB, TOPK * QB), BF16),
            pltpu.VMEM((MOST * QB, TOPK * QB), BF16),
            pltpu.VMEM((ALLW, D), F32),
            pltpu.VMEM((1, D), F32),
            pltpu.VMEM((WO_ROW + 8, 128), F32),
            pltpu.VMEM((WO_ROW + 8, 128), BF16),
            pltpu.SemaphoreType.DMA((1,)),
        ],
        out_shape=[struct((count, D)), struct(flat.shape, BF16)],
        input_output_aliases={16: 1},
        compiler_params=params_for(56),
        name="head_backward",
        cost_estimate=pl.CostEstimate(flops=30_000_000_000, bytes_accessed=24_000_000, transcendentals=0),
    )(
        segments, tokens, gain, wall, routes_t, start, queries, datt, lse, delta, kv, kvt, dlogits, dres,
        dgain_two, extra, flat,
    )


class Mesh3:
    def __init__(self, shards, over):
        shard = lax.axis_index("dp")
        other = lax.axis_index("fsdp")
        self.over = over
        self.many = shards * over
        self.sizes = {"x": 2, "y": shards // 2, "z": over // 2}
        self.here = {"x": lax.rem(other, 2), "y": lax.div(shard, 2), "z": lax.div(other, 2)}
        self.core = lax.rem(shard, 2)
        self.me = shard * over + other
        self.partner = (shard + 1 - 2 * self.core, other)

    def at_z(self, z):
        same = copy.copy(self)
        if z is not None:
            same.here = dict(self.here, z=z)
        return same

    def spots(self):
        x, y, z = (self.sizes[axis] for axis in "xyz")
        return list(itertools.product(range(x), range(y), range(1 - z, z)))

    def round_spots(self):
        return list(itertools.product(*[range(self.sizes[axis]) for axis in "xyz"]))

    def exists(self, z_steps):
        place = self.here["z"] + z_steps
        if isinstance(place, int):
            return 0 <= place < self.sizes["z"]
        return (place >= 0) & (place < self.sizes["z"])

    def device(self, core, spot):
        size = self.sizes["z"]
        x = lax.rem(self.here["x"] + spot[0], self.sizes["x"])
        y = lax.rem(self.here["y"] + spot[1], self.sizes["y"])
        z = self.here["z"] + spot[2]
        z = z % size if isinstance(z, int) else lax.rem(z + size, size)
        return (y * 2 + core, z * 2 + x)

    def number(self, core, spot):
        shard, other = self.device(core, spot)
        return shard * self.over + other

    def greet(self, devices):
        barrier = pltpu.get_barrier_semaphore()
        for device in devices:
            pl.semaphore_signal(barrier, inc=1, device_id=device, device_id_type=MESH)
        pl.semaphore_wait(barrier, len(devices))

    def near(self):
        steps = [at(axis, step) for axis in "xyz" for step in range(1, self.sizes[axis])]
        return [self.device(self.core, step) for step in steps] + [self.partner]

    def column(self):
        steps = [(core, step) for core in range(2) for step in range(self.sizes["z"]) if core or step]
        return [self.device(lax.rem(self.core + core, 2), (0, 0, step)) for core, step in steps]

    def layer(self):
        steps = [(x, y, 0) for x in range(self.sizes["x"]) for y in range(self.sizes["y"]) if x or y]
        return [self.device(self.core, step) for step in steps]


def at(axis, step):
    return tuple(step if one == axis else 0 for one in "xyz")


def last_axis(axes, spot):
    return max([i for i, axis in enumerate(axes) if spot["xyz".index(axis)]], default=-1)


def pieces_of(window, count=2):
    if window < 512:
        return [(0, window)]
    ends = [window // 16 * i // count * 16 for i in range(count)] + [window]
    return [(first, last - first) for first, last in zip(ends, ends[1:])]


def act(condition, action):
    if condition is True:
        action()
    elif condition is not False:
        pl.when(condition)(action)


GATHER_AXES = (("zxy", "yzx"), ("zyx", "xzy"))
REDUCE_PIECES = 2
REDUCE_AXES = ("zxy", "zyx")


def onward(mesh, axes, spot):
    last = last_axis(axes, spot)
    steps = []
    if last >= 0 and axes[last] == "z":
        steps.append(("z", -1 if spot[2] > 0 else 1))
    for axis in axes[last + 1 :]:
        steps += [("z", 1), ("z", -1)] if axis == "z" else [
            (axis, one) for one in range(1, mesh.sizes[axis])
        ]
    return steps


def gather_own_core(mesh, core, land, send_sem, recv_sem, begin):
    window = land.shape[1]
    pieces = pieces_of(window)
    slots = {}
    events = []

    def moved(owner, device, slot, p):
        rows = pl.ds(*pieces[p])
        return pltpu.make_async_remote_copy(
            src_ref=land.at[owner, rows],
            dst_ref=land.at[owner, rows],
            send_sem=send_sem.at[slot, p],
            recv_sem=recv_sem.at[owner, p],
            device_id=device,
            device_id_type=MESH,
        )

    for spot in mesh.spots():
        there = mesh.exists(spot[2])
        if there is False:
            continue
        owner = mesh.number(core, spot)
        turn = 0.5 * abs(spot[2]) + (spot[0] > 0) + (spot[1] > 0) + (0.001 if spot[2] < 0 else 0)
        for p in range(len(pieces)):
            sends = []
            for axis, step in onward(mesh, GATHER_AXES[core][p], spot):
                key = (spot[0], spot[1], spot[2] % mesh.sizes["z"], axis, step)
                away = mesh.exists(step) if axis == "z" else True
                if away is not False:
                    slot = slots.setdefault(key, len(slots))
                    sends.append((mesh.device(core, at(axis, step)), slot, away))
            key = (spot[0], spot[1], spot[2] % mesh.sizes["z"])
            sends.append((mesh.partner, slots.setdefault(key, len(slots)), True))

            def come(owner=owner, spot=spot, p=p, sends=sends):
                if any(spot):
                    moved(owner, mesh.partner, 0, p).wait_recv()
                for device, slot, away in sends:
                    act(away, moved(owner, device, slot, p).start)

            def done(owner=owner, p=p, sends=sends):
                for _, slot, away in sends:
                    act(away, moved(owner, mesh.partner, slot, p).wait_send)

            events.append((turn + 0.01 * p, there, come if begin else done))
    for _, there, action in sorted(events, key=lambda one: one[0]):
        act(there, action)


def gather_blocks(mesh, land, send_sem, recv_sem, begin):
    known = range(mesh.sizes["z"]) if mesh.sizes["z"] <= 4 else [None]
    for core in range(2):
        for z in known:

            @pl.when((mesh.core == core) & (True if z is None else mesh.here["z"] == z))
            def _(core=core, z=z):
                gather_own_core(mesh.at_z(z), core, land, send_sem, recv_sem, begin)


def each_owner(mesh, core, action):
    def one(number, carry):
        shard = 2 * lax.div(number, mesh.over) + core
        action(shard * mesh.over + lax.rem(number, mesh.over))
        return carry

    lax.fori_loop(0, mesh.many // 2, one, 0)


def reduce_blocks(mesh, core, source, mine, outgo, income, send_sem, recv_sem, total_ref, closing):
    pieces = pieces_of(outgo.shape[1], REDUCE_PIECES)
    half = mesh.many // 2
    held = {spot: i for i, spot in enumerate(mesh.round_spots())}

    def across(kind, spot, p):
        slot = held[spot]
        return pltpu.make_async_remote_copy(
            src_ref=source(mesh.number(kind, spot), *pieces[p]),
            dst_ref=income.at[slot, pl.ds(*pieces[p])],
            send_sem=send_sem.at[slot, p],
            recv_sem=recv_sem.at[slot, p],
            device_id=mesh.partner,
            device_id_type=MESH,
        )

    def moved(spot, p, device):
        rows = pl.ds(*pieces[p])
        slot = half + held[spot]
        return pltpu.make_async_remote_copy(
            src_ref=outgo.at[held[spot], rows],
            dst_ref=income.at[slot, rows],
            send_sem=send_sem.at[slot, p],
            recv_sem=recv_sem.at[slot, p],
            device_id=device,
            device_id_type=MESH,
        )

    def far(spot):
        z = {0: 0, 1: 3, 2: 5, 3: 8}.get(spot[2], 2 * spot[2] + 2)
        return z + 2 * (spot[0] > 0) + 2 * (spot[1] > 0)

    axes = REDUCE_AXES[core]

    def hand(spot, p):
        across(1 - core, spot, p).start()

    def pass_on(spot, p):
        rows = pl.ds(*pieces[p])
        across(core, spot, p).wait_recv()
        total = mine(mesh.number(core, spot), *pieces[p]) + income[held[spot], rows].astype(F32)
        last = last_axis(axes, spot)
        for axis in axes[last + 1 :]:
            size = mesh.sizes[axis]
            for step in range(1, size):
                child = tuple(one or other for one, other in zip(spot, at(axis, size - step)))
                moved(child, p, mesh.partner).wait_recv()
                total = total + income[half + held[child], rows].astype(F32)
        if last < 0:
            total_ref[rows, :] = total
        else:
            outgo[held[spot], rows] = total.astype(BF16)
            step = spot["xyz".index(axes[last])]
            moved(spot, p, mesh.device(core, at(axes[last], step))).start()

    every = list(itertools.product(held, range(len(pieces))))
    events = [(-2 * far(spot) - 4 + 0.01 * p, 0, hand, spot, p) for spot, p in every]
    events += [(-2 * far(spot) + 2 * p / len(pieces), 1, pass_on, spot, p) for spot, p in every]
    for _, _, action, spot, p in sorted(events, key=lambda one: one[:2]):
        if not closing:
            action(spot, p)
    for spot, p in every if closing else ():
        across(1 - core, spot, p).wait_send()
        if any(spot):
            moved(spot, p, mesh.partner).wait_send()


def sum_all(mesh, mine, stats, send_sem, recv_sem, meanwhile):
    column = mesh.sizes["z"] * 2
    layer = mesh.sizes["x"] * mesh.sizes["y"]
    groups = (
        (0, column, mesh.here["z"] * 2 + mesh.core, mesh.column()),
        (column, layer, mesh.here["x"] * mesh.sizes["y"] + mesh.here["y"], mesh.layer()),
    )
    total = mine
    for base, size, here, devices in groups:
        stats[base + here] = total

        def sent(j, device, base=base, here=here):
            return pltpu.make_async_remote_copy(
                src_ref=stats.at[base + here],
                dst_ref=stats.at[base + here],
                send_sem=send_sem.at[base + j],
                recv_sem=recv_sem.at[base + here],
                device_id=device,
                device_id_type=MESH,
            )

        def come(place, base=base):
            return pltpu.make_async_remote_copy(
                src_ref=stats.at[base + place],
                dst_ref=stats.at[base + place],
                send_sem=send_sem.at[base],
                recv_sem=recv_sem.at[base + place],
                device_id=mesh.partner,
                device_id_type=MESH,
            )

        for j, device in enumerate(devices):
            sent(j, device).start()
        if not base:
            meanwhile()
        for j in range(1, size):
            come(lax.rem(here + j, size)).wait_recv()
        for j, device in enumerate(devices):
            sent(j, device).wait_send()
        total = stats[base]
        for place in range(1, size):
            total = total + stats[base + place]
    return total


def window_rows(shard_size, many):
    units = [(shard_size * d) // UNIT for d in range(many + 1)]
    return 16 * (max(b - a for a, b in zip(units, units[1:])) + 1)


def first_row(shard_size, number):
    if isinstance(number, int):
        return number * shard_size // UNIT * 16
    return pl.multiple_of(lax.div(number * shard_size, UNIT) * 16, 16)


def inner_units(shard_size, many):
    units = [(shard_size * d) // UNIT for d in range(many + 1)]
    return min(b - a for a, b in zip(units, units[1:]))


def lay_inner(shard_size, many, land, flat, owner):
    count = 16 * inner_units(shard_size, many) - 16
    row = pl.multiple_of(first_row(shard_size, owner) + 16, 16)
    flat[pl.ds(row, count), :] = land[owner, pl.ds(16, count), :].astype(F32)


def lay_edges(shard_size, many, land, flat):
    inner = 16 * inner_units(shard_size, many)
    flat[0:16, :] = jnp.zeros((16, 128), F32)

    def lay(number, carry):
        row = first_row(shard_size, number)
        after = first_row(shard_size, number + 1)
        flat[pl.ds(row, 16), :] += land[number, 0:16, :].astype(F32)
        tail = land[number, pl.ds(inner, 16), :].astype(F32)
        flat[pl.ds(pl.multiple_of(row + inner, 16), 16), :] = tail
        last = pl.multiple_of(after - row, 16)
        flat[pl.ds(after, 16), :] = land[number, pl.ds(last, 16), :].astype(F32)
        return carry

    lax.fori_loop(0, many, lay, 0)


def early_matrices(flat, wall_ref, gain_one_ref, gain_two_ref):
    for c in range(D // 128):
        lanes = slice(c * 128, (c + 1) * 128)
        gain_one_ref[:, lanes] = flat[c : c + 1, :]
        gain_two_ref[:, lanes] = flat[4 + c : 5 + c, :]
    for c in range(QW // 128):
        wall_ref[c * 128 : (c + 1) * 128, :] = flat[pl.ds(WQ_ROW + c, D, stride=12), :].T.astype(BF16)
    for first, row in ((KROW, WK_ROW), (VROW, WV_ROW)):
        pair = flat[row : row + 256, :].T.astype(BF16)
        wall_ref[first : first + H, :] = (
            nn(pair[:H], picks(256, 2, 0).astype(BF16)) + nn(pair[H:], picks(256, 2, 1).astype(BF16))
        ).astype(BF16)
    across = jnp.concatenate(
        [flat[pl.ds(WR_ROW + j, 32, stride=3), :] for j in range(3)], axis=1
    ).T.astype(BF16)
    router_t = jnp.zeros((E, D), F32)
    for part in range(16):
        router_t = router_t + nn(across[part * E : (part + 1) * E, :], picks(32, 16, part).astype(BF16))
    wall_ref[RROW:ALLW, :] = jnp.concatenate(
        [router_t, jnp.zeros((ALLW - RROW - E, D), F32)], axis=0
    ).astype(BF16)


def gather_kernel(
    mesh, shard_size, own_ref,
    wall_out, gain_one_ref, gain_two_ref, wo_out, w1_out, w2_out,
    land, flat, wall_ref, wo_ref, w1_ref, w2_ref, send_sem, recv_sem, out_sem,
):
    mesh = mesh()
    many = mesh.many
    window = land.shape[1]
    begin = mesh.me * shard_size - lax.div(mesh.me * shard_size, UNIT) * UNIT
    row, lane = lax.div(begin, 128), lax.rem(begin, 128)
    flat[0 : window + 48, :] = jnp.zeros((window + 48, 128), F32)
    flat[24 : 24 + own_ref.shape[0], :] = own_ref[...]
    first = pltpu.roll(flat[pl.ds(24 - row, window), :], lane, 1)
    second = pltpu.roll(flat[pl.ds(23 - row, window), :], lane, 1)
    at_lane = lax.broadcasted_iota(jnp.int32, (window, 128), 1)
    land[mesh.me] = jnp.where(at_lane >= lane, first, second).astype(BF16)
    mesh.greet(mesh.near())
    gather_blocks(mesh, land, send_sem, recv_sem, True)
    each_owner(mesh, mesh.core, functools.partial(lay_inner, shard_size, many, land, flat))

    def arrive(owner):
        for p in range(recv_sem.shape[1]):
            rows = pl.ds(*pieces_of(window)[p])
            pltpu.make_async_remote_copy(
                src_ref=land.at[owner, rows],
                dst_ref=land.at[owner, rows],
                send_sem=send_sem.at[0, p],
                recv_sem=recv_sem.at[owner, p],
                device_id=mesh.partner,
                device_id_type=MESH,
            ).wait_recv()
        lay_inner(shard_size, many, land, flat, owner)

    each_owner(mesh, 1 - mesh.core, arrive)
    lay_edges(shard_size, many, land, flat)
    copies = []

    def leave(matrix, out):
        one = pltpu.make_async_copy(matrix, out, out_sem.at[len(copies)])
        one.start()
        copies.append(one)

    for c in range(D // 128):
        wo_ref[:, c * 128 : (c + 1) * 128] = flat[pl.ds(WO_ROW + c, QW, stride=4), :].astype(BF16)
    leave(wo_ref, wo_out)
    for c in range(D // 128):
        w2_ref[:, c * 128 : (c + 1) * 128] = flat[pl.ds(W2_ROW + c, FF, stride=4), :].astype(BF16)
    leave(w2_ref, w2_out)
    for c in range(FF // 128):
        w1_ref[:, c * 128 : (c + 1) * 128] = flat[pl.ds(W1_ROW + c, D, stride=16), :].astype(BF16)
    leave(w1_ref, w1_out)
    early_matrices(flat, wall_ref, gain_one_ref, gain_two_ref)
    leave(wall_ref, wall_out)
    gather_blocks(mesh, land, send_sem, recv_sem, False)
    for one in copies:
        one.wait()


def gather_weights(shards, over, shard_size, window, own):
    many = shards * over
    rows = (shard_size * (many - 1)) // UNIT * 16 + window
    vmem = pl.BlockSpec(memory_space=pltpu.VMEM)
    hbm = pl.BlockSpec(memory_space=pl.ANY)
    mesh = functools.partial(Mesh3, shards, over)
    pieces = len(pieces_of(window))
    return pl.pallas_call(
        functools.partial(gather_kernel, mesh, shard_size),
        in_specs=[vmem],
        out_specs=[hbm, vmem, vmem, hbm, hbm, hbm],
        out_shape=[
            struct((ALLW, D), BF16),
            struct((1, D)),
            struct((1, D)),
            struct((QW, D), BF16),
            struct((D, FF), BF16),
            struct((FF, D), BF16),
        ],
        scratch_shapes=[
            pltpu.VMEM((many, window, 128), BF16),
            pltpu.VMEM((rows, 128), F32),
            pltpu.VMEM((ALLW, D), BF16),
            pltpu.VMEM((QW, D), BF16),
            pltpu.VMEM((D, FF), BF16),
            pltpu.VMEM((FF, D), BF16),
            pltpu.SemaphoreType.DMA((5 * many // 2, pieces)),
            pltpu.SemaphoreType.DMA((many, pieces)),
            pltpu.SemaphoreType.DMA((4,)),
        ],
        compiler_params=pltpu.CompilerParams(
            collective_id=0, has_side_effects=True, vmem_limit_bytes=60 * MIB
        ),
        name="gather_weights",
    )(own)


def reduce_kernel(
    mesh, shard_size, flat_ref, count_ref,
    out_ref, total_ref, gain_ref,
    part, outgo, income, whole_scr, stats, part_sem, send_sem, recv_sem, stat_send, stat_recv,
):
    mesh = mesh()
    window = outgo.shape[1]
    span = part.shape[1]

    def source(owner, first, rows):
        row = pl.multiple_of(first_row(shard_size, owner) + first, 16)
        return flat_ref.at[pl.ds(row, rows), :]

    def fetch(y):
        first = first_row(shard_size, (2 * y + mesh.core) * mesh.over)
        return pltpu.make_async_copy(flat_ref.at[pl.ds(first, span), :], part.at[y], part_sem.at[y])

    def mine(owner, first, rows):
        shard = lax.div(owner, mesh.over)
        row = first_row(shard_size, owner) - first_row(shard_size, shard * mesh.over) + first
        return part[lax.div(shard, 2), pl.ds(pl.multiple_of(row, 16), rows), :].astype(F32)

    for y in range(mesh.sizes["y"]):
        fetch(y).start()
    mesh.greet(mesh.column() + mesh.layer())
    for y in range(mesh.sizes["y"]):
        fetch(y).wait()
    buffers = (source, mine, outgo, income, send_sem, recv_sem, whole_scr)

    def reduce_all(closing):
        for core in range(2):
            pl.when(mesh.core == core)(
                functools.partial(reduce_blocks, mesh, core, *buffers, closing=closing)
            )

    reduce_all(False)

    begin = mesh.me * shard_size - lax.div(mesh.me * shard_size, UNIT) * UNIT
    rows = out_ref.shape[0]
    row, lane = lax.div(begin, 128), lax.rem(begin, 128)
    back = lax.rem(128 - lane, 128)
    first = pltpu.roll(whole_scr[pl.ds(row, rows), :], back, 1)
    second = pltpu.roll(whole_scr[pl.ds(row + 1, rows), :], back, 1)
    at_lane = lax.broadcasted_iota(jnp.int32, (rows, 128), 1)
    place = lax.broadcasted_iota(jnp.int32, (rows, 128), 0) * 128 + at_lane
    total = jnp.where(at_lane < 128 - lane, first, second)
    out_ref[...] = total
    inside = jnp.where(place < shard_size, total, 0.0)
    squares = jnp.sum(jnp.sum(inside * inside, axis=0, keepdims=True), axis=1, keepdims=True)
    lane = lax.broadcasted_iota(jnp.int32, (8, 128), 1)
    row = jnp.where(lane == E, squares, count_ref[...])
    gains = jnp.where(mesh.me == 0, total[0:8, :], 0.0)
    summed = sum_all(
        mesh, jnp.concatenate([row, gains], axis=0), stats, stat_send, stat_recv,
        lambda: reduce_all(True),
    )
    total_ref[...] = summed[0:1, :]
    for c in range(D // 128):
        lanes = slice(c * 128, (c + 1) * 128)
        gain_ref[0:1, lanes] = summed[8 + c : 9 + c, :]
        gain_ref[1:2, lanes] = summed[12 + c : 13 + c, :]


def reduce_grads(shards, over, shard_size, window, flat, counts):
    vmem = pl.BlockSpec(memory_space=pltpu.VMEM)
    many = shards * over
    mesh = functools.partial(Mesh3, shards, over)
    pieces = len(pieces_of(window, REDUCE_PIECES))
    steps = over + shards
    units = [(shard_size * d) // UNIT for d in range(many)]
    span = 16 * max(units[d + over - 1] - units[d] for d in range(0, many, over)) + window
    return pl.pallas_call(
        functools.partial(reduce_kernel, mesh, shard_size),
        in_specs=[pl.BlockSpec(memory_space=pl.ANY), vmem],
        out_specs=[vmem] * 3,
        out_shape=[struct((-(-shard_size // 128), 128)), struct((1, 128)), struct((2, D))],
        scratch_shapes=[
            pltpu.VMEM((shards // 2, span, 128), BF16),
            pltpu.VMEM((many // 2, window, 128), BF16),
            pltpu.VMEM((many, window, 128), BF16),
            pltpu.VMEM((window + 16, 128), F32),
            pltpu.VMEM((steps, 16, 128), F32),
            pltpu.SemaphoreType.DMA((shards // 2,)),
            pltpu.SemaphoreType.DMA((many, pieces)),
            pltpu.SemaphoreType.DMA((many, pieces)),
            pltpu.SemaphoreType.DMA((steps,)),
            pltpu.SemaphoreType.DMA((steps,)),
        ],
        compiler_params=pltpu.CompilerParams(
            collective_id=1, has_side_effects=True, vmem_limit_bytes=56 * MIB
        ),
        name="reduce_grads",
    )(flat, counts)


def local_step(flat_rows, tokens, grad_out, routes, segments, weights):
    wall, gain_one, gain_two, wo, w1, w2 = weights
    queries, attended, gates, lse, kv, kvt, start, routes_t, counts = head_forward(
        tokens, routes.T, segments, wall, gain_one
    )
    output, dres, datt, delta, dlogits, flat, extra, dgain_two = middle(
        flat_rows, tokens, grad_out, gain_two, wo, w1, w2, routes_t, gates, attended
    )
    input_grad, flat = head_backward(
        segments, tokens, gain_one, wall, routes_t, start, queries, datt, lse, delta, kv, kvt, dlogits, dres,
        dgain_two, extra, flat,
    )
    return output, input_grad, flat, counts


def per_device(
    shards, over, tokens, grad_out, routes, segments, params, first_moment, second_moment, ema_weights
):
    shard_size = params.shape[0]
    window = window_rows(shard_size, shards * over)
    flat_rows = (shard_size * (shards * over - 1)) // UNIT * 16 + window + 16
    own_rows = -(-shard_size // 1024) * 8
    own = jnp.pad(params, (0, own_rows * 128 - shard_size)).reshape(own_rows, 128)
    wall, gain_one, gain_two, wo, w1, w2 = gather_weights(shards, over, shard_size, window, own)
    output, input_grad, flat, counts = local_step(
        flat_rows, tokens, grad_out, routes, segments, (wall, gain_one, gain_two, wo, w1, w2)
    )
    reduced, sums, gain_grads = reduce_grads(shards, over, shard_size, window, flat, counts)
    grad_shard = reduced.reshape(-1)[:shard_size]
    total_tokens = tokens.shape[0] * shards * over
    expert_load = sums[0, :E] * (E / (total_tokens * TOPK))
    grad_norm = jnp.sqrt(sums[0, E])
    clipped = grad_shard * (CLIP_LIMIT / jnp.maximum(grad_norm, CLIP_LIMIT))
    new_first = BETA_FIRST * first_moment + (1.0 - BETA_FIRST) * clipped
    new_second = BETA_SECOND * second_moment + (1.0 - BETA_SECOND) * clipped * clipped
    first_hat = new_first / (1.0 - BETA_FIRST**STEP)
    second_hat = new_second / (1.0 - BETA_SECOND**STEP)
    new_params = params * (1.0 - LEARN_RATE * DECAY_RATE) - LEARN_RATE * first_hat / (
        jnp.sqrt(second_hat) + ADAM_EPS
    )
    new_ema = EMA_KEEP * ema_weights + (1.0 - EMA_KEEP) * new_params
    return (
        output,
        input_grad,
        expert_load,
        grad_norm.reshape(1),
        new_params,
        new_first,
        new_second,
        new_ema,
        gain_grads,
    )


def solution(mesh):
    row = P(("dp", "fsdp"), None)
    flat = P(("dp", "fsdp"))
    return jax.shard_map(
        functools.partial(per_device, mesh.shape["dp"], mesh.shape["fsdp"]),
        mesh=mesh,
        in_specs=(row, row, row, row, flat, flat, flat, flat),
        out_specs=(row, row, P(), P(), flat, flat, flat, flat, P()),
        check_vma=False,
    )
```

```python
import copy
import functools
import itertools

import jax
import jax.numpy as jnp
from jax import lax
from jax.experimental import pallas as pl
from jax.experimental.pallas import tpu as pltpu
from jax.sharding import PartitionSpec as P

D = 512
E = 24
TOPK = 8
H = 64
FF = 2048
STEP = 10

NORM_EPS = 1e-06
CLIP_LIMIT = 1.0
BETA_FIRST = 0.9
BETA_SECOND = 0.95
LEARN_RATE = 0.1
DECAY_RATE = 0.1
ADAM_EPS = 1e-08
EMA_KEEP = 0.9
NEG_LARGE = -1e30

QW = E * H
KROW = QW
VROW = QW + H
RROW = QW + 2 * H
ALLW = 1696
LEN = 1024
TB = 512
NB = LEN // TB
QB = 128
SIDE = 4
MOST = 512 // QB + 1
SORT_STEPS = (
    (0, 1), (2, 3), (4, 5), (6, 7), (0, 2), (1, 3), (4, 6), (5, 7), (1, 2), (5, 6),
    (0, 4), (1, 5), (2, 6), (3, 7), (2, 4), (3, 5), (1, 2), (3, 4), (5, 6),
)
FC = 256
MB = 512
MIB = 1 << 20

WR_ROW = 8
WK_ROW = 104
WV_ROW = 360
WQ_ROW = 616
WO_ROW = 6760
W1_ROW = 12904
W2_ROW = 21096
ALL_ROWS = 29288
UNIT = 16 * 128
MESH = pl.DeviceIdType.MESH

F32 = jnp.float32
BF16 = jnp.bfloat16


def nn(a, b):
    return lax.dot_general(a, b, (((1,), (0,)), ((), ())), preferred_element_type=F32)


def nt(a, b):
    return lax.dot_general(a, b, (((1,), (1,)), ((), ())), preferred_element_type=F32)


def tn(a, b):
    return lax.dot_general(a, b, (((0,), (0,)), ((), ())), preferred_element_type=F32)


def rms_scale(values):
    return lax.rsqrt(jnp.mean(values * values, axis=-1, keepdims=True) + NORM_EPS)


def slot_of(routes, k, rows):
    return jnp.broadcast_to(routes[k : k + 1, :], (rows, routes.shape[1]))


def expert_rows(routes, k):
    return jnp.broadcast_to(routes.astype(jnp.int16)[k : k + 1, :], (16, routes.shape[1]))


def pick_heads(routes, source_ref, k):
    tokens = routes.shape[1]
    route = expert_rows(routes, k)
    taken = source_ref[k * H : (k + 1) * H, :].reshape(H // 16, 16, tokens)
    for e in range(k + 1, k + E - TOPK + 1):
        piece = source_ref[e * H : (e + 1) * H, :].reshape(H // 16, 16, tokens)
        taken = jnp.where((route == jnp.int16(e))[None], piece, taken)
    return taken.reshape(H, tokens)


def place_heads(routes, source_ref, target_ref):
    tokens = routes.shape[1]
    rows = [expert_rows(routes, k) for k in range(TOPK)]
    for e in range(E):
        total = jnp.zeros((H // 16, 16, tokens), BF16)
        for k in range(max(0, e - (E - TOPK)), min(TOPK - 1, e) + 1):
            piece = source_ref[k * H : (k + 1) * H, :].reshape(H // 16, 16, tokens)
            total = jnp.where((rows[k] == jnp.int16(e))[None], piece, total)
        target_ref[e * H : (e + 1) * H, :] = total.reshape(H, tokens)


def sorted_rows(rows):
    rows = list(rows)
    for one, two in SORT_STEPS:
        rows[one], rows[two] = jnp.minimum(rows[one], rows[two]), jnp.maximum(rows[one], rows[two])
    return rows


def key_mask(first_key, first_query, rows, start_row):
    keys = lax.broadcasted_iota(jnp.int32, (rows, QB), 0) + first_key
    queries = lax.broadcasted_iota(jnp.int32, (rows, QB), 1) + first_query
    mask = (keys <= queries) & (keys >= start_row)
    return jnp.concatenate([mask] * SIDE, axis=1)


def group_of(ref, k, lanes):
    return jnp.concatenate([ref[i * H : (i + 1) * H, lanes] for i in range(k, k + SIDE)], axis=1)


def row_group(ref, k, lanes):
    return jnp.concatenate([ref[i : i + 1, lanes] for i in range(k, k + SIDE)], axis=1)


def by_span(attend, row, place, segment_ref):
    def one(j, carry):
        block = place * (TB // QB) + j
        first = block * QB
        span = jnp.int32(1)
        for back in range(MOST - 1):
            last = first - back * QB - 1
            same = segment_ref[row, jnp.maximum(last, 0)] == segment_ref[row, first]
            span = span + jnp.where((last >= 0) & same, 1, 0)
        for blocks in range(1, MOST + 1):

            @pl.when(span == blocks)
            def _(blocks=blocks):
                attend(pl.ds(pl.multiple_of(j * QB, QB), QB), block, blocks)

        return carry

    lax.fori_loop(0, TB // QB, one, 0)


def head_forward_kernel(
    steps, segment_smem, x_ref, route_ref, segment_ref, wall_ref, gain_ref,
    q_ref, att_ref, gate_ref, lse_ref, kv_ref, kvt_ref, start_ref, sorted_ref, count_ref,
    all_scr, low_scr, k_scr, vt_scr, count_scr,
):
    step = pl.program_id(0)
    place = lax.rem(step, NB)
    here = pl.multiple_of(place * TB, TB)

    @pl.when(step == 0)
    def _():
        count_scr[...] = jnp.zeros_like(count_scr)

    row = segment_ref[pl.ds(lax.div(step, NB), 1), :]
    segments = segment_ref[pl.ds(lax.div(step, NB), 1), pl.ds(here, TB)]
    start = jnp.zeros((1, TB), jnp.int32)
    for number in range(1, 4):
        below = jnp.sum((row < number).astype(jnp.int32), axis=1, keepdims=True)
        start = jnp.where(segments == number, below, start)
    start_ref[...] = start
    x = x_ref[...].astype(F32)
    normed = (x * rms_scale(x) * gain_ref[...]).astype(BF16)
    all_scr[...] = nt(wall_ref[...], normed)
    kt = all_scr[KROW : KROW + H, :]
    vt = all_scr[VROW : VROW + H, :]
    logits = all_scr[RROW : RROW + E, :]
    kvt = jnp.concatenate([kt, vt], axis=0)
    kv = kvt.T.astype(BF16)
    kv_ref[...] = kv
    kvt_ref[...] = kvt.astype(BF16)
    k_scr[pl.ds(here, TB), :] = kv[:, :H]
    vt_scr[:, pl.ds(here, TB)] = vt.astype(BF16)
    routes = jnp.concatenate(sorted_rows(route_ref[k : k + 1, :] for k in range(TOPK)), axis=0)
    sorted_ref[...] = routes
    experts = lax.broadcasted_iota(jnp.int32, (E, TB), 0)
    chosen = []
    counts = count_scr[...]
    for k in range(TOPK):
        named = slot_of(routes, k, E) == experts
        chosen.append(jnp.sum(jnp.where(named, logits, 0.0), axis=0, keepdims=True))
        counts = counts + named.astype(F32)
    count_scr[...] = counts
    chosen = jnp.concatenate(chosen, axis=0)
    raised = jnp.exp(chosen - jnp.max(chosen, axis=0, keepdims=True))
    gate_ref[...] = raised / jnp.sum(raised, axis=0, keepdims=True)
    low_scr[...] = all_scr[0:QW, :].astype(BF16)
    for k in range(TOPK):
        q_ref[k * H : (k + 1) * H, :] = pick_heads(routes, low_scr, k) * jnp.asarray(H ** (-0.5), BF16)

    def attend(lanes, block, blocks):
        rows = blocks * QB
        first_key = pl.multiple_of((block - (blocks - 1)) * QB, QB)
        mask = key_mask(first_key, block * QB, rows, start_ref[:, lanes])
        keys = k_scr[pl.ds(first_key, rows), :]
        values = vt_scr[:, pl.ds(first_key, rows)]
        groups = [nn(keys, group_of(q_ref, 0, lanes))]
        for k in range(0, TOPK, SIDE):
            if k + SIDE < TOPK:
                groups.append(nn(keys, group_of(q_ref, k + SIDE, lanes)))
            scores = jnp.where(mask, groups[k // SIDE], NEG_LARGE)
            top = jnp.max(scores, axis=0, keepdims=True)
            raised = jnp.exp(scores - top)
            total = jnp.sum(raised, axis=0, keepdims=True)
            out = nn(values, (raised * (1.0 / total)).astype(BF16))
            lse = top + jnp.log(total)
            for side in range(SIDE):
                one = slice(side * QB, (side + 1) * QB)
                att_ref[(k + side) * H : (k + side + 1) * H, lanes] = out[:, one]
                lse_ref[k + side : k + side + 1, lanes] = lse[:, one]

    by_span(attend, lax.div(step, NB), place, segment_smem)

    @pl.when(step == steps - 1)
    def _():
        held = jnp.sum(count_scr[...], axis=1, keepdims=True)
        lane = lax.broadcasted_iota(jnp.int32, (E, 128), 1)
        row = lax.broadcasted_iota(jnp.int32, (E, 128), 0)
        count_ref[...] = jnp.sum(jnp.where(lane == row, held, 0.0), axis=0, keepdims=True)


def picks(rows, stride, first):
    at = lax.broadcasted_iota(jnp.int32, (rows, D), 1)
    row = lax.broadcasted_iota(jnp.int32, (rows, D), 0)
    return (at == row * stride + first).astype(F32)


def exact(product, a, b):
    return lax.dot_general(
        a, b, (product, ((), ())), precision=lax.Precision.HIGHEST, preferred_element_type=F32
    )


def gelu_parts(v):
    cdf = 0.5 + 0.5 * lax.erf(v * 0.7071067811865476)
    return cdf, jnp.exp(v * v * -0.5) * 0.3989422804014327


def middle_kernel(
    x_ref, dy_ref, gain_ref, wo_ref, w1_ref, w2_ref, route_ref, gate_ref, att_ref,
    out_ref, dres_ref, datt_ref, delta_ref, dlogit_ref, flat_ref, extra_ref, dgain_ref,
    slot_scr, head_scr, mix_scr, hidden_scr, dpre_scr, dwo_ref, dw1_ref, dw2t_ref, rows_scr, low_scr, row_sem,
):
    step = pl.program_id(0)

    @pl.when(step == 0)
    def _():
        dwo_ref[...] = jnp.zeros_like(dwo_ref)
        dw1_ref[...] = jnp.zeros_like(dw1_ref)
        dw2t_ref[...] = jnp.zeros_like(dw2t_ref)
        dgain_ref[...] = jnp.zeros_like(dgain_ref)

    routes = route_ref[...]
    tokens = routes.shape[1]
    gates = gate_ref[...]
    for k in range(TOPK):
        rows = slice(k * H, (k + 1) * H)
        slot_scr[rows, :] = (gates[k : k + 1, :] * att_ref[rows, :]).astype(BF16)
    place_heads(routes, slot_scr, mix_scr)
    x = x_ref[...].astype(F32)
    dy = dy_ref[...]
    mixed = mix_scr[...]
    residual = x + tn(mixed, wo_ref[...])
    scale = rms_scale(residual)
    gain = gain_ref[...]
    second = (residual * scale * gain).astype(BF16)
    second_t = second.T
    dy_t = dy.T
    pre = [nn(second, w1_ref[:, 0:FC])]
    back = [nt(dy, w2_ref[0:FC, :])]
    for i in range(FF // FC):
        here = slice(i * FC, (i + 1) * FC)
        if i + 1 < FF // FC:
            after = slice((i + 1) * FC, (i + 2) * FC)
            pre.append(nn(second, w1_ref[:, after]))
            back.append(nt(dy, w2_ref[after, :]))
        cdf, density = gelu_parts(pre[i])
        hidden_scr[:, here] = (pre[i] * cdf).astype(BF16)
        dpre_scr[:, here] = (back[i] * (cdf + pre[i] * density)).astype(BF16)
    dsecond = nt(dpre_scr[...], w1_ref[...])
    out_ref[...] = (residual + nn(hidden_scr[...], w2_ref[...])).astype(BF16)
    dw1_ref[...] += nn(second_t, dpre_scr[...])
    dw2t_ref[...] += nn(dy_t, hidden_scr[...])
    dgain_ref[...] += jnp.sum(dsecond * residual * scale, axis=0, keepdims=True)
    weighted = gain * dsecond
    dres = (
        dy.astype(F32)
        + scale * weighted
        - residual * (scale * scale * scale) * jnp.mean(weighted * residual, axis=-1, keepdims=True)
    )
    dres_ref[...] = dres
    branch = dres.astype(BF16)
    dwo_ref[...] += nn(mixed, branch)
    head_scr[...] = nt(wo_ref[...], branch).astype(BF16)
    dgates = []
    for k in range(TOPK):
        rows = slice(k * H, (k + 1) * H)
        dslot = pick_heads(routes, head_scr, k).astype(F32)
        attended = att_ref[rows, :]
        dgates.append(jnp.sum(dslot * attended, axis=0, keepdims=True))
        datt = (gates[k : k + 1, :] * dslot).astype(BF16)
        datt_ref[rows, :] = datt
        delta_ref[k : k + 1, :] = jnp.sum(datt.astype(F32) * attended, axis=0, keepdims=True)
    dgate = jnp.concatenate(dgates, axis=0)
    dchosen = gates * (dgate - jnp.sum(gates * dgate, axis=0, keepdims=True))
    experts = lax.broadcasted_iota(jnp.int32, (E, tokens), 0)
    dlogits = jnp.zeros((E, tokens), F32)
    for k in range(TOPK):
        dlogits = jnp.where(
            slot_of(routes, k, E) == experts,
            jnp.broadcast_to(dchosen[k : k + 1, :], (E, tokens)),
            dlogits,
        )
    dlogit_ref[...] = dlogits

    @pl.when(step == pl.num_programs(0) - 1)
    def _():
        last = low_scr.shape[0]
        ends = (0, (W1_ROW - WO_ROW - 8) // 16 * 16, (W2_ROW - WO_ROW - 8) // 16 * 16, last)

        def out(number):
            first, count = ends[number], ends[number + 1] - ends[number]
            return pltpu.make_async_copy(
                low_scr.at[pl.ds(first, count), :],
                flat_ref.at[pl.ds(WO_ROW + 8 + first, count), :],
                row_sem.at[number],
            )

        def leave(number):
            first, count = ends[number], ends[number + 1] - ends[number]
            low_scr[pl.ds(first, count), :] = rows_scr[pl.ds(first + 8, count), :].astype(BF16)
            out(number).start()

        for c in range(D // 128):
            rows_scr[pl.ds(c, QW, stride=4), :] = dwo_ref[:, c * 128 : (c + 1) * 128]
        extra_ref[...] = rows_scr[0:8, :]
        leave(0)
        for c in range(FF // 128):
            rows_scr[pl.ds(W1_ROW - WO_ROW + c, D, stride=16), :] = dw1_ref[:, c * 128 : (c + 1) * 128]
        leave(1)
        for c in range(D // 128):
            rows_scr[pl.ds(W2_ROW - WO_ROW + c, FF, stride=4), :] = dw2t_ref[c * 128 : (c + 1) * 128, :].T
        leave(2)
        for number in range(3):
            out(number).wait()


def head_backward_kernel(
    segment_smem, x_ref, gain_ref, wall_ref, route_ref, start_ref, q_ref, datt_ref,
    lse_ref, delta_ref, kv_ref, kvt_ref, dlogit_ref, dres_ref, dgain_two_ref, extra_ref, flat_in,
    dx_ref, flat_ref,
    dk_scr, dv_scr, dq_scr, dall_scr, prob_scr, dscore_scr, dwall_ref, dgain_ref, rows_scr, low_scr, row_sem,
):
    step = pl.program_id(0)
    place = NB - 1 - lax.rem(step, NB)
    here = pl.multiple_of(place * TB, TB)

    @pl.when(step == 0)
    def _():
        dwall_ref[...] = jnp.zeros_like(dwall_ref)
        dgain_ref[...] = jnp.zeros_like(dgain_ref)

    @pl.when(lax.rem(step, NB) == 0)
    def _():
        dk_scr[...] = jnp.zeros_like(dk_scr)
        dv_scr[...] = jnp.zeros_like(dv_scr)

    def attend(lanes, block, blocks):
        rows = blocks * QB
        first_key = pl.multiple_of((block - (blocks - 1)) * QB, QB)
        mask = key_mask(first_key, block * QB, rows, start_ref[:, lanes])
        keys = kv_ref[pl.ds(first_key, rows), :H]
        values = kv_ref[pl.ds(first_key, rows), H:]
        keys_t = kvt_ref[:H, pl.ds(first_key, rows)]
        queries = [group_of(q_ref, k, lanes) for k in range(0, TOPK, SIDE)]
        datts = [group_of(datt_ref, k, lanes) for k in range(0, TOPK, SIDE)]
        scores = [nn(keys, queries[0])]
        dprobs = [nn(values, datts[0])]
        for i in range(TOPK // SIDE):
            if i + 1 < TOPK // SIDE:
                scores.append(nn(keys, queries[i + 1]))
                dprobs.append(nn(values, datts[i + 1]))
            k = i * SIDE
            wide = slice(k * QB, (k + SIDE) * QB)
            probs = jnp.exp(jnp.where(mask, scores[i], NEG_LARGE) - row_group(lse_ref, k, lanes))
            dscore = (probs * (dprobs[i] - row_group(delta_ref, k, lanes))).astype(BF16)
            prob_scr[0:rows, wide] = probs.astype(BF16)
            dscore_scr[0:rows, wide] = dscore
            dq = (nn(keys_t, dscore) * (H ** (-0.5))).astype(BF16)
            for side in range(SIDE):
                dq_scr[(k + side) * H : (k + side + 1) * H, lanes] = dq[:, side * QB : (side + 1) * QB]
        dv_scr[pl.ds(first_key, rows), :] += nt(prob_scr[0:rows, :], jnp.concatenate(datts, axis=1))
        dk_scr[pl.ds(first_key, rows), :] += nt(dscore_scr[0:rows, :], jnp.concatenate(queries, axis=1))

    by_span(attend, lax.div(step, NB), place, segment_smem)
    place_heads(route_ref[...], dq_scr, dall_scr)
    dkv = jnp.concatenate([dk_scr[pl.ds(here, TB), :], dv_scr[pl.ds(here, TB), :]], axis=1)
    dall_scr[KROW : KROW + 2 * H, :] = dkv.T.astype(BF16)
    dall_scr[RROW : RROW + 32, :] = jnp.concatenate(
        [dlogit_ref[...], jnp.zeros((32 - E, TB), F32)], axis=0
    ).astype(BF16)
    x = x_ref[...].astype(F32)
    scale = rms_scale(x)
    gain = gain_ref[...]
    normed = (x * scale * gain).astype(BF16)
    dall = dall_scr[...]
    dwall_ref[...] += nn(dall, normed)
    dnormed = tn(dall, wall_ref[...])
    dgain_ref[...] += jnp.sum(dnormed * x * scale, axis=0, keepdims=True)
    weighted = gain * dnormed
    dx_ref[...] = (
        dres_ref[...]
        + scale * weighted
        - x * (scale * scale * scale) * jnp.mean(weighted * x, axis=-1, keepdims=True)
    )

    @pl.when(step == pl.num_programs(0) - 1)
    def _():
        for c in range(D // 128):
            lanes = slice(c * 128, (c + 1) * 128)
            rows_scr[c : c + 1, :] = dgain_ref[:, lanes]
            rows_scr[4 + c : 5 + c, :] = dgain_two_ref[:, lanes]
        router_t = dwall_ref[RROW : RROW + E, :]
        across = jnp.concatenate(
            [exact(((1,), (1,)), router_t, picks(32, 16, b)) for b in range(16)], axis=0
        ).T
        for j in range(3):
            rows_scr[pl.ds(WR_ROW + j, 32, stride=3), :] = across[:, j * 128 : (j + 1) * 128]
        for first, row in ((KROW, WK_ROW), (VROW, WV_ROW)):
            part = dwall_ref[first : first + H, :]
            rows_scr[row : row + 256, :] = jnp.concatenate(
                [exact(((1,), (1,)), picks(256, 2, b), part) for b in range(2)], axis=1
            )
        for c in range(QW // 128):
            rows_scr[pl.ds(WQ_ROW + c, D, stride=12), :] = dwall_ref[c * 128 : (c + 1) * 128, :].T
        rows_scr[WO_ROW : WO_ROW + 8, :] = extra_ref[...]
        low_scr[...] = rows_scr[...].astype(BF16)
        copy = pltpu.make_async_copy(low_scr, flat_ref.at[pl.ds(0, WO_ROW + 8), :], row_sem.at[0])
        copy.start()
        copy.wait()


def whole(shape):
    return pl.BlockSpec(shape, lambda *_: (0,) * len(shape), pipeline_mode=pl.Buffered(1))


def kept(shape):
    return pl.BlockSpec(shape, lambda *_: (0,) * len(shape))


SMEM = pl.BlockSpec(memory_space=pltpu.SMEM)


def struct(shape, kind=F32):
    return jax.ShapeDtypeStruct(shape, kind)


def params_for(mib):
    return pltpu.CompilerParams(vmem_limit_bytes=mib * MIB)


def head_forward(tokens, routes_t, segments, wall, gain):
    count = tokens.shape[0]
    steps = count // TB
    across = lambda rows: pl.BlockSpec((rows, TB), lambda b: (0, b))
    down = lambda columns: pl.BlockSpec((TB, columns), lambda b: (b, 0))
    return pl.pallas_call(
        functools.partial(head_forward_kernel, steps),
        grid=(steps,),
        in_specs=[SMEM, down(D), across(TOPK), whole(segments.shape), whole((ALLW, D)), whole((1, D))],
        out_specs=[
            across(TOPK * H), across(TOPK * H), across(TOPK), across(TOPK), down(2 * H), across(2 * H),
            across(1), across(TOPK), whole((1, 128)),
        ],
        scratch_shapes=[
            pltpu.VMEM((ALLW, TB), F32),
            pltpu.VMEM((QW, TB), BF16),
            pltpu.VMEM((LEN, H), BF16),
            pltpu.VMEM((H, LEN), BF16),
            pltpu.VMEM((E, TB), F32),
        ],
        out_shape=[
            struct((TOPK * H, count), BF16),
            struct((TOPK * H, count)),
            struct((TOPK, count)),
            struct((TOPK, count)),
            struct((count, 2 * H), BF16),
            struct((2 * H, count), BF16),
            struct((1, count), jnp.int32),
            struct((TOPK, count), jnp.int32),
            struct((1, 128)),
        ],
        compiler_params=params_for(56),
        name="head_forward",
        cost_estimate=pl.CostEstimate(flops=10_000_000_000, bytes_accessed=16_000_000, transcendentals=0),
    )(segments, tokens, routes_t, segments, wall, gain)


def middle(flat_rows, tokens, grad_out, gain, wo, w1, w2, routes_t, gates, attended):
    count = tokens.shape[0]
    steps = count // MB
    across = lambda rows: pl.BlockSpec((rows, MB), lambda b: (0, b))
    down = lambda columns: pl.BlockSpec((MB, columns), lambda b: (b, 0))
    return pl.pallas_call(
        middle_kernel,
        grid=(steps,),
        in_specs=[
            down(D), down(D), whole((1, D)), whole((QW, D)), whole((D, FF)), whole((FF, D)),
            across(TOPK), across(TOPK), across(TOPK * H),
        ],
        out_specs=[
            down(D), down(D), across(TOPK * H), across(TOPK), across(E),
            pl.BlockSpec(memory_space=pl.ANY), whole((8, 128)), whole((1, D)),
        ],
        out_shape=[
            struct((count, D), BF16),
            struct((count, D)),
            struct((TOPK * H, count), BF16),
            struct((TOPK, count)),
            struct((E, count)),
            struct((flat_rows, 128), BF16),
            struct((8, 128)),
            struct((1, D)),
        ],
        scratch_shapes=[
            pltpu.VMEM((TOPK * H, MB), BF16),
            pltpu.VMEM((QW, MB), BF16),
            pltpu.VMEM((QW, MB), BF16),
            pltpu.VMEM((MB, FF), BF16),
            pltpu.VMEM((MB, FF), BF16),
            pltpu.VMEM((QW, D), F32),
            pltpu.VMEM((D, FF), F32),
            pltpu.VMEM((D, FF), F32),
            pltpu.VMEM((flat_rows - WO_ROW, 128), F32),
            pltpu.VMEM((flat_rows - WO_ROW - 8, 128), BF16),
            pltpu.SemaphoreType.DMA((3,)),
        ],
        compiler_params=params_for(60),
        name="middle",
    )(tokens, grad_out, gain, wo, w1, w2, routes_t, gates, attended)


def head_backward(
    segments, tokens, gain, wall, routes_t, start, queries, datt, lse, delta, kv, kvt, dlogits, dres,
    dgain_two, extra, flat,
):
    count = tokens.shape[0]
    steps = count // TB

    def place(b):
        return (b // NB) * NB + NB - 1 - b % NB

    across = lambda rows: pl.BlockSpec((rows, TB), lambda b: (0, place(b)))
    down = lambda columns: pl.BlockSpec((TB, columns), lambda b: (place(b), 0))
    return pl.pallas_call(
        head_backward_kernel,
        grid=(steps,),
        in_specs=[
            SMEM, down(D), whole((1, D)), whole((ALLW, D)), across(TOPK), across(1),
            across(TOPK * H), across(TOPK * H), across(TOPK), across(TOPK),
            pl.BlockSpec((LEN, 2 * H), lambda b: (b // NB, 0)),
            pl.BlockSpec((2 * H, LEN), lambda b: (0, b // NB)),
            across(E), down(D), whole((1, D)), whole((8, 128)), pl.BlockSpec(memory_space=pl.ANY),
        ],
        out_specs=[down(D), pl.BlockSpec(memory_space=pl.ANY)],
        scratch_shapes=[
            pltpu.VMEM((LEN, H), F32),
            pltpu.VMEM((LEN, H), F32),
            pltpu.VMEM((TOPK * H, TB), BF16),
            pltpu.VMEM((ALLW, TB), BF16),
            pltpu.VMEM((MOST * QB, TOPK * QB), BF16),
            pltpu.VMEM((MOST * QB, TOPK * QB), BF16),
            pltpu.VMEM((ALLW, D), F32),
            pltpu.VMEM((1, D), F32),
            pltpu.VMEM((WO_ROW + 8, 128), F32),
            pltpu.VMEM((WO_ROW + 8, 128), BF16),
            pltpu.SemaphoreType.DMA((1,)),
        ],
        out_shape=[struct((count, D)), struct(flat.shape, BF16)],
        input_output_aliases={16: 1},
        compiler_params=params_for(56),
        name="head_backward",
        cost_estimate=pl.CostEstimate(flops=30_000_000_000, bytes_accessed=24_000_000, transcendentals=0),
    )(
        segments, tokens, gain, wall, routes_t, start, queries, datt, lse, delta, kv, kvt, dlogits, dres,
        dgain_two, extra, flat,
    )


class Mesh3:
    def __init__(self, shards, over):
        shard = lax.axis_index("dp")
        other = lax.axis_index("fsdp")
        self.over = over
        self.many = shards * over
        self.sizes = {"x": 2, "y": shards // 2, "z": over // 2}
        self.here = {"x": lax.rem(other, 2), "y": lax.div(shard, 2), "z": lax.div(other, 2)}
        self.core = lax.rem(shard, 2)
        self.me = shard * over + other
        self.partner = (shard + 1 - 2 * self.core, other)

    def at_z(self, z):
        same = copy.copy(self)
        if z is not None:
            same.here = dict(self.here, z=z)
        return same

    def spots(self):
        x, y, z = (self.sizes[axis] for axis in "xyz")
        return list(itertools.product(range(x), range(y), range(1 - z, z)))

    def round_spots(self):
        return list(itertools.product(*[range(self.sizes[axis]) for axis in "xyz"]))

    def exists(self, z_steps):
        place = self.here["z"] + z_steps
        if isinstance(place, int):
            return 0 <= place < self.sizes["z"]
        return (place >= 0) & (place < self.sizes["z"])

    def device(self, core, spot):
        size = self.sizes["z"]
        x = lax.rem(self.here["x"] + spot[0], self.sizes["x"])
        y = lax.rem(self.here["y"] + spot[1], self.sizes["y"])
        z = self.here["z"] + spot[2]
        z = z % size if isinstance(z, int) else lax.rem(z + size, size)
        return (y * 2 + core, z * 2 + x)

    def number(self, core, spot):
        shard, other = self.device(core, spot)
        return shard * self.over + other

    def greet(self, devices):
        barrier = pltpu.get_barrier_semaphore()
        for device in devices:
            pl.semaphore_signal(barrier, inc=1, device_id=device, device_id_type=MESH)
        pl.semaphore_wait(barrier, len(devices))

    def near(self):
        steps = [at(axis, step) for axis in "xyz" for step in range(1, self.sizes[axis])]
        return [self.device(self.core, step) for step in steps] + [self.partner]

    def column(self):
        steps = [(core, step) for core in range(2) for step in range(self.sizes["z"]) if core or step]
        return [self.device(lax.rem(self.core + core, 2), (0, 0, step)) for core, step in steps]

    def layer(self):
        steps = [(x, y, 0) for x in range(self.sizes["x"]) for y in range(self.sizes["y"]) if x or y]
        return [self.device(self.core, step) for step in steps]


def at(axis, step):
    return tuple(step if one == axis else 0 for one in "xyz")


def last_axis(axes, spot):
    return max([i for i, axis in enumerate(axes) if spot["xyz".index(axis)]], default=-1)


def pieces_of(window, count=3):
    if window < 512:
        return [(0, window)]
    ends = [window // 16 * i // count * 16 for i in range(count)] + [window]
    return [(first, last - first) for first, last in zip(ends, ends[1:])]


def act(condition, action):
    if condition is True:
        action()
    elif condition is not False:
        pl.when(condition)(action)


GATHER_AXES = (("zxy", "yzx"), ("zyx", "xzy"))
REDUCE_PIECES = 2
REDUCE_AXES = ("zxy", "zyx")


def onward(mesh, axes, spot):
    last = last_axis(axes, spot)
    steps = []
    if last >= 0 and axes[last] == "z":
        steps.append(("z", -1 if spot[2] > 0 else 1))
    for axis in axes[last + 1 :]:
        steps += [("z", 1), ("z", -1)] if axis == "z" else [
            (axis, one) for one in range(1, mesh.sizes[axis])
        ]
    return steps


def gather_own_core(mesh, core, land, send_sem, recv_sem, begin):
    window = land.shape[1]
    pieces = pieces_of(window)
    slots = {}
    events = []

    def moved(owner, device, slot, p):
        rows = pl.ds(*pieces[p])
        return pltpu.make_async_remote_copy(
            src_ref=land.at[owner, rows],
            dst_ref=land.at[owner, rows],
            send_sem=send_sem.at[slot, p],
            recv_sem=recv_sem.at[owner, p],
            device_id=device,
            device_id_type=MESH,
        )

    for spot in mesh.spots():
        there = mesh.exists(spot[2])
        if there is False:
            continue
        owner = mesh.number(core, spot)
        turn = 0.5 * abs(spot[2]) + (spot[0] > 0) + (spot[1] > 0) + (0.001 if spot[2] < 0 else 0)
        for p in range(len(pieces)):
            sends = []
            for axis, step in onward(mesh, GATHER_AXES[core][p % 2], spot):
                key = (spot[0], spot[1], spot[2] % mesh.sizes["z"], axis, step)
                away = mesh.exists(step) if axis == "z" else True
                if away is not False:
                    slot = slots.setdefault(key, len(slots))
                    sends.append((mesh.device(core, at(axis, step)), slot, away))
            key = (spot[0], spot[1], spot[2] % mesh.sizes["z"])
            sends.append((mesh.partner, slots.setdefault(key, len(slots)), True))

            def come(owner=owner, spot=spot, p=p, sends=sends):
                if any(spot):
                    moved(owner, mesh.partner, 0, p).wait_recv()
                for device, slot, away in sends:
                    act(away, moved(owner, device, slot, p).start)

            def done(owner=owner, p=p, sends=sends):
                for _, slot, away in sends:
                    act(away, moved(owner, mesh.partner, slot, p).wait_send)

            events.append((turn + 0.01 * p, there, come if begin else done))
    for _, there, action in sorted(events, key=lambda one: one[0]):
        act(there, action)


def gather_blocks(mesh, land, send_sem, recv_sem, begin):
    known = range(mesh.sizes["z"]) if mesh.sizes["z"] <= 4 else [None]
    for core in range(2):
        for z in known:

            @pl.when((mesh.core == core) & (True if z is None else mesh.here["z"] == z))
            def _(core=core, z=z):
                gather_own_core(mesh.at_z(z), core, land, send_sem, recv_sem, begin)


def each_owner(mesh, core, action):
    def one(number, carry):
        shard = 2 * lax.div(number, mesh.over) + core
        action(shard * mesh.over + lax.rem(number, mesh.over))
        return carry

    lax.fori_loop(0, mesh.many // 2, one, 0)


def reduce_blocks(mesh, core, source, mine, outgo, income, send_sem, recv_sem, total_ref, closing):
    pieces = pieces_of(outgo.shape[1], REDUCE_PIECES)
    half = mesh.many // 2
    held = {spot: i for i, spot in enumerate(mesh.round_spots())}

    def across(kind, spot, p):
        slot = held[spot]
        return pltpu.make_async_remote_copy(
            src_ref=source(mesh.number(kind, spot), *pieces[p]),
            dst_ref=income.at[slot, pl.ds(*pieces[p])],
            send_sem=send_sem.at[slot, p],
            recv_sem=recv_sem.at[slot, p],
            device_id=mesh.partner,
            device_id_type=MESH,
        )

    def moved(spot, p, device):
        rows = pl.ds(*pieces[p])
        slot = half + held[spot]
        return pltpu.make_async_remote_copy(
            src_ref=outgo.at[held[spot], rows],
            dst_ref=income.at[slot, rows],
            send_sem=send_sem.at[slot, p],
            recv_sem=recv_sem.at[slot, p],
            device_id=device,
            device_id_type=MESH,
        )

    def far(spot):
        z = {0: 0, 1: 3, 2: 5, 3: 8}.get(spot[2], 2 * spot[2] + 2)
        return z + 2 * (spot[0] > 0) + 2 * (spot[1] > 0)

    axes = REDUCE_AXES[core]

    def hand(spot, p):
        across(1 - core, spot, p).start()

    def pass_on(spot, p):
        rows = pl.ds(*pieces[p])
        across(core, spot, p).wait_recv()
        total = mine(mesh.number(core, spot), *pieces[p]) + income[held[spot], rows].astype(F32)
        last = last_axis(axes, spot)
        for axis in axes[last + 1 :]:
            size = mesh.sizes[axis]
            for step in range(1, size):
                child = tuple(one or other for one, other in zip(spot, at(axis, size - step)))
                moved(child, p, mesh.partner).wait_recv()
                total = total + income[half + held[child], rows].astype(F32)
        if last < 0:
            total_ref[rows, :] = total
        else:
            outgo[held[spot], rows] = total.astype(BF16)
            step = spot["xyz".index(axes[last])]
            moved(spot, p, mesh.device(core, at(axes[last], step))).start()

    every = list(itertools.product(held, range(len(pieces))))
    events = [(-2 * far(spot) - 4 + 0.01 * p, 0, hand, spot, p) for spot, p in every]
    events += [(-2 * far(spot) + 2 * p / len(pieces), 1, pass_on, spot, p) for spot, p in every]
    for _, _, action, spot, p in sorted(events, key=lambda one: one[:2]):
        if not closing:
            action(spot, p)
    for spot, p in every if closing else ():
        across(1 - core, spot, p).wait_send()
        if any(spot):
            moved(spot, p, mesh.partner).wait_send()


def sum_all(mesh, mine, stats, send_sem, recv_sem, meanwhile):
    column = mesh.sizes["z"] * 2
    layer = mesh.sizes["x"] * mesh.sizes["y"]
    groups = (
        (0, column, mesh.here["z"] * 2 + mesh.core, mesh.column()),
        (column, layer, mesh.here["x"] * mesh.sizes["y"] + mesh.here["y"], mesh.layer()),
    )
    total = mine
    for base, size, here, devices in groups:
        stats[base + here] = total

        def sent(j, device, base=base, here=here):
            return pltpu.make_async_remote_copy(
                src_ref=stats.at[base + here],
                dst_ref=stats.at[base + here],
                send_sem=send_sem.at[base + j],
                recv_sem=recv_sem.at[base + here],
                device_id=device,
                device_id_type=MESH,
            )

        def come(place, base=base):
            return pltpu.make_async_remote_copy(
                src_ref=stats.at[base + place],
                dst_ref=stats.at[base + place],
                send_sem=send_sem.at[base],
                recv_sem=recv_sem.at[base + place],
                device_id=mesh.partner,
                device_id_type=MESH,
            )

        for j, device in enumerate(devices):
            sent(j, device).start()
        if not base:
            meanwhile()
        for j in range(1, size):
            come(lax.rem(here + j, size)).wait_recv()
        for j, device in enumerate(devices):
            sent(j, device).wait_send()
        total = stats[base]
        for place in range(1, size):
            total = total + stats[base + place]
    return total


def window_rows(shard_size, many):
    units = [(shard_size * d) // UNIT for d in range(many + 1)]
    return 16 * (max(b - a for a, b in zip(units, units[1:])) + 1)


def first_row(shard_size, number):
    if isinstance(number, int):
        return number * shard_size // UNIT * 16
    return pl.multiple_of(lax.div(number * shard_size, UNIT) * 16, 16)


def inner_units(shard_size, many):
    units = [(shard_size * d) // UNIT for d in range(many + 1)]
    return min(b - a for a, b in zip(units, units[1:]))


def lay_inner(shard_size, many, land, flat, owner):
    count = 16 * inner_units(shard_size, many) - 16
    row = pl.multiple_of(first_row(shard_size, owner) + 16, 16)
    flat[pl.ds(row, count), :] = land[owner, pl.ds(16, count), :].astype(F32)


def lay_edges(shard_size, many, land, flat):
    inner = 16 * inner_units(shard_size, many)
    flat[0:16, :] = jnp.zeros((16, 128), F32)

    def lay(number, carry):
        row = first_row(shard_size, number)
        after = first_row(shard_size, number + 1)
        flat[pl.ds(row, 16), :] += land[number, 0:16, :].astype(F32)
        tail = land[number, pl.ds(inner, 16), :].astype(F32)
        flat[pl.ds(pl.multiple_of(row + inner, 16), 16), :] = tail
        last = pl.multiple_of(after - row, 16)
        flat[pl.ds(after, 16), :] = land[number, pl.ds(last, 16), :].astype(F32)
        return carry

    lax.fori_loop(0, many, lay, 0)


def early_matrices(flat, wall_ref, gain_one_ref, gain_two_ref):
    for c in range(D // 128):
        lanes = slice(c * 128, (c + 1) * 128)
        gain_one_ref[:, lanes] = flat[c : c + 1, :]
        gain_two_ref[:, lanes] = flat[4 + c : 5 + c, :]
    for c in range(QW // 128):
        wall_ref[c * 128 : (c + 1) * 128, :] = flat[pl.ds(WQ_ROW + c, D, stride=12), :].T.astype(BF16)
    for first, row in ((KROW, WK_ROW), (VROW, WV_ROW)):
        pair = flat[row : row + 256, :].T.astype(BF16)
        wall_ref[first : first + H, :] = (
            nn(pair[:H], picks(256, 2, 0).astype(BF16)) + nn(pair[H:], picks(256, 2, 1).astype(BF16))
        ).astype(BF16)
    across = jnp.concatenate(
        [flat[pl.ds(WR_ROW + j, 32, stride=3), :] for j in range(3)], axis=1
    ).T.astype(BF16)
    router_t = jnp.zeros((E, D), F32)
    for part in range(16):
        router_t = router_t + nn(across[part * E : (part + 1) * E, :], picks(32, 16, part).astype(BF16))
    wall_ref[RROW:ALLW, :] = jnp.concatenate(
        [router_t, jnp.zeros((ALLW - RROW - E, D), F32)], axis=0
    ).astype(BF16)


def gather_kernel(
    mesh, shard_size, own_ref,
    wall_out, gain_one_ref, gain_two_ref, wo_out, w1_out, w2_out,
    land, flat, wall_ref, wo_ref, w1_ref, w2_ref, send_sem, recv_sem, out_sem,
):
    mesh = mesh()
    many = mesh.many
    window = land.shape[1]
    begin = mesh.me * shard_size - lax.div(mesh.me * shard_size, UNIT) * UNIT
    row, lane = lax.div(begin, 128), lax.rem(begin, 128)
    flat[0 : window + 48, :] = jnp.zeros((window + 48, 128), F32)
    flat[24 : 24 + own_ref.shape[0], :] = own_ref[...]
    first = pltpu.roll(flat[pl.ds(24 - row, window), :], lane, 1)
    second = pltpu.roll(flat[pl.ds(23 - row, window), :], lane, 1)
    at_lane = lax.broadcasted_iota(jnp.int32, (window, 128), 1)
    land[mesh.me] = jnp.where(at_lane >= lane, first, second).astype(BF16)
    mesh.greet(mesh.near())
    gather_blocks(mesh, land, send_sem, recv_sem, True)
    each_owner(mesh, mesh.core, functools.partial(lay_inner, shard_size, many, land, flat))

    def arrive(owner):
        for p in range(recv_sem.shape[1]):
            rows = pl.ds(*pieces_of(window)[p])
            pltpu.make_async_remote_copy(
                src_ref=land.at[owner, rows],
                dst_ref=land.at[owner, rows],
                send_sem=send_sem.at[0, p],
                recv_sem=recv_sem.at[owner, p],
                device_id=mesh.partner,
                device_id_type=MESH,
            ).wait_recv()
        lay_inner(shard_size, many, land, flat, owner)

    each_owner(mesh, 1 - mesh.core, arrive)
    lay_edges(shard_size, many, land, flat)
    copies = []

    def leave(matrix, out):
        one = pltpu.make_async_copy(matrix, out, out_sem.at[len(copies)])
        one.start()
        copies.append(one)

    for c in range(D // 128):
        wo_ref[:, c * 128 : (c + 1) * 128] = flat[pl.ds(WO_ROW + c, QW, stride=4), :].astype(BF16)
    leave(wo_ref, wo_out)
    for c in range(D // 128):
        w2_ref[:, c * 128 : (c + 1) * 128] = flat[pl.ds(W2_ROW + c, FF, stride=4), :].astype(BF16)
    leave(w2_ref, w2_out)
    for c in range(FF // 128):
        w1_ref[:, c * 128 : (c + 1) * 128] = flat[pl.ds(W1_ROW + c, D, stride=16), :].astype(BF16)
    leave(w1_ref, w1_out)
    early_matrices(flat, wall_ref, gain_one_ref, gain_two_ref)
    leave(wall_ref, wall_out)
    gather_blocks(mesh, land, send_sem, recv_sem, False)
    for one in copies:
        one.wait()


def gather_weights(shards, over, shard_size, window, own):
    many = shards * over
    rows = (shard_size * (many - 1)) // UNIT * 16 + window
    vmem = pl.BlockSpec(memory_space=pltpu.VMEM)
    hbm = pl.BlockSpec(memory_space=pl.ANY)
    mesh = functools.partial(Mesh3, shards, over)
    pieces = len(pieces_of(window))
    return pl.pallas_call(
        functools.partial(gather_kernel, mesh, shard_size),
        in_specs=[vmem],
        out_specs=[hbm, vmem, vmem, hbm, hbm, hbm],
        out_shape=[
            struct((ALLW, D), BF16),
            struct((1, D)),
            struct((1, D)),
            struct((QW, D), BF16),
            struct((D, FF), BF16),
            struct((FF, D), BF16),
        ],
        scratch_shapes=[
            pltpu.VMEM((many, window, 128), BF16),
            pltpu.VMEM((rows, 128), F32),
            pltpu.VMEM((ALLW, D), BF16),
            pltpu.VMEM((QW, D), BF16),
            pltpu.VMEM((D, FF), BF16),
            pltpu.VMEM((FF, D), BF16),
            pltpu.SemaphoreType.DMA((5 * many // 2, pieces)),
            pltpu.SemaphoreType.DMA((many, pieces)),
            pltpu.SemaphoreType.DMA((4,)),
        ],
        compiler_params=pltpu.CompilerParams(
            collective_id=0, has_side_effects=True, vmem_limit_bytes=60 * MIB
        ),
        name="gather_weights",
    )(own)


def reduce_kernel(
    mesh, shard_size, flat_ref, count_ref,
    out_ref, total_ref, gain_ref,
    part, outgo, income, whole_scr, stats, part_sem, send_sem, recv_sem, stat_send, stat_recv,
):
    mesh = mesh()
    window = outgo.shape[1]
    span = part.shape[1]

    def source(owner, first, rows):
        row = pl.multiple_of(first_row(shard_size, owner) + first, 16)
        return flat_ref.at[pl.ds(row, rows), :]

    def fetch(y):
        first = first_row(shard_size, (2 * y + mesh.core) * mesh.over)
        return pltpu.make_async_copy(flat_ref.at[pl.ds(first, span), :], part.at[y], part_sem.at[y])

    def mine(owner, first, rows):
        shard = lax.div(owner, mesh.over)
        row = first_row(shard_size, owner) - first_row(shard_size, shard * mesh.over) + first
        return part[lax.div(shard, 2), pl.ds(pl.multiple_of(row, 16), rows), :].astype(F32)

    for y in range(mesh.sizes["y"]):
        fetch(y).start()
    mesh.greet(mesh.column() + mesh.layer())
    for y in range(mesh.sizes["y"]):
        fetch(y).wait()
    buffers = (source, mine, outgo, income, send_sem, recv_sem, whole_scr)

    def reduce_all(closing):
        for core in range(2):
            pl.when(mesh.core == core)(
                functools.partial(reduce_blocks, mesh, core, *buffers, closing=closing)
            )

    reduce_all(False)

    begin = mesh.me * shard_size - lax.div(mesh.me * shard_size, UNIT) * UNIT
    rows = out_ref.shape[0]
    row, lane = lax.div(begin, 128), lax.rem(begin, 128)
    back = lax.rem(128 - lane, 128)
    first = pltpu.roll(whole_scr[pl.ds(row, rows), :], back, 1)
    second = pltpu.roll(whole_scr[pl.ds(row + 1, rows), :], back, 1)
    at_lane = lax.broadcasted_iota(jnp.int32, (rows, 128), 1)
    place = lax.broadcasted_iota(jnp.int32, (rows, 128), 0) * 128 + at_lane
    total = jnp.where(at_lane < 128 - lane, first, second)
    out_ref[...] = total
    inside = jnp.where(place < shard_size, total, 0.0)
    squares = jnp.sum(jnp.sum(inside * inside, axis=0, keepdims=True), axis=1, keepdims=True)
    lane = lax.broadcasted_iota(jnp.int32, (8, 128), 1)
    row = jnp.where(lane == E, squares, count_ref[...])
    gains = jnp.where(mesh.me == 0, total[0:8, :], 0.0)
    summed = sum_all(
        mesh, jnp.concatenate([row, gains], axis=0), stats, stat_send, stat_recv,
        lambda: reduce_all(True),
    )
    total_ref[...] = summed[0:1, :]
    for c in range(D // 128):
        lanes = slice(c * 128, (c + 1) * 128)
        gain_ref[0:1, lanes] = summed[8 + c : 9 + c, :]
        gain_ref[1:2, lanes] = summed[12 + c : 13 + c, :]


def reduce_grads(shards, over, shard_size, window, flat, counts):
    vmem = pl.BlockSpec(memory_space=pltpu.VMEM)
    many = shards * over
    mesh = functools.partial(Mesh3, shards, over)
    pieces = len(pieces_of(window, REDUCE_PIECES))
    steps = over + shards
    units = [(shard_size * d) // UNIT for d in range(many)]
    span = 16 * max(units[d + over - 1] - units[d] for d in range(0, many, over)) + window
    return pl.pallas_call(
        functools.partial(reduce_kernel, mesh, shard_size),
        in_specs=[pl.BlockSpec(memory_space=pl.ANY), vmem],
        out_specs=[vmem] * 3,
        out_shape=[struct((-(-shard_size // 128), 128)), struct((1, 128)), struct((2, D))],
        scratch_shapes=[
            pltpu.VMEM((shards // 2, span, 128), BF16),
            pltpu.VMEM((many // 2, window, 128), BF16),
            pltpu.VMEM((many, window, 128), BF16),
            pltpu.VMEM((window + 16, 128), F32),
            pltpu.VMEM((steps, 16, 128), F32),
            pltpu.SemaphoreType.DMA((shards // 2,)),
            pltpu.SemaphoreType.DMA((many, pieces)),
            pltpu.SemaphoreType.DMA((many, pieces)),
            pltpu.SemaphoreType.DMA((steps,)),
            pltpu.SemaphoreType.DMA((steps,)),
        ],
        compiler_params=pltpu.CompilerParams(
            collective_id=1, has_side_effects=True, vmem_limit_bytes=56 * MIB
        ),
        name="reduce_grads",
    )(flat, counts)


def local_step(flat_rows, tokens, grad_out, routes, segments, weights):
    wall, gain_one, gain_two, wo, w1, w2 = weights
    queries, attended, gates, lse, kv, kvt, start, routes_t, counts = head_forward(
        tokens, routes.T, segments, wall, gain_one
    )
    output, dres, datt, delta, dlogits, flat, extra, dgain_two = middle(
        flat_rows, tokens, grad_out, gain_two, wo, w1, w2, routes_t, gates, attended
    )
    input_grad, flat = head_backward(
        segments, tokens, gain_one, wall, routes_t, start, queries, datt, lse, delta, kv, kvt, dlogits, dres,
        dgain_two, extra, flat,
    )
    return output, input_grad, flat, counts


def per_device(
    shards, over, tokens, grad_out, routes, segments, params, first_moment, second_moment, ema_weights
):
    shard_size = params.shape[0]
    window = window_rows(shard_size, shards * over)
    flat_rows = (shard_size * (shards * over - 1)) // UNIT * 16 + window + 16
    own_rows = -(-shard_size // 1024) * 8
    own = jnp.pad(params, (0, own_rows * 128 - shard_size)).reshape(own_rows, 128)
    wall, gain_one, gain_two, wo, w1, w2 = gather_weights(shards, over, shard_size, window, own)
    output, input_grad, flat, counts = local_step(
        flat_rows, tokens, grad_out, routes, segments, (wall, gain_one, gain_two, wo, w1, w2)
    )
    reduced, sums, gain_grads = reduce_grads(shards, over, shard_size, window, flat, counts)
    grad_shard = reduced.reshape(-1)[:shard_size]
    total_tokens = tokens.shape[0] * shards * over
    expert_load = sums[0, :E] * (E / (total_tokens * TOPK))
    grad_norm = jnp.sqrt(sums[0, E])
    clipped = grad_shard * (CLIP_LIMIT / jnp.maximum(grad_norm, CLIP_LIMIT))
    new_first = BETA_FIRST * first_moment + (1.0 - BETA_FIRST) * clipped
    new_second = BETA_SECOND * second_moment + (1.0 - BETA_SECOND) * clipped * clipped
    first_hat = new_first / (1.0 - BETA_FIRST**STEP)
    second_hat = new_second / (1.0 - BETA_SECOND**STEP)
    new_params = params * (1.0 - LEARN_RATE * DECAY_RATE) - LEARN_RATE * first_hat / (
        jnp.sqrt(second_hat) + ADAM_EPS
    )
    new_ema = EMA_KEEP * ema_weights + (1.0 - EMA_KEEP) * new_params
    return (
        output,
        input_grad,
        expert_load,
        grad_norm.reshape(1),
        new_params,
        new_first,
        new_second,
        new_ema,
        gain_grads,
    )


def solution(mesh):
    row = P(("dp", "fsdp"), None)
    flat = P(("dp", "fsdp"))
    return jax.shard_map(
        functools.partial(per_device, mesh.shape["dp"], mesh.shape["fsdp"]),
        mesh=mesh,
        in_specs=(row, row, row, row, flat, flat, flat, flat),
        out_specs=(row, row, P(), P(), flat, flat, flat, flat, P()),
        check_vma=False,
    )
```
